32 devices in a mesh: dp: 2 (over core), ctx: 4 (over z), head: 4 (over y, x).
Axes of the slice: x: 2, y: 2, z: 4, core: 2. Of those that a mesh axis runs over, the one named last changes fastest.
Arguments:
- queries: bfloat16 [2, 512, 2560], P('dp', 'ctx', 'head'), may hold values from -25 to 25
- keys: bfloat16 [2, 512, 2560], P('dp', 'ctx', 'head'), may hold values from -25 to 25
- values: bfloat16 [2, 512, 2560], P('dp', 'ctx', 'head'), may hold values from -6 to 6
- grad_y: bfloat16 [2, 512, 2560], P('dp', 'ctx', 'head'), may hold values from -6 to 6
- out_gain: float32 [2560], P('head'), may hold values from 0.1 to 1.9
- offsets: int32 [2, 20], P(None, 'head'), may hold values from 0 to 7, as said below
Outputs:
- attended: bfloat16 [2, 512, 2560], P('dp', 'ctx', 'head')
- query_grad: bfloat16 [2, 512, 2560], P('dp', 'ctx', 'head')
- key_grad: bfloat16 [2, 512, 2560], P('dp', 'ctx', 'head')
- value_grad: bfloat16 [2, 512, 2560], P('dp', 'ctx', 'head')
- gain_grad: float32 [2560], P('head')
The draws below stay inside these ranges and needn't reach their ends.
Inputs may be any that keep to these rules, and one draw needn't show every extreme that they name: Row 0 holds offsets below 8, row 1 offsets below 4.
All inputs are finite; a program needn't handle non-finite values.
Results may differ from the reference program's by a relative error of at most 0.011.
Values may be sent and summed in bfloat16 or wider, within the bound.
No kernel may reach another device: no remote copies, remote signals or barrier semaphores. Data moves between devices by JAX's collectives and lax.ppermute only.
A program may use at most 64 MiB of HBM per device.

```python
import math
import jax
import jax.numpy as jnp
from jax import lax

D = 2560
HEADS = 20
TOK_DEV = 128
SPAN = 4
R1 = 8
SEQS = 2
LEN = 512
R2 = 4


def paired_rows(base_key):
    shape = (SEQS, LEN, D)
    split_keys = jax.random.split(base_key, 2)
    base_rows = jnp.clip(jax.random.normal(split_keys[0], shape, jnp.float32), -4.5, 4.5)
    other_rows = jnp.clip(jax.random.normal(split_keys[1], shape, jnp.float32), -4.5, 4.5)
    query_rows = base_rows
    key_rows = other_rows
    return (query_rows, key_rows)


def draw_queries(key, part):
    return paired_rows(jax.random.fold_in(key, 11))[0].astype(jnp.bfloat16)


def draw_keys(key, part):
    return paired_rows(jax.random.fold_in(key, 11))[1].astype(jnp.bfloat16)


def draw_offsets(key, part):
    split_keys = jax.random.split(key, 5)
    head_ids = jnp.arange(HEADS, dtype=jnp.int32)
    middle = jax.random.randint(split_keys[0], (HEADS,), 0, R1, dtype=jnp.int32)
    outer = jax.random.randint(split_keys[1], (HEADS,), 0, R2, dtype=jnp.int32)
    low_head = jax.random.randint(split_keys[2], (), 0, HEADS, dtype=jnp.int32)
    step_head = jax.random.randint(split_keys[3], (), 1, HEADS, dtype=jnp.int32)
    high_head = (low_head + step_head) % HEADS
    outer_head = jax.random.randint(split_keys[4], (), 0, HEADS, dtype=jnp.int32)
    middle = jnp.where(head_ids == high_head, R1 - 1, middle)
    middle = jnp.where(head_ids == low_head, 0, middle)
    outer = jnp.where(head_ids == outer_head, R2 - 1, outer)
    return jnp.stack([middle, outer]).astype(jnp.int32)


def levels(stream_key, shape, pieces, smallest, top_value):
    def one(position, blocks):
        heights = jax.random.uniform(jax.random.fold_in(jax.random.fold_in(stream_key, 6), position), (blocks,), jnp.float32, smallest / len(pieces), top_value / len(pieces))
        return jnp.repeat(jnp.exp(heights), shape[position] // blocks).reshape((-1,) + (1,) * (len(shape) - position - 1))

    factor_of = one(*pieces[0])
    for cut in pieces[1:]:
        factor_of = factor_of * one(*cut)
    return factor_of


def noise(rng, dims, scale, most, shards=(), kind=jnp.bfloat16):
    factor_of = levels(rng, dims, shards, -0.22, 0.18) if shards else 1.0
    array = jax.random.normal(rng, dims, jnp.float32) * scale * factor_of
    return jnp.minimum(jnp.maximum(array, -most), most).astype(kind)


def setup_inputs(seed: int = 0) -> dict:
    arg_keys = jax.random.split(jax.random.key(seed), 7)
    queries = draw_queries(jax.random.fold_in(arg_keys[6], 71), 0)
    keys = draw_keys(jax.random.fold_in(arg_keys[6], 71), 0)
    values = noise(arg_keys[2], (SEQS, LEN, D), 1.0, 6.0, ((0, 2), (1, 4), (2, 4)))
    grad_y = noise(arg_keys[3], (SEQS, LEN, D), 1.0, 6.0, ((0, 2), (1, 4), (2, 4)))
    out_gain = jnp.clip(1.0 + 0.18 * jax.random.normal(arg_keys[4], (D,), jnp.float32), 0.1, 1.9)
    offsets = draw_offsets(jax.random.fold_in(arg_keys[6], 71), 0)
    return dict(queries=queries, keys=keys, values=values, grad_y=grad_y, out_gain=out_gain, offsets=offsets)


EPS = 1e-06

def pick_rows(source_rows, dilation, shifts):
    seq_count, row_count, head_count, head_width = source_rows.shape
    grouped = source_rows.reshape(seq_count, row_count // dilation, dilation, head_count, head_width)
    pick_index = jnp.broadcast_to(shifts.astype(jnp.int32).reshape(1, 1, 1, head_count, 1), (seq_count, row_count // dilation, 1, head_count, head_width))
    return jnp.take_along_axis(grouped, pick_index, axis=2)[:, :, 0]

def place_rows(row_values, dilation, shifts):
    seq_count, row_count, head_count, head_width = row_values.shape
    hit_mask = jnp.arange(dilation, dtype=jnp.int32).reshape(1, 1, dilation, 1, 1) == shifts.astype(jnp.int32).reshape(1, 1, 1, head_count, 1)
    spread = jnp.where(hit_mask, row_values[:, :, None], jnp.zeros((), row_values.dtype))
    return spread.reshape(seq_count, row_count * dilation, head_count, head_width)

def to_segments(row_values, per_seg):
    seq_count, row_count, head_count, head_width = row_values.shape
    split_rows = row_values.reshape(seq_count, row_count // per_seg, per_seg, head_count, head_width)
    return jnp.transpose(split_rows, (3, 0, 1, 2, 4)).reshape(head_count, seq_count * (row_count // per_seg), per_seg, head_width)

def from_segments(blocks, seq_count):
    head_count, groups, per_seg, head_width = blocks.shape
    split_rows = blocks.reshape(head_count, seq_count, groups // seq_count, per_seg, head_width)
    return jnp.transpose(split_rows, (1, 2, 3, 0, 4)).reshape(seq_count, groups // seq_count * per_seg, head_count, head_width)

def level_scores(q_rows, k_rows):
    score_scale = 1.0 / math.sqrt(q_rows.shape[-1])
    return jnp.einsum('gqe,gke->gqk', q_rows.astype(jnp.float32), k_rows.astype(jnp.float32)) * score_scale

def forward_block(inputs):
    q_rows, k_rows, v_rows = inputs
    scores = level_scores(q_rows, k_rows)
    row_max = lax.optimization_barrier(jnp.max(scores, axis=-1, keepdims=True))
    log_total = row_max[..., 0] + jnp.log(lax.optimization_barrier(jnp.sum(jnp.exp(scores - row_max), axis=-1)))
    soft_rows = jnp.exp(scores - log_total[..., None]).astype(jnp.bfloat16)
    level_out = jnp.einsum('gqk,gke->gqe', soft_rows.astype(jnp.float32), v_rows.astype(jnp.float32))
    return (level_out, log_total)

def backward_block(inputs):
    q_rows, k_rows, v_rows, log_total, grad_out, row_shift = inputs
    score_scale = 1.0 / math.sqrt(q_rows.shape[-1])
    scores = level_scores(q_rows, k_rows)
    exact_soft = jnp.exp(scores - log_total[..., None])
    grad_low = grad_out.astype(jnp.bfloat16)
    prob_grad = jnp.einsum('gqe,gke->gqk', grad_low.astype(jnp.float32), v_rows.astype(jnp.float32))
    score_grad = (exact_soft * (prob_grad + row_shift[..., None]) * score_scale).astype(jnp.bfloat16)
    soft_low = exact_soft.astype(jnp.bfloat16)
    q_part = jnp.einsum('gqk,gke->gqe', score_grad.astype(jnp.float32), k_rows.astype(jnp.float32))
    k_part = jnp.einsum('gqk,gqe->gke', score_grad.astype(jnp.float32), q_rows.astype(jnp.float32))
    v_part = jnp.einsum('gqk,gqe->gke', soft_low.astype(jnp.float32), grad_low.astype(jnp.float32))
    return (q_part, k_part, v_part)

def reference(queries, keys, values, grad_y, out_gain, offsets):
    seq_count, seq_len, model_width = queries.shape
    head_count = HEADS
    head_width = model_width // head_count
    full_shape = (seq_count, seq_len, head_count, head_width)
    q_all = queries.reshape(full_shape)
    k_all = keys.reshape(full_shape)
    v_all = values.reshape(full_shape)
    plans = ((1, TOK_DEV, jnp.zeros((head_count,), jnp.int32)), (R1, SPAN * TOK_DEV, offsets[0]), (R2, seq_len, offsets[1]))
    positions = jnp.arange(seq_len, dtype=jnp.int32)
    level_out = []
    level_total = []
    level_hit = []
    level_parts = []
    level_blocks = []
    for dilation, segment, shifts in plans:
        per_seg = segment // dilation
        parts = tuple((to_segments(pick_rows(source_rows, dilation, shifts), per_seg) for source_rows in (q_all, k_all, v_all)))
        out_blocks, total_blocks = lax.map(forward_block, parts)
        compact_out = from_segments(out_blocks, seq_count)
        compact_total = from_segments(total_blocks[..., None], seq_count)
        level_out.append(place_rows(compact_out, dilation, shifts))
        level_total.append(place_rows(compact_total, dilation, shifts)[..., 0])
        level_hit.append((positions % dilation)[None, :, None] == shifts.astype(jnp.int32)[None, None, :])
        level_parts.append(parts)
        level_blocks.append(total_blocks)
    row_max = level_total[0]
    for level in (1, 2):
        row_max = jnp.maximum(row_max, jnp.where(level_hit[level], level_total[level], level_total[0]))
    expos = [jnp.where(level_hit[level], jnp.exp(level_total[level] - row_max), 0.0) for level in range(3)]
    denom = expos[0] + expos[1] + expos[2]
    shares = [expo / denom for expo in expos]
    attn = shares[0][..., None] * level_out[0] + shares[1][..., None] * level_out[1] + shares[2][..., None] * level_out[2]
    inv_rms = lax.rsqrt(lax.optimization_barrier(jnp.mean(attn * attn, axis=-1, keepdims=True)) + EPS)
    normed = attn * inv_rms
    gain_rows = out_gain.reshape(head_count, head_width)
    attended = (normed * gain_rows).astype(jnp.bfloat16).reshape(seq_count, seq_len, model_width)
    grad_full = grad_y.astype(jnp.float32).reshape(full_shape)
    gain_grad = lax.optimization_barrier(jnp.sum(grad_full * normed, axis=(0, 1))).reshape(model_width)
    grad_norm = grad_full * gain_rows
    grad_attn = inv_rms * (grad_norm - normed * lax.optimization_barrier(jnp.mean(grad_norm * normed, axis=-1, keepdims=True)))
    inner = lax.optimization_barrier(jnp.sum(grad_attn * attn, axis=-1))
    sums = []
    for level, (dilation, segment, shifts) in enumerate(plans):
        per_seg = segment // dilation
        share_sel = pick_rows(shares[level][..., None], dilation, shifts)[..., 0]
        grad_out = share_sel[..., None] * pick_rows(grad_attn, dilation, shifts)
        row_shift = -(share_sel * pick_rows(inner[..., None], dilation, shifts)[..., 0])
        q_seg, k_seg, v_seg = level_parts[level]
        shift_seg = to_segments(row_shift[..., None], per_seg)[..., 0]
        grads = lax.map(backward_block, (q_seg, k_seg, v_seg, level_blocks[level], to_segments(grad_out, per_seg), shift_seg))
        sums.append(tuple((place_rows(from_segments(part, seq_count), dilation, shifts) for part in grads)))
    outputs = []
    for which in range(3):
        total = sums[0][which] + sums[1][which] + sums[2][which]
        outputs.append(total.astype(jnp.bfloat16).reshape(seq_count, seq_len, model_width))
    return (attended, outputs[0], outputs[1], outputs[2], gain_grad)
```

```python
import functools
import math

import jax
import jax.numpy as jnp
from jax import lax
from jax.experimental import pallas as pl
from jax.experimental.pallas import tpu as pltpu
from jax.sharding import PartitionSpec as P

HEAD_DIM = 128
SPAN = 4
R1 = 8


EPS = 1e-06


def swapped(block, axis, bit):
    count = lax.axis_size(axis)
    route = []
    for low in range(count):
        high = low | 1 << bit
        if high != low and high < count:
            route += [(low, high), (high, low)]
    return lax.ppermute(block, axis, route)


def pick_rows(source_rows, dilation, shifts):
    row_count, head_count, head_width = source_rows.shape
    grouped = source_rows.reshape(row_count // dilation, dilation, head_count, head_width)
    hit_mask = jnp.arange(dilation, dtype=jnp.int32).reshape(1, dilation, 1, 1) == shifts.reshape(
        1, 1, head_count, 1
    )
    chosen = jnp.where(hit_mask, grouped, jnp.zeros((), source_rows.dtype))
    return jnp.sum(chosen, axis=1, dtype=source_rows.dtype)


def place_rows(row_values, dilation, shifts):
    row_count, head_count, head_width = row_values.shape
    hit_mask = jnp.arange(dilation, dtype=jnp.int32).reshape(1, dilation, 1, 1) == shifts.reshape(
        1, 1, head_count, 1
    )
    spread = jnp.where(hit_mask, row_values[:, None], jnp.zeros((), row_values.dtype))
    return spread.reshape(row_count * dilation, head_count, head_width)


def level_scores(q_rows, k_rows):
    score_scale = 1.0 / math.sqrt(q_rows.shape[-1])
    return (
        jnp.einsum("qhe,khe->hqk", q_rows, k_rows, preferred_element_type=jnp.float32) * score_scale
    )


def attend(q_rows, k_rows, v_rows):
    scores = level_scores(q_rows, k_rows)
    row_max = jnp.max(scores, axis=-1, keepdims=True)
    log_total = row_max[..., 0] + jnp.log(jnp.sum(jnp.exp(scores - row_max), axis=-1))
    soft_rows = jnp.exp(scores - log_total[..., None]).astype(jnp.bfloat16)
    level_out = jnp.einsum("hqk,khe->qhe", soft_rows, v_rows, preferred_element_type=jnp.float32)
    return (level_out, log_total.T)


def score_grads(q_rows, k_rows, v_rows, log_total, grad_low, row_shift):
    score_scale = 1.0 / math.sqrt(q_rows.shape[-1])
    scores = level_scores(q_rows, k_rows)
    exact_soft = jnp.exp(scores - log_total.T[..., None])
    prob_grad = jnp.einsum("qhe,khe->hqk", grad_low, v_rows, preferred_element_type=jnp.float32)
    score_grad = (exact_soft * (prob_grad + row_shift.T[..., None]) * score_scale).astype(
        jnp.bfloat16
    )
    return (score_grad, exact_soft.astype(jnp.bfloat16))


def key_parts(score_grad, soft_low, q_rows, grad_low):
    k_part = jnp.einsum("hqk,qhe->khe", score_grad, q_rows, preferred_element_type=jnp.float32)
    v_part = jnp.einsum("hqk,qhe->khe", soft_low, grad_low, preferred_element_type=jnp.float32)
    return (k_part, v_part)


def query_part(score_grad, k_rows):
    return jnp.einsum("hqk,khe->qhe", score_grad, k_rows, preferred_element_type=jnp.float32)


def general_shards(queries, keys, values, grad_y, out_gain, offsets):
    tokens = queries.shape[1]
    flat_width = queries.shape[2]
    head_count = flat_width // HEAD_DIM
    row_shape = (tokens, head_count, HEAD_DIM)
    q_own = queries[0].reshape(row_shape)
    k_own = keys[0].reshape(row_shape)
    v_own = values[0].reshape(row_shape)
    ctx_size = lax.axis_size("ctx")
    span_bits = SPAN.bit_length() - 1
    my_place = lax.axis_index("ctx")
    mid_shift = offsets[0]
    top_shift = offsets[1]
    positions = jnp.arange(tokens, dtype=jnp.int32)
    mid_hit = (positions % R1)[:, None] == mid_shift[None, :]
    top_hit = (positions % ctx_size)[:, None] == top_shift[None, :]
    mid_q = pick_rows(q_own, R1, mid_shift)
    mid_k = pick_rows(k_own, R1, mid_shift)
    mid_v = pick_rows(v_own, R1, mid_shift)
    top_q = pick_rows(q_own, ctx_size, top_shift)
    top_k = pick_rows(k_own, ctx_size, top_shift)
    top_v = pick_rows(v_own, ctx_size, top_shift)
    mid_keys = mid_k.reshape(-1, flat_width)
    mid_vals = mid_v.reshape(-1, flat_width)
    top_keys = top_k.reshape(-1, flat_width)
    top_vals = top_v.reshape(-1, flat_width)

    def append_peer(mine, received, level_bit):
        upper_side = my_place >> level_bit & 1 == 1
        return jnp.where(
            upper_side, jnp.concatenate([received, mine], 0), jnp.concatenate([mine, received], 0)
        )

    for level_bit in range(span_bits):
        received = swapped((mid_keys, mid_vals), "ctx", level_bit)
        mid_keys = append_peer(mid_keys, received[0], level_bit)
        mid_vals = append_peer(mid_vals, received[1], level_bit)
    top_keys, top_vals = (
        lax.all_gather(top_keys, "ctx", axis=0, tiled=True),
        lax.all_gather(top_vals, "ctx", axis=0, tiled=True),
    )
    mid_keys = mid_keys.reshape(-1, head_count, HEAD_DIM)
    mid_vals = mid_vals.reshape(-1, head_count, HEAD_DIM)
    top_keys = top_keys.reshape(-1, head_count, HEAD_DIM)
    top_vals = top_vals.reshape(-1, head_count, HEAD_DIM)
    base_out, base_total = attend(q_own, k_own, v_own)
    mid_out, mid_total = attend(mid_q, mid_keys, mid_vals)
    top_out, top_total = attend(top_q, top_keys, top_vals)
    mid_full = place_rows(mid_total[..., None], R1, mid_shift)[..., 0]
    top_full = place_rows(top_total[..., None], ctx_size, top_shift)[..., 0]
    row_max = jnp.maximum(base_total, jnp.where(mid_hit, mid_full, base_total))
    row_max = jnp.maximum(row_max, jnp.where(top_hit, top_full, base_total))
    base_expo = jnp.exp(base_total - row_max)
    mid_expo = jnp.where(mid_hit, jnp.exp(mid_full - row_max), 0.0)
    top_expo = jnp.where(top_hit, jnp.exp(top_full - row_max), 0.0)
    denom = base_expo + mid_expo + top_expo
    base_share = base_expo / denom
    mid_share = mid_expo / denom
    top_share = top_expo / denom
    attn = (
        base_share[..., None] * base_out
        + mid_share[..., None] * place_rows(mid_out, R1, mid_shift)
        + top_share[..., None] * place_rows(top_out, ctx_size, top_shift)
    )
    inv_rms = lax.rsqrt(jnp.mean(attn * attn, axis=-1, keepdims=True) + EPS)
    normed = attn * inv_rms
    gain_rows = out_gain.reshape(head_count, HEAD_DIM)
    attended = (normed * gain_rows).astype(jnp.bfloat16).reshape(1, tokens, flat_width)
    grad_full = grad_y[0].reshape(row_shape).astype(jnp.float32)
    gain_part = jnp.sum(grad_full * normed, axis=0).reshape(flat_width)
    gain_grad = lax.psum(gain_part, ("dp", "ctx"))
    grad_norm = grad_full * gain_rows
    grad_attn = inv_rms * (
        grad_norm - normed * jnp.mean(grad_norm * normed, axis=-1, keepdims=True)
    )
    inner = jnp.sum(grad_attn * attn, axis=-1)
    base_low = (base_share[..., None] * grad_attn).astype(jnp.bfloat16)
    base_shift = -(base_share * inner)
    base_grad, base_soft = score_grads(q_own, k_own, v_own, base_total, base_low, base_shift)
    base_dq = query_part(base_grad, k_own)
    base_dk, base_dv = key_parts(base_grad, base_soft, q_own, base_low)
    mid_sel = pick_rows(mid_share[..., None], R1, mid_shift)[..., 0]
    mid_low = (mid_sel[..., None] * pick_rows(grad_attn, R1, mid_shift)).astype(jnp.bfloat16)
    mid_row_shift = -(mid_sel * pick_rows(inner[..., None], R1, mid_shift)[..., 0])
    mid_grad, mid_soft = score_grads(mid_q, mid_keys, mid_vals, mid_total, mid_low, mid_row_shift)
    mid_dq = query_part(mid_grad, mid_keys)
    mid_dk, mid_dv = key_parts(mid_grad, mid_soft, mid_q, mid_low)
    mid_dk = mid_dk.reshape(-1, flat_width)
    mid_dv = mid_dv.reshape(-1, flat_width)
    for level_bit in reversed(range(span_bits)):
        half_rows = mid_dk.shape[0] // 2
        upper_side = my_place >> level_bit & 1 == 1
        keep_k = jnp.where(upper_side, mid_dk[half_rows:], mid_dk[:half_rows])
        keep_v = jnp.where(upper_side, mid_dv[half_rows:], mid_dv[:half_rows])
        send_k = jnp.where(upper_side, mid_dk[:half_rows], mid_dk[half_rows:])
        send_v = jnp.where(upper_side, mid_dv[:half_rows], mid_dv[half_rows:])
        received = (
            swapped(send_k.astype(jnp.bfloat16), "ctx", level_bit).astype(send_k.dtype),
            swapped(send_v.astype(jnp.bfloat16), "ctx", level_bit).astype(send_v.dtype),
        )
        mid_dk = keep_k + received[0]
        mid_dv = keep_v + received[1]
    mid_dk = mid_dk.reshape(-1, head_count, HEAD_DIM)
    mid_dv = mid_dv.reshape(-1, head_count, HEAD_DIM)
    top_sel = pick_rows(top_share[..., None], ctx_size, top_shift)[..., 0]
    top_low = (top_sel[..., None] * pick_rows(grad_attn, ctx_size, top_shift)).astype(jnp.bfloat16)
    top_row_shift = -(top_sel * pick_rows(inner[..., None], ctx_size, top_shift)[..., 0])
    top_grad, top_soft = score_grads(top_q, top_keys, top_vals, top_total, top_low, top_row_shift)
    top_dq = query_part(top_grad, top_keys)
    gathered_dk, gathered_dv = key_parts(top_grad, top_soft, top_q, top_low)
    summed = (
        lax.psum_scatter(
            gathered_dk.reshape(-1, flat_width), "ctx", scatter_dimension=0, tiled=True
        ),
        lax.psum_scatter(
            gathered_dv.reshape(-1, flat_width), "ctx", scatter_dimension=0, tiled=True
        ),
    )
    top_dk = summed[0].reshape(-1, head_count, HEAD_DIM)
    top_dv = summed[1].reshape(-1, head_count, HEAD_DIM)
    query_grad = (
        base_dq + place_rows(mid_dq, R1, mid_shift) + place_rows(top_dq, ctx_size, top_shift)
    )
    key_grad = base_dk + place_rows(mid_dk, R1, mid_shift) + place_rows(top_dk, ctx_size, top_shift)
    value_grad = (
        base_dv + place_rows(mid_dv, R1, mid_shift) + place_rows(top_dv, ctx_size, top_shift)
    )
    out_shape = (1, tokens, flat_width)
    return (
        attended,
        query_grad.astype(jnp.bfloat16).reshape(out_shape),
        key_grad.astype(jnp.bfloat16).reshape(out_shape),
        value_grad.astype(jnp.bfloat16).reshape(out_shape),
        gain_grad,
    )


VMEM_SPEC = pl.BlockSpec(memory_space=pltpu.VMEM)
SMEM_SPEC = pl.BlockSpec(memory_space=pltpu.SMEM)


def contract(left, right, left_dim, right_dim):
    return lax.dot_general(
        left, right, (((left_dim,), (right_dim,)), ((), ())), preferred_element_type=jnp.float32
    )


def pick_matrix(offsets_ref, head, top_rows, mid_rows, tokens, top_step):
    shape = (top_rows + mid_rows, tokens)
    row = lax.broadcasted_iota(jnp.int32, shape, 0)
    position = lax.broadcasted_iota(jnp.int32, shape, 1)
    wanted = jnp.where(
        row < top_rows,
        row * top_step + offsets_ref[1, head],
        (row - top_rows) * R1 + offsets_ref[0, head],
    )
    return jnp.where(position == wanted, 1.0, 0.0).astype(jnp.bfloat16)


def pack_kernel(top_step, offsets_ref, k_ref, v_ref, packed_ref):
    tokens = k_ref.shape[1]
    top_rows, mid_rows = tokens // top_step, tokens // R1
    picked = top_rows + mid_rows
    for head in range(k_ref.shape[2] // HEAD_DIM):
        cols = pl.ds(head * HEAD_DIM, HEAD_DIM)
        picks = pick_matrix(offsets_ref, head, top_rows, mid_rows, tokens, top_step)
        packed_ref[:picked, cols] = contract(picks, k_ref[0, :, cols], 1, 0).astype(jnp.bfloat16)
        packed_ref[picked:, cols] = contract(picks, v_ref[0, :, cols], 1, 0).astype(jnp.bfloat16)


def attend_kernel(
    top_step,
    offsets_ref,
    q_ref,
    k_ref,
    v_ref,
    grad_ref,
    gain_ref,
    *refs,
):
    packed_refs = refs[:SPAN]
    attended_ref, dq_ref, dk_ref, dv_ref, gain_part_ref = refs[SPAN : SPAN + 5]
    part_refs = refs[SPAN + 5 :]
    tokens = q_ref.shape[1]
    top_rows, mid_rows = tokens // top_step, tokens // R1
    picked = top_rows + mid_rows
    key_count = tokens + SPAN * picked
    score_scale = 1.0 / math.sqrt(HEAD_DIM)
    row = lax.broadcasted_iota(jnp.int32, (tokens, 1), 0)
    column = lax.broadcasted_iota(jnp.int32, (1, key_count), 1)
    is_base = column < tokens
    is_top = (column - tokens) % picked < top_rows
    for head in range(q_ref.shape[2] // HEAD_DIM):
        cols = pl.ds(head * HEAD_DIM, HEAD_DIM)
        q_rows = q_ref[0, :, cols]
        k_all = jnp.concatenate(
            [k_ref[0, :, cols]] + [packed[:picked, cols] for packed in packed_refs], 0
        )
        v_all = jnp.concatenate(
            [v_ref[0, :, cols]] + [packed[picked:, cols] for packed in packed_refs], 0
        )
        top_hit = jnp.where(row % top_step == offsets_ref[1, head], 1.0, 0.0)
        mid_hit = jnp.where(row % R1 == offsets_ref[0, head], 1.0, 0.0)
        seen = jnp.where(is_base, 1.0, jnp.where(is_top, top_hit, mid_hit))
        scores = jnp.where(seen > 0.5, contract(q_rows, k_all, 1, 1) * score_scale, -1e30)
        expo = jnp.exp(scores - jnp.max(scores, axis=1, keepdims=True))
        soft = expo / jnp.sum(expo, axis=1, keepdims=True)
        soft_low = soft.astype(jnp.bfloat16)
        attn = contract(soft_low, v_all, 1, 0)
        inv_rms = lax.rsqrt(jnp.mean(attn * attn, axis=1, keepdims=True) + EPS)
        normed = attn * inv_rms
        gain_row = gain_ref[:, cols]
        attended_ref[0, :, cols] = (normed * gain_row).astype(jnp.bfloat16)
        grad_rows = grad_ref[0, :, cols].astype(jnp.float32)
        gain_part_ref[:, cols] = jnp.sum(grad_rows * normed, axis=0, keepdims=True)
        grad_norm = grad_rows * gain_row
        grad_attn = inv_rms * (
            grad_norm - normed * jnp.mean(grad_norm * normed, axis=1, keepdims=True)
        )
        inner = jnp.sum(grad_attn * attn, axis=1, keepdims=True)
        grad_low = grad_attn.astype(jnp.bfloat16)
        prob_grad = contract(grad_low, v_all, 1, 1)
        score_grad = (soft * (prob_grad - inner) * score_scale).astype(jnp.bfloat16)
        dq_ref[0, :, cols] = contract(score_grad, k_all, 1, 0).astype(jnp.bfloat16)
        dk_all = contract(score_grad, q_rows, 0, 0)
        dv_all = contract(soft_low, grad_low, 0, 0)
        dk_ref[:, cols] = dk_all[:tokens]
        dv_ref[:, cols] = dv_all[:tokens]
        for place, part_ref in enumerate(part_refs):
            start = tokens + place * picked
            part_ref[:picked, cols] = dk_all[start : start + picked].astype(part_ref.dtype)
            part_ref[picked:, cols] = dv_all[start : start + picked].astype(part_ref.dtype)


def finish_kernel(top_step, offsets_ref, dk_ref, dv_ref, *refs):
    part_refs = refs[:SPAN]
    gain_refs = refs[SPAN : 2 * SPAN]
    dk_out_ref, dv_out_ref, gain_out_ref = refs[2 * SPAN :]
    tokens = dk_ref.shape[0]
    top_rows, mid_rows = tokens // top_step, tokens // R1
    picked = top_rows + mid_rows
    first, second, third, fourth = [gain_ref[...] for gain_ref in gain_refs]
    gain_out_ref[...] = (first + second) + (third + fourth)
    for head in range(dk_ref.shape[1] // HEAD_DIM):
        cols = pl.ds(head * HEAD_DIM, HEAD_DIM)
        picks = pick_matrix(offsets_ref, head, top_rows, mid_rows, tokens, top_step)
        total = part_refs[0][:, cols]
        for part_ref in part_refs[1:]:
            total = total + part_ref[:, cols].astype(jnp.float32)
        total = total.astype(jnp.bfloat16)
        dk_out_ref[0, :, cols] = (
            dk_ref[:, cols] + contract(picks, total[:picked], 0, 0)
        ).astype(jnp.bfloat16)
        dv_out_ref[0, :, cols] = (
            dv_ref[:, cols] + contract(picks, total[picked:], 0, 0)
        ).astype(jnp.bfloat16)


def across(block, axis, distance):
    route = [(place, place ^ distance) for place in range(lax.axis_size(axis))]
    return lax.ppermute(block, axis, route)


def one_segment_shards(queries, keys, values, grad_y, out_gain, offsets):
    tokens, width = queries.shape[1:]
    top_step = lax.axis_size("ctx")
    packed_rows = 2 * (tokens // top_step + tokens // R1)
    row_block = jax.ShapeDtypeStruct((1, tokens, width), jnp.bfloat16)
    wide_block = jax.ShapeDtypeStruct((tokens, width), jnp.float32)
    low_part = jax.ShapeDtypeStruct((packed_rows, width), jnp.bfloat16)
    own_part = jax.ShapeDtypeStruct((packed_rows, width), jnp.float32)
    gain_row = jax.ShapeDtypeStruct((1, width), jnp.float32)
    distances = range(1, SPAN)
    packed = pl.pallas_call(
        functools.partial(pack_kernel, top_step),
        out_shape=low_part,
        in_specs=[SMEM_SPEC, VMEM_SPEC, VMEM_SPEC],
        out_specs=VMEM_SPEC,
        name="pack",
    )(offsets, keys, values)
    received = {distance: across(packed, "ctx", distance) for distance in reversed(distances)}
    attended, query_grad, dk_base, dv_base, gain_part, own, *parts = pl.pallas_call(
        functools.partial(attend_kernel, top_step),
        out_shape=[row_block, row_block, wide_block, wide_block, gain_row, own_part]
        + [low_part] * (SPAN - 1),
        in_specs=[SMEM_SPEC] + [VMEM_SPEC] * (5 + SPAN),
        out_specs=[VMEM_SPEC] * (5 + SPAN),
        compiler_params=pltpu.CompilerParams(vmem_limit_bytes=32 * 1024 * 1024),
        name="attend",
    )(
        offsets,
        queries,
        keys,
        values,
        grad_y,
        out_gain.reshape(1, width),
        packed,
        *[received[distance] for distance in distances],
    )
    returned = {
        distance: across(parts[distance - 1], "ctx", distance) for distance in reversed(distances)
    }
    gain_pair = gain_part + across(gain_part, "dp", 1)
    gains = [gain_pair] + [across(gain_pair, "ctx", distance) for distance in distances]
    key_grad, value_grad, gain_grad = pl.pallas_call(
        functools.partial(finish_kernel, top_step),
        out_shape=[row_block, row_block, gain_row],
        in_specs=[SMEM_SPEC] + [VMEM_SPEC] * (2 + 2 * SPAN),
        out_specs=[VMEM_SPEC] * 3,
        compiler_params=pltpu.CompilerParams(vmem_limit_bytes=32 * 1024 * 1024),
        name="finish",
    )(
        offsets,
        dk_base,
        dv_base,
        own,
        *[returned[distance] for distance in distances],
        *gains,
    )
    return attended, query_grad, key_grad, value_grad, gain_grad.reshape(width)


def solution(mesh):
    in_specs = (
        P("dp", "ctx", "head"),
        P("dp", "ctx", "head"),
        P("dp", "ctx", "head"),
        P("dp", "ctx", "head"),
        P("head"),
        P(None, "head"),
    )
    out_specs = (
        P("dp", "ctx", "head"),
        P("dp", "ctx", "head"),
        P("dp", "ctx", "head"),
        P("dp", "ctx", "head"),
        P("head"),
    )
    body = one_segment_shards if mesh.shape["ctx"] == SPAN else general_shards
    return jax.shard_map(body, mesh=mesh, in_specs=in_specs, out_specs=out_specs, check_vma=False)
```

```python
import functools
import math

import jax
import jax.numpy as jnp
from jax import lax
from jax.experimental import pallas as pl
from jax.experimental.pallas import tpu as pltpu
from jax.sharding import PartitionSpec as P

HEAD_DIM = 128
SPAN = 4
R1 = 8


EPS = 1e-06


def swapped(block, axis, bit):
    count = lax.axis_size(axis)
    route = []
    for low in range(count):
        high = low | 1 << bit
        if high != low and high < count:
            route += [(low, high), (high, low)]
    return lax.ppermute(block, axis, route)


def pick_rows(source_rows, dilation, shifts):
    row_count, head_count, head_width = source_rows.shape
    grouped = source_rows.reshape(row_count // dilation, dilation, head_count, head_width)
    hit_mask = jnp.arange(dilation, dtype=jnp.int32).reshape(1, dilation, 1, 1) == shifts.reshape(
        1, 1, head_count, 1
    )
    chosen = jnp.where(hit_mask, grouped, jnp.zeros((), source_rows.dtype))
    return jnp.sum(chosen, axis=1, dtype=source_rows.dtype)


def place_rows(row_values, dilation, shifts):
    row_count, head_count, head_width = row_values.shape
    hit_mask = jnp.arange(dilation, dtype=jnp.int32).reshape(1, dilation, 1, 1) == shifts.reshape(
        1, 1, head_count, 1
    )
    spread = jnp.where(hit_mask, row_values[:, None], jnp.zeros((), row_values.dtype))
    return spread.reshape(row_count * dilation, head_count, head_width)


def level_scores(q_rows, k_rows):
    score_scale = 1.0 / math.sqrt(q_rows.shape[-1])
    return (
        jnp.einsum("qhe,khe->hqk", q_rows, k_rows, preferred_element_type=jnp.float32) * score_scale
    )


def attend(q_rows, k_rows, v_rows):
    scores = level_scores(q_rows, k_rows)
    row_max = jnp.max(scores, axis=-1, keepdims=True)
    log_total = row_max[..., 0] + jnp.log(jnp.sum(jnp.exp(scores - row_max), axis=-1))
    soft_rows = jnp.exp(scores - log_total[..., None]).astype(jnp.bfloat16)
    level_out = jnp.einsum("hqk,khe->qhe", soft_rows, v_rows, preferred_element_type=jnp.float32)
    return (level_out, log_total.T)


def score_grads(q_rows, k_rows, v_rows, log_total, grad_low, row_shift):
    score_scale = 1.0 / math.sqrt(q_rows.shape[-1])
    scores = level_scores(q_rows, k_rows)
    exact_soft = jnp.exp(scores - log_total.T[..., None])
    prob_grad = jnp.einsum("qhe,khe->hqk", grad_low, v_rows, preferred_element_type=jnp.float32)
    score_grad = (exact_soft * (prob_grad + row_shift.T[..., None]) * score_scale).astype(
        jnp.bfloat16
    )
    return (score_grad, exact_soft.astype(jnp.bfloat16))


def key_parts(score_grad, soft_low, q_rows, grad_low):
    k_part = jnp.einsum("hqk,qhe->khe", score_grad, q_rows, preferred_element_type=jnp.float32)
    v_part = jnp.einsum("hqk,qhe->khe", soft_low, grad_low, preferred_element_type=jnp.float32)
    return (k_part, v_part)


def query_part(score_grad, k_rows):
    return jnp.einsum("hqk,khe->qhe", score_grad, k_rows, preferred_element_type=jnp.float32)


def general_shards(queries, keys, values, grad_y, out_gain, offsets):
    tokens = queries.shape[1]
    flat_width = queries.shape[2]
    head_count = flat_width // HEAD_DIM
    row_shape = (tokens, head_count, HEAD_DIM)
    q_own = queries[0].reshape(row_shape)
    k_own = keys[0].reshape(row_shape)
    v_own = values[0].reshape(row_shape)
    ctx_size = lax.axis_size("ctx")
    span_bits = SPAN.bit_length() - 1
    my_place = lax.axis_index("ctx")
    mid_shift = offsets[0]
    top_shift = offsets[1]
    positions = jnp.arange(tokens, dtype=jnp.int32)
    mid_hit = (positions % R1)[:, None] == mid_shift[None, :]
    top_hit = (positions % ctx_size)[:, None] == top_shift[None, :]
    mid_q = pick_rows(q_own, R1, mid_shift)
    mid_k = pick_rows(k_own, R1, mid_shift)
    mid_v = pick_rows(v_own, R1, mid_shift)
    top_q = pick_rows(q_own, ctx_size, top_shift)
    top_k = pick_rows(k_own, ctx_size, top_shift)
    top_v = pick_rows(v_own, ctx_size, top_shift)
    mid_keys = mid_k.reshape(-1, flat_width)
    mid_vals = mid_v.reshape(-1, flat_width)
    top_keys = top_k.reshape(-1, flat_width)
    top_vals = top_v.reshape(-1, flat_width)

    def append_peer(mine, received, level_bit):
        upper_side = my_place >> level_bit & 1 == 1
        return jnp.where(
            upper_side, jnp.concatenate([received, mine], 0), jnp.concatenate([mine, received], 0)
        )

    for level_bit in range(span_bits):
        received = swapped((mid_keys, mid_vals), "ctx", level_bit)
        mid_keys = append_peer(mid_keys, received[0], level_bit)
        mid_vals = append_peer(mid_vals, received[1], level_bit)
    top_keys, top_vals = (
        lax.all_gather(top_keys, "ctx", axis=0, tiled=True),
        lax.all_gather(top_vals, "ctx", axis=0, tiled=True),
    )
    mid_keys = mid_keys.reshape(-1, head_count, HEAD_DIM)
    mid_vals = mid_vals.reshape(-1, head_count, HEAD_DIM)
    top_keys = top_keys.reshape(-1, head_count, HEAD_DIM)
    top_vals = top_vals.reshape(-1, head_count, HEAD_DIM)
    base_out, base_total = attend(q_own, k_own, v_own)
    mid_out, mid_total = attend(mid_q, mid_keys, mid_vals)
    top_out, top_total = attend(top_q, top_keys, top_vals)
    mid_full = place_rows(mid_total[..., None], R1, mid_shift)[..., 0]
    top_full = place_rows(top_total[..., None], ctx_size, top_shift)[..., 0]
    row_max = jnp.maximum(base_total, jnp.where(mid_hit, mid_full, base_total))
    row_max = jnp.maximum(row_max, jnp.where(top_hit, top_full, base_total))
    base_expo = jnp.exp(base_total - row_max)
    mid_expo = jnp.where(mid_hit, jnp.exp(mid_full - row_max), 0.0)
    top_expo = jnp.where(top_hit, jnp.exp(top_full - row_max), 0.0)
    denom = base_expo + mid_expo + top_expo
    base_share = base_expo / denom
    mid_share = mid_expo / denom
    top_share = top_expo / denom
    attn = (
        base_share[..., None] * base_out
        + mid_share[..., None] * place_rows(mid_out, R1, mid_shift)
        + top_share[..., None] * place_rows(top_out, ctx_size, top_shift)
    )
    inv_rms = lax.rsqrt(jnp.mean(attn * attn, axis=-1, keepdims=True) + EPS)
    normed = attn * inv_rms
    gain_rows = out_gain.reshape(head_count, HEAD_DIM)
    attended = (normed * gain_rows).astype(jnp.bfloat16).reshape(1, tokens, flat_width)
    grad_full = grad_y[0].reshape(row_shape).astype(jnp.float32)
    gain_part = jnp.sum(grad_full * normed, axis=0).reshape(flat_width)
    gain_grad = lax.psum(gain_part, ("dp", "ctx"))
    grad_norm = grad_full * gain_rows
    grad_attn = inv_rms * (
        grad_norm - normed * jnp.mean(grad_norm * normed, axis=-1, keepdims=True)
    )
    inner = jnp.sum(grad_attn * attn, axis=-1)
    base_low = (base_share[..., None] * grad_attn).astype(jnp.bfloat16)
    base_shift = -(base_share * inner)
    base_grad, base_soft = score_grads(q_own, k_own, v_own, base_total, base_low, base_shift)
    base_dq = query_part(base_grad, k_own)
    base_dk, base_dv = key_parts(base_grad, base_soft, q_own, base_low)
    mid_sel = pick_rows(mid_share[..., None], R1, mid_shift)[..., 0]
    mid_low = (mid_sel[..., None] * pick_rows(grad_attn, R1, mid_shift)).astype(jnp.bfloat16)
    mid_row_shift = -(mid_sel * pick_rows(inner[..., None], R1, mid_shift)[..., 0])
    mid_grad, mid_soft = score_grads(mid_q, mid_keys, mid_vals, mid_total, mid_low, mid_row_shift)
    mid_dq = query_part(mid_grad, mid_keys)
    mid_dk, mid_dv = key_parts(mid_grad, mid_soft, mid_q, mid_low)
    mid_dk = mid_dk.reshape(-1, flat_width)
    mid_dv = mid_dv.reshape(-1, flat_width)
    for level_bit in reversed(range(span_bits)):
        half_rows = mid_dk.shape[0] // 2
        upper_side = my_place >> level_bit & 1 == 1
        keep_k = jnp.where(upper_side, mid_dk[half_rows:], mid_dk[:half_rows])
        keep_v = jnp.where(upper_side, mid_dv[half_rows:], mid_dv[:half_rows])
        send_k = jnp.where(upper_side, mid_dk[:half_rows], mid_dk[half_rows:])
        send_v = jnp.where(upper_side, mid_dv[:half_rows], mid_dv[half_rows:])
        received = (
            swapped(send_k.astype(jnp.bfloat16), "ctx", level_bit).astype(send_k.dtype),
            swapped(send_v.astype(jnp.bfloat16), "ctx", level_bit).astype(send_v.dtype),
        )
        mid_dk = keep_k + received[0]
        mid_dv = keep_v + received[1]
    mid_dk = mid_dk.reshape(-1, head_count, HEAD_DIM)
    mid_dv = mid_dv.reshape(-1, head_count, HEAD_DIM)
    top_sel = pick_rows(top_share[..., None], ctx_size, top_shift)[..., 0]
    top_low = (top_sel[..., None] * pick_rows(grad_attn, ctx_size, top_shift)).astype(jnp.bfloat16)
    top_row_shift = -(top_sel * pick_rows(inner[..., None], ctx_size, top_shift)[..., 0])
    top_grad, top_soft = score_grads(top_q, top_keys, top_vals, top_total, top_low, top_row_shift)
    top_dq = query_part(top_grad, top_keys)
    gathered_dk, gathered_dv = key_parts(top_grad, top_soft, top_q, top_low)
    summed = (
        lax.psum_scatter(
            gathered_dk.reshape(-1, flat_width), "ctx", scatter_dimension=0, tiled=True
        ),
        lax.psum_scatter(
            gathered_dv.reshape(-1, flat_width), "ctx", scatter_dimension=0, tiled=True
        ),
    )
    top_dk = summed[0].reshape(-1, head_count, HEAD_DIM)
    top_dv = summed[1].reshape(-1, head_count, HEAD_DIM)
    query_grad = (
        base_dq + place_rows(mid_dq, R1, mid_shift) + place_rows(top_dq, ctx_size, top_shift)
    )
    key_grad = base_dk + place_rows(mid_dk, R1, mid_shift) + place_rows(top_dk, ctx_size, top_shift)
    value_grad = (
        base_dv + place_rows(mid_dv, R1, mid_shift) + place_rows(top_dv, ctx_size, top_shift)
    )
    out_shape = (1, tokens, flat_width)
    return (
        attended,
        query_grad.astype(jnp.bfloat16).reshape(out_shape),
        key_grad.astype(jnp.bfloat16).reshape(out_shape),
        value_grad.astype(jnp.bfloat16).reshape(out_shape),
        gain_grad,
    )


VMEM_SPEC = pl.BlockSpec(memory_space=pltpu.VMEM)
SMEM_SPEC = pl.BlockSpec(memory_space=pltpu.SMEM)
LANES = 128
PIECES = 3
LOW = jnp.bfloat16
WIDE = jnp.float32


def contract(left, right, left_dim, right_dim):
    return lax.dot_general(
        left, right, (((left_dim,), (right_dim,)), ((), ())), preferred_element_type=WIDE
    )


def head_cols(head):
    return pl.ds(head * HEAD_DIM, HEAD_DIM)


def picked_counts(tokens, top_step):
    return tokens // top_step, tokens // R1


def pick_matrix(offsets_ref, head, tokens, top_step):
    top_rows, mid_rows = picked_counts(tokens, top_step)
    shape = (top_rows + mid_rows, tokens)
    row = lax.broadcasted_iota(jnp.int32, shape, 0)
    position = lax.broadcasted_iota(jnp.int32, shape, 1)
    wanted = jnp.where(
        row < top_rows,
        row * top_step + offsets_ref[1, head],
        (row - top_rows) * R1 + offsets_ref[0, head],
    )
    return jnp.where(position == wanted, 1.0, 0.0).astype(LOW)


def level_hits(offsets_ref, head, shape, axis, top_step):
    position = lax.broadcasted_iota(jnp.int32, shape, axis)
    top_hit = jnp.where(position % top_step == offsets_ref[1, head], 1.0, 0.0)
    mid_hit = jnp.where(position % R1 == offsets_ref[0, head], 1.0, 0.0)
    return top_hit, mid_hit


def picked_mask(offsets_ref, head, tokens, top_step, picked_total):
    top_rows, mid_rows = picked_counts(tokens, top_step)
    top_hit, mid_hit = level_hits(offsets_ref, head, (tokens, 1), 0, top_step)
    column = lax.broadcasted_iota(jnp.int32, (1, picked_total), 1)
    return jnp.where(column % (top_rows + mid_rows) < top_rows, top_hit, mid_hit) > 0.5


def stacked(refs, rows, cols):
    return jnp.concatenate([ref[rows, cols] for ref in refs], 0)


def pack_kernel(top_step, offsets_ref, k_ref, v_ref, packed_ref):
    tokens, width = k_ref.shape[1:]
    picked = sum(picked_counts(tokens, top_step))
    for head in range(width // HEAD_DIM):
        cols = head_cols(head)
        both = jnp.concatenate([k_ref[0, :, cols], v_ref[0, :, cols]], 1)
        rows = contract(pick_matrix(offsets_ref, head, tokens, top_step), both, 1, 0).astype(LOW)
        packed_ref[:picked, cols] = rows[:, :HEAD_DIM]
        packed_ref[picked:, cols] = rows[:, HEAD_DIM:]


def base_kernel(
    top_step, offsets_ref, q_ref, k_ref, v_ref, picked_q_ref, expo_ref, out_ref, stats_ref
):
    tokens, width = q_ref.shape[1:]
    heads = width // HEAD_DIM
    score_scale = 1.0 / math.sqrt(HEAD_DIM)
    for head in range(heads):
        cols = head_cols(head)
        q_rows = q_ref[0, :, cols]
        picks = pick_matrix(offsets_ref, head, tokens, top_step)
        picked_q_ref[:, cols] = contract(picks, q_rows, 1, 0).astype(LOW)
        top_row, mid_row = level_hits(offsets_ref, head, (tokens, 1), 0, top_step)
        top_col, mid_col = level_hits(offsets_ref, head, (1, tokens), 1, top_step)
        times = 1.0 + top_row * top_col + mid_row * mid_col
        scores = contract(q_rows, k_ref[0, :, cols], 1, 1) * score_scale
        row_max = jnp.max(scores, axis=1, keepdims=True)
        expo = times * jnp.exp(scores - row_max)
        expo_low = expo.astype(LOW)
        expo_ref[:, cols] = expo_low
        out_ref[:, cols] = contract(expo_low, v_ref[0, :, cols], 1, 0)
        stats_ref[:, head : head + 1] = row_max
        stats_ref[:, heads + head : heads + head + 1] = jnp.sum(expo, axis=1, keepdims=True)


def low_pieces(values):
    pieces = []
    for _ in range(PIECES):
        piece = values.astype(LOW).astype(WIDE)
        pieces.append(piece)
        values = values - piece
    return pieces


def attend_kernel(
    top_step,
    offsets_ref,
    q_ref,
    grad_ref,
    gain_ref,
    base_out_ref,
    base_stats_ref,
    *refs,
):
    peers = SPAN - 1
    packed_refs = refs[:peers]
    attended_ref, gain_part_ref, sent_ref, grad_low_ref, soft_ref, stats_ref = refs[peers:]
    tokens, width = q_ref.shape[1:]
    heads = width // HEAD_DIM
    picked = sum(picked_counts(tokens, top_step))
    score_scale = 1.0 / math.sqrt(HEAD_DIM)
    lane = lax.broadcasted_iota(jnp.int32, (1, LANES), 1)
    sent_stats = jnp.zeros((picked, LANES), WIDE)
    for head in range(heads):
        cols = head_cols(head)
        k_peers = stacked(packed_refs, pl.ds(0, picked), cols)
        v_peers = stacked(packed_refs, pl.ds(picked, picked), cols)
        seen = picked_mask(offsets_ref, head, tokens, top_step, peers * picked)
        scores = contract(q_ref[0, :, cols], k_peers, 1, 1) * score_scale
        scores = jnp.where(seen, scores, -1e30)
        base_max = base_stats_ref[:, head : head + 1]
        base_total = base_stats_ref[:, heads + head : heads + head + 1]
        row_max = jnp.maximum(base_max, jnp.max(scores, axis=1, keepdims=True))
        base_factor = jnp.exp(base_max - row_max)
        expo = jnp.exp(scores - row_max)
        total = base_factor * base_total + jnp.sum(expo, axis=1, keepdims=True)
        inv_total = 1.0 / total
        soft_low = (expo * inv_total).astype(LOW)
        soft_ref[:, pl.ds(head * 2 * LANES, peers * picked)] = soft_low
        base_factor = base_factor * inv_total
        attn = base_factor * base_out_ref[:, cols] + contract(soft_low, v_peers, 1, 0)
        inv_rms = lax.rsqrt(jnp.mean(attn * attn, axis=1, keepdims=True) + EPS)
        normed = attn * inv_rms
        gain_row = gain_ref[:, cols]
        attended_ref[0, :, cols] = (normed * gain_row).astype(LOW)
        grad_rows = grad_ref[0, :, cols].astype(WIDE)
        gain_part_ref[:, cols] = jnp.sum(grad_rows * normed, axis=0, keepdims=True)
        grad_norm = grad_rows * gain_row
        grad_attn = inv_rms * (
            grad_norm - normed * jnp.mean(grad_norm * normed, axis=1, keepdims=True)
        )
        inner = jnp.sum(grad_attn * attn, axis=1, keepdims=True)
        grad_low = grad_attn.astype(LOW)
        grad_low_ref[:, cols] = grad_low
        stats_ref[:, head : head + 1] = base_factor
        stats_ref[:, heads + head : heads + head + 1] = inner
        log_total = (row_max + jnp.log(total)) * (1.0 / score_scale)
        columns = jnp.zeros((tokens, LANES), WIDE)
        for place, piece in enumerate(low_pieces(log_total) + low_pieces(inner)):
            columns = jnp.where(lane == 2 * PIECES * head + place, piece, columns)
        picks = pick_matrix(offsets_ref, head, tokens, top_step)
        rows = contract(picks, jnp.concatenate([grad_low, columns.astype(LOW)], 1), 1, 0)
        sent_ref[:, cols] = rows[:, :HEAD_DIM].astype(LOW)
        sent_stats = sent_stats + rows[:, HEAD_DIM:]
    sent_ref[:, pl.ds(width, LANES)] = sent_stats.astype(LOW)


def local_grad_kernel(
    top_step, q_ref, k_ref, v_ref, expo_ref, grad_low_ref, soft_ref, stats_ref, *refs
):
    peers = SPAN - 1
    packed_refs = refs[:peers]
    dq_ref, dk_ref, dv_ref = refs[peers:]
    tokens, width = q_ref.shape[1:]
    heads = width // HEAD_DIM
    picked = sum(picked_counts(tokens, top_step))
    score_scale = 1.0 / math.sqrt(HEAD_DIM)
    for head in range(heads):
        cols = head_cols(head)
        k_rows = k_ref[0, :, cols]
        k_peers = stacked(packed_refs, pl.ds(0, picked), cols)
        v_peers = stacked(packed_refs, pl.ds(picked, picked), cols)
        grad_low = grad_low_ref[:, cols]
        inner = stats_ref[:, heads + head : heads + head + 1]
        soft = expo_ref[:, cols].astype(WIDE) * stats_ref[:, head : head + 1]
        prob_grad = contract(grad_low, v_ref[0, :, cols], 1, 1)
        score_grad = (soft * (prob_grad - inner) * score_scale).astype(LOW)
        peer_soft = soft_ref[:, pl.ds(head * 2 * LANES, peers * picked)].astype(WIDE)
        peer_prob_grad = contract(grad_low, v_peers, 1, 1)
        peer_score_grad = (peer_soft * (peer_prob_grad - inner) * score_scale).astype(LOW)
        dq_ref[0, :, cols] = (
            contract(score_grad, k_rows, 1, 0) + contract(peer_score_grad, k_peers, 1, 0)
        ).astype(LOW)
        dk_ref[:, cols] = contract(score_grad, q_ref[0, :, cols], 0, 0)
        dv_ref[:, cols] = contract(soft.astype(LOW), grad_low, 0, 0)


def finish_kernel(top_step, offsets_ref, k_ref, v_ref, dk_ref, dv_ref, *refs):
    peers = SPAN - 1
    q_refs, sent_refs = refs[:peers], refs[peers : 2 * peers]
    dk_out_ref, dv_out_ref = refs[2 * peers :]
    tokens, width = k_ref.shape[1:]
    picked = sum(picked_counts(tokens, top_step))
    score_scale = 1.0 / math.sqrt(HEAD_DIM)
    every = pl.ds(0, picked)
    stats = stacked(sent_refs, every, pl.ds(width, LANES))
    lane = lax.broadcasted_iota(jnp.int32, (tokens, LANES), 1)
    for head in range(width // HEAD_DIM):
        cols = head_cols(head)
        q_peers = stacked(q_refs, every, cols)
        grad_peers = stacked(sent_refs, every, cols)
        first = 2 * PIECES * head
        is_total = (lane >= first) & (lane < first + PIECES)
        is_inner = (lane >= first + PIECES) & (lane < first + 2 * PIECES)
        less_total = jnp.where(is_total, -1.0, 0.0).astype(LOW)
        less_inner = jnp.where(is_inner, -1.0, 0.0).astype(LOW)
        seen = picked_mask(offsets_ref, head, tokens, top_step, peers * picked)
        logs = contract(
            jnp.concatenate([k_ref[0, :, cols], less_total], 1),
            jnp.concatenate([q_peers, stats], 1),
            1,
            1,
        )
        soft = jnp.exp(jnp.where(seen, logs * score_scale, -1e30))
        shifted = contract(
            jnp.concatenate([v_ref[0, :, cols], less_inner], 1),
            jnp.concatenate([grad_peers, stats], 1),
            1,
            1,
        )
        score_grad = (soft * shifted * score_scale).astype(LOW)
        dk_out_ref[0, :, cols] = (
            dk_ref[:, cols] + contract(score_grad, q_peers, 1, 0)
        ).astype(LOW)
        dv_out_ref[0, :, cols] = (
            dv_ref[:, cols] + contract(soft.astype(LOW), grad_peers, 1, 0)
        ).astype(LOW)


def across(block, axis, distance):
    route = [(place, place ^ distance) for place in range(lax.axis_size(axis))]
    return lax.ppermute(block, axis, route)


def to_peers(block):
    farthest_first = [across(block, "ctx", distance) for distance in range(SPAN - 1, 0, -1)]
    return farthest_first[::-1]


def call(kernel, name, operands, results, microseconds):
    return pl.pallas_call(
        kernel,
        out_shape=results,
        in_specs=[SMEM_SPEC if block.dtype == jnp.int32 else VMEM_SPEC for block in operands],
        out_specs=[VMEM_SPEC] * len(results),
        compiler_params=pltpu.CompilerParams(vmem_limit_bytes=16 * 1024 * 1024),
        cost_estimate=pl.CostEstimate(
            flops=microseconds * 10**9, bytes_accessed=10**6, transcendentals=0
        ),
        name=name,
    )(*operands)


def one_segment_shards(queries, keys, values, grad_y, out_gain, offsets):
    tokens, width = queries.shape[1:]
    heads = width // HEAD_DIM
    top_step = lax.axis_size("ctx")
    picked = sum(picked_counts(tokens, top_step))
    shape = jax.ShapeDtypeStruct
    row_block = shape((1, tokens, width), LOW)
    low_block = shape((tokens, width), LOW)
    wide_block = shape((tokens, width), WIDE)
    stats_block = shape((tokens, LANES), WIDE)
    bind = functools.partial
    (packed,) = call(
        bind(pack_kernel, top_step),
        "pack",
        (offsets, keys, values),
        [shape((2 * picked, width), LOW)],
        1,
    )
    packed_peers = to_peers(packed)
    picked_q, expo, base_out, base_stats = call(
        bind(base_kernel, top_step),
        "base",
        (offsets, queries, keys, values),
        [shape((picked, width), LOW), low_block, wide_block, stats_block],
        2,
    )
    q_peers = to_peers(picked_q)
    attended, gain_part, sent, grad_low, soft, stats = call(
        bind(attend_kernel, top_step),
        "attend",
        (
            offsets,
            queries,
            grad_y,
            out_gain.reshape(1, width),
            base_out,
            base_stats,
            *packed_peers,
        ),
        [
            row_block,
            shape((1, width), WIDE),
            shape((picked, width + LANES), LOW),
            low_block,
            shape((tokens, heads * 2 * LANES), LOW),
            stats_block,
        ],
        3,
    )
    sent_peers = to_peers(sent)
    gain_part = gain_part.reshape(width)
    gain_pair = gain_part + across(gain_part, "dp", 1)
    gain_peers = to_peers(gain_pair)
    gain_grad = (gain_pair + gain_peers[0]) + (gain_peers[1] + gain_peers[2])
    query_grad, dk_base, dv_base = call(
        bind(local_grad_kernel, top_step),
        "local_grad",
        (queries, keys, values, expo, grad_low, soft, stats, *packed_peers),
        [row_block, wide_block, wide_block],
        3,
    )
    key_grad, value_grad = call(
        bind(finish_kernel, top_step),
        "finish",
        (offsets, keys, values, dk_base, dv_base, *q_peers, *sent_peers),
        [row_block, row_block],
        2,
    )
    return attended, query_grad, key_grad, value_grad, gain_grad


def solution(mesh):
    in_specs = (
        P("dp", "ctx", "head"),
        P("dp", "ctx", "head"),
        P("dp", "ctx", "head"),
        P("dp", "ctx", "head"),
        P("head"),
        P(None, "head"),
    )
    out_specs = (
        P("dp", "ctx", "head"),
        P("dp", "ctx", "head"),
        P("dp", "ctx", "head"),
        P("dp", "ctx", "head"),
        P("head"),
    )
    body = one_segment_shards if mesh.shape["ctx"] == SPAN else general_shards
    return jax.shard_map(body, mesh=mesh, in_specs=in_specs, out_specs=out_specs, check_vma=False)
```

```python
import functools
import math

import jax
import jax.numpy as jnp
from jax import lax
from jax.experimental import pallas as pl
from jax.experimental.pallas import tpu as pltpu
from jax.sharding import PartitionSpec as P

HEAD_DIM = 128
SPAN = 4
R1 = 8


EPS = 1e-06


def swapped(block, axis, bit):
    count = lax.axis_size(axis)
    route = []
    for low in range(count):
        high = low | 1 << bit
        if high != low and high < count:
            route += [(low, high), (high, low)]
    return lax.ppermute(block, axis, route)


def pick_rows(source_rows, dilation, shifts):
    row_count, head_count, head_width = source_rows.shape
    grouped = source_rows.reshape(row_count // dilation, dilation, head_count, head_width)
    hit_mask = jnp.arange(dilation, dtype=jnp.int32).reshape(1, dilation, 1, 1) == shifts.reshape(
        1, 1, head_count, 1
    )
    chosen = jnp.where(hit_mask, grouped, jnp.zeros((), source_rows.dtype))
    return jnp.sum(chosen, axis=1, dtype=source_rows.dtype)


def place_rows(row_values, dilation, shifts):
    row_count, head_count, head_width = row_values.shape
    hit_mask = jnp.arange(dilation, dtype=jnp.int32).reshape(1, dilation, 1, 1) == shifts.reshape(
        1, 1, head_count, 1
    )
    spread = jnp.where(hit_mask, row_values[:, None], jnp.zeros((), row_values.dtype))
    return spread.reshape(row_count * dilation, head_count, head_width)


def level_scores(q_rows, k_rows):
    score_scale = 1.0 / math.sqrt(q_rows.shape[-1])
    return (
        jnp.einsum("qhe,khe->hqk", q_rows, k_rows, preferred_element_type=jnp.float32) * score_scale
    )


def attend(q_rows, k_rows, v_rows):
    scores = level_scores(q_rows, k_rows)
    row_max = jnp.max(scores, axis=-1, keepdims=True)
    log_total = row_max[..., 0] + jnp.log(jnp.sum(jnp.exp(scores - row_max), axis=-1))
    soft_rows = jnp.exp(scores - log_total[..., None]).astype(jnp.bfloat16)
    level_out = jnp.einsum("hqk,khe->qhe", soft_rows, v_rows, preferred_element_type=jnp.float32)
    return (level_out, log_total.T)


def score_grads(q_rows, k_rows, v_rows, log_total, grad_low, row_shift):
    score_scale = 1.0 / math.sqrt(q_rows.shape[-1])
    scores = level_scores(q_rows, k_rows)
    exact_soft = jnp.exp(scores - log_total.T[..., None])
    prob_grad = jnp.einsum("qhe,khe->hqk", grad_low, v_rows, preferred_element_type=jnp.float32)
    score_grad = (exact_soft * (prob_grad + row_shift.T[..., None]) * score_scale).astype(
        jnp.bfloat16
    )
    return (score_grad, exact_soft.astype(jnp.bfloat16))


def key_parts(score_grad, soft_low, q_rows, grad_low):
    k_part = jnp.einsum("hqk,qhe->khe", score_grad, q_rows, preferred_element_type=jnp.float32)
    v_part = jnp.einsum("hqk,qhe->khe", soft_low, grad_low, preferred_element_type=jnp.float32)
    return (k_part, v_part)


def query_part(score_grad, k_rows):
    return jnp.einsum("hqk,khe->qhe", score_grad, k_rows, preferred_element_type=jnp.float32)


def general_shards(queries, keys, values, grad_y, out_gain, offsets):
    tokens = queries.shape[1]
    flat_width = queries.shape[2]
    head_count = flat_width // HEAD_DIM
    row_shape = (tokens, head_count, HEAD_DIM)
    q_own = queries[0].reshape(row_shape)
    k_own = keys[0].reshape(row_shape)
    v_own = values[0].reshape(row_shape)
    ctx_size = lax.axis_size("ctx")
    span_bits = SPAN.bit_length() - 1
    my_place = lax.axis_index("ctx")
    mid_shift = offsets[0]
    top_shift = offsets[1]
    positions = jnp.arange(tokens, dtype=jnp.int32)
    mid_hit = (positions % R1)[:, None] == mid_shift[None, :]
    top_hit = (positions % ctx_size)[:, None] == top_shift[None, :]
    mid_q = pick_rows(q_own, R1, mid_shift)
    mid_k = pick_rows(k_own, R1, mid_shift)
    mid_v = pick_rows(v_own, R1, mid_shift)
    top_q = pick_rows(q_own, ctx_size, top_shift)
    top_k = pick_rows(k_own, ctx_size, top_shift)
    top_v = pick_rows(v_own, ctx_size, top_shift)
    mid_keys = mid_k.reshape(-1, flat_width)
    mid_vals = mid_v.reshape(-1, flat_width)
    top_keys = top_k.reshape(-1, flat_width)
    top_vals = top_v.reshape(-1, flat_width)

    def append_peer(mine, received, level_bit):
        upper_side = my_place >> level_bit & 1 == 1
        return jnp.where(
            upper_side, jnp.concatenate([received, mine], 0), jnp.concatenate([mine, received], 0)
        )

    for level_bit in range(span_bits):
        received = swapped((mid_keys, mid_vals), "ctx", level_bit)
        mid_keys = append_peer(mid_keys, received[0], level_bit)
        mid_vals = append_peer(mid_vals, received[1], level_bit)
    top_keys, top_vals = (
        lax.all_gather(top_keys, "ctx", axis=0, tiled=True),
        lax.all_gather(top_vals, "ctx", axis=0, tiled=True),
    )
    mid_keys = mid_keys.reshape(-1, head_count, HEAD_DIM)
    mid_vals = mid_vals.reshape(-1, head_count, HEAD_DIM)
    top_keys = top_keys.reshape(-1, head_count, HEAD_DIM)
    top_vals = top_vals.reshape(-1, head_count, HEAD_DIM)
    base_out, base_total = attend(q_own, k_own, v_own)
    mid_out, mid_total = attend(mid_q, mid_keys, mid_vals)
    top_out, top_total = attend(top_q, top_keys, top_vals)
    mid_full = place_rows(mid_total[..., None], R1, mid_shift)[..., 0]
    top_full = place_rows(top_total[..., None], ctx_size, top_shift)[..., 0]
    row_max = jnp.maximum(base_total, jnp.where(mid_hit, mid_full, base_total))
    row_max = jnp.maximum(row_max, jnp.where(top_hit, top_full, base_total))
    base_expo = jnp.exp(base_total - row_max)
    mid_expo = jnp.where(mid_hit, jnp.exp(mid_full - row_max), 0.0)
    top_expo = jnp.where(top_hit, jnp.exp(top_full - row_max), 0.0)
    denom = base_expo + mid_expo + top_expo
    base_share = base_expo / denom
    mid_share = mid_expo / denom
    top_share = top_expo / denom
    attn = (
        base_share[..., None] * base_out
        + mid_share[..., None] * place_rows(mid_out, R1, mid_shift)
        + top_share[..., None] * place_rows(top_out, ctx_size, top_shift)
    )
    inv_rms = lax.rsqrt(jnp.mean(attn * attn, axis=-1, keepdims=True) + EPS)
    normed = attn * inv_rms
    gain_rows = out_gain.reshape(head_count, HEAD_DIM)
    attended = (normed * gain_rows).astype(jnp.bfloat16).reshape(1, tokens, flat_width)
    grad_full = grad_y[0].reshape(row_shape).astype(jnp.float32)
    gain_part = jnp.sum(grad_full * normed, axis=0).reshape(flat_width)
    gain_grad = lax.psum(gain_part, ("dp", "ctx"))
    grad_norm = grad_full * gain_rows
    grad_attn = inv_rms * (
        grad_norm - normed * jnp.mean(grad_norm * normed, axis=-1, keepdims=True)
    )
    inner = jnp.sum(grad_attn * attn, axis=-1)
    base_low = (base_share[..., None] * grad_attn).astype(jnp.bfloat16)
    base_shift = -(base_share * inner)
    base_grad, base_soft = score_grads(q_own, k_own, v_own, base_total, base_low, base_shift)
    base_dq = query_part(base_grad, k_own)
    base_dk, base_dv = key_parts(base_grad, base_soft, q_own, base_low)
    mid_sel = pick_rows(mid_share[..., None], R1, mid_shift)[..., 0]
    mid_low = (mid_sel[..., None] * pick_rows(grad_attn, R1, mid_shift)).astype(jnp.bfloat16)
    mid_row_shift = -(mid_sel * pick_rows(inner[..., None], R1, mid_shift)[..., 0])
    mid_grad, mid_soft = score_grads(mid_q, mid_keys, mid_vals, mid_total, mid_low, mid_row_shift)
    mid_dq = query_part(mid_grad, mid_keys)
    mid_dk, mid_dv = key_parts(mid_grad, mid_soft, mid_q, mid_low)
    mid_dk = mid_dk.reshape(-1, flat_width)
    mid_dv = mid_dv.reshape(-1, flat_width)
    for level_bit in reversed(range(span_bits)):
        half_rows = mid_dk.shape[0] // 2
        upper_side = my_place >> level_bit & 1 == 1
        keep_k = jnp.where(upper_side, mid_dk[half_rows:], mid_dk[:half_rows])
        keep_v = jnp.where(upper_side, mid_dv[half_rows:], mid_dv[:half_rows])
        send_k = jnp.where(upper_side, mid_dk[:half_rows], mid_dk[half_rows:])
        send_v = jnp.where(upper_side, mid_dv[:half_rows], mid_dv[half_rows:])
        received = (
            swapped(send_k.astype(jnp.bfloat16), "ctx", level_bit).astype(send_k.dtype),
            swapped(send_v.astype(jnp.bfloat16), "ctx", level_bit).astype(send_v.dtype),
        )
        mid_dk = keep_k + received[0]
        mid_dv = keep_v + received[1]
    mid_dk = mid_dk.reshape(-1, head_count, HEAD_DIM)
    mid_dv = mid_dv.reshape(-1, head_count, HEAD_DIM)
    top_sel = pick_rows(top_share[..., None], ctx_size, top_shift)[..., 0]
    top_low = (top_sel[..., None] * pick_rows(grad_attn, ctx_size, top_shift)).astype(jnp.bfloat16)
    top_row_shift = -(top_sel * pick_rows(inner[..., None], ctx_size, top_shift)[..., 0])
    top_grad, top_soft = score_grads(top_q, top_keys, top_vals, top_total, top_low, top_row_shift)
    top_dq = query_part(top_grad, top_keys)
    gathered_dk, gathered_dv = key_parts(top_grad, top_soft, top_q, top_low)
    summed = (
        lax.psum_scatter(
            gathered_dk.reshape(-1, flat_width), "ctx", scatter_dimension=0, tiled=True
        ),
        lax.psum_scatter(
            gathered_dv.reshape(-1, flat_width), "ctx", scatter_dimension=0, tiled=True
        ),
    )
    top_dk = summed[0].reshape(-1, head_count, HEAD_DIM)
    top_dv = summed[1].reshape(-1, head_count, HEAD_DIM)
    query_grad = (
        base_dq + place_rows(mid_dq, R1, mid_shift) + place_rows(top_dq, ctx_size, top_shift)
    )
    key_grad = base_dk + place_rows(mid_dk, R1, mid_shift) + place_rows(top_dk, ctx_size, top_shift)
    value_grad = (
        base_dv + place_rows(mid_dv, R1, mid_shift) + place_rows(top_dv, ctx_size, top_shift)
    )
    out_shape = (1, tokens, flat_width)
    return (
        attended,
        query_grad.astype(jnp.bfloat16).reshape(out_shape),
        key_grad.astype(jnp.bfloat16).reshape(out_shape),
        value_grad.astype(jnp.bfloat16).reshape(out_shape),
        gain_grad,
    )


VMEM_SPEC = pl.BlockSpec(memory_space=pltpu.VMEM)
SMEM_SPEC = pl.BlockSpec(memory_space=pltpu.SMEM)
HBM_SPEC = pl.BlockSpec(memory_space=pltpu.HBM)
PEERS = SPAN - 1
STATS_ROWS = 8
NEVER = -1e30
LOW = jnp.bfloat16
WIDE = jnp.float32
HEAD_GROUPS = ((0, 5),)


def contract(left, right, left_dim, right_dim):
    return lax.dot_general(
        left, right, (((left_dim,), (right_dim,)), ((), ())), preferred_element_type=WIDE
    )


def head_cols(head):
    return pl.ds(head * HEAD_DIM, HEAD_DIM)


def picked_counts(tokens, top_step):
    return tokens // top_step, tokens // R1


def pick_matrix(offsets_ref, head, tokens, top_step, picked_axis):
    top_rows, mid_rows = picked_counts(tokens, top_step)
    shape = (top_rows + mid_rows, tokens) if picked_axis == 0 else (tokens, top_rows + mid_rows)
    row = lax.broadcasted_iota(jnp.int32, shape, picked_axis)
    position = lax.broadcasted_iota(jnp.int32, shape, 1 - picked_axis)
    wanted = jnp.where(
        row < top_rows,
        row * top_step + offsets_ref[1, head],
        (row - top_rows) * R1 + offsets_ref[0, head],
    )
    return jnp.where(position == wanted, 1.0, 0.0).astype(LOW)


def stacked(refs, rows, cols):
    return jnp.concatenate([ref[rows, cols] for ref in refs], 0)


def pack_kernel(top_step, groups, offsets_ref, k_hbm, v_hbm, *refs):
    packed_refs, (k_ref, v_ref, sems) = refs[: len(groups)], refs[len(groups) :]
    tokens, width = k_ref.shape
    picked = sum(picked_counts(tokens, top_step))
    copies = []
    for head in range(width // HEAD_DIM):
        cols = head_cols(head)
        pair = [
            pltpu.make_async_copy(source.at[0, :, cols], held.at[:, cols], sems.at[which, head])
            for which, (source, held) in enumerate(((k_hbm, k_ref), (v_hbm, v_ref)))
        ]
        for copy in pair:
            copy.start()
        copies.append(pair)
    for (first, last), packed_ref in zip(groups, packed_refs):
        for head in range(first, last):
            cols = head_cols(head)
            picks = pick_matrix(offsets_ref, head, tokens, top_step, 0)
            for copy in copies[head]:
                copy.wait()
            both = jnp.concatenate([k_ref[:, cols], v_ref[:, cols]], 1)
            rows = contract(picks, both, 1, 0).astype(LOW)
            packed_ref[:picked, head_cols(head - first)] = rows[:, :HEAD_DIM]
            packed_ref[picked:, head_cols(head - first)] = rows[:, HEAD_DIM:]


def fetch(sources, held, sems):
    copies = [
        pltpu.make_async_copy(source.at[0] if len(source.shape) == 3 else source, block, sems.at[i])
        for i, (source, block) in enumerate(zip(sources, held))
    ]
    for copy in copies:
        copy.start()
    for copy in copies:
        copy.wait()


def base_kernel(top_step, offsets_ref, *refs):
    sources, refs = refs[:5], refs[5:]
    held, sems = refs[-6:-1], refs[-1]
    expo_ref, out_ref, grad_norm_ref, q_copy_ref, inv_gain_ref, place_ref, stats_ref = refs[:-6]
    fetch(sources, held, sems)
    q_ref, k_ref, v_ref, grad_ref, gain_ref = held
    tokens, width = q_ref.shape
    picked = sum(picked_counts(tokens, top_step))
    score_scale = 1.0 / math.sqrt(HEAD_DIM)
    key_row = lax.broadcasted_iota(jnp.int32, (tokens, 1), 0)
    query_col = lax.broadcasted_iota(jnp.int32, (1, tokens), 1)
    q_copy_ref[...] = q_ref[...]
    inv_gain_ref[...] = 1.0 / gain_ref[...]
    for head in range(width // HEAD_DIM):
        cols = head_cols(head)
        times = 1.0
        for level, step in ((0, R1), (1, top_step)):
            offset = offsets_ref[level, head]
            hit_row = jnp.where(key_row % step == offset, 1.0, 0.0)
            hit_col = jnp.where(query_col % step == offset, 1.0, 0.0)
            times = times + hit_row * hit_col
            bias_row = (2 + level) * STATS_ROWS + head
            stats_ref[bias_row : bias_row + 1, :] = (1.0 - hit_col) * NEVER
        place_ref[:, pl.ds(head * HEAD_DIM, picked)] = pick_matrix(
            offsets_ref, head, tokens, top_step, 1
        )
        scores = contract(k_ref[:, cols], q_ref[:, cols], 1, 1) * score_scale
        top_score = jnp.max(scores, axis=0, keepdims=True)
        expo = times * jnp.exp(scores - top_score)
        expo_low = expo.astype(LOW)
        expo_ref[:, cols] = expo_low
        out_ref[:, cols] = contract(v_ref[:, cols], expo_low, 0, 0)
        stats_ref[head : head + 1, :] = top_score
        stats_ref[STATS_ROWS + head : STATS_ROWS + head + 1, :] = jnp.sum(
            expo, axis=0, keepdims=True
        )
        grad_norm_ref[:, cols] = (grad_ref[:, cols].astype(WIDE) * gain_ref[:, cols]).T


def attend_kernel(
    top_step,
    first,
    last,
    q_ref,
    base_out_ref,
    grad_norm_ref,
    inv_gain_ref,
    base_stats_ref,
    *refs,
):
    packed_refs = refs[:PEERS]
    gain_part_ref, normed_ref, grad_low_ref, score_grad_ref, stats_ref = refs[PEERS : PEERS + 5]
    part_refs = refs[PEERS + 5 :]
    tokens = q_ref.shape[0]
    top_rows, mid_rows = picked_counts(tokens, top_step)
    picked = top_rows + mid_rows
    score_scale = 1.0 / math.sqrt(HEAD_DIM)
    ones = jnp.ones((STATS_ROWS, tokens), LOW)
    for head in range(first, last):
        cols = head_cols(head)
        own = head_cols(head - first)
        q_rows = q_ref[:, cols]
        k_peers = stacked(packed_refs, pl.ds(0, picked), own)
        v_peers = stacked(packed_refs, pl.ds(picked, picked), own)
        mid_bias, top_bias = [
            base_stats_ref[row + head : row + head + 1, :]
            for row in (2 * STATS_ROWS, 3 * STATS_ROWS)
        ]
        bias = jnp.concatenate(
            [
                jnp.broadcast_to(top_bias, (top_rows, tokens)),
                jnp.broadcast_to(mid_bias, (mid_rows, tokens)),
            ]
            * PEERS,
            0,
        )
        scores = contract(k_peers, q_rows, 1, 1) * score_scale + bias
        base_top = base_stats_ref[head : head + 1, :]
        base_total = base_stats_ref[STATS_ROWS + head : STATS_ROWS + head + 1, :]
        top_score = jnp.maximum(base_top, jnp.max(scores, axis=0, keepdims=True))
        base_factor = jnp.exp(base_top - top_score)
        expo = jnp.exp(scores - top_score)
        inv_total = 1.0 / (base_factor * base_total + jnp.sum(expo, axis=0, keepdims=True))
        soft = expo * inv_total
        soft_low = soft.astype(LOW)
        base_factor = base_factor * inv_total
        attn = base_factor * base_out_ref[:, cols] + contract(v_peers, soft_low, 0, 0)
        inv_rms = lax.rsqrt(jnp.mean(attn * attn, axis=0, keepdims=True) + EPS)
        normed = attn * inv_rms
        normed_ref[:, own] = normed
        grad_norm = grad_norm_ref[:, cols]
        product = grad_norm * normed
        grad_attn = inv_rms * (grad_norm - normed * jnp.mean(product, axis=0, keepdims=True))
        product_high = product.astype(LOW)
        product_rest = (product - product_high.astype(WIDE)).astype(LOW)
        gain_rows = contract(ones, product_high, 1, 1) + contract(ones, product_rest, 1, 1)
        gain_part_ref[:, own] = gain_rows[:1] * inv_gain_ref[:, cols]
        inner = jnp.sum(grad_attn * attn, axis=0, keepdims=True)
        grad_low = grad_attn.astype(LOW)
        grad_low_ref[:, own] = grad_low
        stats_ref[head - first : head - first + 1, :] = base_factor
        stats_ref[STATS_ROWS + head - first : STATS_ROWS + head - first + 1, :] = inner
        prob_grad = contract(v_peers, grad_low, 1, 0)
        score_grad = (soft * (prob_grad - inner) * score_scale).astype(LOW)
        score_grad_ref[:, own] = score_grad
        dk_peers = contract(score_grad, q_rows, 1, 0).astype(LOW)
        dv_peers = contract(soft_low, grad_low, 1, 1).astype(LOW)
        for place, part_ref in enumerate(part_refs):
            part_ref[:picked, own] = dk_peers[place * picked : (place + 1) * picked]
            part_ref[picked:, own] = dv_peers[place * picked : (place + 1) * picked]


def local_grad_kernel(top_step, groups, *refs):
    sources, expo_ref, refs = refs[:4], refs[4], refs[5:]
    held, sems = refs[-5:-1], refs[-1]
    per_group = 4 + PEERS
    group_refs = refs[: per_group * len(groups)]
    attended_ref, dq_ref, dk_ref, dv_ref = refs[per_group * len(groups) : -5]
    fetch(sources, held, sems)
    q_ref, k_ref, v_ref, gain_ref = held
    picked = sum(picked_counts(q_ref.shape[0], top_step))
    score_scale = 1.0 / math.sqrt(HEAD_DIM)
    for place, (first, last) in enumerate(groups):
        normed_ref, grad_low_ref, peer_score_grad_ref, stats_ref, *packed_refs = group_refs[
            place * per_group : (place + 1) * per_group
        ]
        for head in range(first, last):
            cols = head_cols(head)
            own = head_cols(head - first)
            normed = normed_ref[:, own].T
            attended_ref[0, :, cols] = (normed * gain_ref[:, cols]).astype(LOW)
            k_rows = k_ref[:, cols]
            k_peers = stacked(packed_refs, pl.ds(0, picked), own)
            grad_low = grad_low_ref[:, own]
            base_factor = stats_ref[head - first : head - first + 1, :]
            inner = stats_ref[STATS_ROWS + head - first : STATS_ROWS + head - first + 1, :]
            soft = expo_ref[:, cols].astype(WIDE) * base_factor
            prob_grad = contract(v_ref[:, cols], grad_low, 1, 0)
            score_grad = (soft * (prob_grad - inner) * score_scale).astype(LOW)
            dk_ref[:, cols] = contract(score_grad, q_ref[:, cols], 1, 0)
            dv_ref[:, cols] = contract(soft.astype(LOW), grad_low, 1, 1)
            dq_ref[0, :, cols] = (
                contract(score_grad, k_rows, 0, 0)
                + contract(peer_score_grad_ref[:, own], k_peers, 0, 0)
            ).astype(LOW)


def finish_kernel(top_step, groups, place_ref, dk_ref, dv_ref, *refs):
    dk_out_ref, dv_out_ref = refs[PEERS * len(groups) :]
    tokens = dk_ref.shape[0]
    picked = sum(picked_counts(tokens, top_step))
    for place, (first, last) in enumerate(groups):
        part_refs = refs[place * PEERS : (place + 1) * PEERS]
        for head in range(first, last):
            cols = head_cols(head)
            own = head_cols(head - first)
            total = sum(part_ref[:, own].astype(WIDE) for part_ref in part_refs).astype(LOW)
            both = jnp.concatenate([total[:picked], total[picked:]], 1)
            placed = contract(place_ref[:, pl.ds(head * HEAD_DIM, picked)], both, 1, 0)
            dk_out_ref[0, :, cols] = (dk_ref[:, cols] + placed[:, :HEAD_DIM]).astype(LOW)
            dv_out_ref[0, :, cols] = (dv_ref[:, cols] + placed[:, HEAD_DIM:]).astype(LOW)


def across(block, axis, distance):
    route = [(place, place ^ distance) for place in range(lax.axis_size(axis))]
    return lax.ppermute(block, axis, route)


def to_peers(blocks):
    farthest_first = [
        across(blocks[distance - 1], "ctx", distance) for distance in range(PEERS, 0, -1)
    ]
    return farthest_first[::-1]


def call(kernel, name, operands, results, microseconds, **options):
    options.setdefault(
        "in_specs", [SMEM_SPEC if block.dtype == jnp.int32 else VMEM_SPEC for block in operands]
    )
    options.setdefault(
        "compiler_params", pltpu.CompilerParams(vmem_limit_bytes=16 * 1024 * 1024)
    )
    return pl.pallas_call(
        kernel,
        out_shape=results,
        out_specs=[VMEM_SPEC] * len(results),
        cost_estimate=pl.CostEstimate(
            flops=microseconds * 10**9, bytes_accessed=10**6, transcendentals=0
        ),
        name=name,
        **options,
    )(*operands)


def one_segment_shards(queries, keys, values, grad_y, out_gain, offsets):
    tokens, width = queries.shape[1:]
    heads = width // HEAD_DIM
    top_step = lax.axis_size("ctx")
    picked = sum(picked_counts(tokens, top_step))
    shape = jax.ShapeDtypeStruct
    row_block = shape((1, tokens, width), LOW)
    low_block = shape((tokens, width), LOW)
    wide_block = shape((tokens, width), WIDE)
    groups = HEAD_GROUPS
    widths = [(last - first) * HEAD_DIM for first, last in groups]
    bind = functools.partial
    gain_row = out_gain.reshape(1, width)
    packed = call(
        bind(pack_kernel, top_step, groups),
        "pack",
        (offsets, keys, values),
        [shape((2 * picked, group_width), LOW) for group_width in widths],
        1,
        in_specs=[SMEM_SPEC, HBM_SPEC, HBM_SPEC],
        compiler_params=None,
        scratch_shapes=[
            pltpu.VMEM((tokens, width), LOW),
            pltpu.VMEM((tokens, width), LOW),
            pltpu.SemaphoreType.DMA((2, heads)),
        ],
    )
    packed_peers = [to_peers([block] * PEERS) for block in packed]
    row_scratch, gain_scratch = pltpu.VMEM((tokens, width), LOW), pltpu.VMEM((1, width), WIDE)
    expo, base_out, grad_norm, q_copy, inv_gain, place, base_stats = call(
        bind(base_kernel, top_step),
        "base",
        (offsets, queries, keys, values, grad_y, gain_row),
        [
            low_block,
            wide_block,
            wide_block,
            low_block,
            shape((1, width), WIDE),
            low_block,
            shape((4 * STATS_ROWS, tokens), WIDE),
        ],
        2,
        in_specs=[SMEM_SPEC] + [HBM_SPEC] * 5,
        scratch_shapes=[row_scratch] * 4 + [gain_scratch, pltpu.SemaphoreType.DMA((5,))],
    )
    kept, returned, gain_parts = [], [], []
    for (first, last), group_width, peers in zip(groups, widths, packed_peers):
        gain_part, normed, grad_low, score_grad, stats, *parts = call(
            bind(attend_kernel, top_step, first, last),
            "attend",
            (q_copy, base_out, grad_norm, inv_gain, base_stats, *peers),
            [
                shape((1, group_width), WIDE),
                shape((tokens, group_width), WIDE),
                shape((tokens, group_width), LOW),
                shape((PEERS * picked, group_width), LOW),
                shape((2 * STATS_ROWS, tokens), WIDE),
            ]
            + [shape((2 * picked, group_width), LOW)] * PEERS,
            last - first,
        )
        gain_parts.append(gain_part.reshape(group_width))
        kept += [normed, grad_low, score_grad, stats, *peers]
        returned += to_peers(parts)
    gain_part = jnp.concatenate(gain_parts) if len(groups) > 1 else gain_parts[0]
    gain_pair = gain_part + across(gain_part, "dp", 1)
    gain_peers = to_peers([gain_pair] * PEERS)
    gain_grad = (gain_pair + gain_peers[0]) + (gain_peers[1] + gain_peers[2])
    attended, query_grad, dk_base, dv_base = call(
        bind(local_grad_kernel, top_step, groups),
        "local_grad",
        (queries, keys, values, gain_row, expo, *kept),
        [row_block, row_block, wide_block, wide_block],
        3,
        in_specs=[HBM_SPEC] * 4 + [VMEM_SPEC] * (1 + len(kept)),
        scratch_shapes=[row_scratch] * 3 + [gain_scratch, pltpu.SemaphoreType.DMA((4,))],
    )
    key_grad, value_grad = call(
        bind(finish_kernel, top_step, groups),
        "finish",
        (place, dk_base, dv_base, *returned),
        [row_block, row_block],
        2,
    )
    return attended, query_grad, key_grad, value_grad, gain_grad


def solution(mesh):
    in_specs = (
        P("dp", "ctx", "head"),
        P("dp", "ctx", "head"),
        P("dp", "ctx", "head"),
        P("dp", "ctx", "head"),
        P("head"),
        P(None, "head"),
    )
    out_specs = (
        P("dp", "ctx", "head"),
        P("dp", "ctx", "head"),
        P("dp", "ctx", "head"),
        P("dp", "ctx", "head"),
        P("head"),
    )
    body = one_segment_shards if mesh.shape["ctx"] == SPAN else general_shards
    return jax.shard_map(body, mesh=mesh, in_specs=in_specs, out_specs=out_specs, check_vma=False)
```

```python
import functools
import math

import jax
import jax.numpy as jnp
from jax import lax
from jax.experimental import pallas as pl
from jax.experimental.pallas import tpu as pltpu
from jax.sharding import PartitionSpec as P

HEAD_DIM = 128
SPAN = 4
R1 = 8


EPS = 1e-06


def swapped(block, axis, bit):
    count = lax.axis_size(axis)
    route = []
    for low in range(count):
        high = low | 1 << bit
        if high != low and high < count:
            route += [(low, high), (high, low)]
    return lax.ppermute(block, axis, route)


def pick_rows(source_rows, dilation, shifts):
    row_count, head_count, head_width = source_rows.shape
    grouped = source_rows.reshape(row_count // dilation, dilation, head_count, head_width)
    hit_mask = jnp.arange(dilation, dtype=jnp.int32).reshape(1, dilation, 1, 1) == shifts.reshape(
        1, 1, head_count, 1
    )
    chosen = jnp.where(hit_mask, grouped, jnp.zeros((), source_rows.dtype))
    return jnp.sum(chosen, axis=1, dtype=source_rows.dtype)


def place_rows(row_values, dilation, shifts):
    row_count, head_count, head_width = row_values.shape
    hit_mask = jnp.arange(dilation, dtype=jnp.int32).reshape(1, dilation, 1, 1) == shifts.reshape(
        1, 1, head_count, 1
    )
    spread = jnp.where(hit_mask, row_values[:, None], jnp.zeros((), row_values.dtype))
    return spread.reshape(row_count * dilation, head_count, head_width)


def level_scores(q_rows, k_rows):
    score_scale = 1.0 / math.sqrt(q_rows.shape[-1])
    return (
        jnp.einsum("qhe,khe->hqk", q_rows, k_rows, preferred_element_type=jnp.float32) * score_scale
    )


def attend(q_rows, k_rows, v_rows):
    scores = level_scores(q_rows, k_rows)
    row_max = jnp.max(scores, axis=-1, keepdims=True)
    log_total = row_max[..., 0] + jnp.log(jnp.sum(jnp.exp(scores - row_max), axis=-1))
    soft_rows = jnp.exp(scores - log_total[..., None]).astype(jnp.bfloat16)
    level_out = jnp.einsum("hqk,khe->qhe", soft_rows, v_rows, preferred_element_type=jnp.float32)
    return (level_out, log_total.T)


def score_grads(q_rows, k_rows, v_rows, log_total, grad_low, row_shift):
    score_scale = 1.0 / math.sqrt(q_rows.shape[-1])
    scores = level_scores(q_rows, k_rows)
    exact_soft = jnp.exp(scores - log_total.T[..., None])
    prob_grad = jnp.einsum("qhe,khe->hqk", grad_low, v_rows, preferred_element_type=jnp.float32)
    score_grad = (exact_soft * (prob_grad + row_shift.T[..., None]) * score_scale).astype(
        jnp.bfloat16
    )
    return (score_grad, exact_soft.astype(jnp.bfloat16))


def key_parts(score_grad, soft_low, q_rows, grad_low):
    k_part = jnp.einsum("hqk,qhe->khe", score_grad, q_rows, preferred_element_type=jnp.float32)
    v_part = jnp.einsum("hqk,qhe->khe", soft_low, grad_low, preferred_element_type=jnp.float32)
    return (k_part, v_part)


def query_part(score_grad, k_rows):
    return jnp.einsum("hqk,khe->qhe", score_grad, k_rows, preferred_element_type=jnp.float32)


def general_shards(queries, keys, values, grad_y, out_gain, offsets):
    tokens = queries.shape[1]
    flat_width = queries.shape[2]
    head_count = flat_width // HEAD_DIM
    row_shape = (tokens, head_count, HEAD_DIM)
    q_own = queries[0].reshape(row_shape)
    k_own = keys[0].reshape(row_shape)
    v_own = values[0].reshape(row_shape)
    ctx_size = lax.axis_size("ctx")
    span_bits = SPAN.bit_length() - 1
    my_place = lax.axis_index("ctx")
    mid_shift = offsets[0]
    top_shift = offsets[1]
    positions = jnp.arange(tokens, dtype=jnp.int32)
    mid_hit = (positions % R1)[:, None] == mid_shift[None, :]
    top_hit = (positions % ctx_size)[:, None] == top_shift[None, :]
    mid_q = pick_rows(q_own, R1, mid_shift)
    mid_k = pick_rows(k_own, R1, mid_shift)
    mid_v = pick_rows(v_own, R1, mid_shift)
    top_q = pick_rows(q_own, ctx_size, top_shift)
    top_k = pick_rows(k_own, ctx_size, top_shift)
    top_v = pick_rows(v_own, ctx_size, top_shift)
    mid_keys = mid_k.reshape(-1, flat_width)
    mid_vals = mid_v.reshape(-1, flat_width)
    top_keys = top_k.reshape(-1, flat_width)
    top_vals = top_v.reshape(-1, flat_width)

    def append_peer(mine, received, level_bit):
        upper_side = my_place >> level_bit & 1 == 1
        return jnp.where(
            upper_side, jnp.concatenate([received, mine], 0), jnp.concatenate([mine, received], 0)
        )

    for level_bit in range(span_bits):
        received = swapped((mid_keys, mid_vals), "ctx", level_bit)
        mid_keys = append_peer(mid_keys, received[0], level_bit)
        mid_vals = append_peer(mid_vals, received[1], level_bit)
    top_keys, top_vals = (
        lax.all_gather(top_keys, "ctx", axis=0, tiled=True),
        lax.all_gather(top_vals, "ctx", axis=0, tiled=True),
    )
    mid_keys = mid_keys.reshape(-1, head_count, HEAD_DIM)
    mid_vals = mid_vals.reshape(-1, head_count, HEAD_DIM)
    top_keys = top_keys.reshape(-1, head_count, HEAD_DIM)
    top_vals = top_vals.reshape(-1, head_count, HEAD_DIM)
    base_out, base_total = attend(q_own, k_own, v_own)
    mid_out, mid_total = attend(mid_q, mid_keys, mid_vals)
    top_out, top_total = attend(top_q, top_keys, top_vals)
    mid_full = place_rows(mid_total[..., None], R1, mid_shift)[..., 0]
    top_full = place_rows(top_total[..., None], ctx_size, top_shift)[..., 0]
    row_max = jnp.maximum(base_total, jnp.where(mid_hit, mid_full, base_total))
    row_max = jnp.maximum(row_max, jnp.where(top_hit, top_full, base_total))
    base_expo = jnp.exp(base_total - row_max)
    mid_expo = jnp.where(mid_hit, jnp.exp(mid_full - row_max), 0.0)
    top_expo = jnp.where(top_hit, jnp.exp(top_full - row_max), 0.0)
    denom = base_expo + mid_expo + top_expo
    base_share = base_expo / denom
    mid_share = mid_expo / denom
    top_share = top_expo / denom
    attn = (
        base_share[..., None] * base_out
        + mid_share[..., None] * place_rows(mid_out, R1, mid_shift)
        + top_share[..., None] * place_rows(top_out, ctx_size, top_shift)
    )
    inv_rms = lax.rsqrt(jnp.mean(attn * attn, axis=-1, keepdims=True) + EPS)
    normed = attn * inv_rms
    gain_rows = out_gain.reshape(head_count, HEAD_DIM)
    attended = (normed * gain_rows).astype(jnp.bfloat16).reshape(1, tokens, flat_width)
    grad_full = grad_y[0].reshape(row_shape).astype(jnp.float32)
    gain_part = jnp.sum(grad_full * normed, axis=0).reshape(flat_width)
    gain_grad = lax.psum(gain_part, ("dp", "ctx"))
    grad_norm = grad_full * gain_rows
    grad_attn = inv_rms * (
        grad_norm - normed * jnp.mean(grad_norm * normed, axis=-1, keepdims=True)
    )
    inner = jnp.sum(grad_attn * attn, axis=-1)
    base_low = (base_share[..., None] * grad_attn).astype(jnp.bfloat16)
    base_shift = -(base_share * inner)
    base_grad, base_soft = score_grads(q_own, k_own, v_own, base_total, base_low, base_shift)
    base_dq = query_part(base_grad, k_own)
    base_dk, base_dv = key_parts(base_grad, base_soft, q_own, base_low)
    mid_sel = pick_rows(mid_share[..., None], R1, mid_shift)[..., 0]
    mid_low = (mid_sel[..., None] * pick_rows(grad_attn, R1, mid_shift)).astype(jnp.bfloat16)
    mid_row_shift = -(mid_sel * pick_rows(inner[..., None], R1, mid_shift)[..., 0])
    mid_grad, mid_soft = score_grads(mid_q, mid_keys, mid_vals, mid_total, mid_low, mid_row_shift)
    mid_dq = query_part(mid_grad, mid_keys)
    mid_dk, mid_dv = key_parts(mid_grad, mid_soft, mid_q, mid_low)
    mid_dk = mid_dk.reshape(-1, flat_width)
    mid_dv = mid_dv.reshape(-1, flat_width)
    for level_bit in reversed(range(span_bits)):
        half_rows = mid_dk.shape[0] // 2
        upper_side = my_place >> level_bit & 1 == 1
        keep_k = jnp.where(upper_side, mid_dk[half_rows:], mid_dk[:half_rows])
        keep_v = jnp.where(upper_side, mid_dv[half_rows:], mid_dv[:half_rows])
        send_k = jnp.where(upper_side, mid_dk[:half_rows], mid_dk[half_rows:])
        send_v = jnp.where(upper_side, mid_dv[:half_rows], mid_dv[half_rows:])
        received = (
            swapped(send_k.astype(jnp.bfloat16), "ctx", level_bit).astype(send_k.dtype),
            swapped(send_v.astype(jnp.bfloat16), "ctx", level_bit).astype(send_v.dtype),
        )
        mid_dk = keep_k + received[0]
        mid_dv = keep_v + received[1]
    mid_dk = mid_dk.reshape(-1, head_count, HEAD_DIM)
    mid_dv = mid_dv.reshape(-1, head_count, HEAD_DIM)
    top_sel = pick_rows(top_share[..., None], ctx_size, top_shift)[..., 0]
    top_low = (top_sel[..., None] * pick_rows(grad_attn, ctx_size, top_shift)).astype(jnp.bfloat16)
    top_row_shift = -(top_sel * pick_rows(inner[..., None], ctx_size, top_shift)[..., 0])
    top_grad, top_soft = score_grads(top_q, top_keys, top_vals, top_total, top_low, top_row_shift)
    top_dq = query_part(top_grad, top_keys)
    gathered_dk, gathered_dv = key_parts(top_grad, top_soft, top_q, top_low)
    summed = (
        lax.psum_scatter(
            gathered_dk.reshape(-1, flat_width), "ctx", scatter_dimension=0, tiled=True
        ),
        lax.psum_scatter(
            gathered_dv.reshape(-1, flat_width), "ctx", scatter_dimension=0, tiled=True
        ),
    )
    top_dk = summed[0].reshape(-1, head_count, HEAD_DIM)
    top_dv = summed[1].reshape(-1, head_count, HEAD_DIM)
    query_grad = (
        base_dq + place_rows(mid_dq, R1, mid_shift) + place_rows(top_dq, ctx_size, top_shift)
    )
    key_grad = base_dk + place_rows(mid_dk, R1, mid_shift) + place_rows(top_dk, ctx_size, top_shift)
    value_grad = (
        base_dv + place_rows(mid_dv, R1, mid_shift) + place_rows(top_dv, ctx_size, top_shift)
    )
    out_shape = (1, tokens, flat_width)
    return (
        attended,
        query_grad.astype(jnp.bfloat16).reshape(out_shape),
        key_grad.astype(jnp.bfloat16).reshape(out_shape),
        value_grad.astype(jnp.bfloat16).reshape(out_shape),
        gain_grad,
    )


VMEM_SPEC = pl.BlockSpec(memory_space=pltpu.VMEM)
SMEM_SPEC = pl.BlockSpec(memory_space=pltpu.SMEM)
HBM_SPEC = pl.BlockSpec(memory_space=pltpu.HBM)
PEERS = SPAN - 1
STATS_ROWS = 8
NEVER = -1e30
LOW = jnp.bfloat16
WIDE = jnp.float32
HEAD_GROUPS = ((0, 5),)
PACK_VMEM = 65408 * 1024


def contract(left, right, left_dim, right_dim):
    return lax.dot_general(
        left, right, (((left_dim,), (right_dim,)), ((), ())), preferred_element_type=WIDE
    )


def head_cols(head):
    return pl.ds(head * HEAD_DIM, HEAD_DIM)


def picked_counts(tokens, top_step):
    return tokens // top_step, tokens // R1


def pick_matrix(offsets_ref, head, tokens, top_step, picked_axis):
    top_rows, mid_rows = picked_counts(tokens, top_step)
    shape = (top_rows + mid_rows, tokens) if picked_axis == 0 else (tokens, top_rows + mid_rows)
    row = lax.broadcasted_iota(jnp.int32, shape, picked_axis)
    position = lax.broadcasted_iota(jnp.int32, shape, 1 - picked_axis)
    wanted = jnp.where(
        row < top_rows,
        row * top_step + offsets_ref[1, head],
        (row - top_rows) * R1 + offsets_ref[0, head],
    )
    return jnp.where(position == wanted, 1.0, 0.0).astype(LOW)


def stacked(refs, rows, cols):
    return jnp.concatenate([ref[rows, cols] for ref in refs], 0)


def pack_kernel(top_step, groups, offsets_ref, k_hbm, v_hbm, *refs):
    packed_refs, (k_ref, v_ref, sems) = refs[: len(groups)], refs[len(groups) :]
    tokens, width = k_ref.shape
    picked = sum(picked_counts(tokens, top_step))
    copies = []
    for head in range(width // HEAD_DIM):
        cols = head_cols(head)
        pair = [
            pltpu.make_async_copy(source.at[0, :, cols], held.at[:, cols], sems.at[which, head])
            for which, (source, held) in enumerate(((k_hbm, k_ref), (v_hbm, v_ref)))
        ]
        for copy in pair:
            copy.start()
        copies.append(pair)
    for (first, last), packed_ref in zip(groups, packed_refs):
        for head in range(first, last):
            cols = head_cols(head)
            picks = pick_matrix(offsets_ref, head, tokens, top_step, 0)
            for copy in copies[head]:
                copy.wait()
            both = jnp.concatenate([k_ref[:, cols], v_ref[:, cols]], 1)
            rows = contract(picks, both, 1, 0).astype(LOW)
            packed_ref[:picked, head_cols(head - first)] = rows[:, :HEAD_DIM]
            packed_ref[picked:, head_cols(head - first)] = rows[:, HEAD_DIM:]


def fetch(sources, held, sems):
    copies = [
        pltpu.make_async_copy(source.at[0] if len(source.shape) == 3 else source, block, sems.at[i])
        for i, (source, block) in enumerate(zip(sources, held))
    ]
    for copy in copies:
        copy.start()
    for copy in copies:
        copy.wait()


def base_kernel(top_step, offsets_ref, *refs):
    sources, refs = refs[:5], refs[5:]
    held, sems = refs[-6:-1], refs[-1]
    expo_ref, out_ref, grad_norm_ref, q_copy_ref, inv_gain_ref, place_ref, stats_ref = refs[:-6]
    fetch(sources, held, sems)
    q_ref, k_ref, v_ref, grad_ref, gain_ref = held
    tokens, width = q_ref.shape
    picked = sum(picked_counts(tokens, top_step))
    score_scale = 1.0 / math.sqrt(HEAD_DIM)
    key_row = lax.broadcasted_iota(jnp.int32, (tokens, 1), 0)
    query_col = lax.broadcasted_iota(jnp.int32, (1, tokens), 1)
    q_copy_ref[...] = q_ref[...]
    inv_gain_ref[...] = 1.0 / gain_ref[...]
    for head in range(width // HEAD_DIM):
        cols = head_cols(head)
        times = 1.0
        for level, step in ((0, R1), (1, top_step)):
            offset = offsets_ref[level, head]
            hit_row = jnp.where(key_row % step == offset, 1.0, 0.0)
            hit_col = jnp.where(query_col % step == offset, 1.0, 0.0)
            times = times + hit_row * hit_col
            bias_row = (2 + level) * STATS_ROWS + head
            stats_ref[bias_row : bias_row + 1, :] = (1.0 - hit_col) * NEVER
        place_ref[:, pl.ds(head * HEAD_DIM, picked)] = pick_matrix(
            offsets_ref, head, tokens, top_step, 1
        )
        scores = contract(k_ref[:, cols], q_ref[:, cols], 1, 1) * score_scale
        top_score = jnp.max(scores, axis=0, keepdims=True)
        expo = times * jnp.exp(scores - top_score)
        expo_low = expo.astype(LOW)
        expo_ref[:, cols] = expo_low
        out_ref[:, cols] = contract(v_ref[:, cols], expo_low, 0, 0)
        stats_ref[head : head + 1, :] = top_score
        stats_ref[STATS_ROWS + head : STATS_ROWS + head + 1, :] = jnp.sum(
            expo, axis=0, keepdims=True
        )
        grad_norm_ref[:, cols] = (grad_ref[:, cols].astype(WIDE) * gain_ref[:, cols]).T


def attend_kernel(
    top_step,
    first,
    last,
    q_ref,
    base_out_ref,
    grad_norm_ref,
    inv_gain_ref,
    base_stats_ref,
    *refs,
):
    packed_refs = refs[:PEERS]
    gain_part_ref, normed_ref, grad_low_ref, score_grad_ref, stats_ref = refs[PEERS : PEERS + 5]
    part_refs = refs[PEERS + 5 :]
    tokens = q_ref.shape[0]
    top_rows, mid_rows = picked_counts(tokens, top_step)
    picked = top_rows + mid_rows
    score_scale = 1.0 / math.sqrt(HEAD_DIM)
    ones = jnp.ones((STATS_ROWS, tokens), LOW)
    for head in range(first, last):
        cols = head_cols(head)
        own = head_cols(head - first)
        q_rows = q_ref[:, cols]
        k_peers = stacked(packed_refs, pl.ds(0, picked), own)
        v_peers = stacked(packed_refs, pl.ds(picked, picked), own)
        mid_bias, top_bias = [
            base_stats_ref[row + head : row + head + 1, :]
            for row in (2 * STATS_ROWS, 3 * STATS_ROWS)
        ]
        bias = jnp.concatenate(
            [
                jnp.broadcast_to(top_bias, (top_rows, tokens)),
                jnp.broadcast_to(mid_bias, (mid_rows, tokens)),
            ]
            * PEERS,
            0,
        )
        scores = contract(k_peers, q_rows, 1, 1) * score_scale + bias
        base_top = base_stats_ref[head : head + 1, :]
        base_total = base_stats_ref[STATS_ROWS + head : STATS_ROWS + head + 1, :]
        top_score = jnp.maximum(base_top, jnp.max(scores, axis=0, keepdims=True))
        base_factor = jnp.exp(base_top - top_score)
        expo = jnp.exp(scores - top_score)
        inv_total = 1.0 / (base_factor * base_total + jnp.sum(expo, axis=0, keepdims=True))
        soft = expo * inv_total
        soft_low = soft.astype(LOW)
        base_factor = base_factor * inv_total
        attn = base_factor * base_out_ref[:, cols] + contract(v_peers, soft_low, 0, 0)
        inv_rms = lax.rsqrt(jnp.mean(attn * attn, axis=0, keepdims=True) + EPS)
        normed = attn * inv_rms
        normed_ref[:, own] = normed
        grad_norm = grad_norm_ref[:, cols]
        product = grad_norm * normed
        grad_attn = inv_rms * (grad_norm - normed * jnp.mean(product, axis=0, keepdims=True))
        product_high = product.astype(LOW)
        product_rest = (product - product_high.astype(WIDE)).astype(LOW)
        gain_rows = contract(ones, product_high, 1, 1) + contract(ones, product_rest, 1, 1)
        gain_part_ref[:, own] = gain_rows[:1] * inv_gain_ref[:, cols]
        inner = jnp.sum(grad_attn * attn, axis=0, keepdims=True)
        grad_low = grad_attn.astype(LOW)
        grad_low_ref[:, own] = grad_low
        stats_ref[head - first : head - first + 1, :] = base_factor
        stats_ref[STATS_ROWS + head - first : STATS_ROWS + head - first + 1, :] = inner
        prob_grad = contract(v_peers, grad_low, 1, 0)
        score_grad = (soft * (prob_grad - inner) * score_scale).astype(LOW)
        score_grad_ref[:, own] = score_grad
        dk_peers = contract(score_grad, q_rows, 1, 0).astype(LOW)
        dv_peers = contract(soft_low, grad_low, 1, 1).astype(LOW)
        for place, part_ref in enumerate(part_refs):
            part_ref[:picked, own] = dk_peers[place * picked : (place + 1) * picked]
            part_ref[picked:, own] = dv_peers[place * picked : (place + 1) * picked]


def query_grad_kernel(top_step, groups, *refs):
    sources, expo_ref, refs = refs[:3], refs[3], refs[4:]
    held, sems = refs[-4:-1], refs[-1]
    per_group = 4 + PEERS
    group_refs = refs[: per_group * len(groups)]
    attended_ref, dq_ref, score_grad_ref, soft_ref = refs[per_group * len(groups) : -4]
    fetch(sources, held, sems)
    k_ref, v_ref, gain_ref = held
    picked = sum(picked_counts(k_ref.shape[0], top_step))
    score_scale = 1.0 / math.sqrt(HEAD_DIM)
    for place, (first, last) in enumerate(groups):
        normed_ref, grad_low_ref, peer_score_grad_ref, stats_ref, *packed_refs = group_refs[
            place * per_group : (place + 1) * per_group
        ]
        for head in range(first, last):
            cols = head_cols(head)
            own = head_cols(head - first)
            attended_ref[0, :, cols] = (normed_ref[:, own].T * gain_ref[:, cols]).astype(LOW)
            k_peers = stacked(packed_refs, pl.ds(0, picked), own)
            base_factor = stats_ref[head - first : head - first + 1, :]
            inner = stats_ref[STATS_ROWS + head - first : STATS_ROWS + head - first + 1, :]
            soft = expo_ref[:, cols].astype(WIDE) * base_factor
            prob_grad = contract(v_ref[:, cols], grad_low_ref[:, own], 1, 0)
            score_grad = (soft * (prob_grad - inner) * score_scale).astype(LOW)
            score_grad_ref[:, cols] = score_grad
            soft_ref[:, cols] = soft.astype(LOW)
            dq_ref[0, :, cols] = (
                contract(score_grad, k_ref[:, cols], 0, 0)
                + contract(peer_score_grad_ref[:, own], k_peers, 0, 0)
            ).astype(LOW)


def key_grad_kernel(groups, q_ref, score_grad_ref, soft_ref, *refs):
    grad_low_refs, (dk_ref, dv_ref) = refs[: len(groups)], refs[len(groups) :]
    for (first, last), grad_low_ref in zip(groups, grad_low_refs):
        for head in range(first, last):
            cols = head_cols(head)
            dk_ref[:, cols] = contract(score_grad_ref[:, cols], q_ref[:, cols], 1, 0)
            dv_ref[:, cols] = contract(
                soft_ref[:, cols], grad_low_ref[:, head_cols(head - first)], 1, 1
            )


def finish_kernel(top_step, groups, place_ref, dk_ref, dv_ref, *refs):
    dk_out_ref, dv_out_ref = refs[PEERS * len(groups) :]
    tokens = dk_ref.shape[0]
    picked = sum(picked_counts(tokens, top_step))
    for place, (first, last) in enumerate(groups):
        part_refs = refs[place * PEERS : (place + 1) * PEERS]
        for head in range(first, last):
            cols = head_cols(head)
            own = head_cols(head - first)
            total = sum(part_ref[:, own].astype(WIDE) for part_ref in part_refs).astype(LOW)
            both = jnp.concatenate([total[:picked], total[picked:]], 1)
            placed = contract(place_ref[:, pl.ds(head * HEAD_DIM, picked)], both, 1, 0)
            dk_out_ref[0, :, cols] = (dk_ref[:, cols] + placed[:, :HEAD_DIM]).astype(LOW)
            dv_out_ref[0, :, cols] = (dv_ref[:, cols] + placed[:, HEAD_DIM:]).astype(LOW)


def across(block, axis, distance):
    route = [(place, place ^ distance) for place in range(lax.axis_size(axis))]
    return lax.ppermute(block, axis, route)


def to_peers(blocks):
    farthest_first = [
        across(blocks[distance - 1], "ctx", distance) for distance in range(PEERS, 0, -1)
    ]
    return farthest_first[::-1]


def call(kernel, name, operands, results, microseconds, **options):
    options.setdefault(
        "in_specs", [SMEM_SPEC if block.dtype == jnp.int32 else VMEM_SPEC for block in operands]
    )
    options.setdefault(
        "compiler_params", pltpu.CompilerParams(vmem_limit_bytes=16 * 1024 * 1024)
    )
    return pl.pallas_call(
        kernel,
        out_shape=results,
        out_specs=[VMEM_SPEC] * len(results),
        cost_estimate=pl.CostEstimate(
            flops=microseconds * 10**9, bytes_accessed=10**6, transcendentals=0
        ),
        name=name,
        **options,
    )(*operands)


def one_segment_shards(queries, keys, values, grad_y, out_gain, offsets):
    tokens, width = queries.shape[1:]
    heads = width // HEAD_DIM
    top_step = lax.axis_size("ctx")
    picked = sum(picked_counts(tokens, top_step))
    shape = jax.ShapeDtypeStruct
    row_block = shape((1, tokens, width), LOW)
    low_block = shape((tokens, width), LOW)
    wide_block = shape((tokens, width), WIDE)
    groups = HEAD_GROUPS
    widths = [(last - first) * HEAD_DIM for first, last in groups]
    bind = functools.partial
    gain_row = out_gain.reshape(1, width)
    packed = call(
        bind(pack_kernel, top_step, groups),
        "pack",
        (offsets, keys, values),
        [shape((2 * picked, group_width), LOW) for group_width in widths],
        1,
        in_specs=[SMEM_SPEC, HBM_SPEC, HBM_SPEC],
        compiler_params=pltpu.CompilerParams(vmem_limit_bytes=PACK_VMEM),
        scratch_shapes=[
            pltpu.VMEM((tokens, width), LOW),
            pltpu.VMEM((tokens, width), LOW),
            pltpu.SemaphoreType.DMA((2, heads)),
        ],
    )
    packed_peers = [to_peers([block] * PEERS) for block in packed]
    row_scratch, gain_scratch = pltpu.VMEM((tokens, width), LOW), pltpu.VMEM((1, width), WIDE)
    expo, base_out, grad_norm, q_copy, inv_gain, place, base_stats = call(
        bind(base_kernel, top_step),
        "base",
        (offsets, queries, keys, values, grad_y, gain_row),
        [
            low_block,
            wide_block,
            wide_block,
            low_block,
            shape((1, width), WIDE),
            low_block,
            shape((4 * STATS_ROWS, tokens), WIDE),
        ],
        2,
        in_specs=[SMEM_SPEC] + [HBM_SPEC] * 5,
        scratch_shapes=[row_scratch] * 4 + [gain_scratch, pltpu.SemaphoreType.DMA((5,))],
    )
    kept, returned, gain_parts, grad_lows = [], [], [], []
    for (first, last), group_width, peers in zip(groups, widths, packed_peers):
        gain_part, normed, grad_low, score_grad, stats, *parts = call(
            bind(attend_kernel, top_step, first, last),
            "attend",
            (q_copy, base_out, grad_norm, inv_gain, base_stats, *peers),
            [
                shape((1, group_width), WIDE),
                shape((tokens, group_width), WIDE),
                shape((tokens, group_width), LOW),
                shape((PEERS * picked, group_width), LOW),
                shape((2 * STATS_ROWS, tokens), WIDE),
            ]
            + [shape((2 * picked, group_width), LOW)] * PEERS,
            last - first,
        )
        gain_parts.append(gain_part.reshape(group_width))
        grad_lows.append(grad_low)
        kept += [normed, grad_low, score_grad, stats, *peers]
        returned += to_peers(parts)
    gain_part = jnp.concatenate(gain_parts) if len(groups) > 1 else gain_parts[0]
    gain_grad = gain_part + across(gain_part, "dp", 1)
    for distance in (1, 2):
        gain_grad = gain_grad + across(gain_grad, "ctx", distance)
    attended, query_grad, score_grad, soft = call(
        bind(query_grad_kernel, top_step, groups),
        "query_grad",
        (keys, values, gain_row, expo, *kept),
        [row_block, row_block, low_block, low_block],
        20,
        in_specs=[HBM_SPEC] * 3 + [VMEM_SPEC] * (1 + len(kept)),
        scratch_shapes=[row_scratch] * 2 + [gain_scratch, pltpu.SemaphoreType.DMA((3,))],
    )
    dk_base, dv_base = call(
        bind(key_grad_kernel, groups),
        "key_grad",
        (q_copy, score_grad, soft, *grad_lows),
        [wide_block, wide_block],
        20,
    )
    key_grad, value_grad = call(
        bind(finish_kernel, top_step, groups),
        "finish",
        (place, dk_base, dv_base, *returned),
        [row_block, row_block],
        2,
    )
    return attended, query_grad, key_grad, value_grad, gain_grad


def solution(mesh):
    in_specs = (
        P("dp", "ctx", "head"),
        P("dp", "ctx", "head"),
        P("dp", "ctx", "head"),
        P("dp", "ctx", "head"),
        P("head"),
        P(None, "head"),
    )
    out_specs = (
        P("dp", "ctx", "head"),
        P("dp", "ctx", "head"),
        P("dp", "ctx", "head"),
        P("dp", "ctx", "head"),
        P("head"),
    )
    body = one_segment_shards if mesh.shape["ctx"] == SPAN else general_shards
    return jax.shard_map(body, mesh=mesh, in_specs=in_specs, out_specs=out_specs, check_vma=False)
```

```python
import functools
import math

import jax
import jax.numpy as jnp
from jax import lax
from jax.experimental import pallas as pl
from jax.experimental.pallas import tpu as pltpu
from jax.sharding import PartitionSpec as P

HEAD_DIM = 128
SPAN = 4
R1 = 8


EPS = 1e-06


def swapped(block, axis, bit):
    count = lax.axis_size(axis)
    route = []
    for low in range(count):
        high = low | 1 << bit
        if high != low and high < count:
            route += [(low, high), (high, low)]
    return lax.ppermute(block, axis, route)


def pick_rows(source_rows, dilation, shifts):
    row_count, head_count, head_width = source_rows.shape
    grouped = source_rows.reshape(row_count // dilation, dilation, head_count, head_width)
    hit_mask = jnp.arange(dilation, dtype=jnp.int32).reshape(1, dilation, 1, 1) == shifts.reshape(
        1, 1, head_count, 1
    )
    chosen = jnp.where(hit_mask, grouped, jnp.zeros((), source_rows.dtype))
    return jnp.sum(chosen, axis=1, dtype=source_rows.dtype)


def place_rows(row_values, dilation, shifts):
    row_count, head_count, head_width = row_values.shape
    hit_mask = jnp.arange(dilation, dtype=jnp.int32).reshape(1, dilation, 1, 1) == shifts.reshape(
        1, 1, head_count, 1
    )
    spread = jnp.where(hit_mask, row_values[:, None], jnp.zeros((), row_values.dtype))
    return spread.reshape(row_count * dilation, head_count, head_width)


def level_scores(q_rows, k_rows):
    score_scale = 1.0 / math.sqrt(q_rows.shape[-1])
    return (
        jnp.einsum("qhe,khe->hqk", q_rows, k_rows, preferred_element_type=jnp.float32) * score_scale
    )


def attend(q_rows, k_rows, v_rows):
    scores = level_scores(q_rows, k_rows)
    row_max = jnp.max(scores, axis=-1, keepdims=True)
    log_total = row_max[..., 0] + jnp.log(jnp.sum(jnp.exp(scores - row_max), axis=-1))
    soft_rows = jnp.exp(scores - log_total[..., None]).astype(jnp.bfloat16)
    level_out = jnp.einsum("hqk,khe->qhe", soft_rows, v_rows, preferred_element_type=jnp.float32)
    return (level_out, log_total.T)


def score_grads(q_rows, k_rows, v_rows, log_total, grad_low, row_shift):
    score_scale = 1.0 / math.sqrt(q_rows.shape[-1])
    scores = level_scores(q_rows, k_rows)
    exact_soft = jnp.exp(scores - log_total.T[..., None])
    prob_grad = jnp.einsum("qhe,khe->hqk", grad_low, v_rows, preferred_element_type=jnp.float32)
    score_grad = (exact_soft * (prob_grad + row_shift.T[..., None]) * score_scale).astype(
        jnp.bfloat16
    )
    return (score_grad, exact_soft.astype(jnp.bfloat16))


def key_parts(score_grad, soft_low, q_rows, grad_low):
    k_part = jnp.einsum("hqk,qhe->khe", score_grad, q_rows, preferred_element_type=jnp.float32)
    v_part = jnp.einsum("hqk,qhe->khe", soft_low, grad_low, preferred_element_type=jnp.float32)
    return (k_part, v_part)


def query_part(score_grad, k_rows):
    return jnp.einsum("hqk,khe->qhe", score_grad, k_rows, preferred_element_type=jnp.float32)


def general_shards(queries, keys, values, grad_y, out_gain, offsets):
    tokens = queries.shape[1]
    flat_width = queries.shape[2]
    head_count = flat_width // HEAD_DIM
    row_shape = (tokens, head_count, HEAD_DIM)
    q_own = queries[0].reshape(row_shape)
    k_own = keys[0].reshape(row_shape)
    v_own = values[0].reshape(row_shape)
    ctx_size = lax.axis_size("ctx")
    span_bits = SPAN.bit_length() - 1
    my_place = lax.axis_index("ctx")
    mid_shift = offsets[0]
    top_shift = offsets[1]
    positions = jnp.arange(tokens, dtype=jnp.int32)
    mid_hit = (positions % R1)[:, None] == mid_shift[None, :]
    top_hit = (positions % ctx_size)[:, None] == top_shift[None, :]
    mid_q = pick_rows(q_own, R1, mid_shift)
    mid_k = pick_rows(k_own, R1, mid_shift)
    mid_v = pick_rows(v_own, R1, mid_shift)
    top_q = pick_rows(q_own, ctx_size, top_shift)
    top_k = pick_rows(k_own, ctx_size, top_shift)
    top_v = pick_rows(v_own, ctx_size, top_shift)
    mid_keys = mid_k.reshape(-1, flat_width)
    mid_vals = mid_v.reshape(-1, flat_width)
    top_keys = top_k.reshape(-1, flat_width)
    top_vals = top_v.reshape(-1, flat_width)

    def append_peer(mine, received, level_bit):
        upper_side = my_place >> level_bit & 1 == 1
        return jnp.where(
            upper_side, jnp.concatenate([received, mine], 0), jnp.concatenate([mine, received], 0)
        )

    for level_bit in range(span_bits):
        received = swapped((mid_keys, mid_vals), "ctx", level_bit)
        mid_keys = append_peer(mid_keys, received[0], level_bit)
        mid_vals = append_peer(mid_vals, received[1], level_bit)
    top_keys, top_vals = (
        lax.all_gather(top_keys, "ctx", axis=0, tiled=True),
        lax.all_gather(top_vals, "ctx", axis=0, tiled=True),
    )
    mid_keys = mid_keys.reshape(-1, head_count, HEAD_DIM)
    mid_vals = mid_vals.reshape(-1, head_count, HEAD_DIM)
    top_keys = top_keys.reshape(-1, head_count, HEAD_DIM)
    top_vals = top_vals.reshape(-1, head_count, HEAD_DIM)
    base_out, base_total = attend(q_own, k_own, v_own)
    mid_out, mid_total = attend(mid_q, mid_keys, mid_vals)
    top_out, top_total = attend(top_q, top_keys, top_vals)
    mid_full = place_rows(mid_total[..., None], R1, mid_shift)[..., 0]
    top_full = place_rows(top_total[..., None], ctx_size, top_shift)[..., 0]
    row_max = jnp.maximum(base_total, jnp.where(mid_hit, mid_full, base_total))
    row_max = jnp.maximum(row_max, jnp.where(top_hit, top_full, base_total))
    base_expo = jnp.exp(base_total - row_max)
    mid_expo = jnp.where(mid_hit, jnp.exp(mid_full - row_max), 0.0)
    top_expo = jnp.where(top_hit, jnp.exp(top_full - row_max), 0.0)
    denom = base_expo + mid_expo + top_expo
    base_share = base_expo / denom
    mid_share = mid_expo / denom
    top_share = top_expo / denom
    attn = (
        base_share[..., None] * base_out
        + mid_share[..., None] * place_rows(mid_out, R1, mid_shift)
        + top_share[..., None] * place_rows(top_out, ctx_size, top_shift)
    )
    inv_rms = lax.rsqrt(jnp.mean(attn * attn, axis=-1, keepdims=True) + EPS)
    normed = attn * inv_rms
    gain_rows = out_gain.reshape(head_count, HEAD_DIM)
    attended = (normed * gain_rows).astype(jnp.bfloat16).reshape(1, tokens, flat_width)
    grad_full = grad_y[0].reshape(row_shape).astype(jnp.float32)
    gain_part = jnp.sum(grad_full * normed, axis=0).reshape(flat_width)
    gain_grad = lax.psum(gain_part, ("dp", "ctx"))
    grad_norm = grad_full * gain_rows
    grad_attn = inv_rms * (
        grad_norm - normed * jnp.mean(grad_norm * normed, axis=-1, keepdims=True)
    )
    inner = jnp.sum(grad_attn * attn, axis=-1)
    base_low = (base_share[..., None] * grad_attn).astype(jnp.bfloat16)
    base_shift = -(base_share * inner)
    base_grad, base_soft = score_grads(q_own, k_own, v_own, base_total, base_low, base_shift)
    base_dq = query_part(base_grad, k_own)
    base_dk, base_dv = key_parts(base_grad, base_soft, q_own, base_low)
    mid_sel = pick_rows(mid_share[..., None], R1, mid_shift)[..., 0]
    mid_low = (mid_sel[..., None] * pick_rows(grad_attn, R1, mid_shift)).astype(jnp.bfloat16)
    mid_row_shift = -(mid_sel * pick_rows(inner[..., None], R1, mid_shift)[..., 0])
    mid_grad, mid_soft = score_grads(mid_q, mid_keys, mid_vals, mid_total, mid_low, mid_row_shift)
    mid_dq = query_part(mid_grad, mid_keys)
    mid_dk, mid_dv = key_parts(mid_grad, mid_soft, mid_q, mid_low)
    mid_dk = mid_dk.reshape(-1, flat_width)
    mid_dv = mid_dv.reshape(-1, flat_width)
    for level_bit in reversed(range(span_bits)):
        half_rows = mid_dk.shape[0] // 2
        upper_side = my_place >> level_bit & 1 == 1
        keep_k = jnp.where(upper_side, mid_dk[half_rows:], mid_dk[:half_rows])
        keep_v = jnp.where(upper_side, mid_dv[half_rows:], mid_dv[:half_rows])
        send_k = jnp.where(upper_side, mid_dk[:half_rows], mid_dk[half_rows:])
        send_v = jnp.where(upper_side, mid_dv[:half_rows], mid_dv[half_rows:])
        received = (
            swapped(send_k.astype(jnp.bfloat16), "ctx", level_bit).astype(send_k.dtype),
            swapped(send_v.astype(jnp.bfloat16), "ctx", level_bit).astype(send_v.dtype),
        )
        mid_dk = keep_k + received[0]
        mid_dv = keep_v + received[1]
    mid_dk = mid_dk.reshape(-1, head_count, HEAD_DIM)
    mid_dv = mid_dv.reshape(-1, head_count, HEAD_DIM)
    top_sel = pick_rows(top_share[..., None], ctx_size, top_shift)[..., 0]
    top_low = (top_sel[..., None] * pick_rows(grad_attn, ctx_size, top_shift)).astype(jnp.bfloat16)
    top_row_shift = -(top_sel * pick_rows(inner[..., None], ctx_size, top_shift)[..., 0])
    top_grad, top_soft = score_grads(top_q, top_keys, top_vals, top_total, top_low, top_row_shift)
    top_dq = query_part(top_grad, top_keys)
    gathered_dk, gathered_dv = key_parts(top_grad, top_soft, top_q, top_low)
    summed = (
        lax.psum_scatter(
            gathered_dk.reshape(-1, flat_width), "ctx", scatter_dimension=0, tiled=True
        ),
        lax.psum_scatter(
            gathered_dv.reshape(-1, flat_width), "ctx", scatter_dimension=0, tiled=True
        ),
    )
    top_dk = summed[0].reshape(-1, head_count, HEAD_DIM)
    top_dv = summed[1].reshape(-1, head_count, HEAD_DIM)
    query_grad = (
        base_dq + place_rows(mid_dq, R1, mid_shift) + place_rows(top_dq, ctx_size, top_shift)
    )
    key_grad = base_dk + place_rows(mid_dk, R1, mid_shift) + place_rows(top_dk, ctx_size, top_shift)
    value_grad = (
        base_dv + place_rows(mid_dv, R1, mid_shift) + place_rows(top_dv, ctx_size, top_shift)
    )
    out_shape = (1, tokens, flat_width)
    return (
        attended,
        query_grad.astype(jnp.bfloat16).reshape(out_shape),
        key_grad.astype(jnp.bfloat16).reshape(out_shape),
        value_grad.astype(jnp.bfloat16).reshape(out_shape),
        gain_grad,
    )


VMEM_SPEC = pl.BlockSpec(memory_space=pltpu.VMEM)
SMEM_SPEC = pl.BlockSpec(memory_space=pltpu.SMEM)
HBM_SPEC = pl.BlockSpec(memory_space=pltpu.HBM)
PEERS = SPAN - 1
STATS_ROWS = 8
NEVER = -1e30
LOW = jnp.bfloat16
WIDE = jnp.float32
HEAD_GROUPS = ((0, 5),)
LOAD_PIECES = 4
PACK_VMEM = 65408 * 1024


def contract(left, right, left_dim, right_dim):
    return lax.dot_general(
        left, right, (((left_dim,), (right_dim,)), ((), ())), preferred_element_type=WIDE
    )


def head_cols(head):
    return pl.ds(head * HEAD_DIM, HEAD_DIM)


def picked_counts(tokens, top_step):
    return tokens // top_step, tokens // R1


def pick_matrix(offsets_ref, head, tokens, top_step, picked_axis):
    top_rows, mid_rows = picked_counts(tokens, top_step)
    shape = (top_rows + mid_rows, tokens) if picked_axis == 0 else (tokens, top_rows + mid_rows)
    row = lax.broadcasted_iota(jnp.int32, shape, picked_axis)
    position = lax.broadcasted_iota(jnp.int32, shape, 1 - picked_axis)
    wanted = jnp.where(
        row < top_rows,
        row * top_step + offsets_ref[1, head],
        (row - top_rows) * R1 + offsets_ref[0, head],
    )
    return jnp.where(position == wanted, 1.0, 0.0).astype(LOW)


def stacked(refs, rows, cols):
    return jnp.concatenate([ref[rows, cols] for ref in refs], 0)


def pack_kernel(top_step, groups, offsets_ref, k_hbm, v_hbm, *refs):
    packed_refs, (k_ref, v_ref, sems) = refs[: len(groups)], refs[len(groups) :]
    tokens, width = k_ref.shape
    picked = sum(picked_counts(tokens, top_step))
    step = tokens // LOAD_PIECES
    copies = [
        pltpu.make_async_copy(
            source.at[0, pl.ds(piece * step, step)],
            held.at[pl.ds(piece * step, step)],
            sems.at[which, piece],
        )
        for which, (source, held) in enumerate(((k_hbm, k_ref), (v_hbm, v_ref)))
        for piece in range(LOAD_PIECES)
    ]
    for copy in copies:
        copy.start()
    for copy in copies:
        copy.wait()
    for (first, last), packed_ref in zip(groups, packed_refs):
        for head in range(first, last):
            cols = head_cols(head)
            picks = pick_matrix(offsets_ref, head, tokens, top_step, 0)
            both = jnp.concatenate([k_ref[:, cols], v_ref[:, cols]], 1)
            rows = contract(picks, both, 1, 0).astype(LOW)
            packed_ref[:picked, head_cols(head - first)] = rows[:, :HEAD_DIM]
            packed_ref[picked:, head_cols(head - first)] = rows[:, HEAD_DIM:]


def fetch(sources, held, sems):
    copies = [
        pltpu.make_async_copy(source.at[0] if len(source.shape) == 3 else source, block, sems.at[i])
        for i, (source, block) in enumerate(zip(sources, held))
    ]
    for copy in copies:
        copy.start()
    for copy in copies:
        copy.wait()


def base_kernel(top_step, offsets_ref, *refs):
    sources, refs = refs[:5], refs[5:]
    held, sems = refs[-6:-1], refs[-1]
    expo_ref, out_ref, grad_norm_ref, q_copy_ref, inv_gain_ref, place_ref, stats_ref = refs[:-6]
    fetch(sources, held, sems)
    q_ref, k_ref, v_ref, grad_ref, gain_ref = held
    tokens, width = q_ref.shape
    picked = sum(picked_counts(tokens, top_step))
    score_scale = 1.0 / math.sqrt(HEAD_DIM)
    key_row = lax.broadcasted_iota(jnp.int32, (tokens, 1), 0)
    query_col = lax.broadcasted_iota(jnp.int32, (1, tokens), 1)
    q_copy_ref[...] = q_ref[...]
    inv_gain_ref[...] = 1.0 / gain_ref[...]
    for head in range(width // HEAD_DIM):
        cols = head_cols(head)
        times = 1.0
        for level, step in ((0, R1), (1, top_step)):
            offset = offsets_ref[level, head]
            hit_row = jnp.where(key_row % step == offset, 1.0, 0.0)
            hit_col = jnp.where(query_col % step == offset, 1.0, 0.0)
            times = times + hit_row * hit_col
            bias_row = (2 + level) * STATS_ROWS + head
            stats_ref[bias_row : bias_row + 1, :] = (1.0 - hit_col) * NEVER
        place_ref[:, pl.ds(head * HEAD_DIM, picked)] = pick_matrix(
            offsets_ref, head, tokens, top_step, 1
        )
        scores = contract(k_ref[:, cols], q_ref[:, cols], 1, 1) * score_scale
        top_score = jnp.max(scores, axis=0, keepdims=True)
        expo = times * jnp.exp(scores - top_score)
        expo_low = expo.astype(LOW)
        expo_ref[:, cols] = expo_low
        out_ref[:, cols] = contract(v_ref[:, cols], expo_low, 0, 0)
        stats_ref[head : head + 1, :] = top_score
        stats_ref[STATS_ROWS + head : STATS_ROWS + head + 1, :] = jnp.sum(
            expo, axis=0, keepdims=True
        )
        grad_norm_ref[:, cols] = (grad_ref[:, cols].astype(WIDE) * gain_ref[:, cols]).T


def attend_kernel(
    top_step,
    first,
    last,
    q_ref,
    base_out_ref,
    grad_norm_ref,
    inv_gain_ref,
    base_stats_ref,
    *refs,
):
    packed_refs = refs[:PEERS]
    gain_part_ref, normed_ref, grad_low_ref, score_grad_ref, stats_ref = refs[PEERS : PEERS + 5]
    part_refs = refs[PEERS + 5 :]
    tokens = q_ref.shape[0]
    top_rows, mid_rows = picked_counts(tokens, top_step)
    picked = top_rows + mid_rows
    score_scale = 1.0 / math.sqrt(HEAD_DIM)
    ones = jnp.ones((STATS_ROWS, tokens), LOW)
    for head in range(first, last):
        cols = head_cols(head)
        own = head_cols(head - first)
        q_rows = q_ref[:, cols]
        k_peers = stacked(packed_refs, pl.ds(0, picked), own)
        v_peers = stacked(packed_refs, pl.ds(picked, picked), own)
        mid_bias, top_bias = [
            base_stats_ref[row + head : row + head + 1, :]
            for row in (2 * STATS_ROWS, 3 * STATS_ROWS)
        ]
        bias = jnp.concatenate(
            [
                jnp.broadcast_to(top_bias, (top_rows, tokens)),
                jnp.broadcast_to(mid_bias, (mid_rows, tokens)),
            ]
            * PEERS,
            0,
        )
        scores = contract(k_peers, q_rows, 1, 1) * score_scale + bias
        base_top = base_stats_ref[head : head + 1, :]
        base_total = base_stats_ref[STATS_ROWS + head : STATS_ROWS + head + 1, :]
        top_score = jnp.maximum(base_top, jnp.max(scores, axis=0, keepdims=True))
        base_factor = jnp.exp(base_top - top_score)
        expo = jnp.exp(scores - top_score)
        inv_total = 1.0 / (base_factor * base_total + jnp.sum(expo, axis=0, keepdims=True))
        soft = expo * inv_total
        soft_low = soft.astype(LOW)
        base_factor = base_factor * inv_total
        attn = base_factor * base_out_ref[:, cols] + contract(v_peers, soft_low, 0, 0)
        inv_rms = lax.rsqrt(jnp.mean(attn * attn, axis=0, keepdims=True) + EPS)
        normed = attn * inv_rms
        normed_ref[:, own] = normed
        grad_norm = grad_norm_ref[:, cols]
        product = grad_norm * normed
        grad_attn = inv_rms * (grad_norm - normed * jnp.mean(product, axis=0, keepdims=True))
        product_high = product.astype(LOW)
        product_rest = (product - product_high.astype(WIDE)).astype(LOW)
        gain_rows = contract(ones, product_high, 1, 1) + contract(ones, product_rest, 1, 1)
        gain_part_ref[:, own] = gain_rows[:1] * inv_gain_ref[:, cols]
        inner = jnp.sum(grad_attn * attn, axis=0, keepdims=True)
        grad_low = grad_attn.astype(LOW)
        grad_low_ref[:, own] = grad_low
        stats_ref[head - first : head - first + 1, :] = base_factor
        stats_ref[STATS_ROWS + head - first : STATS_ROWS + head - first + 1, :] = inner
        prob_grad = contract(v_peers, grad_low, 1, 0)
        score_grad = (soft * (prob_grad - inner) * score_scale).astype(LOW)
        score_grad_ref[:, own] = score_grad
        dk_peers = contract(score_grad, q_rows, 1, 0).astype(LOW)
        dv_peers = contract(soft_low, grad_low, 1, 1).astype(LOW)
        for place, part_ref in enumerate(part_refs):
            part_ref[:picked, own] = dk_peers[place * picked : (place + 1) * picked]
            part_ref[picked:, own] = dv_peers[place * picked : (place + 1) * picked]


def query_grad_kernel(top_step, groups, *refs):
    sources, expo_ref, refs = refs[:3], refs[3], refs[4:]
    held, sems = refs[-4:-1], refs[-1]
    per_group = 4 + PEERS
    group_refs = refs[: per_group * len(groups)]
    attended_ref, dq_ref, score_grad_ref, soft_ref = refs[per_group * len(groups) : -4]
    fetch(sources, held, sems)
    k_ref, v_ref, gain_ref = held
    picked = sum(picked_counts(k_ref.shape[0], top_step))
    score_scale = 1.0 / math.sqrt(HEAD_DIM)
    for place, (first, last) in enumerate(groups):
        normed_ref, grad_low_ref, peer_score_grad_ref, stats_ref, *packed_refs = group_refs[
            place * per_group : (place + 1) * per_group
        ]
        for head in range(first, last):
            cols = head_cols(head)
            own = head_cols(head - first)
            attended_ref[0, :, cols] = (normed_ref[:, own].T * gain_ref[:, cols]).astype(LOW)
            k_peers = stacked(packed_refs, pl.ds(0, picked), own)
            base_factor = stats_ref[head - first : head - first + 1, :]
            inner = stats_ref[STATS_ROWS + head - first : STATS_ROWS + head - first + 1, :]
            soft = expo_ref[:, cols].astype(WIDE) * base_factor
            prob_grad = contract(v_ref[:, cols], grad_low_ref[:, own], 1, 0)
            score_grad = (soft * (prob_grad - inner) * score_scale).astype(LOW)
            score_grad_ref[:, cols] = score_grad
            soft_ref[:, cols] = soft.astype(LOW)
            dq_ref[0, :, cols] = (
                contract(score_grad, k_ref[:, cols], 0, 0)
                + contract(peer_score_grad_ref[:, own], k_peers, 0, 0)
            ).astype(LOW)


def key_grad_kernel(groups, q_ref, score_grad_ref, soft_ref, *refs):
    grad_low_refs, (dk_ref, dv_ref) = refs[: len(groups)], refs[len(groups) :]
    for (first, last), grad_low_ref in zip(groups, grad_low_refs):
        for head in range(first, last):
            cols = head_cols(head)
            dk_ref[:, cols] = contract(score_grad_ref[:, cols], q_ref[:, cols], 1, 0)
            dv_ref[:, cols] = contract(
                soft_ref[:, cols], grad_low_ref[:, head_cols(head - first)], 1, 1
            )


def finish_kernel(top_step, groups, gain_ref, place_ref, dk_ref, dv_ref, *refs):
    dk_out_ref, dv_out_ref, gain_out_ref = refs[PEERS * len(groups) :]
    gain_out_ref[...] = gain_ref[...]
    tokens = dk_ref.shape[0]
    picked = sum(picked_counts(tokens, top_step))
    for place, (first, last) in enumerate(groups):
        part_refs = refs[place * PEERS : (place + 1) * PEERS]
        for head in range(first, last):
            cols = head_cols(head)
            own = head_cols(head - first)
            total = sum(part_ref[:, own].astype(WIDE) for part_ref in part_refs).astype(LOW)
            both = jnp.concatenate([total[:picked], total[picked:]], 1)
            placed = contract(place_ref[:, pl.ds(head * HEAD_DIM, picked)], both, 1, 0)
            dk_out_ref[0, :, cols] = (dk_ref[:, cols] + placed[:, :HEAD_DIM]).astype(LOW)
            dv_out_ref[0, :, cols] = (dv_ref[:, cols] + placed[:, HEAD_DIM:]).astype(LOW)


def across(block, axis, distance):
    route = [(place, place ^ distance) for place in range(lax.axis_size(axis))]
    return lax.ppermute(block, axis, route)


def to_peers(blocks):
    farthest_first = [
        across(blocks[distance - 1], "ctx", distance) for distance in range(PEERS, 0, -1)
    ]
    return farthest_first[::-1]


def call(kernel, name, operands, results, microseconds, **options):
    options.setdefault(
        "in_specs", [SMEM_SPEC if block.dtype == jnp.int32 else VMEM_SPEC for block in operands]
    )
    options.setdefault(
        "compiler_params", pltpu.CompilerParams(vmem_limit_bytes=16 * 1024 * 1024)
    )
    return pl.pallas_call(
        kernel,
        out_shape=results,
        out_specs=[VMEM_SPEC] * len(results),
        cost_estimate=pl.CostEstimate(
            flops=int(microseconds * 10**9), bytes_accessed=0, transcendentals=0
        ),
        name=name,
        **options,
    )(*operands)


def one_segment_shards(queries, keys, values, grad_y, out_gain, offsets):
    tokens, width = queries.shape[1:]
    heads = width // HEAD_DIM
    top_step = lax.axis_size("ctx")
    picked = sum(picked_counts(tokens, top_step))
    shape = jax.ShapeDtypeStruct
    row_block = shape((1, tokens, width), LOW)
    low_block = shape((tokens, width), LOW)
    wide_block = shape((tokens, width), WIDE)
    groups = HEAD_GROUPS
    widths = [(last - first) * HEAD_DIM for first, last in groups]
    bind = functools.partial
    gain_row = out_gain.reshape(1, width)
    packed = call(
        bind(pack_kernel, top_step, groups),
        "pack",
        (offsets, keys, values),
        [shape((2 * picked, group_width), LOW) for group_width in widths],
        1,
        in_specs=[SMEM_SPEC, HBM_SPEC, HBM_SPEC],
        compiler_params=pltpu.CompilerParams(vmem_limit_bytes=PACK_VMEM),
        scratch_shapes=[
            pltpu.VMEM((tokens, width), LOW),
            pltpu.VMEM((tokens, width), LOW),
            pltpu.SemaphoreType.DMA((2, LOAD_PIECES)),
        ],
    )
    packed_peers = [to_peers([block] * PEERS) for block in packed]
    row_scratch, gain_scratch = pltpu.VMEM((tokens, width), LOW), pltpu.VMEM((1, width), WIDE)
    expo, base_out, grad_norm, q_copy, inv_gain, place, base_stats = call(
        bind(base_kernel, top_step),
        "base",
        (offsets, queries, keys, values, grad_y, gain_row),
        [
            low_block,
            wide_block,
            wide_block,
            low_block,
            shape((1, width), WIDE),
            low_block,
            shape((4 * STATS_ROWS, tokens), WIDE),
        ],
        2,
        in_specs=[SMEM_SPEC] + [HBM_SPEC] * 5,
        scratch_shapes=[row_scratch] * 4 + [gain_scratch, pltpu.SemaphoreType.DMA((5,))],
    )
    kept, returned, gain_parts, grad_lows = [], [], [], []
    for (first, last), group_width, peers in zip(groups, widths, packed_peers):
        gain_part, normed, grad_low, score_grad, stats, *parts = call(
            bind(attend_kernel, top_step, first, last),
            "attend",
            (q_copy, base_out, grad_norm, inv_gain, base_stats, *peers),
            [
                shape((1, group_width), WIDE),
                shape((tokens, group_width), WIDE),
                shape((tokens, group_width), LOW),
                shape((PEERS * picked, group_width), LOW),
                shape((2 * STATS_ROWS, tokens), WIDE),
            ]
            + [shape((2 * picked, group_width), LOW)] * PEERS,
            last - first,
        )
        gain_parts.append(gain_part)
        grad_lows.append(grad_low)
        kept += [normed, grad_low, score_grad, stats, *peers]
        returned += to_peers(parts)[::-1]
    gain_part = jnp.concatenate(gain_parts, 1) if len(groups) > 1 else gain_parts[0]
    gain_grad = gain_part + across(gain_part, "dp", 1)
    gain_grad = gain_grad + across(gain_grad, "ctx", 1)
    gain_rest = across(gain_grad, "ctx", 2)
    attended, query_grad, score_grad, soft = call(
        bind(query_grad_kernel, top_step, groups),
        "query_grad",
        (keys, values, gain_row, expo, *kept),
        [row_block, row_block, low_block, low_block],
        0.5,
        in_specs=[HBM_SPEC] * 3 + [VMEM_SPEC] * (1 + len(kept)),
        scratch_shapes=[row_scratch] * 2 + [gain_scratch, pltpu.SemaphoreType.DMA((3,))],
    )
    dk_base, dv_base = call(
        bind(key_grad_kernel, groups),
        "key_grad",
        (q_copy, score_grad, soft, *grad_lows),
        [wide_block, wide_block],
        0.5,
    )
    key_grad, value_grad, gain_grad = call(
        bind(finish_kernel, top_step, groups),
        "finish",
        (gain_grad, place, dk_base, dv_base, *returned),
        [row_block, row_block, shape((1, width), WIDE)],
        1,
    )
    gain_grad = (gain_grad + gain_rest).reshape(width)
    return attended, query_grad, key_grad, value_grad, gain_grad


def solution(mesh):
    in_specs = (
        P("dp", "ctx", "head"),
        P("dp", "ctx", "head"),
        P("dp", "ctx", "head"),
        P("dp", "ctx", "head"),
        P("head"),
        P(None, "head"),
    )
    out_specs = (
        P("dp", "ctx", "head"),
        P("dp", "ctx", "head"),
        P("dp", "ctx", "head"),
        P("dp", "ctx", "head"),
        P("head"),
    )
    body = one_segment_shards if mesh.shape["ctx"] == SPAN else general_shards
    return jax.shard_map(body, mesh=mesh, in_specs=in_specs, out_specs=out_specs, check_vma=False)
```

```python
import functools
import math

import jax
import jax.numpy as jnp
from jax import lax
from jax.experimental import pallas as pl
from jax.experimental.pallas import tpu as pltpu
from jax.sharding import PartitionSpec as P

HEAD_DIM = 128
SPAN = 4
R1 = 8


EPS = 1e-06


def swapped(block, axis, bit):
    count = lax.axis_size(axis)
    route = []
    for low in range(count):
        high = low | 1 << bit
        if high != low and high < count:
            route += [(low, high), (high, low)]
    return lax.ppermute(block, axis, route)


def pick_rows(source_rows, dilation, shifts):
    row_count, head_count, head_width = source_rows.shape
    grouped = source_rows.reshape(row_count // dilation, dilation, head_count, head_width)
    hit_mask = jnp.arange(dilation, dtype=jnp.int32).reshape(1, dilation, 1, 1) == shifts.reshape(
        1, 1, head_count, 1
    )
    chosen = jnp.where(hit_mask, grouped, jnp.zeros((), source_rows.dtype))
    return jnp.sum(chosen, axis=1, dtype=source_rows.dtype)


def place_rows(row_values, dilation, shifts):
    row_count, head_count, head_width = row_values.shape
    hit_mask = jnp.arange(dilation, dtype=jnp.int32).reshape(1, dilation, 1, 1) == shifts.reshape(
        1, 1, head_count, 1
    )
    spread = jnp.where(hit_mask, row_values[:, None], jnp.zeros((), row_values.dtype))
    return spread.reshape(row_count * dilation, head_count, head_width)


def level_scores(q_rows, k_rows):
    score_scale = 1.0 / math.sqrt(q_rows.shape[-1])
    return (
        jnp.einsum("qhe,khe->hqk", q_rows, k_rows, preferred_element_type=jnp.float32) * score_scale
    )


def attend(q_rows, k_rows, v_rows):
    scores = level_scores(q_rows, k_rows)
    row_max = jnp.max(scores, axis=-1, keepdims=True)
    log_total = row_max[..., 0] + jnp.log(jnp.sum(jnp.exp(scores - row_max), axis=-1))
    soft_rows = jnp.exp(scores - log_total[..., None]).astype(jnp.bfloat16)
    level_out = jnp.einsum("hqk,khe->qhe", soft_rows, v_rows, preferred_element_type=jnp.float32)
    return (level_out, log_total.T)


def score_grads(q_rows, k_rows, v_rows, log_total, grad_low, row_shift):
    score_scale = 1.0 / math.sqrt(q_rows.shape[-1])
    scores = level_scores(q_rows, k_rows)
    exact_soft = jnp.exp(scores - log_total.T[..., None])
    prob_grad = jnp.einsum("qhe,khe->hqk", grad_low, v_rows, preferred_element_type=jnp.float32)
    score_grad = (exact_soft * (prob_grad + row_shift.T[..., None]) * score_scale).astype(
        jnp.bfloat16
    )
    return (score_grad, exact_soft.astype(jnp.bfloat16))


def key_parts(score_grad, soft_low, q_rows, grad_low):
    k_part = jnp.einsum("hqk,qhe->khe", score_grad, q_rows, preferred_element_type=jnp.float32)
    v_part = jnp.einsum("hqk,qhe->khe", soft_low, grad_low, preferred_element_type=jnp.float32)
    return (k_part, v_part)


def query_part(score_grad, k_rows):
    return jnp.einsum("hqk,khe->qhe", score_grad, k_rows, preferred_element_type=jnp.float32)


def general_shards(queries, keys, values, grad_y, out_gain, offsets):
    tokens = queries.shape[1]
    flat_width = queries.shape[2]
    head_count = flat_width // HEAD_DIM
    row_shape = (tokens, head_count, HEAD_DIM)
    q_own = queries[0].reshape(row_shape)
    k_own = keys[0].reshape(row_shape)
    v_own = values[0].reshape(row_shape)
    ctx_size = lax.axis_size("ctx")
    span_bits = SPAN.bit_length() - 1
    my_place = lax.axis_index("ctx")
    mid_shift = offsets[0]
    top_shift = offsets[1]
    positions = jnp.arange(tokens, dtype=jnp.int32)
    mid_hit = (positions % R1)[:, None] == mid_shift[None, :]
    top_hit = (positions % ctx_size)[:, None] == top_shift[None, :]
    mid_q = pick_rows(q_own, R1, mid_shift)
    mid_k = pick_rows(k_own, R1, mid_shift)
    mid_v = pick_rows(v_own, R1, mid_shift)
    top_q = pick_rows(q_own, ctx_size, top_shift)
    top_k = pick_rows(k_own, ctx_size, top_shift)
    top_v = pick_rows(v_own, ctx_size, top_shift)
    mid_keys = mid_k.reshape(-1, flat_width)
    mid_vals = mid_v.reshape(-1, flat_width)
    top_keys = top_k.reshape(-1, flat_width)
    top_vals = top_v.reshape(-1, flat_width)

    def append_peer(mine, received, level_bit):
        upper_side = my_place >> level_bit & 1 == 1
        return jnp.where(
            upper_side, jnp.concatenate([received, mine], 0), jnp.concatenate([mine, received], 0)
        )

    for level_bit in range(span_bits):
        received = swapped((mid_keys, mid_vals), "ctx", level_bit)
        mid_keys = append_peer(mid_keys, received[0], level_bit)
        mid_vals = append_peer(mid_vals, received[1], level_bit)
    top_keys, top_vals = (
        lax.all_gather(top_keys, "ctx", axis=0, tiled=True),
        lax.all_gather(top_vals, "ctx", axis=0, tiled=True),
    )
    mid_keys = mid_keys.reshape(-1, head_count, HEAD_DIM)
    mid_vals = mid_vals.reshape(-1, head_count, HEAD_DIM)
    top_keys = top_keys.reshape(-1, head_count, HEAD_DIM)
    top_vals = top_vals.reshape(-1, head_count, HEAD_DIM)
    base_out, base_total = attend(q_own, k_own, v_own)
    mid_out, mid_total = attend(mid_q, mid_keys, mid_vals)
    top_out, top_total = attend(top_q, top_keys, top_vals)
    mid_full = place_rows(mid_total[..., None], R1, mid_shift)[..., 0]
    top_full = place_rows(top_total[..., None], ctx_size, top_shift)[..., 0]
    row_max = jnp.maximum(base_total, jnp.where(mid_hit, mid_full, base_total))
    row_max = jnp.maximum(row_max, jnp.where(top_hit, top_full, base_total))
    base_expo = jnp.exp(base_total - row_max)
    mid_expo = jnp.where(mid_hit, jnp.exp(mid_full - row_max), 0.0)
    top_expo = jnp.where(top_hit, jnp.exp(top_full - row_max), 0.0)
    denom = base_expo + mid_expo + top_expo
    base_share = base_expo / denom
    mid_share = mid_expo / denom
    top_share = top_expo / denom
    attn = (
        base_share[..., None] * base_out
        + mid_share[..., None] * place_rows(mid_out, R1, mid_shift)
        + top_share[..., None] * place_rows(top_out, ctx_size, top_shift)
    )
    inv_rms = lax.rsqrt(jnp.mean(attn * attn, axis=-1, keepdims=True) + EPS)
    normed = attn * inv_rms
    gain_rows = out_gain.reshape(head_count, HEAD_DIM)
    attended = (normed * gain_rows).astype(jnp.bfloat16).reshape(1, tokens, flat_width)
    grad_full = grad_y[0].reshape(row_shape).astype(jnp.float32)
    gain_part = jnp.sum(grad_full * normed, axis=0).reshape(flat_width)
    gain_grad = lax.psum(gain_part, ("dp", "ctx"))
    grad_norm = grad_full * gain_rows
    grad_attn = inv_rms * (
        grad_norm - normed * jnp.mean(grad_norm * normed, axis=-1, keepdims=True)
    )
    inner = jnp.sum(grad_attn * attn, axis=-1)
    base_low = (base_share[..., None] * grad_attn).astype(jnp.bfloat16)
    base_shift = -(base_share * inner)
    base_grad, base_soft = score_grads(q_own, k_own, v_own, base_total, base_low, base_shift)
    base_dq = query_part(base_grad, k_own)
    base_dk, base_dv = key_parts(base_grad, base_soft, q_own, base_low)
    mid_sel = pick_rows(mid_share[..., None], R1, mid_shift)[..., 0]
    mid_low = (mid_sel[..., None] * pick_rows(grad_attn, R1, mid_shift)).astype(jnp.bfloat16)
    mid_row_shift = -(mid_sel * pick_rows(inner[..., None], R1, mid_shift)[..., 0])
    mid_grad, mid_soft = score_grads(mid_q, mid_keys, mid_vals, mid_total, mid_low, mid_row_shift)
    mid_dq = query_part(mid_grad, mid_keys)
    mid_dk, mid_dv = key_parts(mid_grad, mid_soft, mid_q, mid_low)
    mid_dk = mid_dk.reshape(-1, flat_width)
    mid_dv = mid_dv.reshape(-1, flat_width)
    for level_bit in reversed(range(span_bits)):
        half_rows = mid_dk.shape[0] // 2
        upper_side = my_place >> level_bit & 1 == 1
        keep_k = jnp.where(upper_side, mid_dk[half_rows:], mid_dk[:half_rows])
        keep_v = jnp.where(upper_side, mid_dv[half_rows:], mid_dv[:half_rows])
        send_k = jnp.where(upper_side, mid_dk[:half_rows], mid_dk[half_rows:])
        send_v = jnp.where(upper_side, mid_dv[:half_rows], mid_dv[half_rows:])
        received = (
            swapped(send_k.astype(jnp.bfloat16), "ctx", level_bit).astype(send_k.dtype),
            swapped(send_v.astype(jnp.bfloat16), "ctx", level_bit).astype(send_v.dtype),
        )
        mid_dk = keep_k + received[0]
        mid_dv = keep_v + received[1]
    mid_dk = mid_dk.reshape(-1, head_count, HEAD_DIM)
    mid_dv = mid_dv.reshape(-1, head_count, HEAD_DIM)
    top_sel = pick_rows(top_share[..., None], ctx_size, top_shift)[..., 0]
    top_low = (top_sel[..., None] * pick_rows(grad_attn, ctx_size, top_shift)).astype(jnp.bfloat16)
    top_row_shift = -(top_sel * pick_rows(inner[..., None], ctx_size, top_shift)[..., 0])
    top_grad, top_soft = score_grads(top_q, top_keys, top_vals, top_total, top_low, top_row_shift)
    top_dq = query_part(top_grad, top_keys)
    gathered_dk, gathered_dv = key_parts(top_grad, top_soft, top_q, top_low)
    summed = (
        lax.psum_scatter(
            gathered_dk.reshape(-1, flat_width), "ctx", scatter_dimension=0, tiled=True
        ),
        lax.psum_scatter(
            gathered_dv.reshape(-1, flat_width), "ctx", scatter_dimension=0, tiled=True
        ),
    )
    top_dk = summed[0].reshape(-1, head_count, HEAD_DIM)
    top_dv = summed[1].reshape(-1, head_count, HEAD_DIM)
    query_grad = (
        base_dq + place_rows(mid_dq, R1, mid_shift) + place_rows(top_dq, ctx_size, top_shift)
    )
    key_grad = base_dk + place_rows(mid_dk, R1, mid_shift) + place_rows(top_dk, ctx_size, top_shift)
    value_grad = (
        base_dv + place_rows(mid_dv, R1, mid_shift) + place_rows(top_dv, ctx_size, top_shift)
    )
    out_shape = (1, tokens, flat_width)
    return (
        attended,
        query_grad.astype(jnp.bfloat16).reshape(out_shape),
        key_grad.astype(jnp.bfloat16).reshape(out_shape),
        value_grad.astype(jnp.bfloat16).reshape(out_shape),
        gain_grad,
    )


VMEM_SPEC = pl.BlockSpec(memory_space=pltpu.VMEM)
SMEM_SPEC = pl.BlockSpec(memory_space=pltpu.SMEM)
HBM_SPEC = pl.BlockSpec(memory_space=pltpu.HBM)
PEERS = SPAN - 1
STATS_ROWS = 8
NEVER = -1e30
LOW = jnp.bfloat16
WIDE = jnp.float32
HEAD_GROUPS = ((0, 5),)
LOAD_PIECES = 1
PACK_VMEM = 65408 * 1024


def contract(left, right, left_dim, right_dim):
    return lax.dot_general(
        left, right, (((left_dim,), (right_dim,)), ((), ())), preferred_element_type=WIDE
    )


def head_cols(head):
    return pl.ds(head * HEAD_DIM, HEAD_DIM)


def picked_counts(tokens, top_step):
    return tokens // top_step, tokens // R1


def pick_matrix(offsets_ref, head, tokens, top_step, picked_axis):
    top_rows, mid_rows = picked_counts(tokens, top_step)
    shape = (top_rows + mid_rows, tokens) if picked_axis == 0 else (tokens, top_rows + mid_rows)
    row = lax.broadcasted_iota(jnp.int32, shape, picked_axis)
    position = lax.broadcasted_iota(jnp.int32, shape, 1 - picked_axis)
    wanted = jnp.where(
        row < top_rows,
        row * top_step + offsets_ref[1, head],
        (row - top_rows) * R1 + offsets_ref[0, head],
    )
    return jnp.where(position == wanted, 1.0, 0.0).astype(LOW)


def stacked(refs, rows, cols):
    return jnp.concatenate([ref[rows, cols] for ref in refs], 0)


def pack_kernel(top_step, groups, offsets_ref, k_hbm, v_hbm, *refs):
    packed_refs, (k_ref, v_ref, sems) = refs[: len(groups)], refs[len(groups) :]
    tokens, width = k_ref.shape
    picked = sum(picked_counts(tokens, top_step))
    step = tokens // LOAD_PIECES
    copies = [
        pltpu.make_async_copy(
            source.at[0, pl.ds(piece * step, step)],
            held.at[pl.ds(piece * step, step)],
            sems.at[which, piece],
        )
        for which, (source, held) in enumerate(((k_hbm, k_ref), (v_hbm, v_ref)))
        for piece in range(LOAD_PIECES)
    ]
    for copy in copies:
        copy.start()
    heads = range(width // HEAD_DIM)
    picks = [pick_matrix(offsets_ref, head, tokens, top_step, 0) for head in heads]
    for copy in copies:
        copy.wait()
    both = [
        jnp.concatenate([k_ref[:, head_cols(head)], v_ref[:, head_cols(head)]], 1) for head in heads
    ]
    rows = [contract(picks[head], both[head], 1, 0).astype(LOW) for head in heads]
    for (first, last), packed_ref in zip(groups, packed_refs):
        for head in range(first, last):
            packed_ref[:picked, head_cols(head - first)] = rows[head][:, :HEAD_DIM]
            packed_ref[picked:, head_cols(head - first)] = rows[head][:, HEAD_DIM:]


def fetch(sources, held, sems):
    copies = [
        pltpu.make_async_copy(source.at[0] if len(source.shape) == 3 else source, block, sems.at[i])
        for i, (source, block) in enumerate(zip(sources, held))
    ]
    for copy in copies:
        copy.start()
    for copy in copies:
        copy.wait()


def base_kernel(top_step, offsets_ref, *refs):
    sources, refs = refs[:5], refs[5:]
    held, sems = refs[-6:-1], refs[-1]
    expo_ref, out_ref, grad_norm_ref, q_copy_ref, inv_gain_ref, place_ref, stats_ref = refs[:-6]
    fetch(sources, held, sems)
    q_ref, k_ref, v_ref, grad_ref, gain_ref = held
    tokens, width = q_ref.shape
    picked = sum(picked_counts(tokens, top_step))
    score_scale = 1.0 / math.sqrt(HEAD_DIM)
    key_row = lax.broadcasted_iota(jnp.int32, (tokens, 1), 0)
    query_col = lax.broadcasted_iota(jnp.int32, (1, tokens), 1)
    q_copy_ref[...] = q_ref[...]
    inv_gain_ref[...] = 1.0 / gain_ref[...]
    for head in range(width // HEAD_DIM):
        cols = head_cols(head)
        times = 1.0
        for level, step in ((0, R1), (1, top_step)):
            offset = offsets_ref[level, head]
            hit_row = jnp.where(key_row % step == offset, 1.0, 0.0)
            hit_col = jnp.where(query_col % step == offset, 1.0, 0.0)
            times = times + hit_row * hit_col
            bias_row = (2 + level) * STATS_ROWS + head
            stats_ref[bias_row : bias_row + 1, :] = (1.0 - hit_col) * NEVER
        place_ref[:, pl.ds(head * HEAD_DIM, picked)] = pick_matrix(
            offsets_ref, head, tokens, top_step, 1
        )
        scores = contract(k_ref[:, cols], q_ref[:, cols], 1, 1) * score_scale
        top_score = jnp.max(scores, axis=0, keepdims=True)
        expo = times * jnp.exp(scores - top_score)
        expo_low = expo.astype(LOW)
        expo_ref[:, cols] = expo_low
        out_ref[:, cols] = contract(v_ref[:, cols], expo_low, 0, 0)
        stats_ref[head : head + 1, :] = top_score
        stats_ref[STATS_ROWS + head : STATS_ROWS + head + 1, :] = jnp.sum(
            expo, axis=0, keepdims=True
        )
        grad_norm_ref[:, cols] = (grad_ref[:, cols].astype(WIDE) * gain_ref[:, cols]).T


def attend_kernel(
    top_step,
    first,
    last,
    q_ref,
    base_out_ref,
    grad_norm_ref,
    inv_gain_ref,
    base_stats_ref,
    *refs,
):
    packed_refs = refs[:PEERS]
    gain_part_ref, normed_ref, grad_low_ref, score_grad_ref, stats_ref = refs[PEERS : PEERS + 5]
    part_refs = refs[PEERS + 5 :]
    tokens = q_ref.shape[0]
    top_rows, mid_rows = picked_counts(tokens, top_step)
    picked = top_rows + mid_rows
    score_scale = 1.0 / math.sqrt(HEAD_DIM)
    ones = jnp.ones((STATS_ROWS, tokens), LOW)
    heads = range(last - first)
    every = [head_cols(head) for head in range(first, last)]
    own = [head_cols(head) for head in heads]

    def stat(block, head):
        row = block * STATS_ROWS + first + head
        return base_stats_ref[row : row + 1, :]

    q_rows = [q_ref[:, cols] for cols in every]
    k_peers = [stacked(packed_refs, pl.ds(0, picked), cols) for cols in own]
    v_peers = [stacked(packed_refs, pl.ds(picked, picked), cols) for cols in own]
    products = [contract(k_peers[head], q_rows[head], 1, 1) for head in heads]
    expos, factors, inv_totals = [], [], []
    for head in heads:
        bias = jnp.concatenate(
            [
                jnp.broadcast_to(stat(3, head), (top_rows, tokens)),
                jnp.broadcast_to(stat(2, head), (mid_rows, tokens)),
            ]
            * PEERS,
            0,
        )
        scores = products[head] * score_scale + bias
        top_score = jnp.maximum(stat(0, head), jnp.max(scores, axis=0, keepdims=True))
        expos.append(jnp.exp(scores - top_score))
        factors.append(jnp.exp(stat(0, head) - top_score))
    for head in heads:
        total = factors[head] * stat(1, head) + jnp.sum(expos[head], axis=0, keepdims=True)
        inv_totals.append(1.0 / total)
        factors[head] = factors[head] * inv_totals[head]
        stats_ref[head : head + 1, :] = factors[head]
    softs = [expos[head] * inv_totals[head] for head in heads]
    soft_lows = [soft.astype(LOW) for soft in softs]
    mixed = [contract(v_peers[head], soft_lows[head], 0, 0) for head in heads]
    grad_lows, inners, gain_products = [], [], []
    for head in heads:
        attn = factors[head] * base_out_ref[:, every[head]] + mixed[head]
        inv_rms = lax.rsqrt(jnp.mean(attn * attn, axis=0, keepdims=True) + EPS)
        normed = attn * inv_rms
        normed_ref[:, own[head]] = normed
        grad_norm = grad_norm_ref[:, every[head]]
        product = grad_norm * normed
        gain_products.append(product)
        grad_attn = inv_rms * (grad_norm - normed * jnp.mean(product, axis=0, keepdims=True))
        inners.append(jnp.sum(grad_attn * attn, axis=0, keepdims=True))
        stats_ref[STATS_ROWS + head : STATS_ROWS + head + 1, :] = inners[head]
        grad_lows.append(grad_attn.astype(LOW))
        grad_low_ref[:, own[head]] = grad_lows[head]
    prob_grads = [contract(v_peers[head], grad_lows[head], 1, 0) for head in heads]
    dv_peers = [contract(soft_lows[head], grad_lows[head], 1, 1).astype(LOW) for head in heads]
    score_grads = [
        (softs[head] * (prob_grads[head] - inners[head]) * score_scale).astype(LOW)
        for head in heads
    ]
    dk_peers = [contract(score_grads[head], q_rows[head], 1, 0).astype(LOW) for head in heads]
    for head in heads:
        score_grad_ref[:, own[head]] = score_grads[head]
        product_high = gain_products[head].astype(LOW)
        product_rest = (gain_products[head] - product_high.astype(WIDE)).astype(LOW)
        gain_rows = contract(ones, product_high, 1, 1) + contract(ones, product_rest, 1, 1)
        gain_part_ref[:, own[head]] = gain_rows[:1] * inv_gain_ref[:, every[head]]
        for place, part_ref in enumerate(part_refs):
            start = place * picked
            part_ref[:picked, own[head]] = dk_peers[head][start : start + picked]
            part_ref[picked:, own[head]] = dv_peers[head][start : start + picked]


def query_grad_kernel(top_step, groups, *refs):
    sources, expo_ref, refs = refs[:3], refs[3], refs[4:]
    held, sems = refs[-4:-1], refs[-1]
    per_group = 4 + PEERS
    group_refs = refs[: per_group * len(groups)]
    attended_ref, dq_ref, score_grad_ref, soft_ref = refs[per_group * len(groups) : -4]
    fetch(sources, held, sems)
    k_ref, v_ref, gain_ref = held
    picked = sum(picked_counts(k_ref.shape[0], top_step))
    score_scale = 1.0 / math.sqrt(HEAD_DIM)
    for place, (first, last) in enumerate(groups):
        normed_ref, grad_low_ref, peer_score_grad_ref, stats_ref, *packed_refs = group_refs[
            place * per_group : (place + 1) * per_group
        ]
        for head in range(first, last):
            cols = head_cols(head)
            own = head_cols(head - first)
            attended_ref[0, :, cols] = (normed_ref[:, own].T * gain_ref[:, cols]).astype(LOW)
            k_peers = stacked(packed_refs, pl.ds(0, picked), own)
            base_factor = stats_ref[head - first : head - first + 1, :]
            inner = stats_ref[STATS_ROWS + head - first : STATS_ROWS + head - first + 1, :]
            soft = expo_ref[:, cols].astype(WIDE) * base_factor
            prob_grad = contract(v_ref[:, cols], grad_low_ref[:, own], 1, 0)
            score_grad = (soft * (prob_grad - inner) * score_scale).astype(LOW)
            score_grad_ref[:, cols] = score_grad
            soft_ref[:, cols] = soft.astype(LOW)
            dq_ref[0, :, cols] = (
                contract(score_grad, k_ref[:, cols], 0, 0)
                + contract(peer_score_grad_ref[:, own], k_peers, 0, 0)
            ).astype(LOW)


def key_grad_kernel(groups, q_ref, score_grad_ref, soft_ref, *refs):
    grad_low_refs, (dk_ref, dv_ref) = refs[: len(groups)], refs[len(groups) :]
    for (first, last), grad_low_ref in zip(groups, grad_low_refs):
        for head in range(first, last):
            cols = head_cols(head)
            dk_ref[:, cols] = contract(score_grad_ref[:, cols], q_ref[:, cols], 1, 0)
            dv_ref[:, cols] = contract(
                soft_ref[:, cols], grad_low_ref[:, head_cols(head - first)], 1, 1
            )


def finish_kernel(top_step, groups, gain_ref, place_ref, dk_ref, dv_ref, *refs):
    dk_out_ref, dv_out_ref, gain_out_ref = refs[PEERS * len(groups) :]
    gain_out_ref[...] = gain_ref[...]
    tokens = dk_ref.shape[0]
    picked = sum(picked_counts(tokens, top_step))
    for place, (first, last) in enumerate(groups):
        part_refs = refs[place * PEERS : (place + 1) * PEERS]
        for head in range(first, last):
            cols = head_cols(head)
            own = head_cols(head - first)
            total = sum(part_ref[:, own].astype(WIDE) for part_ref in part_refs).astype(LOW)
            both = jnp.concatenate([total[:picked], total[picked:]], 1)
            placed = contract(place_ref[:, pl.ds(head * HEAD_DIM, picked)], both, 1, 0)
            dk_out_ref[0, :, cols] = (dk_ref[:, cols] + placed[:, :HEAD_DIM]).astype(LOW)
            dv_out_ref[0, :, cols] = (dv_ref[:, cols] + placed[:, HEAD_DIM:]).astype(LOW)


def across(block, axis, distance):
    route = [(place, place ^ distance) for place in range(lax.axis_size(axis))]
    return lax.ppermute(block, axis, route)


def to_peers(blocks):
    farthest_first = [
        across(blocks[distance - 1], "ctx", distance) for distance in range(PEERS, 0, -1)
    ]
    return farthest_first[::-1]


def call(kernel, name, operands, results, microseconds, **options):
    options.setdefault(
        "in_specs", [SMEM_SPEC if block.dtype == jnp.int32 else VMEM_SPEC for block in operands]
    )
    options.setdefault(
        "compiler_params", pltpu.CompilerParams(vmem_limit_bytes=16 * 1024 * 1024)
    )
    return pl.pallas_call(
        kernel,
        out_shape=results,
        out_specs=[VMEM_SPEC] * len(results),
        cost_estimate=pl.CostEstimate(
            flops=int(microseconds * 10**9), bytes_accessed=0, transcendentals=0
        ),
        name=name,
        **options,
    )(*operands)


def one_segment_shards(queries, keys, values, grad_y, out_gain, offsets):
    tokens, width = queries.shape[1:]
    heads = width // HEAD_DIM
    top_step = lax.axis_size("ctx")
    picked = sum(picked_counts(tokens, top_step))
    shape = jax.ShapeDtypeStruct
    row_block = shape((1, tokens, width), LOW)
    low_block = shape((tokens, width), LOW)
    wide_block = shape((tokens, width), WIDE)
    groups = HEAD_GROUPS
    widths = [(last - first) * HEAD_DIM for first, last in groups]
    bind = functools.partial
    gain_row = out_gain.reshape(1, width)
    packed = call(
        bind(pack_kernel, top_step, groups),
        "pack",
        (offsets, keys, values),
        [shape((2 * picked, group_width), LOW) for group_width in widths],
        1,
        in_specs=[SMEM_SPEC, HBM_SPEC, HBM_SPEC],
        compiler_params=pltpu.CompilerParams(vmem_limit_bytes=PACK_VMEM),
        scratch_shapes=[
            pltpu.VMEM((tokens, width), LOW),
            pltpu.VMEM((tokens, width), LOW),
            pltpu.SemaphoreType.DMA((2, LOAD_PIECES)),
        ],
    )
    packed_peers = [to_peers([block] * PEERS) for block in packed]
    row_scratch, gain_scratch = pltpu.VMEM((tokens, width), LOW), pltpu.VMEM((1, width), WIDE)
    expo, base_out, grad_norm, q_copy, inv_gain, place, base_stats = call(
        bind(base_kernel, top_step),
        "base",
        (offsets, queries, keys, values, grad_y, gain_row),
        [
            low_block,
            wide_block,
            wide_block,
            low_block,
            shape((1, width), WIDE),
            low_block,
            shape((4 * STATS_ROWS, tokens), WIDE),
        ],
        2,
        in_specs=[SMEM_SPEC] + [HBM_SPEC] * 5,
        scratch_shapes=[row_scratch] * 4 + [gain_scratch, pltpu.SemaphoreType.DMA((5,))],
    )
    kept, returned, gain_parts, grad_lows = [], [], [], []
    for (first, last), group_width, peers in zip(groups, widths, packed_peers):
        gain_part, normed, grad_low, score_grad, stats, *parts = call(
            bind(attend_kernel, top_step, first, last),
            "attend",
            (q_copy, base_out, grad_norm, inv_gain, base_stats, *peers),
            [
                shape((1, group_width), WIDE),
                shape((tokens, group_width), WIDE),
                shape((tokens, group_width), LOW),
                shape((PEERS * picked, group_width), LOW),
                shape((2 * STATS_ROWS, tokens), WIDE),
            ]
            + [shape((2 * picked, group_width), LOW)] * PEERS,
            last - first,
        )
        gain_parts.append(gain_part)
        grad_lows.append(grad_low)
        kept += [normed, grad_low, score_grad, stats, *peers]
        returned += to_peers(parts)[::-1]
    gain_part = jnp.concatenate(gain_parts, 1) if len(groups) > 1 else gain_parts[0]
    gain_grad = gain_part + across(gain_part, "ctx", 2)
    gain_grad = gain_grad + across(gain_grad, "dp", 1)
    gain_rest = across(gain_grad, "ctx", 1)
    attended, query_grad, score_grad, soft = call(
        bind(query_grad_kernel, top_step, groups),
        "query_grad",
        (keys, values, gain_row, expo, *kept),
        [row_block, row_block, low_block, low_block],
        20,
        in_specs=[HBM_SPEC] * 3 + [VMEM_SPEC] * (1 + len(kept)),
        scratch_shapes=[row_scratch] * 2 + [gain_scratch, pltpu.SemaphoreType.DMA((3,))],
    )
    dk_base, dv_base = call(
        bind(key_grad_kernel, groups),
        "key_grad",
        (q_copy, score_grad, soft, *grad_lows),
        [wide_block, wide_block],
        20,
    )
    key_grad, value_grad, gain_grad = call(
        bind(finish_kernel, top_step, groups),
        "finish",
        (gain_grad, place, dk_base, dv_base, *returned),
        [row_block, row_block, shape((1, width), WIDE)],
        1,
    )
    gain_grad = (gain_grad + gain_rest).reshape(width)
    return attended, query_grad, key_grad, value_grad, gain_grad


def solution(mesh):
    in_specs = (
        P("dp", "ctx", "head"),
        P("dp", "ctx", "head"),
        P("dp", "ctx", "head"),
        P("dp", "ctx", "head"),
        P("head"),
        P(None, "head"),
    )
    out_specs = (
        P("dp", "ctx", "head"),
        P("dp", "ctx", "head"),
        P("dp", "ctx", "head"),
        P("dp", "ctx", "head"),
        P("head"),
    )
    body = one_segment_shards if mesh.shape["ctx"] == SPAN else general_shards
    return jax.shard_map(body, mesh=mesh, in_specs=in_specs, out_specs=out_specs, check_vma=False)
```

```python
import functools
import math

import jax
import jax.numpy as jnp
from jax import lax
from jax.experimental import pallas as pl
from jax.experimental.pallas import tpu as pltpu
from jax.sharding import PartitionSpec as P

HEAD_DIM = 128
SPAN = 4
R1 = 8


EPS = 1e-06


def swapped(block, axis, bit):
    count = lax.axis_size(axis)
    route = []
    for low in range(count):
        high = low | 1 << bit
        if high != low and high < count:
            route += [(low, high), (high, low)]
    return lax.ppermute(block, axis, route)


def pick_rows(source_rows, dilation, shifts):
    row_count, head_count, head_width = source_rows.shape
    grouped = source_rows.reshape(row_count // dilation, dilation, head_count, head_width)
    hit_mask = jnp.arange(dilation, dtype=jnp.int32).reshape(1, dilation, 1, 1) == shifts.reshape(
        1, 1, head_count, 1
    )
    chosen = jnp.where(hit_mask, grouped, jnp.zeros((), source_rows.dtype))
    return jnp.sum(chosen, axis=1, dtype=source_rows.dtype)


def place_rows(row_values, dilation, shifts):
    row_count, head_count, head_width = row_values.shape
    hit_mask = jnp.arange(dilation, dtype=jnp.int32).reshape(1, dilation, 1, 1) == shifts.reshape(
        1, 1, head_count, 1
    )
    spread = jnp.where(hit_mask, row_values[:, None], jnp.zeros((), row_values.dtype))
    return spread.reshape(row_count * dilation, head_count, head_width)


def level_scores(q_rows, k_rows):
    score_scale = 1.0 / math.sqrt(q_rows.shape[-1])
    return (
        jnp.einsum("qhe,khe->hqk", q_rows, k_rows, preferred_element_type=jnp.float32) * score_scale
    )


def attend(q_rows, k_rows, v_rows):
    scores = level_scores(q_rows, k_rows)
    row_max = jnp.max(scores, axis=-1, keepdims=True)
    log_total = row_max[..., 0] + jnp.log(jnp.sum(jnp.exp(scores - row_max), axis=-1))
    soft_rows = jnp.exp(scores - log_total[..., None]).astype(jnp.bfloat16)
    level_out = jnp.einsum("hqk,khe->qhe", soft_rows, v_rows, preferred_element_type=jnp.float32)
    return (level_out, log_total.T)


def score_grads(q_rows, k_rows, v_rows, log_total, grad_low, row_shift):
    score_scale = 1.0 / math.sqrt(q_rows.shape[-1])
    scores = level_scores(q_rows, k_rows)
    exact_soft = jnp.exp(scores - log_total.T[..., None])
    prob_grad = jnp.einsum("qhe,khe->hqk", grad_low, v_rows, preferred_element_type=jnp.float32)
    score_grad = (exact_soft * (prob_grad + row_shift.T[..., None]) * score_scale).astype(
        jnp.bfloat16
    )
    return (score_grad, exact_soft.astype(jnp.bfloat16))


def key_parts(score_grad, soft_low, q_rows, grad_low):
    k_part = jnp.einsum("hqk,qhe->khe", score_grad, q_rows, preferred_element_type=jnp.float32)
    v_part = jnp.einsum("hqk,qhe->khe", soft_low, grad_low, preferred_element_type=jnp.float32)
    return (k_part, v_part)


def query_part(score_grad, k_rows):
    return jnp.einsum("hqk,khe->qhe", score_grad, k_rows, preferred_element_type=jnp.float32)


def general_shards(queries, keys, values, grad_y, out_gain, offsets):
    tokens = queries.shape[1]
    flat_width = queries.shape[2]
    head_count = flat_width // HEAD_DIM
    row_shape = (tokens, head_count, HEAD_DIM)
    q_own = queries[0].reshape(row_shape)
    k_own = keys[0].reshape(row_shape)
    v_own = values[0].reshape(row_shape)
    ctx_size = lax.axis_size("ctx")
    span_bits = SPAN.bit_length() - 1
    my_place = lax.axis_index("ctx")
    mid_shift = offsets[0]
    top_shift = offsets[1]
    positions = jnp.arange(tokens, dtype=jnp.int32)
    mid_hit = (positions % R1)[:, None] == mid_shift[None, :]
    top_hit = (positions % ctx_size)[:, None] == top_shift[None, :]
    mid_q = pick_rows(q_own, R1, mid_shift)
    mid_k = pick_rows(k_own, R1, mid_shift)
    mid_v = pick_rows(v_own, R1, mid_shift)
    top_q = pick_rows(q_own, ctx_size, top_shift)
    top_k = pick_rows(k_own, ctx_size, top_shift)
    top_v = pick_rows(v_own, ctx_size, top_shift)
    mid_keys = mid_k.reshape(-1, flat_width)
    mid_vals = mid_v.reshape(-1, flat_width)
    top_keys = top_k.reshape(-1, flat_width)
    top_vals = top_v.reshape(-1, flat_width)

    def append_peer(mine, received, level_bit):
        upper_side = my_place >> level_bit & 1 == 1
        return jnp.where(
            upper_side, jnp.concatenate([received, mine], 0), jnp.concatenate([mine, received], 0)
        )

    for level_bit in range(span_bits):
        received = swapped((mid_keys, mid_vals), "ctx", level_bit)
        mid_keys = append_peer(mid_keys, received[0], level_bit)
        mid_vals = append_peer(mid_vals, received[1], level_bit)
    top_keys, top_vals = (
        lax.all_gather(top_keys, "ctx", axis=0, tiled=True),
        lax.all_gather(top_vals, "ctx", axis=0, tiled=True),
    )
    mid_keys = mid_keys.reshape(-1, head_count, HEAD_DIM)
    mid_vals = mid_vals.reshape(-1, head_count, HEAD_DIM)
    top_keys = top_keys.reshape(-1, head_count, HEAD_DIM)
    top_vals = top_vals.reshape(-1, head_count, HEAD_DIM)
    base_out, base_total = attend(q_own, k_own, v_own)
    mid_out, mid_total = attend(mid_q, mid_keys, mid_vals)
    top_out, top_total = attend(top_q, top_keys, top_vals)
    mid_full = place_rows(mid_total[..., None], R1, mid_shift)[..., 0]
    top_full = place_rows(top_total[..., None], ctx_size, top_shift)[..., 0]
    row_max = jnp.maximum(base_total, jnp.where(mid_hit, mid_full, base_total))
    row_max = jnp.maximum(row_max, jnp.where(top_hit, top_full, base_total))
    base_expo = jnp.exp(base_total - row_max)
    mid_expo = jnp.where(mid_hit, jnp.exp(mid_full - row_max), 0.0)
    top_expo = jnp.where(top_hit, jnp.exp(top_full - row_max), 0.0)
    denom = base_expo + mid_expo + top_expo
    base_share = base_expo / denom
    mid_share = mid_expo / denom
    top_share = top_expo / denom
    attn = (
        base_share[..., None] * base_out
        + mid_share[..., None] * place_rows(mid_out, R1, mid_shift)
        + top_share[..., None] * place_rows(top_out, ctx_size, top_shift)
    )
    inv_rms = lax.rsqrt(jnp.mean(attn * attn, axis=-1, keepdims=True) + EPS)
    normed = attn * inv_rms
    gain_rows = out_gain.reshape(head_count, HEAD_DIM)
    attended = (normed * gain_rows).astype(jnp.bfloat16).reshape(1, tokens, flat_width)
    grad_full = grad_y[0].reshape(row_shape).astype(jnp.float32)
    gain_part = jnp.sum(grad_full * normed, axis=0).reshape(flat_width)
    gain_grad = lax.psum(gain_part, ("dp", "ctx"))
    grad_norm = grad_full * gain_rows
    grad_attn = inv_rms * (
        grad_norm - normed * jnp.mean(grad_norm * normed, axis=-1, keepdims=True)
    )
    inner = jnp.sum(grad_attn * attn, axis=-1)
    base_low = (base_share[..., None] * grad_attn).astype(jnp.bfloat16)
    base_shift = -(base_share * inner)
    base_grad, base_soft = score_grads(q_own, k_own, v_own, base_total, base_low, base_shift)
    base_dq = query_part(base_grad, k_own)
    base_dk, base_dv = key_parts(base_grad, base_soft, q_own, base_low)
    mid_sel = pick_rows(mid_share[..., None], R1, mid_shift)[..., 0]
    mid_low = (mid_sel[..., None] * pick_rows(grad_attn, R1, mid_shift)).astype(jnp.bfloat16)
    mid_row_shift = -(mid_sel * pick_rows(inner[..., None], R1, mid_shift)[..., 0])
    mid_grad, mid_soft = score_grads(mid_q, mid_keys, mid_vals, mid_total, mid_low, mid_row_shift)
    mid_dq = query_part(mid_grad, mid_keys)
    mid_dk, mid_dv = key_parts(mid_grad, mid_soft, mid_q, mid_low)
    mid_dk = mid_dk.reshape(-1, flat_width)
    mid_dv = mid_dv.reshape(-1, flat_width)
    for level_bit in reversed(range(span_bits)):
        half_rows = mid_dk.shape[0] // 2
        upper_side = my_place >> level_bit & 1 == 1
        keep_k = jnp.where(upper_side, mid_dk[half_rows:], mid_dk[:half_rows])
        keep_v = jnp.where(upper_side, mid_dv[half_rows:], mid_dv[:half_rows])
        send_k = jnp.where(upper_side, mid_dk[:half_rows], mid_dk[half_rows:])
        send_v = jnp.where(upper_side, mid_dv[:half_rows], mid_dv[half_rows:])
        received = (
            swapped(send_k.astype(jnp.bfloat16), "ctx", level_bit).astype(send_k.dtype),
            swapped(send_v.astype(jnp.bfloat16), "ctx", level_bit).astype(send_v.dtype),
        )
        mid_dk = keep_k + received[0]
        mid_dv = keep_v + received[1]
    mid_dk = mid_dk.reshape(-1, head_count, HEAD_DIM)
    mid_dv = mid_dv.reshape(-1, head_count, HEAD_DIM)
    top_sel = pick_rows(top_share[..., None], ctx_size, top_shift)[..., 0]
    top_low = (top_sel[..., None] * pick_rows(grad_attn, ctx_size, top_shift)).astype(jnp.bfloat16)
    top_row_shift = -(top_sel * pick_rows(inner[..., None], ctx_size, top_shift)[..., 0])
    top_grad, top_soft = score_grads(top_q, top_keys, top_vals, top_total, top_low, top_row_shift)
    top_dq = query_part(top_grad, top_keys)
    gathered_dk, gathered_dv = key_parts(top_grad, top_soft, top_q, top_low)
    summed = (
        lax.psum_scatter(
            gathered_dk.reshape(-1, flat_width), "ctx", scatter_dimension=0, tiled=True
        ),
        lax.psum_scatter(
            gathered_dv.reshape(-1, flat_width), "ctx", scatter_dimension=0, tiled=True
        ),
    )
    top_dk = summed[0].reshape(-1, head_count, HEAD_DIM)
    top_dv = summed[1].reshape(-1, head_count, HEAD_DIM)
    query_grad = (
        base_dq + place_rows(mid_dq, R1, mid_shift) + place_rows(top_dq, ctx_size, top_shift)
    )
    key_grad = base_dk + place_rows(mid_dk, R1, mid_shift) + place_rows(top_dk, ctx_size, top_shift)
    value_grad = (
        base_dv + place_rows(mid_dv, R1, mid_shift) + place_rows(top_dv, ctx_size, top_shift)
    )
    out_shape = (1, tokens, flat_width)
    return (
        attended,
        query_grad.astype(jnp.bfloat16).reshape(out_shape),
        key_grad.astype(jnp.bfloat16).reshape(out_shape),
        value_grad.astype(jnp.bfloat16).reshape(out_shape),
        gain_grad,
    )


VMEM_SPEC = pl.BlockSpec(memory_space=pltpu.VMEM)
SMEM_SPEC = pl.BlockSpec(memory_space=pltpu.SMEM)
HBM_SPEC = pl.BlockSpec(memory_space=pltpu.HBM)
PEERS = SPAN - 1
STATS_ROWS = 8
NEVER = -1e30
LOW = jnp.bfloat16
WIDE = jnp.float32
HEAD_GROUPS = ((0, 5),)
PACK_VMEM = 65408 * 1024


def contract(left, right, left_dim, right_dim):
    return lax.dot_general(
        left, right, (((left_dim,), (right_dim,)), ((), ())), preferred_element_type=WIDE
    )


def head_cols(head):
    return pl.ds(head * HEAD_DIM, HEAD_DIM)


def picked_counts(tokens, top_step):
    return tokens // top_step, tokens // R1


def pick_matrix(offsets_ref, head, tokens, top_step, picked_axis):
    top_rows, mid_rows = picked_counts(tokens, top_step)
    shape = (top_rows + mid_rows, tokens) if picked_axis == 0 else (tokens, top_rows + mid_rows)
    row = lax.broadcasted_iota(jnp.int32, shape, picked_axis)
    position = lax.broadcasted_iota(jnp.int32, shape, 1 - picked_axis)
    wanted = jnp.where(
        row < top_rows,
        row * top_step + offsets_ref[1, head],
        (row - top_rows) * R1 + offsets_ref[0, head],
    )
    return jnp.where(position == wanted, 1.0, 0.0).astype(LOW)


def stacked(refs, rows, cols):
    return jnp.concatenate([ref[rows, cols] for ref in refs], 0)


def pack_kernel(top_step, groups, offsets_ref, k_ref, v_ref, *packed_refs):
    tokens, width = k_ref.shape[1:]
    picked = sum(picked_counts(tokens, top_step))
    every = [head_cols(head) for head in range(width // HEAD_DIM)]
    picks = [
        pick_matrix(offsets_ref, head, tokens, top_step, 0) for head in range(width // HEAD_DIM)
    ]
    both = [jnp.concatenate([k_ref[0, :, cols], v_ref[0, :, cols]], 1) for cols in every]
    rows = [contract(pick, block, 1, 0).astype(LOW) for pick, block in zip(picks, both)]
    for (first, last), packed_ref in zip(groups, packed_refs):
        for head in range(first, last):
            packed_ref[:picked, head_cols(head - first)] = rows[head][:, :HEAD_DIM]
            packed_ref[picked:, head_cols(head - first)] = rows[head][:, HEAD_DIM:]


def fetch(sources, held, sems):
    copies = [
        pltpu.make_async_copy(source.at[0] if len(source.shape) == 3 else source, block, sems.at[i])
        for i, (source, block) in enumerate(zip(sources, held))
    ]
    for copy in copies:
        copy.start()
    for copy in copies:
        copy.wait()


def base_kernel(top_step, offsets_ref, *refs):
    sources, refs = refs[:5], refs[5:]
    held, sems = refs[-6:-1], refs[-1]
    expo_ref, out_ref, grad_norm_ref, q_copy_ref, inv_gain_ref, place_ref, stats_ref = refs[:-6]
    fetch(sources, held, sems)
    q_ref, k_ref, v_ref, grad_ref, gain_ref = held
    tokens, width = q_ref.shape
    picked = sum(picked_counts(tokens, top_step))
    score_scale = 1.0 / math.sqrt(HEAD_DIM)
    key_row = lax.broadcasted_iota(jnp.int32, (tokens, 1), 0)
    query_col = lax.broadcasted_iota(jnp.int32, (1, tokens), 1)
    q_copy_ref[...] = q_ref[...]
    inv_gain_ref[...] = 1.0 / gain_ref[...]
    for head in range(width // HEAD_DIM):
        cols = head_cols(head)
        times = 1.0
        for level, step in ((0, R1), (1, top_step)):
            offset = offsets_ref[level, head]
            hit_row = jnp.where(key_row % step == offset, 1.0, 0.0)
            hit_col = jnp.where(query_col % step == offset, 1.0, 0.0)
            times = times + hit_row * hit_col
            bias_row = (2 + level) * STATS_ROWS + head
            stats_ref[bias_row : bias_row + 1, :] = (1.0 - hit_col) * NEVER
        place_ref[:, pl.ds(head * HEAD_DIM, picked)] = pick_matrix(
            offsets_ref, head, tokens, top_step, 1
        )
        scores = contract(k_ref[:, cols], q_ref[:, cols], 1, 1) * score_scale
        top_score = jnp.max(scores, axis=0, keepdims=True)
        expo = times * jnp.exp(scores - top_score)
        expo_low = expo.astype(LOW)
        expo_ref[:, cols] = expo_low
        out_ref[:, cols] = contract(v_ref[:, cols], expo_low, 0, 0)
        stats_ref[head : head + 1, :] = top_score
        stats_ref[STATS_ROWS + head : STATS_ROWS + head + 1, :] = jnp.sum(
            expo, axis=0, keepdims=True
        )
        grad_norm_ref[:, cols] = (grad_ref[:, cols].astype(WIDE) * gain_ref[:, cols]).T


def attend_kernel(
    top_step,
    first,
    last,
    q_ref,
    base_out_ref,
    grad_norm_ref,
    inv_gain_ref,
    base_stats_ref,
    *refs,
):
    packed_refs = refs[:PEERS]
    gain_part_ref, normed_ref, grad_low_ref, score_grad_ref, stats_ref = refs[PEERS : PEERS + 5]
    part_refs = refs[PEERS + 5 :]
    tokens = q_ref.shape[0]
    top_rows, mid_rows = picked_counts(tokens, top_step)
    picked = top_rows + mid_rows
    score_scale = 1.0 / math.sqrt(HEAD_DIM)
    ones = jnp.ones((STATS_ROWS, tokens), LOW)
    heads = range(last - first)
    every = [head_cols(head) for head in range(first, last)]
    own = [head_cols(head) for head in heads]

    def stat(block, head):
        row = block * STATS_ROWS + first + head
        return base_stats_ref[row : row + 1, :]

    q_rows = [q_ref[:, cols] for cols in every]
    k_peers = [stacked(packed_refs, pl.ds(0, picked), cols) for cols in own]
    v_peers = [stacked(packed_refs, pl.ds(picked, picked), cols) for cols in own]
    products = [contract(k_peers[head], q_rows[head], 1, 1) for head in heads]
    expos, factors, inv_totals = [], [], []
    for head in heads:
        bias = jnp.concatenate(
            [
                jnp.broadcast_to(stat(3, head), (top_rows, tokens)),
                jnp.broadcast_to(stat(2, head), (mid_rows, tokens)),
            ]
            * PEERS,
            0,
        )
        scores = products[head] * score_scale + bias
        top_score = jnp.maximum(stat(0, head), jnp.max(scores, axis=0, keepdims=True))
        expos.append(jnp.exp(scores - top_score))
        factors.append(jnp.exp(stat(0, head) - top_score))
    for head in heads:
        total = factors[head] * stat(1, head) + jnp.sum(expos[head], axis=0, keepdims=True)
        inv_totals.append(1.0 / total)
        factors[head] = factors[head] * inv_totals[head]
        stats_ref[head : head + 1, :] = factors[head]
    softs = [expos[head] * inv_totals[head] for head in heads]
    soft_lows = [soft.astype(LOW) for soft in softs]
    mixed = [contract(v_peers[head], soft_lows[head], 0, 0) for head in heads]
    grad_lows, inners, gain_products = [], [], []
    for head in heads:
        attn = factors[head] * base_out_ref[:, every[head]] + mixed[head]
        inv_rms = lax.rsqrt(jnp.mean(attn * attn, axis=0, keepdims=True) + EPS)
        normed = attn * inv_rms
        normed_ref[:, own[head]] = normed
        grad_norm = grad_norm_ref[:, every[head]]
        product = grad_norm * normed
        gain_products.append(product)
        grad_attn = inv_rms * (grad_norm - normed * jnp.mean(product, axis=0, keepdims=True))
        inners.append(jnp.sum(grad_attn * attn, axis=0, keepdims=True))
        stats_ref[STATS_ROWS + head : STATS_ROWS + head + 1, :] = inners[head]
        grad_lows.append(grad_attn.astype(LOW))
        grad_low_ref[:, own[head]] = grad_lows[head]
    prob_grads = [contract(v_peers[head], grad_lows[head], 1, 0) for head in heads]
    dv_peers = [contract(soft_lows[head], grad_lows[head], 1, 1).astype(LOW) for head in heads]
    score_grads = [
        (softs[head] * (prob_grads[head] - inners[head]) * score_scale).astype(LOW)
        for head in heads
    ]
    dk_peers = [contract(score_grads[head], q_rows[head], 1, 0).astype(LOW) for head in heads]
    for head in heads:
        score_grad_ref[:, own[head]] = score_grads[head]
        product_high = gain_products[head].astype(LOW)
        product_rest = (gain_products[head] - product_high.astype(WIDE)).astype(LOW)
        gain_rows = contract(ones, product_high, 1, 1) + contract(ones, product_rest, 1, 1)
        gain_part_ref[:, own[head]] = gain_rows[:1] * inv_gain_ref[:, every[head]]
        for place, part_ref in enumerate(part_refs):
            start = place * picked
            part_ref[:picked, own[head]] = dk_peers[head][start : start + picked]
            part_ref[picked:, own[head]] = dv_peers[head][start : start + picked]


def query_grad_kernel(top_step, groups, *refs):
    sources, expo_ref, refs = refs[:3], refs[3], refs[4:]
    held, sems = refs[-4:-1], refs[-1]
    per_group = 4 + PEERS
    group_refs = refs[: per_group * len(groups)]
    attended_ref, dq_ref, score_grad_ref, soft_ref = refs[per_group * len(groups) : -4]
    fetch(sources, held, sems)
    k_ref, v_ref, gain_ref = held
    picked = sum(picked_counts(k_ref.shape[0], top_step))
    score_scale = 1.0 / math.sqrt(HEAD_DIM)
    for place, (first, last) in enumerate(groups):
        normed_ref, grad_low_ref, peer_score_grad_ref, stats_ref, *packed_refs = group_refs[
            place * per_group : (place + 1) * per_group
        ]
        for head in range(first, last):
            cols = head_cols(head)
            own = head_cols(head - first)
            attended_ref[0, :, cols] = (normed_ref[:, own].T * gain_ref[:, cols]).astype(LOW)
            k_peers = stacked(packed_refs, pl.ds(0, picked), own)
            base_factor = stats_ref[head - first : head - first + 1, :]
            inner = stats_ref[STATS_ROWS + head - first : STATS_ROWS + head - first + 1, :]
            soft = expo_ref[:, cols].astype(WIDE) * base_factor
            prob_grad = contract(v_ref[:, cols], grad_low_ref[:, own], 1, 0)
            score_grad = (soft * (prob_grad - inner) * score_scale).astype(LOW)
            score_grad_ref[:, cols] = score_grad
            soft_ref[:, cols] = soft.astype(LOW)
            dq_ref[0, :, cols] = (
                contract(score_grad, k_ref[:, cols], 0, 0)
                + contract(peer_score_grad_ref[:, own], k_peers, 0, 0)
            ).astype(LOW)


def key_grad_kernel(groups, q_ref, score_grad_ref, soft_ref, *refs):
    grad_low_refs, (dk_ref, dv_ref) = refs[: len(groups)], refs[len(groups) :]
    for (first, last), grad_low_ref in zip(groups, grad_low_refs):
        for head in range(first, last):
            cols = head_cols(head)
            dk_ref[:, cols] = contract(score_grad_ref[:, cols], q_ref[:, cols], 1, 0)
            dv_ref[:, cols] = contract(
                soft_ref[:, cols], grad_low_ref[:, head_cols(head - first)], 1, 1
            )


def finish_kernel(groups, place_ref, dk_ref, dv_ref, *refs):
    dk_out_ref, dv_out_ref = refs[PEERS * len(groups) :]
    picked = refs[0].shape[0] // 2
    everyone = []
    for place, (first, last) in enumerate(groups):
        part_refs = refs[place * PEERS : (place + 1) * PEERS]
        for head in range(first, last):
            own = head_cols(head - first)
            total = sum(part_ref[:, own].astype(WIDE) for part_ref in part_refs).astype(LOW)
            everyone.append(jnp.concatenate([total[:picked], total[picked:]], 1))
    placed = [
        contract(place_ref[:, pl.ds(head * HEAD_DIM, picked)], both, 1, 0)
        for head, both in enumerate(everyone)
    ]
    for head, rows in enumerate(placed):
        cols = head_cols(head)
        dk_out_ref[0, :, cols] = (dk_ref[:, cols] + rows[:, :HEAD_DIM]).astype(LOW)
        dv_out_ref[0, :, cols] = (dv_ref[:, cols] + rows[:, HEAD_DIM:]).astype(LOW)


def across(block, axis, distance):
    route = [(place, place ^ distance) for place in range(lax.axis_size(axis))]
    return lax.ppermute(block, axis, route)


def to_peers(blocks):
    farthest_first = [
        across(blocks[distance - 1], "ctx", distance) for distance in range(PEERS, 0, -1)
    ]
    return farthest_first[::-1]


def call(kernel, name, operands, results, microseconds, **options):
    options.setdefault(
        "in_specs", [SMEM_SPEC if block.dtype == jnp.int32 else VMEM_SPEC for block in operands]
    )
    options.setdefault(
        "compiler_params", pltpu.CompilerParams(vmem_limit_bytes=16 * 1024 * 1024)
    )
    return pl.pallas_call(
        kernel,
        out_shape=results,
        out_specs=[VMEM_SPEC] * len(results),
        cost_estimate=pl.CostEstimate(
            flops=int(microseconds * 10**9), bytes_accessed=0, transcendentals=0
        ),
        name=name,
        **options,
    )(*operands)


def one_segment_shards(queries, keys, values, grad_y, out_gain, offsets):
    tokens, width = queries.shape[1:]
    heads = width // HEAD_DIM
    top_step = lax.axis_size("ctx")
    picked = sum(picked_counts(tokens, top_step))
    shape = jax.ShapeDtypeStruct
    row_block = shape((1, tokens, width), LOW)
    low_block = shape((tokens, width), LOW)
    wide_block = shape((tokens, width), WIDE)
    groups = HEAD_GROUPS
    widths = [(last - first) * HEAD_DIM for first, last in groups]
    bind = functools.partial
    gain_row = out_gain.reshape(1, width)
    packed = call(
        bind(pack_kernel, top_step, groups),
        "pack",
        (offsets, keys, values),
        [shape((2 * picked, group_width), LOW) for group_width in widths],
        1,
        compiler_params=pltpu.CompilerParams(vmem_limit_bytes=PACK_VMEM),
    )
    packed_peers = [to_peers([block] * PEERS) for block in packed]
    row_scratch, gain_scratch = pltpu.VMEM((tokens, width), LOW), pltpu.VMEM((1, width), WIDE)
    expo, base_out, grad_norm, q_copy, inv_gain, place, base_stats = call(
        bind(base_kernel, top_step),
        "base",
        (offsets, queries, keys, values, grad_y, gain_row),
        [
            low_block,
            wide_block,
            wide_block,
            low_block,
            shape((1, width), WIDE),
            low_block,
            shape((4 * STATS_ROWS, tokens), WIDE),
        ],
        2,
        in_specs=[SMEM_SPEC] + [HBM_SPEC] * 5,
        scratch_shapes=[row_scratch] * 4 + [gain_scratch, pltpu.SemaphoreType.DMA((5,))],
    )
    kept, returned, gain_parts, grad_lows = [], [], [], []
    for (first, last), group_width, peers in zip(groups, widths, packed_peers):
        gain_part, normed, grad_low, score_grad, stats, *parts = call(
            bind(attend_kernel, top_step, first, last),
            "attend",
            (q_copy, base_out, grad_norm, inv_gain, base_stats, *peers),
            [
                shape((1, group_width), WIDE),
                shape((tokens, group_width), WIDE),
                shape((tokens, group_width), LOW),
                shape((PEERS * picked, group_width), LOW),
                shape((2 * STATS_ROWS, tokens), WIDE),
            ]
            + [shape((2 * picked, group_width), LOW)] * PEERS,
            last - first,
        )
        gain_parts.append(gain_part)
        grad_lows.append(grad_low)
        kept += [normed, grad_low, score_grad, stats, *peers]
        returned += to_peers(parts)[::-1]
    gain_part = jnp.concatenate(gain_parts, 1) if len(groups) > 1 else gain_parts[0]
    gain_grad = gain_part + across(gain_part, "ctx", 2)
    gain_grad = gain_grad + across(gain_grad, "dp", 1)
    gain_grad = (gain_grad + across(gain_grad, "ctx", 1)).reshape(width)
    attended, query_grad, score_grad, soft = call(
        bind(query_grad_kernel, top_step, groups),
        "query_grad",
        (keys, values, gain_row, expo, *kept),
        [row_block, row_block, low_block, low_block],
        20,
        in_specs=[HBM_SPEC] * 3 + [VMEM_SPEC] * (1 + len(kept)),
        scratch_shapes=[row_scratch] * 2 + [gain_scratch, pltpu.SemaphoreType.DMA((3,))],
    )
    dk_base, dv_base = call(
        bind(key_grad_kernel, groups),
        "key_grad",
        (q_copy, score_grad, soft, *grad_lows),
        [wide_block, wide_block],
        20,
    )
    key_grad, value_grad = call(
        bind(finish_kernel, groups),
        "finish",
        (place, dk_base, dv_base, *returned),
        [row_block, row_block],
        1,
    )
    return attended, query_grad, key_grad, value_grad, gain_grad


def solution(mesh):
    in_specs = (
        P("dp", "ctx", "head"),
        P("dp", "ctx", "head"),
        P("dp", "ctx", "head"),
        P("dp", "ctx", "head"),
        P("head"),
        P(None, "head"),
    )
    out_specs = (
        P("dp", "ctx", "head"),
        P("dp", "ctx", "head"),
        P("dp", "ctx", "head"),
        P("dp", "ctx", "head"),
        P("head"),
    )
    body = one_segment_shards if mesh.shape["ctx"] == SPAN else general_shards
    return jax.shard_map(body, mesh=mesh, in_specs=in_specs, out_specs=out_specs, check_vma=False)
```

```python
import functools
import math

import jax
import jax.numpy as jnp
from jax import lax
from jax.experimental import pallas as pl
from jax.experimental.pallas import tpu as pltpu
from jax.sharding import PartitionSpec as P

HEAD_DIM = 128
SPAN = 4
R1 = 8


EPS = 1e-06


def swapped(block, axis, bit):
    count = lax.axis_size(axis)
    route = []
    for low in range(count):
        high = low | 1 << bit
        if high != low and high < count:
            route += [(low, high), (high, low)]
    return lax.ppermute(block, axis, route)


def pick_rows(source_rows, dilation, shifts):
    row_count, head_count, head_width = source_rows.shape
    grouped = source_rows.reshape(row_count // dilation, dilation, head_count, head_width)
    hit_mask = jnp.arange(dilation, dtype=jnp.int32).reshape(1, dilation, 1, 1) == shifts.reshape(
        1, 1, head_count, 1
    )
    chosen = jnp.where(hit_mask, grouped, jnp.zeros((), source_rows.dtype))
    return jnp.sum(chosen, axis=1, dtype=source_rows.dtype)


def place_rows(row_values, dilation, shifts):
    row_count, head_count, head_width = row_values.shape
    hit_mask = jnp.arange(dilation, dtype=jnp.int32).reshape(1, dilation, 1, 1) == shifts.reshape(
        1, 1, head_count, 1
    )
    spread = jnp.where(hit_mask, row_values[:, None], jnp.zeros((), row_values.dtype))
    return spread.reshape(row_count * dilation, head_count, head_width)


def level_scores(q_rows, k_rows):
    score_scale = 1.0 / math.sqrt(q_rows.shape[-1])
    return (
        jnp.einsum("qhe,khe->hqk", q_rows, k_rows, preferred_element_type=jnp.float32) * score_scale
    )


def attend(q_rows, k_rows, v_rows):
    scores = level_scores(q_rows, k_rows)
    row_max = jnp.max(scores, axis=-1, keepdims=True)
    log_total = row_max[..., 0] + jnp.log(jnp.sum(jnp.exp(scores - row_max), axis=-1))
    soft_rows = jnp.exp(scores - log_total[..., None]).astype(jnp.bfloat16)
    level_out = jnp.einsum("hqk,khe->qhe", soft_rows, v_rows, preferred_element_type=jnp.float32)
    return (level_out, log_total.T)


def score_grads(q_rows, k_rows, v_rows, log_total, grad_low, row_shift):
    score_scale = 1.0 / math.sqrt(q_rows.shape[-1])
    scores = level_scores(q_rows, k_rows)
    exact_soft = jnp.exp(scores - log_total.T[..., None])
    prob_grad = jnp.einsum("qhe,khe->hqk", grad_low, v_rows, preferred_element_type=jnp.float32)
    score_grad = (exact_soft * (prob_grad + row_shift.T[..., None]) * score_scale).astype(
        jnp.bfloat16
    )
    return (score_grad, exact_soft.astype(jnp.bfloat16))


def key_parts(score_grad, soft_low, q_rows, grad_low):
    k_part = jnp.einsum("hqk,qhe->khe", score_grad, q_rows, preferred_element_type=jnp.float32)
    v_part = jnp.einsum("hqk,qhe->khe", soft_low, grad_low, preferred_element_type=jnp.float32)
    return (k_part, v_part)


def query_part(score_grad, k_rows):
    return jnp.einsum("hqk,khe->qhe", score_grad, k_rows, preferred_element_type=jnp.float32)


def general_shards(queries, keys, values, grad_y, out_gain, offsets):
    tokens = queries.shape[1]
    flat_width = queries.shape[2]
    head_count = flat_width // HEAD_DIM
    row_shape = (tokens, head_count, HEAD_DIM)
    q_own = queries[0].reshape(row_shape)
    k_own = keys[0].reshape(row_shape)
    v_own = values[0].reshape(row_shape)
    ctx_size = lax.axis_size("ctx")
    span_bits = SPAN.bit_length() - 1
    my_place = lax.axis_index("ctx")
    mid_shift = offsets[0]
    top_shift = offsets[1]
    positions = jnp.arange(tokens, dtype=jnp.int32)
    mid_hit = (positions % R1)[:, None] == mid_shift[None, :]
    top_hit = (positions % ctx_size)[:, None] == top_shift[None, :]
    mid_q = pick_rows(q_own, R1, mid_shift)
    mid_k = pick_rows(k_own, R1, mid_shift)
    mid_v = pick_rows(v_own, R1, mid_shift)
    top_q = pick_rows(q_own, ctx_size, top_shift)
    top_k = pick_rows(k_own, ctx_size, top_shift)
    top_v = pick_rows(v_own, ctx_size, top_shift)
    mid_keys = mid_k.reshape(-1, flat_width)
    mid_vals = mid_v.reshape(-1, flat_width)
    top_keys = top_k.reshape(-1, flat_width)
    top_vals = top_v.reshape(-1, flat_width)

    def append_peer(mine, received, level_bit):
        upper_side = my_place >> level_bit & 1 == 1
        return jnp.where(
            upper_side, jnp.concatenate([received, mine], 0), jnp.concatenate([mine, received], 0)
        )

    for level_bit in range(span_bits):
        received = swapped((mid_keys, mid_vals), "ctx", level_bit)
        mid_keys = append_peer(mid_keys, received[0], level_bit)
        mid_vals = append_peer(mid_vals, received[1], level_bit)
    top_keys, top_vals = (
        lax.all_gather(top_keys, "ctx", axis=0, tiled=True),
        lax.all_gather(top_vals, "ctx", axis=0, tiled=True),
    )
    mid_keys = mid_keys.reshape(-1, head_count, HEAD_DIM)
    mid_vals = mid_vals.reshape(-1, head_count, HEAD_DIM)
    top_keys = top_keys.reshape(-1, head_count, HEAD_DIM)
    top_vals = top_vals.reshape(-1, head_count, HEAD_DIM)
    base_out, base_total = attend(q_own, k_own, v_own)
    mid_out, mid_total = attend(mid_q, mid_keys, mid_vals)
    top_out, top_total = attend(top_q, top_keys, top_vals)
    mid_full = place_rows(mid_total[..., None], R1, mid_shift)[..., 0]
    top_full = place_rows(top_total[..., None], ctx_size, top_shift)[..., 0]
    row_max = jnp.maximum(base_total, jnp.where(mid_hit, mid_full, base_total))
    row_max = jnp.maximum(row_max, jnp.where(top_hit, top_full, base_total))
    base_expo = jnp.exp(base_total - row_max)
    mid_expo = jnp.where(mid_hit, jnp.exp(mid_full - row_max), 0.0)
    top_expo = jnp.where(top_hit, jnp.exp(top_full - row_max), 0.0)
    denom = base_expo + mid_expo + top_expo
    base_share = base_expo / denom
    mid_share = mid_expo / denom
    top_share = top_expo / denom
    attn = (
        base_share[..., None] * base_out
        + mid_share[..., None] * place_rows(mid_out, R1, mid_shift)
        + top_share[..., None] * place_rows(top_out, ctx_size, top_shift)
    )
    inv_rms = lax.rsqrt(jnp.mean(attn * attn, axis=-1, keepdims=True) + EPS)
    normed = attn * inv_rms
    gain_rows = out_gain.reshape(head_count, HEAD_DIM)
    attended = (normed * gain_rows).astype(jnp.bfloat16).reshape(1, tokens, flat_width)
    grad_full = grad_y[0].reshape(row_shape).astype(jnp.float32)
    gain_part = jnp.sum(grad_full * normed, axis=0).reshape(flat_width)
    gain_grad = lax.psum(gain_part, ("dp", "ctx"))
    grad_norm = grad_full * gain_rows
    grad_attn = inv_rms * (
        grad_norm - normed * jnp.mean(grad_norm * normed, axis=-1, keepdims=True)
    )
    inner = jnp.sum(grad_attn * attn, axis=-1)
    base_low = (base_share[..., None] * grad_attn).astype(jnp.bfloat16)
    base_shift = -(base_share * inner)
    base_grad, base_soft = score_grads(q_own, k_own, v_own, base_total, base_low, base_shift)
    base_dq = query_part(base_grad, k_own)
    base_dk, base_dv = key_parts(base_grad, base_soft, q_own, base_low)
    mid_sel = pick_rows(mid_share[..., None], R1, mid_shift)[..., 0]
    mid_low = (mid_sel[..., None] * pick_rows(grad_attn, R1, mid_shift)).astype(jnp.bfloat16)
    mid_row_shift = -(mid_sel * pick_rows(inner[..., None], R1, mid_shift)[..., 0])
    mid_grad, mid_soft = score_grads(mid_q, mid_keys, mid_vals, mid_total, mid_low, mid_row_shift)
    mid_dq = query_part(mid_grad, mid_keys)
    mid_dk, mid_dv = key_parts(mid_grad, mid_soft, mid_q, mid_low)
    mid_dk = mid_dk.reshape(-1, flat_width)
    mid_dv = mid_dv.reshape(-1, flat_width)
    for level_bit in reversed(range(span_bits)):
        half_rows = mid_dk.shape[0] // 2
        upper_side = my_place >> level_bit & 1 == 1
        keep_k = jnp.where(upper_side, mid_dk[half_rows:], mid_dk[:half_rows])
        keep_v = jnp.where(upper_side, mid_dv[half_rows:], mid_dv[:half_rows])
        send_k = jnp.where(upper_side, mid_dk[:half_rows], mid_dk[half_rows:])
        send_v = jnp.where(upper_side, mid_dv[:half_rows], mid_dv[half_rows:])
        received = (
            swapped(send_k.astype(jnp.bfloat16), "ctx", level_bit).astype(send_k.dtype),
            swapped(send_v.astype(jnp.bfloat16), "ctx", level_bit).astype(send_v.dtype),
        )
        mid_dk = keep_k + received[0]
        mid_dv = keep_v + received[1]
    mid_dk = mid_dk.reshape(-1, head_count, HEAD_DIM)
    mid_dv = mid_dv.reshape(-1, head_count, HEAD_DIM)
    top_sel = pick_rows(top_share[..., None], ctx_size, top_shift)[..., 0]
    top_low = (top_sel[..., None] * pick_rows(grad_attn, ctx_size, top_shift)).astype(jnp.bfloat16)
    top_row_shift = -(top_sel * pick_rows(inner[..., None], ctx_size, top_shift)[..., 0])
    top_grad, top_soft = score_grads(top_q, top_keys, top_vals, top_total, top_low, top_row_shift)
    top_dq = query_part(top_grad, top_keys)
    gathered_dk, gathered_dv = key_parts(top_grad, top_soft, top_q, top_low)
    summed = (
        lax.psum_scatter(
            gathered_dk.reshape(-1, flat_width), "ctx", scatter_dimension=0, tiled=True
        ),
        lax.psum_scatter(
            gathered_dv.reshape(-1, flat_width), "ctx", scatter_dimension=0, tiled=True
        ),
    )
    top_dk = summed[0].reshape(-1, head_count, HEAD_DIM)
    top_dv = summed[1].reshape(-1, head_count, HEAD_DIM)
    query_grad = (
        base_dq + place_rows(mid_dq, R1, mid_shift) + place_rows(top_dq, ctx_size, top_shift)
    )
    key_grad = base_dk + place_rows(mid_dk, R1, mid_shift) + place_rows(top_dk, ctx_size, top_shift)
    value_grad = (
        base_dv + place_rows(mid_dv, R1, mid_shift) + place_rows(top_dv, ctx_size, top_shift)
    )
    out_shape = (1, tokens, flat_width)
    return (
        attended,
        query_grad.astype(jnp.bfloat16).reshape(out_shape),
        key_grad.astype(jnp.bfloat16).reshape(out_shape),
        value_grad.astype(jnp.bfloat16).reshape(out_shape),
        gain_grad,
    )


VMEM_SPEC = pl.BlockSpec(memory_space=pltpu.VMEM)
SMEM_SPEC = pl.BlockSpec(memory_space=pltpu.SMEM)
PEERS = SPAN - 1
OWNED = SPAN
TILE = 8
STAT_TILES = 2 * TILE
PIECES = 3
NEVER = -1e30
LOW = jnp.bfloat16
WIDE = jnp.float32
PACK_VMEM = 65408 * 1024
PLAIN_VMEM = 16 * 1024 * 1024


def contract(left, right, left_dim, right_dim):
    return lax.dot_general(
        left, right, (((left_dim,), (right_dim,)), ((), ())), preferred_element_type=WIDE
    )


def head_cols(head):
    return pl.ds(head * HEAD_DIM, HEAD_DIM)


def picked_counts(tokens, top_step):
    return tokens // top_step, tokens // R1


def pick_matrix(offsets_ref, head, tokens, top_step, picked_axis):
    top_rows, mid_rows = picked_counts(tokens, top_step)
    shape = (top_rows + mid_rows, tokens) if picked_axis == 0 else (tokens, top_rows + mid_rows)
    row = lax.broadcasted_iota(jnp.int32, shape, picked_axis)
    position = lax.broadcasted_iota(jnp.int32, shape, 1 - picked_axis)
    wanted = jnp.where(
        row < top_rows,
        row * top_step + offsets_ref[1, head],
        (row - top_rows) * R1 + offsets_ref[0, head],
    )
    return jnp.where(position == wanted, 1.0, 0.0).astype(LOW)


def slot_matrix(offset, step, slot, tokens):
    count = tokens // step
    position = lax.broadcasted_iota(jnp.int32, (tokens, tokens), 0)
    index = lax.broadcasted_iota(jnp.int32, (tokens, tokens), 1) - slot * count
    inside = (index >= 0) & (index < count)
    return jnp.where(inside & (position == index * step + offset), 1.0, 0.0).astype(LOW)


def hit_row(offset, step, tokens):
    position = lax.broadcasted_iota(jnp.int32, (1, tokens), 1)
    return jnp.where(position % step == offset, 1.0, 0.0)


def piece_rows(row):
    pieces = []
    for _ in range(PIECES):
        piece = row.astype(LOW).astype(WIDE)
        pieces.append(piece)
        row = row - piece
    return jnp.concatenate(pieces + [jnp.zeros((TILE - PIECES, row.shape[1]), WIDE)], 0)


def joined_row(rows, first):
    total = rows[first : first + 1]
    for piece in range(1, PIECES):
        total = total + rows[first + piece : first + piece + 1]
    return total


def gain_row_of(ones, product):
    high = product.astype(LOW)
    rest = (product - high.astype(WIDE)).astype(LOW)
    return (contract(ones, high, 1, 1) + contract(ones, rest, 1, 1))[:1]


def column_mean(block):
    return jnp.mean(block, axis=0, keepdims=True)


def norm_backward(attn, grad_norm):
    inv_rms = lax.rsqrt(column_mean(attn * attn) + EPS)
    normed = attn * inv_rms
    product = grad_norm * normed
    grad_attn = inv_rms * (grad_norm - normed * column_mean(product))
    inner = jnp.sum(grad_attn * attn, axis=0, keepdims=True)
    return normed, product, grad_attn.astype(LOW), inner


def nearest_first(refs):
    return [refs[0], *refs[:0:-1]]


def pack_kernel(top_step, offsets_ref, q_ref, k_ref, v_ref, grad_ref, *refs):
    payload_refs, (expo_ref, out_ref, stats_ref, held_ref) = refs[:SPAN], refs[SPAN:]
    tokens, width = q_ref.shape[1:]
    heads = range(width // HEAD_DIM)
    owned = range(OWNED)
    me = lax.axis_index("ctx")
    picked = sum(picked_counts(tokens, top_step))
    score_scale = 1.0 / math.sqrt(HEAD_DIM)
    q_rows, k_rows, v_rows, grad_rows = [
        [ref[0, :, head_cols(head)] for head in heads] for ref in (q_ref, k_ref, v_ref, grad_ref)
    ]
    picks = [pick_matrix(offsets_ref, head, tokens, top_step, 0) for head in heads]
    scores = [contract(k_rows[head], q_rows[head], 1, 1) * score_scale for head in heads]
    moved = [
        contract(
            picks[head],
            jnp.concatenate([q_rows[head], k_rows[head], v_rows[head], grad_rows[head]], 1),
            1,
            0,
        ).astype(LOW)
        for head in owned
    ]
    shared = [
        contract(picks[head], jnp.concatenate([k_rows[head], v_rows[head]], 1), 1, 0).astype(LOW)
        for head in heads[OWNED:]
    ]
    top_scores = [jnp.max(block, axis=0, keepdims=True) for block in scores]
    expos = [jnp.exp(scores[head] - top_scores[head]) for head in heads]
    for head in heads[OWNED:]:
        key_row = lax.broadcasted_iota(jnp.int32, (tokens, 1), 0)
        times = 1.0
        for level, step in ((0, R1), (1, top_step)):
            offset = offsets_ref[level, head]
            hit_column = jnp.where(key_row % step == offset, 1.0, 0.0)
            times = times + hit_column * hit_row(offset, step, tokens)
        expos[head] = times * expos[head]
    expo_lows = [expo.astype(LOW) for expo in expos]
    outs = [contract(v_rows[head], expo_lows[head], 0, 0) for head in heads]
    totals = [jnp.sum(expo, axis=0, keepdims=True) for expo in expos]
    for head in heads:
        expo_ref[:, head_cols(head)] = expo_lows[head]
        stats_ref[head : head + 1, :] = top_scores[head]
        stats_ref[TILE + head : TILE + head + 1, :] = totals[head]
    for head in owned:
        outs[head] = outs[head] * (1.0 / totals[head])
    picked_outs = [contract(picks[head], outs[head].astype(LOW), 1, 1).astype(LOW) for head in owned]
    for head in heads:
        out_ref[:, head_cols(head)] = outs[head]
    for head in owned:
        pieces = piece_rows(top_scores[head] + jnp.log(totals[head])).astype(LOW)
        slot = me ^ head
        stat_rows = [
            contract(pieces, slot_matrix(offsets_ref[level, head], step, slot, tokens), 1, 0)
            for level, step in ((1, top_step), (0, R1))
        ]
        blocks = [moved[head][:, block * HEAD_DIM : (block + 1) * HEAD_DIM] for block in range(4)]
        blocks.append(picked_outs[head])
        blocks += [shared[0][:, :HEAD_DIM], shared[0][:, HEAD_DIM:]]
        blocks.append(jnp.concatenate(stat_rows, 0).astype(LOW))
        held_ref[head] = jnp.concatenate(blocks, 0)
    for distance, payload_ref in enumerate(payload_refs):
        payload_ref[...] = held_ref[me ^ distance]


def prepare_kernel(top_step, offsets_ref, grad_ref, gain_ref, out_ref, *refs):
    grad_norm_ref, gain_part_ref, place_ref, slots_ref = refs
    tokens, width = grad_ref.shape[1:]
    heads = range(width // HEAD_DIM)
    me = lax.axis_index("ctx")
    picked = sum(picked_counts(tokens, top_step))
    top_rows = tokens // top_step
    ones = jnp.ones((TILE, tokens), LOW)
    column = lax.broadcasted_iota(jnp.int32, (tokens, picked), 1)
    gain_part_ref[...] = jnp.zeros(gain_part_ref.shape, WIDE)
    grad_norms = [
        (grad_ref[0, :, head_cols(head)].astype(WIDE) * gain_ref[:, head_cols(head)]).T
        for head in heads
    ]
    for head in heads:
        cols = head_cols(head)
        grad_norm_ref[:, cols] = grad_norms[head]
        picks = pick_matrix(offsets_ref, head, tokens, top_step, 1)
        place_ref[:, pl.ds(head * HEAD_DIM, picked)] = picks
    for head in range(OWNED):
        cols = head_cols(head)
        mid_offset, top_offset = offsets_ref[0, head], offsets_ref[1, head]
        seen = jnp.maximum(
            hit_row(top_offset, top_step, tokens), hit_row(mid_offset, R1, tokens)
        )
        attn = out_ref[:, cols]
        normed = attn * lax.rsqrt(column_mean(attn * attn) + EPS)
        product = grad_norms[head] * normed * (1.0 - seen)
        gain_part_ref[:, cols] = gain_row_of(ones, product) / gain_ref[:, cols]
        both = mid_offset % top_step == top_offset
        kept = jnp.where(column < top_rows, 1.0, jnp.where(both, 0.0, 1.0)).astype(LOW)
        picks = pick_matrix(offsets_ref, head, tokens, top_step, 1)
        place_ref[:, pl.ds(width + head * HEAD_DIM, picked)] = picks * kept
        for index, (offset, step) in enumerate(((top_offset, top_step), (mid_offset, R1))):
            slots_ref[:, head_cols(2 * head + index)] = slot_matrix(
                offset, step, me ^ head, tokens
            )


def owner_kernel(top_step, offsets_ref, q_ref, gain_ref, out_ref, grad_norm_ref, *refs):
    stats_ref, gain_base_ref = refs[:2]
    payload_refs, refs = nearest_first(refs[2 : 2 + SPAN]), refs[2 + SPAN :]
    gain_part_ref, normed_ref, grad_low_ref, score_grad_ref, kept_ref = refs[:5]
    return_refs = refs[5:]
    tokens = q_ref.shape[1]
    heads = q_ref.shape[2] // HEAD_DIM
    top_rows, mid_rows = picked_counts(tokens, top_step)
    picked = top_rows + mid_rows
    top_all, mid_all = SPAN * top_rows, SPAN * mid_rows
    queries = top_all + mid_all
    score_scale = 1.0 / math.sqrt(HEAD_DIM)
    me = lax.axis_index("ctx")
    ones = jnp.ones((TILE, tokens), LOW)

    def by_level(block):
        start = block * picked
        return jnp.concatenate(
            [ref[start : start + top_rows] for ref in payload_refs]
            + [ref[start + top_rows : start + picked] for ref in payload_refs],
            0,
        )

    def per_level(top_row, mid_row):
        return jnp.concatenate(
            [
                jnp.broadcast_to(top_row, (top_all, queries)),
                jnp.broadcast_to(mid_row, (mid_all, queries)),
            ],
            0,
        )

    q_rows, k_rows, v_rows, grad_rows, base_rows = [by_level(block) for block in range(5)]
    stat_start = 7 * picked
    stat_rows = sum(
        ref[stat_start : stat_start + STAT_TILES].astype(WIDE) for ref in payload_refs
    )
    base_log = jnp.concatenate(
        [joined_row(stat_rows, 0), joined_row(stat_rows, TILE)[:, :mid_all]], 1
    )
    gain_row = jnp.zeros((1, HEAD_DIM), WIDE)
    for head in range(OWNED):
        gain_row = gain_row + jnp.where(me == head, 1.0, 0.0) * gain_ref[:, head_cols(head)]
    mid_offset, top_offset = offsets_ref[0, me], offsets_ref[1, me]
    both = mid_offset % top_step == top_offset
    lane = lax.broadcasted_iota(jnp.int32, (1, queries), 1)
    is_top = jnp.where(lane < top_all, 1.0, 0.0)
    top_in_mid = jnp.where(((lane % top_rows) * top_step + top_offset) % R1 == mid_offset, 1.0, 0.0)
    both_flag = jnp.where(both, 1.0, 0.0)
    sees_top = is_top + (1.0 - is_top) * both_flag
    sees_mid = is_top * top_in_mid + (1.0 - is_top)
    bias = per_level((1.0 - sees_top) * NEVER, (1.0 - sees_mid) * NEVER)
    same_level = per_level(is_top, 1.0 - is_top)
    last = heads - 1
    cols = head_cols(last)
    peers = payload_refs[1:]
    q_last = q_ref[0, :, cols]
    k_peers = jnp.concatenate([ref[5 * picked : 6 * picked] for ref in peers], 0)
    v_peers = jnp.concatenate([ref[6 * picked : 7 * picked] for ref in peers], 0)
    last_biases = [
        jnp.broadcast_to((1.0 - hit_row(offsets_ref[level, last], step, tokens)) * NEVER, shape)
        for level, step, shape in (
            (1, top_step, (top_rows, tokens)),
            (0, R1, (mid_rows, tokens)),
        )
    ]
    scores = contract(k_rows, q_rows, 1, 1) * score_scale + bias
    scores_last = contract(k_peers, q_last, 1, 1) * score_scale + jnp.concatenate(
        last_biases * PEERS, 0
    )
    base_attn = base_rows.astype(WIDE).T
    grad_norm = (grad_rows.astype(WIDE) * gain_row).T
    top_score = jnp.maximum(base_log, jnp.max(scores, axis=0, keepdims=True))
    base_top, base_total = stats_ref[last : last + 1, :], stats_ref[TILE + last : TILE + last + 1, :]
    top_last = jnp.maximum(base_top, jnp.max(scores_last, axis=0, keepdims=True))
    expo = jnp.exp(scores - top_score)
    expo_last = jnp.exp(scores_last - top_last)
    factor = jnp.exp(base_log - top_score)
    factor_last = jnp.exp(base_top - top_last)
    total = factor + jnp.sum(expo, axis=0, keepdims=True)
    total_last = factor_last * base_total + jnp.sum(expo_last, axis=0, keepdims=True)
    inv_total, inv_last = 1.0 / total, 1.0 / total_last
    soft, soft_last = expo * inv_total, expo_last * inv_last
    soft_low, soft_last_low = soft.astype(LOW), soft_last.astype(LOW)
    factor_last = factor_last * inv_last
    attn = (factor * inv_total) * base_attn + contract(v_rows, soft_low, 0, 0)
    attn_last = factor_last * out_ref[:, cols] + contract(v_peers, soft_last_low, 0, 0)
    _, product, grad_low, inner = norm_backward(attn, grad_norm)
    normed_last, product_last, grad_last_low, inner_last = norm_backward(
        attn_last, grad_norm_ref[:, cols]
    )
    prob_grad = contract(v_rows, grad_low, 1, 0)
    prob_grad_last = contract(v_peers, grad_last_low, 1, 0)
    soft = soft * same_level
    score_grad = (soft * (prob_grad - inner) * score_scale).astype(LOW)
    score_grad_last = (soft_last * (prob_grad_last - inner_last) * score_scale).astype(LOW)
    dk = contract(score_grad, q_rows, 1, 0).astype(LOW)
    dk_last = contract(score_grad_last, q_last, 1, 0).astype(LOW)
    dv = contract(soft.astype(LOW), grad_low, 1, 1).astype(LOW)
    dv_last = contract(soft_last_low, grad_last_low, 1, 1).astype(LOW)
    dq = contract(score_grad, k_rows, 0, 0).astype(LOW)
    attn_rows = attn.T.astype(LOW)
    log_total = top_score + jnp.log(total)
    padding = jnp.zeros((1, top_all - mid_all), WIDE)
    log_rows = jnp.concatenate(
        [
            piece_rows(log_total[:, :top_all]),
            piece_rows(jnp.concatenate([log_total[:, top_all:], padding], 1)),
        ],
        0,
    ).astype(LOW)
    for distance, return_ref in enumerate(return_refs):
        blocks = []
        for rows in (dq, dk, dv, attn_rows):
            mid_start = top_all + distance * mid_rows
            blocks.append(rows[distance * top_rows : (distance + 1) * top_rows])
            blocks.append(rows[mid_start : mid_start + mid_rows])
        start = max(distance - 1, 0) * picked
        blocks += [dk_last[start : start + picked], dv_last[start : start + picked], log_rows]
        return_ref[...] = jnp.concatenate(blocks, 0)
    normed_ref[...] = normed_last
    grad_low_ref[...] = grad_last_low
    score_grad_ref[...] = score_grad_last
    kept_ref[0:1, :] = factor_last
    kept_ref[1:2, :] = inner_last
    once = is_top + (1.0 - is_top) * (1.0 - both_flag)
    ones_all = jnp.ones((TILE, queries), LOW)
    own_gain = gain_row_of(ones_all, product * once) / gain_row
    last_gain = gain_row_of(ones, product_last) / gain_ref[:, cols]
    for head in range(OWNED):
        gain_part_ref[:, head_cols(head)] = gain_base_ref[:, head_cols(head)] + (
            jnp.where(me == head, 1.0, 0.0) * own_gain
        )
    gain_part_ref[:, cols] = last_gain


def last_head_kernel(top_step, *refs):
    gain_part_ref, gain_peer_ref, q_ref, k_ref, v_ref, gain_ref, expo_ref, *refs = refs
    normed_ref, grad_low_ref, peer_score_grad_ref, kept_ref, *peers = refs[: 4 + PEERS]
    peers = peers[::-1]
    attended_ref, dq_ref, dk_ref, dv_ref, gain_sum_ref = refs[4 + PEERS :]
    gain_sum_ref[...] = gain_part_ref[...] + gain_peer_ref[...]
    picked = sum(picked_counts(q_ref.shape[1], top_step))
    score_scale = 1.0 / math.sqrt(HEAD_DIM)
    cols = head_cols(q_ref.shape[2] // HEAD_DIM - 1)
    attended_ref[...] = (normed_ref[...].T * gain_ref[:, cols]).astype(LOW)
    k_peers = jnp.concatenate([ref[5 * picked : 6 * picked] for ref in peers], 0)
    grad_low = grad_low_ref[...]
    soft = expo_ref[:, cols].astype(WIDE) * kept_ref[0:1, :]
    prob_grad = contract(v_ref[0, :, cols], grad_low, 1, 0)
    score_grad = (soft * (prob_grad - kept_ref[1:2, :]) * score_scale).astype(LOW)
    dk_ref[...] = contract(score_grad, q_ref[0, :, cols], 1, 0)
    dv_ref[...] = contract(soft.astype(LOW), grad_low, 1, 1)
    dq_ref[...] = (
        contract(score_grad, k_ref[0, :, cols], 0, 0)
        + contract(peer_score_grad_ref[...], k_peers, 0, 0)
    ).astype(LOW)


def finish_kernel(top_step, offsets_ref, q_ref, k_ref, v_ref, gain_ref, expo_ref, out_ref, *refs):
    grad_norm_ref, stats_ref, place_ref, slots_ref = refs[:4]
    gain_in_ref, last_attended_ref, last_dq_ref, last_dk_ref, last_dv_ref = refs[4:9]
    return_refs, refs = nearest_first(refs[9 : 9 + SPAN]), refs[9 + SPAN :]
    attended_ref, dq_ref, dk_ref, dv_ref, gain_out_ref, held_ref = refs
    gain_out_ref[...] = gain_in_ref[...]
    tokens, width = q_ref.shape[1:]
    picked = sum(picked_counts(tokens, top_step))
    score_scale = 1.0 / math.sqrt(HEAD_DIM)
    me = lax.axis_index("ctx")
    heads = range(OWNED)
    every = [head_cols(head) for head in heads]
    for distance, return_ref in enumerate(return_refs):
        held_ref[me ^ distance] = return_ref[...]
    blocks = [
        [held_ref[head, block * picked : (block + 1) * picked] for block in range(4)]
        for head in heads
    ]
    log_rows = [held_ref[head, 6 * picked : 6 * picked + STAT_TILES] for head in heads]
    attn_parts = [
        contract(blocks[head][3], place_ref[:, pl.ds(width + head * HEAD_DIM, picked)], 0, 1)
        for head in heads
    ]
    log_parts = [
        [contract(log_rows[head], slots_ref[:, head_cols(2 * head + level)], 1, 1) for level in (0, 1)]
        for head in heads
    ]
    placed = [
        contract(
            place_ref[:, pl.ds(head * HEAD_DIM, picked)],
            jnp.concatenate(blocks[head][:3], 1),
            1,
            0,
        )
        for head in heads
    ]
    factors, normeds, grad_lows, inners = [], [], [], []
    for head in heads:
        top_hit = hit_row(offsets_ref[1, head], top_step, tokens)
        mid_hit = hit_row(offsets_ref[0, head], R1, tokens)
        seen = jnp.maximum(top_hit, mid_hit) > 0.5
        top_log, mid_log = joined_row(log_parts[head][0], 0), joined_row(log_parts[head][1], TILE)
        top_score, total = stats_ref[head : head + 1, :], stats_ref[TILE + head : TILE + head + 1, :]
        log_total = jnp.where(
            top_hit > 0.5, top_log, jnp.where(mid_hit > 0.5, mid_log, top_score + jnp.log(total))
        )
        factors.append(jnp.exp(top_score - log_total))
        attn = jnp.where(seen, attn_parts[head], out_ref[:, every[head]])
        normed, _, grad_low, inner = norm_backward(attn, grad_norm_ref[:, every[head]])
        normeds.append(normed)
        grad_lows.append(grad_low)
        inners.append(inner)
    prob_grads = [contract(v_ref[0, :, every[head]], grad_lows[head], 1, 0) for head in heads]
    softs = [expo_ref[:, every[head]].astype(WIDE) * factors[head] for head in heads]
    dvs = [contract(softs[head].astype(LOW), grad_lows[head], 1, 1) for head in heads]
    score_grads = [
        (softs[head] * (prob_grads[head] - inners[head]) * score_scale).astype(LOW)
        for head in heads
    ]
    dks = [contract(score_grads[head], q_ref[0, :, every[head]], 1, 0) for head in heads]
    dqs = [contract(score_grads[head], k_ref[0, :, every[head]], 0, 0) for head in heads]
    for head in heads:
        cols = every[head]
        attended_ref[0, :, cols] = (normeds[head].T * gain_ref[:, cols]).astype(LOW)
        for which, (block, out_block_ref) in enumerate(
            ((dqs[head], dq_ref), (dks[head], dk_ref), (dvs[head], dv_ref))
        ):
            part = placed[head][:, which * HEAD_DIM : (which + 1) * HEAD_DIM]
            out_block_ref[0, :, cols] = (block + part).astype(LOW)
    last = width // HEAD_DIM - 1
    cols = head_cols(last)
    total = sum(ref[4 * picked : 6 * picked].astype(WIDE) for ref in return_refs[1:]).astype(LOW)
    rows = contract(
        place_ref[:, pl.ds(last * HEAD_DIM, picked)],
        jnp.concatenate([total[:picked], total[picked:]], 1),
        1,
        0,
    )
    attended_ref[0, :, cols] = last_attended_ref[...]
    dq_ref[0, :, cols] = last_dq_ref[...]
    dk_ref[0, :, cols] = (last_dk_ref[...] + rows[:, :HEAD_DIM]).astype(LOW)
    dv_ref[0, :, cols] = (last_dv_ref[...] + rows[:, HEAD_DIM:]).astype(LOW)


def across(block, axis, distance):
    route = [(place, place ^ distance) for place in range(lax.axis_size(axis))]
    return lax.ppermute(block, axis, route)


def to_peers(blocks):
    return [across(blocks[distance - 1], "ctx", distance) for distance in range(PEERS, 0, -1)]


def call(kernel, name, operands, results, microseconds, vmem=PLAIN_VMEM, scratch=()):
    return pl.pallas_call(
        kernel,
        out_shape=results,
        in_specs=[SMEM_SPEC if block.dtype == jnp.int32 else VMEM_SPEC for block in operands],
        out_specs=[VMEM_SPEC] * len(results),
        scratch_shapes=scratch,
        compiler_params=pltpu.CompilerParams(vmem_limit_bytes=vmem),
        cost_estimate=pl.CostEstimate(
            flops=int(microseconds * 10**9), bytes_accessed=0, transcendentals=0
        ),
        name=name,
    )(*operands)


def one_segment_shards(queries, keys, values, grad_y, out_gain, offsets):
    tokens, width = queries.shape[1:]
    heads = width // HEAD_DIM
    top_step = lax.axis_size("ctx")
    picked = sum(picked_counts(tokens, top_step))
    shape = jax.ShapeDtypeStruct
    row_block = shape((1, tokens, width), LOW)
    low_block, wide_block = shape((tokens, width), LOW), shape((tokens, width), WIDE)
    low_head, wide_head = shape((tokens, HEAD_DIM), LOW), shape((tokens, HEAD_DIM), WIDE)
    gain_block = shape((1, width), WIDE)
    stats_block = shape((2 * TILE, tokens), WIDE)
    payload = shape((7 * picked + STAT_TILES, HEAD_DIM), LOW)
    answer = shape((6 * picked + STAT_TILES, HEAD_DIM), LOW)
    bind = functools.partial
    gain_row = out_gain.reshape(1, width)
    own, *sent, expo, base_out, stats = call(
        bind(pack_kernel, top_step),
        "pack",
        (offsets, queries, keys, values, grad_y),
        [payload] * SPAN + [low_block, wide_block, stats_block],
        1,
        vmem=PACK_VMEM,
        scratch=[pltpu.VMEM((OWNED, *payload.shape), LOW)],
    )
    received = to_peers(sent)
    grad_norm, gain_base, place, slots = call(
        bind(prepare_kernel, top_step),
        "prepare",
        (offsets, grad_y, gain_row, base_out),
        [wide_block, gain_block, shape((tokens, 2 * width), LOW), shape((tokens, 2 * OWNED * tokens), LOW)],
        2,
    )
    gain_part, normed, grad_low, score_grad, kept, own_answer, *answers = call(
        bind(owner_kernel, top_step),
        "owner",
        (offsets, queries, gain_row, base_out, grad_norm, stats, gain_base, own, *received),
        [
            gain_block,
            wide_head,
            low_head,
            shape((PEERS * picked, HEAD_DIM), LOW),
            shape((TILE, tokens), WIDE),
        ]
        + [answer] * SPAN,
        3,
    )
    returned = to_peers(answers)
    *last_results, gain_sum = call(
        bind(last_head_kernel, top_step),
        "last_head",
        (
            gain_part,
            across(gain_part, "ctx", 2),
            queries,
            keys,
            values,
            gain_row,
            expo,
            normed,
            grad_low,
            score_grad,
            kept,
            *received,
        ),
        [low_head, low_head, wide_head, wide_head, gain_block],
        20,
    )
    gain_sum = gain_sum + across(gain_sum, "dp", 1)
    gain_rest = across(gain_sum, "ctx", 1)
    attended, query_grad, key_grad, value_grad, gain_sum = call(
        bind(finish_kernel, top_step),
        "finish",
        (
            offsets,
            queries,
            keys,
            values,
            gain_row,
            expo,
            base_out,
            grad_norm,
            stats,
            place,
            slots,
            gain_sum,
            *last_results,
            own_answer,
            *returned,
        ),
        [row_block] * 4 + [gain_block],
        1,
        scratch=[pltpu.VMEM((OWNED, *answer.shape), LOW)],
    )
    gain_grad = (gain_sum + gain_rest).reshape(width)
    return attended, query_grad, key_grad, value_grad, gain_grad


def solution(mesh):
    in_specs = (
        P("dp", "ctx", "head"),
        P("dp", "ctx", "head"),
        P("dp", "ctx", "head"),
        P("dp", "ctx", "head"),
        P("head"),
        P(None, "head"),
    )
    out_specs = (
        P("dp", "ctx", "head"),
        P("dp", "ctx", "head"),
        P("dp", "ctx", "head"),
        P("dp", "ctx", "head"),
        P("head"),
    )
    body = one_segment_shards if mesh.shape["ctx"] == SPAN else general_shards
    return jax.shard_map(body, mesh=mesh, in_specs=in_specs, out_specs=out_specs, check_vma=False)
```

```python
import functools
import math

import jax
import jax.numpy as jnp
from jax import lax
from jax.experimental import pallas as pl
from jax.experimental.pallas import tpu as pltpu
from jax.sharding import PartitionSpec as P

HEAD_DIM = 128
SPAN = 4
R1 = 8


EPS = 1e-06


def swapped(block, axis, bit):
    count = lax.axis_size(axis)
    route = []
    for low in range(count):
        high = low | 1 << bit
        if high != low and high < count:
            route += [(low, high), (high, low)]
    return lax.ppermute(block, axis, route)


def pick_rows(source_rows, dilation, shifts):
    row_count, head_count, head_width = source_rows.shape
    grouped = source_rows.reshape(row_count // dilation, dilation, head_count, head_width)
    hit_mask = jnp.arange(dilation, dtype=jnp.int32).reshape(1, dilation, 1, 1) == shifts.reshape(
        1, 1, head_count, 1
    )
    chosen = jnp.where(hit_mask, grouped, jnp.zeros((), source_rows.dtype))
    return jnp.sum(chosen, axis=1, dtype=source_rows.dtype)


def place_rows(row_values, dilation, shifts):
    row_count, head_count, head_width = row_values.shape
    hit_mask = jnp.arange(dilation, dtype=jnp.int32).reshape(1, dilation, 1, 1) == shifts.reshape(
        1, 1, head_count, 1
    )
    spread = jnp.where(hit_mask, row_values[:, None], jnp.zeros((), row_values.dtype))
    return spread.reshape(row_count * dilation, head_count, head_width)


def level_scores(q_rows, k_rows):
    score_scale = 1.0 / math.sqrt(q_rows.shape[-1])
    return (
        jnp.einsum("qhe,khe->hqk", q_rows, k_rows, preferred_element_type=jnp.float32) * score_scale
    )


def attend(q_rows, k_rows, v_rows):
    scores = level_scores(q_rows, k_rows)
    row_max = jnp.max(scores, axis=-1, keepdims=True)
    log_total = row_max[..., 0] + jnp.log(jnp.sum(jnp.exp(scores - row_max), axis=-1))
    soft_rows = jnp.exp(scores - log_total[..., None]).astype(jnp.bfloat16)
    level_out = jnp.einsum("hqk,khe->qhe", soft_rows, v_rows, preferred_element_type=jnp.float32)
    return (level_out, log_total.T)


def score_grads(q_rows, k_rows, v_rows, log_total, grad_low, row_shift):
    score_scale = 1.0 / math.sqrt(q_rows.shape[-1])
    scores = level_scores(q_rows, k_rows)
    exact_soft = jnp.exp(scores - log_total.T[..., None])
    prob_grad = jnp.einsum("qhe,khe->hqk", grad_low, v_rows, preferred_element_type=jnp.float32)
    score_grad = (exact_soft * (prob_grad + row_shift.T[..., None]) * score_scale).astype(
        jnp.bfloat16
    )
    return (score_grad, exact_soft.astype(jnp.bfloat16))


def key_parts(score_grad, soft_low, q_rows, grad_low):
    k_part = jnp.einsum("hqk,qhe->khe", score_grad, q_rows, preferred_element_type=jnp.float32)
    v_part = jnp.einsum("hqk,qhe->khe", soft_low, grad_low, preferred_element_type=jnp.float32)
    return (k_part, v_part)


def query_part(score_grad, k_rows):
    return jnp.einsum("hqk,khe->qhe", score_grad, k_rows, preferred_element_type=jnp.float32)


def general_shards(queries, keys, values, grad_y, out_gain, offsets):
    tokens = queries.shape[1]
    flat_width = queries.shape[2]
    head_count = flat_width // HEAD_DIM
    row_shape = (tokens, head_count, HEAD_DIM)
    q_own = queries[0].reshape(row_shape)
    k_own = keys[0].reshape(row_shape)
    v_own = values[0].reshape(row_shape)
    ctx_size = lax.axis_size("ctx")
    span_bits = SPAN.bit_length() - 1
    my_place = lax.axis_index("ctx")
    mid_shift = offsets[0]
    top_shift = offsets[1]
    positions = jnp.arange(tokens, dtype=jnp.int32)
    mid_hit = (positions % R1)[:, None] == mid_shift[None, :]
    top_hit = (positions % ctx_size)[:, None] == top_shift[None, :]
    mid_q = pick_rows(q_own, R1, mid_shift)
    mid_k = pick_rows(k_own, R1, mid_shift)
    mid_v = pick_rows(v_own, R1, mid_shift)
    top_q = pick_rows(q_own, ctx_size, top_shift)
    top_k = pick_rows(k_own, ctx_size, top_shift)
    top_v = pick_rows(v_own, ctx_size, top_shift)
    mid_keys = mid_k.reshape(-1, flat_width)
    mid_vals = mid_v.reshape(-1, flat_width)
    top_keys = top_k.reshape(-1, flat_width)
    top_vals = top_v.reshape(-1, flat_width)

    def append_peer(mine, received, level_bit):
        upper_side = my_place >> level_bit & 1 == 1
        return jnp.where(
            upper_side, jnp.concatenate([received, mine], 0), jnp.concatenate([mine, received], 0)
        )

    for level_bit in range(span_bits):
        received = swapped((mid_keys, mid_vals), "ctx", level_bit)
        mid_keys = append_peer(mid_keys, received[0], level_bit)
        mid_vals = append_peer(mid_vals, received[1], level_bit)
    top_keys, top_vals = (
        lax.all_gather(top_keys, "ctx", axis=0, tiled=True),
        lax.all_gather(top_vals, "ctx", axis=0, tiled=True),
    )
    mid_keys = mid_keys.reshape(-1, head_count, HEAD_DIM)
    mid_vals = mid_vals.reshape(-1, head_count, HEAD_DIM)
    top_keys = top_keys.reshape(-1, head_count, HEAD_DIM)
    top_vals = top_vals.reshape(-1, head_count, HEAD_DIM)
    base_out, base_total = attend(q_own, k_own, v_own)
    mid_out, mid_total = attend(mid_q, mid_keys, mid_vals)
    top_out, top_total = attend(top_q, top_keys, top_vals)
    mid_full = place_rows(mid_total[..., None], R1, mid_shift)[..., 0]
    top_full = place_rows(top_total[..., None], ctx_size, top_shift)[..., 0]
    row_max = jnp.maximum(base_total, jnp.where(mid_hit, mid_full, base_total))
    row_max = jnp.maximum(row_max, jnp.where(top_hit, top_full, base_total))
    base_expo = jnp.exp(base_total - row_max)
    mid_expo = jnp.where(mid_hit, jnp.exp(mid_full - row_max), 0.0)
    top_expo = jnp.where(top_hit, jnp.exp(top_full - row_max), 0.0)
    denom = base_expo + mid_expo + top_expo
    base_share = base_expo / denom
    mid_share = mid_expo / denom
    top_share = top_expo / denom
    attn = (
        base_share[..., None] * base_out
        + mid_share[..., None] * place_rows(mid_out, R1, mid_shift)
        + top_share[..., None] * place_rows(top_out, ctx_size, top_shift)
    )
    inv_rms = lax.rsqrt(jnp.mean(attn * attn, axis=-1, keepdims=True) + EPS)
    normed = attn * inv_rms
    gain_rows = out_gain.reshape(head_count, HEAD_DIM)
    attended = (normed * gain_rows).astype(jnp.bfloat16).reshape(1, tokens, flat_width)
    grad_full = grad_y[0].reshape(row_shape).astype(jnp.float32)
    gain_part = jnp.sum(grad_full * normed, axis=0).reshape(flat_width)
    gain_grad = lax.psum(gain_part, ("dp", "ctx"))
    grad_norm = grad_full * gain_rows
    grad_attn = inv_rms * (
        grad_norm - normed * jnp.mean(grad_norm * normed, axis=-1, keepdims=True)
    )
    inner = jnp.sum(grad_attn * attn, axis=-1)
    base_low = (base_share[..., None] * grad_attn).astype(jnp.bfloat16)
    base_shift = -(base_share * inner)
    base_grad, base_soft = score_grads(q_own, k_own, v_own, base_total, base_low, base_shift)
    base_dq = query_part(base_grad, k_own)
    base_dk, base_dv = key_parts(base_grad, base_soft, q_own, base_low)
    mid_sel = pick_rows(mid_share[..., None], R1, mid_shift)[..., 0]
    mid_low = (mid_sel[..., None] * pick_rows(grad_attn, R1, mid_shift)).astype(jnp.bfloat16)
    mid_row_shift = -(mid_sel * pick_rows(inner[..., None], R1, mid_shift)[..., 0])
    mid_grad, mid_soft = score_grads(mid_q, mid_keys, mid_vals, mid_total, mid_low, mid_row_shift)
    mid_dq = query_part(mid_grad, mid_keys)
    mid_dk, mid_dv = key_parts(mid_grad, mid_soft, mid_q, mid_low)
    mid_dk = mid_dk.reshape(-1, flat_width)
    mid_dv = mid_dv.reshape(-1, flat_width)
    for level_bit in reversed(range(span_bits)):
        half_rows = mid_dk.shape[0] // 2
        upper_side = my_place >> level_bit & 1 == 1
        keep_k = jnp.where(upper_side, mid_dk[half_rows:], mid_dk[:half_rows])
        keep_v = jnp.where(upper_side, mid_dv[half_rows:], mid_dv[:half_rows])
        send_k = jnp.where(upper_side, mid_dk[:half_rows], mid_dk[half_rows:])
        send_v = jnp.where(upper_side, mid_dv[:half_rows], mid_dv[half_rows:])
        received = (
            swapped(send_k.astype(jnp.bfloat16), "ctx", level_bit).astype(send_k.dtype),
            swapped(send_v.astype(jnp.bfloat16), "ctx", level_bit).astype(send_v.dtype),
        )
        mid_dk = keep_k + received[0]
        mid_dv = keep_v + received[1]
    mid_dk = mid_dk.reshape(-1, head_count, HEAD_DIM)
    mid_dv = mid_dv.reshape(-1, head_count, HEAD_DIM)
    top_sel = pick_rows(top_share[..., None], ctx_size, top_shift)[..., 0]
    top_low = (top_sel[..., None] * pick_rows(grad_attn, ctx_size, top_shift)).astype(jnp.bfloat16)
    top_row_shift = -(top_sel * pick_rows(inner[..., None], ctx_size, top_shift)[..., 0])
    top_grad, top_soft = score_grads(top_q, top_keys, top_vals, top_total, top_low, top_row_shift)
    top_dq = query_part(top_grad, top_keys)
    gathered_dk, gathered_dv = key_parts(top_grad, top_soft, top_q, top_low)
    summed = (
        lax.psum_scatter(
            gathered_dk.reshape(-1, flat_width), "ctx", scatter_dimension=0, tiled=True
        ),
        lax.psum_scatter(
            gathered_dv.reshape(-1, flat_width), "ctx", scatter_dimension=0, tiled=True
        ),
    )
    top_dk = summed[0].reshape(-1, head_count, HEAD_DIM)
    top_dv = summed[1].reshape(-1, head_count, HEAD_DIM)
    query_grad = (
        base_dq + place_rows(mid_dq, R1, mid_shift) + place_rows(top_dq, ctx_size, top_shift)
    )
    key_grad = base_dk + place_rows(mid_dk, R1, mid_shift) + place_rows(top_dk, ctx_size, top_shift)
    value_grad = (
        base_dv + place_rows(mid_dv, R1, mid_shift) + place_rows(top_dv, ctx_size, top_shift)
    )
    out_shape = (1, tokens, flat_width)
    return (
        attended,
        query_grad.astype(jnp.bfloat16).reshape(out_shape),
        key_grad.astype(jnp.bfloat16).reshape(out_shape),
        value_grad.astype(jnp.bfloat16).reshape(out_shape),
        gain_grad,
    )


VMEM_SPEC = pl.BlockSpec(memory_space=pltpu.VMEM)
SMEM_SPEC = pl.BlockSpec(memory_space=pltpu.SMEM)
HBM_SPEC = pl.BlockSpec(memory_space=pltpu.HBM)
PEERS = SPAN - 1
OWNED = SPAN
TILE = 8
STAT_TILES = 2 * TILE
PIECES = 3
NEVER = -1e30
LOW = jnp.bfloat16
WIDE = jnp.float32
PACK_VMEM = 65408 * 1024
PLAIN_VMEM = 16 * 1024 * 1024


def contract(left, right, left_dim, right_dim):
    return lax.dot_general(
        left, right, (((left_dim,), (right_dim,)), ((), ())), preferred_element_type=WIDE
    )


def head_cols(head):
    return pl.ds(head * HEAD_DIM, HEAD_DIM)


def picked_counts(tokens, top_step):
    return tokens // top_step, tokens // R1


def pick_matrix(offsets_ref, head, tokens, top_step, picked_axis):
    top_rows, mid_rows = picked_counts(tokens, top_step)
    shape = (top_rows + mid_rows, tokens) if picked_axis == 0 else (tokens, top_rows + mid_rows)
    row = lax.broadcasted_iota(jnp.int32, shape, picked_axis)
    position = lax.broadcasted_iota(jnp.int32, shape, 1 - picked_axis)
    wanted = jnp.where(
        row < top_rows,
        row * top_step + offsets_ref[1, head],
        (row - top_rows) * R1 + offsets_ref[0, head],
    )
    return jnp.where(position == wanted, 1.0, 0.0).astype(LOW)


def slot_matrix(offset, step, slot, tokens):
    count = tokens // step
    position = lax.broadcasted_iota(jnp.int32, (tokens, tokens), 0)
    index = lax.broadcasted_iota(jnp.int32, (tokens, tokens), 1) - slot * count
    inside = (index >= 0) & (index < count)
    return jnp.where(inside & (position == index * step + offset), 1.0, 0.0).astype(LOW)


def hit_row(offset, step, tokens):
    position = lax.broadcasted_iota(jnp.int32, (1, tokens), 1)
    return jnp.where(position % step == offset, 1.0, 0.0)


def piece_rows(row):
    pieces = []
    for _ in range(PIECES):
        piece = row.astype(LOW).astype(WIDE)
        pieces.append(piece)
        row = row - piece
    return jnp.concatenate(pieces + [jnp.zeros((TILE - PIECES, row.shape[1]), WIDE)], 0)


def joined_row(rows, first):
    total = rows[first : first + 1]
    for piece in range(1, PIECES):
        total = total + rows[first + piece : first + piece + 1]
    return total


def gain_row_of(ones, product):
    high = product.astype(LOW)
    rest = (product - high.astype(WIDE)).astype(LOW)
    return (contract(ones, high, 1, 1) + contract(ones, rest, 1, 1))[:1]


def column_mean(block):
    return jnp.mean(block, axis=0, keepdims=True)


def norm_backward(attn, grad_norm):
    inv_rms = lax.rsqrt(column_mean(attn * attn) + EPS)
    normed = attn * inv_rms
    product = grad_norm * normed
    grad_attn = inv_rms * (grad_norm - normed * column_mean(product))
    inner = jnp.sum(grad_attn * attn, axis=0, keepdims=True)
    return normed, product, grad_attn.astype(LOW), inner


def nearest_first(refs):
    return [refs[0], *refs[:0:-1]]


def pack_kernel(top_step, offsets_ref, q_ref, k_ref, v_ref, grad_ref, *refs):
    payload_refs, refs = refs[:SPAN], refs[SPAN:]
    stats_ref, expo_hbm, out_hbm, held_ref, expo_ref, out_ref, sems = refs
    tokens, width = q_ref.shape[1:]
    heads = range(width // HEAD_DIM)
    owned = range(OWNED)
    me = lax.axis_index("ctx")
    picked = sum(picked_counts(tokens, top_step))
    score_scale = 1.0 / math.sqrt(HEAD_DIM)
    q_rows, k_rows, v_rows, grad_rows = [
        [ref[0, :, head_cols(head)] for head in heads] for ref in (q_ref, k_ref, v_ref, grad_ref)
    ]
    picks = [pick_matrix(offsets_ref, head, tokens, top_step, 0) for head in heads]
    scores = [contract(k_rows[head], q_rows[head], 1, 1) * score_scale for head in heads]
    moved = [
        contract(
            picks[head],
            jnp.concatenate([q_rows[head], k_rows[head], v_rows[head], grad_rows[head]], 1),
            1,
            0,
        ).astype(LOW)
        for head in owned
    ]
    shared = [
        contract(picks[head], jnp.concatenate([k_rows[head], v_rows[head]], 1), 1, 0).astype(LOW)
        for head in heads[OWNED:]
    ]
    top_scores = [jnp.max(block, axis=0, keepdims=True) for block in scores]
    expos = [jnp.exp(scores[head] - top_scores[head]) for head in heads]
    for head in heads[OWNED:]:
        key_row = lax.broadcasted_iota(jnp.int32, (tokens, 1), 0)
        times = 1.0
        for level, step in ((0, R1), (1, top_step)):
            offset = offsets_ref[level, head]
            hit_column = jnp.where(key_row % step == offset, 1.0, 0.0)
            times = times + hit_column * hit_row(offset, step, tokens)
        expos[head] = times * expos[head]
    expo_lows = [expo.astype(LOW) for expo in expos]
    outs = [contract(v_rows[head], expo_lows[head], 0, 0) for head in heads]
    totals = [jnp.sum(expo, axis=0, keepdims=True) for expo in expos]
    for head in heads:
        expo_ref[:, head_cols(head)] = expo_lows[head]
        stats_ref[head : head + 1, :] = top_scores[head]
        stats_ref[TILE + head : TILE + head + 1, :] = totals[head]
    for head in owned:
        outs[head] = outs[head] * (1.0 / totals[head])
    for head in heads:
        out_ref[:, head_cols(head)] = outs[head]
    copies = [
        pltpu.make_async_copy(expo_ref, expo_hbm, sems.at[0]),
        pltpu.make_async_copy(out_ref, out_hbm, sems.at[1]),
    ]
    for copy in copies:
        copy.start()
    picked_outs = [contract(picks[head], outs[head].astype(LOW), 1, 1).astype(LOW) for head in owned]
    for head in owned:
        pieces = piece_rows(top_scores[head] + jnp.log(totals[head])).astype(LOW)
        slot = me ^ head
        stat_rows = [
            contract(pieces, slot_matrix(offsets_ref[level, head], step, slot, tokens), 1, 0)
            for level, step in ((1, top_step), (0, R1))
        ]
        blocks = [moved[head][:, block * HEAD_DIM : (block + 1) * HEAD_DIM] for block in range(4)]
        blocks.append(picked_outs[head])
        blocks += [shared[0][:, :HEAD_DIM], shared[0][:, HEAD_DIM:]]
        blocks.append(jnp.concatenate(stat_rows, 0).astype(LOW))
        held_ref[head] = jnp.concatenate(blocks, 0)
    for distance, payload_ref in enumerate(payload_refs):
        payload_ref[...] = held_ref[me ^ distance]
    for copy in copies:
        copy.wait()


def prepare_kernel(top_step, offsets_ref, grad_ref, gain_ref, out_ref, *refs):
    grad_norm_ref, gain_part_ref, place_ref, slots_ref = refs
    tokens, width = grad_ref.shape[1:]
    heads = range(width // HEAD_DIM)
    me = lax.axis_index("ctx")
    picked = sum(picked_counts(tokens, top_step))
    top_rows = tokens // top_step
    ones = jnp.ones((TILE, tokens), LOW)
    column = lax.broadcasted_iota(jnp.int32, (tokens, picked), 1)
    gain_part_ref[...] = jnp.zeros(gain_part_ref.shape, WIDE)
    grad_norms = [
        (grad_ref[0, :, head_cols(head)].astype(WIDE) * gain_ref[:, head_cols(head)]).T
        for head in heads
    ]
    for head in heads:
        cols = head_cols(head)
        grad_norm_ref[:, cols] = grad_norms[head]
        picks = pick_matrix(offsets_ref, head, tokens, top_step, 1)
        place_ref[:, pl.ds(head * HEAD_DIM, picked)] = picks
    for head in range(OWNED):
        cols = head_cols(head)
        mid_offset, top_offset = offsets_ref[0, head], offsets_ref[1, head]
        seen = jnp.maximum(
            hit_row(top_offset, top_step, tokens), hit_row(mid_offset, R1, tokens)
        )
        attn = out_ref[:, cols]
        normed = attn * lax.rsqrt(column_mean(attn * attn) + EPS)
        product = grad_norms[head] * normed * (1.0 - seen)
        gain_part_ref[:, cols] = gain_row_of(ones, product) / gain_ref[:, cols]
        both = mid_offset % top_step == top_offset
        kept = jnp.where(column < top_rows, 1.0, jnp.where(both, 0.0, 1.0)).astype(LOW)
        picks = pick_matrix(offsets_ref, head, tokens, top_step, 1)
        place_ref[:, pl.ds(width + head * HEAD_DIM, picked)] = picks * kept
        for index, (offset, step) in enumerate(((top_offset, top_step), (mid_offset, R1))):
            slots_ref[:, head_cols(2 * head + index)] = slot_matrix(
                offset, step, me ^ head, tokens
            )


def owner_kernel(top_step, offsets_ref, q_ref, gain_ref, out_ref, grad_norm_ref, *refs):
    stats_ref, gain_base_ref = refs[:2]
    payload_refs, refs = nearest_first(refs[2 : 2 + SPAN]), refs[2 + SPAN :]
    gain_part_ref, normed_ref, grad_low_ref, score_grad_ref, kept_ref = refs[:5]
    return_refs = refs[5:]
    tokens = q_ref.shape[1]
    heads = q_ref.shape[2] // HEAD_DIM
    top_rows, mid_rows = picked_counts(tokens, top_step)
    picked = top_rows + mid_rows
    top_all, mid_all = SPAN * top_rows, SPAN * mid_rows
    queries = top_all + mid_all
    score_scale = 1.0 / math.sqrt(HEAD_DIM)
    me = lax.axis_index("ctx")
    ones = jnp.ones((TILE, tokens), LOW)

    def by_level(block):
        start = block * picked
        return jnp.concatenate(
            [ref[start : start + top_rows] for ref in payload_refs]
            + [ref[start + top_rows : start + picked] for ref in payload_refs],
            0,
        )

    def per_level(top_row, mid_row):
        return jnp.concatenate(
            [
                jnp.broadcast_to(top_row, (top_all, queries)),
                jnp.broadcast_to(mid_row, (mid_all, queries)),
            ],
            0,
        )

    q_rows, k_rows, v_rows, grad_rows, base_rows = [by_level(block) for block in range(5)]
    stat_start = 7 * picked
    stat_rows = sum(
        ref[stat_start : stat_start + STAT_TILES].astype(WIDE) for ref in payload_refs
    )
    base_log = jnp.concatenate(
        [joined_row(stat_rows, 0), joined_row(stat_rows, TILE)[:, :mid_all]], 1
    )
    gain_row = jnp.zeros((1, HEAD_DIM), WIDE)
    for head in range(OWNED):
        gain_row = gain_row + jnp.where(me == head, 1.0, 0.0) * gain_ref[:, head_cols(head)]
    mid_offset, top_offset = offsets_ref[0, me], offsets_ref[1, me]
    both = mid_offset % top_step == top_offset
    lane = lax.broadcasted_iota(jnp.int32, (1, queries), 1)
    is_top = jnp.where(lane < top_all, 1.0, 0.0)
    top_in_mid = jnp.where(((lane % top_rows) * top_step + top_offset) % R1 == mid_offset, 1.0, 0.0)
    both_flag = jnp.where(both, 1.0, 0.0)
    sees_top = is_top + (1.0 - is_top) * both_flag
    sees_mid = is_top * top_in_mid + (1.0 - is_top)
    bias = per_level((1.0 - sees_top) * NEVER, (1.0 - sees_mid) * NEVER)
    same_level = per_level(is_top, 1.0 - is_top)
    last = heads - 1
    cols = head_cols(last)
    peers = payload_refs[1:]
    q_last = q_ref[0, :, cols]
    k_peers = jnp.concatenate([ref[5 * picked : 6 * picked] for ref in peers], 0)
    v_peers = jnp.concatenate([ref[6 * picked : 7 * picked] for ref in peers], 0)
    last_biases = [
        jnp.broadcast_to((1.0 - hit_row(offsets_ref[level, last], step, tokens)) * NEVER, shape)
        for level, step, shape in (
            (1, top_step, (top_rows, tokens)),
            (0, R1, (mid_rows, tokens)),
        )
    ]
    scores = contract(k_rows, q_rows, 1, 1) * score_scale + bias
    scores_last = contract(k_peers, q_last, 1, 1) * score_scale + jnp.concatenate(
        last_biases * PEERS, 0
    )
    base_attn = base_rows.astype(WIDE).T
    grad_norm = (grad_rows.astype(WIDE) * gain_row).T
    top_score = jnp.maximum(base_log, jnp.max(scores, axis=0, keepdims=True))
    base_top, base_total = stats_ref[last : last + 1, :], stats_ref[TILE + last : TILE + last + 1, :]
    top_last = jnp.maximum(base_top, jnp.max(scores_last, axis=0, keepdims=True))
    expo = jnp.exp(scores - top_score)
    expo_last = jnp.exp(scores_last - top_last)
    factor = jnp.exp(base_log - top_score)
    factor_last = jnp.exp(base_top - top_last)
    total = factor + jnp.sum(expo, axis=0, keepdims=True)
    total_last = factor_last * base_total + jnp.sum(expo_last, axis=0, keepdims=True)
    inv_total, inv_last = 1.0 / total, 1.0 / total_last
    soft, soft_last = expo * inv_total, expo_last * inv_last
    soft_low, soft_last_low = soft.astype(LOW), soft_last.astype(LOW)
    factor_last = factor_last * inv_last
    attn = (factor * inv_total) * base_attn + contract(v_rows, soft_low, 0, 0)
    attn_last = factor_last * out_ref[:, cols] + contract(v_peers, soft_last_low, 0, 0)
    _, product, grad_low, inner = norm_backward(attn, grad_norm)
    normed_last, product_last, grad_last_low, inner_last = norm_backward(
        attn_last, grad_norm_ref[:, cols]
    )
    prob_grad = contract(v_rows, grad_low, 1, 0)
    prob_grad_last = contract(v_peers, grad_last_low, 1, 0)
    soft = soft * same_level
    score_grad = (soft * (prob_grad - inner) * score_scale).astype(LOW)
    score_grad_last = (soft_last * (prob_grad_last - inner_last) * score_scale).astype(LOW)
    dk = contract(score_grad, q_rows, 1, 0).astype(LOW)
    dk_last = contract(score_grad_last, q_last, 1, 0).astype(LOW)
    dv = contract(soft.astype(LOW), grad_low, 1, 1).astype(LOW)
    dv_last = contract(soft_last_low, grad_last_low, 1, 1).astype(LOW)
    dq = contract(score_grad, k_rows, 0, 0).astype(LOW)
    attn_rows = attn.T.astype(LOW)
    log_total = top_score + jnp.log(total)
    padding = jnp.zeros((1, top_all - mid_all), WIDE)
    log_rows = jnp.concatenate(
        [
            piece_rows(log_total[:, :top_all]),
            piece_rows(jnp.concatenate([log_total[:, top_all:], padding], 1)),
        ],
        0,
    ).astype(LOW)
    for distance, return_ref in enumerate(return_refs):
        blocks = []
        for rows in (dq, dk, dv, attn_rows):
            mid_start = top_all + distance * mid_rows
            blocks.append(rows[distance * top_rows : (distance + 1) * top_rows])
            blocks.append(rows[mid_start : mid_start + mid_rows])
        start = max(distance - 1, 0) * picked
        blocks += [dk_last[start : start + picked], dv_last[start : start + picked], log_rows]
        return_ref[...] = jnp.concatenate(blocks, 0)
    normed_ref[...] = normed_last
    grad_low_ref[...] = grad_last_low
    score_grad_ref[...] = score_grad_last
    kept_ref[0:1, :] = factor_last
    kept_ref[1:2, :] = inner_last
    once = is_top + (1.0 - is_top) * (1.0 - both_flag)
    ones_all = jnp.ones((TILE, queries), LOW)
    own_gain = gain_row_of(ones_all, product * once) / gain_row
    last_gain = gain_row_of(ones, product_last) / gain_ref[:, cols]
    for head in range(OWNED):
        gain_part_ref[:, head_cols(head)] = gain_base_ref[:, head_cols(head)] + (
            jnp.where(me == head, 1.0, 0.0) * own_gain
        )
    gain_part_ref[:, cols] = last_gain


def last_head_kernel(top_step, *refs):
    gain_part_ref, gain_peer_ref, q_ref, k_ref, v_ref, gain_ref, expo_ref, *refs = refs
    normed_ref, grad_low_ref, peer_score_grad_ref, kept_ref, *peers = refs[: 4 + PEERS]
    peers = peers[::-1]
    attended_ref, dq_ref, dk_ref, dv_ref, gain_sum_ref = refs[4 + PEERS :]
    gain_sum_ref[...] = gain_part_ref[...] + gain_peer_ref[...]
    picked = sum(picked_counts(q_ref.shape[1], top_step))
    score_scale = 1.0 / math.sqrt(HEAD_DIM)
    cols = head_cols(q_ref.shape[2] // HEAD_DIM - 1)
    attended_ref[...] = (normed_ref[...].T * gain_ref[:, cols]).astype(LOW)
    k_peers = jnp.concatenate([ref[5 * picked : 6 * picked] for ref in peers], 0)
    grad_low = grad_low_ref[...]
    soft = expo_ref[:, cols].astype(WIDE) * kept_ref[0:1, :]
    prob_grad = contract(v_ref[0, :, cols], grad_low, 1, 0)
    score_grad = (soft * (prob_grad - kept_ref[1:2, :]) * score_scale).astype(LOW)
    dk_ref[...] = contract(score_grad, q_ref[0, :, cols], 1, 0)
    dv_ref[...] = contract(soft.astype(LOW), grad_low, 1, 1)
    dq_ref[...] = (
        contract(score_grad, k_ref[0, :, cols], 0, 0)
        + contract(peer_score_grad_ref[...], k_peers, 0, 0)
    ).astype(LOW)


def finish_kernel(top_step, offsets_ref, q_ref, k_ref, v_ref, gain_ref, expo_ref, out_ref, *refs):
    grad_norm_ref, stats_ref, place_ref, slots_ref = refs[:4]
    gain_refs, refs = refs[4:6], refs[6:]
    last_attended_ref, last_dq_ref, last_dk_ref, last_dv_ref = refs[:4]
    return_refs, refs = nearest_first(refs[4 : 4 + SPAN]), refs[4 + SPAN :]
    gain_out_ref, *result_hbm = refs[:5]
    held_ref, attended_ref, dq_ref, dk_ref, dv_ref, sems = refs[5:]
    gain_out_ref[...] = (gain_refs[0][...] + gain_refs[1][...]).reshape(gain_out_ref.shape)
    copies = [
        pltpu.make_async_copy(ref, hbm.at[0], sems.at[which])
        for which, (ref, hbm) in enumerate(zip((attended_ref, dq_ref, dk_ref, dv_ref), result_hbm))
    ]
    tokens, width = q_ref.shape[1:]
    picked = sum(picked_counts(tokens, top_step))
    score_scale = 1.0 / math.sqrt(HEAD_DIM)
    me = lax.axis_index("ctx")
    heads = range(OWNED)
    every = [head_cols(head) for head in heads]
    for distance, return_ref in enumerate(return_refs):
        held_ref[me ^ distance] = return_ref[...]
    blocks = [
        [held_ref[head, block * picked : (block + 1) * picked] for block in range(4)]
        for head in heads
    ]
    log_rows = [held_ref[head, 6 * picked : 6 * picked + STAT_TILES] for head in heads]
    attn_parts = [
        contract(blocks[head][3], place_ref[:, pl.ds(width + head * HEAD_DIM, picked)], 0, 1)
        for head in heads
    ]
    log_parts = [
        [contract(log_rows[head], slots_ref[:, head_cols(2 * head + level)], 1, 1) for level in (0, 1)]
        for head in heads
    ]
    placed = [
        contract(
            place_ref[:, pl.ds(head * HEAD_DIM, picked)],
            jnp.concatenate(blocks[head][:3], 1),
            1,
            0,
        )
        for head in heads
    ]
    factors, normeds, grad_lows, inners = [], [], [], []
    for head in heads:
        top_hit = hit_row(offsets_ref[1, head], top_step, tokens)
        mid_hit = hit_row(offsets_ref[0, head], R1, tokens)
        seen = jnp.maximum(top_hit, mid_hit) > 0.5
        top_log, mid_log = joined_row(log_parts[head][0], 0), joined_row(log_parts[head][1], TILE)
        top_score, total = stats_ref[head : head + 1, :], stats_ref[TILE + head : TILE + head + 1, :]
        log_total = jnp.where(
            top_hit > 0.5, top_log, jnp.where(mid_hit > 0.5, mid_log, top_score + jnp.log(total))
        )
        factors.append(jnp.exp(top_score - log_total))
        attn = jnp.where(seen, attn_parts[head], out_ref[:, every[head]])
        normed, _, grad_low, inner = norm_backward(attn, grad_norm_ref[:, every[head]])
        normeds.append(normed)
        grad_lows.append(grad_low)
        inners.append(inner)
    last = width // HEAD_DIM - 1
    last_cols = head_cols(last)
    prob_grads = [contract(v_ref[0, :, every[head]], grad_lows[head], 1, 0) for head in heads]
    for head in heads:
        attended_ref[:, every[head]] = (normeds[head].T * gain_ref[:, every[head]]).astype(LOW)
    attended_ref[:, last_cols] = last_attended_ref[...]
    copies[0].start()
    total = sum(ref[4 * picked : 6 * picked].astype(WIDE) for ref in return_refs[1:]).astype(LOW)
    rows = contract(
        place_ref[:, pl.ds(last * HEAD_DIM, picked)],
        jnp.concatenate([total[:picked], total[picked:]], 1),
        1,
        0,
    )
    softs = [expo_ref[:, every[head]].astype(WIDE) * factors[head] for head in heads]

    def put(block_ref, which, blocks, last_block):
        for head in heads:
            part = placed[head][:, which * HEAD_DIM : (which + 1) * HEAD_DIM]
            block_ref[:, every[head]] = (blocks[head] + part).astype(LOW)
        block_ref[:, last_cols] = last_block.astype(LOW)
        copies[which + 1].start()

    dvs = [contract(softs[head].astype(LOW), grad_lows[head], 1, 1) for head in heads]
    put(dv_ref, 2, dvs, last_dv_ref[...] + rows[:, HEAD_DIM:])
    score_grads = [
        (softs[head] * (prob_grads[head] - inners[head]) * score_scale).astype(LOW)
        for head in heads
    ]
    dks = [contract(score_grads[head], q_ref[0, :, every[head]], 1, 0) for head in heads]
    put(dk_ref, 1, dks, last_dk_ref[...] + rows[:, :HEAD_DIM])
    dqs = [contract(score_grads[head], k_ref[0, :, every[head]], 0, 0) for head in heads]
    put(dq_ref, 0, dqs, last_dq_ref[...])
    for copy in copies:
        copy.wait()


def across(block, axis, distance):
    route = [(place, place ^ distance) for place in range(lax.axis_size(axis))]
    return lax.ppermute(block, axis, route)


def to_peers(blocks):
    return [across(blocks[distance - 1], "ctx", distance) for distance in range(PEERS, 0, -1)]


def call(
    kernel, name, operands, results, microseconds, vmem=PLAIN_VMEM, scratch=(), in_hbm=0
):
    return pl.pallas_call(
        kernel,
        out_shape=results,
        in_specs=[SMEM_SPEC if block.dtype == jnp.int32 else VMEM_SPEC for block in operands],
        out_specs=[VMEM_SPEC] * (len(results) - in_hbm) + [HBM_SPEC] * in_hbm,
        scratch_shapes=scratch,
        compiler_params=pltpu.CompilerParams(vmem_limit_bytes=vmem),
        cost_estimate=pl.CostEstimate(
            flops=int(microseconds * 10**9), bytes_accessed=0, transcendentals=0
        ),
        name=name,
    )(*operands)


def one_segment_shards(queries, keys, values, grad_y, out_gain, offsets):
    tokens, width = queries.shape[1:]
    heads = width // HEAD_DIM
    top_step = lax.axis_size("ctx")
    picked = sum(picked_counts(tokens, top_step))
    shape = jax.ShapeDtypeStruct
    row_block = shape((1, tokens, width), LOW)
    low_block, wide_block = shape((tokens, width), LOW), shape((tokens, width), WIDE)
    low_head, wide_head = shape((tokens, HEAD_DIM), LOW), shape((tokens, HEAD_DIM), WIDE)
    gain_block = shape((1, width), WIDE)
    stats_block = shape((2 * TILE, tokens), WIDE)
    payload = shape((7 * picked + STAT_TILES, HEAD_DIM), LOW)
    answer = shape((6 * picked + STAT_TILES, HEAD_DIM), LOW)
    bind = functools.partial
    gain_row = out_gain.reshape(1, width)
    own, *sent, stats, expo, base_out = call(
        bind(pack_kernel, top_step),
        "pack",
        (offsets, queries, keys, values, grad_y),
        [payload] * SPAN + [stats_block, low_block, wide_block],
        1,
        vmem=PACK_VMEM,
        scratch=[
            pltpu.VMEM((OWNED, *payload.shape), LOW),
            pltpu.VMEM(low_block.shape, LOW),
            pltpu.VMEM(wide_block.shape, WIDE),
            pltpu.SemaphoreType.DMA((2,)),
        ],
        in_hbm=2,
    )
    received = to_peers(sent)
    grad_norm, gain_base, place, slots = call(
        bind(prepare_kernel, top_step),
        "prepare",
        (offsets, grad_y, gain_row, base_out),
        [wide_block, gain_block, shape((tokens, 2 * width), LOW), shape((tokens, 2 * OWNED * tokens), LOW)],
        2,
    )
    gain_part, normed, grad_low, score_grad, kept, own_answer, *answers = call(
        bind(owner_kernel, top_step),
        "owner",
        (offsets, queries, gain_row, base_out, grad_norm, stats, gain_base, own, *received),
        [
            gain_block,
            wide_head,
            low_head,
            shape((PEERS * picked, HEAD_DIM), LOW),
            shape((TILE, tokens), WIDE),
        ]
        + [answer] * SPAN,
        3,
    )
    returned = to_peers(answers)
    *last_results, gain_sum = call(
        bind(last_head_kernel, top_step),
        "last_head",
        (
            gain_part,
            across(gain_part, "ctx", 2),
            queries,
            keys,
            values,
            gain_row,
            expo,
            normed,
            grad_low,
            score_grad,
            kept,
            *received,
        ),
        [low_head, low_head, wide_head, wide_head, gain_block],
        20,
    )
    gain_sum = gain_sum + across(gain_sum, "dp", 1)
    gain_rest = across(gain_sum, "ctx", 1)
    gain_grad, attended, query_grad, key_grad, value_grad = call(
        bind(finish_kernel, top_step),
        "finish",
        (
            offsets,
            queries,
            keys,
            values,
            gain_row,
            expo,
            base_out,
            grad_norm,
            stats,
            place,
            slots,
            gain_sum,
            gain_rest,
            *last_results,
            own_answer,
            *returned,
        ),
        [shape((width,), WIDE)] + [row_block] * 4,
        1,
        scratch=[pltpu.VMEM((OWNED, *answer.shape), LOW)]
        + [pltpu.VMEM(low_block.shape, LOW)] * 4
        + [pltpu.SemaphoreType.DMA((4,))],
        in_hbm=4,
    )
    return attended, query_grad, key_grad, value_grad, gain_grad


def solution(mesh):
    in_specs = (
        P("dp", "ctx", "head"),
        P("dp", "ctx", "head"),
        P("dp", "ctx", "head"),
        P("dp", "ctx", "head"),
        P("head"),
        P(None, "head"),
    )
    out_specs = (
        P("dp", "ctx", "head"),
        P("dp", "ctx", "head"),
        P("dp", "ctx", "head"),
        P("dp", "ctx", "head"),
        P("head"),
    )
    body = one_segment_shards if mesh.shape["ctx"] == SPAN else general_shards
    return jax.shard_map(body, mesh=mesh, in_specs=in_specs, out_specs=out_specs, check_vma=False)
```

```python
import functools
import math

import jax
import jax.numpy as jnp
from jax import lax
from jax.experimental import pallas as pl
from jax.experimental.pallas import tpu as pltpu
from jax.sharding import PartitionSpec as P

HEAD_DIM = 128
SPAN = 4
R1 = 8


EPS = 1e-06


def swapped(block, axis, bit):
    count = lax.axis_size(axis)
    route = []
    for low in range(count):
        high = low | 1 << bit
        if high != low and high < count:
            route += [(low, high), (high, low)]
    return lax.ppermute(block, axis, route)


def pick_rows(source_rows, dilation, shifts):
    row_count, head_count, head_width = source_rows.shape
    grouped = source_rows.reshape(row_count // dilation, dilation, head_count, head_width)
    hit_mask = jnp.arange(dilation, dtype=jnp.int32).reshape(1, dilation, 1, 1) == shifts.reshape(
        1, 1, head_count, 1
    )
    chosen = jnp.where(hit_mask, grouped, jnp.zeros((), source_rows.dtype))
    return jnp.sum(chosen, axis=1, dtype=source_rows.dtype)


def place_rows(row_values, dilation, shifts):
    row_count, head_count, head_width = row_values.shape
    hit_mask = jnp.arange(dilation, dtype=jnp.int32).reshape(1, dilation, 1, 1) == shifts.reshape(
        1, 1, head_count, 1
    )
    spread = jnp.where(hit_mask, row_values[:, None], jnp.zeros((), row_values.dtype))
    return spread.reshape(row_count * dilation, head_count, head_width)


def level_scores(q_rows, k_rows):
    score_scale = 1.0 / math.sqrt(q_rows.shape[-1])
    return (
        jnp.einsum("qhe,khe->hqk", q_rows, k_rows, preferred_element_type=jnp.float32) * score_scale
    )


def attend(q_rows, k_rows, v_rows):
    scores = level_scores(q_rows, k_rows)
    row_max = jnp.max(scores, axis=-1, keepdims=True)
    log_total = row_max[..., 0] + jnp.log(jnp.sum(jnp.exp(scores - row_max), axis=-1))
    soft_rows = jnp.exp(scores - log_total[..., None]).astype(jnp.bfloat16)
    level_out = jnp.einsum("hqk,khe->qhe", soft_rows, v_rows, preferred_element_type=jnp.float32)
    return (level_out, log_total.T)


def score_grads(q_rows, k_rows, v_rows, log_total, grad_low, row_shift):
    score_scale = 1.0 / math.sqrt(q_rows.shape[-1])
    scores = level_scores(q_rows, k_rows)
    exact_soft = jnp.exp(scores - log_total.T[..., None])
    prob_grad = jnp.einsum("qhe,khe->hqk", grad_low, v_rows, preferred_element_type=jnp.float32)
    score_grad = (exact_soft * (prob_grad + row_shift.T[..., None]) * score_scale).astype(
        jnp.bfloat16
    )
    return (score_grad, exact_soft.astype(jnp.bfloat16))


def key_parts(score_grad, soft_low, q_rows, grad_low):
    k_part = jnp.einsum("hqk,qhe->khe", score_grad, q_rows, preferred_element_type=jnp.float32)
    v_part = jnp.einsum("hqk,qhe->khe", soft_low, grad_low, preferred_element_type=jnp.float32)
    return (k_part, v_part)


def query_part(score_grad, k_rows):
    return jnp.einsum("hqk,khe->qhe", score_grad, k_rows, preferred_element_type=jnp.float32)


def general_shards(queries, keys, values, grad_y, out_gain, offsets):
    tokens = queries.shape[1]
    flat_width = queries.shape[2]
    head_count = flat_width // HEAD_DIM
    row_shape = (tokens, head_count, HEAD_DIM)
    q_own = queries[0].reshape(row_shape)
    k_own = keys[0].reshape(row_shape)
    v_own = values[0].reshape(row_shape)
    ctx_size = lax.axis_size("ctx")
    span_bits = SPAN.bit_length() - 1
    my_place = lax.axis_index("ctx")
    mid_shift = offsets[0]
    top_shift = offsets[1]
    positions = jnp.arange(tokens, dtype=jnp.int32)
    mid_hit = (positions % R1)[:, None] == mid_shift[None, :]
    top_hit = (positions % ctx_size)[:, None] == top_shift[None, :]
    mid_q = pick_rows(q_own, R1, mid_shift)
    mid_k = pick_rows(k_own, R1, mid_shift)
    mid_v = pick_rows(v_own, R1, mid_shift)
    top_q = pick_rows(q_own, ctx_size, top_shift)
    top_k = pick_rows(k_own, ctx_size, top_shift)
    top_v = pick_rows(v_own, ctx_size, top_shift)
    mid_keys = mid_k.reshape(-1, flat_width)
    mid_vals = mid_v.reshape(-1, flat_width)
    top_keys = top_k.reshape(-1, flat_width)
    top_vals = top_v.reshape(-1, flat_width)

    def append_peer(mine, received, level_bit):
        upper_side = my_place >> level_bit & 1 == 1
        return jnp.where(
            upper_side, jnp.concatenate([received, mine], 0), jnp.concatenate([mine, received], 0)
        )

    for level_bit in range(span_bits):
        received = swapped((mid_keys, mid_vals), "ctx", level_bit)
        mid_keys = append_peer(mid_keys, received[0], level_bit)
        mid_vals = append_peer(mid_vals, received[1], level_bit)
    top_keys, top_vals = (
        lax.all_gather(top_keys, "ctx", axis=0, tiled=True),
        lax.all_gather(top_vals, "ctx", axis=0, tiled=True),
    )
    mid_keys = mid_keys.reshape(-1, head_count, HEAD_DIM)
    mid_vals = mid_vals.reshape(-1, head_count, HEAD_DIM)
    top_keys = top_keys.reshape(-1, head_count, HEAD_DIM)
    top_vals = top_vals.reshape(-1, head_count, HEAD_DIM)
    base_out, base_total = attend(q_own, k_own, v_own)
    mid_out, mid_total = attend(mid_q, mid_keys, mid_vals)
    top_out, top_total = attend(top_q, top_keys, top_vals)
    mid_full = place_rows(mid_total[..., None], R1, mid_shift)[..., 0]
    top_full = place_rows(top_total[..., None], ctx_size, top_shift)[..., 0]
    row_max = jnp.maximum(base_total, jnp.where(mid_hit, mid_full, base_total))
    row_max = jnp.maximum(row_max, jnp.where(top_hit, top_full, base_total))
    base_expo = jnp.exp(base_total - row_max)
    mid_expo = jnp.where(mid_hit, jnp.exp(mid_full - row_max), 0.0)
    top_expo = jnp.where(top_hit, jnp.exp(top_full - row_max), 0.0)
    denom = base_expo + mid_expo + top_expo
    base_share = base_expo / denom
    mid_share = mid_expo / denom
    top_share = top_expo / denom
    attn = (
        base_share[..., None] * base_out
        + mid_share[..., None] * place_rows(mid_out, R1, mid_shift)
        + top_share[..., None] * place_rows(top_out, ctx_size, top_shift)
    )
    inv_rms = lax.rsqrt(jnp.mean(attn * attn, axis=-1, keepdims=True) + EPS)
    normed = attn * inv_rms
    gain_rows = out_gain.reshape(head_count, HEAD_DIM)
    attended = (normed * gain_rows).astype(jnp.bfloat16).reshape(1, tokens, flat_width)
    grad_full = grad_y[0].reshape(row_shape).astype(jnp.float32)
    gain_part = jnp.sum(grad_full * normed, axis=0).reshape(flat_width)
    gain_grad = lax.psum(gain_part, ("dp", "ctx"))
    grad_norm = grad_full * gain_rows
    grad_attn = inv_rms * (
        grad_norm - normed * jnp.mean(grad_norm * normed, axis=-1, keepdims=True)
    )
    inner = jnp.sum(grad_attn * attn, axis=-1)
    base_low = (base_share[..., None] * grad_attn).astype(jnp.bfloat16)
    base_shift = -(base_share * inner)
    base_grad, base_soft = score_grads(q_own, k_own, v_own, base_total, base_low, base_shift)
    base_dq = query_part(base_grad, k_own)
    base_dk, base_dv = key_parts(base_grad, base_soft, q_own, base_low)
    mid_sel = pick_rows(mid_share[..., None], R1, mid_shift)[..., 0]
    mid_low = (mid_sel[..., None] * pick_rows(grad_attn, R1, mid_shift)).astype(jnp.bfloat16)
    mid_row_shift = -(mid_sel * pick_rows(inner[..., None], R1, mid_shift)[..., 0])
    mid_grad, mid_soft = score_grads(mid_q, mid_keys, mid_vals, mid_total, mid_low, mid_row_shift)
    mid_dq = query_part(mid_grad, mid_keys)
    mid_dk, mid_dv = key_parts(mid_grad, mid_soft, mid_q, mid_low)
    mid_dk = mid_dk.reshape(-1, flat_width)
    mid_dv = mid_dv.reshape(-1, flat_width)
    for level_bit in reversed(range(span_bits)):
        half_rows = mid_dk.shape[0] // 2
        upper_side = my_place >> level_bit & 1 == 1
        keep_k = jnp.where(upper_side, mid_dk[half_rows:], mid_dk[:half_rows])
        keep_v = jnp.where(upper_side, mid_dv[half_rows:], mid_dv[:half_rows])
        send_k = jnp.where(upper_side, mid_dk[:half_rows], mid_dk[half_rows:])
        send_v = jnp.where(upper_side, mid_dv[:half_rows], mid_dv[half_rows:])
        received = (
            swapped(send_k.astype(jnp.bfloat16), "ctx", level_bit).astype(send_k.dtype),
            swapped(send_v.astype(jnp.bfloat16), "ctx", level_bit).astype(send_v.dtype),
        )
        mid_dk = keep_k + received[0]
        mid_dv = keep_v + received[1]
    mid_dk = mid_dk.reshape(-1, head_count, HEAD_DIM)
    mid_dv = mid_dv.reshape(-1, head_count, HEAD_DIM)
    top_sel = pick_rows(top_share[..., None], ctx_size, top_shift)[..., 0]
    top_low = (top_sel[..., None] * pick_rows(grad_attn, ctx_size, top_shift)).astype(jnp.bfloat16)
    top_row_shift = -(top_sel * pick_rows(inner[..., None], ctx_size, top_shift)[..., 0])
    top_grad, top_soft = score_grads(top_q, top_keys, top_vals, top_total, top_low, top_row_shift)
    top_dq = query_part(top_grad, top_keys)
    gathered_dk, gathered_dv = key_parts(top_grad, top_soft, top_q, top_low)
    summed = (
        lax.psum_scatter(
            gathered_dk.reshape(-1, flat_width), "ctx", scatter_dimension=0, tiled=True
        ),
        lax.psum_scatter(
            gathered_dv.reshape(-1, flat_width), "ctx", scatter_dimension=0, tiled=True
        ),
    )
    top_dk = summed[0].reshape(-1, head_count, HEAD_DIM)
    top_dv = summed[1].reshape(-1, head_count, HEAD_DIM)
    query_grad = (
        base_dq + place_rows(mid_dq, R1, mid_shift) + place_rows(top_dq, ctx_size, top_shift)
    )
    key_grad = base_dk + place_rows(mid_dk, R1, mid_shift) + place_rows(top_dk, ctx_size, top_shift)
    value_grad = (
        base_dv + place_rows(mid_dv, R1, mid_shift) + place_rows(top_dv, ctx_size, top_shift)
    )
    out_shape = (1, tokens, flat_width)
    return (
        attended,
        query_grad.astype(jnp.bfloat16).reshape(out_shape),
        key_grad.astype(jnp.bfloat16).reshape(out_shape),
        value_grad.astype(jnp.bfloat16).reshape(out_shape),
        gain_grad,
    )


VMEM_SPEC = pl.BlockSpec(memory_space=pltpu.VMEM)
SMEM_SPEC = pl.BlockSpec(memory_space=pltpu.SMEM)
PEERS = SPAN - 1
OWNED = SPAN
TILE = 8
STAT_TILES = 2 * TILE
PIECES = 3
NEVER = -1e30
LOW = jnp.bfloat16
WIDE = jnp.float32
PACK_VMEM = 65408 * 1024
PLAIN_VMEM = 16 * 1024 * 1024


def contract(left, right, left_dim, right_dim):
    return lax.dot_general(
        left, right, (((left_dim,), (right_dim,)), ((), ())), preferred_element_type=WIDE
    )


def head_cols(head):
    return pl.ds(head * HEAD_DIM, HEAD_DIM)


def picked_counts(tokens, top_step):
    return tokens // top_step, tokens // R1


def pick_matrix(offsets_ref, head, tokens, top_step, picked_axis):
    top_rows, mid_rows = picked_counts(tokens, top_step)
    shape = (top_rows + mid_rows, tokens) if picked_axis == 0 else (tokens, top_rows + mid_rows)
    row = lax.broadcasted_iota(jnp.int32, shape, picked_axis)
    position = lax.broadcasted_iota(jnp.int32, shape, 1 - picked_axis)
    wanted = jnp.where(
        row < top_rows,
        row * top_step + offsets_ref[1, head],
        (row - top_rows) * R1 + offsets_ref[0, head],
    )
    return jnp.where(position == wanted, 1.0, 0.0).astype(LOW)


def slot_matrix(offset, step, slot, tokens):
    count = tokens // step
    position = lax.broadcasted_iota(jnp.int32, (tokens, tokens), 0)
    index = lax.broadcasted_iota(jnp.int32, (tokens, tokens), 1) - slot * count
    inside = (index >= 0) & (index < count)
    return jnp.where(inside & (position == index * step + offset), 1.0, 0.0).astype(LOW)


def hit_row(offset, step, tokens):
    position = lax.broadcasted_iota(jnp.int32, (1, tokens), 1)
    return jnp.where(position % step == offset, 1.0, 0.0)


def piece_rows(row, others=None):
    pieces = []
    for _ in range(PIECES):
        piece = row.astype(LOW).astype(WIDE)
        pieces.append(piece)
        row = row - piece
    if others is None:
        others = jnp.zeros((TILE - PIECES, row.shape[1]), WIDE)
    return jnp.concatenate(pieces + [others], 0)


def gain_pieces(rows):
    high = rows.astype(LOW)
    return high, (rows - high.astype(WIDE)).astype(LOW)


def joined_row(rows, first):
    total = rows[first : first + 1]
    for piece in range(1, PIECES):
        total = total + rows[first + piece : first + piece + 1]
    return total


def gain_row_of(ones, product):
    high, rest = gain_pieces(product)
    return (contract(ones, high, 1, 1) + contract(ones, rest, 1, 1))[:1]


def column_mean(block):
    return jnp.mean(block, axis=0, keepdims=True)


def norm_backward(attn, grad_norm):
    inv_rms = lax.rsqrt(column_mean(attn * attn) + EPS)
    normed = attn * inv_rms
    product = grad_norm * normed
    grad_attn = inv_rms * (grad_norm - normed * column_mean(product))
    inner = jnp.sum(grad_attn * attn, axis=0, keepdims=True)
    return normed, product, grad_attn.astype(LOW), inner


def nearest_first(refs):
    return [refs[0], *refs[:0:-1]]


def pack_kernel(top_step, offsets_ref, q_ref, k_ref, v_ref, grad_ref, *refs):
    payload_refs, (expo_ref, out_ref, stats_ref, held_ref) = refs[:SPAN], refs[SPAN:]
    tokens, width = q_ref.shape[1:]
    heads = range(width // HEAD_DIM)
    owned = range(OWNED)
    me = lax.axis_index("ctx")
    picked = sum(picked_counts(tokens, top_step))
    score_scale = 1.0 / math.sqrt(HEAD_DIM)
    q_rows, k_rows, v_rows, grad_rows = [
        [ref[0, :, head_cols(head)] for head in heads] for ref in (q_ref, k_ref, v_ref, grad_ref)
    ]
    picks = [pick_matrix(offsets_ref, head, tokens, top_step, 0) for head in heads]
    scores = [contract(k_rows[head], q_rows[head], 1, 1) * score_scale for head in heads]
    moved = [
        contract(
            picks[head],
            jnp.concatenate([q_rows[head], k_rows[head], v_rows[head], grad_rows[head]], 1),
            1,
            0,
        ).astype(LOW)
        for head in owned
    ]
    shared = [
        contract(picks[head], jnp.concatenate([k_rows[head], v_rows[head]], 1), 1, 0).astype(LOW)
        for head in heads[OWNED:]
    ]
    top_scores = [jnp.max(block, axis=0, keepdims=True) for block in scores]
    expos = [jnp.exp(scores[head] - top_scores[head]) for head in heads]
    for head in heads[OWNED:]:
        key_row = lax.broadcasted_iota(jnp.int32, (tokens, 1), 0)
        times = 1.0
        for level, step in ((0, R1), (1, top_step)):
            offset = offsets_ref[level, head]
            hit_column = jnp.where(key_row % step == offset, 1.0, 0.0)
            times = times + hit_column * hit_row(offset, step, tokens)
        expos[head] = times * expos[head]
    expo_lows = [expo.astype(LOW) for expo in expos]
    outs = [contract(v_rows[head], expo_lows[head], 0, 0) for head in heads]
    totals = [jnp.sum(expo, axis=0, keepdims=True) for expo in expos]
    for head in heads:
        expo_ref[:, head_cols(head)] = expo_lows[head]
        stats_ref[head : head + 1, :] = top_scores[head]
        stats_ref[TILE + head : TILE + head + 1, :] = totals[head]
    for head in owned:
        outs[head] = outs[head] * (1.0 / totals[head])
    outs = [out.astype(LOW) for out in outs]
    picked_outs = [contract(picks[head], outs[head], 1, 1).astype(LOW) for head in owned]
    for head in heads:
        out_ref[:, head_cols(head)] = outs[head]
    for head in owned:
        pieces = piece_rows(top_scores[head] + jnp.log(totals[head])).astype(LOW)
        slot = me ^ head
        stat_rows = [
            contract(pieces, slot_matrix(offsets_ref[level, head], step, slot, tokens), 1, 0)
            for level, step in ((1, top_step), (0, R1))
        ]
        blocks = [moved[head][:, block * HEAD_DIM : (block + 1) * HEAD_DIM] for block in range(4)]
        blocks.append(picked_outs[head])
        blocks += [shared[0][:, :HEAD_DIM], shared[0][:, HEAD_DIM:]]
        blocks.append(jnp.concatenate(stat_rows, 0).astype(LOW))
        held_ref[head] = jnp.concatenate(blocks, 0)
    for distance, payload_ref in enumerate(payload_refs):
        payload_ref[...] = held_ref[me ^ distance]


def prepare_kernel(top_step, offsets_ref, grad_ref, gain_ref, out_ref, *refs):
    grad_norm_ref, gain_part_ref, place_ref, slots_ref = refs
    tokens, width = grad_ref.shape[1:]
    heads = range(width // HEAD_DIM)
    me = lax.axis_index("ctx")
    picked = sum(picked_counts(tokens, top_step))
    top_rows = tokens // top_step
    ones = jnp.ones((TILE, tokens), LOW)
    column = lax.broadcasted_iota(jnp.int32, (tokens, picked), 1)
    gain_part_ref[...] = jnp.zeros(gain_part_ref.shape, WIDE)
    grad_norms = [
        (grad_ref[0, :, head_cols(head)].astype(WIDE) * gain_ref[:, head_cols(head)]).T
        for head in heads
    ]
    for head in heads:
        cols = head_cols(head)
        grad_norm_ref[:, cols] = grad_norms[head]
        picks = pick_matrix(offsets_ref, head, tokens, top_step, 1)
        place_ref[:, pl.ds(head * HEAD_DIM, picked)] = picks
    for head in range(OWNED):
        cols = head_cols(head)
        mid_offset, top_offset = offsets_ref[0, head], offsets_ref[1, head]
        seen = jnp.maximum(
            hit_row(top_offset, top_step, tokens), hit_row(mid_offset, R1, tokens)
        )
        attn = out_ref[:, cols].astype(WIDE)
        normed = attn * lax.rsqrt(column_mean(attn * attn) + EPS)
        product = grad_norms[head] * normed * (1.0 - seen)
        gain_part_ref[:, cols] = gain_row_of(ones, product) / gain_ref[:, cols]
        both = mid_offset % top_step == top_offset
        kept = jnp.where(column < top_rows, 1.0, jnp.where(both, 0.0, 1.0)).astype(LOW)
        picks = pick_matrix(offsets_ref, head, tokens, top_step, 1)
        place_ref[:, pl.ds(width + head * HEAD_DIM, picked)] = picks * kept
        for index, (offset, step) in enumerate(((top_offset, top_step), (mid_offset, R1))):
            slots_ref[:, head_cols(2 * head + index)] = slot_matrix(
                offset, step, me ^ head, tokens
            )


def owner_kernel(top_step, offsets_ref, q_ref, gain_ref, out_ref, grad_norm_ref, *refs):
    stats_ref, gain_base_ref = refs[:2]
    payload_refs, refs = nearest_first(refs[2 : 2 + SPAN]), refs[2 + SPAN :]
    normed_ref, grad_low_ref, score_grad_ref, kept_ref = refs[:4]
    return_refs = refs[4:]
    tokens = q_ref.shape[1]
    heads = q_ref.shape[2] // HEAD_DIM
    top_rows, mid_rows = picked_counts(tokens, top_step)
    picked = top_rows + mid_rows
    top_all, mid_all = SPAN * top_rows, SPAN * mid_rows
    queries = top_all + mid_all
    score_scale = 1.0 / math.sqrt(HEAD_DIM)
    me = lax.axis_index("ctx")
    ones = jnp.ones((TILE, tokens), LOW)

    def by_level(block):
        start = block * picked
        return jnp.concatenate(
            [ref[start : start + top_rows] for ref in payload_refs]
            + [ref[start + top_rows : start + picked] for ref in payload_refs],
            0,
        )

    def per_level(top_row, mid_row):
        return jnp.concatenate(
            [
                jnp.broadcast_to(top_row, (top_all, queries)),
                jnp.broadcast_to(mid_row, (mid_all, queries)),
            ],
            0,
        )

    q_rows, k_rows, v_rows, grad_rows, base_rows = [by_level(block) for block in range(5)]
    stat_start = 7 * picked
    stat_rows = sum(
        ref[stat_start : stat_start + STAT_TILES].astype(WIDE) for ref in payload_refs
    )
    base_log = jnp.concatenate(
        [joined_row(stat_rows, 0), joined_row(stat_rows, TILE)[:, :mid_all]], 1
    )
    gain_row = jnp.zeros((1, HEAD_DIM), WIDE)
    for head in range(OWNED):
        gain_row = gain_row + jnp.where(me == head, 1.0, 0.0) * gain_ref[:, head_cols(head)]
    mid_offset, top_offset = offsets_ref[0, me], offsets_ref[1, me]
    both = mid_offset % top_step == top_offset
    lane = lax.broadcasted_iota(jnp.int32, (1, queries), 1)
    is_top = jnp.where(lane < top_all, 1.0, 0.0)
    top_in_mid = jnp.where(((lane % top_rows) * top_step + top_offset) % R1 == mid_offset, 1.0, 0.0)
    both_flag = jnp.where(both, 1.0, 0.0)
    sees_top = is_top + (1.0 - is_top) * both_flag
    sees_mid = is_top * top_in_mid + (1.0 - is_top)
    bias = per_level((1.0 - sees_top) * NEVER, (1.0 - sees_mid) * NEVER)
    same_level = per_level(is_top, 1.0 - is_top)
    last = heads - 1
    cols = head_cols(last)
    peers = payload_refs[1:]
    q_last = q_ref[0, :, cols]
    k_peers = jnp.concatenate([ref[5 * picked : 6 * picked] for ref in peers], 0)
    v_peers = jnp.concatenate([ref[6 * picked : 7 * picked] for ref in peers], 0)
    last_biases = [
        jnp.broadcast_to((1.0 - hit_row(offsets_ref[level, last], step, tokens)) * NEVER, shape)
        for level, step, shape in (
            (1, top_step, (top_rows, tokens)),
            (0, R1, (mid_rows, tokens)),
        )
    ]
    scores = contract(k_rows, q_rows, 1, 1) * score_scale + bias
    scores_last = contract(k_peers, q_last, 1, 1) * score_scale + jnp.concatenate(
        last_biases * PEERS, 0
    )
    base_attn = base_rows.astype(WIDE).T
    grad_norm = (grad_rows.astype(WIDE) * gain_row).T
    top_score = jnp.maximum(base_log, jnp.max(scores, axis=0, keepdims=True))
    base_top, base_total = stats_ref[last : last + 1, :], stats_ref[TILE + last : TILE + last + 1, :]
    top_last = jnp.maximum(base_top, jnp.max(scores_last, axis=0, keepdims=True))
    expo = jnp.exp(scores - top_score)
    expo_last = jnp.exp(scores_last - top_last)
    factor = jnp.exp(base_log - top_score)
    factor_last = jnp.exp(base_top - top_last)
    total = factor + jnp.sum(expo, axis=0, keepdims=True)
    total_last = factor_last * base_total + jnp.sum(expo_last, axis=0, keepdims=True)
    inv_total, inv_last = 1.0 / total, 1.0 / total_last
    soft, soft_last = expo * inv_total, expo_last * inv_last
    soft_low, soft_last_low = soft.astype(LOW), soft_last.astype(LOW)
    factor_last = factor_last * inv_last
    attn = (factor * inv_total) * base_attn + contract(v_rows, soft_low, 0, 0)
    attn_last = factor_last * out_ref[:, cols].astype(WIDE) + contract(v_peers, soft_last_low, 0, 0)
    _, product, grad_low, inner = norm_backward(attn, grad_norm)
    normed_last, product_last, grad_last_low, inner_last = norm_backward(
        attn_last, grad_norm_ref[:, cols]
    )
    prob_grad = contract(v_rows, grad_low, 1, 0)
    prob_grad_last = contract(v_peers, grad_last_low, 1, 0)
    soft = soft * same_level
    score_grad = (soft * (prob_grad - inner) * score_scale).astype(LOW)
    score_grad_last = (soft_last * (prob_grad_last - inner_last) * score_scale).astype(LOW)
    dk = contract(score_grad, q_rows, 1, 0).astype(LOW)
    dk_last = contract(score_grad_last, q_last, 1, 0).astype(LOW)
    dv = contract(soft.astype(LOW), grad_low, 1, 1).astype(LOW)
    dv_last = contract(soft_last_low, grad_last_low, 1, 1).astype(LOW)
    dq = contract(score_grad, k_rows, 0, 0).astype(LOW)
    attn_rows = attn.T.astype(LOW)
    log_total = top_score + jnp.log(total)
    padding = jnp.zeros((1, top_all - mid_all), WIDE)
    once = is_top + (1.0 - is_top) * (1.0 - both_flag)
    ones_all = jnp.ones((TILE, queries), LOW)
    own_gain = gain_row_of(ones_all, product * once) / gain_row
    gain_rows = [
        gain_base_ref[:, head_cols(head)] + jnp.where(me == head, 1.0, 0.0) * own_gain
        for head in range(OWNED)
    ]
    gain_rows.append(gain_row_of(ones, product_last) / gain_ref[:, cols])
    gain_high, gain_rest = gain_pieces(jnp.concatenate(gain_rows, 0))
    log_rows = jnp.concatenate(
        [
            piece_rows(log_total[:, :top_all], gain_high.astype(WIDE)),
            piece_rows(
                jnp.concatenate([log_total[:, top_all:], padding], 1), gain_rest.astype(WIDE)
            ),
        ],
        0,
    ).astype(LOW)
    for distance, return_ref in enumerate(return_refs):
        blocks = []
        for rows in (dq, dk, dv, attn_rows):
            mid_start = top_all + distance * mid_rows
            blocks.append(rows[distance * top_rows : (distance + 1) * top_rows])
            blocks.append(rows[mid_start : mid_start + mid_rows])
        start = max(distance - 1, 0) * picked
        blocks += [dk_last[start : start + picked], dv_last[start : start + picked], log_rows]
        return_ref[...] = jnp.concatenate(blocks, 0)
    normed_ref[...] = normed_last
    grad_low_ref[...] = grad_last_low
    score_grad_ref[...] = score_grad_last
    kept_ref[0:1, :] = factor_last
    kept_ref[1:2, :] = inner_last


def last_head_kernel(top_step, q_ref, k_ref, v_ref, gain_ref, expo_ref, *refs):
    normed_ref, grad_low_ref, peer_score_grad_ref, kept_ref, *peers = refs[: 4 + PEERS]
    peers = peers[::-1]
    attended_ref, dq_ref, dk_ref, dv_ref = refs[4 + PEERS :]
    picked = sum(picked_counts(q_ref.shape[1], top_step))
    score_scale = 1.0 / math.sqrt(HEAD_DIM)
    cols = head_cols(q_ref.shape[2] // HEAD_DIM - 1)
    attended_ref[...] = (normed_ref[...].T * gain_ref[:, cols]).astype(LOW)
    k_peers = jnp.concatenate([ref[5 * picked : 6 * picked] for ref in peers], 0)
    grad_low = grad_low_ref[...]
    soft = expo_ref[:, cols].astype(WIDE) * kept_ref[0:1, :]
    prob_grad = contract(v_ref[0, :, cols], grad_low, 1, 0)
    score_grad = (soft * (prob_grad - kept_ref[1:2, :]) * score_scale).astype(LOW)
    dk_ref[...] = contract(score_grad, q_ref[0, :, cols], 1, 0)
    dv_ref[...] = contract(soft.astype(LOW), grad_low, 1, 1)
    dq_ref[...] = (
        contract(score_grad, k_ref[0, :, cols], 0, 0)
        + contract(peer_score_grad_ref[...], k_peers, 0, 0)
    ).astype(LOW)


def gain_kernel(picked, *refs):
    return_refs, gain_ref = nearest_first(refs[:SPAN]), refs[SPAN]
    tiles = [ref[6 * picked : 6 * picked + STAT_TILES].astype(WIDE) for ref in return_refs]
    parts = [tile[PIECES:TILE] + tile[TILE + PIECES :] for tile in tiles]
    total = (parts[0] + parts[1]) + (parts[2] + parts[3])
    for head in range(gain_ref.shape[1] // HEAD_DIM):
        gain_ref[:, head_cols(head)] = total[head : head + 1]


def finish_kernel(top_step, offsets_ref, q_ref, k_ref, v_ref, gain_ref, expo_ref, out_ref, *refs):
    grad_norm_ref, stats_ref, place_ref, slots_ref = refs[:4]
    gain_in_ref, last_attended_ref, last_dq_ref, last_dk_ref, last_dv_ref = refs[4:9]
    return_refs, refs = nearest_first(refs[9 : 9 + SPAN]), refs[9 + SPAN :]
    attended_ref, dq_ref, dk_ref, dv_ref, gain_out_ref, held_ref = refs
    gain_out_ref[...] = gain_in_ref[...]
    tokens, width = q_ref.shape[1:]
    picked = sum(picked_counts(tokens, top_step))
    score_scale = 1.0 / math.sqrt(HEAD_DIM)
    me = lax.axis_index("ctx")
    heads = range(OWNED)
    every = [head_cols(head) for head in heads]
    for distance, return_ref in enumerate(return_refs):
        held_ref[me ^ distance] = return_ref[...]
    blocks = [
        [held_ref[head, block * picked : (block + 1) * picked] for block in range(4)]
        for head in heads
    ]
    log_rows = [held_ref[head, 6 * picked : 6 * picked + STAT_TILES] for head in heads]
    attn_parts = [
        contract(blocks[head][3], place_ref[:, pl.ds(width + head * HEAD_DIM, picked)], 0, 1)
        for head in heads
    ]
    log_parts = [
        [contract(log_rows[head], slots_ref[:, head_cols(2 * head + level)], 1, 1) for level in (0, 1)]
        for head in heads
    ]
    placed = [
        contract(
            place_ref[:, pl.ds(head * HEAD_DIM, picked)],
            jnp.concatenate(blocks[head][:3], 1),
            1,
            0,
        )
        for head in heads
    ]
    factors, normeds, grad_lows, inners = [], [], [], []
    for head in heads:
        top_hit = hit_row(offsets_ref[1, head], top_step, tokens)
        mid_hit = hit_row(offsets_ref[0, head], R1, tokens)
        seen = jnp.maximum(top_hit, mid_hit) > 0.5
        top_log, mid_log = joined_row(log_parts[head][0], 0), joined_row(log_parts[head][1], TILE)
        top_score, total = stats_ref[head : head + 1, :], stats_ref[TILE + head : TILE + head + 1, :]
        log_total = jnp.where(
            top_hit > 0.5, top_log, jnp.where(mid_hit > 0.5, mid_log, top_score + jnp.log(total))
        )
        factors.append(jnp.exp(top_score - log_total))
        attn = jnp.where(seen, attn_parts[head], out_ref[:, every[head]].astype(WIDE))
        normed, _, grad_low, inner = norm_backward(attn, grad_norm_ref[:, every[head]])
        normeds.append(normed)
        grad_lows.append(grad_low)
        inners.append(inner)
    prob_grads = [contract(v_ref[0, :, every[head]], grad_lows[head], 1, 0) for head in heads]
    softs = [expo_ref[:, every[head]].astype(WIDE) * factors[head] for head in heads]
    dvs = [contract(softs[head].astype(LOW), grad_lows[head], 1, 1) for head in heads]
    score_grads = [
        (softs[head] * (prob_grads[head] - inners[head]) * score_scale).astype(LOW)
        for head in heads
    ]
    dks = [contract(score_grads[head], q_ref[0, :, every[head]], 1, 0) for head in heads]
    dqs = [contract(score_grads[head], k_ref[0, :, every[head]], 0, 0) for head in heads]
    for head in heads:
        cols = every[head]
        attended_ref[0, :, cols] = (normeds[head].T * gain_ref[:, cols]).astype(LOW)
        for which, (block, out_block_ref) in enumerate(
            ((dqs[head], dq_ref), (dks[head], dk_ref), (dvs[head], dv_ref))
        ):
            part = placed[head][:, which * HEAD_DIM : (which + 1) * HEAD_DIM]
            out_block_ref[0, :, cols] = (block + part).astype(LOW)
    last = width // HEAD_DIM - 1
    cols = head_cols(last)
    total = sum(ref[4 * picked : 6 * picked].astype(WIDE) for ref in return_refs[1:]).astype(LOW)
    rows = contract(
        place_ref[:, pl.ds(last * HEAD_DIM, picked)],
        jnp.concatenate([total[:picked], total[picked:]], 1),
        1,
        0,
    )
    attended_ref[0, :, cols] = last_attended_ref[...]
    dq_ref[0, :, cols] = last_dq_ref[...]
    dk_ref[0, :, cols] = (last_dk_ref[...] + rows[:, :HEAD_DIM]).astype(LOW)
    dv_ref[0, :, cols] = (last_dv_ref[...] + rows[:, HEAD_DIM:]).astype(LOW)


def across(block, axis, distance):
    route = [(place, place ^ distance) for place in range(lax.axis_size(axis))]
    return lax.ppermute(block, axis, route)


def to_peers(blocks):
    return [across(blocks[distance - 1], "ctx", distance) for distance in range(PEERS, 0, -1)]


def call(kernel, name, operands, results, microseconds, vmem=PLAIN_VMEM, scratch=()):
    return pl.pallas_call(
        kernel,
        out_shape=results,
        in_specs=[SMEM_SPEC if block.dtype == jnp.int32 else VMEM_SPEC for block in operands],
        out_specs=[VMEM_SPEC] * len(results),
        scratch_shapes=scratch,
        compiler_params=pltpu.CompilerParams(vmem_limit_bytes=vmem),
        cost_estimate=pl.CostEstimate(
            flops=int(microseconds * 10**9), bytes_accessed=0, transcendentals=0
        ),
        name=name,
    )(*operands)


def one_segment_shards(queries, keys, values, grad_y, out_gain, offsets):
    tokens, width = queries.shape[1:]
    heads = width // HEAD_DIM
    top_step = lax.axis_size("ctx")
    picked = sum(picked_counts(tokens, top_step))
    shape = jax.ShapeDtypeStruct
    row_block = shape((1, tokens, width), LOW)
    low_block, wide_block = shape((tokens, width), LOW), shape((tokens, width), WIDE)
    low_head, wide_head = shape((tokens, HEAD_DIM), LOW), shape((tokens, HEAD_DIM), WIDE)
    gain_block = shape((1, width), WIDE)
    stats_block = shape((2 * TILE, tokens), WIDE)
    payload = shape((7 * picked + STAT_TILES, HEAD_DIM), LOW)
    answer = shape((6 * picked + STAT_TILES, HEAD_DIM), LOW)
    bind = functools.partial
    gain_row = out_gain.reshape(1, width)
    own, *sent, expo, base_out, stats = call(
        bind(pack_kernel, top_step),
        "pack",
        (offsets, queries, keys, values, grad_y),
        [payload] * SPAN + [low_block, low_block, stats_block],
        1,
        vmem=PACK_VMEM,
        scratch=[pltpu.VMEM((OWNED, *payload.shape), LOW)],
    )
    received = to_peers(sent)
    grad_norm, gain_base, place, slots = call(
        bind(prepare_kernel, top_step),
        "prepare",
        (offsets, grad_y, gain_row, base_out),
        [wide_block, gain_block, shape((tokens, 2 * width), LOW), shape((tokens, 2 * OWNED * tokens), LOW)],
        2,
    )
    normed, grad_low, score_grad, kept, own_answer, *answers = call(
        bind(owner_kernel, top_step),
        "owner",
        (offsets, queries, gain_row, base_out, grad_norm, stats, gain_base, own, *received),
        [
            wide_head,
            low_head,
            shape((PEERS * picked, HEAD_DIM), LOW),
            shape((TILE, tokens), WIDE),
        ]
        + [answer] * SPAN,
        3,
    )
    returned = to_peers(answers)
    last_results = call(
        bind(last_head_kernel, top_step),
        "last_head",
        (queries, keys, values, gain_row, expo, normed, grad_low, score_grad, kept, *received),
        [low_head, low_head, wide_head, wide_head],
        20,
    )
    (gain_sum,) = call(bind(gain_kernel, picked), "gain", (own_answer, *returned), [gain_block], 1)
    gain_rest = across(gain_sum, "dp", 1)
    attended, query_grad, key_grad, value_grad, gain_sum = call(
        bind(finish_kernel, top_step),
        "finish",
        (
            offsets,
            queries,
            keys,
            values,
            gain_row,
            expo,
            base_out,
            grad_norm,
            stats,
            place,
            slots,
            gain_sum,
            *last_results,
            own_answer,
            *returned,
        ),
        [row_block] * 4 + [gain_block],
        1,
        scratch=[pltpu.VMEM((OWNED, *answer.shape), LOW)],
    )
    gain_grad = (gain_sum + gain_rest).reshape(width)
    return attended, query_grad, key_grad, value_grad, gain_grad


def shards(*operands):
    one_segment = lax.axis_size("ctx") == SPAN
    if one_segment and operands[0].shape[2] == (OWNED + 1) * HEAD_DIM:
        return one_segment_shards(*operands)
    return general_shards(*operands)


def solution(mesh):
    in_specs = (
        P("dp", "ctx", "head"),
        P("dp", "ctx", "head"),
        P("dp", "ctx", "head"),
        P("dp", "ctx", "head"),
        P("head"),
        P(None, "head"),
    )
    out_specs = (
        P("dp", "ctx", "head"),
        P("dp", "ctx", "head"),
        P("dp", "ctx", "head"),
        P("dp", "ctx", "head"),
        P("head"),
    )
    return jax.shard_map(shards, mesh=mesh, in_specs=in_specs, out_specs=out_specs, check_vma=False)
```

```python
import functools
import math

import jax
import jax.numpy as jnp
from jax import lax
from jax.experimental import pallas as pl
from jax.experimental.pallas import tpu as pltpu
from jax.sharding import PartitionSpec as P

HEAD_DIM = 128
SPAN = 4
R1 = 8


EPS = 1e-06


def swapped(block, axis, bit):
    count = lax.axis_size(axis)
    route = []
    for low in range(count):
        high = low | 1 << bit
        if high != low and high < count:
            route += [(low, high), (high, low)]
    return lax.ppermute(block, axis, route)


def pick_rows(source_rows, dilation, shifts):
    row_count, head_count, head_width = source_rows.shape
    grouped = source_rows.reshape(row_count // dilation, dilation, head_count, head_width)
    hit_mask = jnp.arange(dilation, dtype=jnp.int32).reshape(1, dilation, 1, 1) == shifts.reshape(
        1, 1, head_count, 1
    )
    chosen = jnp.where(hit_mask, grouped, jnp.zeros((), source_rows.dtype))
    return jnp.sum(chosen, axis=1, dtype=source_rows.dtype)


def place_rows(row_values, dilation, shifts):
    row_count, head_count, head_width = row_values.shape
    hit_mask = jnp.arange(dilation, dtype=jnp.int32).reshape(1, dilation, 1, 1) == shifts.reshape(
        1, 1, head_count, 1
    )
    spread = jnp.where(hit_mask, row_values[:, None], jnp.zeros((), row_values.dtype))
    return spread.reshape(row_count * dilation, head_count, head_width)


def level_scores(q_rows, k_rows):
    score_scale = 1.0 / math.sqrt(q_rows.shape[-1])
    return (
        jnp.einsum("qhe,khe->hqk", q_rows, k_rows, preferred_element_type=jnp.float32) * score_scale
    )


def attend(q_rows, k_rows, v_rows):
    scores = level_scores(q_rows, k_rows)
    row_max = jnp.max(scores, axis=-1, keepdims=True)
    log_total = row_max[..., 0] + jnp.log(jnp.sum(jnp.exp(scores - row_max), axis=-1))
    soft_rows = jnp.exp(scores - log_total[..., None]).astype(jnp.bfloat16)
    level_out = jnp.einsum("hqk,khe->qhe", soft_rows, v_rows, preferred_element_type=jnp.float32)
    return (level_out, log_total.T)


def score_grads(q_rows, k_rows, v_rows, log_total, grad_low, row_shift):
    score_scale = 1.0 / math.sqrt(q_rows.shape[-1])
    scores = level_scores(q_rows, k_rows)
    exact_soft = jnp.exp(scores - log_total.T[..., None])
    prob_grad = jnp.einsum("qhe,khe->hqk", grad_low, v_rows, preferred_element_type=jnp.float32)
    score_grad = (exact_soft * (prob_grad + row_shift.T[..., None]) * score_scale).astype(
        jnp.bfloat16
    )
    return (score_grad, exact_soft.astype(jnp.bfloat16))


def key_parts(score_grad, soft_low, q_rows, grad_low):
    k_part = jnp.einsum("hqk,qhe->khe", score_grad, q_rows, preferred_element_type=jnp.float32)
    v_part = jnp.einsum("hqk,qhe->khe", soft_low, grad_low, preferred_element_type=jnp.float32)
    return (k_part, v_part)


def query_part(score_grad, k_rows):
    return jnp.einsum("hqk,khe->qhe", score_grad, k_rows, preferred_element_type=jnp.float32)


def general_shards(queries, keys, values, grad_y, out_gain, offsets):
    tokens = queries.shape[1]
    flat_width = queries.shape[2]
    head_count = flat_width // HEAD_DIM
    row_shape = (tokens, head_count, HEAD_DIM)
    q_own = queries[0].reshape(row_shape)
    k_own = keys[0].reshape(row_shape)
    v_own = values[0].reshape(row_shape)
    ctx_size = lax.axis_size("ctx")
    span_bits = SPAN.bit_length() - 1
    my_place = lax.axis_index("ctx")
    mid_shift = offsets[0]
    top_shift = offsets[1]
    positions = jnp.arange(tokens, dtype=jnp.int32)
    mid_hit = (positions % R1)[:, None] == mid_shift[None, :]
    top_hit = (positions % ctx_size)[:, None] == top_shift[None, :]
    mid_q = pick_rows(q_own, R1, mid_shift)
    mid_k = pick_rows(k_own, R1, mid_shift)
    mid_v = pick_rows(v_own, R1, mid_shift)
    top_q = pick_rows(q_own, ctx_size, top_shift)
    top_k = pick_rows(k_own, ctx_size, top_shift)
    top_v = pick_rows(v_own, ctx_size, top_shift)
    mid_keys = mid_k.reshape(-1, flat_width)
    mid_vals = mid_v.reshape(-1, flat_width)
    top_keys = top_k.reshape(-1, flat_width)
    top_vals = top_v.reshape(-1, flat_width)

    def append_peer(mine, received, level_bit):
        upper_side = my_place >> level_bit & 1 == 1
        return jnp.where(
            upper_side, jnp.concatenate([received, mine], 0), jnp.concatenate([mine, received], 0)
        )

    for level_bit in range(span_bits):
        received = swapped((mid_keys, mid_vals), "ctx", level_bit)
        mid_keys = append_peer(mid_keys, received[0], level_bit)
        mid_vals = append_peer(mid_vals, received[1], level_bit)
    top_keys, top_vals = (
        lax.all_gather(top_keys, "ctx", axis=0, tiled=True),
        lax.all_gather(top_vals, "ctx", axis=0, tiled=True),
    )
    mid_keys = mid_keys.reshape(-1, head_count, HEAD_DIM)
    mid_vals = mid_vals.reshape(-1, head_count, HEAD_DIM)
    top_keys = top_keys.reshape(-1, head_count, HEAD_DIM)
    top_vals = top_vals.reshape(-1, head_count, HEAD_DIM)
    base_out, base_total = attend(q_own, k_own, v_own)
    mid_out, mid_total = attend(mid_q, mid_keys, mid_vals)
    top_out, top_total = attend(top_q, top_keys, top_vals)
    mid_full = place_rows(mid_total[..., None], R1, mid_shift)[..., 0]
    top_full = place_rows(top_total[..., None], ctx_size, top_shift)[..., 0]
    row_max = jnp.maximum(base_total, jnp.where(mid_hit, mid_full, base_total))
    row_max = jnp.maximum(row_max, jnp.where(top_hit, top_full, base_total))
    base_expo = jnp.exp(base_total - row_max)
    mid_expo = jnp.where(mid_hit, jnp.exp(mid_full - row_max), 0.0)
    top_expo = jnp.where(top_hit, jnp.exp(top_full - row_max), 0.0)
    denom = base_expo + mid_expo + top_expo
    base_share = base_expo / denom
    mid_share = mid_expo / denom
    top_share = top_expo / denom
    attn = (
        base_share[..., None] * base_out
        + mid_share[..., None] * place_rows(mid_out, R1, mid_shift)
        + top_share[..., None] * place_rows(top_out, ctx_size, top_shift)
    )
    inv_rms = lax.rsqrt(jnp.mean(attn * attn, axis=-1, keepdims=True) + EPS)
    normed = attn * inv_rms
    gain_rows = out_gain.reshape(head_count, HEAD_DIM)
    attended = (normed * gain_rows).astype(jnp.bfloat16).reshape(1, tokens, flat_width)
    grad_full = grad_y[0].reshape(row_shape).astype(jnp.float32)
    gain_part = jnp.sum(grad_full * normed, axis=0).reshape(flat_width)
    gain_grad = lax.psum(gain_part, ("dp", "ctx"))
    grad_norm = grad_full * gain_rows
    grad_attn = inv_rms * (
        grad_norm - normed * jnp.mean(grad_norm * normed, axis=-1, keepdims=True)
    )
    inner = jnp.sum(grad_attn * attn, axis=-1)
    base_low = (base_share[..., None] * grad_attn).astype(jnp.bfloat16)
    base_shift = -(base_share * inner)
    base_grad, base_soft = score_grads(q_own, k_own, v_own, base_total, base_low, base_shift)
    base_dq = query_part(base_grad, k_own)
    base_dk, base_dv = key_parts(base_grad, base_soft, q_own, base_low)
    mid_sel = pick_rows(mid_share[..., None], R1, mid_shift)[..., 0]
    mid_low = (mid_sel[..., None] * pick_rows(grad_attn, R1, mid_shift)).astype(jnp.bfloat16)
    mid_row_shift = -(mid_sel * pick_rows(inner[..., None], R1, mid_shift)[..., 0])
    mid_grad, mid_soft = score_grads(mid_q, mid_keys, mid_vals, mid_total, mid_low, mid_row_shift)
    mid_dq = query_part(mid_grad, mid_keys)
    mid_dk, mid_dv = key_parts(mid_grad, mid_soft, mid_q, mid_low)
    mid_dk = mid_dk.reshape(-1, flat_width)
    mid_dv = mid_dv.reshape(-1, flat_width)
    for level_bit in reversed(range(span_bits)):
        half_rows = mid_dk.shape[0] // 2
        upper_side = my_place >> level_bit & 1 == 1
        keep_k = jnp.where(upper_side, mid_dk[half_rows:], mid_dk[:half_rows])
        keep_v = jnp.where(upper_side, mid_dv[half_rows:], mid_dv[:half_rows])
        send_k = jnp.where(upper_side, mid_dk[:half_rows], mid_dk[half_rows:])
        send_v = jnp.where(upper_side, mid_dv[:half_rows], mid_dv[half_rows:])
        received = (
            swapped(send_k.astype(jnp.bfloat16), "ctx", level_bit).astype(send_k.dtype),
            swapped(send_v.astype(jnp.bfloat16), "ctx", level_bit).astype(send_v.dtype),
        )
        mid_dk = keep_k + received[0]
        mid_dv = keep_v + received[1]
    mid_dk = mid_dk.reshape(-1, head_count, HEAD_DIM)
    mid_dv = mid_dv.reshape(-1, head_count, HEAD_DIM)
    top_sel = pick_rows(top_share[..., None], ctx_size, top_shift)[..., 0]
    top_low = (top_sel[..., None] * pick_rows(grad_attn, ctx_size, top_shift)).astype(jnp.bfloat16)
    top_row_shift = -(top_sel * pick_rows(inner[..., None], ctx_size, top_shift)[..., 0])
    top_grad, top_soft = score_grads(top_q, top_keys, top_vals, top_total, top_low, top_row_shift)
    top_dq = query_part(top_grad, top_keys)
    gathered_dk, gathered_dv = key_parts(top_grad, top_soft, top_q, top_low)
    summed = (
        lax.psum_scatter(
            gathered_dk.reshape(-1, flat_width), "ctx", scatter_dimension=0, tiled=True
        ),
        lax.psum_scatter(
            gathered_dv.reshape(-1, flat_width), "ctx", scatter_dimension=0, tiled=True
        ),
    )
    top_dk = summed[0].reshape(-1, head_count, HEAD_DIM)
    top_dv = summed[1].reshape(-1, head_count, HEAD_DIM)
    query_grad = (
        base_dq + place_rows(mid_dq, R1, mid_shift) + place_rows(top_dq, ctx_size, top_shift)
    )
    key_grad = base_dk + place_rows(mid_dk, R1, mid_shift) + place_rows(top_dk, ctx_size, top_shift)
    value_grad = (
        base_dv + place_rows(mid_dv, R1, mid_shift) + place_rows(top_dv, ctx_size, top_shift)
    )
    out_shape = (1, tokens, flat_width)
    return (
        attended,
        query_grad.astype(jnp.bfloat16).reshape(out_shape),
        key_grad.astype(jnp.bfloat16).reshape(out_shape),
        value_grad.astype(jnp.bfloat16).reshape(out_shape),
        gain_grad,
    )


VMEM_SPEC = pl.BlockSpec(memory_space=pltpu.VMEM)
SMEM_SPEC = pl.BlockSpec(memory_space=pltpu.SMEM)
PEERS = SPAN - 1
OWNED = SPAN
TILE = 8
STAT_TILES = 2 * TILE
PIECES = 3
NEVER = -1e30
LOW = jnp.bfloat16
WIDE = jnp.float32
PACK_VMEM = 65408 * 1024
PLAIN_VMEM = 16 * 1024 * 1024


def contract(left, right, left_dim, right_dim):
    return lax.dot_general(
        left, right, (((left_dim,), (right_dim,)), ((), ())), preferred_element_type=WIDE
    )


def head_cols(head):
    return pl.ds(head * HEAD_DIM, HEAD_DIM)


def picked_counts(tokens, top_step):
    return tokens // top_step, tokens // R1


def pick_matrix(offsets_ref, head, tokens, top_step, picked_axis):
    top_rows, _ = picked_counts(tokens, top_step)
    row = lax.broadcasted_iota(jnp.int32, (tokens, tokens), picked_axis)
    position = lax.broadcasted_iota(jnp.int32, (tokens, tokens), 1 - picked_axis)
    wanted = jnp.where(
        row < top_rows,
        row * top_step + offsets_ref[1, head],
        (row - top_rows) * R1 + offsets_ref[0, head],
    )
    return jnp.where(position == wanted, 1.0, 0.0).astype(LOW)


def rolled(row, shift):
    return pltpu.roll(row, shift % row.shape[1], 1)


def lane_window(row, start, count):
    lane = lax.broadcasted_iota(jnp.int32, row.shape, 1)
    return jnp.where((lane >= start) & (lane < start + count), row, 0.0)


def hit_row(offset, step, tokens):
    position = lax.broadcasted_iota(jnp.int32, (1, tokens), 1)
    return jnp.where(position % step == offset, 1.0, 0.0)


def piece_rows(row, others=None):
    pieces = []
    for _ in range(PIECES):
        piece = row.astype(LOW).astype(WIDE)
        pieces.append(piece)
        row = row - piece
    if others is None:
        others = jnp.zeros((TILE - PIECES, row.shape[1]), WIDE)
    return jnp.concatenate(pieces + [others], 0)


def gain_pieces(rows):
    high = rows.astype(LOW)
    return high, (rows - high.astype(WIDE)).astype(LOW)


def joined_row(rows, first):
    total = rows[first : first + 1]
    for piece in range(1, PIECES):
        total = total + rows[first + piece : first + piece + 1]
    return total


def gain_row_of(ones, product):
    high, rest = gain_pieces(product)
    return (contract(ones, high, 1, 1) + contract(ones, rest, 1, 1))[:1]


def column_mean(block):
    return jnp.mean(block, axis=0, keepdims=True)


def norm_backward(attn, grad_norm):
    inv_rms = lax.rsqrt(column_mean(attn * attn) + EPS)
    normed = attn * inv_rms
    product = grad_norm * normed
    grad_attn = inv_rms * (grad_norm - normed * column_mean(product))
    inner = jnp.sum(grad_attn * attn, axis=0, keepdims=True)
    return normed, product, grad_attn.astype(LOW), inner


def nearest_first(refs):
    return [refs[0], *refs[:0:-1]]


def pack_kernel(top_step, offsets_ref, q_ref, k_ref, v_ref, grad_ref, *refs):
    payload_refs, (expo_ref, out_ref, stats_ref, held_ref) = refs[:SPAN], refs[SPAN:]
    tokens, width = q_ref.shape[1:]
    heads = range(width // HEAD_DIM)
    owned = range(OWNED)
    me = lax.axis_index("ctx")
    picked = sum(picked_counts(tokens, top_step))
    score_scale = 1.0 / math.sqrt(HEAD_DIM)
    q_rows, k_rows, v_rows, grad_rows = [
        [ref[0, :, head_cols(head)] for head in heads] for ref in (q_ref, k_ref, v_ref, grad_ref)
    ]
    picks = [pick_matrix(offsets_ref, head, tokens, top_step, 0) for head in heads]
    scores = [contract(k_rows[head], q_rows[head], 1, 1) * score_scale for head in heads]
    moved = [
        contract(
            picks[head][:picked],
            jnp.concatenate([q_rows[head], k_rows[head], v_rows[head], grad_rows[head]], 1),
            1,
            0,
        ).astype(LOW)
        for head in owned
    ]
    shared = [
        contract(
            picks[head][:picked], jnp.concatenate([k_rows[head], v_rows[head]], 1), 1, 0
        ).astype(LOW)
        for head in heads[OWNED:]
    ]
    top_scores = [jnp.max(block, axis=0, keepdims=True) for block in scores]
    expos = [jnp.exp(scores[head] - top_scores[head]) for head in heads]
    for head in heads[OWNED:]:
        key_row = lax.broadcasted_iota(jnp.int32, (tokens, 1), 0)
        times = 1.0
        for level, step in ((0, R1), (1, top_step)):
            offset = offsets_ref[level, head]
            hit_column = jnp.where(key_row % step == offset, 1.0, 0.0)
            times = times + hit_column * hit_row(offset, step, tokens)
        expos[head] = times * expos[head]
    expo_lows = [expo.astype(LOW) for expo in expos]
    outs = [contract(v_rows[head], expo_lows[head], 0, 0) for head in heads]
    totals = [jnp.sum(expo, axis=0, keepdims=True) for expo in expos]
    for head in heads:
        expo_ref[:, head_cols(head)] = expo_lows[head]
        stats_ref[head : head + 1, :] = top_scores[head]
        stats_ref[TILE + head : TILE + head + 1, :] = totals[head]
    for head in owned:
        outs[head] = outs[head] * (1.0 / totals[head])
    outs = [out.astype(LOW) for out in outs]
    picked_outs = [
        contract(picks[head][:picked], outs[head], 1, 1).astype(LOW) for head in owned
    ]
    for head in heads:
        out_ref[:, head_cols(head)] = outs[head]
    for head in owned:
        pieces = piece_rows(top_scores[head] + jnp.log(totals[head])).astype(LOW)
        stat_rows = contract(pieces, picks[head], 1, 1)
        blocks = [moved[head][:, block * HEAD_DIM : (block + 1) * HEAD_DIM] for block in range(4)]
        blocks.append(picked_outs[head])
        blocks += [shared[0][:, :HEAD_DIM], shared[0][:, HEAD_DIM:]]
        blocks.append(jnp.concatenate([stat_rows, jnp.zeros_like(stat_rows)], 0).astype(LOW))
        held_ref[head] = jnp.concatenate(blocks, 0)
    for distance, payload_ref in enumerate(payload_refs):
        payload_ref[...] = held_ref[me ^ distance]


def prepare_kernel(top_step, offsets_ref, grad_ref, gain_ref, out_ref, *refs):
    grad_norm_ref, gain_part_ref, place_ref = refs
    tokens, width = grad_ref.shape[1:]
    heads = range(width // HEAD_DIM)
    top_rows = tokens // top_step
    ones = jnp.ones((TILE, tokens), LOW)
    column = lax.broadcasted_iota(jnp.int32, (tokens, tokens), 1)
    gain_part_ref[...] = jnp.zeros(gain_part_ref.shape, WIDE)
    grad_norms = [
        (grad_ref[0, :, head_cols(head)].astype(WIDE) * gain_ref[:, head_cols(head)]).T
        for head in heads
    ]
    for head in heads:
        cols = head_cols(head)
        grad_norm_ref[:, cols] = grad_norms[head]
        picks = pick_matrix(offsets_ref, head, tokens, top_step, 1)
        place_ref[:, cols] = picks
    for head in range(OWNED):
        cols = head_cols(head)
        mid_offset, top_offset = offsets_ref[0, head], offsets_ref[1, head]
        seen = jnp.maximum(
            hit_row(top_offset, top_step, tokens), hit_row(mid_offset, R1, tokens)
        )
        attn = out_ref[:, cols].astype(WIDE)
        normed = attn * lax.rsqrt(column_mean(attn * attn) + EPS)
        product = grad_norms[head] * normed * (1.0 - seen)
        gain_part_ref[:, cols] = gain_row_of(ones, product) / gain_ref[:, cols]
        both = mid_offset % top_step == top_offset
        kept = jnp.where(column < top_rows, 1.0, jnp.where(both, 0.0, 1.0)).astype(LOW)
        picks = pick_matrix(offsets_ref, head, tokens, top_step, 1)
        place_ref[:, head_cols(len(heads) + head)] = picks * kept


def owner_kernel(top_step, offsets_ref, q_ref, gain_ref, out_ref, grad_norm_ref, *refs):
    stats_ref, gain_base_ref = refs[:2]
    payload_refs, refs = nearest_first(refs[2 : 2 + SPAN]), refs[2 + SPAN :]
    normed_ref, grad_low_ref, score_grad_ref, kept_ref = refs[:4]
    return_refs = refs[4:]
    tokens = q_ref.shape[1]
    heads = q_ref.shape[2] // HEAD_DIM
    top_rows, mid_rows = picked_counts(tokens, top_step)
    picked = top_rows + mid_rows
    top_all, mid_all = SPAN * top_rows, SPAN * mid_rows
    queries = top_all + mid_all
    score_scale = 1.0 / math.sqrt(HEAD_DIM)
    me = lax.axis_index("ctx")
    ones = jnp.ones((TILE, tokens), LOW)

    def by_level(block):
        start = block * picked
        return jnp.concatenate(
            [ref[start : start + top_rows] for ref in payload_refs]
            + [ref[start + top_rows : start + picked] for ref in payload_refs],
            0,
        )

    def per_level(top_row, mid_row):
        return jnp.concatenate(
            [
                jnp.broadcast_to(top_row, (top_all, queries)),
                jnp.broadcast_to(mid_row, (mid_all, queries)),
            ],
            0,
        )

    q_rows, k_rows, v_rows, grad_rows, base_rows = [by_level(block) for block in range(5)]
    stat_start = 7 * picked
    logs = [
        joined_row(ref[stat_start : stat_start + STAT_TILES].astype(WIDE), 0)
        for ref in payload_refs
    ]
    base_top_log = sum(
        rolled(lane_window(log, 0, top_rows), slot * top_rows) for slot, log in enumerate(logs)
    )
    base_mid_log = sum(
        rolled(lane_window(log, top_rows, mid_rows), slot * mid_rows - top_rows)
        for slot, log in enumerate(logs)
    )
    base_log = jnp.concatenate([base_top_log, base_mid_log[:, :mid_all]], 1)
    gain_row = jnp.zeros((1, HEAD_DIM), WIDE)
    for head in range(OWNED):
        gain_row = gain_row + jnp.where(me == head, 1.0, 0.0) * gain_ref[:, head_cols(head)]
    mid_offset, top_offset = offsets_ref[0, me], offsets_ref[1, me]
    both = mid_offset % top_step == top_offset
    lane = lax.broadcasted_iota(jnp.int32, (1, queries), 1)
    is_top = jnp.where(lane < top_all, 1.0, 0.0)
    top_in_mid = jnp.where(((lane % top_rows) * top_step + top_offset) % R1 == mid_offset, 1.0, 0.0)
    both_flag = jnp.where(both, 1.0, 0.0)
    sees_top = is_top + (1.0 - is_top) * both_flag
    sees_mid = is_top * top_in_mid + (1.0 - is_top)
    bias = per_level((1.0 - sees_top) * NEVER, (1.0 - sees_mid) * NEVER)
    last = heads - 1
    cols = head_cols(last)
    peers = payload_refs[1:]
    q_last = q_ref[0, :, cols]
    k_peers = jnp.concatenate([ref[5 * picked : 6 * picked] for ref in peers], 0)
    v_peers = jnp.concatenate([ref[6 * picked : 7 * picked] for ref in peers], 0)
    last_biases = [
        jnp.broadcast_to((1.0 - hit_row(offsets_ref[level, last], step, tokens)) * NEVER, shape)
        for level, step, shape in (
            (1, top_step, (top_rows, tokens)),
            (0, R1, (mid_rows, tokens)),
        )
    ]
    scores = contract(k_rows, q_rows, 1, 1) * score_scale + bias
    scores_last = contract(k_peers, q_last, 1, 1) * score_scale + jnp.concatenate(
        last_biases * PEERS, 0
    )
    base_attn = base_rows.astype(WIDE).T
    grad_norm = (grad_rows.astype(WIDE) * gain_row).T
    top_score = jnp.maximum(base_log, jnp.max(scores, axis=0, keepdims=True))
    base_top, base_total = stats_ref[last : last + 1, :], stats_ref[TILE + last : TILE + last + 1, :]
    top_last = jnp.maximum(base_top, jnp.max(scores_last, axis=0, keepdims=True))
    expo = jnp.exp(scores - top_score)
    expo_last = jnp.exp(scores_last - top_last)
    factor = jnp.exp(base_log - top_score)
    factor_last = jnp.exp(base_top - top_last)
    total = factor + jnp.sum(expo, axis=0, keepdims=True)
    total_last = factor_last * base_total + jnp.sum(expo_last, axis=0, keepdims=True)
    inv_total, inv_last = 1.0 / total, 1.0 / total_last
    soft, soft_last = expo * inv_total, expo_last * inv_last
    soft_low, soft_last_low = soft.astype(LOW), soft_last.astype(LOW)
    factor_last = factor_last * inv_last
    attn = (factor * inv_total) * base_attn + contract(v_rows, soft_low, 0, 0)
    attn_last = factor_last * out_ref[:, cols].astype(WIDE) + contract(v_peers, soft_last_low, 0, 0)
    _, product, grad_low, inner = norm_backward(attn, grad_norm)
    normed_last, product_last, grad_last_low, inner_last = norm_backward(
        attn_last, grad_norm_ref[:, cols]
    )
    spans = (slice(0, top_all), slice(top_all, queries))
    prob_grads = [contract(v_rows[span], grad_low[:, span], 1, 0) for span in spans]
    prob_grad_last = contract(v_peers, grad_last_low, 1, 0)
    score_grads = [
        (soft[span, span] * (prob_grad - inner[:, span]) * score_scale).astype(LOW)
        for span, prob_grad in zip(spans, prob_grads)
    ]
    score_grad_last = (soft_last * (prob_grad_last - inner_last) * score_scale).astype(LOW)
    dks = [
        contract(score_grad, q_rows[span], 1, 0).astype(LOW)
        for span, score_grad in zip(spans, score_grads)
    ]
    dk_last = contract(score_grad_last, q_last, 1, 0).astype(LOW)
    dvs = [
        contract(soft_low[span, span], grad_low[:, span], 1, 1).astype(LOW) for span in spans
    ]
    dv_last = contract(soft_last_low, grad_last_low, 1, 1).astype(LOW)
    dqs = [
        contract(score_grad, k_rows[span], 0, 0).astype(LOW)
        for span, score_grad in zip(spans, score_grads)
    ]
    attn_rows = attn.T.astype(LOW)
    attn_parts = [attn_rows[span] for span in spans]
    log_total = top_score + jnp.log(total)
    padding = jnp.zeros((1, top_all - mid_all), WIDE)
    once = is_top + (1.0 - is_top) * (1.0 - both_flag)
    ones_all = jnp.ones((TILE, queries), LOW)
    own_gain = gain_row_of(ones_all, product * once) / gain_row
    gain_rows = [
        gain_base_ref[:, head_cols(head)] + jnp.where(me == head, 1.0, 0.0) * own_gain
        for head in range(OWNED)
    ]
    gain_rows.append(gain_row_of(ones, product_last) / gain_ref[:, cols])
    gain_high, gain_rest = [
        rows.astype(WIDE) for rows in gain_pieces(jnp.concatenate(gain_rows, 0))
    ]
    top_log, mid_log = log_total[:, :top_all], jnp.concatenate(
        [log_total[:, top_all:], padding], 1
    )
    empty = jnp.zeros((PIECES, HEAD_DIM), WIDE)
    for distance, return_ref in enumerate(return_refs):
        blocks = []
        for top_block, mid_block in (dqs, dks, dvs, attn_parts):
            blocks.append(top_block[distance * top_rows : (distance + 1) * top_rows])
            blocks.append(mid_block[distance * mid_rows : (distance + 1) * mid_rows])
        start = max(distance - 1, 0) * picked
        blocks += [dk_last[start : start + picked], dv_last[start : start + picked]]
        log_row = lane_window(rolled(top_log, -distance * top_rows), 0, top_rows) + lane_window(
            rolled(mid_log, top_rows - distance * mid_rows), top_rows, mid_rows
        )
        log_rows = [piece_rows(log_row, gain_high), empty, gain_rest]
        blocks.append(jnp.concatenate(log_rows, 0).astype(LOW))
        return_ref[...] = jnp.concatenate(blocks, 0)
    normed_ref[...] = normed_last
    grad_low_ref[...] = grad_last_low
    score_grad_ref[...] = score_grad_last
    kept_ref[0:1, :] = factor_last
    kept_ref[1:2, :] = inner_last


def last_head_kernel(top_step, q_ref, k_ref, v_ref, gain_ref, expo_ref, *refs):
    normed_ref, grad_low_ref, peer_score_grad_ref, kept_ref, *peers = refs[: 4 + PEERS]
    peers = peers[::-1]
    attended_ref, dq_ref, dk_ref, dv_ref = refs[4 + PEERS :]
    picked = sum(picked_counts(q_ref.shape[1], top_step))
    score_scale = 1.0 / math.sqrt(HEAD_DIM)
    cols = head_cols(q_ref.shape[2] // HEAD_DIM - 1)
    attended_ref[...] = (normed_ref[...].T * gain_ref[:, cols]).astype(LOW)
    k_peers = jnp.concatenate([ref[5 * picked : 6 * picked] for ref in peers], 0)
    grad_low = grad_low_ref[...]
    soft = expo_ref[:, cols].astype(WIDE) * kept_ref[0:1, :]
    prob_grad = contract(v_ref[0, :, cols], grad_low, 1, 0)
    score_grad = (soft * (prob_grad - kept_ref[1:2, :]) * score_scale).astype(LOW)
    dk_ref[...] = contract(score_grad, q_ref[0, :, cols], 1, 0)
    dv_ref[...] = contract(soft.astype(LOW), grad_low, 1, 1)
    dq_ref[...] = (
        contract(score_grad, k_ref[0, :, cols], 0, 0)
        + contract(peer_score_grad_ref[...], k_peers, 0, 0)
    ).astype(LOW)


def gain_kernel(picked, *refs):
    return_refs, gain_ref = nearest_first(refs[:SPAN]), refs[SPAN]
    tiles = [ref[6 * picked : 6 * picked + STAT_TILES].astype(WIDE) for ref in return_refs]
    parts = [tile[PIECES:TILE] + tile[TILE + PIECES :] for tile in tiles]
    total = (parts[0] + parts[1]) + (parts[2] + parts[3])
    for head in range(gain_ref.shape[1] // HEAD_DIM):
        gain_ref[:, head_cols(head)] = total[head : head + 1]


def mix_kernel(top_step, offsets_ref, v_ref, gain_ref, expo_ref, out_ref, *refs):
    grad_norm_ref, stats_ref, place_ref = refs[:3]
    return_refs, refs = nearest_first(refs[3 : 3 + SPAN]), refs[3 + SPAN :]
    attended_ref, grad_low_ref, soft_ref, score_grad_ref, placed_ref = refs
    tokens, width = v_ref.shape[1:]
    count = width // HEAD_DIM
    picked = sum(picked_counts(tokens, top_step))
    score_scale = 1.0 / math.sqrt(HEAD_DIM)
    me = lax.axis_index("ctx")
    heads = range(OWNED)
    every = [head_cols(head) for head in heads]
    for distance, return_ref in enumerate(return_refs):
        placed_ref[me ^ distance] = return_ref[...]
    once = [place_ref[:, head_cols(count + head)] for head in heads]
    attn_parts = [
        contract(placed_ref[head, 3 * picked : 4 * picked], once[head][:, :picked], 0, 1)
        for head in heads
    ]
    log_parts = [
        contract(placed_ref[head, 6 * picked : 6 * picked + STAT_TILES], once[head], 1, 1)
        for head in heads
    ]
    factors, normeds, grad_lows, inners = [], [], [], []
    for head in heads:
        top_hit = hit_row(offsets_ref[1, head], top_step, tokens)
        mid_hit = hit_row(offsets_ref[0, head], R1, tokens)
        seen = jnp.maximum(top_hit, mid_hit) > 0.5
        top_score, total = stats_ref[head : head + 1, :], stats_ref[TILE + head : TILE + head + 1, :]
        log_total = jnp.where(seen, joined_row(log_parts[head], 0), top_score + jnp.log(total))
        factors.append(jnp.exp(top_score - log_total))
        attn = jnp.where(seen, attn_parts[head], out_ref[:, every[head]].astype(WIDE))
        normed, _, grad_low, inner = norm_backward(attn, grad_norm_ref[:, every[head]])
        normeds.append(normed)
        grad_lows.append(grad_low)
        inners.append(inner)
    prob_grads = [contract(v_ref[0, :, every[head]], grad_lows[head], 1, 0) for head in heads]
    softs = [expo_ref[:, every[head]].astype(WIDE) * factors[head] for head in heads]
    for head in heads:
        cols = every[head]
        grad_low_ref[:, cols] = grad_lows[head]
        soft_ref[:, cols] = softs[head].astype(LOW)
        score_grad_ref[:, cols] = (
            softs[head] * (prob_grads[head] - inners[head]) * score_scale
        ).astype(LOW)
        attended_ref[:, cols] = (normeds[head].T * gain_ref[:, cols]).astype(LOW)


def finish_kernel(top_step, *refs):
    gain_refs, (q_ref, k_ref, place_ref), refs = refs[:2], refs[2:5], refs[5:]
    mixed_refs, (last_attended_ref, last_dq_ref, last_dk_ref, last_dv_ref) = refs[:5], refs[5:9]
    return_refs, refs = nearest_first(refs[9 : 9 + SPAN]), refs[9 + SPAN :]
    mixed_ref, grad_low_ref, soft_ref, score_grad_ref, returned_ref = mixed_refs
    attended_ref, dq_ref, dk_ref, dv_ref, gain_out_ref = refs
    tokens, width = q_ref.shape[1:]
    picked = sum(picked_counts(tokens, top_step))
    heads = range(OWNED)
    every = [head_cols(head) for head in heads]
    gain_out_ref[...] = (gain_refs[0][...] + gain_refs[1][...]).reshape(gain_out_ref.shape)
    score_grads = [score_grad_ref[:, cols] for cols in every]
    dqs = [contract(score_grads[head], k_ref[0, :, every[head]], 0, 0) for head in heads]
    placed = [
        contract(
            place_ref[:, pl.ds(head * HEAD_DIM, picked)],
            jnp.concatenate(
                [returned_ref[head, block * picked : (block + 1) * picked] for block in range(3)], 1
            ),
            1,
            0,
        )
        for head in heads
    ]
    dks = [contract(score_grads[head], q_ref[0, :, every[head]], 1, 0) for head in heads]
    dvs = [contract(soft_ref[:, cols], grad_low_ref[:, cols], 1, 1) for cols in every]
    last = width // HEAD_DIM - 1
    total = sum(ref[4 * picked : 6 * picked].astype(WIDE) for ref in return_refs[1:]).astype(LOW)
    rows = contract(
        place_ref[:, pl.ds(last * HEAD_DIM, picked)],
        jnp.concatenate([total[:picked], total[picked:]], 1),
        1,
        0,
    )
    for head in heads:
        cols = every[head]
        attended_ref[0, :, cols] = mixed_ref[:, cols]
        for which, (block, out_block_ref) in enumerate(
            ((dqs[head], dq_ref), (dks[head], dk_ref), (dvs[head], dv_ref))
        ):
            part = placed[head][:, which * HEAD_DIM : (which + 1) * HEAD_DIM]
            out_block_ref[0, :, cols] = (block + part).astype(LOW)
    cols = head_cols(last)
    attended_ref[0, :, cols] = last_attended_ref[...]
    dq_ref[0, :, cols] = last_dq_ref[...]
    dk_ref[0, :, cols] = (last_dk_ref[...] + rows[:, :HEAD_DIM]).astype(LOW)
    dv_ref[0, :, cols] = (last_dv_ref[...] + rows[:, HEAD_DIM:]).astype(LOW)


def across(block, axis, distance):
    route = [(place, place ^ distance) for place in range(lax.axis_size(axis))]
    return lax.ppermute(block, axis, route)


def to_peers(blocks):
    return [across(blocks[distance - 1], "ctx", distance) for distance in range(PEERS, 0, -1)]


def call(kernel, name, operands, results, microseconds, vmem=PLAIN_VMEM, scratch=()):
    return pl.pallas_call(
        kernel,
        out_shape=results,
        in_specs=[SMEM_SPEC if block.dtype == jnp.int32 else VMEM_SPEC for block in operands],
        out_specs=[VMEM_SPEC] * len(results),
        scratch_shapes=scratch,
        compiler_params=pltpu.CompilerParams(vmem_limit_bytes=vmem),
        cost_estimate=pl.CostEstimate(
            flops=int(microseconds * 10**9), bytes_accessed=0, transcendentals=0
        ),
        name=name,
    )(*operands)


def one_segment_shards(queries, keys, values, grad_y, out_gain, offsets):
    tokens, width = queries.shape[1:]
    heads = width // HEAD_DIM
    top_step = lax.axis_size("ctx")
    picked = sum(picked_counts(tokens, top_step))
    shape = jax.ShapeDtypeStruct
    row_block = shape((1, tokens, width), LOW)
    low_block, wide_block = shape((tokens, width), LOW), shape((tokens, width), WIDE)
    low_head, wide_head = shape((tokens, HEAD_DIM), LOW), shape((tokens, HEAD_DIM), WIDE)
    gain_block = shape((1, width), WIDE)
    stats_block = shape((2 * TILE, tokens), WIDE)
    payload = shape((7 * picked + STAT_TILES, HEAD_DIM), LOW)
    answer = shape((6 * picked + STAT_TILES, HEAD_DIM), LOW)
    bind = functools.partial
    gain_row = out_gain.reshape(1, width)
    own, *sent, expo, base_out, stats = call(
        bind(pack_kernel, top_step),
        "pack",
        (offsets, queries, keys, values, grad_y),
        [payload] * SPAN + [low_block, low_block, stats_block],
        1,
        vmem=PACK_VMEM,
        scratch=[pltpu.VMEM((OWNED, *payload.shape), LOW)],
    )
    received = to_peers(sent)
    grad_norm, gain_base, place = call(
        bind(prepare_kernel, top_step),
        "prepare",
        (offsets, grad_y, gain_row, base_out),
        [wide_block, gain_block, shape((tokens, 2 * width), LOW)],
        2,
    )
    normed, grad_low, score_grad, kept, own_answer, *answers = call(
        bind(owner_kernel, top_step),
        "owner",
        (offsets, queries, gain_row, base_out, grad_norm, stats, gain_base, own, *received),
        [
            wide_head,
            low_head,
            shape((PEERS * picked, HEAD_DIM), LOW),
            shape((TILE, tokens), WIDE),
        ]
        + [answer] * SPAN,
        3,
    )
    returned = to_peers(answers)
    last_results = call(
        bind(last_head_kernel, top_step),
        "last_head",
        (queries, keys, values, gain_row, expo, normed, grad_low, score_grad, kept, *received),
        [low_head, low_head, wide_head, wide_head],
        20,
    )
    (gain_sum,) = call(bind(gain_kernel, picked), "gain", (own_answer, *returned), [gain_block], 1)
    gain_rest = across(gain_sum, "dp", 1)
    mixed_block = shape((tokens, OWNED * HEAD_DIM), LOW)
    mixed = call(
        bind(mix_kernel, top_step),
        "mix",
        (
            offsets,
            values,
            gain_row,
            expo,
            base_out,
            grad_norm,
            stats,
            place,
            own_answer,
            *returned,
        ),
        [mixed_block] * 4 + [shape((OWNED, *answer.shape), LOW)],
        20,
    )
    attended, query_grad, key_grad, value_grad, gain_grad = call(
        bind(finish_kernel, top_step),
        "finish",
        (
            gain_sum,
            gain_rest,
            queries,
            keys,
            place,
            *mixed,
            *last_results,
            own_answer,
            *returned,
        ),
        [row_block] * 4 + [shape((width,), WIDE)],
        1,
    )
    return attended, query_grad, key_grad, value_grad, gain_grad


def shards(*operands):
    one_segment = lax.axis_size("ctx") == SPAN
    if one_segment and operands[0].shape[2] == (OWNED + 1) * HEAD_DIM:
        return one_segment_shards(*operands)
    return general_shards(*operands)


def solution(mesh):
    in_specs = (
        P("dp", "ctx", "head"),
        P("dp", "ctx", "head"),
        P("dp", "ctx", "head"),
        P("dp", "ctx", "head"),
        P("head"),
        P(None, "head"),
    )
    out_specs = (
        P("dp", "ctx", "head"),
        P("dp", "ctx", "head"),
        P("dp", "ctx", "head"),
        P("dp", "ctx", "head"),
        P("head"),
    )
    return jax.shard_map(shards, mesh=mesh, in_specs=in_specs, out_specs=out_specs, check_vma=False)
```

```python
import functools
import math

import jax
import jax.numpy as jnp
from jax import lax
from jax.experimental import pallas as pl
from jax.experimental.pallas import tpu as pltpu
from jax.sharding import PartitionSpec as P

HEAD_DIM = 128
SPAN = 4
R1 = 8


EPS = 1e-06


def swapped(block, axis, bit):
    count = lax.axis_size(axis)
    route = []
    for low in range(count):
        high = low | 1 << bit
        if high != low and high < count:
            route += [(low, high), (high, low)]
    return lax.ppermute(block, axis, route)


def pick_rows(source_rows, dilation, shifts):
    row_count, head_count, head_width = source_rows.shape
    grouped = source_rows.reshape(row_count // dilation, dilation, head_count, head_width)
    hit_mask = jnp.arange(dilation, dtype=jnp.int32).reshape(1, dilation, 1, 1) == shifts.reshape(
        1, 1, head_count, 1
    )
    chosen = jnp.where(hit_mask, grouped, jnp.zeros((), source_rows.dtype))
    return jnp.sum(chosen, axis=1, dtype=source_rows.dtype)


def place_rows(row_values, dilation, shifts):
    row_count, head_count, head_width = row_values.shape
    hit_mask = jnp.arange(dilation, dtype=jnp.int32).reshape(1, dilation, 1, 1) == shifts.reshape(
        1, 1, head_count, 1
    )
    spread = jnp.where(hit_mask, row_values[:, None], jnp.zeros((), row_values.dtype))
    return spread.reshape(row_count * dilation, head_count, head_width)


def level_scores(q_rows, k_rows):
    score_scale = 1.0 / math.sqrt(q_rows.shape[-1])
    return (
        jnp.einsum("qhe,khe->hqk", q_rows, k_rows, preferred_element_type=jnp.float32) * score_scale
    )


def attend(q_rows, k_rows, v_rows):
    scores = level_scores(q_rows, k_rows)
    row_max = jnp.max(scores, axis=-1, keepdims=True)
    log_total = row_max[..., 0] + jnp.log(jnp.sum(jnp.exp(scores - row_max), axis=-1))
    soft_rows = jnp.exp(scores - log_total[..., None]).astype(jnp.bfloat16)
    level_out = jnp.einsum("hqk,khe->qhe", soft_rows, v_rows, preferred_element_type=jnp.float32)
    return (level_out, log_total.T)


def score_grads(q_rows, k_rows, v_rows, log_total, grad_low, row_shift):
    score_scale = 1.0 / math.sqrt(q_rows.shape[-1])
    scores = level_scores(q_rows, k_rows)
    exact_soft = jnp.exp(scores - log_total.T[..., None])
    prob_grad = jnp.einsum("qhe,khe->hqk", grad_low, v_rows, preferred_element_type=jnp.float32)
    score_grad = (exact_soft * (prob_grad + row_shift.T[..., None]) * score_scale).astype(
        jnp.bfloat16
    )
    return (score_grad, exact_soft.astype(jnp.bfloat16))


def key_parts(score_grad, soft_low, q_rows, grad_low):
    k_part = jnp.einsum("hqk,qhe->khe", score_grad, q_rows, preferred_element_type=jnp.float32)
    v_part = jnp.einsum("hqk,qhe->khe", soft_low, grad_low, preferred_element_type=jnp.float32)
    return (k_part, v_part)


def query_part(score_grad, k_rows):
    return jnp.einsum("hqk,khe->qhe", score_grad, k_rows, preferred_element_type=jnp.float32)


def general_shards(queries, keys, values, grad_y, out_gain, offsets):
    tokens = queries.shape[1]
    flat_width = queries.shape[2]
    head_count = flat_width // HEAD_DIM
    row_shape = (tokens, head_count, HEAD_DIM)
    q_own = queries[0].reshape(row_shape)
    k_own = keys[0].reshape(row_shape)
    v_own = values[0].reshape(row_shape)
    ctx_size = lax.axis_size("ctx")
    span_bits = SPAN.bit_length() - 1
    my_place = lax.axis_index("ctx")
    mid_shift = offsets[0]
    top_shift = offsets[1]
    positions = jnp.arange(tokens, dtype=jnp.int32)
    mid_hit = (positions % R1)[:, None] == mid_shift[None, :]
    top_hit = (positions % ctx_size)[:, None] == top_shift[None, :]
    mid_q = pick_rows(q_own, R1, mid_shift)
    mid_k = pick_rows(k_own, R1, mid_shift)
    mid_v = pick_rows(v_own, R1, mid_shift)
    top_q = pick_rows(q_own, ctx_size, top_shift)
    top_k = pick_rows(k_own, ctx_size, top_shift)
    top_v = pick_rows(v_own, ctx_size, top_shift)
    mid_keys = mid_k.reshape(-1, flat_width)
    mid_vals = mid_v.reshape(-1, flat_width)
    top_keys = top_k.reshape(-1, flat_width)
    top_vals = top_v.reshape(-1, flat_width)

    def append_peer(mine, received, level_bit):
        upper_side = my_place >> level_bit & 1 == 1
        return jnp.where(
            upper_side, jnp.concatenate([received, mine], 0), jnp.concatenate([mine, received], 0)
        )

    for level_bit in range(span_bits):
        received = swapped((mid_keys, mid_vals), "ctx", level_bit)
        mid_keys = append_peer(mid_keys, received[0], level_bit)
        mid_vals = append_peer(mid_vals, received[1], level_bit)
    top_keys, top_vals = (
        lax.all_gather(top_keys, "ctx", axis=0, tiled=True),
        lax.all_gather(top_vals, "ctx", axis=0, tiled=True),
    )
    mid_keys = mid_keys.reshape(-1, head_count, HEAD_DIM)
    mid_vals = mid_vals.reshape(-1, head_count, HEAD_DIM)
    top_keys = top_keys.reshape(-1, head_count, HEAD_DIM)
    top_vals = top_vals.reshape(-1, head_count, HEAD_DIM)
    base_out, base_total = attend(q_own, k_own, v_own)
    mid_out, mid_total = attend(mid_q, mid_keys, mid_vals)
    top_out, top_total = attend(top_q, top_keys, top_vals)
    mid_full = place_rows(mid_total[..., None], R1, mid_shift)[..., 0]
    top_full = place_rows(top_total[..., None], ctx_size, top_shift)[..., 0]
    row_max = jnp.maximum(base_total, jnp.where(mid_hit, mid_full, base_total))
    row_max = jnp.maximum(row_max, jnp.where(top_hit, top_full, base_total))
    base_expo = jnp.exp(base_total - row_max)
    mid_expo = jnp.where(mid_hit, jnp.exp(mid_full - row_max), 0.0)
    top_expo = jnp.where(top_hit, jnp.exp(top_full - row_max), 0.0)
    denom = base_expo + mid_expo + top_expo
    base_share = base_expo / denom
    mid_share = mid_expo / denom
    top_share = top_expo / denom
    attn = (
        base_share[..., None] * base_out
        + mid_share[..., None] * place_rows(mid_out, R1, mid_shift)
        + top_share[..., None] * place_rows(top_out, ctx_size, top_shift)
    )
    inv_rms = lax.rsqrt(jnp.mean(attn * attn, axis=-1, keepdims=True) + EPS)
    normed = attn * inv_rms
    gain_rows = out_gain.reshape(head_count, HEAD_DIM)
    attended = (normed * gain_rows).astype(jnp.bfloat16).reshape(1, tokens, flat_width)
    grad_full = grad_y[0].reshape(row_shape).astype(jnp.float32)
    gain_part = jnp.sum(grad_full * normed, axis=0).reshape(flat_width)
    gain_grad = lax.psum(gain_part, ("dp", "ctx"))
    grad_norm = grad_full * gain_rows
    grad_attn = inv_rms * (
        grad_norm - normed * jnp.mean(grad_norm * normed, axis=-1, keepdims=True)
    )
    inner = jnp.sum(grad_attn * attn, axis=-1)
    base_low = (base_share[..., None] * grad_attn).astype(jnp.bfloat16)
    base_shift = -(base_share * inner)
    base_grad, base_soft = score_grads(q_own, k_own, v_own, base_total, base_low, base_shift)
    base_dq = query_part(base_grad, k_own)
    base_dk, base_dv = key_parts(base_grad, base_soft, q_own, base_low)
    mid_sel = pick_rows(mid_share[..., None], R1, mid_shift)[..., 0]
    mid_low = (mid_sel[..., None] * pick_rows(grad_attn, R1, mid_shift)).astype(jnp.bfloat16)
    mid_row_shift = -(mid_sel * pick_rows(inner[..., None], R1, mid_shift)[..., 0])
    mid_grad, mid_soft = score_grads(mid_q, mid_keys, mid_vals, mid_total, mid_low, mid_row_shift)
    mid_dq = query_part(mid_grad, mid_keys)
    mid_dk, mid_dv = key_parts(mid_grad, mid_soft, mid_q, mid_low)
    mid_dk = mid_dk.reshape(-1, flat_width)
    mid_dv = mid_dv.reshape(-1, flat_width)
    for level_bit in reversed(range(span_bits)):
        half_rows = mid_dk.shape[0] // 2
        upper_side = my_place >> level_bit & 1 == 1
        keep_k = jnp.where(upper_side, mid_dk[half_rows:], mid_dk[:half_rows])
        keep_v = jnp.where(upper_side, mid_dv[half_rows:], mid_dv[:half_rows])
        send_k = jnp.where(upper_side, mid_dk[:half_rows], mid_dk[half_rows:])
        send_v = jnp.where(upper_side, mid_dv[:half_rows], mid_dv[half_rows:])
        received = (
            swapped(send_k.astype(jnp.bfloat16), "ctx", level_bit).astype(send_k.dtype),
            swapped(send_v.astype(jnp.bfloat16), "ctx", level_bit).astype(send_v.dtype),
        )
        mid_dk = keep_k + received[0]
        mid_dv = keep_v + received[1]
    mid_dk = mid_dk.reshape(-1, head_count, HEAD_DIM)
    mid_dv = mid_dv.reshape(-1, head_count, HEAD_DIM)
    top_sel = pick_rows(top_share[..., None], ctx_size, top_shift)[..., 0]
    top_low = (top_sel[..., None] * pick_rows(grad_attn, ctx_size, top_shift)).astype(jnp.bfloat16)
    top_row_shift = -(top_sel * pick_rows(inner[..., None], ctx_size, top_shift)[..., 0])
    top_grad, top_soft = score_grads(top_q, top_keys, top_vals, top_total, top_low, top_row_shift)
    top_dq = query_part(top_grad, top_keys)
    gathered_dk, gathered_dv = key_parts(top_grad, top_soft, top_q, top_low)
    summed = (
        lax.psum_scatter(
            gathered_dk.reshape(-1, flat_width), "ctx", scatter_dimension=0, tiled=True
        ),
        lax.psum_scatter(
            gathered_dv.reshape(-1, flat_width), "ctx", scatter_dimension=0, tiled=True
        ),
    )
    top_dk = summed[0].reshape(-1, head_count, HEAD_DIM)
    top_dv = summed[1].reshape(-1, head_count, HEAD_DIM)
    query_grad = (
        base_dq + place_rows(mid_dq, R1, mid_shift) + place_rows(top_dq, ctx_size, top_shift)
    )
    key_grad = base_dk + place_rows(mid_dk, R1, mid_shift) + place_rows(top_dk, ctx_size, top_shift)
    value_grad = (
        base_dv + place_rows(mid_dv, R1, mid_shift) + place_rows(top_dv, ctx_size, top_shift)
    )
    out_shape = (1, tokens, flat_width)
    return (
        attended,
        query_grad.astype(jnp.bfloat16).reshape(out_shape),
        key_grad.astype(jnp.bfloat16).reshape(out_shape),
        value_grad.astype(jnp.bfloat16).reshape(out_shape),
        gain_grad,
    )


VMEM_SPEC = pl.BlockSpec(memory_space=pltpu.VMEM)
SMEM_SPEC = pl.BlockSpec(memory_space=pltpu.SMEM)
PEERS = SPAN - 1
OWNED = SPAN
TILE = 8
STAT_TILES = 2 * TILE
PIECES = 3
NEVER = -1e30
START_ORDER = (3, 1, 2)
LOW = jnp.bfloat16
WIDE = jnp.float32
PACK_VMEM = 65408 * 1024
PLAIN_VMEM = 16 * 1024 * 1024


def contract(left, right, left_dim, right_dim):
    return lax.dot_general(
        left, right, (((left_dim,), (right_dim,)), ((), ())), preferred_element_type=WIDE
    )


def head_cols(head):
    return pl.ds(head * HEAD_DIM, HEAD_DIM)


def picked_counts(tokens, top_step):
    return tokens // top_step, tokens // R1


def pick_matrix(offsets_ref, head, tokens, top_step, picked_axis):
    top_rows, _ = picked_counts(tokens, top_step)
    row = lax.broadcasted_iota(jnp.int32, (tokens, tokens), picked_axis)
    position = lax.broadcasted_iota(jnp.int32, (tokens, tokens), 1 - picked_axis)
    wanted = jnp.where(
        row < top_rows,
        row * top_step + offsets_ref[1, head],
        (row - top_rows) * R1 + offsets_ref[0, head],
    )
    return jnp.where(position == wanted, 1.0, 0.0).astype(LOW)


def rolled(row, shift):
    return pltpu.roll(row, shift % row.shape[1], 1)


def lane_window(row, start, count):
    lane = lax.broadcasted_iota(jnp.int32, row.shape, 1)
    return jnp.where((lane >= start) & (lane < start + count), row, 0.0)


def hit_row(offset, step, tokens):
    position = lax.broadcasted_iota(jnp.int32, (1, tokens), 1)
    return jnp.where(position % step == offset, 1.0, 0.0)


def piece_rows(row, others=None):
    pieces = []
    for _ in range(PIECES):
        piece = row.astype(LOW).astype(WIDE)
        pieces.append(piece)
        row = row - piece
    if others is None:
        others = jnp.zeros((TILE - PIECES, row.shape[1]), WIDE)
    return jnp.concatenate(pieces + [others], 0)


def gain_pieces(rows):
    high = rows.astype(LOW)
    return high, (rows - high.astype(WIDE)).astype(LOW)


def joined_row(rows, first):
    total = rows[first : first + 1]
    for piece in range(1, PIECES):
        total = total + rows[first + piece : first + piece + 1]
    return total


def gain_row_of(ones, product):
    high, rest = gain_pieces(product)
    return (contract(ones, high, 1, 1) + contract(ones, rest, 1, 1))[:1]


def column_mean(block):
    return jnp.mean(block, axis=0, keepdims=True)


def norm_backward(attn, grad_norm):
    inv_rms = lax.rsqrt(column_mean(attn * attn) + EPS)
    normed = attn * inv_rms
    product = grad_norm * normed
    grad_attn = inv_rms * (grad_norm - normed * column_mean(product))
    inner = jnp.sum(grad_attn * attn, axis=0, keepdims=True)
    return normed, product, grad_attn.astype(LOW), inner


def nearest_first(refs):
    by_distance = dict(zip(START_ORDER, refs[1:]))
    return [refs[0], *[by_distance[distance] for distance in range(1, SPAN)]]


def pack_kernel(top_step, offsets_ref, q_ref, k_ref, v_ref, grad_ref, *refs):
    payload_refs, (expo_ref, out_ref, stats_ref, held_ref) = refs[:SPAN], refs[SPAN:]
    tokens, width = q_ref.shape[1:]
    heads = range(width // HEAD_DIM)
    owned = range(OWNED)
    me = lax.axis_index("ctx")
    picked = sum(picked_counts(tokens, top_step))
    score_scale = 1.0 / math.sqrt(HEAD_DIM)
    q_rows, k_rows, v_rows, grad_rows = [
        [ref[0, :, head_cols(head)] for head in heads] for ref in (q_ref, k_ref, v_ref, grad_ref)
    ]
    picks = [pick_matrix(offsets_ref, head, tokens, top_step, 0) for head in heads]
    scores = [contract(k_rows[head], q_rows[head], 1, 1) * score_scale for head in heads]
    moved = [
        contract(
            picks[head][:picked],
            jnp.concatenate([q_rows[head], k_rows[head], v_rows[head], grad_rows[head]], 1),
            1,
            0,
        ).astype(LOW)
        for head in owned
    ]
    shared = [
        contract(
            picks[head][:picked], jnp.concatenate([k_rows[head], v_rows[head]], 1), 1, 0
        ).astype(LOW)
        for head in heads[OWNED:]
    ]
    top_scores = [jnp.max(block, axis=0, keepdims=True) for block in scores]
    expos = [jnp.exp(scores[head] - top_scores[head]) for head in heads]
    for head in heads[OWNED:]:
        key_row = lax.broadcasted_iota(jnp.int32, (tokens, 1), 0)
        times = 1.0
        for level, step in ((0, R1), (1, top_step)):
            offset = offsets_ref[level, head]
            hit_column = jnp.where(key_row % step == offset, 1.0, 0.0)
            times = times + hit_column * hit_row(offset, step, tokens)
        expos[head] = times * expos[head]
    expo_lows = [expo.astype(LOW) for expo in expos]
    outs = [contract(v_rows[head], expo_lows[head], 0, 0) for head in heads]
    totals = [jnp.sum(expo, axis=0, keepdims=True) for expo in expos]
    for head in heads:
        expo_ref[:, head_cols(head)] = expo_lows[head]
        stats_ref[head : head + 1, :] = top_scores[head]
        stats_ref[TILE + head : TILE + head + 1, :] = totals[head]
    for head in owned:
        outs[head] = outs[head] * (1.0 / totals[head])
    outs = [out.astype(LOW) for out in outs]
    picked_outs = [
        contract(picks[head][:picked], outs[head], 1, 1).astype(LOW) for head in owned
    ]
    for head in heads:
        out_ref[:, head_cols(head)] = outs[head]
    for head in owned:
        pieces = piece_rows(top_scores[head] + jnp.log(totals[head])).astype(LOW)
        stat_rows = contract(pieces, picks[head], 1, 1)
        blocks = [moved[head][:, block * HEAD_DIM : (block + 1) * HEAD_DIM] for block in range(4)]
        blocks.append(picked_outs[head])
        blocks += [shared[0][:, :HEAD_DIM], shared[0][:, HEAD_DIM:]]
        blocks.append(jnp.concatenate([stat_rows, jnp.zeros_like(stat_rows)], 0).astype(LOW))
        held_ref[head] = jnp.concatenate(blocks, 0)
    for distance, payload_ref in enumerate(payload_refs):
        payload_ref[...] = held_ref[me ^ distance]


def prepare_kernel(top_step, offsets_ref, grad_ref, gain_ref, out_ref, *refs):
    grad_norm_ref, gain_part_ref, place_ref = refs
    tokens, width = grad_ref.shape[1:]
    heads = range(width // HEAD_DIM)
    top_rows = tokens // top_step
    ones = jnp.ones((TILE, tokens), LOW)
    column = lax.broadcasted_iota(jnp.int32, (tokens, tokens), 1)
    gain_part_ref[...] = jnp.zeros(gain_part_ref.shape, WIDE)
    grad_norms = [
        (grad_ref[0, :, head_cols(head)].astype(WIDE) * gain_ref[:, head_cols(head)]).T
        for head in heads
    ]
    for head in heads:
        cols = head_cols(head)
        grad_norm_ref[:, cols] = grad_norms[head]
        picks = pick_matrix(offsets_ref, head, tokens, top_step, 1)
        place_ref[:, cols] = picks
    for head in range(OWNED):
        cols = head_cols(head)
        mid_offset, top_offset = offsets_ref[0, head], offsets_ref[1, head]
        seen = jnp.maximum(
            hit_row(top_offset, top_step, tokens), hit_row(mid_offset, R1, tokens)
        )
        attn = out_ref[:, cols].astype(WIDE)
        normed = attn * lax.rsqrt(column_mean(attn * attn) + EPS)
        product = grad_norms[head] * normed * (1.0 - seen)
        gain_part_ref[:, cols] = gain_row_of(ones, product) / gain_ref[:, cols]
        both = mid_offset % top_step == top_offset
        kept = jnp.where(column < top_rows, 1.0, jnp.where(both, 0.0, 1.0)).astype(LOW)
        picks = pick_matrix(offsets_ref, head, tokens, top_step, 1)
        place_ref[:, head_cols(len(heads) + head)] = picks * kept


def owner_kernel(top_step, offsets_ref, q_ref, gain_ref, out_ref, grad_norm_ref, *refs):
    stats_ref, gain_base_ref = refs[:2]
    payload_refs, refs = nearest_first(refs[2 : 2 + SPAN]), refs[2 + SPAN :]
    normed_ref, grad_low_ref, score_grad_ref, kept_ref = refs[:4]
    return_refs = refs[4:]
    tokens = q_ref.shape[1]
    heads = q_ref.shape[2] // HEAD_DIM
    top_rows, mid_rows = picked_counts(tokens, top_step)
    picked = top_rows + mid_rows
    top_all, mid_all = SPAN * top_rows, SPAN * mid_rows
    queries = top_all + mid_all
    score_scale = 1.0 / math.sqrt(HEAD_DIM)
    me = lax.axis_index("ctx")
    ones = jnp.ones((TILE, tokens), LOW)

    def by_level(block):
        start = block * picked
        return jnp.concatenate(
            [ref[start : start + top_rows] for ref in payload_refs]
            + [ref[start + top_rows : start + picked] for ref in payload_refs],
            0,
        )

    def per_level(top_row, mid_row):
        return jnp.concatenate(
            [
                jnp.broadcast_to(top_row, (top_all, queries)),
                jnp.broadcast_to(mid_row, (mid_all, queries)),
            ],
            0,
        )

    q_rows, k_rows, v_rows, grad_rows, base_rows = [by_level(block) for block in range(5)]
    stat_start = 7 * picked
    logs = [
        joined_row(ref[stat_start : stat_start + STAT_TILES].astype(WIDE), 0)
        for ref in payload_refs
    ]
    base_top_log = sum(
        rolled(lane_window(log, 0, top_rows), slot * top_rows) for slot, log in enumerate(logs)
    )
    base_mid_log = sum(
        rolled(lane_window(log, top_rows, mid_rows), slot * mid_rows - top_rows)
        for slot, log in enumerate(logs)
    )
    base_log = jnp.concatenate([base_top_log, base_mid_log[:, :mid_all]], 1)
    gain_row = jnp.zeros((1, HEAD_DIM), WIDE)
    for head in range(OWNED):
        gain_row = gain_row + jnp.where(me == head, 1.0, 0.0) * gain_ref[:, head_cols(head)]
    mid_offset, top_offset = offsets_ref[0, me], offsets_ref[1, me]
    both = mid_offset % top_step == top_offset
    lane = lax.broadcasted_iota(jnp.int32, (1, queries), 1)
    is_top = jnp.where(lane < top_all, 1.0, 0.0)
    top_in_mid = jnp.where(((lane % top_rows) * top_step + top_offset) % R1 == mid_offset, 1.0, 0.0)
    both_flag = jnp.where(both, 1.0, 0.0)
    sees_top = is_top + (1.0 - is_top) * both_flag
    sees_mid = is_top * top_in_mid + (1.0 - is_top)
    bias = per_level((1.0 - sees_top) * NEVER, (1.0 - sees_mid) * NEVER)
    last = heads - 1
    cols = head_cols(last)
    peers = payload_refs[1:]
    q_last = q_ref[0, :, cols]
    k_peers = jnp.concatenate([ref[5 * picked : 6 * picked] for ref in peers], 0)
    v_peers = jnp.concatenate([ref[6 * picked : 7 * picked] for ref in peers], 0)
    last_biases = [
        jnp.broadcast_to((1.0 - hit_row(offsets_ref[level, last], step, tokens)) * NEVER, shape)
        for level, step, shape in (
            (1, top_step, (top_rows, tokens)),
            (0, R1, (mid_rows, tokens)),
        )
    ]
    scores = contract(k_rows, q_rows, 1, 1) * score_scale + bias
    scores_last = contract(k_peers, q_last, 1, 1) * score_scale + jnp.concatenate(
        last_biases * PEERS, 0
    )
    base_attn = base_rows.astype(WIDE).T
    grad_norm = (grad_rows.astype(WIDE) * gain_row).T
    top_score = jnp.maximum(base_log, jnp.max(scores, axis=0, keepdims=True))
    base_top, base_total = stats_ref[last : last + 1, :], stats_ref[TILE + last : TILE + last + 1, :]
    top_last = jnp.maximum(base_top, jnp.max(scores_last, axis=0, keepdims=True))
    expo = jnp.exp(scores - top_score)
    expo_last = jnp.exp(scores_last - top_last)
    factor = jnp.exp(base_log - top_score)
    factor_last = jnp.exp(base_top - top_last)
    total = factor + jnp.sum(expo, axis=0, keepdims=True)
    total_last = factor_last * base_total + jnp.sum(expo_last, axis=0, keepdims=True)
    inv_total, inv_last = 1.0 / total, 1.0 / total_last
    soft, soft_last = expo * inv_total, expo_last * inv_last
    soft_low, soft_last_low = soft.astype(LOW), soft_last.astype(LOW)
    factor_last = factor_last * inv_last
    attn = (factor * inv_total) * base_attn + contract(v_rows, soft_low, 0, 0)
    attn_last = factor_last * out_ref[:, cols].astype(WIDE) + contract(v_peers, soft_last_low, 0, 0)
    _, product, grad_low, inner = norm_backward(attn, grad_norm)
    normed_last, product_last, grad_last_low, inner_last = norm_backward(
        attn_last, grad_norm_ref[:, cols]
    )
    spans = (slice(0, top_all), slice(top_all, queries))
    prob_grads = [contract(v_rows[span], grad_low[:, span], 1, 0) for span in spans]
    prob_grad_last = contract(v_peers, grad_last_low, 1, 0)
    score_grads = [
        (soft[span, span] * (prob_grad - inner[:, span]) * score_scale).astype(LOW)
        for span, prob_grad in zip(spans, prob_grads)
    ]
    score_grad_last = (soft_last * (prob_grad_last - inner_last) * score_scale).astype(LOW)
    dks = [
        contract(score_grad, q_rows[span], 1, 0).astype(LOW)
        for span, score_grad in zip(spans, score_grads)
    ]
    dk_last = contract(score_grad_last, q_last, 1, 0).astype(LOW)
    dvs = [
        contract(soft_low[span, span], grad_low[:, span], 1, 1).astype(LOW) for span in spans
    ]
    dv_last = contract(soft_last_low, grad_last_low, 1, 1).astype(LOW)
    dqs = [
        contract(score_grad, k_rows[span], 0, 0).astype(LOW)
        for span, score_grad in zip(spans, score_grads)
    ]
    attn_rows = attn.T.astype(LOW)
    attn_parts = [attn_rows[span] for span in spans]
    log_total = top_score + jnp.log(total)
    padding = jnp.zeros((1, top_all - mid_all), WIDE)
    once = is_top + (1.0 - is_top) * (1.0 - both_flag)
    ones_all = jnp.ones((TILE, queries), LOW)
    own_gain = gain_row_of(ones_all, product * once) / gain_row
    gain_rows = [
        gain_base_ref[:, head_cols(head)] + jnp.where(me == head, 1.0, 0.0) * own_gain
        for head in range(OWNED)
    ]
    gain_rows.append(gain_row_of(ones, product_last) / gain_ref[:, cols])
    gain_high, gain_rest = [
        rows.astype(WIDE) for rows in gain_pieces(jnp.concatenate(gain_rows, 0))
    ]
    top_log, mid_log = log_total[:, :top_all], jnp.concatenate(
        [log_total[:, top_all:], padding], 1
    )
    empty = jnp.zeros((PIECES, HEAD_DIM), WIDE)
    for distance, return_ref in enumerate(return_refs):
        blocks = []
        for top_block, mid_block in (dqs, dks, dvs, attn_parts):
            blocks.append(top_block[distance * top_rows : (distance + 1) * top_rows])
            blocks.append(mid_block[distance * mid_rows : (distance + 1) * mid_rows])
        start = max(distance - 1, 0) * picked
        blocks += [dk_last[start : start + picked], dv_last[start : start + picked]]
        log_row = lane_window(rolled(top_log, -distance * top_rows), 0, top_rows) + lane_window(
            rolled(mid_log, top_rows - distance * mid_rows), top_rows, mid_rows
        )
        log_rows = [piece_rows(log_row, gain_high), empty, gain_rest]
        blocks.append(jnp.concatenate(log_rows, 0).astype(LOW))
        return_ref[...] = jnp.concatenate(blocks, 0)
    normed_ref[...] = normed_last
    grad_low_ref[...] = grad_last_low
    score_grad_ref[...] = score_grad_last
    kept_ref[0:1, :] = factor_last
    kept_ref[1:2, :] = inner_last


def last_head_kernel(top_step, q_ref, k_ref, v_ref, gain_ref, expo_ref, *refs):
    normed_ref, grad_low_ref, peer_score_grad_ref, kept_ref, *peers = refs[: 4 + PEERS]
    peers = nearest_first([None, *peers])[1:]
    attended_ref, dq_ref, dk_ref, dv_ref = refs[4 + PEERS :]
    picked = sum(picked_counts(q_ref.shape[1], top_step))
    score_scale = 1.0 / math.sqrt(HEAD_DIM)
    cols = head_cols(q_ref.shape[2] // HEAD_DIM - 1)
    attended_ref[...] = (normed_ref[...].T * gain_ref[:, cols]).astype(LOW)
    k_peers = jnp.concatenate([ref[5 * picked : 6 * picked] for ref in peers], 0)
    grad_low = grad_low_ref[...]
    soft = expo_ref[:, cols].astype(WIDE) * kept_ref[0:1, :]
    prob_grad = contract(v_ref[0, :, cols], grad_low, 1, 0)
    score_grad = (soft * (prob_grad - kept_ref[1:2, :]) * score_scale).astype(LOW)
    dk_ref[...] = contract(score_grad, q_ref[0, :, cols], 1, 0)
    dv_ref[...] = contract(soft.astype(LOW), grad_low, 1, 1)
    dq_ref[...] = (
        contract(score_grad, k_ref[0, :, cols], 0, 0)
        + contract(peer_score_grad_ref[...], k_peers, 0, 0)
    ).astype(LOW)


def gain_kernel(picked, *refs):
    return_refs, gain_ref = nearest_first(refs[:SPAN]), refs[SPAN]
    tiles = [ref[6 * picked : 6 * picked + STAT_TILES].astype(WIDE) for ref in return_refs]
    parts = [tile[PIECES:TILE] + tile[TILE + PIECES :] for tile in tiles]
    total = (parts[0] + parts[1]) + (parts[2] + parts[3])
    for head in range(gain_ref.shape[1] // HEAD_DIM):
        gain_ref[:, head_cols(head)] = total[head : head + 1]


def mix_kernel(top_step, offsets_ref, v_ref, gain_ref, expo_ref, out_ref, *refs):
    grad_norm_ref, stats_ref, place_ref = refs[:3]
    return_refs, refs = nearest_first(refs[3 : 3 + SPAN]), refs[3 + SPAN :]
    attended_ref, grad_low_ref, soft_ref, score_grad_ref, placed_ref = refs
    tokens, width = v_ref.shape[1:]
    count = width // HEAD_DIM
    picked = sum(picked_counts(tokens, top_step))
    score_scale = 1.0 / math.sqrt(HEAD_DIM)
    me = lax.axis_index("ctx")
    heads = range(OWNED)
    every = [head_cols(head) for head in heads]
    for distance, return_ref in enumerate(return_refs):
        placed_ref[me ^ distance] = return_ref[...]
    once = [place_ref[:, head_cols(count + head)] for head in heads]
    attn_parts = [
        contract(placed_ref[head, 3 * picked : 4 * picked], once[head][:, :picked], 0, 1)
        for head in heads
    ]
    log_parts = [
        contract(placed_ref[head, 6 * picked : 6 * picked + STAT_TILES], once[head], 1, 1)
        for head in heads
    ]
    factors, normeds, grad_lows, inners = [], [], [], []
    for head in heads:
        top_hit = hit_row(offsets_ref[1, head], top_step, tokens)
        mid_hit = hit_row(offsets_ref[0, head], R1, tokens)
        seen = jnp.maximum(top_hit, mid_hit) > 0.5
        top_score, total = stats_ref[head : head + 1, :], stats_ref[TILE + head : TILE + head + 1, :]
        log_total = jnp.where(seen, joined_row(log_parts[head], 0), top_score + jnp.log(total))
        factors.append(jnp.exp(top_score - log_total))
        attn = jnp.where(seen, attn_parts[head], out_ref[:, every[head]].astype(WIDE))
        normed, _, grad_low, inner = norm_backward(attn, grad_norm_ref[:, every[head]])
        normeds.append(normed)
        grad_lows.append(grad_low)
        inners.append(inner)
    prob_grads = [contract(v_ref[0, :, every[head]], grad_lows[head], 1, 0) for head in heads]
    softs = [expo_ref[:, every[head]].astype(WIDE) * factors[head] for head in heads]
    for head in heads:
        cols = every[head]
        grad_low_ref[:, cols] = grad_lows[head]
        soft_ref[:, cols] = softs[head].astype(LOW)
        score_grad_ref[:, cols] = (
            softs[head] * (prob_grads[head] - inners[head]) * score_scale
        ).astype(LOW)
        attended_ref[:, cols] = (normeds[head].T * gain_ref[:, cols]).astype(LOW)


def finish_kernel(top_step, *refs):
    gain_refs, (q_ref, k_ref, place_ref), refs = refs[:2], refs[2:5], refs[5:]
    mixed_refs, (last_attended_ref, last_dq_ref, last_dk_ref, last_dv_ref) = refs[:5], refs[5:9]
    return_refs, refs = nearest_first(refs[9 : 9 + SPAN]), refs[9 + SPAN :]
    mixed_ref, grad_low_ref, soft_ref, score_grad_ref, returned_ref = mixed_refs
    attended_ref, dq_ref, dk_ref, dv_ref, gain_out_ref = refs
    tokens, width = q_ref.shape[1:]
    picked = sum(picked_counts(tokens, top_step))
    heads = range(OWNED)
    every = [head_cols(head) for head in heads]
    gain_out_ref[...] = (gain_refs[0][...] + gain_refs[1][...]).reshape(gain_out_ref.shape)
    score_grads = [score_grad_ref[:, cols] for cols in every]
    dqs = [contract(score_grads[head], k_ref[0, :, every[head]], 0, 0) for head in heads]
    placed = [
        contract(
            place_ref[:, pl.ds(head * HEAD_DIM, picked)],
            jnp.concatenate(
                [returned_ref[head, block * picked : (block + 1) * picked] for block in range(3)], 1
            ),
            1,
            0,
        )
        for head in heads
    ]
    dks = [contract(score_grads[head], q_ref[0, :, every[head]], 1, 0) for head in heads]
    dvs = [contract(soft_ref[:, cols], grad_low_ref[:, cols], 1, 1) for cols in every]
    last = width // HEAD_DIM - 1
    total = sum(ref[4 * picked : 6 * picked].astype(WIDE) for ref in return_refs[1:]).astype(LOW)
    rows = contract(
        place_ref[:, pl.ds(last * HEAD_DIM, picked)],
        jnp.concatenate([total[:picked], total[picked:]], 1),
        1,
        0,
    )
    for head in heads:
        cols = every[head]
        attended_ref[0, :, cols] = mixed_ref[:, cols]
        for which, (block, out_block_ref) in enumerate(
            ((dqs[head], dq_ref), (dks[head], dk_ref), (dvs[head], dv_ref))
        ):
            part = placed[head][:, which * HEAD_DIM : (which + 1) * HEAD_DIM]
            out_block_ref[0, :, cols] = (block + part).astype(LOW)
    cols = head_cols(last)
    attended_ref[0, :, cols] = last_attended_ref[...]
    dq_ref[0, :, cols] = last_dq_ref[...]
    dk_ref[0, :, cols] = (last_dk_ref[...] + rows[:, :HEAD_DIM]).astype(LOW)
    dv_ref[0, :, cols] = (last_dv_ref[...] + rows[:, HEAD_DIM:]).astype(LOW)


def across(block, axis, distance):
    route = [(place, place ^ distance) for place in range(lax.axis_size(axis))]
    return lax.ppermute(block, axis, route)


def to_peers(blocks):
    return [across(blocks[distance - 1], "ctx", distance) for distance in START_ORDER]


def call(kernel, name, operands, results, microseconds, vmem=PLAIN_VMEM, scratch=()):
    return pl.pallas_call(
        kernel,
        out_shape=results,
        in_specs=[SMEM_SPEC if block.dtype == jnp.int32 else VMEM_SPEC for block in operands],
        out_specs=[VMEM_SPEC] * len(results),
        scratch_shapes=scratch,
        compiler_params=pltpu.CompilerParams(vmem_limit_bytes=vmem),
        cost_estimate=pl.CostEstimate(
            flops=int(microseconds * 10**9), bytes_accessed=0, transcendentals=0
        ),
        name=name,
    )(*operands)


def one_segment_shards(queries, keys, values, grad_y, out_gain, offsets):
    tokens, width = queries.shape[1:]
    heads = width // HEAD_DIM
    top_step = lax.axis_size("ctx")
    picked = sum(picked_counts(tokens, top_step))
    shape = jax.ShapeDtypeStruct
    row_block = shape((1, tokens, width), LOW)
    low_block, wide_block = shape((tokens, width), LOW), shape((tokens, width), WIDE)
    low_head, wide_head = shape((tokens, HEAD_DIM), LOW), shape((tokens, HEAD_DIM), WIDE)
    gain_block = shape((1, width), WIDE)
    stats_block = shape((2 * TILE, tokens), WIDE)
    payload = shape((7 * picked + STAT_TILES, HEAD_DIM), LOW)
    answer = shape((6 * picked + STAT_TILES, HEAD_DIM), LOW)
    bind = functools.partial
    gain_row = out_gain.reshape(1, width)
    own, *sent, expo, base_out, stats = call(
        bind(pack_kernel, top_step),
        "pack",
        (offsets, queries, keys, values, grad_y),
        [payload] * SPAN + [low_block, low_block, stats_block],
        1,
        vmem=PACK_VMEM,
        scratch=[pltpu.VMEM((OWNED, *payload.shape), LOW)],
    )
    received = to_peers(sent)
    grad_norm, gain_base, place = call(
        bind(prepare_kernel, top_step),
        "prepare",
        (offsets, grad_y, gain_row, base_out),
        [wide_block, gain_block, shape((tokens, 2 * width), LOW)],
        2,
    )
    normed, grad_low, score_grad, kept, own_answer, *answers = call(
        bind(owner_kernel, top_step),
        "owner",
        (offsets, queries, gain_row, base_out, grad_norm, stats, gain_base, own, *received),
        [
            wide_head,
            low_head,
            shape((PEERS * picked, HEAD_DIM), LOW),
            shape((TILE, tokens), WIDE),
        ]
        + [answer] * SPAN,
        3,
    )
    returned = to_peers(answers)
    last_results = call(
        bind(last_head_kernel, top_step),
        "last_head",
        (queries, keys, values, gain_row, expo, normed, grad_low, score_grad, kept, *received),
        [low_head, low_head, wide_head, wide_head],
        20,
    )
    (gain_sum,) = call(bind(gain_kernel, picked), "gain", (own_answer, *returned), [gain_block], 1)
    gain_rest = across(gain_sum, "dp", 1)
    mixed_block = shape((tokens, OWNED * HEAD_DIM), LOW)
    mixed = call(
        bind(mix_kernel, top_step),
        "mix",
        (
            offsets,
            values,
            gain_row,
            expo,
            base_out,
            grad_norm,
            stats,
            place,
            own_answer,
            *returned,
        ),
        [mixed_block] * 4 + [shape((OWNED, *answer.shape), LOW)],
        20,
    )
    attended, query_grad, key_grad, value_grad, gain_grad = call(
        bind(finish_kernel, top_step),
        "finish",
        (
            gain_sum,
            gain_rest,
            queries,
            keys,
            place,
            *mixed,
            *last_results,
            own_answer,
            *returned,
        ),
        [row_block] * 4 + [shape((width,), WIDE)],
        1,
    )
    return attended, query_grad, key_grad, value_grad, gain_grad


def shards(*operands):
    one_segment = lax.axis_size("ctx") == SPAN
    if one_segment and operands[0].shape[2] == (OWNED + 1) * HEAD_DIM:
        return one_segment_shards(*operands)
    return general_shards(*operands)


def solution(mesh):
    in_specs = (
        P("dp", "ctx", "head"),
        P("dp", "ctx", "head"),
        P("dp", "ctx", "head"),
        P("dp", "ctx", "head"),
        P("head"),
        P(None, "head"),
    )
    out_specs = (
        P("dp", "ctx", "head"),
        P("dp", "ctx", "head"),
        P("dp", "ctx", "head"),
        P("dp", "ctx", "head"),
        P("head"),
    )
    return jax.shard_map(shards, mesh=mesh, in_specs=in_specs, out_specs=out_specs, check_vma=False)
```

```python
import functools
import math

import jax
import jax.numpy as jnp
from jax import lax
from jax.experimental import pallas as pl
from jax.experimental.pallas import tpu as pltpu
from jax.sharding import PartitionSpec as P

HEAD_DIM = 128
SPAN = 4
R1 = 8


EPS = 1e-06


def swapped(block, axis, bit):
    count = lax.axis_size(axis)
    route = []
    for low in range(count):
        high = low | 1 << bit
        if high != low and high < count:
            route += [(low, high), (high, low)]
    return lax.ppermute(block, axis, route)


def pick_rows(source_rows, dilation, shifts):
    row_count, head_count, head_width = source_rows.shape
    grouped = source_rows.reshape(row_count // dilation, dilation, head_count, head_width)
    hit_mask = jnp.arange(dilation, dtype=jnp.int32).reshape(1, dilation, 1, 1) == shifts.reshape(
        1, 1, head_count, 1
    )
    chosen = jnp.where(hit_mask, grouped, jnp.zeros((), source_rows.dtype))
    return jnp.sum(chosen, axis=1, dtype=source_rows.dtype)


def place_rows(row_values, dilation, shifts):
    row_count, head_count, head_width = row_values.shape
    hit_mask = jnp.arange(dilation, dtype=jnp.int32).reshape(1, dilation, 1, 1) == shifts.reshape(
        1, 1, head_count, 1
    )
    spread = jnp.where(hit_mask, row_values[:, None], jnp.zeros((), row_values.dtype))
    return spread.reshape(row_count * dilation, head_count, head_width)


def level_scores(q_rows, k_rows):
    score_scale = 1.0 / math.sqrt(q_rows.shape[-1])
    return (
        jnp.einsum("qhe,khe->hqk", q_rows, k_rows, preferred_element_type=jnp.float32) * score_scale
    )


def attend(q_rows, k_rows, v_rows):
    scores = level_scores(q_rows, k_rows)
    row_max = jnp.max(scores, axis=-1, keepdims=True)
    log_total = row_max[..., 0] + jnp.log(jnp.sum(jnp.exp(scores - row_max), axis=-1))
    soft_rows = jnp.exp(scores - log_total[..., None]).astype(jnp.bfloat16)
    level_out = jnp.einsum("hqk,khe->qhe", soft_rows, v_rows, preferred_element_type=jnp.float32)
    return (level_out, log_total.T)


def score_grads(q_rows, k_rows, v_rows, log_total, grad_low, row_shift):
    score_scale = 1.0 / math.sqrt(q_rows.shape[-1])
    scores = level_scores(q_rows, k_rows)
    exact_soft = jnp.exp(scores - log_total.T[..., None])
    prob_grad = jnp.einsum("qhe,khe->hqk", grad_low, v_rows, preferred_element_type=jnp.float32)
    score_grad = (exact_soft * (prob_grad + row_shift.T[..., None]) * score_scale).astype(
        jnp.bfloat16
    )
    return (score_grad, exact_soft.astype(jnp.bfloat16))


def key_parts(score_grad, soft_low, q_rows, grad_low):
    k_part = jnp.einsum("hqk,qhe->khe", score_grad, q_rows, preferred_element_type=jnp.float32)
    v_part = jnp.einsum("hqk,qhe->khe", soft_low, grad_low, preferred_element_type=jnp.float32)
    return (k_part, v_part)


def query_part(score_grad, k_rows):
    return jnp.einsum("hqk,khe->qhe", score_grad, k_rows, preferred_element_type=jnp.float32)


def general_shards(queries, keys, values, grad_y, out_gain, offsets):
    tokens = queries.shape[1]
    flat_width = queries.shape[2]
    head_count = flat_width // HEAD_DIM
    row_shape = (tokens, head_count, HEAD_DIM)
    q_own = queries[0].reshape(row_shape)
    k_own = keys[0].reshape(row_shape)
    v_own = values[0].reshape(row_shape)
    ctx_size = lax.axis_size("ctx")
    span_bits = SPAN.bit_length() - 1
    my_place = lax.axis_index("ctx")
    mid_shift = offsets[0]
    top_shift = offsets[1]
    positions = jnp.arange(tokens, dtype=jnp.int32)
    mid_hit = (positions % R1)[:, None] == mid_shift[None, :]
    top_hit = (positions % ctx_size)[:, None] == top_shift[None, :]
    mid_q = pick_rows(q_own, R1, mid_shift)
    mid_k = pick_rows(k_own, R1, mid_shift)
    mid_v = pick_rows(v_own, R1, mid_shift)
    top_q = pick_rows(q_own, ctx_size, top_shift)
    top_k = pick_rows(k_own, ctx_size, top_shift)
    top_v = pick_rows(v_own, ctx_size, top_shift)
    mid_keys = mid_k.reshape(-1, flat_width)
    mid_vals = mid_v.reshape(-1, flat_width)
    top_keys = top_k.reshape(-1, flat_width)
    top_vals = top_v.reshape(-1, flat_width)

    def append_peer(mine, received, level_bit):
        upper_side = my_place >> level_bit & 1 == 1
        return jnp.where(
            upper_side, jnp.concatenate([received, mine], 0), jnp.concatenate([mine, received], 0)
        )

    for level_bit in range(span_bits):
        received = swapped((mid_keys, mid_vals), "ctx", level_bit)
        mid_keys = append_peer(mid_keys, received[0], level_bit)
        mid_vals = append_peer(mid_vals, received[1], level_bit)
    top_keys, top_vals = (
        lax.all_gather(top_keys, "ctx", axis=0, tiled=True),
        lax.all_gather(top_vals, "ctx", axis=0, tiled=True),
    )
    mid_keys = mid_keys.reshape(-1, head_count, HEAD_DIM)
    mid_vals = mid_vals.reshape(-1, head_count, HEAD_DIM)
    top_keys = top_keys.reshape(-1, head_count, HEAD_DIM)
    top_vals = top_vals.reshape(-1, head_count, HEAD_DIM)
    base_out, base_total = attend(q_own, k_own, v_own)
    mid_out, mid_total = attend(mid_q, mid_keys, mid_vals)
    top_out, top_total = attend(top_q, top_keys, top_vals)
    mid_full = place_rows(mid_total[..., None], R1, mid_shift)[..., 0]
    top_full = place_rows(top_total[..., None], ctx_size, top_shift)[..., 0]
    row_max = jnp.maximum(base_total, jnp.where(mid_hit, mid_full, base_total))
    row_max = jnp.maximum(row_max, jnp.where(top_hit, top_full, base_total))
    base_expo = jnp.exp(base_total - row_max)
    mid_expo = jnp.where(mid_hit, jnp.exp(mid_full - row_max), 0.0)
    top_expo = jnp.where(top_hit, jnp.exp(top_full - row_max), 0.0)
    denom = base_expo + mid_expo + top_expo
    base_share = base_expo / denom
    mid_share = mid_expo / denom
    top_share = top_expo / denom
    attn = (
        base_share[..., None] * base_out
        + mid_share[..., None] * place_rows(mid_out, R1, mid_shift)
        + top_share[..., None] * place_rows(top_out, ctx_size, top_shift)
    )
    inv_rms = lax.rsqrt(jnp.mean(attn * attn, axis=-1, keepdims=True) + EPS)
    normed = attn * inv_rms
    gain_rows = out_gain.reshape(head_count, HEAD_DIM)
    attended = (normed * gain_rows).astype(jnp.bfloat16).reshape(1, tokens, flat_width)
    grad_full = grad_y[0].reshape(row_shape).astype(jnp.float32)
    gain_part = jnp.sum(grad_full * normed, axis=0).reshape(flat_width)
    gain_grad = lax.psum(gain_part, ("dp", "ctx"))
    grad_norm = grad_full * gain_rows
    grad_attn = inv_rms * (
        grad_norm - normed * jnp.mean(grad_norm * normed, axis=-1, keepdims=True)
    )
    inner = jnp.sum(grad_attn * attn, axis=-1)
    base_low = (base_share[..., None] * grad_attn).astype(jnp.bfloat16)
    base_shift = -(base_share * inner)
    base_grad, base_soft = score_grads(q_own, k_own, v_own, base_total, base_low, base_shift)
    base_dq = query_part(base_grad, k_own)
    base_dk, base_dv = key_parts(base_grad, base_soft, q_own, base_low)
    mid_sel = pick_rows(mid_share[..., None], R1, mid_shift)[..., 0]
    mid_low = (mid_sel[..., None] * pick_rows(grad_attn, R1, mid_shift)).astype(jnp.bfloat16)
    mid_row_shift = -(mid_sel * pick_rows(inner[..., None], R1, mid_shift)[..., 0])
    mid_grad, mid_soft = score_grads(mid_q, mid_keys, mid_vals, mid_total, mid_low, mid_row_shift)
    mid_dq = query_part(mid_grad, mid_keys)
    mid_dk, mid_dv = key_parts(mid_grad, mid_soft, mid_q, mid_low)
    mid_dk = mid_dk.reshape(-1, flat_width)
    mid_dv = mid_dv.reshape(-1, flat_width)
    for level_bit in reversed(range(span_bits)):
        half_rows = mid_dk.shape[0] // 2
        upper_side = my_place >> level_bit & 1 == 1
        keep_k = jnp.where(upper_side, mid_dk[half_rows:], mid_dk[:half_rows])
        keep_v = jnp.where(upper_side, mid_dv[half_rows:], mid_dv[:half_rows])
        send_k = jnp.where(upper_side, mid_dk[:half_rows], mid_dk[half_rows:])
        send_v = jnp.where(upper_side, mid_dv[:half_rows], mid_dv[half_rows:])
        received = (
            swapped(send_k.astype(jnp.bfloat16), "ctx", level_bit).astype(send_k.dtype),
            swapped(send_v.astype(jnp.bfloat16), "ctx", level_bit).astype(send_v.dtype),
        )
        mid_dk = keep_k + received[0]
        mid_dv = keep_v + received[1]
    mid_dk = mid_dk.reshape(-1, head_count, HEAD_DIM)
    mid_dv = mid_dv.reshape(-1, head_count, HEAD_DIM)
    top_sel = pick_rows(top_share[..., None], ctx_size, top_shift)[..., 0]
    top_low = (top_sel[..., None] * pick_rows(grad_attn, ctx_size, top_shift)).astype(jnp.bfloat16)
    top_row_shift = -(top_sel * pick_rows(inner[..., None], ctx_size, top_shift)[..., 0])
    top_grad, top_soft = score_grads(top_q, top_keys, top_vals, top_total, top_low, top_row_shift)
    top_dq = query_part(top_grad, top_keys)
    gathered_dk, gathered_dv = key_parts(top_grad, top_soft, top_q, top_low)
    summed = (
        lax.psum_scatter(
            gathered_dk.reshape(-1, flat_width), "ctx", scatter_dimension=0, tiled=True
        ),
        lax.psum_scatter(
            gathered_dv.reshape(-1, flat_width), "ctx", scatter_dimension=0, tiled=True
        ),
    )
    top_dk = summed[0].reshape(-1, head_count, HEAD_DIM)
    top_dv = summed[1].reshape(-1, head_count, HEAD_DIM)
    query_grad = (
        base_dq + place_rows(mid_dq, R1, mid_shift) + place_rows(top_dq, ctx_size, top_shift)
    )
    key_grad = base_dk + place_rows(mid_dk, R1, mid_shift) + place_rows(top_dk, ctx_size, top_shift)
    value_grad = (
        base_dv + place_rows(mid_dv, R1, mid_shift) + place_rows(top_dv, ctx_size, top_shift)
    )
    out_shape = (1, tokens, flat_width)
    return (
        attended,
        query_grad.astype(jnp.bfloat16).reshape(out_shape),
        key_grad.astype(jnp.bfloat16).reshape(out_shape),
        value_grad.astype(jnp.bfloat16).reshape(out_shape),
        gain_grad,
    )


VMEM_SPEC = pl.BlockSpec(memory_space=pltpu.VMEM)
SMEM_SPEC = pl.BlockSpec(memory_space=pltpu.SMEM)
PEERS = SPAN - 1
OWNED = SPAN
TILE = 8
STAT_TILES = 2 * TILE
PIECES = 3
NEVER = -1e30
START_ORDER = (2, 1, 3)
LOW = jnp.bfloat16
WIDE = jnp.float32
PACK_VMEM = 65408 * 1024
PLAIN_VMEM = 16 * 1024 * 1024


def contract(left, right, left_dim, right_dim):
    return lax.dot_general(
        left, right, (((left_dim,), (right_dim,)), ((), ())), preferred_element_type=WIDE
    )


def head_cols(head):
    return pl.ds(head * HEAD_DIM, HEAD_DIM)


def picked_counts(tokens, top_step):
    return tokens // top_step, tokens // R1


def pick_matrix(offsets_ref, head, tokens, top_step, picked_axis):
    top_rows, _ = picked_counts(tokens, top_step)
    row = lax.broadcasted_iota(jnp.int32, (tokens, tokens), picked_axis)
    position = lax.broadcasted_iota(jnp.int32, (tokens, tokens), 1 - picked_axis)
    wanted = jnp.where(
        row < top_rows,
        row * top_step + offsets_ref[1, head],
        (row - top_rows) * R1 + offsets_ref[0, head],
    )
    return jnp.where(position == wanted, 1.0, 0.0).astype(LOW)


def rolled(row, shift):
    return pltpu.roll(row, shift % row.shape[1], 1)


def lane_window(row, start, count):
    lane = lax.broadcasted_iota(jnp.int32, row.shape, 1)
    return jnp.where((lane >= start) & (lane < start + count), row, 0.0)


def hit_row(offset, step, tokens):
    position = lax.broadcasted_iota(jnp.int32, (1, tokens), 1)
    return jnp.where(position % step == offset, 1.0, 0.0)


def piece_rows(row, others=None):
    pieces = []
    for _ in range(PIECES):
        piece = row.astype(LOW).astype(WIDE)
        pieces.append(piece)
        row = row - piece
    if others is None:
        others = jnp.zeros((TILE - PIECES, row.shape[1]), WIDE)
    return jnp.concatenate(pieces + [others], 0)


def gain_pieces(rows):
    high = rows.astype(LOW)
    return high, (rows - high.astype(WIDE)).astype(LOW)


def joined_row(rows, first):
    total = rows[first : first + 1]
    for piece in range(1, PIECES):
        total = total + rows[first + piece : first + piece + 1]
    return total


def gain_row_of(ones, product):
    high, rest = gain_pieces(product)
    return (contract(ones, high, 1, 1) + contract(ones, rest, 1, 1))[:1]


def column_mean(block):
    return jnp.mean(block, axis=0, keepdims=True)


def norm_backward(attn, grad_norm):
    inv_rms = lax.rsqrt(column_mean(attn * attn) + EPS)
    normed = attn * inv_rms
    product = grad_norm * normed
    grad_attn = inv_rms * (grad_norm - normed * column_mean(product))
    inner = jnp.sum(grad_attn * attn, axis=0, keepdims=True)
    return normed, product, grad_attn.astype(LOW), inner


def nearest_first(refs):
    by_distance = dict(zip(START_ORDER, refs[1:]))
    return [refs[0], *[by_distance[distance] for distance in range(1, SPAN)]]


def pack_kernel(top_step, offsets_ref, q_ref, k_ref, v_ref, grad_ref, *refs):
    payload_refs, (expo_ref, out_ref, stats_ref, held_ref) = refs[:SPAN], refs[SPAN:]
    tokens, width = q_ref.shape[1:]
    heads = range(width // HEAD_DIM)
    owned = range(OWNED)
    me = lax.axis_index("ctx")
    picked = sum(picked_counts(tokens, top_step))
    score_scale = 1.0 / math.sqrt(HEAD_DIM)
    q_rows, k_rows, v_rows, grad_rows = [
        [ref[0, :, head_cols(head)] for head in heads] for ref in (q_ref, k_ref, v_ref, grad_ref)
    ]
    picks = [pick_matrix(offsets_ref, head, tokens, top_step, 0) for head in heads]
    scores = [contract(k_rows[head], q_rows[head], 1, 1) * score_scale for head in heads]
    moved = [
        contract(
            picks[head][:picked],
            jnp.concatenate([q_rows[head], k_rows[head], v_rows[head], grad_rows[head]], 1),
            1,
            0,
        ).astype(LOW)
        for head in owned
    ]
    shared = [
        contract(
            picks[head][:picked], jnp.concatenate([k_rows[head], v_rows[head]], 1), 1, 0
        ).astype(LOW)
        for head in heads[OWNED:]
    ]
    top_scores = [jnp.max(block, axis=0, keepdims=True) for block in scores]
    expos = [jnp.exp(scores[head] - top_scores[head]) for head in heads]
    for head in heads[OWNED:]:
        key_row = lax.broadcasted_iota(jnp.int32, (tokens, 1), 0)
        times = 1.0
        for level, step in ((0, R1), (1, top_step)):
            offset = offsets_ref[level, head]
            hit_column = jnp.where(key_row % step == offset, 1.0, 0.0)
            times = times + hit_column * hit_row(offset, step, tokens)
        expos[head] = times * expos[head]
    expo_lows = [expo.astype(LOW) for expo in expos]
    outs = [contract(v_rows[head], expo_lows[head], 0, 0) for head in heads]
    totals = [jnp.sum(expo, axis=0, keepdims=True) for expo in expos]
    for head in heads:
        expo_ref[:, head_cols(head)] = expo_lows[head]
        stats_ref[head : head + 1, :] = top_scores[head]
        stats_ref[TILE + head : TILE + head + 1, :] = totals[head]
    for head in owned:
        outs[head] = outs[head] * (1.0 / totals[head])
    outs = [out.astype(LOW) for out in outs]
    picked_outs = [
        contract(picks[head][:picked], outs[head], 1, 1).astype(LOW) for head in owned
    ]
    for head in heads:
        out_ref[:, head_cols(head)] = outs[head]
    for head in owned:
        pieces = piece_rows(top_scores[head] + jnp.log(totals[head])).astype(LOW)
        stat_rows = contract(pieces, picks[head], 1, 1)
        blocks = [moved[head][:, block * HEAD_DIM : (block + 1) * HEAD_DIM] for block in range(4)]
        blocks.append(picked_outs[head])
        blocks += [shared[0][:, :HEAD_DIM], shared[0][:, HEAD_DIM:]]
        blocks.append(jnp.concatenate([stat_rows, jnp.zeros_like(stat_rows)], 0).astype(LOW))
        held_ref[head] = jnp.concatenate(blocks, 0)
    for distance, payload_ref in enumerate(payload_refs):
        payload_ref[...] = held_ref[me ^ distance]


def prepare_kernel(top_step, offsets_ref, grad_ref, gain_ref, out_ref, *refs):
    grad_norm_ref, gain_part_ref, place_ref = refs
    tokens, width = grad_ref.shape[1:]
    heads = range(width // HEAD_DIM)
    top_rows = tokens // top_step
    ones = jnp.ones((TILE, tokens), LOW)
    column = lax.broadcasted_iota(jnp.int32, (tokens, tokens), 1)
    gain_part_ref[...] = jnp.zeros(gain_part_ref.shape, WIDE)
    grad_norms = [
        (grad_ref[0, :, head_cols(head)].astype(WIDE) * gain_ref[:, head_cols(head)]).T
        for head in heads
    ]
    for head in heads:
        cols = head_cols(head)
        grad_norm_ref[:, cols] = grad_norms[head]
        picks = pick_matrix(offsets_ref, head, tokens, top_step, 1)
        place_ref[:, cols] = picks
    for head in range(OWNED):
        cols = head_cols(head)
        mid_offset, top_offset = offsets_ref[0, head], offsets_ref[1, head]
        seen = jnp.maximum(
            hit_row(top_offset, top_step, tokens), hit_row(mid_offset, R1, tokens)
        )
        attn = out_ref[:, cols].astype(WIDE)
        normed = attn * lax.rsqrt(column_mean(attn * attn) + EPS)
        product = grad_norms[head] * normed * (1.0 - seen)
        gain_part_ref[:, cols] = gain_row_of(ones, product) / gain_ref[:, cols]
        both = mid_offset % top_step == top_offset
        kept = jnp.where(column < top_rows, 1.0, jnp.where(both, 0.0, 1.0)).astype(LOW)
        picks = pick_matrix(offsets_ref, head, tokens, top_step, 1)
        place_ref[:, head_cols(len(heads) + head)] = picks * kept


def owner_kernel(top_step, offsets_ref, q_ref, gain_ref, out_ref, grad_norm_ref, *refs):
    stats_ref, gain_base_ref = refs[:2]
    payload_refs, refs = nearest_first(refs[2 : 2 + SPAN]), refs[2 + SPAN :]
    normed_ref, grad_low_ref, score_grad_ref, kept_ref = refs[:4]
    return_refs = refs[4:]
    tokens = q_ref.shape[1]
    heads = q_ref.shape[2] // HEAD_DIM
    top_rows, mid_rows = picked_counts(tokens, top_step)
    picked = top_rows + mid_rows
    top_all, mid_all = SPAN * top_rows, SPAN * mid_rows
    queries = top_all + mid_all
    score_scale = 1.0 / math.sqrt(HEAD_DIM)
    me = lax.axis_index("ctx")
    ones = jnp.ones((TILE, tokens), LOW)

    def by_level(block):
        start = block * picked
        return jnp.concatenate(
            [ref[start : start + top_rows] for ref in payload_refs]
            + [ref[start + top_rows : start + picked] for ref in payload_refs],
            0,
        )

    def per_level(top_row, mid_row):
        return jnp.concatenate(
            [
                jnp.broadcast_to(top_row, (top_all, queries)),
                jnp.broadcast_to(mid_row, (mid_all, queries)),
            ],
            0,
        )

    q_rows, k_rows, v_rows, grad_rows, base_rows = [by_level(block) for block in range(5)]
    stat_start = 7 * picked
    logs = [
        joined_row(ref[stat_start : stat_start + STAT_TILES].astype(WIDE), 0)
        for ref in payload_refs
    ]
    base_top_log = sum(
        rolled(lane_window(log, 0, top_rows), slot * top_rows) for slot, log in enumerate(logs)
    )
    base_mid_log = sum(
        rolled(lane_window(log, top_rows, mid_rows), slot * mid_rows - top_rows)
        for slot, log in enumerate(logs)
    )
    base_log = jnp.concatenate([base_top_log, base_mid_log[:, :mid_all]], 1)
    gain_row = jnp.zeros((1, HEAD_DIM), WIDE)
    for head in range(OWNED):
        gain_row = gain_row + jnp.where(me == head, 1.0, 0.0) * gain_ref[:, head_cols(head)]
    mid_offset, top_offset = offsets_ref[0, me], offsets_ref[1, me]
    both = mid_offset % top_step == top_offset
    lane = lax.broadcasted_iota(jnp.int32, (1, queries), 1)
    is_top = jnp.where(lane < top_all, 1.0, 0.0)
    top_in_mid = jnp.where(((lane % top_rows) * top_step + top_offset) % R1 == mid_offset, 1.0, 0.0)
    both_flag = jnp.where(both, 1.0, 0.0)
    sees_top = is_top + (1.0 - is_top) * both_flag
    sees_mid = is_top * top_in_mid + (1.0 - is_top)
    bias = per_level((1.0 - sees_top) * NEVER, (1.0 - sees_mid) * NEVER)
    last = heads - 1
    cols = head_cols(last)
    peers = payload_refs[1:]
    q_last = q_ref[0, :, cols]
    k_peers = jnp.concatenate([ref[5 * picked : 6 * picked] for ref in peers], 0)
    v_peers = jnp.concatenate([ref[6 * picked : 7 * picked] for ref in peers], 0)
    last_biases = [
        jnp.broadcast_to((1.0 - hit_row(offsets_ref[level, last], step, tokens)) * NEVER, shape)
        for level, step, shape in (
            (1, top_step, (top_rows, tokens)),
            (0, R1, (mid_rows, tokens)),
        )
    ]
    scores = contract(k_rows, q_rows, 1, 1) * score_scale + bias
    scores_last = contract(k_peers, q_last, 1, 1) * score_scale + jnp.concatenate(
        last_biases * PEERS, 0
    )
    base_attn = base_rows.astype(WIDE).T
    grad_norm = (grad_rows.astype(WIDE) * gain_row).T
    top_score = jnp.maximum(base_log, jnp.max(scores, axis=0, keepdims=True))
    base_top, base_total = stats_ref[last : last + 1, :], stats_ref[TILE + last : TILE + last + 1, :]
    top_last = jnp.maximum(base_top, jnp.max(scores_last, axis=0, keepdims=True))
    expo = jnp.exp(scores - top_score)
    expo_last = jnp.exp(scores_last - top_last)
    factor = jnp.exp(base_log - top_score)
    factor_last = jnp.exp(base_top - top_last)
    total = factor + jnp.sum(expo, axis=0, keepdims=True)
    total_last = factor_last * base_total + jnp.sum(expo_last, axis=0, keepdims=True)
    inv_total, inv_last = 1.0 / total, 1.0 / total_last
    soft, soft_last = expo * inv_total, expo_last * inv_last
    soft_low, soft_last_low = soft.astype(LOW), soft_last.astype(LOW)
    factor_last = factor_last * inv_last
    attn = (factor * inv_total) * base_attn + contract(v_rows, soft_low, 0, 0)
    attn_last = factor_last * out_ref[:, cols].astype(WIDE) + contract(v_peers, soft_last_low, 0, 0)
    _, product, grad_low, inner = norm_backward(attn, grad_norm)
    normed_last, product_last, grad_last_low, inner_last = norm_backward(
        attn_last, grad_norm_ref[:, cols]
    )
    spans = (slice(0, top_all), slice(top_all, queries))
    prob_grads = [contract(v_rows[span], grad_low[:, span], 1, 0) for span in spans]
    prob_grad_last = contract(v_peers, grad_last_low, 1, 0)
    score_grads = [
        (soft[span, span] * (prob_grad - inner[:, span]) * score_scale).astype(LOW)
        for span, prob_grad in zip(spans, prob_grads)
    ]
    score_grad_last = (soft_last * (prob_grad_last - inner_last) * score_scale).astype(LOW)
    dks = [
        contract(score_grad, q_rows[span], 1, 0).astype(LOW)
        for span, score_grad in zip(spans, score_grads)
    ]
    dk_last = contract(score_grad_last, q_last, 1, 0).astype(LOW)
    dvs = [
        contract(soft_low[span, span], grad_low[:, span], 1, 1).astype(LOW) for span in spans
    ]
    dv_last = contract(soft_last_low, grad_last_low, 1, 1).astype(LOW)
    dqs = [
        contract(score_grad, k_rows[span], 0, 0).astype(LOW)
        for span, score_grad in zip(spans, score_grads)
    ]
    attn_rows = attn.T.astype(LOW)
    attn_parts = [attn_rows[span] for span in spans]
    log_total = top_score + jnp.log(total)
    padding = jnp.zeros((1, top_all - mid_all), WIDE)
    once = is_top + (1.0 - is_top) * (1.0 - both_flag)
    ones_all = jnp.ones((TILE, queries), LOW)
    own_gain = gain_row_of(ones_all, product * once) / gain_row
    gain_rows = [
        gain_base_ref[:, head_cols(head)] + jnp.where(me == head, 1.0, 0.0) * own_gain
        for head in range(OWNED)
    ]
    gain_rows.append(gain_row_of(ones, product_last) / gain_ref[:, cols])
    gain_high, gain_rest = [
        rows.astype(WIDE) for rows in gain_pieces(jnp.concatenate(gain_rows, 0))
    ]
    top_log, mid_log = log_total[:, :top_all], jnp.concatenate(
        [log_total[:, top_all:], padding], 1
    )
    empty = jnp.zeros((PIECES, HEAD_DIM), WIDE)
    for distance, return_ref in enumerate(return_refs):
        blocks = []
        for top_block, mid_block in (dqs, dks, dvs, attn_parts):
            blocks.append(top_block[distance * top_rows : (distance + 1) * top_rows])
            blocks.append(mid_block[distance * mid_rows : (distance + 1) * mid_rows])
        start = max(distance - 1, 0) * picked
        blocks += [dk_last[start : start + picked], dv_last[start : start + picked]]
        log_row = lane_window(rolled(top_log, -distance * top_rows), 0, top_rows) + lane_window(
            rolled(mid_log, top_rows - distance * mid_rows), top_rows, mid_rows
        )
        log_rows = [piece_rows(log_row, gain_high), empty, gain_rest]
        blocks.append(jnp.concatenate(log_rows, 0).astype(LOW))
        return_ref[...] = jnp.concatenate(blocks, 0)
    normed_ref[...] = normed_last
    grad_low_ref[...] = grad_last_low
    score_grad_ref[...] = score_grad_last
    kept_ref[0:1, :] = factor_last
    kept_ref[1:2, :] = inner_last


def last_head_kernel(top_step, q_ref, k_ref, v_ref, gain_ref, expo_ref, *refs):
    normed_ref, grad_low_ref, peer_score_grad_ref, kept_ref, *peers = refs[: 4 + PEERS]
    peers = nearest_first([None, *peers])[1:]
    attended_ref, dq_ref, dk_ref, dv_ref = refs[4 + PEERS :]
    picked = sum(picked_counts(q_ref.shape[1], top_step))
    score_scale = 1.0 / math.sqrt(HEAD_DIM)
    cols = head_cols(q_ref.shape[2] // HEAD_DIM - 1)
    attended_ref[...] = (normed_ref[...].T * gain_ref[:, cols]).astype(LOW)
    k_peers = jnp.concatenate([ref[5 * picked : 6 * picked] for ref in peers], 0)
    grad_low = grad_low_ref[...]
    soft = expo_ref[:, cols].astype(WIDE) * kept_ref[0:1, :]
    prob_grad = contract(v_ref[0, :, cols], grad_low, 1, 0)
    score_grad = (soft * (prob_grad - kept_ref[1:2, :]) * score_scale).astype(LOW)
    dk_ref[...] = contract(score_grad, q_ref[0, :, cols], 1, 0)
    dv_ref[...] = contract(soft.astype(LOW), grad_low, 1, 1)
    dq_ref[...] = (
        contract(score_grad, k_ref[0, :, cols], 0, 0)
        + contract(peer_score_grad_ref[...], k_peers, 0, 0)
    ).astype(LOW)


def gain_kernel(picked, *refs):
    return_refs, gain_ref = nearest_first(refs[:SPAN]), refs[SPAN]
    tiles = [ref[6 * picked : 6 * picked + STAT_TILES].astype(WIDE) for ref in return_refs]
    parts = [tile[PIECES:TILE] + tile[TILE + PIECES :] for tile in tiles]
    total = (parts[0] + parts[1]) + (parts[2] + parts[3])
    for head in range(gain_ref.shape[1] // HEAD_DIM):
        gain_ref[:, head_cols(head)] = total[head : head + 1]


def mix_kernel(top_step, offsets_ref, v_ref, gain_ref, expo_ref, out_ref, *refs):
    grad_norm_ref, stats_ref, place_ref = refs[:3]
    return_refs, refs = nearest_first(refs[3 : 3 + SPAN]), refs[3 + SPAN :]
    attended_ref, grad_low_ref, soft_ref, score_grad_ref, placed_ref = refs
    tokens, width = v_ref.shape[1:]
    count = width // HEAD_DIM
    picked = sum(picked_counts(tokens, top_step))
    score_scale = 1.0 / math.sqrt(HEAD_DIM)
    me = lax.axis_index("ctx")
    heads = range(OWNED)
    every = [head_cols(head) for head in heads]
    for distance, return_ref in enumerate(return_refs):
        placed_ref[me ^ distance] = return_ref[...]
    once = [place_ref[:, head_cols(count + head)] for head in heads]
    attn_parts = [
        contract(placed_ref[head, 3 * picked : 4 * picked], once[head][:, :picked], 0, 1)
        for head in heads
    ]
    log_parts = [
        contract(placed_ref[head, 6 * picked : 6 * picked + STAT_TILES], once[head], 1, 1)
        for head in heads
    ]
    factors, normeds, grad_lows, inners = [], [], [], []
    for head in heads:
        top_hit = hit_row(offsets_ref[1, head], top_step, tokens)
        mid_hit = hit_row(offsets_ref[0, head], R1, tokens)
        seen = jnp.maximum(top_hit, mid_hit) > 0.5
        top_score, total = stats_ref[head : head + 1, :], stats_ref[TILE + head : TILE + head + 1, :]
        log_total = jnp.where(seen, joined_row(log_parts[head], 0), top_score + jnp.log(total))
        factors.append(jnp.exp(top_score - log_total))
        attn = jnp.where(seen, attn_parts[head], out_ref[:, every[head]].astype(WIDE))
        normed, _, grad_low, inner = norm_backward(attn, grad_norm_ref[:, every[head]])
        normeds.append(normed)
        grad_lows.append(grad_low)
        inners.append(inner)
    prob_grads = [contract(v_ref[0, :, every[head]], grad_lows[head], 1, 0) for head in heads]
    softs = [expo_ref[:, every[head]].astype(WIDE) * factors[head] for head in heads]
    for head in heads:
        cols = every[head]
        grad_low_ref[:, cols] = grad_lows[head]
        soft_ref[:, cols] = softs[head].astype(LOW)
        score_grad_ref[:, cols] = (
            softs[head] * (prob_grads[head] - inners[head]) * score_scale
        ).astype(LOW)
        attended_ref[:, cols] = (normeds[head].T * gain_ref[:, cols]).astype(LOW)


def finish_kernel(top_step, *refs):
    gain_refs, (q_ref, k_ref, place_ref), refs = refs[:2], refs[2:5], refs[5:]
    mixed_refs, (last_attended_ref, last_dq_ref, last_dk_ref, last_dv_ref) = refs[:5], refs[5:9]
    return_refs, refs = nearest_first(refs[9 : 9 + SPAN]), refs[9 + SPAN :]
    mixed_ref, grad_low_ref, soft_ref, score_grad_ref, returned_ref = mixed_refs
    attended_ref, dq_ref, dk_ref, dv_ref, gain_out_ref = refs
    tokens, width = q_ref.shape[1:]
    picked = sum(picked_counts(tokens, top_step))
    heads = range(OWNED)
    every = [head_cols(head) for head in heads]
    gain_out_ref[...] = (gain_refs[0][...] + gain_refs[1][...]).reshape(gain_out_ref.shape)
    score_grads = [score_grad_ref[:, cols] for cols in every]
    dqs = [contract(score_grads[head], k_ref[0, :, every[head]], 0, 0) for head in heads]
    placed = [
        contract(
            place_ref[:, pl.ds(head * HEAD_DIM, picked)],
            jnp.concatenate(
                [returned_ref[head, block * picked : (block + 1) * picked] for block in range(3)], 1
            ),
            1,
            0,
        )
        for head in heads
    ]
    dks = [contract(score_grads[head], q_ref[0, :, every[head]], 1, 0) for head in heads]
    dvs = [contract(soft_ref[:, cols], grad_low_ref[:, cols], 1, 1) for cols in every]
    last = width // HEAD_DIM - 1
    total = sum(ref[4 * picked : 6 * picked].astype(WIDE) for ref in return_refs[1:]).astype(LOW)
    rows = contract(
        place_ref[:, pl.ds(last * HEAD_DIM, picked)],
        jnp.concatenate([total[:picked], total[picked:]], 1),
        1,
        0,
    )
    for head in heads:
        cols = every[head]
        attended_ref[0, :, cols] = mixed_ref[:, cols]
        for which, (block, out_block_ref) in enumerate(
            ((dqs[head], dq_ref), (dks[head], dk_ref), (dvs[head], dv_ref))
        ):
            part = placed[head][:, which * HEAD_DIM : (which + 1) * HEAD_DIM]
            out_block_ref[0, :, cols] = (block + part).astype(LOW)
    cols = head_cols(last)
    attended_ref[0, :, cols] = last_attended_ref[...]
    dq_ref[0, :, cols] = last_dq_ref[...]
    dk_ref[0, :, cols] = (last_dk_ref[...] + rows[:, :HEAD_DIM]).astype(LOW)
    dv_ref[0, :, cols] = (last_dv_ref[...] + rows[:, HEAD_DIM:]).astype(LOW)


def across(block, axis, distance):
    route = [(place, place ^ distance) for place in range(lax.axis_size(axis))]
    return lax.ppermute(block, axis, route)


def to_peers(blocks):
    return [across(blocks[distance - 1], "ctx", distance) for distance in START_ORDER]


def call(kernel, name, operands, results, microseconds, vmem=PLAIN_VMEM, scratch=()):
    return pl.pallas_call(
        kernel,
        out_shape=results,
        in_specs=[SMEM_SPEC if block.dtype == jnp.int32 else VMEM_SPEC for block in operands],
        out_specs=[VMEM_SPEC] * len(results),
        scratch_shapes=scratch,
        compiler_params=pltpu.CompilerParams(vmem_limit_bytes=vmem),
        cost_estimate=pl.CostEstimate(
            flops=int(microseconds * 10**9), bytes_accessed=0, transcendentals=0
        ),
        name=name,
    )(*operands)


def one_segment_shards(queries, keys, values, grad_y, out_gain, offsets):
    tokens, width = queries.shape[1:]
    heads = width // HEAD_DIM
    top_step = lax.axis_size("ctx")
    picked = sum(picked_counts(tokens, top_step))
    shape = jax.ShapeDtypeStruct
    row_block = shape((1, tokens, width), LOW)
    low_block, wide_block = shape((tokens, width), LOW), shape((tokens, width), WIDE)
    low_head, wide_head = shape((tokens, HEAD_DIM), LOW), shape((tokens, HEAD_DIM), WIDE)
    gain_block = shape((1, width), WIDE)
    stats_block = shape((2 * TILE, tokens), WIDE)
    payload = shape((7 * picked + STAT_TILES, HEAD_DIM), LOW)
    answer = shape((6 * picked + STAT_TILES, HEAD_DIM), LOW)
    bind = functools.partial
    gain_row = out_gain.reshape(1, width)
    own, *sent, expo, base_out, stats = call(
        bind(pack_kernel, top_step),
        "pack",
        (offsets, queries, keys, values, grad_y),
        [payload] * SPAN + [low_block, low_block, stats_block],
        1,
        vmem=PACK_VMEM,
        scratch=[pltpu.VMEM((OWNED, *payload.shape), LOW)],
    )
    received = to_peers(sent)
    grad_norm, gain_base, place = call(
        bind(prepare_kernel, top_step),
        "prepare",
        (offsets, grad_y, gain_row, base_out),
        [wide_block, gain_block, shape((tokens, 2 * width), LOW)],
        2,
    )
    normed, grad_low, score_grad, kept, own_answer, *answers = call(
        bind(owner_kernel, top_step),
        "owner",
        (offsets, queries, gain_row, base_out, grad_norm, stats, gain_base, own, *received),
        [
            wide_head,
            low_head,
            shape((PEERS * picked, HEAD_DIM), LOW),
            shape((TILE, tokens), WIDE),
        ]
        + [answer] * SPAN,
        3,
    )
    returned = to_peers(answers)
    last_results = call(
        bind(last_head_kernel, top_step),
        "last_head",
        (queries, keys, values, gain_row, expo, normed, grad_low, score_grad, kept, *received),
        [low_head, low_head, wide_head, wide_head],
        20,
    )
    (gain_sum,) = call(bind(gain_kernel, picked), "gain", (own_answer, *returned), [gain_block], 1)
    gain_rest = across(gain_sum, "dp", 1)
    mixed_block = shape((tokens, OWNED * HEAD_DIM), LOW)
    mixed = call(
        bind(mix_kernel, top_step),
        "mix",
        (
            offsets,
            values,
            gain_row,
            expo,
            base_out,
            grad_norm,
            stats,
            place,
            own_answer,
            *returned,
        ),
        [mixed_block] * 4 + [shape((OWNED, *answer.shape), LOW)],
        20,
    )
    attended, query_grad, key_grad, value_grad, gain_grad = call(
        bind(finish_kernel, top_step),
        "finish",
        (
            gain_sum,
            gain_rest,
            queries,
            keys,
            place,
            *mixed,
            *last_results,
            own_answer,
            *returned,
        ),
        [row_block] * 4 + [shape((width,), WIDE)],
        1,
    )
    return attended, query_grad, key_grad, value_grad, gain_grad


def shards(*operands):
    one_segment = lax.axis_size("ctx") == SPAN
    if one_segment and operands[0].shape[2] == (OWNED + 1) * HEAD_DIM:
        return one_segment_shards(*operands)
    return general_shards(*operands)


def solution(mesh):
    in_specs = (
        P("dp", "ctx", "head"),
        P("dp", "ctx", "head"),
        P("dp", "ctx", "head"),
        P("dp", "ctx", "head"),
        P("head"),
        P(None, "head"),
    )
    out_specs = (
        P("dp", "ctx", "head"),
        P("dp", "ctx", "head"),
        P("dp", "ctx", "head"),
        P("dp", "ctx", "head"),
        P("head"),
    )
    return jax.shard_map(shards, mesh=mesh, in_specs=in_specs, out_specs=out_specs, check_vma=False)
```

```python
import functools
import math

import jax
import jax.numpy as jnp
from jax import lax
from jax.experimental import pallas as pl
from jax.experimental.pallas import tpu as pltpu
from jax.sharding import PartitionSpec as P

HEAD_DIM = 128
SPAN = 4
R1 = 8


EPS = 1e-06


def swapped(block, axis, bit):
    count = lax.axis_size(axis)
    route = []
    for low in range(count):
        high = low | 1 << bit
        if high != low and high < count:
            route += [(low, high), (high, low)]
    return lax.ppermute(block, axis, route)


def pick_rows(source_rows, dilation, shifts):
    row_count, head_count, head_width = source_rows.shape
    grouped = source_rows.reshape(row_count // dilation, dilation, head_count, head_width)
    hit_mask = jnp.arange(dilation, dtype=jnp.int32).reshape(1, dilation, 1, 1) == shifts.reshape(
        1, 1, head_count, 1
    )
    chosen = jnp.where(hit_mask, grouped, jnp.zeros((), source_rows.dtype))
    return jnp.sum(chosen, axis=1, dtype=source_rows.dtype)


def place_rows(row_values, dilation, shifts):
    row_count, head_count, head_width = row_values.shape
    hit_mask = jnp.arange(dilation, dtype=jnp.int32).reshape(1, dilation, 1, 1) == shifts.reshape(
        1, 1, head_count, 1
    )
    spread = jnp.where(hit_mask, row_values[:, None], jnp.zeros((), row_values.dtype))
    return spread.reshape(row_count * dilation, head_count, head_width)


def level_scores(q_rows, k_rows):
    score_scale = 1.0 / math.sqrt(q_rows.shape[-1])
    return (
        jnp.einsum("qhe,khe->hqk", q_rows, k_rows, preferred_element_type=jnp.float32) * score_scale
    )


def attend(q_rows, k_rows, v_rows):
    scores = level_scores(q_rows, k_rows)
    row_max = jnp.max(scores, axis=-1, keepdims=True)
    log_total = row_max[..., 0] + jnp.log(jnp.sum(jnp.exp(scores - row_max), axis=-1))
    soft_rows = jnp.exp(scores - log_total[..., None]).astype(jnp.bfloat16)
    level_out = jnp.einsum("hqk,khe->qhe", soft_rows, v_rows, preferred_element_type=jnp.float32)
    return (level_out, log_total.T)


def score_grads(q_rows, k_rows, v_rows, log_total, grad_low, row_shift):
    score_scale = 1.0 / math.sqrt(q_rows.shape[-1])
    scores = level_scores(q_rows, k_rows)
    exact_soft = jnp.exp(scores - log_total.T[..., None])
    prob_grad = jnp.einsum("qhe,khe->hqk", grad_low, v_rows, preferred_element_type=jnp.float32)
    score_grad = (exact_soft * (prob_grad + row_shift.T[..., None]) * score_scale).astype(
        jnp.bfloat16
    )
    return (score_grad, exact_soft.astype(jnp.bfloat16))


def key_parts(score_grad, soft_low, q_rows, grad_low):
    k_part = jnp.einsum("hqk,qhe->khe", score_grad, q_rows, preferred_element_type=jnp.float32)
    v_part = jnp.einsum("hqk,qhe->khe", soft_low, grad_low, preferred_element_type=jnp.float32)
    return (k_part, v_part)


def query_part(score_grad, k_rows):
    return jnp.einsum("hqk,khe->qhe", score_grad, k_rows, preferred_element_type=jnp.float32)


def general_shards(queries, keys, values, grad_y, out_gain, offsets):
    tokens = queries.shape[1]
    flat_width = queries.shape[2]
    head_count = flat_width // HEAD_DIM
    row_shape = (tokens, head_count, HEAD_DIM)
    q_own = queries[0].reshape(row_shape)
    k_own = keys[0].reshape(row_shape)
    v_own = values[0].reshape(row_shape)
    ctx_size = lax.axis_size("ctx")
    span_bits = SPAN.bit_length() - 1
    my_place = lax.axis_index("ctx")
    mid_shift = offsets[0]
    top_shift = offsets[1]
    positions = jnp.arange(tokens, dtype=jnp.int32)
    mid_hit = (positions % R1)[:, None] == mid_shift[None, :]
    top_hit = (positions % ctx_size)[:, None] == top_shift[None, :]
    mid_q = pick_rows(q_own, R1, mid_shift)
    mid_k = pick_rows(k_own, R1, mid_shift)
    mid_v = pick_rows(v_own, R1, mid_shift)
    top_q = pick_rows(q_own, ctx_size, top_shift)
    top_k = pick_rows(k_own, ctx_size, top_shift)
    top_v = pick_rows(v_own, ctx_size, top_shift)
    mid_keys = mid_k.reshape(-1, flat_width)
    mid_vals = mid_v.reshape(-1, flat_width)
    top_keys = top_k.reshape(-1, flat_width)
    top_vals = top_v.reshape(-1, flat_width)

    def append_peer(mine, received, level_bit):
        upper_side = my_place >> level_bit & 1 == 1
        return jnp.where(
            upper_side, jnp.concatenate([received, mine], 0), jnp.concatenate([mine, received], 0)
        )

    for level_bit in range(span_bits):
        received = swapped((mid_keys, mid_vals), "ctx", level_bit)
        mid_keys = append_peer(mid_keys, received[0], level_bit)
        mid_vals = append_peer(mid_vals, received[1], level_bit)
    top_keys, top_vals = (
        lax.all_gather(top_keys, "ctx", axis=0, tiled=True),
        lax.all_gather(top_vals, "ctx", axis=0, tiled=True),
    )
    mid_keys = mid_keys.reshape(-1, head_count, HEAD_DIM)
    mid_vals = mid_vals.reshape(-1, head_count, HEAD_DIM)
    top_keys = top_keys.reshape(-1, head_count, HEAD_DIM)
    top_vals = top_vals.reshape(-1, head_count, HEAD_DIM)
    base_out, base_total = attend(q_own, k_own, v_own)
    mid_out, mid_total = attend(mid_q, mid_keys, mid_vals)
    top_out, top_total = attend(top_q, top_keys, top_vals)
    mid_full = place_rows(mid_total[..., None], R1, mid_shift)[..., 0]
    top_full = place_rows(top_total[..., None], ctx_size, top_shift)[..., 0]
    row_max = jnp.maximum(base_total, jnp.where(mid_hit, mid_full, base_total))
    row_max = jnp.maximum(row_max, jnp.where(top_hit, top_full, base_total))
    base_expo = jnp.exp(base_total - row_max)
    mid_expo = jnp.where(mid_hit, jnp.exp(mid_full - row_max), 0.0)
    top_expo = jnp.where(top_hit, jnp.exp(top_full - row_max), 0.0)
    denom = base_expo + mid_expo + top_expo
    base_share = base_expo / denom
    mid_share = mid_expo / denom
    top_share = top_expo / denom
    attn = (
        base_share[..., None] * base_out
        + mid_share[..., None] * place_rows(mid_out, R1, mid_shift)
        + top_share[..., None] * place_rows(top_out, ctx_size, top_shift)
    )
    inv_rms = lax.rsqrt(jnp.mean(attn * attn, axis=-1, keepdims=True) + EPS)
    normed = attn * inv_rms
    gain_rows = out_gain.reshape(head_count, HEAD_DIM)
    attended = (normed * gain_rows).astype(jnp.bfloat16).reshape(1, tokens, flat_width)
    grad_full = grad_y[0].reshape(row_shape).astype(jnp.float32)
    gain_part = jnp.sum(grad_full * normed, axis=0).reshape(flat_width)
    gain_grad = lax.psum(gain_part, ("dp", "ctx"))
    grad_norm = grad_full * gain_rows
    grad_attn = inv_rms * (
        grad_norm - normed * jnp.mean(grad_norm * normed, axis=-1, keepdims=True)
    )
    inner = jnp.sum(grad_attn * attn, axis=-1)
    base_low = (base_share[..., None] * grad_attn).astype(jnp.bfloat16)
    base_shift = -(base_share * inner)
    base_grad, base_soft = score_grads(q_own, k_own, v_own, base_total, base_low, base_shift)
    base_dq = query_part(base_grad, k_own)
    base_dk, base_dv = key_parts(base_grad, base_soft, q_own, base_low)
    mid_sel = pick_rows(mid_share[..., None], R1, mid_shift)[..., 0]
    mid_low = (mid_sel[..., None] * pick_rows(grad_attn, R1, mid_shift)).astype(jnp.bfloat16)
    mid_row_shift = -(mid_sel * pick_rows(inner[..., None], R1, mid_shift)[..., 0])
    mid_grad, mid_soft = score_grads(mid_q, mid_keys, mid_vals, mid_total, mid_low, mid_row_shift)
    mid_dq = query_part(mid_grad, mid_keys)
    mid_dk, mid_dv = key_parts(mid_grad, mid_soft, mid_q, mid_low)
    mid_dk = mid_dk.reshape(-1, flat_width)
    mid_dv = mid_dv.reshape(-1, flat_width)
    for level_bit in reversed(range(span_bits)):
        half_rows = mid_dk.shape[0] // 2
        upper_side = my_place >> level_bit & 1 == 1
        keep_k = jnp.where(upper_side, mid_dk[half_rows:], mid_dk[:half_rows])
        keep_v = jnp.where(upper_side, mid_dv[half_rows:], mid_dv[:half_rows])
        send_k = jnp.where(upper_side, mid_dk[:half_rows], mid_dk[half_rows:])
        send_v = jnp.where(upper_side, mid_dv[:half_rows], mid_dv[half_rows:])
        received = (
            swapped(send_k.astype(jnp.bfloat16), "ctx", level_bit).astype(send_k.dtype),
            swapped(send_v.astype(jnp.bfloat16), "ctx", level_bit).astype(send_v.dtype),
        )
        mid_dk = keep_k + received[0]
        mid_dv = keep_v + received[1]
    mid_dk = mid_dk.reshape(-1, head_count, HEAD_DIM)
    mid_dv = mid_dv.reshape(-1, head_count, HEAD_DIM)
    top_sel = pick_rows(top_share[..., None], ctx_size, top_shift)[..., 0]
    top_low = (top_sel[..., None] * pick_rows(grad_attn, ctx_size, top_shift)).astype(jnp.bfloat16)
    top_row_shift = -(top_sel * pick_rows(inner[..., None], ctx_size, top_shift)[..., 0])
    top_grad, top_soft = score_grads(top_q, top_keys, top_vals, top_total, top_low, top_row_shift)
    top_dq = query_part(top_grad, top_keys)
    gathered_dk, gathered_dv = key_parts(top_grad, top_soft, top_q, top_low)
    summed = (
        lax.psum_scatter(
            gathered_dk.reshape(-1, flat_width), "ctx", scatter_dimension=0, tiled=True
        ),
        lax.psum_scatter(
            gathered_dv.reshape(-1, flat_width), "ctx", scatter_dimension=0, tiled=True
        ),
    )
    top_dk = summed[0].reshape(-1, head_count, HEAD_DIM)
    top_dv = summed[1].reshape(-1, head_count, HEAD_DIM)
    query_grad = (
        base_dq + place_rows(mid_dq, R1, mid_shift) + place_rows(top_dq, ctx_size, top_shift)
    )
    key_grad = base_dk + place_rows(mid_dk, R1, mid_shift) + place_rows(top_dk, ctx_size, top_shift)
    value_grad = (
        base_dv + place_rows(mid_dv, R1, mid_shift) + place_rows(top_dv, ctx_size, top_shift)
    )
    out_shape = (1, tokens, flat_width)
    return (
        attended,
        query_grad.astype(jnp.bfloat16).reshape(out_shape),
        key_grad.astype(jnp.bfloat16).reshape(out_shape),
        value_grad.astype(jnp.bfloat16).reshape(out_shape),
        gain_grad,
    )


VMEM_SPEC = pl.BlockSpec(memory_space=pltpu.VMEM)
SMEM_SPEC = pl.BlockSpec(memory_space=pltpu.SMEM)
PEERS = SPAN - 1
OWNED = SPAN
TILE = 8
STAT_TILES = 2 * TILE
PIECES = 3
NEVER = -1e30
LOW = jnp.bfloat16
WIDE = jnp.float32
PACK_VMEM = 65408 * 1024
PLAIN_VMEM = 16 * 1024 * 1024


def contract(left, right, left_dim, right_dim):
    return lax.dot_general(
        left, right, (((left_dim,), (right_dim,)), ((), ())), preferred_element_type=WIDE
    )


def head_cols(head):
    return pl.ds(head * HEAD_DIM, HEAD_DIM)


def picked_counts(tokens, top_step):
    return tokens // top_step, tokens // R1


def pick_matrix(offsets_ref, head, tokens, top_step, picked_axis):
    top_rows, _ = picked_counts(tokens, top_step)
    row = lax.broadcasted_iota(jnp.int32, (tokens, tokens), picked_axis)
    position = lax.broadcasted_iota(jnp.int32, (tokens, tokens), 1 - picked_axis)
    wanted = jnp.where(
        row < top_rows,
        row * top_step + offsets_ref[1, head],
        (row - top_rows) * R1 + offsets_ref[0, head],
    )
    return jnp.where(position == wanted, 1.0, 0.0).astype(LOW)


def rolled(row, shift):
    return pltpu.roll(row, shift % row.shape[1], 1)


def lane_window(row, start, count):
    lane = lax.broadcasted_iota(jnp.int32, row.shape, 1)
    return jnp.where((lane >= start) & (lane < start + count), row, 0.0)


def hit_row(offset, step, tokens):
    position = lax.broadcasted_iota(jnp.int32, (1, tokens), 1)
    return jnp.where(position % step == offset, 1.0, 0.0)


def piece_rows(row, others=None):
    pieces = []
    for _ in range(PIECES):
        piece = row.astype(LOW).astype(WIDE)
        pieces.append(piece)
        row = row - piece
    if others is None:
        others = jnp.zeros((TILE - PIECES, row.shape[1]), WIDE)
    return jnp.concatenate(pieces + [others], 0)


def gain_pieces(rows):
    high = rows.astype(LOW)
    return high, (rows - high.astype(WIDE)).astype(LOW)


def joined_row(rows, first):
    total = rows[first : first + 1]
    for piece in range(1, PIECES):
        total = total + rows[first + piece : first + piece + 1]
    return total


def gain_row_of(ones, product):
    high, rest = gain_pieces(product)
    return (contract(ones, high, 1, 1) + contract(ones, rest, 1, 1))[:1]


def column_mean(block):
    return jnp.mean(block, axis=0, keepdims=True)


def norm_backward(attn, grad_norm):
    inv_rms = lax.rsqrt(column_mean(attn * attn) + EPS)
    normed = attn * inv_rms
    product = grad_norm * normed
    grad_attn = inv_rms * (grad_norm - normed * column_mean(product))
    inner = jnp.sum(grad_attn * attn, axis=0, keepdims=True)
    return normed, product, grad_attn.astype(LOW), inner


def last_owner_of(dp_place):
    return 1 + dp_place % 2


def last_owner():
    return last_owner_of(lax.axis_index("dp"))


def pack_kernel(top_step, offsets_ref, q_ref, k_ref, v_ref, grad_ref, *refs):
    long_refs, short_refs, refs = refs[:SPAN], refs[SPAN : SPAN + 2], refs[SPAN + 2 :]
    expo_ref, out_ref, stats_ref, held_ref = refs
    tokens, width = q_ref.shape[1:]
    heads = range(width // HEAD_DIM)
    me = lax.axis_index("ctx")
    picked = sum(picked_counts(tokens, top_step))
    rows = held_ref.shape[1]
    score_scale = 1.0 / math.sqrt(HEAD_DIM)
    q_rows, k_rows, v_rows, grad_rows = [
        [ref[0, :, head_cols(head)] for head in heads] for ref in (q_ref, k_ref, v_ref, grad_ref)
    ]
    picks = [pick_matrix(offsets_ref, head, tokens, top_step, 0) for head in heads]
    scores = [contract(k_rows[head], q_rows[head], 1, 1) * score_scale for head in heads]
    moved = [
        contract(
            picks[head][:picked],
            jnp.concatenate([q_rows[head], k_rows[head], v_rows[head], grad_rows[head]], 1),
            1,
            0,
        ).astype(LOW)
        for head in heads
    ]
    top_scores = [jnp.max(block, axis=0, keepdims=True) for block in scores]
    expos = [jnp.exp(scores[head] - top_scores[head]) for head in heads]
    expo_lows = [expo.astype(LOW) for expo in expos]
    outs = [contract(v_rows[head], expo_lows[head], 0, 0) for head in heads]
    totals = [jnp.sum(expo, axis=0, keepdims=True) for expo in expos]
    for head in heads:
        expo_ref[:, head_cols(head)] = expo_lows[head]
        stats_ref[head : head + 1, :] = top_scores[head]
        stats_ref[TILE + head : TILE + head + 1, :] = totals[head]
    outs = [(outs[head] * (1.0 / totals[head])).astype(LOW) for head in heads]
    picked_outs = [
        contract(picks[head][:picked], outs[head], 1, 1).astype(LOW) for head in heads
    ]
    for head in heads:
        out_ref[:, head_cols(head)] = outs[head]
    for head in heads:
        pieces = piece_rows(top_scores[head] + jnp.log(totals[head])).astype(LOW)
        stat_rows = contract(pieces, picks[head], 1, 1)
        blocks = [moved[head][:, block * HEAD_DIM : (block + 1) * HEAD_DIM] for block in range(4)]
        blocks.append(picked_outs[head])
        blocks.append(jnp.concatenate([stat_rows, jnp.zeros_like(stat_rows)], 0).astype(LOW))
        held_ref[head] = jnp.concatenate(blocks, 0)
    for distance, long_ref in enumerate(long_refs):
        long_ref[:rows] = held_ref[me ^ distance]
        long_ref[rows:] = held_ref[heads[-1]]
    for distance, short_ref in zip((2, 3), short_refs):
        short_ref[...] = held_ref[me ^ distance]


def prepare_kernel(top_step, offsets_ref, grad_ref, gain_ref, out_ref, *refs):
    grad_norm_ref, gain_part_ref, place_ref = refs
    tokens, width = grad_ref.shape[1:]
    heads = range(width // HEAD_DIM)
    top_rows = tokens // top_step
    ones = jnp.ones((TILE, tokens), LOW)
    column = lax.broadcasted_iota(jnp.int32, (tokens, tokens), 1)
    gain_part_ref[...] = jnp.zeros(gain_part_ref.shape, WIDE)
    grad_norms = [
        (grad_ref[0, :, head_cols(head)].astype(WIDE) * gain_ref[:, head_cols(head)]).T
        for head in heads
    ]
    for head in heads:
        cols = head_cols(head)
        grad_norm_ref[:, cols] = grad_norms[head]
        picks = pick_matrix(offsets_ref, head, tokens, top_step, 1)
        place_ref[:, cols] = picks
    for head in heads:
        cols = head_cols(head)
        mid_offset, top_offset = offsets_ref[0, head], offsets_ref[1, head]
        seen = jnp.maximum(
            hit_row(top_offset, top_step, tokens), hit_row(mid_offset, R1, tokens)
        )
        attn = out_ref[:, cols].astype(WIDE)
        normed = attn * lax.rsqrt(column_mean(attn * attn) + EPS)
        product = grad_norms[head] * normed * (1.0 - seen)
        gain_part_ref[:, cols] = gain_row_of(ones, product) / gain_ref[:, cols]
        both = mid_offset % top_step == top_offset
        kept = jnp.where(column < top_rows, 1.0, jnp.where(both, 0.0, 1.0)).astype(LOW)
        picks = pick_matrix(offsets_ref, head, tokens, top_step, 1)
        place_ref[:, head_cols(len(heads) + head)] = picks * kept


def owner_kernel(top_step, offsets_ref, gain_ref, gain_base_ref, *refs):
    own_ref, far_long, far_short, near, middle_long, middle_short = refs[:6]
    answer_refs, short_refs = refs[6 : 6 + SPAN], refs[6 + SPAN : 8 + SPAN]
    far_ref, middle_ref = refs[8 + SPAN :]
    heads = gain_ref.shape[1] // HEAD_DIM
    last = heads - 1
    top_rows, mid_rows = picked_counts(HEAD_DIM, top_step)
    picked = top_rows + mid_rows
    top_all, mid_all = SPAN * top_rows, SPAN * mid_rows
    queries = top_all + mid_all
    rows = far_short.shape[0]
    score_scale = 1.0 / math.sqrt(HEAD_DIM)
    me = lax.axis_index("ctx")
    owns_last = me == last_owner()

    @pl.when(owns_last)
    def _():
        far_ref[...] = far_long[:rows]
        middle_ref[...] = middle_long[:rows]

    @pl.when(jnp.logical_not(owns_last))
    def _():
        far_ref[...] = far_short[...]
        middle_ref[...] = middle_short[...]

    sources = (
        ((own_ref, 0), (near, 0), (middle_ref, 0), (far_ref, 0)),
        ((own_ref, rows), (near, rows), (middle_long, rows), (far_long, rows)),
    )
    both_heads = range(2)
    gain_row = jnp.zeros((1, HEAD_DIM), WIDE)
    for head in range(OWNED):
        gain_row = gain_row + jnp.where(me == head, 1.0, 0.0) * gain_ref[:, head_cols(head)]
    gain_rows = [gain_row, gain_ref[:, head_cols(last)]]
    lane = lax.broadcasted_iota(jnp.int32, (1, queries), 1)
    is_top = jnp.where(lane < top_all, 1.0, 0.0)

    def by_level(which, block):
        start = block * picked
        return jnp.concatenate(
            [ref[at + start : at + start + top_rows] for ref, at in sources[which]]
            + [ref[at + start + top_rows : at + start + picked] for ref, at in sources[which]],
            0,
        )

    def per_level(top_row, mid_row):
        return jnp.concatenate(
            [
                jnp.broadcast_to(top_row, (top_all, queries)),
                jnp.broadcast_to(mid_row, (mid_all, queries)),
            ],
            0,
        )

    def base_log_of(which):
        start = 5 * picked
        logs = [
            joined_row(ref[at + start : at + start + STAT_TILES].astype(WIDE), 0)
            for ref, at in sources[which]
        ]
        top_log = sum(
            rolled(lane_window(log, 0, top_rows), slot * top_rows) for slot, log in enumerate(logs)
        )
        mid_log = sum(
            rolled(lane_window(log, top_rows, mid_rows), slot * mid_rows - top_rows)
            for slot, log in enumerate(logs)
        )
        return jnp.concatenate([top_log, mid_log[:, :mid_all]], 1)

    def masks(head):
        mid_offset, top_offset = offsets_ref[0, head], offsets_ref[1, head]
        top_in_mid = ((lane % top_rows) * top_step + top_offset) % R1 == mid_offset
        both = jnp.where(mid_offset % top_step == top_offset, 1.0, 0.0)
        sees_top = is_top + (1.0 - is_top) * both
        sees_mid = is_top * jnp.where(top_in_mid, 1.0, 0.0) + (1.0 - is_top)
        once = is_top + (1.0 - is_top) * (1.0 - both)
        return per_level((1.0 - sees_top) * NEVER, (1.0 - sees_mid) * NEVER), once

    q_rows, k_rows, v_rows, grad_rows, base_rows = [
        [by_level(which, block) for which in both_heads] for block in range(5)
    ]
    biases, onces = zip(*[masks(head) for head in (me, last)])
    scores = [
        contract(k_rows[which], q_rows[which], 1, 1) * score_scale + biases[which]
        for which in both_heads
    ]
    base_logs = [base_log_of(which) for which in both_heads]
    base_attns = [block.astype(WIDE).T for block in base_rows]
    grad_norms = [
        (grad_rows[which].astype(WIDE) * gain_rows[which]).T for which in both_heads
    ]
    top_scores = [
        jnp.maximum(base_logs[which], jnp.max(scores[which], axis=0, keepdims=True))
        for which in both_heads
    ]
    expos = [jnp.exp(scores[which] - top_scores[which]) for which in both_heads]
    factors = [jnp.exp(base_logs[which] - top_scores[which]) for which in both_heads]
    totals = [
        factors[which] + jnp.sum(expos[which], axis=0, keepdims=True) for which in both_heads
    ]
    inv_totals = [1.0 / total for total in totals]
    softs = [expos[which] * inv_totals[which] for which in both_heads]
    soft_lows = [soft.astype(LOW) for soft in softs]
    attns = [
        (factors[which] * inv_totals[which]) * base_attns[which]
        + contract(v_rows[which], soft_lows[which], 0, 0)
        for which in both_heads
    ]
    _, products, grad_lows, inners = zip(
        *[norm_backward(attns[which], grad_norms[which]) for which in both_heads]
    )
    spans = (slice(0, top_all), slice(top_all, queries))
    cases = [(which, span) for which in both_heads for span in spans]
    prob_grads = [
        contract(v_rows[which][span], grad_lows[which][:, span], 1, 0) for which, span in cases
    ]
    dvs = [
        contract(soft_lows[which][span, span], grad_lows[which][:, span], 1, 1).astype(LOW)
        for which, span in cases
    ]
    score_grads = [
        (softs[which][span, span] * (prob_grad - inners[which][:, span]) * score_scale).astype(LOW)
        for (which, span), prob_grad in zip(cases, prob_grads)
    ]
    dks = [
        contract(score_grad, q_rows[which][span], 1, 0).astype(LOW)
        for (which, span), score_grad in zip(cases, score_grads)
    ]
    dqs = [
        contract(score_grad, k_rows[which][span], 0, 0).astype(LOW)
        for (which, span), score_grad in zip(cases, score_grads)
    ]
    attn_rows = [attn.T.astype(LOW) for attn in attns]
    attn_parts = [attn_rows[which][span] for which, span in cases]
    ones = jnp.ones((TILE, queries), LOW)
    own_gains = [
        gain_row_of(ones, products[which] * onces[which]) / gain_rows[which]
        for which in both_heads
    ]
    gains = [
        gain_base_ref[:, head_cols(head)] + jnp.where(me == head, 1.0, 0.0) * own_gains[0]
        for head in range(OWNED)
    ]
    gains.append(
        gain_base_ref[:, head_cols(last)] + jnp.where(owns_last, 1.0, 0.0) * own_gains[1]
    )
    gain_high, gain_rest = [
        block.astype(WIDE) for block in gain_pieces(jnp.concatenate(gains, 0))
    ]
    padding = jnp.zeros((1, top_all - mid_all), WIDE)
    empty = jnp.zeros((PIECES, HEAD_DIM), WIDE)
    answers = []
    for which in both_heads:
        log_total = top_scores[which] + jnp.log(totals[which])
        top_log = log_total[:, :top_all]
        mid_log = jnp.concatenate([log_total[:, top_all:], padding], 1)
        answers.append([])
        for distance in range(SPAN):
            blocks = []
            for block in (dqs, dks, dvs, attn_parts):
                top_block, mid_block = block[2 * which : 2 * which + 2]
                blocks.append(top_block[distance * top_rows : (distance + 1) * top_rows])
                blocks.append(mid_block[distance * mid_rows : (distance + 1) * mid_rows])
            log_row = lane_window(
                rolled(top_log, -distance * top_rows), 0, top_rows
            ) + lane_window(
                rolled(mid_log, top_rows - distance * mid_rows), top_rows, mid_rows
            )
            log_rows = [piece_rows(log_row, gain_high), empty, gain_rest]
            blocks.append(jnp.concatenate(log_rows, 0).astype(LOW))
            answers[-1].append(jnp.concatenate(blocks, 0))
    rows = answers[0][0].shape[0]
    for distance, answer_ref in enumerate(answer_refs):
        answer_ref[:rows] = answers[0][distance]
        answer_ref[rows:] = answers[1][distance]
    for distance, short_ref in zip((2, 3), short_refs):
        short_ref[...] = answers[0][distance]


def gain_kernel(picked, own_ref, far_long, far_short, near, middle_long, middle_short, gain_ref):
    me = lax.axis_index("ctx")

    def part(ref):
        tile = ref[4 * picked : 4 * picked + STAT_TILES].astype(WIDE)
        return tile[PIECES:TILE] + tile[TILE + PIECES :]

    far = jnp.where(me ^ 3 == last_owner(), part(far_long), part(far_short))
    middle = jnp.where(me ^ 2 == last_owner(), part(middle_long), part(middle_short))
    total = (part(own_ref) + part(near)) + (middle + far)
    for head in range(gain_ref.shape[1] // HEAD_DIM):
        gain_ref[:, head_cols(head)] = total[head : head + 1]


def mix_kernel(top_step, offsets_ref, v_ref, gain_ref, expo_ref, out_ref, *refs):
    grad_norm_ref, stats_ref, place_ref = refs[:3]
    own_ref, far_long, far_short, near, middle_long, middle_short = refs[3:9]
    attended_ref, grad_low_ref, soft_ref, score_grad_ref, placed_ref = refs[9:]
    tokens, width = v_ref.shape[1:]
    count = width // HEAD_DIM
    picked = sum(picked_counts(tokens, top_step))
    score_scale = 1.0 / math.sqrt(HEAD_DIM)
    me = lax.axis_index("ctx")
    heads = range(count)
    every = [head_cols(head) for head in heads]
    rows = far_short.shape[0]
    placed_ref[me] = own_ref[:rows]
    placed_ref[me ^ 1] = near[:rows]
    for distance, long_ref, short_ref in ((2, middle_long, middle_short), (3, far_long, far_short)):

        @pl.when(me ^ distance == last_owner())
        def _():
            placed_ref[me ^ distance] = long_ref[:rows]

        @pl.when(me ^ distance != last_owner())
        def _():
            placed_ref[me ^ distance] = short_ref[...]

    for distance, long_ref in enumerate((own_ref, near, middle_long, far_long)):

        @pl.when(me ^ distance == last_owner())
        def _():
            placed_ref[count - 1] = long_ref[rows:]

    once = [place_ref[:, head_cols(count + head)] for head in heads]
    attn_parts = [
        contract(placed_ref[head, 3 * picked : 4 * picked], once[head][:, :picked], 0, 1)
        for head in heads
    ]
    log_parts = [
        contract(placed_ref[head, 4 * picked : 4 * picked + STAT_TILES], once[head], 1, 1)
        for head in heads
    ]
    factors, normeds, grad_lows, inners = [], [], [], []
    for head in heads:
        top_hit = hit_row(offsets_ref[1, head], top_step, tokens)
        mid_hit = hit_row(offsets_ref[0, head], R1, tokens)
        seen = jnp.maximum(top_hit, mid_hit) > 0.5
        top_score, total = stats_ref[head : head + 1, :], stats_ref[TILE + head : TILE + head + 1, :]
        log_total = jnp.where(seen, joined_row(log_parts[head], 0), top_score + jnp.log(total))
        factors.append(jnp.exp(top_score - log_total))
        attn = jnp.where(seen, attn_parts[head], out_ref[:, every[head]].astype(WIDE))
        normed, _, grad_low, inner = norm_backward(attn, grad_norm_ref[:, every[head]])
        normeds.append(normed)
        grad_lows.append(grad_low)
        inners.append(inner)
    prob_grads = [contract(v_ref[0, :, every[head]], grad_lows[head], 1, 0) for head in heads]
    softs = [expo_ref[:, every[head]].astype(WIDE) * factors[head] for head in heads]
    for head in heads:
        cols = every[head]
        grad_low_ref[:, cols] = grad_lows[head]
        soft_ref[:, cols] = softs[head].astype(LOW)
        score_grad_ref[:, cols] = (
            softs[head] * (prob_grads[head] - inners[head]) * score_scale
        ).astype(LOW)
        attended_ref[:, cols] = (normeds[head].T * gain_ref[:, cols]).astype(LOW)


def finish_kernel(
    top_step,
    gain_ref,
    gain_rest_ref,
    q_ref,
    k_ref,
    place_ref,
    mixed_ref,
    grad_low_ref,
    soft_ref,
    score_grad_ref,
    returned_ref,
    attended_ref,
    dq_ref,
    dk_ref,
    dv_ref,
    gain_out_ref,
):
    tokens, width = q_ref.shape[1:]
    picked = sum(picked_counts(tokens, top_step))
    heads = range(width // HEAD_DIM)
    every = [head_cols(head) for head in heads]
    gain_out_ref[...] = (gain_ref[...] + gain_rest_ref[...]).reshape(gain_out_ref.shape)
    attended_ref[0] = mixed_ref[...]
    score_grads = [score_grad_ref[:, cols] for cols in every]
    dqs = [contract(score_grads[head], k_ref[0, :, every[head]], 0, 0) for head in heads]
    placed = [
        contract(
            place_ref[:, pl.ds(head * HEAD_DIM, picked)],
            jnp.concatenate(
                [returned_ref[head, block * picked : (block + 1) * picked] for block in range(3)], 1
            ),
            1,
            0,
        )
        for head in heads
    ]
    dks = [contract(score_grads[head], q_ref[0, :, every[head]], 1, 0) for head in heads]
    dvs = [contract(soft_ref[:, cols], grad_low_ref[:, cols], 1, 1) for cols in every]
    for head in heads:
        for which, (block, out_block_ref) in enumerate(
            ((dqs[head], dq_ref), (dks[head], dk_ref), (dvs[head], dv_ref))
        ):
            part = placed[head][:, which * HEAD_DIM : (which + 1) * HEAD_DIM]
            out_block_ref[0, :, every[head]] = (block + part).astype(LOW)


def across(block, axis, distance):
    route = [(place, place ^ distance) for place in range(lax.axis_size(axis))]
    return lax.ppermute(block, axis, route)


def across_some(block, distance, chosen):
    route = []
    for dp_place in range(lax.axis_size("dp")):
        for place in range(SPAN):
            if chosen(last_owner_of(dp_place), place, place ^ distance):
                start = dp_place * SPAN
                route.append((start + place, start + (place ^ distance)))
    return lax.ppermute(block, ("dp", "ctx"), route)


def to_peers(near, middle, far, takes_long):
    def takes_short(*ends):
        return not takes_long(*ends)

    far_pair = [across_some(far[i], 3, rule) for i, rule in enumerate((takes_long, takes_short))]
    near_block = across(near, "ctx", 1)
    middle_pair = [
        across_some(middle[i], 2, rule) for i, rule in enumerate((takes_long, takes_short))
    ]
    return [*far_pair, near_block, *middle_pair]


def call(kernel, name, operands, results, microseconds, vmem=PLAIN_VMEM, scratch=()):
    return pl.pallas_call(
        kernel,
        out_shape=results,
        in_specs=[SMEM_SPEC if block.dtype == jnp.int32 else VMEM_SPEC for block in operands],
        out_specs=[VMEM_SPEC] * len(results),
        scratch_shapes=scratch,
        compiler_params=pltpu.CompilerParams(vmem_limit_bytes=vmem),
        cost_estimate=pl.CostEstimate(
            flops=int(microseconds * 10**9), bytes_accessed=0, transcendentals=0
        ),
        name=name,
    )(*operands)


def one_segment_shards(queries, keys, values, grad_y, out_gain, offsets):
    tokens, width = queries.shape[1:]
    heads = width // HEAD_DIM
    top_step = lax.axis_size("ctx")
    picked = sum(picked_counts(tokens, top_step))
    shape = jax.ShapeDtypeStruct
    row_block = shape((1, tokens, width), LOW)
    low_block, wide_block = shape((tokens, width), LOW), shape((tokens, width), WIDE)

    gain_block = shape((1, width), WIDE)
    stats_block = shape((2 * TILE, tokens), WIDE)
    payload_rows, answer_rows = 5 * picked + STAT_TILES, 4 * picked + STAT_TILES
    long_payload, payload = [shape((n * payload_rows, HEAD_DIM), LOW) for n in (2, 1)]
    long_answer, answer = [shape((n * answer_rows, HEAD_DIM), LOW) for n in (2, 1)]
    bind = functools.partial
    gain_row = out_gain.reshape(1, width)
    own, near, middle, far, short_middle, short_far, expo, base_out, stats = call(
        bind(pack_kernel, top_step),
        "pack",
        (offsets, queries, keys, values, grad_y),
        [long_payload] * SPAN + [payload] * 2 + [low_block, low_block, stats_block],
        1,
        vmem=PACK_VMEM,
        scratch=[pltpu.VMEM((heads, *payload.shape), LOW)],
    )
    received = to_peers(
        near, (middle, short_middle), (far, short_far), lambda owner, source, target: target == owner
    )
    grad_norm, gain_base, place = call(
        bind(prepare_kernel, top_step),
        "prepare",
        (offsets, grad_y, gain_row, base_out),
        [wide_block, gain_block, shape((tokens, 2 * width), LOW)],
        2,
    )
    own, near, middle, far, short_middle, short_far = call(
        bind(owner_kernel, top_step),
        "owner",
        (offsets, gain_row, gain_base, own, *received),
        [long_answer] * SPAN + [answer] * 2,
        3,
        scratch=[pltpu.VMEM(payload.shape, LOW)] * 2,
    )
    returned = to_peers(
        near, (middle, short_middle), (far, short_far), lambda owner, source, target: source == owner
    )
    (gain_sum,) = call(bind(gain_kernel, picked), "gain", (own, *returned), [gain_block], 1)
    gain_rest = across(gain_sum, "dp", 1)
    mixed = call(
        bind(mix_kernel, top_step),
        "mix",
        (
            offsets,
            values,
            gain_row,
            expo,
            base_out,
            grad_norm,
            stats,
            place,
            own,
            *returned,
        ),
        [low_block] * 4 + [shape((heads, *answer.shape), LOW)],
        20,
    )
    attended, query_grad, key_grad, value_grad, gain_grad = call(
        bind(finish_kernel, top_step),
        "finish",
        (
            gain_sum,
            gain_rest,
            queries,
            keys,
            place,
            *mixed,
        ),
        [row_block] * 4 + [shape((width,), WIDE)],
        1,
    )
    return attended, query_grad, key_grad, value_grad, gain_grad


def shards(*operands):
    one_segment = lax.axis_size("ctx") == SPAN
    if one_segment and operands[0].shape[2] == (OWNED + 1) * HEAD_DIM:
        return one_segment_shards(*operands)
    return general_shards(*operands)


def solution(mesh):
    in_specs = (
        P("dp", "ctx", "head"),
        P("dp", "ctx", "head"),
        P("dp", "ctx", "head"),
        P("dp", "ctx", "head"),
        P("head"),
        P(None, "head"),
    )
    out_specs = (
        P("dp", "ctx", "head"),
        P("dp", "ctx", "head"),
        P("dp", "ctx", "head"),
        P("dp", "ctx", "head"),
        P("head"),
    )
    return jax.shard_map(shards, mesh=mesh, in_specs=in_specs, out_specs=out_specs, check_vma=False)
```

```python
import functools
import math

import jax
import jax.numpy as jnp
from jax import lax
from jax.experimental import pallas as pl
from jax.experimental.pallas import tpu as pltpu
from jax.sharding import PartitionSpec as P

HEAD_DIM = 128
SPAN = 4
R1 = 8


EPS = 1e-06


def swapped(block, axis, bit):
    count = lax.axis_size(axis)
    route = []
    for low in range(count):
        high = low | 1 << bit
        if high != low and high < count:
            route += [(low, high), (high, low)]
    return lax.ppermute(block, axis, route)


def pick_rows(source_rows, dilation, shifts):
    row_count, head_count, head_width = source_rows.shape
    grouped = source_rows.reshape(row_count // dilation, dilation, head_count, head_width)
    hit_mask = jnp.arange(dilation, dtype=jnp.int32).reshape(1, dilation, 1, 1) == shifts.reshape(
        1, 1, head_count, 1
    )
    chosen = jnp.where(hit_mask, grouped, jnp.zeros((), source_rows.dtype))
    return jnp.sum(chosen, axis=1, dtype=source_rows.dtype)


def place_rows(row_values, dilation, shifts):
    row_count, head_count, head_width = row_values.shape
    hit_mask = jnp.arange(dilation, dtype=jnp.int32).reshape(1, dilation, 1, 1) == shifts.reshape(
        1, 1, head_count, 1
    )
    spread = jnp.where(hit_mask, row_values[:, None], jnp.zeros((), row_values.dtype))
    return spread.reshape(row_count * dilation, head_count, head_width)


def level_scores(q_rows, k_rows):
    score_scale = 1.0 / math.sqrt(q_rows.shape[-1])
    return (
        jnp.einsum("qhe,khe->hqk", q_rows, k_rows, preferred_element_type=jnp.float32) * score_scale
    )


def attend(q_rows, k_rows, v_rows):
    scores = level_scores(q_rows, k_rows)
    row_max = jnp.max(scores, axis=-1, keepdims=True)
    log_total = row_max[..., 0] + jnp.log(jnp.sum(jnp.exp(scores - row_max), axis=-1))
    soft_rows = jnp.exp(scores - log_total[..., None]).astype(jnp.bfloat16)
    level_out = jnp.einsum("hqk,khe->qhe", soft_rows, v_rows, preferred_element_type=jnp.float32)
    return (level_out, log_total.T)


def score_grads(q_rows, k_rows, v_rows, log_total, grad_low, row_shift):
    score_scale = 1.0 / math.sqrt(q_rows.shape[-1])
    scores = level_scores(q_rows, k_rows)
    exact_soft = jnp.exp(scores - log_total.T[..., None])
    prob_grad = jnp.einsum("qhe,khe->hqk", grad_low, v_rows, preferred_element_type=jnp.float32)
    score_grad = (exact_soft * (prob_grad + row_shift.T[..., None]) * score_scale).astype(
        jnp.bfloat16
    )
    return (score_grad, exact_soft.astype(jnp.bfloat16))


def key_parts(score_grad, soft_low, q_rows, grad_low):
    k_part = jnp.einsum("hqk,qhe->khe", score_grad, q_rows, preferred_element_type=jnp.float32)
    v_part = jnp.einsum("hqk,qhe->khe", soft_low, grad_low, preferred_element_type=jnp.float32)
    return (k_part, v_part)


def query_part(score_grad, k_rows):
    return jnp.einsum("hqk,khe->qhe", score_grad, k_rows, preferred_element_type=jnp.float32)


def general_shards(queries, keys, values, grad_y, out_gain, offsets):
    tokens = queries.shape[1]
    flat_width = queries.shape[2]
    head_count = flat_width // HEAD_DIM
    row_shape = (tokens, head_count, HEAD_DIM)
    q_own = queries[0].reshape(row_shape)
    k_own = keys[0].reshape(row_shape)
    v_own = values[0].reshape(row_shape)
    ctx_size = lax.axis_size("ctx")
    span_bits = SPAN.bit_length() - 1
    my_place = lax.axis_index("ctx")
    mid_shift = offsets[0]
    top_shift = offsets[1]
    positions = jnp.arange(tokens, dtype=jnp.int32)
    mid_hit = (positions % R1)[:, None] == mid_shift[None, :]
    top_hit = (positions % ctx_size)[:, None] == top_shift[None, :]
    mid_q = pick_rows(q_own, R1, mid_shift)
    mid_k = pick_rows(k_own, R1, mid_shift)
    mid_v = pick_rows(v_own, R1, mid_shift)
    top_q = pick_rows(q_own, ctx_size, top_shift)
    top_k = pick_rows(k_own, ctx_size, top_shift)
    top_v = pick_rows(v_own, ctx_size, top_shift)
    mid_keys = mid_k.reshape(-1, flat_width)
    mid_vals = mid_v.reshape(-1, flat_width)
    top_keys = top_k.reshape(-1, flat_width)
    top_vals = top_v.reshape(-1, flat_width)

    def append_peer(mine, received, level_bit):
        upper_side = my_place >> level_bit & 1 == 1
        return jnp.where(
            upper_side, jnp.concatenate([received, mine], 0), jnp.concatenate([mine, received], 0)
        )

    for level_bit in range(span_bits):
        received = swapped((mid_keys, mid_vals), "ctx", level_bit)
        mid_keys = append_peer(mid_keys, received[0], level_bit)
        mid_vals = append_peer(mid_vals, received[1], level_bit)
    top_keys, top_vals = (
        lax.all_gather(top_keys, "ctx", axis=0, tiled=True),
        lax.all_gather(top_vals, "ctx", axis=0, tiled=True),
    )
    mid_keys = mid_keys.reshape(-1, head_count, HEAD_DIM)
    mid_vals = mid_vals.reshape(-1, head_count, HEAD_DIM)
    top_keys = top_keys.reshape(-1, head_count, HEAD_DIM)
    top_vals = top_vals.reshape(-1, head_count, HEAD_DIM)
    base_out, base_total = attend(q_own, k_own, v_own)
    mid_out, mid_total = attend(mid_q, mid_keys, mid_vals)
    top_out, top_total = attend(top_q, top_keys, top_vals)
    mid_full = place_rows(mid_total[..., None], R1, mid_shift)[..., 0]
    top_full = place_rows(top_total[..., None], ctx_size, top_shift)[..., 0]
    row_max = jnp.maximum(base_total, jnp.where(mid_hit, mid_full, base_total))
    row_max = jnp.maximum(row_max, jnp.where(top_hit, top_full, base_total))
    base_expo = jnp.exp(base_total - row_max)
    mid_expo = jnp.where(mid_hit, jnp.exp(mid_full - row_max), 0.0)
    top_expo = jnp.where(top_hit, jnp.exp(top_full - row_max), 0.0)
    denom = base_expo + mid_expo + top_expo
    base_share = base_expo / denom
    mid_share = mid_expo / denom
    top_share = top_expo / denom
    attn = (
        base_share[..., None] * base_out
        + mid_share[..., None] * place_rows(mid_out, R1, mid_shift)
        + top_share[..., None] * place_rows(top_out, ctx_size, top_shift)
    )
    inv_rms = lax.rsqrt(jnp.mean(attn * attn, axis=-1, keepdims=True) + EPS)
    normed = attn * inv_rms
    gain_rows = out_gain.reshape(head_count, HEAD_DIM)
    attended = (normed * gain_rows).astype(jnp.bfloat16).reshape(1, tokens, flat_width)
    grad_full = grad_y[0].reshape(row_shape).astype(jnp.float32)
    gain_part = jnp.sum(grad_full * normed, axis=0).reshape(flat_width)
    gain_grad = lax.psum(gain_part, ("dp", "ctx"))
    grad_norm = grad_full * gain_rows
    grad_attn = inv_rms * (
        grad_norm - normed * jnp.mean(grad_norm * normed, axis=-1, keepdims=True)
    )
    inner = jnp.sum(grad_attn * attn, axis=-1)
    base_low = (base_share[..., None] * grad_attn).astype(jnp.bfloat16)
    base_shift = -(base_share * inner)
    base_grad, base_soft = score_grads(q_own, k_own, v_own, base_total, base_low, base_shift)
    base_dq = query_part(base_grad, k_own)
    base_dk, base_dv = key_parts(base_grad, base_soft, q_own, base_low)
    mid_sel = pick_rows(mid_share[..., None], R1, mid_shift)[..., 0]
    mid_low = (mid_sel[..., None] * pick_rows(grad_attn, R1, mid_shift)).astype(jnp.bfloat16)
    mid_row_shift = -(mid_sel * pick_rows(inner[..., None], R1, mid_shift)[..., 0])
    mid_grad, mid_soft = score_grads(mid_q, mid_keys, mid_vals, mid_total, mid_low, mid_row_shift)
    mid_dq = query_part(mid_grad, mid_keys)
    mid_dk, mid_dv = key_parts(mid_grad, mid_soft, mid_q, mid_low)
    mid_dk = mid_dk.reshape(-1, flat_width)
    mid_dv = mid_dv.reshape(-1, flat_width)
    for level_bit in reversed(range(span_bits)):
        half_rows = mid_dk.shape[0] // 2
        upper_side = my_place >> level_bit & 1 == 1
        keep_k = jnp.where(upper_side, mid_dk[half_rows:], mid_dk[:half_rows])
        keep_v = jnp.where(upper_side, mid_dv[half_rows:], mid_dv[:half_rows])
        send_k = jnp.where(upper_side, mid_dk[:half_rows], mid_dk[half_rows:])
        send_v = jnp.where(upper_side, mid_dv[:half_rows], mid_dv[half_rows:])
        received = (
            swapped(send_k.astype(jnp.bfloat16), "ctx", level_bit).astype(send_k.dtype),
            swapped(send_v.astype(jnp.bfloat16), "ctx", level_bit).astype(send_v.dtype),
        )
        mid_dk = keep_k + received[0]
        mid_dv = keep_v + received[1]
    mid_dk = mid_dk.reshape(-1, head_count, HEAD_DIM)
    mid_dv = mid_dv.reshape(-1, head_count, HEAD_DIM)
    top_sel = pick_rows(top_share[..., None], ctx_size, top_shift)[..., 0]
    top_low = (top_sel[..., None] * pick_rows(grad_attn, ctx_size, top_shift)).astype(jnp.bfloat16)
    top_row_shift = -(top_sel * pick_rows(inner[..., None], ctx_size, top_shift)[..., 0])
    top_grad, top_soft = score_grads(top_q, top_keys, top_vals, top_total, top_low, top_row_shift)
    top_dq = query_part(top_grad, top_keys)
    gathered_dk, gathered_dv = key_parts(top_grad, top_soft, top_q, top_low)
    summed = (
        lax.psum_scatter(
            gathered_dk.reshape(-1, flat_width), "ctx", scatter_dimension=0, tiled=True
        ),
        lax.psum_scatter(
            gathered_dv.reshape(-1, flat_width), "ctx", scatter_dimension=0, tiled=True
        ),
    )
    top_dk = summed[0].reshape(-1, head_count, HEAD_DIM)
    top_dv = summed[1].reshape(-1, head_count, HEAD_DIM)
    query_grad = (
        base_dq + place_rows(mid_dq, R1, mid_shift) + place_rows(top_dq, ctx_size, top_shift)
    )
    key_grad = base_dk + place_rows(mid_dk, R1, mid_shift) + place_rows(top_dk, ctx_size, top_shift)
    value_grad = (
        base_dv + place_rows(mid_dv, R1, mid_shift) + place_rows(top_dv, ctx_size, top_shift)
    )
    out_shape = (1, tokens, flat_width)
    return (
        attended,
        query_grad.astype(jnp.bfloat16).reshape(out_shape),
        key_grad.astype(jnp.bfloat16).reshape(out_shape),
        value_grad.astype(jnp.bfloat16).reshape(out_shape),
        gain_grad,
    )


VMEM_SPEC = pl.BlockSpec(memory_space=pltpu.VMEM)
SMEM_SPEC = pl.BlockSpec(memory_space=pltpu.SMEM)
PEERS = SPAN - 1
OWNED = SPAN
TILE = 8
STAT_TILES = 2 * TILE
PIECES = 3
NEVER = -1e30
START_ORDER = (3, 1, 2)
LOW = jnp.bfloat16
WIDE = jnp.float32
PACK_VMEM = 65408 * 1024
PLAIN_VMEM = 16 * 1024 * 1024


def contract(left, right, left_dim, right_dim):
    return lax.dot_general(
        left, right, (((left_dim,), (right_dim,)), ((), ())), preferred_element_type=WIDE
    )


def head_cols(head):
    return pl.ds(head * HEAD_DIM, HEAD_DIM)


def picked_counts(tokens, top_step):
    return tokens // top_step, tokens // R1


def pick_matrix(offsets_ref, head, tokens, top_step, picked_axis):
    top_rows, _ = picked_counts(tokens, top_step)
    row = lax.broadcasted_iota(jnp.int32, (tokens, tokens), picked_axis)
    position = lax.broadcasted_iota(jnp.int32, (tokens, tokens), 1 - picked_axis)
    wanted = jnp.where(
        row < top_rows,
        row * top_step + offsets_ref[1, head],
        (row - top_rows) * R1 + offsets_ref[0, head],
    )
    return jnp.where(position == wanted, 1.0, 0.0).astype(LOW)


def rolled(row, shift):
    return pltpu.roll(row, shift % row.shape[1], 1)


def lane_window(row, start, count):
    lane = lax.broadcasted_iota(jnp.int32, row.shape, 1)
    return jnp.where((lane >= start) & (lane < start + count), row, 0.0)


def hit_row(offset, step, tokens):
    position = lax.broadcasted_iota(jnp.int32, (1, tokens), 1)
    return jnp.where(position % step == offset, 1.0, 0.0)


def piece_rows(row, others=None):
    pieces = []
    for _ in range(PIECES):
        piece = row.astype(LOW).astype(WIDE)
        pieces.append(piece)
        row = row - piece
    if others is None:
        others = jnp.zeros((TILE - PIECES, row.shape[1]), WIDE)
    return jnp.concatenate(pieces + [others], 0)


def gain_pieces(rows):
    high = rows.astype(LOW)
    return high, (rows - high.astype(WIDE)).astype(LOW)


def joined_row(rows, first):
    total = rows[first : first + 1]
    for piece in range(1, PIECES):
        total = total + rows[first + piece : first + piece + 1]
    return total


def gain_row_of(ones, product):
    high, rest = gain_pieces(product)
    return (contract(ones, high, 1, 1) + contract(ones, rest, 1, 1))[:1]


def column_mean(block):
    return jnp.mean(block, axis=0, keepdims=True)


def norm_backward(attn, grad_norm):
    inv_rms = lax.rsqrt(column_mean(attn * attn) + EPS)
    normed = attn * inv_rms
    product = grad_norm * normed
    grad_attn = inv_rms * (grad_norm - normed * column_mean(product))
    inner = jnp.sum(grad_attn * attn, axis=0, keepdims=True)
    return normed, product, grad_attn.astype(LOW), inner


def nearest_first(refs):
    by_distance = dict(zip(START_ORDER, refs[1:]))
    return [refs[0], *[by_distance[distance] for distance in range(1, SPAN)]]


def pack_kernel(top_step, offsets_ref, q_ref, k_ref, v_ref, grad_ref, *refs):
    payload_refs, (expo_ref, out_ref, stats_ref, held_ref) = refs[:SPAN], refs[SPAN:]
    tokens, width = q_ref.shape[1:]
    heads = range(width // HEAD_DIM)
    owned = range(OWNED)
    me = lax.axis_index("ctx")
    picked = sum(picked_counts(tokens, top_step))
    score_scale = 1.0 / math.sqrt(HEAD_DIM)
    q_rows, k_rows, v_rows, grad_rows = [
        [ref[0, :, head_cols(head)] for head in heads] for ref in (q_ref, k_ref, v_ref, grad_ref)
    ]
    picks = [pick_matrix(offsets_ref, head, tokens, top_step, 0) for head in heads]
    scores = [contract(k_rows[head], q_rows[head], 1, 1) * score_scale for head in heads]
    moved = [
        contract(
            picks[head][:picked],
            jnp.concatenate([q_rows[head], k_rows[head], v_rows[head], grad_rows[head]], 1),
            1,
            0,
        ).astype(LOW)
        for head in owned
    ]
    shared = [
        contract(
            picks[head][:picked], jnp.concatenate([k_rows[head], v_rows[head]], 1), 1, 0
        ).astype(LOW)
        for head in heads[OWNED:]
    ]
    top_scores = [jnp.max(block, axis=0, keepdims=True) for block in scores]
    expos = [jnp.exp(scores[head] - top_scores[head]) for head in heads]
    for head in heads[OWNED:]:
        key_row = lax.broadcasted_iota(jnp.int32, (tokens, 1), 0)
        times = 1.0
        for level, step in ((0, R1), (1, top_step)):
            offset = offsets_ref[level, head]
            hit_column = jnp.where(key_row % step == offset, 1.0, 0.0)
            times = times + hit_column * hit_row(offset, step, tokens)
        expos[head] = times * expos[head]
    expo_lows = [expo.astype(LOW) for expo in expos]
    outs = [contract(v_rows[head], expo_lows[head], 0, 0) for head in heads]
    totals = [jnp.sum(expo, axis=0, keepdims=True) for expo in expos]
    for head in heads:
        expo_ref[:, head_cols(head)] = expo_lows[head]
        stats_ref[head : head + 1, :] = top_scores[head]
        stats_ref[TILE + head : TILE + head + 1, :] = totals[head]
    for head in owned:
        outs[head] = outs[head] * (1.0 / totals[head])
    outs = [out.astype(LOW) for out in outs]
    picked_outs = [
        contract(picks[head][:picked], outs[head], 1, 1).astype(LOW) for head in owned
    ]
    for head in heads:
        out_ref[:, head_cols(head)] = outs[head]
    for head in owned:
        pieces = piece_rows(top_scores[head] + jnp.log(totals[head])).astype(LOW)
        stat_rows = contract(pieces, picks[head], 1, 1)
        blocks = [moved[head][:, block * HEAD_DIM : (block + 1) * HEAD_DIM] for block in range(4)]
        blocks.append(picked_outs[head])
        blocks += [shared[0][:, :HEAD_DIM], shared[0][:, HEAD_DIM:]]
        blocks.append(jnp.concatenate([stat_rows, jnp.zeros_like(stat_rows)], 0).astype(LOW))
        held_ref[head] = jnp.concatenate(blocks, 0)
    for distance, payload_ref in enumerate(payload_refs):
        payload_ref[...] = held_ref[me ^ distance]


def prepare_kernel(top_step, offsets_ref, grad_ref, gain_ref, out_ref, *refs):
    grad_norm_ref, gain_part_ref, place_ref, masks_ref = refs
    tokens, width = grad_ref.shape[1:]
    heads = range(width // HEAD_DIM)
    top_rows = tokens // top_step
    ones = jnp.ones((TILE, tokens), LOW)
    column = lax.broadcasted_iota(jnp.int32, (tokens, tokens), 1)
    gain_part_ref[...] = jnp.zeros(gain_part_ref.shape, WIDE)
    me = lax.axis_index("ctx")
    mid_rows = tokens // R1
    top_all, queries = SPAN * top_rows, SPAN * (top_rows + mid_rows)
    mid_offset, top_offset = offsets_ref[0, me], offsets_ref[1, me]
    lane = lax.broadcasted_iota(jnp.int32, (1, queries), 1)
    is_top = jnp.where(lane < top_all, 1.0, 0.0)
    top_in_mid = jnp.where(((lane % top_rows) * top_step + top_offset) % R1 == mid_offset, 1.0, 0.0)
    both_flag = jnp.where(mid_offset % top_step == top_offset, 1.0, 0.0)
    sees_top = is_top + (1.0 - is_top) * both_flag
    sees_mid = is_top * top_in_mid + (1.0 - is_top)
    masks_ref[0:1, :queries] = (1.0 - sees_top) * NEVER
    masks_ref[1:2, :queries] = (1.0 - sees_mid) * NEVER
    masks_ref[2:3, :queries] = is_top + (1.0 - is_top) * (1.0 - both_flag)
    last = len(heads) - 1
    for row, (level, step) in enumerate(((1, top_step), (0, R1))):
        hits = hit_row(offsets_ref[level, last], step, tokens)
        masks_ref[3 + row : 4 + row, :tokens] = (1.0 - hits) * NEVER
    grad_norms = [
        (grad_ref[0, :, head_cols(head)].astype(WIDE) * gain_ref[:, head_cols(head)]).T
        for head in heads
    ]
    for head in heads:
        cols = head_cols(head)
        grad_norm_ref[:, cols] = grad_norms[head]
        picks = pick_matrix(offsets_ref, head, tokens, top_step, 1)
        place_ref[:, cols] = picks
    for head in range(OWNED):
        cols = head_cols(head)
        mid_offset, top_offset = offsets_ref[0, head], offsets_ref[1, head]
        seen = jnp.maximum(
            hit_row(top_offset, top_step, tokens), hit_row(mid_offset, R1, tokens)
        )
        masks_ref[TILE + head : TILE + head + 1, :tokens] = seen
        attn = out_ref[:, cols].astype(WIDE)
        normed = attn * lax.rsqrt(column_mean(attn * attn) + EPS)
        product = grad_norms[head] * normed * (1.0 - seen)
        gain_part_ref[:, cols] = gain_row_of(ones, product) / gain_ref[:, cols]
        both = mid_offset % top_step == top_offset
        kept = jnp.where(column < top_rows, 1.0, jnp.where(both, 0.0, 1.0)).astype(LOW)
        picks = pick_matrix(offsets_ref, head, tokens, top_step, 1)
        place_ref[:, head_cols(len(heads) + head)] = picks * kept


def owner_kernel(top_step, q_ref, gain_ref, out_ref, grad_norm_ref, *refs):
    stats_ref, gain_base_ref, masks_ref = refs[:3]
    payload_refs, refs = nearest_first(refs[3 : 3 + SPAN]), refs[3 + SPAN :]
    normed_ref, grad_low_ref, score_grad_ref, kept_ref = refs[:4]
    return_refs = refs[4:]
    tokens = q_ref.shape[1]
    heads = q_ref.shape[2] // HEAD_DIM
    top_rows, mid_rows = picked_counts(tokens, top_step)
    picked = top_rows + mid_rows
    top_all, mid_all = SPAN * top_rows, SPAN * mid_rows
    queries = top_all + mid_all
    score_scale = 1.0 / math.sqrt(HEAD_DIM)
    me = lax.axis_index("ctx")
    ones = jnp.ones((TILE, tokens), LOW)

    def by_level(block):
        start = block * picked
        return jnp.concatenate(
            [ref[start : start + top_rows] for ref in payload_refs]
            + [ref[start + top_rows : start + picked] for ref in payload_refs],
            0,
        )

    def per_level(top_row, mid_row):
        return jnp.concatenate(
            [
                jnp.broadcast_to(top_row, (top_all, queries)),
                jnp.broadcast_to(mid_row, (mid_all, queries)),
            ],
            0,
        )

    q_rows, k_rows, v_rows, grad_rows, base_rows = [by_level(block) for block in range(5)]
    stat_start = 7 * picked
    logs = [
        joined_row(ref[stat_start : stat_start + STAT_TILES].astype(WIDE), 0)
        for ref in payload_refs
    ]
    base_top_log = sum(
        rolled(lane_window(log, 0, top_rows), slot * top_rows) for slot, log in enumerate(logs)
    )
    base_mid_log = sum(
        rolled(lane_window(log, top_rows, mid_rows), slot * mid_rows - top_rows)
        for slot, log in enumerate(logs)
    )
    base_log = jnp.concatenate([base_top_log, base_mid_log[:, :mid_all]], 1)
    gain_row = jnp.zeros((1, HEAD_DIM), WIDE)
    for head in range(OWNED):
        gain_row = gain_row + jnp.where(me == head, 1.0, 0.0) * gain_ref[:, head_cols(head)]
    lane = lax.broadcasted_iota(jnp.int32, (1, queries), 1)
    is_top = jnp.where(lane < top_all, 1.0, 0.0)
    bias = per_level(masks_ref[0:1, :queries], masks_ref[1:2, :queries])
    last = heads - 1
    cols = head_cols(last)
    peers = payload_refs[1:]
    q_last = q_ref[0, :, cols]
    k_peers = jnp.concatenate([ref[5 * picked : 6 * picked] for ref in peers], 0)
    v_peers = jnp.concatenate([ref[6 * picked : 7 * picked] for ref in peers], 0)
    last_biases = [
        jnp.broadcast_to(masks_ref[row : row + 1, :tokens], (count, tokens))
        for row, count in ((3, top_rows), (4, mid_rows))
    ]
    scores = contract(k_rows, q_rows, 1, 1) * score_scale + bias
    scores_last = contract(k_peers, q_last, 1, 1) * score_scale + jnp.concatenate(
        last_biases * PEERS, 0
    )
    base_attn = base_rows.astype(WIDE).T
    grad_norm = (grad_rows.astype(WIDE) * gain_row).T
    top_score = jnp.maximum(base_log, jnp.max(scores, axis=0, keepdims=True))
    base_top, base_total = stats_ref[last : last + 1, :], stats_ref[TILE + last : TILE + last + 1, :]
    top_last = jnp.maximum(base_top, jnp.max(scores_last, axis=0, keepdims=True))
    expo = jnp.exp(scores - top_score)
    expo_last = jnp.exp(scores_last - top_last)
    factor = jnp.exp(base_log - top_score)
    factor_last = jnp.exp(base_top - top_last)
    total = factor + jnp.sum(expo, axis=0, keepdims=True)
    total_last = factor_last * base_total + jnp.sum(expo_last, axis=0, keepdims=True)
    inv_total, inv_last = 1.0 / total, 1.0 / total_last
    soft, soft_last = expo * inv_total, expo_last * inv_last
    soft_low, soft_last_low = soft.astype(LOW), soft_last.astype(LOW)
    factor_last = factor_last * inv_last
    attn = (factor * inv_total) * base_attn + contract(v_rows, soft_low, 0, 0)
    attn_last = factor_last * out_ref[:, cols].astype(WIDE) + contract(v_peers, soft_last_low, 0, 0)
    _, product, grad_low, inner = norm_backward(attn, grad_norm)
    normed_last, product_last, grad_last_low, inner_last = norm_backward(
        attn_last, grad_norm_ref[:, cols]
    )
    spans = (slice(0, top_all), slice(top_all, queries))
    prob_grads = [contract(v_rows[span], grad_low[:, span], 1, 0) for span in spans]
    prob_grad_last = contract(v_peers, grad_last_low, 1, 0)
    score_grads = [
        (soft[span, span] * (prob_grad - inner[:, span]) * score_scale).astype(LOW)
        for span, prob_grad in zip(spans, prob_grads)
    ]
    score_grad_last = (soft_last * (prob_grad_last - inner_last) * score_scale).astype(LOW)
    dks = [
        contract(score_grad, q_rows[span], 1, 0).astype(LOW)
        for span, score_grad in zip(spans, score_grads)
    ]
    dk_last = contract(score_grad_last, q_last, 1, 0).astype(LOW)
    dvs = [
        contract(soft_low[span, span], grad_low[:, span], 1, 1).astype(LOW) for span in spans
    ]
    dv_last = contract(soft_last_low, grad_last_low, 1, 1).astype(LOW)
    dqs = [
        contract(score_grad, k_rows[span], 0, 0).astype(LOW)
        for span, score_grad in zip(spans, score_grads)
    ]
    attn_rows = attn.T.astype(LOW)
    attn_parts = [attn_rows[span] for span in spans]
    log_total = top_score + jnp.log(total)
    padding = jnp.zeros((1, top_all - mid_all), WIDE)
    once = masks_ref[2:3, :queries]
    ones_all = jnp.ones((TILE, queries), LOW)
    own_gain = gain_row_of(ones_all, product * once) / gain_row
    gain_rows = [
        gain_base_ref[:, head_cols(head)] + jnp.where(me == head, 1.0, 0.0) * own_gain
        for head in range(OWNED)
    ]
    gain_rows.append(gain_row_of(ones, product_last) / gain_ref[:, cols])
    gain_high, gain_rest = [
        rows.astype(WIDE) for rows in gain_pieces(jnp.concatenate(gain_rows, 0))
    ]
    top_log, mid_log = log_total[:, :top_all], jnp.concatenate(
        [log_total[:, top_all:], padding], 1
    )
    empty = jnp.zeros((PIECES, HEAD_DIM), WIDE)
    for distance, return_ref in enumerate(return_refs):
        blocks = []
        for top_block, mid_block in (dqs, dks, dvs, attn_parts):
            blocks.append(top_block[distance * top_rows : (distance + 1) * top_rows])
            blocks.append(mid_block[distance * mid_rows : (distance + 1) * mid_rows])
        start = max(distance - 1, 0) * picked
        blocks += [dk_last[start : start + picked], dv_last[start : start + picked]]
        log_row = lane_window(rolled(top_log, -distance * top_rows), 0, top_rows) + lane_window(
            rolled(mid_log, top_rows - distance * mid_rows), top_rows, mid_rows
        )
        log_rows = [piece_rows(log_row, gain_high), empty, gain_rest]
        blocks.append(jnp.concatenate(log_rows, 0).astype(LOW))
        return_ref[...] = jnp.concatenate(blocks, 0)
    normed_ref[...] = normed_last
    grad_low_ref[...] = grad_last_low
    score_grad_ref[...] = score_grad_last
    kept_ref[0:1, :] = factor_last
    kept_ref[1:2, :] = inner_last


def last_head_kernel(top_step, q_ref, k_ref, v_ref, gain_ref, expo_ref, *refs):
    normed_ref, grad_low_ref, peer_score_grad_ref, kept_ref, *peers = refs[: 4 + PEERS]
    peers = nearest_first([None, *peers])[1:]
    attended_ref, dq_ref, dk_ref, dv_ref = refs[4 + PEERS :]
    picked = sum(picked_counts(q_ref.shape[1], top_step))
    score_scale = 1.0 / math.sqrt(HEAD_DIM)
    cols = head_cols(q_ref.shape[2] // HEAD_DIM - 1)
    attended_ref[...] = (normed_ref[...].T * gain_ref[:, cols]).astype(LOW)
    k_peers = jnp.concatenate([ref[5 * picked : 6 * picked] for ref in peers], 0)
    grad_low = grad_low_ref[...]
    soft = expo_ref[:, cols].astype(WIDE) * kept_ref[0:1, :]
    prob_grad = contract(v_ref[0, :, cols], grad_low, 1, 0)
    score_grad = (soft * (prob_grad - kept_ref[1:2, :]) * score_scale).astype(LOW)
    dk_ref[...] = contract(score_grad, q_ref[0, :, cols], 1, 0)
    dv_ref[...] = contract(soft.astype(LOW), grad_low, 1, 1)
    dq_ref[...] = (
        contract(score_grad, k_ref[0, :, cols], 0, 0)
        + contract(peer_score_grad_ref[...], k_peers, 0, 0)
    ).astype(LOW)


def gain_kernel(picked, *refs):
    return_refs, gain_ref = nearest_first(refs[:SPAN]), refs[SPAN]
    tiles = [ref[6 * picked : 6 * picked + STAT_TILES].astype(WIDE) for ref in return_refs]
    parts = [tile[PIECES:TILE] + tile[TILE + PIECES :] for tile in tiles]
    total = (parts[0] + parts[1]) + (parts[2] + parts[3])
    for head in range(gain_ref.shape[1] // HEAD_DIM):
        gain_ref[:, head_cols(head)] = total[head : head + 1]


def mix_kernel(top_step, v_ref, gain_ref, expo_ref, out_ref, *refs):
    grad_norm_ref, stats_ref, place_ref, masks_ref = refs[:4]
    return_refs, refs = nearest_first(refs[4 : 4 + SPAN]), refs[4 + SPAN :]
    attended_ref, grad_low_ref, soft_ref, score_grad_ref, placed_ref = refs
    tokens, width = v_ref.shape[1:]
    count = width // HEAD_DIM
    picked = sum(picked_counts(tokens, top_step))
    score_scale = 1.0 / math.sqrt(HEAD_DIM)
    me = lax.axis_index("ctx")
    heads = range(OWNED)
    every = [head_cols(head) for head in heads]
    for distance, return_ref in enumerate(return_refs):
        placed_ref[me ^ distance] = return_ref[...]
    once = [place_ref[:, head_cols(count + head)] for head in heads]
    attn_parts = [
        contract(placed_ref[head, 3 * picked : 4 * picked], once[head][:, :picked], 0, 1)
        for head in heads
    ]
    log_parts = [
        contract(placed_ref[head, 6 * picked : 6 * picked + STAT_TILES], once[head], 1, 1)
        for head in heads
    ]
    factors, normeds, grad_lows, inners = [], [], [], []
    for head in heads:
        seen = masks_ref[TILE + head : TILE + head + 1, :tokens] > 0.5
        top_score, total = stats_ref[head : head + 1, :], stats_ref[TILE + head : TILE + head + 1, :]
        log_total = jnp.where(seen, joined_row(log_parts[head], 0), top_score + jnp.log(total))
        factors.append(jnp.exp(top_score - log_total))
        attn = jnp.where(seen, attn_parts[head], out_ref[:, every[head]].astype(WIDE))
        normed, _, grad_low, inner = norm_backward(attn, grad_norm_ref[:, every[head]])
        normeds.append(normed)
        grad_lows.append(grad_low)
        inners.append(inner)
    prob_grads = [contract(v_ref[0, :, every[head]], grad_lows[head], 1, 0) for head in heads]
    softs = [expo_ref[:, every[head]].astype(WIDE) * factors[head] for head in heads]
    for head in heads:
        cols = every[head]
        grad_low_ref[:, cols] = grad_lows[head]
        soft_ref[:, cols] = softs[head].astype(LOW)
        score_grad_ref[:, cols] = (
            softs[head] * (prob_grads[head] - inners[head]) * score_scale
        ).astype(LOW)
        attended_ref[:, cols] = (normeds[head].T * gain_ref[:, cols]).astype(LOW)


def finish_kernel(top_step, *refs):
    gain_refs, (q_ref, k_ref, place_ref), refs = refs[:2], refs[2:5], refs[5:]
    mixed_refs, (last_attended_ref, last_dq_ref, last_dk_ref, last_dv_ref) = refs[:5], refs[5:9]
    return_refs, refs = nearest_first(refs[9 : 9 + SPAN]), refs[9 + SPAN :]
    mixed_ref, grad_low_ref, soft_ref, score_grad_ref, returned_ref = mixed_refs
    attended_ref, dq_ref, dk_ref, dv_ref, gain_out_ref = refs
    tokens, width = q_ref.shape[1:]
    picked = sum(picked_counts(tokens, top_step))
    heads = range(OWNED)
    every = [head_cols(head) for head in heads]
    gain_out_ref[...] = (gain_refs[0][...] + gain_refs[1][...]).reshape(gain_out_ref.shape)
    score_grads = [score_grad_ref[:, cols] for cols in every]
    dqs = [contract(score_grads[head], k_ref[0, :, every[head]], 0, 0) for head in heads]
    placed = [
        contract(
            place_ref[:, pl.ds(head * HEAD_DIM, picked)],
            jnp.concatenate(
                [returned_ref[head, block * picked : (block + 1) * picked] for block in range(3)], 1
            ),
            1,
            0,
        )
        for head in heads
    ]
    dks = [contract(score_grads[head], q_ref[0, :, every[head]], 1, 0) for head in heads]
    dvs = [contract(soft_ref[:, cols], grad_low_ref[:, cols], 1, 1) for cols in every]
    last = width // HEAD_DIM - 1
    total = sum(ref[4 * picked : 6 * picked].astype(WIDE) for ref in return_refs[1:]).astype(LOW)
    rows = contract(
        place_ref[:, pl.ds(last * HEAD_DIM, picked)],
        jnp.concatenate([total[:picked], total[picked:]], 1),
        1,
        0,
    )
    for head in heads:
        cols = every[head]
        attended_ref[0, :, cols] = mixed_ref[:, cols]
        for which, (block, out_block_ref) in enumerate(
            ((dqs[head], dq_ref), (dks[head], dk_ref), (dvs[head], dv_ref))
        ):
            part = placed[head][:, which * HEAD_DIM : (which + 1) * HEAD_DIM]
            out_block_ref[0, :, cols] = (block + part).astype(LOW)
    cols = head_cols(last)
    attended_ref[0, :, cols] = last_attended_ref[...]
    dq_ref[0, :, cols] = last_dq_ref[...]
    dk_ref[0, :, cols] = (last_dk_ref[...] + rows[:, :HEAD_DIM]).astype(LOW)
    dv_ref[0, :, cols] = (last_dv_ref[...] + rows[:, HEAD_DIM:]).astype(LOW)


def across(block, axis, distance):
    route = [(place, place ^ distance) for place in range(lax.axis_size(axis))]
    return lax.ppermute(block, axis, route)


def to_peers(blocks):
    return [across(blocks[distance - 1], "ctx", distance) for distance in START_ORDER]


def call(kernel, name, operands, results, microseconds, vmem=PLAIN_VMEM, scratch=()):
    return pl.pallas_call(
        kernel,
        out_shape=results,
        in_specs=[SMEM_SPEC if block.dtype == jnp.int32 else VMEM_SPEC for block in operands],
        out_specs=[VMEM_SPEC] * len(results),
        scratch_shapes=scratch,
        compiler_params=pltpu.CompilerParams(vmem_limit_bytes=vmem),
        cost_estimate=pl.CostEstimate(
            flops=int(microseconds * 10**9), bytes_accessed=0, transcendentals=0
        ),
        name=name,
    )(*operands)


def one_segment_shards(queries, keys, values, grad_y, out_gain, offsets):
    tokens, width = queries.shape[1:]
    heads = width // HEAD_DIM
    top_step = lax.axis_size("ctx")
    picked = sum(picked_counts(tokens, top_step))
    shape = jax.ShapeDtypeStruct
    row_block = shape((1, tokens, width), LOW)
    low_block, wide_block = shape((tokens, width), LOW), shape((tokens, width), WIDE)
    low_head, wide_head = shape((tokens, HEAD_DIM), LOW), shape((tokens, HEAD_DIM), WIDE)
    gain_block = shape((1, width), WIDE)
    stats_block = shape((2 * TILE, tokens), WIDE)
    payload = shape((7 * picked + STAT_TILES, HEAD_DIM), LOW)
    answer = shape((6 * picked + STAT_TILES, HEAD_DIM), LOW)
    bind = functools.partial
    gain_row = out_gain.reshape(1, width)
    own, *sent, expo, base_out, stats = call(
        bind(pack_kernel, top_step),
        "pack",
        (offsets, queries, keys, values, grad_y),
        [payload] * SPAN + [low_block, low_block, stats_block],
        1,
        vmem=PACK_VMEM,
        scratch=[pltpu.VMEM((OWNED, *payload.shape), LOW)],
    )
    received = to_peers(sent)
    grad_norm, gain_base, place, masks = call(
        bind(prepare_kernel, top_step),
        "prepare",
        (offsets, grad_y, gain_row, base_out),
        [
            wide_block,
            gain_block,
            shape((tokens, 2 * width), LOW),
            shape((2 * TILE, 2 * tokens), WIDE),
        ],
        2,
    )
    normed, grad_low, score_grad, kept, own_answer, *answers = call(
        bind(owner_kernel, top_step),
        "owner",
        (queries, gain_row, base_out, grad_norm, stats, gain_base, masks, own, *received),
        [
            wide_head,
            low_head,
            shape((PEERS * picked, HEAD_DIM), LOW),
            shape((TILE, tokens), WIDE),
        ]
        + [answer] * SPAN,
        3,
    )
    returned = to_peers(answers)
    last_results = call(
        bind(last_head_kernel, top_step),
        "last_head",
        (queries, keys, values, gain_row, expo, normed, grad_low, score_grad, kept, *received),
        [low_head, low_head, wide_head, wide_head],
        20,
    )
    (gain_sum,) = call(bind(gain_kernel, picked), "gain", (own_answer, *returned), [gain_block], 1)
    gain_rest = across(gain_sum, "dp", 1)
    mixed_block = shape((tokens, OWNED * HEAD_DIM), LOW)
    mixed = call(
        bind(mix_kernel, top_step),
        "mix",
        (
            values,
            gain_row,
            expo,
            base_out,
            grad_norm,
            stats,
            place,
            masks,
            own_answer,
            *returned,
        ),
        [mixed_block] * 4 + [shape((OWNED, *answer.shape), LOW)],
        20,
    )
    attended, query_grad, key_grad, value_grad, gain_grad = call(
        bind(finish_kernel, top_step),
        "finish",
        (
            gain_sum,
            gain_rest,
            queries,
            keys,
            place,
            *mixed,
            *last_results,
            own_answer,
            *returned,
        ),
        [row_block] * 4 + [shape((width,), WIDE)],
        1,
    )
    return attended, query_grad, key_grad, value_grad, gain_grad


def shards(*operands):
    one_segment = lax.axis_size("ctx") == SPAN
    if one_segment and operands[0].shape[2] == (OWNED + 1) * HEAD_DIM:
        return one_segment_shards(*operands)
    return general_shards(*operands)


def solution(mesh):
    in_specs = (
        P("dp", "ctx", "head"),
        P("dp", "ctx", "head"),
        P("dp", "ctx", "head"),
        P("dp", "ctx", "head"),
        P("head"),
        P(None, "head"),
    )
    out_specs = (
        P("dp", "ctx", "head"),
        P("dp", "ctx", "head"),
        P("dp", "ctx", "head"),
        P("dp", "ctx", "head"),
        P("head"),
    )
    return jax.shard_map(shards, mesh=mesh, in_specs=in_specs, out_specs=out_specs, check_vma=False)
```

```python
import functools
import math

import jax
import jax.numpy as jnp
from jax import lax
from jax.experimental import pallas as pl
from jax.experimental.pallas import tpu as pltpu
from jax.sharding import PartitionSpec as P

HEAD_DIM = 128
SPAN = 4
R1 = 8


EPS = 1e-06


def swapped(block, axis, bit):
    count = lax.axis_size(axis)
    route = []
    for low in range(count):
        high = low | 1 << bit
        if high != low and high < count:
            route += [(low, high), (high, low)]
    return lax.ppermute(block, axis, route)


def pick_rows(source_rows, dilation, shifts):
    row_count, head_count, head_width = source_rows.shape
    grouped = source_rows.reshape(row_count // dilation, dilation, head_count, head_width)
    hit_mask = jnp.arange(dilation, dtype=jnp.int32).reshape(1, dilation, 1, 1) == shifts.reshape(
        1, 1, head_count, 1
    )
    chosen = jnp.where(hit_mask, grouped, jnp.zeros((), source_rows.dtype))
    return jnp.sum(chosen, axis=1, dtype=source_rows.dtype)


def place_rows(row_values, dilation, shifts):
    row_count, head_count, head_width = row_values.shape
    hit_mask = jnp.arange(dilation, dtype=jnp.int32).reshape(1, dilation, 1, 1) == shifts.reshape(
        1, 1, head_count, 1
    )
    spread = jnp.where(hit_mask, row_values[:, None], jnp.zeros((), row_values.dtype))
    return spread.reshape(row_count * dilation, head_count, head_width)


def level_scores(q_rows, k_rows):
    score_scale = 1.0 / math.sqrt(q_rows.shape[-1])
    return (
        jnp.einsum("qhe,khe->hqk", q_rows, k_rows, preferred_element_type=jnp.float32) * score_scale
    )


def attend(q_rows, k_rows, v_rows):
    scores = level_scores(q_rows, k_rows)
    row_max = jnp.max(scores, axis=-1, keepdims=True)
    log_total = row_max[..., 0] + jnp.log(jnp.sum(jnp.exp(scores - row_max), axis=-1))
    soft_rows = jnp.exp(scores - log_total[..., None]).astype(jnp.bfloat16)
    level_out = jnp.einsum("hqk,khe->qhe", soft_rows, v_rows, preferred_element_type=jnp.float32)
    return (level_out, log_total.T)


def score_grads(q_rows, k_rows, v_rows, log_total, grad_low, row_shift):
    score_scale = 1.0 / math.sqrt(q_rows.shape[-1])
    scores = level_scores(q_rows, k_rows)
    exact_soft = jnp.exp(scores - log_total.T[..., None])
    prob_grad = jnp.einsum("qhe,khe->hqk", grad_low, v_rows, preferred_element_type=jnp.float32)
    score_grad = (exact_soft * (prob_grad + row_shift.T[..., None]) * score_scale).astype(
        jnp.bfloat16
    )
    return (score_grad, exact_soft.astype(jnp.bfloat16))


def key_parts(score_grad, soft_low, q_rows, grad_low):
    k_part = jnp.einsum("hqk,qhe->khe", score_grad, q_rows, preferred_element_type=jnp.float32)
    v_part = jnp.einsum("hqk,qhe->khe", soft_low, grad_low, preferred_element_type=jnp.float32)
    return (k_part, v_part)


def query_part(score_grad, k_rows):
    return jnp.einsum("hqk,khe->qhe", score_grad, k_rows, preferred_element_type=jnp.float32)


def general_shards(queries, keys, values, grad_y, out_gain, offsets):
    tokens = queries.shape[1]
    flat_width = queries.shape[2]
    head_count = flat_width // HEAD_DIM
    row_shape = (tokens, head_count, HEAD_DIM)
    q_own = queries[0].reshape(row_shape)
    k_own = keys[0].reshape(row_shape)
    v_own = values[0].reshape(row_shape)
    ctx_size = lax.axis_size("ctx")
    span_bits = SPAN.bit_length() - 1
    my_place = lax.axis_index("ctx")
    mid_shift = offsets[0]
    top_shift = offsets[1]
    positions = jnp.arange(tokens, dtype=jnp.int32)
    mid_hit = (positions % R1)[:, None] == mid_shift[None, :]
    top_hit = (positions % ctx_size)[:, None] == top_shift[None, :]
    mid_q = pick_rows(q_own, R1, mid_shift)
    mid_k = pick_rows(k_own, R1, mid_shift)
    mid_v = pick_rows(v_own, R1, mid_shift)
    top_q = pick_rows(q_own, ctx_size, top_shift)
    top_k = pick_rows(k_own, ctx_size, top_shift)
    top_v = pick_rows(v_own, ctx_size, top_shift)
    mid_keys = mid_k.reshape(-1, flat_width)
    mid_vals = mid_v.reshape(-1, flat_width)
    top_keys = top_k.reshape(-1, flat_width)
    top_vals = top_v.reshape(-1, flat_width)

    def append_peer(mine, received, level_bit):
        upper_side = my_place >> level_bit & 1 == 1
        return jnp.where(
            upper_side, jnp.concatenate([received, mine], 0), jnp.concatenate([mine, received], 0)
        )

    for level_bit in range(span_bits):
        received = swapped((mid_keys, mid_vals), "ctx", level_bit)
        mid_keys = append_peer(mid_keys, received[0], level_bit)
        mid_vals = append_peer(mid_vals, received[1], level_bit)
    top_keys, top_vals = (
        lax.all_gather(top_keys, "ctx", axis=0, tiled=True),
        lax.all_gather(top_vals, "ctx", axis=0, tiled=True),
    )
    mid_keys = mid_keys.reshape(-1, head_count, HEAD_DIM)
    mid_vals = mid_vals.reshape(-1, head_count, HEAD_DIM)
    top_keys = top_keys.reshape(-1, head_count, HEAD_DIM)
    top_vals = top_vals.reshape(-1, head_count, HEAD_DIM)
    base_out, base_total = attend(q_own, k_own, v_own)
    mid_out, mid_total = attend(mid_q, mid_keys, mid_vals)
    top_out, top_total = attend(top_q, top_keys, top_vals)
    mid_full = place_rows(mid_total[..., None], R1, mid_shift)[..., 0]
    top_full = place_rows(top_total[..., None], ctx_size, top_shift)[..., 0]
    row_max = jnp.maximum(base_total, jnp.where(mid_hit, mid_full, base_total))
    row_max = jnp.maximum(row_max, jnp.where(top_hit, top_full, base_total))
    base_expo = jnp.exp(base_total - row_max)
    mid_expo = jnp.where(mid_hit, jnp.exp(mid_full - row_max), 0.0)
    top_expo = jnp.where(top_hit, jnp.exp(top_full - row_max), 0.0)
    denom = base_expo + mid_expo + top_expo
    base_share = base_expo / denom
    mid_share = mid_expo / denom
    top_share = top_expo / denom
    attn = (
        base_share[..., None] * base_out
        + mid_share[..., None] * place_rows(mid_out, R1, mid_shift)
        + top_share[..., None] * place_rows(top_out, ctx_size, top_shift)
    )
    inv_rms = lax.rsqrt(jnp.mean(attn * attn, axis=-1, keepdims=True) + EPS)
    normed = attn * inv_rms
    gain_rows = out_gain.reshape(head_count, HEAD_DIM)
    attended = (normed * gain_rows).astype(jnp.bfloat16).reshape(1, tokens, flat_width)
    grad_full = grad_y[0].reshape(row_shape).astype(jnp.float32)
    gain_part = jnp.sum(grad_full * normed, axis=0).reshape(flat_width)
    gain_grad = lax.psum(gain_part, ("dp", "ctx"))
    grad_norm = grad_full * gain_rows
    grad_attn = inv_rms * (
        grad_norm - normed * jnp.mean(grad_norm * normed, axis=-1, keepdims=True)
    )
    inner = jnp.sum(grad_attn * attn, axis=-1)
    base_low = (base_share[..., None] * grad_attn).astype(jnp.bfloat16)
    base_shift = -(base_share * inner)
    base_grad, base_soft = score_grads(q_own, k_own, v_own, base_total, base_low, base_shift)
    base_dq = query_part(base_grad, k_own)
    base_dk, base_dv = key_parts(base_grad, base_soft, q_own, base_low)
    mid_sel = pick_rows(mid_share[..., None], R1, mid_shift)[..., 0]
    mid_low = (mid_sel[..., None] * pick_rows(grad_attn, R1, mid_shift)).astype(jnp.bfloat16)
    mid_row_shift = -(mid_sel * pick_rows(inner[..., None], R1, mid_shift)[..., 0])
    mid_grad, mid_soft = score_grads(mid_q, mid_keys, mid_vals, mid_total, mid_low, mid_row_shift)
    mid_dq = query_part(mid_grad, mid_keys)
    mid_dk, mid_dv = key_parts(mid_grad, mid_soft, mid_q, mid_low)
    mid_dk = mid_dk.reshape(-1, flat_width)
    mid_dv = mid_dv.reshape(-1, flat_width)
    for level_bit in reversed(range(span_bits)):
        half_rows = mid_dk.shape[0] // 2
        upper_side = my_place >> level_bit & 1 == 1
        keep_k = jnp.where(upper_side, mid_dk[half_rows:], mid_dk[:half_rows])
        keep_v = jnp.where(upper_side, mid_dv[half_rows:], mid_dv[:half_rows])
        send_k = jnp.where(upper_side, mid_dk[:half_rows], mid_dk[half_rows:])
        send_v = jnp.where(upper_side, mid_dv[:half_rows], mid_dv[half_rows:])
        received = (
            swapped(send_k.astype(jnp.bfloat16), "ctx", level_bit).astype(send_k.dtype),
            swapped(send_v.astype(jnp.bfloat16), "ctx", level_bit).astype(send_v.dtype),
        )
        mid_dk = keep_k + received[0]
        mid_dv = keep_v + received[1]
    mid_dk = mid_dk.reshape(-1, head_count, HEAD_DIM)
    mid_dv = mid_dv.reshape(-1, head_count, HEAD_DIM)
    top_sel = pick_rows(top_share[..., None], ctx_size, top_shift)[..., 0]
    top_low = (top_sel[..., None] * pick_rows(grad_attn, ctx_size, top_shift)).astype(jnp.bfloat16)
    top_row_shift = -(top_sel * pick_rows(inner[..., None], ctx_size, top_shift)[..., 0])
    top_grad, top_soft = score_grads(top_q, top_keys, top_vals, top_total, top_low, top_row_shift)
    top_dq = query_part(top_grad, top_keys)
    gathered_dk, gathered_dv = key_parts(top_grad, top_soft, top_q, top_low)
    summed = (
        lax.psum_scatter(
            gathered_dk.reshape(-1, flat_width), "ctx", scatter_dimension=0, tiled=True
        ),
        lax.psum_scatter(
            gathered_dv.reshape(-1, flat_width), "ctx", scatter_dimension=0, tiled=True
        ),
    )
    top_dk = summed[0].reshape(-1, head_count, HEAD_DIM)
    top_dv = summed[1].reshape(-1, head_count, HEAD_DIM)
    query_grad = (
        base_dq + place_rows(mid_dq, R1, mid_shift) + place_rows(top_dq, ctx_size, top_shift)
    )
    key_grad = base_dk + place_rows(mid_dk, R1, mid_shift) + place_rows(top_dk, ctx_size, top_shift)
    value_grad = (
        base_dv + place_rows(mid_dv, R1, mid_shift) + place_rows(top_dv, ctx_size, top_shift)
    )
    out_shape = (1, tokens, flat_width)
    return (
        attended,
        query_grad.astype(jnp.bfloat16).reshape(out_shape),
        key_grad.astype(jnp.bfloat16).reshape(out_shape),
        value_grad.astype(jnp.bfloat16).reshape(out_shape),
        gain_grad,
    )


VMEM_SPEC = pl.BlockSpec(memory_space=pltpu.VMEM)
PEERS = SPAN - 1
OWNED = SPAN
TILE = 8
STAT_TILES = 2 * TILE
PIECES = 3
NEVER = -1e30
START_ORDER = (3, 1, 2)
LOW = jnp.bfloat16
WIDE = jnp.float32
PACK_VMEM = 65408 * 1024
PLAIN_VMEM = 16 * 1024 * 1024


def contract(left, right, left_dim, right_dim):
    return lax.dot_general(
        left, right, (((left_dim,), (right_dim,)), ((), ())), preferred_element_type=WIDE
    )


def head_cols(head):
    return pl.ds(head * HEAD_DIM, HEAD_DIM)


def picked_counts(tokens, top_step):
    return tokens // top_step, tokens // R1


def offset_of(offsets_ref, level, head):
    return offsets_ref[level : level + 1, head : head + 1]


def pick_matrix(offsets_ref, head, tokens, top_step, picked_axis):
    top_rows, _ = picked_counts(tokens, top_step)
    row = lax.broadcasted_iota(jnp.int32, (tokens, tokens), picked_axis)
    position = lax.broadcasted_iota(jnp.int32, (tokens, tokens), 1 - picked_axis)
    wanted = jnp.where(
        row < top_rows,
        row * top_step + offset_of(offsets_ref, 1, head),
        (row - top_rows) * R1 + offset_of(offsets_ref, 0, head),
    )
    return jnp.where(position == wanted, 1.0, 0.0).astype(LOW)


def rolled(row, shift):
    return pltpu.roll(row, shift % row.shape[1], 1)


def lane_window(row, start, count):
    lane = lax.broadcasted_iota(jnp.int32, row.shape, 1)
    return jnp.where((lane >= start) & (lane < start + count), row, 0.0)


def hit_row(offset, step, tokens):
    position = lax.broadcasted_iota(jnp.int32, (1, tokens), 1)
    return jnp.where(position % step == offset, 1.0, 0.0)


def piece_rows(row, others=None):
    pieces = []
    for _ in range(PIECES):
        piece = row.astype(LOW).astype(WIDE)
        pieces.append(piece)
        row = row - piece
    if others is None:
        others = jnp.zeros((TILE - PIECES, row.shape[1]), WIDE)
    return jnp.concatenate(pieces + [others], 0)


def gain_pieces(rows):
    high = rows.astype(LOW)
    return high, (rows - high.astype(WIDE)).astype(LOW)


def joined_row(rows, first):
    total = rows[first : first + 1]
    for piece in range(1, PIECES):
        total = total + rows[first + piece : first + piece + 1]
    return total


def gain_row_of(ones, product):
    high, rest = gain_pieces(product)
    return (contract(ones, high, 1, 1) + contract(ones, rest, 1, 1))[:1]


def column_mean(block):
    return jnp.mean(block, axis=0, keepdims=True)


def norm_backward(attn, grad_norm):
    inv_rms = lax.rsqrt(column_mean(attn * attn) + EPS)
    normed = attn * inv_rms
    product = grad_norm * normed
    grad_attn = inv_rms * (grad_norm - normed * column_mean(product))
    inner = jnp.sum(grad_attn * attn, axis=0, keepdims=True)
    return normed, product, grad_attn.astype(LOW), inner


def nearest_first(refs):
    by_distance = dict(zip(START_ORDER, refs[1:]))
    return [refs[0], *[by_distance[distance] for distance in range(1, SPAN)]]


def pack_kernel(top_step, offsets_ref, q_ref, k_ref, v_ref, grad_ref, *refs):
    payload_refs, (expo_ref, out_ref, stats_ref, held_ref) = refs[:SPAN], refs[SPAN:]
    tokens, width = q_ref.shape[1:]
    heads = range(width // HEAD_DIM)
    owned = range(OWNED)
    me = lax.axis_index("ctx")
    picked = sum(picked_counts(tokens, top_step))
    score_scale = 1.0 / math.sqrt(HEAD_DIM)
    q_rows, k_rows, v_rows, grad_rows = [
        [ref[0, :, head_cols(head)] for head in heads] for ref in (q_ref, k_ref, v_ref, grad_ref)
    ]
    picks = [pick_matrix(offsets_ref, head, tokens, top_step, 0) for head in heads]
    scores = [contract(k_rows[head], q_rows[head], 1, 1) * score_scale for head in heads]
    moved = [
        contract(
            picks[head][:picked],
            jnp.concatenate([q_rows[head], k_rows[head], v_rows[head], grad_rows[head]], 1),
            1,
            0,
        ).astype(LOW)
        for head in owned
    ]
    shared = [
        contract(
            picks[head][:picked], jnp.concatenate([k_rows[head], v_rows[head]], 1), 1, 0
        ).astype(LOW)
        for head in heads[OWNED:]
    ]
    top_scores = [jnp.max(block, axis=0, keepdims=True) for block in scores]
    expos = [jnp.exp(scores[head] - top_scores[head]) for head in heads]
    for head in heads[OWNED:]:
        key_row = lax.broadcasted_iota(jnp.int32, (tokens, 1), 0)
        times = 1.0
        for level, step in ((0, R1), (1, top_step)):
            offset = offset_of(offsets_ref, level, head)
            hit_column = jnp.where(key_row % step == offset, 1.0, 0.0)
            times = times + hit_column * hit_row(offset, step, tokens)
        expos[head] = times * expos[head]
    expo_lows = [expo.astype(LOW) for expo in expos]
    outs = [contract(v_rows[head], expo_lows[head], 0, 0) for head in heads]
    totals = [jnp.sum(expo, axis=0, keepdims=True) for expo in expos]
    for head in heads:
        expo_ref[:, head_cols(head)] = expo_lows[head]
        stats_ref[head : head + 1, :] = top_scores[head]
        stats_ref[TILE + head : TILE + head + 1, :] = totals[head]
    for head in owned:
        outs[head] = outs[head] * (1.0 / totals[head])
    outs = [out.astype(LOW) for out in outs]
    picked_outs = [
        contract(picks[head][:picked], outs[head], 1, 1).astype(LOW) for head in owned
    ]
    for head in heads:
        out_ref[:, head_cols(head)] = outs[head]
    for head in owned:
        pieces = piece_rows(top_scores[head] + jnp.log(totals[head])).astype(LOW)
        stat_rows = contract(pieces, picks[head], 1, 1)
        blocks = [moved[head][:, block * HEAD_DIM : (block + 1) * HEAD_DIM] for block in range(4)]
        blocks.append(picked_outs[head])
        blocks += [shared[0][:, :HEAD_DIM], shared[0][:, HEAD_DIM:]]
        blocks.append(jnp.concatenate([stat_rows, jnp.zeros_like(stat_rows)], 0).astype(LOW))
        held_ref[head] = jnp.concatenate(blocks, 0)
    for distance, payload_ref in enumerate(payload_refs):
        payload_ref[...] = held_ref[me ^ distance]


def prepare_kernel(top_step, offsets_ref, grad_ref, gain_ref, out_ref, *refs):
    grad_norm_ref, gain_part_ref, place_ref, masks_ref = refs
    tokens, width = grad_ref.shape[1:]
    heads = range(width // HEAD_DIM)
    top_rows = tokens // top_step
    ones = jnp.ones((TILE, tokens), LOW)
    column = lax.broadcasted_iota(jnp.int32, (tokens, tokens), 1)
    gain_part_ref[...] = jnp.zeros(gain_part_ref.shape, WIDE)
    me = lax.axis_index("ctx")
    mid_rows = tokens // R1
    top_all, queries = SPAN * top_rows, SPAN * (top_rows + mid_rows)
    mid_offset, top_offset = [
        sum(
            jnp.where(me == head, offset_of(offsets_ref, level, head), 0) for head in range(OWNED)
        )
        for level in (0, 1)
    ]
    lane = lax.broadcasted_iota(jnp.int32, (1, queries), 1)
    is_top = jnp.where(lane < top_all, 1.0, 0.0)
    top_in_mid = jnp.where(((lane % top_rows) * top_step + top_offset) % R1 == mid_offset, 1.0, 0.0)
    both_flag = jnp.where(mid_offset % top_step == top_offset, 1.0, 0.0)
    sees_top = is_top + (1.0 - is_top) * both_flag
    sees_mid = is_top * top_in_mid + (1.0 - is_top)
    masks_ref[0:1, :queries] = (1.0 - sees_top) * NEVER
    masks_ref[1:2, :queries] = (1.0 - sees_mid) * NEVER
    masks_ref[2:3, :queries] = is_top + (1.0 - is_top) * (1.0 - both_flag)
    last = len(heads) - 1
    for row, (level, step) in enumerate(((1, top_step), (0, R1))):
        hits = hit_row(offset_of(offsets_ref, level, last), step, tokens)
        masks_ref[3 + row : 4 + row, :tokens] = (1.0 - hits) * NEVER
    grad_norms = [
        (grad_ref[0, :, head_cols(head)].astype(WIDE) * gain_ref[:, head_cols(head)]).T
        for head in heads
    ]
    for head in heads:
        cols = head_cols(head)
        grad_norm_ref[:, cols] = grad_norms[head]
        picks = pick_matrix(offsets_ref, head, tokens, top_step, 1)
        place_ref[:, cols] = picks
    for head in range(OWNED):
        cols = head_cols(head)
        mid_offset, top_offset = [offset_of(offsets_ref, level, head) for level in (0, 1)]
        seen = jnp.maximum(
            hit_row(top_offset, top_step, tokens), hit_row(mid_offset, R1, tokens)
        )
        masks_ref[TILE + head : TILE + head + 1, :tokens] = seen
        attn = out_ref[:, cols].astype(WIDE)
        normed = attn * lax.rsqrt(column_mean(attn * attn) + EPS)
        product = grad_norms[head] * normed * (1.0 - seen)
        gain_part_ref[:, cols] = gain_row_of(ones, product) / gain_ref[:, cols]
        both = mid_offset % top_step == top_offset
        kept = jnp.where(column < top_rows, 1.0, jnp.where(both, 0.0, 1.0)).astype(LOW)
        picks = pick_matrix(offsets_ref, head, tokens, top_step, 1)
        place_ref[:, head_cols(len(heads) + head)] = picks * kept


def owner_kernel(top_step, q_ref, gain_ref, out_ref, grad_norm_ref, *refs):
    stats_ref, gain_base_ref, masks_ref = refs[:3]
    payload_refs, refs = nearest_first(refs[3 : 3 + SPAN]), refs[3 + SPAN :]
    normed_ref, grad_low_ref, score_grad_ref, kept_ref = refs[:4]
    return_refs = refs[4:]
    tokens = q_ref.shape[1]
    heads = q_ref.shape[2] // HEAD_DIM
    top_rows, mid_rows = picked_counts(tokens, top_step)
    picked = top_rows + mid_rows
    top_all, mid_all = SPAN * top_rows, SPAN * mid_rows
    queries = top_all + mid_all
    score_scale = 1.0 / math.sqrt(HEAD_DIM)
    me = lax.axis_index("ctx")
    ones = jnp.ones((TILE, tokens), LOW)

    def by_level(block):
        start = block * picked
        return jnp.concatenate(
            [ref[start : start + top_rows] for ref in payload_refs]
            + [ref[start + top_rows : start + picked] for ref in payload_refs],
            0,
        )

    def per_level(top_row, mid_row):
        return jnp.concatenate(
            [
                jnp.broadcast_to(top_row, (top_all, queries)),
                jnp.broadcast_to(mid_row, (mid_all, queries)),
            ],
            0,
        )

    q_rows, k_rows, v_rows, grad_rows, base_rows = [by_level(block) for block in range(5)]
    stat_start = 7 * picked
    logs = [
        joined_row(ref[stat_start : stat_start + STAT_TILES].astype(WIDE), 0)
        for ref in payload_refs
    ]
    base_top_log = sum(
        rolled(lane_window(log, 0, top_rows), slot * top_rows) for slot, log in enumerate(logs)
    )
    base_mid_log = sum(
        rolled(lane_window(log, top_rows, mid_rows), slot * mid_rows - top_rows)
        for slot, log in enumerate(logs)
    )
    base_log = jnp.concatenate([base_top_log, base_mid_log[:, :mid_all]], 1)
    gain_row = jnp.zeros((1, HEAD_DIM), WIDE)
    for head in range(OWNED):
        gain_row = gain_row + jnp.where(me == head, 1.0, 0.0) * gain_ref[:, head_cols(head)]
    lane = lax.broadcasted_iota(jnp.int32, (1, queries), 1)
    is_top = jnp.where(lane < top_all, 1.0, 0.0)
    bias = per_level(masks_ref[0:1, :queries], masks_ref[1:2, :queries])
    last = heads - 1
    cols = head_cols(last)
    peers = payload_refs[1:]
    q_last = q_ref[0, :, cols]
    k_peers = jnp.concatenate([ref[5 * picked : 6 * picked] for ref in peers], 0)
    v_peers = jnp.concatenate([ref[6 * picked : 7 * picked] for ref in peers], 0)
    last_biases = [
        jnp.broadcast_to(masks_ref[row : row + 1, :tokens], (count, tokens))
        for row, count in ((3, top_rows), (4, mid_rows))
    ]
    scores = contract(k_rows, q_rows, 1, 1) * score_scale + bias
    scores_last = contract(k_peers, q_last, 1, 1) * score_scale + jnp.concatenate(
        last_biases * PEERS, 0
    )
    base_attn = base_rows.astype(WIDE).T
    grad_norm = (grad_rows.astype(WIDE) * gain_row).T
    top_score = jnp.maximum(base_log, jnp.max(scores, axis=0, keepdims=True))
    base_top, base_total = stats_ref[last : last + 1, :], stats_ref[TILE + last : TILE + last + 1, :]
    top_last = jnp.maximum(base_top, jnp.max(scores_last, axis=0, keepdims=True))
    expo = jnp.exp(scores - top_score)
    expo_last = jnp.exp(scores_last - top_last)
    factor = jnp.exp(base_log - top_score)
    factor_last = jnp.exp(base_top - top_last)
    total = factor + jnp.sum(expo, axis=0, keepdims=True)
    total_last = factor_last * base_total + jnp.sum(expo_last, axis=0, keepdims=True)
    inv_total, inv_last = 1.0 / total, 1.0 / total_last
    soft, soft_last = expo * inv_total, expo_last * inv_last
    soft_low, soft_last_low = soft.astype(LOW), soft_last.astype(LOW)
    factor_last = factor_last * inv_last
    attn = (factor * inv_total) * base_attn + contract(v_rows, soft_low, 0, 0)
    attn_last = factor_last * out_ref[:, cols].astype(WIDE) + contract(v_peers, soft_last_low, 0, 0)
    _, product, grad_low, inner = norm_backward(attn, grad_norm)
    normed_last, product_last, grad_last_low, inner_last = norm_backward(
        attn_last, grad_norm_ref[:, cols]
    )
    spans = (slice(0, top_all), slice(top_all, queries))
    prob_grads = [contract(v_rows[span], grad_low[:, span], 1, 0) for span in spans]
    prob_grad_last = contract(v_peers, grad_last_low, 1, 0)
    score_grads = [
        (soft[span, span] * (prob_grad - inner[:, span]) * score_scale).astype(LOW)
        for span, prob_grad in zip(spans, prob_grads)
    ]
    score_grad_last = (soft_last * (prob_grad_last - inner_last) * score_scale).astype(LOW)
    dks = [
        contract(score_grad, q_rows[span], 1, 0).astype(LOW)
        for span, score_grad in zip(spans, score_grads)
    ]
    dk_last = contract(score_grad_last, q_last, 1, 0).astype(LOW)
    dvs = [
        contract(soft_low[span, span], grad_low[:, span], 1, 1).astype(LOW) for span in spans
    ]
    dv_last = contract(soft_last_low, grad_last_low, 1, 1).astype(LOW)
    dqs = [
        contract(score_grad, k_rows[span], 0, 0).astype(LOW)
        for span, score_grad in zip(spans, score_grads)
    ]
    attn_rows = attn.T.astype(LOW)
    attn_parts = [attn_rows[span] for span in spans]
    log_total = top_score + jnp.log(total)
    padding = jnp.zeros((1, top_all - mid_all), WIDE)
    once = masks_ref[2:3, :queries]
    ones_all = jnp.ones((TILE, queries), LOW)
    own_gain = gain_row_of(ones_all, product * once) / gain_row
    gain_rows = [
        gain_base_ref[:, head_cols(head)] + jnp.where(me == head, 1.0, 0.0) * own_gain
        for head in range(OWNED)
    ]
    gain_rows.append(gain_row_of(ones, product_last) / gain_ref[:, cols])
    gain_high, gain_rest = [
        rows.astype(WIDE) for rows in gain_pieces(jnp.concatenate(gain_rows, 0))
    ]
    top_log, mid_log = log_total[:, :top_all], jnp.concatenate(
        [log_total[:, top_all:], padding], 1
    )
    empty = jnp.zeros((PIECES, HEAD_DIM), WIDE)
    for distance, return_ref in enumerate(return_refs):
        blocks = []
        for top_block, mid_block in (dqs, dks, dvs, attn_parts):
            blocks.append(top_block[distance * top_rows : (distance + 1) * top_rows])
            blocks.append(mid_block[distance * mid_rows : (distance + 1) * mid_rows])
        start = max(distance - 1, 0) * picked
        blocks += [dk_last[start : start + picked], dv_last[start : start + picked]]
        log_row = lane_window(rolled(top_log, -distance * top_rows), 0, top_rows) + lane_window(
            rolled(mid_log, top_rows - distance * mid_rows), top_rows, mid_rows
        )
        log_rows = [piece_rows(log_row, gain_high), empty, gain_rest]
        blocks.append(jnp.concatenate(log_rows, 0).astype(LOW))
        return_ref[...] = jnp.concatenate(blocks, 0)
    normed_ref[...] = normed_last
    grad_low_ref[...] = grad_last_low
    score_grad_ref[...] = score_grad_last
    kept_ref[0:1, :] = factor_last
    kept_ref[1:2, :] = inner_last


def last_head_kernel(top_step, q_ref, k_ref, v_ref, gain_ref, expo_ref, *refs):
    normed_ref, grad_low_ref, peer_score_grad_ref, kept_ref, *peers = refs[: 4 + PEERS]
    peers = nearest_first([None, *peers])[1:]
    attended_ref, dq_ref, dk_ref, dv_ref = refs[4 + PEERS :]
    picked = sum(picked_counts(q_ref.shape[1], top_step))
    score_scale = 1.0 / math.sqrt(HEAD_DIM)
    cols = head_cols(q_ref.shape[2] // HEAD_DIM - 1)
    attended_ref[...] = (normed_ref[...].T * gain_ref[:, cols]).astype(LOW)
    k_peers = jnp.concatenate([ref[5 * picked : 6 * picked] for ref in peers], 0)
    grad_low = grad_low_ref[...]
    soft = expo_ref[:, cols].astype(WIDE) * kept_ref[0:1, :]
    prob_grad = contract(v_ref[0, :, cols], grad_low, 1, 0)
    score_grad = (soft * (prob_grad - kept_ref[1:2, :]) * score_scale).astype(LOW)
    dk_ref[...] = contract(score_grad, q_ref[0, :, cols], 1, 0)
    dv_ref[...] = contract(soft.astype(LOW), grad_low, 1, 1)
    dq_ref[...] = (
        contract(score_grad, k_ref[0, :, cols], 0, 0)
        + contract(peer_score_grad_ref[...], k_peers, 0, 0)
    ).astype(LOW)


def gain_kernel(picked, *refs):
    return_refs, gain_ref = nearest_first(refs[:SPAN]), refs[SPAN]
    tiles = [ref[6 * picked : 6 * picked + STAT_TILES].astype(WIDE) for ref in return_refs]
    parts = [tile[PIECES:TILE] + tile[TILE + PIECES :] for tile in tiles]
    total = (parts[0] + parts[1]) + (parts[2] + parts[3])
    for head in range(gain_ref.shape[1] // HEAD_DIM):
        gain_ref[:, head_cols(head)] = total[head : head + 1]


def mix_kernel(top_step, q_ref, k_ref, v_ref, gain_ref, expo_ref, out_ref, *refs):
    grad_norm_ref, stats_ref, place_ref, masks_ref = refs[:4]
    last_attended_ref, last_dq_ref, last_dk_ref, last_dv_ref = refs[4:8]
    return_refs, refs = nearest_first(refs[8 : 8 + SPAN]), refs[8 + SPAN :]
    attended_ref, dq_ref, dk_ref, dv_ref, placed_ref = refs
    tokens, width = v_ref.shape[1:]
    count = width // HEAD_DIM
    picked = sum(picked_counts(tokens, top_step))
    score_scale = 1.0 / math.sqrt(HEAD_DIM)
    me = lax.axis_index("ctx")
    heads = range(OWNED)
    every = [head_cols(head) for head in heads]
    for distance, return_ref in enumerate(return_refs):
        placed_ref[me ^ distance] = return_ref[...]
    once = [place_ref[:, head_cols(count + head)] for head in heads]
    attn_parts = [
        contract(placed_ref[head, 3 * picked : 4 * picked], once[head][:, :picked], 0, 1)
        for head in heads
    ]
    log_parts = [
        contract(placed_ref[head, 6 * picked : 6 * picked + STAT_TILES], once[head], 1, 1)
        for head in heads
    ]
    factors, normeds, grad_lows, inners = [], [], [], []
    for head in heads:
        seen = masks_ref[TILE + head : TILE + head + 1, :tokens] > 0.5
        top_score, total = stats_ref[head : head + 1, :], stats_ref[TILE + head : TILE + head + 1, :]
        log_total = jnp.where(seen, joined_row(log_parts[head], 0), top_score + jnp.log(total))
        factors.append(jnp.exp(top_score - log_total))
        attn = jnp.where(seen, attn_parts[head], out_ref[:, every[head]].astype(WIDE))
        normed, _, grad_low, inner = norm_backward(attn, grad_norm_ref[:, every[head]])
        normeds.append(normed)
        grad_lows.append(grad_low)
        inners.append(inner)
    prob_grads = [contract(v_ref[0, :, every[head]], grad_lows[head], 1, 0) for head in heads]
    softs = [expo_ref[:, every[head]].astype(WIDE) * factors[head] for head in heads]
    soft_lows = [soft.astype(LOW) for soft in softs]
    score_grads = [
        (softs[head] * (prob_grads[head] - inners[head]) * score_scale).astype(LOW)
        for head in heads
    ]
    dqs = [contract(score_grads[head], k_ref[0, :, every[head]], 0, 0) for head in heads]
    placed = [
        contract(
            place_ref[:, pl.ds(head * HEAD_DIM, picked)],
            jnp.concatenate(
                [placed_ref[head, block * picked : (block + 1) * picked] for block in range(3)], 1
            ),
            1,
            0,
        )
        for head in heads
    ]
    dks = [contract(score_grads[head], q_ref[0, :, every[head]], 1, 0) for head in heads]
    dvs = [contract(soft_lows[head], grad_lows[head], 1, 1) for head in heads]
    last = count - 1
    total = sum(ref[4 * picked : 6 * picked].astype(WIDE) for ref in return_refs[1:]).astype(LOW)
    rows = contract(
        place_ref[:, pl.ds(last * HEAD_DIM, picked)],
        jnp.concatenate([total[:picked], total[picked:]], 1),
        1,
        0,
    )
    for head in heads:
        cols = every[head]
        attended_ref[:, cols] = (normeds[head].T * gain_ref[:, cols]).astype(LOW)
        for which, (block, out_block_ref) in enumerate(
            ((dqs[head], dq_ref), (dks[head], dk_ref), (dvs[head], dv_ref))
        ):
            part = placed[head][:, which * HEAD_DIM : (which + 1) * HEAD_DIM]
            out_block_ref[:, cols] = (block + part).astype(LOW)
    cols = head_cols(last)
    attended_ref[:, cols] = last_attended_ref[...]
    dq_ref[:, cols] = last_dq_ref[...]
    dk_ref[:, cols] = (last_dk_ref[...] + rows[:, :HEAD_DIM]).astype(LOW)
    dv_ref[:, cols] = (last_dv_ref[...] + rows[:, HEAD_DIM:]).astype(LOW)


def finish_kernel(gain_ref, gain_rest_ref, *refs):
    block_refs, result_refs, gain_out_ref = refs[:4], refs[4:8], refs[8]
    for block_ref, result_ref in zip(block_refs, result_refs):
        result_ref[0] = block_ref[...]
    gain_out_ref[...] = (gain_ref[...] + gain_rest_ref[...]).reshape(gain_out_ref.shape)


def across(block, axis, distance):
    route = [(place, place ^ distance) for place in range(lax.axis_size(axis))]
    return lax.ppermute(block, axis, route)


def to_peers(blocks):
    return [across(blocks[distance - 1], "ctx", distance) for distance in START_ORDER]


def call(kernel, name, operands, results, microseconds, vmem=PLAIN_VMEM, scratch=()):
    return pl.pallas_call(
        kernel,
        out_shape=results,
        in_specs=[VMEM_SPEC] * len(operands),
        out_specs=[VMEM_SPEC] * len(results),
        scratch_shapes=scratch,
        compiler_params=pltpu.CompilerParams(vmem_limit_bytes=vmem),
        cost_estimate=pl.CostEstimate(
            flops=int(microseconds * 10**9), bytes_accessed=0, transcendentals=0
        ),
        name=name,
    )(*operands)


def one_segment_shards(queries, keys, values, grad_y, out_gain, offsets):
    tokens, width = queries.shape[1:]
    heads = width // HEAD_DIM
    top_step = lax.axis_size("ctx")
    picked = sum(picked_counts(tokens, top_step))
    shape = jax.ShapeDtypeStruct
    row_block = shape((1, tokens, width), LOW)
    low_block, wide_block = shape((tokens, width), LOW), shape((tokens, width), WIDE)
    low_head, wide_head = shape((tokens, HEAD_DIM), LOW), shape((tokens, HEAD_DIM), WIDE)
    gain_block = shape((1, width), WIDE)
    stats_block = shape((2 * TILE, tokens), WIDE)
    payload = shape((7 * picked + STAT_TILES, HEAD_DIM), LOW)
    answer = shape((6 * picked + STAT_TILES, HEAD_DIM), LOW)
    bind = functools.partial
    gain_row = out_gain.reshape(1, width)
    own, *sent, expo, base_out, stats = call(
        bind(pack_kernel, top_step),
        "pack",
        (offsets, queries, keys, values, grad_y),
        [payload] * SPAN + [low_block, low_block, stats_block],
        1,
        vmem=PACK_VMEM,
        scratch=[pltpu.VMEM((OWNED, *payload.shape), LOW)],
    )
    received = to_peers(sent)
    grad_norm, gain_base, place, masks = call(
        bind(prepare_kernel, top_step),
        "prepare",
        (offsets, grad_y, gain_row, base_out),
        [
            wide_block,
            gain_block,
            shape((tokens, 2 * width), LOW),
            shape((2 * TILE, 2 * tokens), WIDE),
        ],
        2,
    )
    normed, grad_low, score_grad, kept, own_answer, *answers = call(
        bind(owner_kernel, top_step),
        "owner",
        (queries, gain_row, base_out, grad_norm, stats, gain_base, masks, own, *received),
        [
            wide_head,
            low_head,
            shape((PEERS * picked, HEAD_DIM), LOW),
            shape((TILE, tokens), WIDE),
        ]
        + [answer] * SPAN,
        3,
    )
    returned = to_peers(answers)
    last_results = call(
        bind(last_head_kernel, top_step),
        "last_head",
        (queries, keys, values, gain_row, expo, normed, grad_low, score_grad, kept, *received),
        [low_head, low_head, wide_head, wide_head],
        20,
    )
    (gain_sum,) = call(bind(gain_kernel, picked), "gain", (own_answer, *returned), [gain_block], 1)
    gain_rest = across(gain_sum, "dp", 1)
    mixed = call(
        bind(mix_kernel, top_step),
        "mix",
        (
            queries,
            keys,
            values,
            gain_row,
            expo,
            base_out,
            grad_norm,
            stats,
            place,
            masks,
            *last_results,
            own_answer,
            *returned,
        ),
        [low_block] * 4,
        20,
        scratch=[pltpu.VMEM((OWNED, *answer.shape), LOW)],
    )
    attended, query_grad, key_grad, value_grad, gain_grad = call(
        finish_kernel,
        "finish",
        (gain_sum, gain_rest, *mixed),
        [row_block] * 4 + [shape((width,), WIDE)],
        1,
    )
    return attended, query_grad, key_grad, value_grad, gain_grad


def shards(*operands):
    one_segment = lax.axis_size("ctx") == SPAN
    if one_segment and operands[0].shape[2] == (OWNED + 1) * HEAD_DIM:
        return one_segment_shards(*operands)
    return general_shards(*operands)


def solution(mesh):
    in_specs = (
        P("dp", "ctx", "head"),
        P("dp", "ctx", "head"),
        P("dp", "ctx", "head"),
        P("dp", "ctx", "head"),
        P("head"),
        P(None, "head"),
    )
    out_specs = (
        P("dp", "ctx", "head"),
        P("dp", "ctx", "head"),
        P("dp", "ctx", "head"),
        P("dp", "ctx", "head"),
        P("head"),
    )
    return jax.shard_map(shards, mesh=mesh, in_specs=in_specs, out_specs=out_specs, check_vma=False)
```

```python
import functools
import math

import jax
import jax.numpy as jnp
from jax import lax
from jax.experimental import pallas as pl
from jax.experimental.pallas import tpu as pltpu
from jax.sharding import PartitionSpec as P

HEAD_DIM = 128
SPAN = 4
R1 = 8


EPS = 1e-06


def swapped(block, axis, bit):
    count = lax.axis_size(axis)
    route = []
    for low in range(count):
        high = low | 1 << bit
        if high != low and high < count:
            route += [(low, high), (high, low)]
    return lax.ppermute(block, axis, route)


def pick_rows(source_rows, dilation, shifts):
    row_count, head_count, head_width = source_rows.shape
    grouped = source_rows.reshape(row_count // dilation, dilation, head_count, head_width)
    hit_mask = jnp.arange(dilation, dtype=jnp.int32).reshape(1, dilation, 1, 1) == shifts.reshape(
        1, 1, head_count, 1
    )
    chosen = jnp.where(hit_mask, grouped, jnp.zeros((), source_rows.dtype))
    return jnp.sum(chosen, axis=1, dtype=source_rows.dtype)


def place_rows(row_values, dilation, shifts):
    row_count, head_count, head_width = row_values.shape
    hit_mask = jnp.arange(dilation, dtype=jnp.int32).reshape(1, dilation, 1, 1) == shifts.reshape(
        1, 1, head_count, 1
    )
    spread = jnp.where(hit_mask, row_values[:, None], jnp.zeros((), row_values.dtype))
    return spread.reshape(row_count * dilation, head_count, head_width)


def level_scores(q_rows, k_rows):
    score_scale = 1.0 / math.sqrt(q_rows.shape[-1])
    return (
        jnp.einsum("qhe,khe->hqk", q_rows, k_rows, preferred_element_type=jnp.float32) * score_scale
    )


def attend(q_rows, k_rows, v_rows):
    scores = level_scores(q_rows, k_rows)
    row_max = jnp.max(scores, axis=-1, keepdims=True)
    log_total = row_max[..., 0] + jnp.log(jnp.sum(jnp.exp(scores - row_max), axis=-1))
    soft_rows = jnp.exp(scores - log_total[..., None]).astype(jnp.bfloat16)
    level_out = jnp.einsum("hqk,khe->qhe", soft_rows, v_rows, preferred_element_type=jnp.float32)
    return (level_out, log_total.T)


def score_grads(q_rows, k_rows, v_rows, log_total, grad_low, row_shift):
    score_scale = 1.0 / math.sqrt(q_rows.shape[-1])
    scores = level_scores(q_rows, k_rows)
    exact_soft = jnp.exp(scores - log_total.T[..., None])
    prob_grad = jnp.einsum("qhe,khe->hqk", grad_low, v_rows, preferred_element_type=jnp.float32)
    score_grad = (exact_soft * (prob_grad + row_shift.T[..., None]) * score_scale).astype(
        jnp.bfloat16
    )
    return (score_grad, exact_soft.astype(jnp.bfloat16))


def key_parts(score_grad, soft_low, q_rows, grad_low):
    k_part = jnp.einsum("hqk,qhe->khe", score_grad, q_rows, preferred_element_type=jnp.float32)
    v_part = jnp.einsum("hqk,qhe->khe", soft_low, grad_low, preferred_element_type=jnp.float32)
    return (k_part, v_part)


def query_part(score_grad, k_rows):
    return jnp.einsum("hqk,khe->qhe", score_grad, k_rows, preferred_element_type=jnp.float32)


def general_shards(queries, keys, values, grad_y, out_gain, offsets):
    tokens = queries.shape[1]
    flat_width = queries.shape[2]
    head_count = flat_width // HEAD_DIM
    row_shape = (tokens, head_count, HEAD_DIM)
    q_own = queries[0].reshape(row_shape)
    k_own = keys[0].reshape(row_shape)
    v_own = values[0].reshape(row_shape)
    ctx_size = lax.axis_size("ctx")
    span_bits = SPAN.bit_length() - 1
    my_place = lax.axis_index("ctx")
    mid_shift = offsets[0]
    top_shift = offsets[1]
    positions = jnp.arange(tokens, dtype=jnp.int32)
    mid_hit = (positions % R1)[:, None] == mid_shift[None, :]
    top_hit = (positions % ctx_size)[:, None] == top_shift[None, :]
    mid_q = pick_rows(q_own, R1, mid_shift)
    mid_k = pick_rows(k_own, R1, mid_shift)
    mid_v = pick_rows(v_own, R1, mid_shift)
    top_q = pick_rows(q_own, ctx_size, top_shift)
    top_k = pick_rows(k_own, ctx_size, top_shift)
    top_v = pick_rows(v_own, ctx_size, top_shift)
    mid_keys = mid_k.reshape(-1, flat_width)
    mid_vals = mid_v.reshape(-1, flat_width)
    top_keys = top_k.reshape(-1, flat_width)
    top_vals = top_v.reshape(-1, flat_width)

    def append_peer(mine, received, level_bit):
        upper_side = my_place >> level_bit & 1 == 1
        return jnp.where(
            upper_side, jnp.concatenate([received, mine], 0), jnp.concatenate([mine, received], 0)
        )

    for level_bit in range(span_bits):
        received = swapped((mid_keys, mid_vals), "ctx", level_bit)
        mid_keys = append_peer(mid_keys, received[0], level_bit)
        mid_vals = append_peer(mid_vals, received[1], level_bit)
    top_keys, top_vals = (
        lax.all_gather(top_keys, "ctx", axis=0, tiled=True),
        lax.all_gather(top_vals, "ctx", axis=0, tiled=True),
    )
    mid_keys = mid_keys.reshape(-1, head_count, HEAD_DIM)
    mid_vals = mid_vals.reshape(-1, head_count, HEAD_DIM)
    top_keys = top_keys.reshape(-1, head_count, HEAD_DIM)
    top_vals = top_vals.reshape(-1, head_count, HEAD_DIM)
    base_out, base_total = attend(q_own, k_own, v_own)
    mid_out, mid_total = attend(mid_q, mid_keys, mid_vals)
    top_out, top_total = attend(top_q, top_keys, top_vals)
    mid_full = place_rows(mid_total[..., None], R1, mid_shift)[..., 0]
    top_full = place_rows(top_total[..., None], ctx_size, top_shift)[..., 0]
    row_max = jnp.maximum(base_total, jnp.where(mid_hit, mid_full, base_total))
    row_max = jnp.maximum(row_max, jnp.where(top_hit, top_full, base_total))
    base_expo = jnp.exp(base_total - row_max)
    mid_expo = jnp.where(mid_hit, jnp.exp(mid_full - row_max), 0.0)
    top_expo = jnp.where(top_hit, jnp.exp(top_full - row_max), 0.0)
    denom = base_expo + mid_expo + top_expo
    base_share = base_expo / denom
    mid_share = mid_expo / denom
    top_share = top_expo / denom
    attn = (
        base_share[..., None] * base_out
        + mid_share[..., None] * place_rows(mid_out, R1, mid_shift)
        + top_share[..., None] * place_rows(top_out, ctx_size, top_shift)
    )
    inv_rms = lax.rsqrt(jnp.mean(attn * attn, axis=-1, keepdims=True) + EPS)
    normed = attn * inv_rms
    gain_rows = out_gain.reshape(head_count, HEAD_DIM)
    attended = (normed * gain_rows).astype(jnp.bfloat16).reshape(1, tokens, flat_width)
    grad_full = grad_y[0].reshape(row_shape).astype(jnp.float32)
    gain_part = jnp.sum(grad_full * normed, axis=0).reshape(flat_width)
    gain_grad = lax.psum(gain_part, ("dp", "ctx"))
    grad_norm = grad_full * gain_rows
    grad_attn = inv_rms * (
        grad_norm - normed * jnp.mean(grad_norm * normed, axis=-1, keepdims=True)
    )
    inner = jnp.sum(grad_attn * attn, axis=-1)
    base_low = (base_share[..., None] * grad_attn).astype(jnp.bfloat16)
    base_shift = -(base_share * inner)
    base_grad, base_soft = score_grads(q_own, k_own, v_own, base_total, base_low, base_shift)
    base_dq = query_part(base_grad, k_own)
    base_dk, base_dv = key_parts(base_grad, base_soft, q_own, base_low)
    mid_sel = pick_rows(mid_share[..., None], R1, mid_shift)[..., 0]
    mid_low = (mid_sel[..., None] * pick_rows(grad_attn, R1, mid_shift)).astype(jnp.bfloat16)
    mid_row_shift = -(mid_sel * pick_rows(inner[..., None], R1, mid_shift)[..., 0])
    mid_grad, mid_soft = score_grads(mid_q, mid_keys, mid_vals, mid_total, mid_low, mid_row_shift)
    mid_dq = query_part(mid_grad, mid_keys)
    mid_dk, mid_dv = key_parts(mid_grad, mid_soft, mid_q, mid_low)
    mid_dk = mid_dk.reshape(-1, flat_width)
    mid_dv = mid_dv.reshape(-1, flat_width)
    for level_bit in reversed(range(span_bits)):
        half_rows = mid_dk.shape[0] // 2
        upper_side = my_place >> level_bit & 1 == 1
        keep_k = jnp.where(upper_side, mid_dk[half_rows:], mid_dk[:half_rows])
        keep_v = jnp.where(upper_side, mid_dv[half_rows:], mid_dv[:half_rows])
        send_k = jnp.where(upper_side, mid_dk[:half_rows], mid_dk[half_rows:])
        send_v = jnp.where(upper_side, mid_dv[:half_rows], mid_dv[half_rows:])
        received = (
            swapped(send_k.astype(jnp.bfloat16), "ctx", level_bit).astype(send_k.dtype),
            swapped(send_v.astype(jnp.bfloat16), "ctx", level_bit).astype(send_v.dtype),
        )
        mid_dk = keep_k + received[0]
        mid_dv = keep_v + received[1]
    mid_dk = mid_dk.reshape(-1, head_count, HEAD_DIM)
    mid_dv = mid_dv.reshape(-1, head_count, HEAD_DIM)
    top_sel = pick_rows(top_share[..., None], ctx_size, top_shift)[..., 0]
    top_low = (top_sel[..., None] * pick_rows(grad_attn, ctx_size, top_shift)).astype(jnp.bfloat16)
    top_row_shift = -(top_sel * pick_rows(inner[..., None], ctx_size, top_shift)[..., 0])
    top_grad, top_soft = score_grads(top_q, top_keys, top_vals, top_total, top_low, top_row_shift)
    top_dq = query_part(top_grad, top_keys)
    gathered_dk, gathered_dv = key_parts(top_grad, top_soft, top_q, top_low)
    summed = (
        lax.psum_scatter(
            gathered_dk.reshape(-1, flat_width), "ctx", scatter_dimension=0, tiled=True
        ),
        lax.psum_scatter(
            gathered_dv.reshape(-1, flat_width), "ctx", scatter_dimension=0, tiled=True
        ),
    )
    top_dk = summed[0].reshape(-1, head_count, HEAD_DIM)
    top_dv = summed[1].reshape(-1, head_count, HEAD_DIM)
    query_grad = (
        base_dq + place_rows(mid_dq, R1, mid_shift) + place_rows(top_dq, ctx_size, top_shift)
    )
    key_grad = base_dk + place_rows(mid_dk, R1, mid_shift) + place_rows(top_dk, ctx_size, top_shift)
    value_grad = (
        base_dv + place_rows(mid_dv, R1, mid_shift) + place_rows(top_dv, ctx_size, top_shift)
    )
    out_shape = (1, tokens, flat_width)
    return (
        attended,
        query_grad.astype(jnp.bfloat16).reshape(out_shape),
        key_grad.astype(jnp.bfloat16).reshape(out_shape),
        value_grad.astype(jnp.bfloat16).reshape(out_shape),
        gain_grad,
    )


VMEM_SPEC = pl.BlockSpec(memory_space=pltpu.VMEM)
PEERS = SPAN - 1
OWNED = SPAN
TILE = 8
STAT_TILES = 2 * TILE
PIECES = 3
NEVER = -1e30
START_ORDER = (3, 1, 2)
LOW = jnp.bfloat16
WIDE = jnp.float32
PACK_VMEM = 65408 * 1024
PLAIN_VMEM = 16 * 1024 * 1024


def contract(left, right, left_dim, right_dim):
    return lax.dot_general(
        left, right, (((left_dim,), (right_dim,)), ((), ())), preferred_element_type=WIDE
    )


def head_cols(head):
    return pl.ds(head * HEAD_DIM, HEAD_DIM)


def picked_counts(tokens, top_step):
    return tokens // top_step, tokens // R1


def offset_of(offsets_ref, level, head):
    return offsets_ref[level : level + 1, head : head + 1]


def pick_matrix(offsets_ref, head, tokens, top_step, picked_axis):
    top_rows, _ = picked_counts(tokens, top_step)
    row = lax.broadcasted_iota(jnp.int32, (tokens, tokens), picked_axis)
    position = lax.broadcasted_iota(jnp.int32, (tokens, tokens), 1 - picked_axis)
    wanted = jnp.where(
        row < top_rows,
        row * top_step + offset_of(offsets_ref, 1, head),
        (row - top_rows) * R1 + offset_of(offsets_ref, 0, head),
    )
    return jnp.where(position == wanted, 1.0, 0.0).astype(LOW)


def rolled(row, shift):
    return pltpu.roll(row, shift % row.shape[1], 1)


def lane_window(row, start, count):
    lane = lax.broadcasted_iota(jnp.int32, row.shape, 1)
    return jnp.where((lane >= start) & (lane < start + count), row, 0.0)


def hit_row(offset, step, tokens):
    position = lax.broadcasted_iota(jnp.int32, (1, tokens), 1)
    return jnp.where(position % step == offset, 1.0, 0.0)


def piece_rows(row, others=None):
    pieces = []
    for _ in range(PIECES):
        piece = row.astype(LOW).astype(WIDE)
        pieces.append(piece)
        row = row - piece
    if others is None:
        others = jnp.zeros((TILE - PIECES, row.shape[1]), WIDE)
    return jnp.concatenate(pieces + [others], 0)


def gain_pieces(rows):
    high = rows.astype(LOW)
    return high, (rows - high.astype(WIDE)).astype(LOW)


def joined_row(rows, first):
    total = rows[first : first + 1]
    for piece in range(1, PIECES):
        total = total + rows[first + piece : first + piece + 1]
    return total


def gain_row_of(ones, product):
    high, rest = gain_pieces(product)
    return (contract(ones, high, 1, 1) + contract(ones, rest, 1, 1))[:1]


def column_mean(block):
    return jnp.mean(block, axis=0, keepdims=True)


def norm_backward(attn, grad_norm):
    inv_rms = lax.rsqrt(column_mean(attn * attn) + EPS)
    normed = attn * inv_rms
    product = grad_norm * normed
    grad_attn = inv_rms * (grad_norm - normed * column_mean(product))
    inner = jnp.sum(grad_attn * attn, axis=0, keepdims=True)
    return normed, product, grad_attn, inner


def nearest_first(refs):
    by_distance = dict(zip(START_ORDER, refs[1:]))
    return [refs[0], *[by_distance[distance] for distance in range(1, SPAN)]]


def pack_kernel(top_step, offsets_ref, q_ref, k_ref, v_ref, grad_ref, *refs):
    payload_refs, (expo_ref, out_ref, stats_ref, held_ref) = refs[:SPAN], refs[SPAN:]
    tokens, width = q_ref.shape[1:]
    heads = range(width // HEAD_DIM)
    owned = range(OWNED)
    me = lax.axis_index("ctx")
    picked = sum(picked_counts(tokens, top_step))
    score_scale = 1.0 / math.sqrt(HEAD_DIM)
    q_rows, k_rows, v_rows, grad_rows = [
        [ref[0, :, head_cols(head)] for head in heads] for ref in (q_ref, k_ref, v_ref, grad_ref)
    ]
    picks = [pick_matrix(offsets_ref, head, tokens, top_step, 0) for head in heads]
    scores = [contract(k_rows[head], q_rows[head], 1, 1) * score_scale for head in heads]
    moved = [
        contract(
            picks[head][:picked],
            jnp.concatenate([q_rows[head], k_rows[head], v_rows[head], grad_rows[head]], 1),
            1,
            0,
        ).astype(LOW)
        for head in owned
    ]
    shared = [
        contract(
            picks[head][:picked], jnp.concatenate([k_rows[head], v_rows[head]], 1), 1, 0
        ).astype(LOW)
        for head in heads[OWNED:]
    ]
    top_scores = [jnp.max(block, axis=0, keepdims=True) for block in scores]
    expos = [jnp.exp(scores[head] - top_scores[head]) for head in heads]
    for head in heads[OWNED:]:
        key_row = lax.broadcasted_iota(jnp.int32, (tokens, 1), 0)
        times = 1.0
        for level, step in ((0, R1), (1, top_step)):
            offset = offset_of(offsets_ref, level, head)
            hit_column = jnp.where(key_row % step == offset, 1.0, 0.0)
            times = times + hit_column * hit_row(offset, step, tokens)
        expos[head] = times * expos[head]
    expo_lows = [expo.astype(LOW) for expo in expos]
    outs = [contract(v_rows[head], expo_lows[head], 0, 0) for head in heads]
    totals = [jnp.sum(expo, axis=0, keepdims=True) for expo in expos]
    for head in heads:
        expo_ref[:, head_cols(head)] = expo_lows[head]
        stats_ref[head : head + 1, :] = top_scores[head]
        stats_ref[TILE + head : TILE + head + 1, :] = totals[head]
    for head in owned:
        outs[head] = outs[head] * (1.0 / totals[head])
    outs = [out.astype(LOW) for out in outs]
    picked_outs = [
        contract(picks[head][:picked], outs[head], 1, 1).astype(LOW) for head in owned
    ]
    for head in heads:
        out_ref[:, head_cols(head)] = outs[head]
    for head in owned:
        pieces = piece_rows(top_scores[head] + jnp.log(totals[head])).astype(LOW)
        stat_rows = contract(pieces, picks[head], 1, 1)
        blocks = [moved[head][:, block * HEAD_DIM : (block + 1) * HEAD_DIM] for block in range(4)]
        blocks.append(picked_outs[head])
        blocks += [shared[0][:, :HEAD_DIM], shared[0][:, HEAD_DIM:]]
        blocks.append(jnp.concatenate([stat_rows, jnp.zeros_like(stat_rows)], 0).astype(LOW))
        held_ref[head] = jnp.concatenate(blocks, 0)
    for distance, payload_ref in enumerate(payload_refs):
        payload_ref[...] = held_ref[me ^ distance]


def prepare_kernel(top_step, offsets_ref, grad_ref, gain_ref, out_ref, *refs):
    grad_norm_ref, gain_part_ref, place_ref, masks_ref = refs
    tokens, width = grad_ref.shape[1:]
    heads = range(width // HEAD_DIM)
    top_rows = tokens // top_step
    ones = jnp.ones((TILE, tokens), LOW)
    column = lax.broadcasted_iota(jnp.int32, (tokens, tokens), 1)
    gain_part_ref[...] = jnp.zeros(gain_part_ref.shape, WIDE)
    me = lax.axis_index("ctx")
    mid_rows = tokens // R1
    top_all, queries = SPAN * top_rows, SPAN * (top_rows + mid_rows)
    mid_offset, top_offset = [
        sum(
            jnp.where(me == head, offset_of(offsets_ref, level, head), 0) for head in range(OWNED)
        )
        for level in (0, 1)
    ]
    lane = lax.broadcasted_iota(jnp.int32, (1, queries), 1)
    is_top = jnp.where(lane < top_all, 1.0, 0.0)
    top_in_mid = jnp.where(((lane % top_rows) * top_step + top_offset) % R1 == mid_offset, 1.0, 0.0)
    both_flag = jnp.where(mid_offset % top_step == top_offset, 1.0, 0.0)
    sees_top = is_top + (1.0 - is_top) * both_flag
    sees_mid = is_top * top_in_mid + (1.0 - is_top)
    masks_ref[0:1, :queries] = (1.0 - sees_top) * NEVER
    masks_ref[1:2, :queries] = (1.0 - sees_mid) * NEVER
    masks_ref[2:3, :queries] = is_top + (1.0 - is_top) * (1.0 - both_flag)
    last = len(heads) - 1
    for row, (level, step) in enumerate(((1, top_step), (0, R1))):
        hits = hit_row(offset_of(offsets_ref, level, last), step, tokens)
        masks_ref[3 + row : 4 + row, :tokens] = (1.0 - hits) * NEVER
    grad_norms = [
        (grad_ref[0, :, head_cols(head)].astype(WIDE) * gain_ref[:, head_cols(head)]).T
        for head in heads
    ]
    for head in heads:
        cols = head_cols(head)
        grad_norm_ref[:, cols] = grad_norms[head]
        picks = pick_matrix(offsets_ref, head, tokens, top_step, 1)
        place_ref[:, cols] = picks
    for head in range(OWNED):
        cols = head_cols(head)
        mid_offset, top_offset = [offset_of(offsets_ref, level, head) for level in (0, 1)]
        seen = jnp.maximum(
            hit_row(top_offset, top_step, tokens), hit_row(mid_offset, R1, tokens)
        )
        masks_ref[TILE + head : TILE + head + 1, :tokens] = seen
        attn = out_ref[:, cols].astype(WIDE)
        normed = attn * lax.rsqrt(column_mean(attn * attn) + EPS)
        product = grad_norms[head] * normed * (1.0 - seen)
        gain_part_ref[:, cols] = gain_row_of(ones, product) / gain_ref[:, cols]
        both = mid_offset % top_step == top_offset
        kept = jnp.where(column < top_rows, 1.0, jnp.where(both, 0.0, 1.0)).astype(LOW)
        picks = pick_matrix(offsets_ref, head, tokens, top_step, 1)
        place_ref[:, head_cols(len(heads) + head)] = picks * kept


def owner_kernel(top_step, q_ref, gain_ref, out_ref, grad_norm_ref, *refs):
    stats_ref, gain_base_ref, masks_ref = refs[:3]
    payload_refs, refs = nearest_first(refs[3 : 3 + SPAN]), refs[3 + SPAN :]
    normed_ref, grad_low_ref, score_grad_ref, kept_ref = refs[:4]
    return_refs = refs[4:]
    tokens = q_ref.shape[1]
    heads = q_ref.shape[2] // HEAD_DIM
    top_rows, mid_rows = picked_counts(tokens, top_step)
    picked = top_rows + mid_rows
    top_all, mid_all = SPAN * top_rows, SPAN * mid_rows
    queries = top_all + mid_all
    score_scale = 1.0 / math.sqrt(HEAD_DIM)
    me = lax.axis_index("ctx")
    ones = jnp.ones((TILE, tokens), LOW)

    def by_level(block):
        start = block * picked
        return jnp.concatenate(
            [ref[start : start + top_rows] for ref in payload_refs]
            + [ref[start + top_rows : start + picked] for ref in payload_refs],
            0,
        )

    def per_level(top_row, mid_row):
        return jnp.concatenate(
            [
                jnp.broadcast_to(top_row, (top_all, queries)),
                jnp.broadcast_to(mid_row, (mid_all, queries)),
            ],
            0,
        )

    q_rows, k_rows, v_rows, grad_rows, base_rows = [by_level(block) for block in range(5)]
    stat_start = 7 * picked
    logs = [
        joined_row(ref[stat_start : stat_start + STAT_TILES].astype(WIDE), 0)
        for ref in payload_refs
    ]
    base_top_log = sum(
        rolled(lane_window(log, 0, top_rows), slot * top_rows) for slot, log in enumerate(logs)
    )
    base_mid_log = sum(
        rolled(lane_window(log, top_rows, mid_rows), slot * mid_rows - top_rows)
        for slot, log in enumerate(logs)
    )
    base_log = jnp.concatenate([base_top_log, base_mid_log[:, :mid_all]], 1)
    gain_row = jnp.zeros((1, HEAD_DIM), WIDE)
    for head in range(OWNED):
        gain_row = gain_row + jnp.where(me == head, 1.0, 0.0) * gain_ref[:, head_cols(head)]
    lane = lax.broadcasted_iota(jnp.int32, (1, queries), 1)
    is_top = jnp.where(lane < top_all, 1.0, 0.0)
    bias = per_level(masks_ref[0:1, :queries], masks_ref[1:2, :queries])
    last = heads - 1
    cols = head_cols(last)
    peers = payload_refs[1:]
    q_last = q_ref[0, :, cols]
    k_peers = jnp.concatenate([ref[5 * picked : 6 * picked] for ref in peers], 0)
    v_peers = jnp.concatenate([ref[6 * picked : 7 * picked] for ref in peers], 0)
    last_biases = [
        jnp.broadcast_to(masks_ref[row : row + 1, :tokens], (count, tokens))
        for row, count in ((3, top_rows), (4, mid_rows))
    ]
    scores = contract(k_rows, q_rows, 1, 1) * score_scale + bias
    scores_last = contract(k_peers, q_last, 1, 1) * score_scale + jnp.concatenate(
        last_biases * PEERS, 0
    )
    base_attn = base_rows.astype(WIDE).T
    grad_norm = (grad_rows.astype(WIDE) * gain_row).T
    top_score = jnp.maximum(base_log, jnp.max(scores, axis=0, keepdims=True))
    base_top, base_total = stats_ref[last : last + 1, :], stats_ref[TILE + last : TILE + last + 1, :]
    top_last = jnp.maximum(base_top, jnp.max(scores_last, axis=0, keepdims=True))
    expo = jnp.exp(scores - top_score)
    expo_last = jnp.exp(scores_last - top_last)
    factor = jnp.exp(base_log - top_score)
    factor_last = jnp.exp(base_top - top_last)
    total = factor + jnp.sum(expo, axis=0, keepdims=True)
    total_last = factor_last * base_total + jnp.sum(expo_last, axis=0, keepdims=True)
    inv_total, inv_last = 1.0 / total, 1.0 / total_last
    expo_low, expo_last_low = expo.astype(LOW), expo_last.astype(LOW)
    attn = (factor * base_attn + contract(v_rows, expo_low, 0, 0)) * inv_total
    attn_last = (
        factor_last * out_ref[:, cols].astype(WIDE) + contract(v_peers, expo_last_low, 0, 0)
    ) * inv_last
    _, product, grad_attn, inner = norm_backward(attn, grad_norm)
    normed_last, product_last, grad_attn_last, inner_last = norm_backward(
        attn_last, grad_norm_ref[:, cols]
    )
    grad_low, inner = (grad_attn * inv_total).astype(LOW), inner * inv_total
    grad_last_low = (grad_attn_last * inv_last).astype(LOW)
    base_factor = factor_last * inv_last
    spans = (slice(0, top_all), slice(top_all, queries))
    prob_grads = [contract(v_rows[span], grad_low[:, span], 1, 0) for span in spans]
    prob_grad_last = contract(v_peers, grad_last_low, 1, 0)
    score_grads = [
        (expo[span, span] * (prob_grad - inner[:, span]) * score_scale).astype(LOW)
        for span, prob_grad in zip(spans, prob_grads)
    ]
    score_grad_last = (
        expo_last * (prob_grad_last - inner_last * inv_last) * score_scale
    ).astype(LOW)
    dks = [
        contract(score_grad, q_rows[span], 1, 0).astype(LOW)
        for span, score_grad in zip(spans, score_grads)
    ]
    dk_last = contract(score_grad_last, q_last, 1, 0).astype(LOW)
    dvs = [
        contract(expo_low[span, span], grad_low[:, span], 1, 1).astype(LOW) for span in spans
    ]
    dv_last = contract(expo_last_low, grad_last_low, 1, 1).astype(LOW)
    dqs = [
        contract(score_grad, k_rows[span], 0, 0).astype(LOW)
        for span, score_grad in zip(spans, score_grads)
    ]
    attn_rows = attn.T.astype(LOW)
    attn_parts = [attn_rows[span] for span in spans]
    log_total = top_score + jnp.log(total)
    padding = jnp.zeros((1, top_all - mid_all), WIDE)
    once = masks_ref[2:3, :queries]
    ones_all = jnp.ones((TILE, queries), LOW)
    own_gain = gain_row_of(ones_all, product * once) / gain_row
    gain_rows = [
        gain_base_ref[:, head_cols(head)] + jnp.where(me == head, 1.0, 0.0) * own_gain
        for head in range(OWNED)
    ]
    gain_rows.append(gain_row_of(ones, product_last) / gain_ref[:, cols])
    gain_high, gain_rest = [
        rows.astype(WIDE) for rows in gain_pieces(jnp.concatenate(gain_rows, 0))
    ]
    top_log, mid_log = log_total[:, :top_all], jnp.concatenate(
        [log_total[:, top_all:], padding], 1
    )
    empty = jnp.zeros((PIECES, HEAD_DIM), WIDE)
    for distance, return_ref in enumerate(return_refs):
        blocks = []
        for top_block, mid_block in (dqs, dks, dvs, attn_parts):
            blocks.append(top_block[distance * top_rows : (distance + 1) * top_rows])
            blocks.append(mid_block[distance * mid_rows : (distance + 1) * mid_rows])
        start = max(distance - 1, 0) * picked
        blocks += [dk_last[start : start + picked], dv_last[start : start + picked]]
        log_row = lane_window(rolled(top_log, -distance * top_rows), 0, top_rows) + lane_window(
            rolled(mid_log, top_rows - distance * mid_rows), top_rows, mid_rows
        )
        log_rows = [piece_rows(log_row, gain_high), empty, gain_rest]
        blocks.append(jnp.concatenate(log_rows, 0).astype(LOW))
        return_ref[...] = jnp.concatenate(blocks, 0)
    normed_ref[...] = normed_last
    grad_low_ref[...] = (grad_attn_last * base_factor).astype(LOW)
    score_grad_ref[...] = score_grad_last
    kept_ref[0:1, :] = inner_last * base_factor


def last_head_kernel(top_step, q_ref, k_ref, v_ref, gain_ref, expo_ref, *refs):
    normed_ref, grad_low_ref, peer_score_grad_ref, kept_ref, *peers = refs[: 4 + PEERS]
    peers = nearest_first([None, *peers])[1:]
    attended_ref, dq_ref, dk_ref, dv_ref = refs[4 + PEERS :]
    picked = sum(picked_counts(q_ref.shape[1], top_step))
    score_scale = 1.0 / math.sqrt(HEAD_DIM)
    cols = head_cols(q_ref.shape[2] // HEAD_DIM - 1)
    attended_ref[...] = (normed_ref[...].T * gain_ref[:, cols]).astype(LOW)
    k_peers = jnp.concatenate([ref[5 * picked : 6 * picked] for ref in peers], 0)
    grad_low = grad_low_ref[...]
    expo_low = expo_ref[:, cols]
    prob_grad = contract(v_ref[0, :, cols], grad_low, 1, 0)
    score_grad = (
        expo_low.astype(WIDE) * (prob_grad - kept_ref[0:1, :]) * score_scale
    ).astype(LOW)
    dk_ref[...] = contract(score_grad, q_ref[0, :, cols], 1, 0)
    dv_ref[...] = contract(expo_low, grad_low, 1, 1)
    dq_ref[...] = (
        contract(score_grad, k_ref[0, :, cols], 0, 0)
        + contract(peer_score_grad_ref[...], k_peers, 0, 0)
    ).astype(LOW)


def gain_kernel(picked, *refs):
    return_refs, gain_ref = nearest_first(refs[:SPAN]), refs[SPAN]
    tiles = [ref[6 * picked : 6 * picked + STAT_TILES].astype(WIDE) for ref in return_refs]
    parts = [tile[PIECES:TILE] + tile[TILE + PIECES :] for tile in tiles]
    total = (parts[0] + parts[1]) + (parts[2] + parts[3])
    for head in range(gain_ref.shape[1] // HEAD_DIM):
        gain_ref[:, head_cols(head)] = total[head : head + 1]


def mix_kernel(top_step, q_ref, k_ref, v_ref, gain_ref, expo_ref, out_ref, *refs):
    grad_norm_ref, stats_ref, place_ref, masks_ref = refs[:4]
    last_attended_ref, last_dq_ref, last_dk_ref, last_dv_ref = refs[4:8]
    return_refs, refs = nearest_first(refs[8 : 8 + SPAN]), refs[8 + SPAN :]
    attended_ref, dq_ref, dk_ref, dv_ref, placed_ref = refs
    tokens, width = v_ref.shape[1:]
    count = width // HEAD_DIM
    picked = sum(picked_counts(tokens, top_step))
    score_scale = 1.0 / math.sqrt(HEAD_DIM)
    me = lax.axis_index("ctx")
    heads = range(OWNED)
    every = [head_cols(head) for head in heads]
    for distance, return_ref in enumerate(return_refs):
        placed_ref[me ^ distance] = return_ref[...]
    once = [place_ref[:, head_cols(count + head)] for head in heads]
    attn_parts = [
        contract(placed_ref[head, 3 * picked : 4 * picked], once[head][:, :picked], 0, 1)
        for head in heads
    ]
    log_parts = [
        contract(placed_ref[head, 6 * picked : 6 * picked + STAT_TILES], once[head], 1, 1)
        for head in heads
    ]
    normeds, grad_lows, inners, inv_totals = [], [], [], []
    for head in heads:
        seen = masks_ref[TILE + head : TILE + head + 1, :tokens] > 0.5
        top_score, total = stats_ref[head : head + 1, :], stats_ref[TILE + head : TILE + head + 1, :]
        base_log = top_score + jnp.log(total)
        log_total = jnp.where(seen, joined_row(log_parts[head], 0), base_log)
        share = jnp.exp(base_log - log_total)
        inv_totals.append(1.0 / total)
        attn = jnp.where(seen, attn_parts[head], out_ref[:, every[head]].astype(WIDE))
        normed, _, grad_attn, inner = norm_backward(attn, grad_norm_ref[:, every[head]])
        normeds.append(normed)
        grad_lows.append((share * grad_attn).astype(LOW))
        inners.append(share * inner)
    prob_grads = [contract(v_ref[0, :, every[head]], grad_lows[head], 1, 0) for head in heads]
    softs = [expo_ref[:, every[head]].astype(WIDE) * inv_totals[head] for head in heads]
    soft_lows = [soft.astype(LOW) for soft in softs]
    score_grads = [
        (softs[head] * (prob_grads[head] - inners[head]) * score_scale).astype(LOW)
        for head in heads
    ]
    dqs = [contract(score_grads[head], k_ref[0, :, every[head]], 0, 0) for head in heads]
    placed = [
        contract(
            place_ref[:, pl.ds(head * HEAD_DIM, picked)],
            jnp.concatenate(
                [placed_ref[head, block * picked : (block + 1) * picked] for block in range(3)], 1
            ),
            1,
            0,
        )
        for head in heads
    ]
    dks = [contract(score_grads[head], q_ref[0, :, every[head]], 1, 0) for head in heads]
    dvs = [contract(soft_lows[head], grad_lows[head], 1, 1) for head in heads]
    last = count - 1
    total = sum(ref[4 * picked : 6 * picked].astype(WIDE) for ref in return_refs[1:]).astype(LOW)
    rows = contract(
        place_ref[:, pl.ds(last * HEAD_DIM, picked)],
        jnp.concatenate([total[:picked], total[picked:]], 1),
        1,
        0,
    )
    for head in heads:
        cols = every[head]
        attended_ref[:, cols] = (normeds[head].T * gain_ref[:, cols]).astype(LOW)
        for which, (block, out_block_ref) in enumerate(
            ((dqs[head], dq_ref), (dks[head], dk_ref), (dvs[head], dv_ref))
        ):
            part = placed[head][:, which * HEAD_DIM : (which + 1) * HEAD_DIM]
            out_block_ref[:, cols] = (block + part).astype(LOW)
    cols = head_cols(last)
    attended_ref[:, cols] = last_attended_ref[...]
    dq_ref[:, cols] = last_dq_ref[...]
    dk_ref[:, cols] = (last_dk_ref[...] + rows[:, :HEAD_DIM]).astype(LOW)
    dv_ref[:, cols] = (last_dv_ref[...] + rows[:, HEAD_DIM:]).astype(LOW)


def finish_kernel(gain_ref, gain_rest_ref, *refs):
    block_refs, result_refs, gain_out_ref = refs[:4], refs[4:8], refs[8]
    for block_ref, result_ref in zip(block_refs, result_refs):
        result_ref[0] = block_ref[...]
    gain_out_ref[...] = (gain_ref[...] + gain_rest_ref[...]).reshape(gain_out_ref.shape)


def across(block, axis, distance):
    route = [(place, place ^ distance) for place in range(lax.axis_size(axis))]
    return lax.ppermute(block, axis, route)


def to_peers(blocks):
    return [across(blocks[distance - 1], "ctx", distance) for distance in START_ORDER]


def call(kernel, name, operands, results, microseconds, vmem=PLAIN_VMEM, scratch=()):
    return pl.pallas_call(
        kernel,
        out_shape=results,
        in_specs=[VMEM_SPEC] * len(operands),
        out_specs=[VMEM_SPEC] * len(results),
        scratch_shapes=scratch,
        compiler_params=pltpu.CompilerParams(vmem_limit_bytes=vmem),
        cost_estimate=pl.CostEstimate(
            flops=int(microseconds * 10**9), bytes_accessed=0, transcendentals=0
        ),
        name=name,
    )(*operands)


def one_segment_shards(queries, keys, values, grad_y, out_gain, offsets):
    tokens, width = queries.shape[1:]
    heads = width // HEAD_DIM
    top_step = lax.axis_size("ctx")
    picked = sum(picked_counts(tokens, top_step))
    shape = jax.ShapeDtypeStruct
    row_block = shape((1, tokens, width), LOW)
    low_block, wide_block = shape((tokens, width), LOW), shape((tokens, width), WIDE)
    low_head, wide_head = shape((tokens, HEAD_DIM), LOW), shape((tokens, HEAD_DIM), WIDE)
    gain_block = shape((1, width), WIDE)
    stats_block = shape((2 * TILE, tokens), WIDE)
    payload = shape((7 * picked + STAT_TILES, HEAD_DIM), LOW)
    answer = shape((6 * picked + STAT_TILES, HEAD_DIM), LOW)
    bind = functools.partial
    gain_row = out_gain.reshape(1, width)
    own, *sent, expo, base_out, stats = call(
        bind(pack_kernel, top_step),
        "pack",
        (offsets, queries, keys, values, grad_y),
        [payload] * SPAN + [low_block, low_block, stats_block],
        1,
        vmem=PACK_VMEM,
        scratch=[pltpu.VMEM((OWNED, *payload.shape), LOW)],
    )
    received = to_peers(sent)
    grad_norm, gain_base, place, masks = call(
        bind(prepare_kernel, top_step),
        "prepare",
        (offsets, grad_y, gain_row, base_out),
        [
            wide_block,
            gain_block,
            shape((tokens, 2 * width), LOW),
            shape((2 * TILE, 2 * tokens), WIDE),
        ],
        2,
    )
    normed, grad_low, score_grad, kept, own_answer, *answers = call(
        bind(owner_kernel, top_step),
        "owner",
        (queries, gain_row, base_out, grad_norm, stats, gain_base, masks, own, *received),
        [
            wide_head,
            low_head,
            shape((PEERS * picked, HEAD_DIM), LOW),
            shape((TILE, tokens), WIDE),
        ]
        + [answer] * SPAN,
        3,
    )
    returned = to_peers(answers)
    last_results = call(
        bind(last_head_kernel, top_step),
        "last_head",
        (queries, keys, values, gain_row, expo, normed, grad_low, score_grad, kept, *received),
        [low_head, low_head, wide_head, wide_head],
        20,
    )
    (gain_sum,) = call(bind(gain_kernel, picked), "gain", (own_answer, *returned), [gain_block], 1)
    gain_rest = across(gain_sum, "dp", 1)
    mixed = call(
        bind(mix_kernel, top_step),
        "mix",
        (
            queries,
            keys,
            values,
            gain_row,
            expo,
            base_out,
            grad_norm,
            stats,
            place,
            masks,
            *last_results,
            own_answer,
            *returned,
        ),
        [low_block] * 4,
        20,
        scratch=[pltpu.VMEM((OWNED, *answer.shape), LOW)],
    )
    attended, query_grad, key_grad, value_grad, gain_grad = call(
        finish_kernel,
        "finish",
        (gain_sum, gain_rest, *mixed),
        [row_block] * 4 + [shape((width,), WIDE)],
        1,
    )
    return attended, query_grad, key_grad, value_grad, gain_grad


def shards(*operands):
    one_segment = lax.axis_size("ctx") == SPAN
    if one_segment and operands[0].shape[2] == (OWNED + 1) * HEAD_DIM:
        return one_segment_shards(*operands)
    return general_shards(*operands)


def solution(mesh):
    in_specs = (
        P("dp", "ctx", "head"),
        P("dp", "ctx", "head"),
        P("dp", "ctx", "head"),
        P("dp", "ctx", "head"),
        P("head"),
        P(None, "head"),
    )
    out_specs = (
        P("dp", "ctx", "head"),
        P("dp", "ctx", "head"),
        P("dp", "ctx", "head"),
        P("dp", "ctx", "head"),
        P("head"),
    )
    return jax.shard_map(shards, mesh=mesh, in_specs=in_specs, out_specs=out_specs, check_vma=False)
```

```python
import functools
import math

import jax
import jax.numpy as jnp
from jax import lax
from jax.experimental import pallas as pl
from jax.experimental.pallas import tpu as pltpu
from jax.sharding import PartitionSpec as P

HEAD_DIM = 128
SPAN = 4
R1 = 8


EPS = 1e-06


def swapped(block, axis, bit):
    count = lax.axis_size(axis)
    route = []
    for low in range(count):
        high = low | 1 << bit
        if high != low and high < count:
            route += [(low, high), (high, low)]
    return lax.ppermute(block, axis, route)


def pick_rows(source_rows, dilation, shifts):
    row_count, head_count, head_width = source_rows.shape
    grouped = source_rows.reshape(row_count // dilation, dilation, head_count, head_width)
    hit_mask = jnp.arange(dilation, dtype=jnp.int32).reshape(1, dilation, 1, 1) == shifts.reshape(
        1, 1, head_count, 1
    )
    chosen = jnp.where(hit_mask, grouped, jnp.zeros((), source_rows.dtype))
    return jnp.sum(chosen, axis=1, dtype=source_rows.dtype)


def place_rows(row_values, dilation, shifts):
    row_count, head_count, head_width = row_values.shape
    hit_mask = jnp.arange(dilation, dtype=jnp.int32).reshape(1, dilation, 1, 1) == shifts.reshape(
        1, 1, head_count, 1
    )
    spread = jnp.where(hit_mask, row_values[:, None], jnp.zeros((), row_values.dtype))
    return spread.reshape(row_count * dilation, head_count, head_width)


def level_scores(q_rows, k_rows):
    score_scale = 1.0 / math.sqrt(q_rows.shape[-1])
    return (
        jnp.einsum("qhe,khe->hqk", q_rows, k_rows, preferred_element_type=jnp.float32) * score_scale
    )


def attend(q_rows, k_rows, v_rows):
    scores = level_scores(q_rows, k_rows)
    row_max = jnp.max(scores, axis=-1, keepdims=True)
    log_total = row_max[..., 0] + jnp.log(jnp.sum(jnp.exp(scores - row_max), axis=-1))
    soft_rows = jnp.exp(scores - log_total[..., None]).astype(jnp.bfloat16)
    level_out = jnp.einsum("hqk,khe->qhe", soft_rows, v_rows, preferred_element_type=jnp.float32)
    return (level_out, log_total.T)


def score_grads(q_rows, k_rows, v_rows, log_total, grad_low, row_shift):
    score_scale = 1.0 / math.sqrt(q_rows.shape[-1])
    scores = level_scores(q_rows, k_rows)
    exact_soft = jnp.exp(scores - log_total.T[..., None])
    prob_grad = jnp.einsum("qhe,khe->hqk", grad_low, v_rows, preferred_element_type=jnp.float32)
    score_grad = (exact_soft * (prob_grad + row_shift.T[..., None]) * score_scale).astype(
        jnp.bfloat16
    )
    return (score_grad, exact_soft.astype(jnp.bfloat16))


def key_parts(score_grad, soft_low, q_rows, grad_low):
    k_part = jnp.einsum("hqk,qhe->khe", score_grad, q_rows, preferred_element_type=jnp.float32)
    v_part = jnp.einsum("hqk,qhe->khe", soft_low, grad_low, preferred_element_type=jnp.float32)
    return (k_part, v_part)


def query_part(score_grad, k_rows):
    return jnp.einsum("hqk,khe->qhe", score_grad, k_rows, preferred_element_type=jnp.float32)


def general_shards(queries, keys, values, grad_y, out_gain, offsets):
    tokens = queries.shape[1]
    flat_width = queries.shape[2]
    head_count = flat_width // HEAD_DIM
    row_shape = (tokens, head_count, HEAD_DIM)
    q_own = queries[0].reshape(row_shape)
    k_own = keys[0].reshape(row_shape)
    v_own = values[0].reshape(row_shape)
    ctx_size = lax.axis_size("ctx")
    span_bits = SPAN.bit_length() - 1
    my_place = lax.axis_index("ctx")
    mid_shift = offsets[0]
    top_shift = offsets[1]
    positions = jnp.arange(tokens, dtype=jnp.int32)
    mid_hit = (positions % R1)[:, None] == mid_shift[None, :]
    top_hit = (positions % ctx_size)[:, None] == top_shift[None, :]
    mid_q = pick_rows(q_own, R1, mid_shift)
    mid_k = pick_rows(k_own, R1, mid_shift)
    mid_v = pick_rows(v_own, R1, mid_shift)
    top_q = pick_rows(q_own, ctx_size, top_shift)
    top_k = pick_rows(k_own, ctx_size, top_shift)
    top_v = pick_rows(v_own, ctx_size, top_shift)
    mid_keys = mid_k.reshape(-1, flat_width)
    mid_vals = mid_v.reshape(-1, flat_width)
    top_keys = top_k.reshape(-1, flat_width)
    top_vals = top_v.reshape(-1, flat_width)

    def append_peer(mine, received, level_bit):
        upper_side = my_place >> level_bit & 1 == 1
        return jnp.where(
            upper_side, jnp.concatenate([received, mine], 0), jnp.concatenate([mine, received], 0)
        )

    for level_bit in range(span_bits):
        received = swapped((mid_keys, mid_vals), "ctx", level_bit)
        mid_keys = append_peer(mid_keys, received[0], level_bit)
        mid_vals = append_peer(mid_vals, received[1], level_bit)
    top_keys, top_vals = (
        lax.all_gather(top_keys, "ctx", axis=0, tiled=True),
        lax.all_gather(top_vals, "ctx", axis=0, tiled=True),
    )
    mid_keys = mid_keys.reshape(-1, head_count, HEAD_DIM)
    mid_vals = mid_vals.reshape(-1, head_count, HEAD_DIM)
    top_keys = top_keys.reshape(-1, head_count, HEAD_DIM)
    top_vals = top_vals.reshape(-1, head_count, HEAD_DIM)
    base_out, base_total = attend(q_own, k_own, v_own)
    mid_out, mid_total = attend(mid_q, mid_keys, mid_vals)
    top_out, top_total = attend(top_q, top_keys, top_vals)
    mid_full = place_rows(mid_total[..., None], R1, mid_shift)[..., 0]
    top_full = place_rows(top_total[..., None], ctx_size, top_shift)[..., 0]
    row_max = jnp.maximum(base_total, jnp.where(mid_hit, mid_full, base_total))
    row_max = jnp.maximum(row_max, jnp.where(top_hit, top_full, base_total))
    base_expo = jnp.exp(base_total - row_max)
    mid_expo = jnp.where(mid_hit, jnp.exp(mid_full - row_max), 0.0)
    top_expo = jnp.where(top_hit, jnp.exp(top_full - row_max), 0.0)
    denom = base_expo + mid_expo + top_expo
    base_share = base_expo / denom
    mid_share = mid_expo / denom
    top_share = top_expo / denom
    attn = (
        base_share[..., None] * base_out
        + mid_share[..., None] * place_rows(mid_out, R1, mid_shift)
        + top_share[..., None] * place_rows(top_out, ctx_size, top_shift)
    )
    inv_rms = lax.rsqrt(jnp.mean(attn * attn, axis=-1, keepdims=True) + EPS)
    normed = attn * inv_rms
    gain_rows = out_gain.reshape(head_count, HEAD_DIM)
    attended = (normed * gain_rows).astype(jnp.bfloat16).reshape(1, tokens, flat_width)
    grad_full = grad_y[0].reshape(row_shape).astype(jnp.float32)
    gain_part = jnp.sum(grad_full * normed, axis=0).reshape(flat_width)
    gain_grad = lax.psum(gain_part, ("dp", "ctx"))
    grad_norm = grad_full * gain_rows
    grad_attn = inv_rms * (
        grad_norm - normed * jnp.mean(grad_norm * normed, axis=-1, keepdims=True)
    )
    inner = jnp.sum(grad_attn * attn, axis=-1)
    base_low = (base_share[..., None] * grad_attn).astype(jnp.bfloat16)
    base_shift = -(base_share * inner)
    base_grad, base_soft = score_grads(q_own, k_own, v_own, base_total, base_low, base_shift)
    base_dq = query_part(base_grad, k_own)
    base_dk, base_dv = key_parts(base_grad, base_soft, q_own, base_low)
    mid_sel = pick_rows(mid_share[..., None], R1, mid_shift)[..., 0]
    mid_low = (mid_sel[..., None] * pick_rows(grad_attn, R1, mid_shift)).astype(jnp.bfloat16)
    mid_row_shift = -(mid_sel * pick_rows(inner[..., None], R1, mid_shift)[..., 0])
    mid_grad, mid_soft = score_grads(mid_q, mid_keys, mid_vals, mid_total, mid_low, mid_row_shift)
    mid_dq = query_part(mid_grad, mid_keys)
    mid_dk, mid_dv = key_parts(mid_grad, mid_soft, mid_q, mid_low)
    mid_dk = mid_dk.reshape(-1, flat_width)
    mid_dv = mid_dv.reshape(-1, flat_width)
    for level_bit in reversed(range(span_bits)):
        half_rows = mid_dk.shape[0] // 2
        upper_side = my_place >> level_bit & 1 == 1
        keep_k = jnp.where(upper_side, mid_dk[half_rows:], mid_dk[:half_rows])
        keep_v = jnp.where(upper_side, mid_dv[half_rows:], mid_dv[:half_rows])
        send_k = jnp.where(upper_side, mid_dk[:half_rows], mid_dk[half_rows:])
        send_v = jnp.where(upper_side, mid_dv[:half_rows], mid_dv[half_rows:])
        received = (
            swapped(send_k.astype(jnp.bfloat16), "ctx", level_bit).astype(send_k.dtype),
            swapped(send_v.astype(jnp.bfloat16), "ctx", level_bit).astype(send_v.dtype),
        )
        mid_dk = keep_k + received[0]
        mid_dv = keep_v + received[1]
    mid_dk = mid_dk.reshape(-1, head_count, HEAD_DIM)
    mid_dv = mid_dv.reshape(-1, head_count, HEAD_DIM)
    top_sel = pick_rows(top_share[..., None], ctx_size, top_shift)[..., 0]
    top_low = (top_sel[..., None] * pick_rows(grad_attn, ctx_size, top_shift)).astype(jnp.bfloat16)
    top_row_shift = -(top_sel * pick_rows(inner[..., None], ctx_size, top_shift)[..., 0])
    top_grad, top_soft = score_grads(top_q, top_keys, top_vals, top_total, top_low, top_row_shift)
    top_dq = query_part(top_grad, top_keys)
    gathered_dk, gathered_dv = key_parts(top_grad, top_soft, top_q, top_low)
    summed = (
        lax.psum_scatter(
            gathered_dk.reshape(-1, flat_width), "ctx", scatter_dimension=0, tiled=True
        ),
        lax.psum_scatter(
            gathered_dv.reshape(-1, flat_width), "ctx", scatter_dimension=0, tiled=True
        ),
    )
    top_dk = summed[0].reshape(-1, head_count, HEAD_DIM)
    top_dv = summed[1].reshape(-1, head_count, HEAD_DIM)
    query_grad = (
        base_dq + place_rows(mid_dq, R1, mid_shift) + place_rows(top_dq, ctx_size, top_shift)
    )
    key_grad = base_dk + place_rows(mid_dk, R1, mid_shift) + place_rows(top_dk, ctx_size, top_shift)
    value_grad = (
        base_dv + place_rows(mid_dv, R1, mid_shift) + place_rows(top_dv, ctx_size, top_shift)
    )
    out_shape = (1, tokens, flat_width)
    return (
        attended,
        query_grad.astype(jnp.bfloat16).reshape(out_shape),
        key_grad.astype(jnp.bfloat16).reshape(out_shape),
        value_grad.astype(jnp.bfloat16).reshape(out_shape),
        gain_grad,
    )


VMEM_SPEC = pl.BlockSpec(memory_space=pltpu.VMEM)
PEERS = SPAN - 1
OWNED = SPAN
TILE = 8
STAT_TILES = 2 * TILE
PIECES = 3
NEVER = -1e30
START_ORDER = (3, 1, 2)
LOW = jnp.bfloat16
WIDE = jnp.float32
PLAIN_VMEM = 16 * 1024 * 1024


def contract(left, right, left_dim, right_dim):
    return lax.dot_general(
        left, right, (((left_dim,), (right_dim,)), ((), ())), preferred_element_type=WIDE
    )


def head_cols(head):
    return pl.ds(head * HEAD_DIM, HEAD_DIM)


def picked_counts(tokens, top_step):
    return tokens // top_step, tokens // R1


def offset_of(offsets_ref, level, head):
    return offsets_ref[level : level + 1, head : head + 1]


def pick_matrix(offsets_ref, head, tokens, top_step, picked_axis):
    top_rows, _ = picked_counts(tokens, top_step)
    row = lax.broadcasted_iota(jnp.int32, (tokens, tokens), picked_axis)
    position = lax.broadcasted_iota(jnp.int32, (tokens, tokens), 1 - picked_axis)
    wanted = jnp.where(
        row < top_rows,
        row * top_step + offset_of(offsets_ref, 1, head),
        (row - top_rows) * R1 + offset_of(offsets_ref, 0, head),
    )
    return jnp.where(position == wanted, 1.0, 0.0).astype(LOW)


def rolled(row, shift):
    return pltpu.roll(row, shift % row.shape[1], 1)


def lane_window(row, start, count):
    lane = lax.broadcasted_iota(jnp.int32, row.shape, 1)
    return jnp.where((lane >= start) & (lane < start + count), row, 0.0)


def hit_row(offset, step, tokens):
    position = lax.broadcasted_iota(jnp.int32, (1, tokens), 1)
    return jnp.where(position % step == offset, 1.0, 0.0)


def piece_rows(row, others=None):
    pieces = []
    for _ in range(PIECES):
        piece = row.astype(LOW).astype(WIDE)
        pieces.append(piece)
        row = row - piece
    if others is None:
        others = jnp.zeros((TILE - PIECES, row.shape[1]), WIDE)
    return jnp.concatenate(pieces + [others], 0)


def gain_pieces(rows):
    high = rows.astype(LOW)
    return high, (rows - high.astype(WIDE)).astype(LOW)


def joined_row(rows, first):
    total = rows[first : first + 1]
    for piece in range(1, PIECES):
        total = total + rows[first + piece : first + piece + 1]
    return total


def gain_row_of(ones, product):
    high, rest = gain_pieces(product)
    return (contract(ones, high, 1, 1) + contract(ones, rest, 1, 1))[:1]


def column_mean(block):
    return jnp.mean(block, axis=0, keepdims=True)


def norm_backward(attn, grad_norm):
    inv_rms = lax.rsqrt(column_mean(attn * attn) + EPS)
    normed = attn * inv_rms
    product = grad_norm * normed
    grad_attn = inv_rms * (grad_norm - normed * column_mean(product))
    inner = jnp.sum(grad_attn * attn, axis=0, keepdims=True)
    return normed, product, grad_attn, inner


def nearest_first(refs):
    by_distance = dict(zip(START_ORDER, refs[1:]))
    return [refs[0], *[by_distance[distance] for distance in range(1, SPAN)]]


def picks_kernel(top_step, offsets_ref, picks_ref):
    tokens = picks_ref.shape[0]
    last = offsets_ref.shape[1] - 1
    for head in range(last + 1):
        picks_ref[:, head_cols(head)] = pick_matrix(offsets_ref, head, tokens, top_step, 0)
    key_row = lax.broadcasted_iota(jnp.int32, (tokens, 1), 0)
    times = 1.0
    for level, step in ((0, R1), (1, top_step)):
        offset = offset_of(offsets_ref, level, last)
        hit_column = jnp.where(key_row % step == offset, 1.0, 0.0)
        times = times + hit_column * hit_row(offset, step, tokens)
    picks_ref[:, head_cols(last + 1)] = times.astype(LOW)


def pack_kernel(top_step, picks_ref, q_ref, k_ref, v_ref, grad_ref, *refs):
    payload_refs, (expo_ref, out_ref, stats_ref, held_ref) = refs[:SPAN], refs[SPAN:]
    tokens, width = q_ref.shape[1:]
    heads = range(width // HEAD_DIM)
    owned = range(OWNED)
    me = lax.axis_index("ctx")
    picked = sum(picked_counts(tokens, top_step))
    score_scale = 1.0 / math.sqrt(HEAD_DIM)
    q_rows, k_rows, v_rows, grad_rows = [
        [ref[0, :, head_cols(head)] for head in heads] for ref in (q_ref, k_ref, v_ref, grad_ref)
    ]
    picks = [picks_ref[:, head_cols(head)] for head in heads]
    scores = [contract(k_rows[head], q_rows[head], 1, 1) * score_scale for head in heads]
    moved = [
        contract(
            picks[head][:picked],
            jnp.concatenate([q_rows[head], k_rows[head], v_rows[head], grad_rows[head]], 1),
            1,
            0,
        ).astype(LOW)
        for head in owned
    ]
    shared = [
        contract(
            picks[head][:picked], jnp.concatenate([k_rows[head], v_rows[head]], 1), 1, 0
        ).astype(LOW)
        for head in heads[OWNED:]
    ]
    top_scores = [jnp.max(block, axis=0, keepdims=True) for block in scores]
    expos = [jnp.exp(scores[head] - top_scores[head]) for head in heads]
    times = picks_ref[:, head_cols(len(heads))].astype(WIDE)
    for head in heads[OWNED:]:
        expos[head] = times * expos[head]
    expo_lows = [expo.astype(LOW) for expo in expos]
    outs = [contract(v_rows[head], expo_lows[head], 0, 0) for head in heads]
    totals = [jnp.sum(expo, axis=0, keepdims=True) for expo in expos]
    for head in heads:
        expo_ref[:, head_cols(head)] = expo_lows[head]
        stats_ref[head : head + 1, :] = top_scores[head]
        stats_ref[TILE + head : TILE + head + 1, :] = totals[head]
    for head in owned:
        outs[head] = outs[head] * (1.0 / totals[head])
    outs = [out.astype(LOW) for out in outs]
    picked_outs = [
        contract(picks[head][:picked], outs[head], 1, 1).astype(LOW) for head in owned
    ]
    for head in heads:
        out_ref[:, head_cols(head)] = outs[head]
    for head in owned:
        pieces = piece_rows(top_scores[head] + jnp.log(totals[head])).astype(LOW)
        stat_rows = contract(pieces, picks[head], 1, 1)
        blocks = [moved[head][:, block * HEAD_DIM : (block + 1) * HEAD_DIM] for block in range(4)]
        blocks.append(picked_outs[head])
        blocks += [shared[0][:, :HEAD_DIM], shared[0][:, HEAD_DIM:]]
        blocks.append(jnp.concatenate([stat_rows, jnp.zeros_like(stat_rows)], 0).astype(LOW))
        held_ref[head] = jnp.concatenate(blocks, 0)
    for distance, payload_ref in enumerate(payload_refs):
        payload_ref[...] = held_ref[me ^ distance]


def prepare_kernel(top_step, offsets_ref, grad_ref, gain_ref, out_ref, *refs):
    grad_norm_ref, gain_part_ref, place_ref, masks_ref = refs
    tokens, width = grad_ref.shape[1:]
    heads = range(width // HEAD_DIM)
    top_rows = tokens // top_step
    ones = jnp.ones((TILE, tokens), LOW)
    column = lax.broadcasted_iota(jnp.int32, (tokens, tokens), 1)
    gain_part_ref[...] = jnp.zeros(gain_part_ref.shape, WIDE)
    me = lax.axis_index("ctx")
    mid_rows = tokens // R1
    top_all, queries = SPAN * top_rows, SPAN * (top_rows + mid_rows)
    mid_offset, top_offset = [
        sum(
            jnp.where(me == head, offset_of(offsets_ref, level, head), 0) for head in range(OWNED)
        )
        for level in (0, 1)
    ]
    lane = lax.broadcasted_iota(jnp.int32, (1, queries), 1)
    is_top = jnp.where(lane < top_all, 1.0, 0.0)
    top_in_mid = jnp.where(((lane % top_rows) * top_step + top_offset) % R1 == mid_offset, 1.0, 0.0)
    both_flag = jnp.where(mid_offset % top_step == top_offset, 1.0, 0.0)
    sees_top = is_top + (1.0 - is_top) * both_flag
    sees_mid = is_top * top_in_mid + (1.0 - is_top)
    masks_ref[0:1, :queries] = (1.0 - sees_top) * NEVER
    masks_ref[1:2, :queries] = (1.0 - sees_mid) * NEVER
    masks_ref[2:3, :queries] = is_top + (1.0 - is_top) * (1.0 - both_flag)
    last = len(heads) - 1
    for row, (level, step) in enumerate(((1, top_step), (0, R1))):
        hits = hit_row(offset_of(offsets_ref, level, last), step, tokens)
        masks_ref[3 + row : 4 + row, :tokens] = (1.0 - hits) * NEVER
    grad_norms = [
        (grad_ref[0, :, head_cols(head)].astype(WIDE) * gain_ref[:, head_cols(head)]).T
        for head in heads
    ]
    for head in heads:
        cols = head_cols(head)
        grad_norm_ref[:, cols] = grad_norms[head]
        picks = pick_matrix(offsets_ref, head, tokens, top_step, 1)
        place_ref[:, cols] = picks
    for head in range(OWNED):
        cols = head_cols(head)
        mid_offset, top_offset = [offset_of(offsets_ref, level, head) for level in (0, 1)]
        seen = jnp.maximum(
            hit_row(top_offset, top_step, tokens), hit_row(mid_offset, R1, tokens)
        )
        masks_ref[TILE + head : TILE + head + 1, :tokens] = seen
        attn = out_ref[:, cols].astype(WIDE)
        normed = attn * lax.rsqrt(column_mean(attn * attn) + EPS)
        product = grad_norms[head] * normed * (1.0 - seen)
        gain_part_ref[:, cols] = gain_row_of(ones, product) / gain_ref[:, cols]
        both = mid_offset % top_step == top_offset
        kept = jnp.where(column < top_rows, 1.0, jnp.where(both, 0.0, 1.0)).astype(LOW)
        picks = pick_matrix(offsets_ref, head, tokens, top_step, 1)
        place_ref[:, head_cols(len(heads) + head)] = picks * kept


def owner_kernel(top_step, q_ref, gain_ref, out_ref, grad_norm_ref, *refs):
    stats_ref, gain_base_ref, masks_ref = refs[:3]
    payload_refs, refs = nearest_first(refs[3 : 3 + SPAN]), refs[3 + SPAN :]
    normed_ref, grad_low_ref, score_grad_ref, kept_ref = refs[:4]
    return_refs = refs[4:]
    tokens = q_ref.shape[1]
    heads = q_ref.shape[2] // HEAD_DIM
    top_rows, mid_rows = picked_counts(tokens, top_step)
    picked = top_rows + mid_rows
    top_all, mid_all = SPAN * top_rows, SPAN * mid_rows
    queries = top_all + mid_all
    score_scale = 1.0 / math.sqrt(HEAD_DIM)
    me = lax.axis_index("ctx")
    ones = jnp.ones((TILE, tokens), LOW)

    def by_level(block):
        start = block * picked
        return jnp.concatenate(
            [ref[start : start + top_rows] for ref in payload_refs]
            + [ref[start + top_rows : start + picked] for ref in payload_refs],
            0,
        )

    def per_level(top_row, mid_row):
        return jnp.concatenate(
            [
                jnp.broadcast_to(top_row, (top_all, queries)),
                jnp.broadcast_to(mid_row, (mid_all, queries)),
            ],
            0,
        )

    q_rows, k_rows, v_rows, grad_rows, base_rows = [by_level(block) for block in range(5)]
    stat_start = 7 * picked
    logs = [
        joined_row(ref[stat_start : stat_start + STAT_TILES].astype(WIDE), 0)
        for ref in payload_refs
    ]
    base_top_log = sum(
        rolled(lane_window(log, 0, top_rows), slot * top_rows) for slot, log in enumerate(logs)
    )
    base_mid_log = sum(
        rolled(lane_window(log, top_rows, mid_rows), slot * mid_rows - top_rows)
        for slot, log in enumerate(logs)
    )
    base_log = jnp.concatenate([base_top_log, base_mid_log[:, :mid_all]], 1)
    gain_row = jnp.zeros((1, HEAD_DIM), WIDE)
    for head in range(OWNED):
        gain_row = gain_row + jnp.where(me == head, 1.0, 0.0) * gain_ref[:, head_cols(head)]
    lane = lax.broadcasted_iota(jnp.int32, (1, queries), 1)
    is_top = jnp.where(lane < top_all, 1.0, 0.0)
    bias = per_level(masks_ref[0:1, :queries], masks_ref[1:2, :queries])
    last = heads - 1
    cols = head_cols(last)
    peers = payload_refs[1:]
    q_last = q_ref[0, :, cols]
    k_peers = jnp.concatenate([ref[5 * picked : 6 * picked] for ref in peers], 0)
    v_peers = jnp.concatenate([ref[6 * picked : 7 * picked] for ref in peers], 0)
    last_biases = [
        jnp.broadcast_to(masks_ref[row : row + 1, :tokens], (count, tokens))
        for row, count in ((3, top_rows), (4, mid_rows))
    ]
    scores = contract(k_rows, q_rows, 1, 1) * score_scale + bias
    scores_last = contract(k_peers, q_last, 1, 1) * score_scale + jnp.concatenate(
        last_biases * PEERS, 0
    )
    base_attn = base_rows.astype(WIDE).T
    grad_norm = (grad_rows.astype(WIDE) * gain_row).T
    top_score = jnp.maximum(base_log, jnp.max(scores, axis=0, keepdims=True))
    base_top, base_total = stats_ref[last : last + 1, :], stats_ref[TILE + last : TILE + last + 1, :]
    top_last = jnp.maximum(base_top, jnp.max(scores_last, axis=0, keepdims=True))
    expo = jnp.exp(scores - top_score)
    expo_last = jnp.exp(scores_last - top_last)
    factor = jnp.exp(base_log - top_score)
    factor_last = jnp.exp(base_top - top_last)
    total = factor + jnp.sum(expo, axis=0, keepdims=True)
    total_last = factor_last * base_total + jnp.sum(expo_last, axis=0, keepdims=True)
    inv_total, inv_last = 1.0 / total, 1.0 / total_last
    expo_low, expo_last_low = expo.astype(LOW), expo_last.astype(LOW)
    attn = (factor * base_attn + contract(v_rows, expo_low, 0, 0)) * inv_total
    attn_last = (
        factor_last * out_ref[:, cols].astype(WIDE) + contract(v_peers, expo_last_low, 0, 0)
    ) * inv_last
    _, product, grad_attn, inner = norm_backward(attn, grad_norm)
    normed_last, product_last, grad_attn_last, inner_last = norm_backward(
        attn_last, grad_norm_ref[:, cols]
    )
    grad_low, inner = (grad_attn * inv_total).astype(LOW), inner * inv_total
    grad_last_low = (grad_attn_last * inv_last).astype(LOW)
    base_factor = factor_last * inv_last
    spans = (slice(0, top_all), slice(top_all, queries))
    prob_grads = [contract(v_rows[span], grad_low[:, span], 1, 0) for span in spans]
    prob_grad_last = contract(v_peers, grad_last_low, 1, 0)
    score_grads = [
        (expo[span, span] * (prob_grad - inner[:, span]) * score_scale).astype(LOW)
        for span, prob_grad in zip(spans, prob_grads)
    ]
    score_grad_last = (
        expo_last * (prob_grad_last - inner_last * inv_last) * score_scale
    ).astype(LOW)
    dks = [
        contract(score_grad, q_rows[span], 1, 0).astype(LOW)
        for span, score_grad in zip(spans, score_grads)
    ]
    dk_last = contract(score_grad_last, q_last, 1, 0).astype(LOW)
    dvs = [
        contract(expo_low[span, span], grad_low[:, span], 1, 1).astype(LOW) for span in spans
    ]
    dv_last = contract(expo_last_low, grad_last_low, 1, 1).astype(LOW)
    dqs = [
        contract(score_grad, k_rows[span], 0, 0).astype(LOW)
        for span, score_grad in zip(spans, score_grads)
    ]
    attn_rows = attn.T.astype(LOW)
    attn_parts = [attn_rows[span] for span in spans]
    log_total = top_score + jnp.log(total)
    padding = jnp.zeros((1, top_all - mid_all), WIDE)
    once = masks_ref[2:3, :queries]
    ones_all = jnp.ones((TILE, queries), LOW)
    own_gain = gain_row_of(ones_all, product * once) / gain_row
    gain_rows = [
        gain_base_ref[:, head_cols(head)] + jnp.where(me == head, 1.0, 0.0) * own_gain
        for head in range(OWNED)
    ]
    gain_rows.append(gain_row_of(ones, product_last) / gain_ref[:, cols])
    gain_high, gain_rest = [
        rows.astype(WIDE) for rows in gain_pieces(jnp.concatenate(gain_rows, 0))
    ]
    top_log, mid_log = log_total[:, :top_all], jnp.concatenate(
        [log_total[:, top_all:], padding], 1
    )
    empty = jnp.zeros((PIECES, HEAD_DIM), WIDE)
    for distance, return_ref in enumerate(return_refs):
        blocks = []
        for top_block, mid_block in (dqs, dks, dvs, attn_parts):
            blocks.append(top_block[distance * top_rows : (distance + 1) * top_rows])
            blocks.append(mid_block[distance * mid_rows : (distance + 1) * mid_rows])
        start = max(distance - 1, 0) * picked
        blocks += [dk_last[start : start + picked], dv_last[start : start + picked]]
        log_row = lane_window(rolled(top_log, -distance * top_rows), 0, top_rows) + lane_window(
            rolled(mid_log, top_rows - distance * mid_rows), top_rows, mid_rows
        )
        log_rows = [piece_rows(log_row, gain_high), empty, gain_rest]
        blocks.append(jnp.concatenate(log_rows, 0).astype(LOW))
        return_ref[...] = jnp.concatenate(blocks, 0)
    normed_ref[...] = normed_last
    grad_low_ref[...] = (grad_attn_last * base_factor).astype(LOW)
    score_grad_ref[...] = score_grad_last
    kept_ref[0:1, :] = inner_last * base_factor


def last_head_kernel(top_step, q_ref, k_ref, v_ref, gain_ref, expo_ref, *refs):
    normed_ref, grad_low_ref, peer_score_grad_ref, kept_ref, *peers = refs[: 4 + PEERS]
    peers = nearest_first([None, *peers])[1:]
    attended_ref, dq_ref, dk_ref, dv_ref = refs[4 + PEERS :]
    picked = sum(picked_counts(q_ref.shape[1], top_step))
    score_scale = 1.0 / math.sqrt(HEAD_DIM)
    cols = head_cols(q_ref.shape[2] // HEAD_DIM - 1)
    attended_ref[...] = (normed_ref[...].T * gain_ref[:, cols]).astype(LOW)
    k_peers = jnp.concatenate([ref[5 * picked : 6 * picked] for ref in peers], 0)
    grad_low = grad_low_ref[...]
    expo_low = expo_ref[:, cols]
    prob_grad = contract(v_ref[0, :, cols], grad_low, 1, 0)
    score_grad = (
        expo_low.astype(WIDE) * (prob_grad - kept_ref[0:1, :]) * score_scale
    ).astype(LOW)
    dk_ref[...] = contract(score_grad, q_ref[0, :, cols], 1, 0)
    dv_ref[...] = contract(expo_low, grad_low, 1, 1)
    dq_ref[...] = (
        contract(score_grad, k_ref[0, :, cols], 0, 0)
        + contract(peer_score_grad_ref[...], k_peers, 0, 0)
    ).astype(LOW)


def gain_kernel(picked, *refs):
    return_refs, gain_ref = nearest_first(refs[:SPAN]), refs[SPAN]
    tiles = [ref[6 * picked : 6 * picked + STAT_TILES].astype(WIDE) for ref in return_refs]
    parts = [tile[PIECES:TILE] + tile[TILE + PIECES :] for tile in tiles]
    total = (parts[0] + parts[1]) + (parts[2] + parts[3])
    for head in range(gain_ref.shape[1] // HEAD_DIM):
        gain_ref[:, head_cols(head)] = total[head : head + 1]


def mix_kernel(top_step, q_ref, k_ref, v_ref, gain_ref, expo_ref, out_ref, *refs):
    grad_norm_ref, stats_ref, place_ref, masks_ref = refs[:4]
    last_attended_ref, last_dq_ref, last_dk_ref, last_dv_ref = refs[4:8]
    return_refs, refs = nearest_first(refs[8 : 8 + SPAN]), refs[8 + SPAN :]
    attended_ref, dq_ref, dk_ref, dv_ref, placed_ref = refs
    tokens, width = v_ref.shape[1:]
    count = width // HEAD_DIM
    picked = sum(picked_counts(tokens, top_step))
    score_scale = 1.0 / math.sqrt(HEAD_DIM)
    me = lax.axis_index("ctx")
    heads = range(OWNED)
    every = [head_cols(head) for head in heads]
    for distance, return_ref in enumerate(return_refs):
        placed_ref[me ^ distance] = return_ref[...]
    once = [place_ref[:, head_cols(count + head)] for head in heads]
    attn_parts = [
        contract(placed_ref[head, 3 * picked : 4 * picked], once[head][:, :picked], 0, 1)
        for head in heads
    ]
    log_parts = [
        contract(placed_ref[head, 6 * picked : 6 * picked + STAT_TILES], once[head], 1, 1)
        for head in heads
    ]
    normeds, grad_lows, inners, inv_totals = [], [], [], []
    for head in heads:
        seen = masks_ref[TILE + head : TILE + head + 1, :tokens] > 0.5
        top_score, total = stats_ref[head : head + 1, :], stats_ref[TILE + head : TILE + head + 1, :]
        base_log = top_score + jnp.log(total)
        log_total = jnp.where(seen, joined_row(log_parts[head], 0), base_log)
        share = jnp.exp(base_log - log_total)
        inv_totals.append(1.0 / total)
        attn = jnp.where(seen, attn_parts[head], out_ref[:, every[head]].astype(WIDE))
        normed, _, grad_attn, inner = norm_backward(attn, grad_norm_ref[:, every[head]])
        normeds.append(normed)
        grad_lows.append((share * grad_attn).astype(LOW))
        inners.append(share * inner)
    prob_grads = [contract(v_ref[0, :, every[head]], grad_lows[head], 1, 0) for head in heads]
    softs = [expo_ref[:, every[head]].astype(WIDE) * inv_totals[head] for head in heads]
    soft_lows = [soft.astype(LOW) for soft in softs]
    score_grads = [
        (softs[head] * (prob_grads[head] - inners[head]) * score_scale).astype(LOW)
        for head in heads
    ]
    dqs = [contract(score_grads[head], k_ref[0, :, every[head]], 0, 0) for head in heads]
    placed = [
        contract(
            place_ref[:, pl.ds(head * HEAD_DIM, picked)],
            jnp.concatenate(
                [placed_ref[head, block * picked : (block + 1) * picked] for block in range(3)], 1
            ),
            1,
            0,
        )
        for head in heads
    ]
    dks = [contract(score_grads[head], q_ref[0, :, every[head]], 1, 0) for head in heads]
    dvs = [contract(soft_lows[head], grad_lows[head], 1, 1) for head in heads]
    last = count - 1
    total = sum(ref[4 * picked : 6 * picked].astype(WIDE) for ref in return_refs[1:]).astype(LOW)
    rows = contract(
        place_ref[:, pl.ds(last * HEAD_DIM, picked)],
        jnp.concatenate([total[:picked], total[picked:]], 1),
        1,
        0,
    )
    for head in heads:
        cols = every[head]
        attended_ref[:, cols] = (normeds[head].T * gain_ref[:, cols]).astype(LOW)
        for which, (block, out_block_ref) in enumerate(
            ((dqs[head], dq_ref), (dks[head], dk_ref), (dvs[head], dv_ref))
        ):
            part = placed[head][:, which * HEAD_DIM : (which + 1) * HEAD_DIM]
            out_block_ref[:, cols] = (block + part).astype(LOW)
    cols = head_cols(last)
    attended_ref[:, cols] = last_attended_ref[...]
    dq_ref[:, cols] = last_dq_ref[...]
    dk_ref[:, cols] = (last_dk_ref[...] + rows[:, :HEAD_DIM]).astype(LOW)
    dv_ref[:, cols] = (last_dv_ref[...] + rows[:, HEAD_DIM:]).astype(LOW)


def finish_kernel(gain_ref, gain_rest_ref, *refs):
    block_refs, result_refs, gain_out_ref = refs[:4], refs[4:8], refs[8]
    for block_ref, result_ref in zip(block_refs, result_refs):
        result_ref[0] = block_ref[...]
    gain_out_ref[...] = (gain_ref[...] + gain_rest_ref[...]).reshape(gain_out_ref.shape)


def across(block, axis, distance):
    route = [(place, place ^ distance) for place in range(lax.axis_size(axis))]
    return lax.ppermute(block, axis, route)


def to_peers(blocks):
    return [across(blocks[distance - 1], "ctx", distance) for distance in START_ORDER]


def call(kernel, name, operands, results, microseconds, vmem=PLAIN_VMEM, scratch=()):
    return pl.pallas_call(
        kernel,
        out_shape=results,
        in_specs=[VMEM_SPEC] * len(operands),
        out_specs=[VMEM_SPEC] * len(results),
        scratch_shapes=scratch,
        compiler_params=pltpu.CompilerParams(vmem_limit_bytes=vmem),
        cost_estimate=pl.CostEstimate(
            flops=int(microseconds * 10**9), bytes_accessed=0, transcendentals=0
        ),
        name=name,
    )(*operands)


def one_segment_shards(queries, keys, values, grad_y, out_gain, offsets):
    tokens, width = queries.shape[1:]
    heads = width // HEAD_DIM
    top_step = lax.axis_size("ctx")
    picked = sum(picked_counts(tokens, top_step))
    shape = jax.ShapeDtypeStruct
    row_block = shape((1, tokens, width), LOW)
    low_block, wide_block = shape((tokens, width), LOW), shape((tokens, width), WIDE)
    low_head, wide_head = shape((tokens, HEAD_DIM), LOW), shape((tokens, HEAD_DIM), WIDE)
    gain_block = shape((1, width), WIDE)
    stats_block = shape((2 * TILE, tokens), WIDE)
    payload = shape((7 * picked + STAT_TILES, HEAD_DIM), LOW)
    answer = shape((6 * picked + STAT_TILES, HEAD_DIM), LOW)
    bind = functools.partial
    gain_row = out_gain.reshape(1, width)
    (picks,) = call(
        bind(picks_kernel, top_step), "picks", (offsets,), [shape((tokens, width + tokens), LOW)], 20
    )
    own, *sent, expo, base_out, stats = call(
        bind(pack_kernel, top_step),
        "pack",
        (picks, queries, keys, values, grad_y),
        [payload] * SPAN + [low_block, low_block, stats_block],
        1,
        scratch=[pltpu.VMEM((OWNED, *payload.shape), LOW)],
    )
    received = to_peers(sent)
    grad_norm, gain_base, place, masks = call(
        bind(prepare_kernel, top_step),
        "prepare",
        (offsets, grad_y, gain_row, base_out),
        [
            wide_block,
            gain_block,
            shape((tokens, 2 * width), LOW),
            shape((2 * TILE, 2 * tokens), WIDE),
        ],
        2,
    )
    normed, grad_low, score_grad, kept, own_answer, *answers = call(
        bind(owner_kernel, top_step),
        "owner",
        (queries, gain_row, base_out, grad_norm, stats, gain_base, masks, own, *received),
        [
            wide_head,
            low_head,
            shape((PEERS * picked, HEAD_DIM), LOW),
            shape((TILE, tokens), WIDE),
        ]
        + [answer] * SPAN,
        3,
    )
    returned = to_peers(answers)
    last_results = call(
        bind(last_head_kernel, top_step),
        "last_head",
        (queries, keys, values, gain_row, expo, normed, grad_low, score_grad, kept, *received),
        [low_head, low_head, wide_head, wide_head],
        20,
    )
    (gain_sum,) = call(bind(gain_kernel, picked), "gain", (own_answer, *returned), [gain_block], 1)
    gain_rest = across(gain_sum, "dp", 1)
    mixed = call(
        bind(mix_kernel, top_step),
        "mix",
        (
            queries,
            keys,
            values,
            gain_row,
            expo,
            base_out,
            grad_norm,
            stats,
            place,
            masks,
            *last_results,
            own_answer,
            *returned,
        ),
        [low_block] * 4,
        20,
        scratch=[pltpu.VMEM((OWNED, *answer.shape), LOW)],
    )
    attended, query_grad, key_grad, value_grad, gain_grad = call(
        finish_kernel,
        "finish",
        (gain_sum, gain_rest, *mixed),
        [row_block] * 4 + [shape((width,), WIDE)],
        1,
    )
    return attended, query_grad, key_grad, value_grad, gain_grad


def shards(*operands):
    one_segment = lax.axis_size("ctx") == SPAN
    if one_segment and operands[0].shape[2] == (OWNED + 1) * HEAD_DIM:
        return one_segment_shards(*operands)
    return general_shards(*operands)


def solution(mesh):
    in_specs = (
        P("dp", "ctx", "head"),
        P("dp", "ctx", "head"),
        P("dp", "ctx", "head"),
        P("dp", "ctx", "head"),
        P("head"),
        P(None, "head"),
    )
    out_specs = (
        P("dp", "ctx", "head"),
        P("dp", "ctx", "head"),
        P("dp", "ctx", "head"),
        P("dp", "ctx", "head"),
        P("head"),
    )
    return jax.shard_map(shards, mesh=mesh, in_specs=in_specs, out_specs=out_specs, check_vma=False)
```

```python
import functools
import math

import jax
import jax.numpy as jnp
from jax import lax
from jax.experimental import pallas as pl
from jax.experimental.pallas import tpu as pltpu
from jax.sharding import PartitionSpec as P

HEAD_DIM = 128
SPAN = 4
R1 = 8


EPS = 1e-06


def swapped(block, axis, bit):
    count = lax.axis_size(axis)
    route = []
    for low in range(count):
        high = low | 1 << bit
        if high != low and high < count:
            route += [(low, high), (high, low)]
    return lax.ppermute(block, axis, route)


def pick_rows(source_rows, dilation, shifts):
    row_count, head_count, head_width = source_rows.shape
    grouped = source_rows.reshape(row_count // dilation, dilation, head_count, head_width)
    hit_mask = jnp.arange(dilation, dtype=jnp.int32).reshape(1, dilation, 1, 1) == shifts.reshape(
        1, 1, head_count, 1
    )
    chosen = jnp.where(hit_mask, grouped, jnp.zeros((), source_rows.dtype))
    return jnp.sum(chosen, axis=1, dtype=source_rows.dtype)


def place_rows(row_values, dilation, shifts):
    row_count, head_count, head_width = row_values.shape
    hit_mask = jnp.arange(dilation, dtype=jnp.int32).reshape(1, dilation, 1, 1) == shifts.reshape(
        1, 1, head_count, 1
    )
    spread = jnp.where(hit_mask, row_values[:, None], jnp.zeros((), row_values.dtype))
    return spread.reshape(row_count * dilation, head_count, head_width)


def level_scores(q_rows, k_rows):
    score_scale = 1.0 / math.sqrt(q_rows.shape[-1])
    return (
        jnp.einsum("qhe,khe->hqk", q_rows, k_rows, preferred_element_type=jnp.float32) * score_scale
    )


def attend(q_rows, k_rows, v_rows):
    scores = level_scores(q_rows, k_rows)
    row_max = jnp.max(scores, axis=-1, keepdims=True)
    log_total = row_max[..., 0] + jnp.log(jnp.sum(jnp.exp(scores - row_max), axis=-1))
    soft_rows = jnp.exp(scores - log_total[..., None]).astype(jnp.bfloat16)
    level_out = jnp.einsum("hqk,khe->qhe", soft_rows, v_rows, preferred_element_type=jnp.float32)
    return (level_out, log_total.T)


def score_grads(q_rows, k_rows, v_rows, log_total, grad_low, row_shift):
    score_scale = 1.0 / math.sqrt(q_rows.shape[-1])
    scores = level_scores(q_rows, k_rows)
    exact_soft = jnp.exp(scores - log_total.T[..., None])
    prob_grad = jnp.einsum("qhe,khe->hqk", grad_low, v_rows, preferred_element_type=jnp.float32)
    score_grad = (exact_soft * (prob_grad + row_shift.T[..., None]) * score_scale).astype(
        jnp.bfloat16
    )
    return (score_grad, exact_soft.astype(jnp.bfloat16))


def key_parts(score_grad, soft_low, q_rows, grad_low):
    k_part = jnp.einsum("hqk,qhe->khe", score_grad, q_rows, preferred_element_type=jnp.float32)
    v_part = jnp.einsum("hqk,qhe->khe", soft_low, grad_low, preferred_element_type=jnp.float32)
    return (k_part, v_part)


def query_part(score_grad, k_rows):
    return jnp.einsum("hqk,khe->qhe", score_grad, k_rows, preferred_element_type=jnp.float32)


def general_shards(queries, keys, values, grad_y, out_gain, offsets):
    tokens = queries.shape[1]
    flat_width = queries.shape[2]
    head_count = flat_width // HEAD_DIM
    row_shape = (tokens, head_count, HEAD_DIM)
    q_own = queries[0].reshape(row_shape)
    k_own = keys[0].reshape(row_shape)
    v_own = values[0].reshape(row_shape)
    ctx_size = lax.axis_size("ctx")
    span_bits = SPAN.bit_length() - 1
    my_place = lax.axis_index("ctx")
    mid_shift = offsets[0]
    top_shift = offsets[1]
    positions = jnp.arange(tokens, dtype=jnp.int32)
    mid_hit = (positions % R1)[:, None] == mid_shift[None, :]
    top_hit = (positions % ctx_size)[:, None] == top_shift[None, :]
    mid_q = pick_rows(q_own, R1, mid_shift)
    mid_k = pick_rows(k_own, R1, mid_shift)
    mid_v = pick_rows(v_own, R1, mid_shift)
    top_q = pick_rows(q_own, ctx_size, top_shift)
    top_k = pick_rows(k_own, ctx_size, top_shift)
    top_v = pick_rows(v_own, ctx_size, top_shift)
    mid_keys = mid_k.reshape(-1, flat_width)
    mid_vals = mid_v.reshape(-1, flat_width)
    top_keys = top_k.reshape(-1, flat_width)
    top_vals = top_v.reshape(-1, flat_width)

    def append_peer(mine, received, level_bit):
        upper_side = my_place >> level_bit & 1 == 1
        return jnp.where(
            upper_side, jnp.concatenate([received, mine], 0), jnp.concatenate([mine, received], 0)
        )

    for level_bit in range(span_bits):
        received = swapped((mid_keys, mid_vals), "ctx", level_bit)
        mid_keys = append_peer(mid_keys, received[0], level_bit)
        mid_vals = append_peer(mid_vals, received[1], level_bit)
    top_keys, top_vals = (
        lax.all_gather(top_keys, "ctx", axis=0, tiled=True),
        lax.all_gather(top_vals, "ctx", axis=0, tiled=True),
    )
    mid_keys = mid_keys.reshape(-1, head_count, HEAD_DIM)
    mid_vals = mid_vals.reshape(-1, head_count, HEAD_DIM)
    top_keys = top_keys.reshape(-1, head_count, HEAD_DIM)
    top_vals = top_vals.reshape(-1, head_count, HEAD_DIM)
    base_out, base_total = attend(q_own, k_own, v_own)
    mid_out, mid_total = attend(mid_q, mid_keys, mid_vals)
    top_out, top_total = attend(top_q, top_keys, top_vals)
    mid_full = place_rows(mid_total[..., None], R1, mid_shift)[..., 0]
    top_full = place_rows(top_total[..., None], ctx_size, top_shift)[..., 0]
    row_max = jnp.maximum(base_total, jnp.where(mid_hit, mid_full, base_total))
    row_max = jnp.maximum(row_max, jnp.where(top_hit, top_full, base_total))
    base_expo = jnp.exp(base_total - row_max)
    mid_expo = jnp.where(mid_hit, jnp.exp(mid_full - row_max), 0.0)
    top_expo = jnp.where(top_hit, jnp.exp(top_full - row_max), 0.0)
    denom = base_expo + mid_expo + top_expo
    base_share = base_expo / denom
    mid_share = mid_expo / denom
    top_share = top_expo / denom
    attn = (
        base_share[..., None] * base_out
        + mid_share[..., None] * place_rows(mid_out, R1, mid_shift)
        + top_share[..., None] * place_rows(top_out, ctx_size, top_shift)
    )
    inv_rms = lax.rsqrt(jnp.mean(attn * attn, axis=-1, keepdims=True) + EPS)
    normed = attn * inv_rms
    gain_rows = out_gain.reshape(head_count, HEAD_DIM)
    attended = (normed * gain_rows).astype(jnp.bfloat16).reshape(1, tokens, flat_width)
    grad_full = grad_y[0].reshape(row_shape).astype(jnp.float32)
    gain_part = jnp.sum(grad_full * normed, axis=0).reshape(flat_width)
    gain_grad = lax.psum(gain_part, ("dp", "ctx"))
    grad_norm = grad_full * gain_rows
    grad_attn = inv_rms * (
        grad_norm - normed * jnp.mean(grad_norm * normed, axis=-1, keepdims=True)
    )
    inner = jnp.sum(grad_attn * attn, axis=-1)
    base_low = (base_share[..., None] * grad_attn).astype(jnp.bfloat16)
    base_shift = -(base_share * inner)
    base_grad, base_soft = score_grads(q_own, k_own, v_own, base_total, base_low, base_shift)
    base_dq = query_part(base_grad, k_own)
    base_dk, base_dv = key_parts(base_grad, base_soft, q_own, base_low)
    mid_sel = pick_rows(mid_share[..., None], R1, mid_shift)[..., 0]
    mid_low = (mid_sel[..., None] * pick_rows(grad_attn, R1, mid_shift)).astype(jnp.bfloat16)
    mid_row_shift = -(mid_sel * pick_rows(inner[..., None], R1, mid_shift)[..., 0])
    mid_grad, mid_soft = score_grads(mid_q, mid_keys, mid_vals, mid_total, mid_low, mid_row_shift)
    mid_dq = query_part(mid_grad, mid_keys)
    mid_dk, mid_dv = key_parts(mid_grad, mid_soft, mid_q, mid_low)
    mid_dk = mid_dk.reshape(-1, flat_width)
    mid_dv = mid_dv.reshape(-1, flat_width)
    for level_bit in reversed(range(span_bits)):
        half_rows = mid_dk.shape[0] // 2
        upper_side = my_place >> level_bit & 1 == 1
        keep_k = jnp.where(upper_side, mid_dk[half_rows:], mid_dk[:half_rows])
        keep_v = jnp.where(upper_side, mid_dv[half_rows:], mid_dv[:half_rows])
        send_k = jnp.where(upper_side, mid_dk[:half_rows], mid_dk[half_rows:])
        send_v = jnp.where(upper_side, mid_dv[:half_rows], mid_dv[half_rows:])
        received = (
            swapped(send_k.astype(jnp.bfloat16), "ctx", level_bit).astype(send_k.dtype),
            swapped(send_v.astype(jnp.bfloat16), "ctx", level_bit).astype(send_v.dtype),
        )
        mid_dk = keep_k + received[0]
        mid_dv = keep_v + received[1]
    mid_dk = mid_dk.reshape(-1, head_count, HEAD_DIM)
    mid_dv = mid_dv.reshape(-1, head_count, HEAD_DIM)
    top_sel = pick_rows(top_share[..., None], ctx_size, top_shift)[..., 0]
    top_low = (top_sel[..., None] * pick_rows(grad_attn, ctx_size, top_shift)).astype(jnp.bfloat16)
    top_row_shift = -(top_sel * pick_rows(inner[..., None], ctx_size, top_shift)[..., 0])
    top_grad, top_soft = score_grads(top_q, top_keys, top_vals, top_total, top_low, top_row_shift)
    top_dq = query_part(top_grad, top_keys)
    gathered_dk, gathered_dv = key_parts(top_grad, top_soft, top_q, top_low)
    summed = (
        lax.psum_scatter(
            gathered_dk.reshape(-1, flat_width), "ctx", scatter_dimension=0, tiled=True
        ),
        lax.psum_scatter(
            gathered_dv.reshape(-1, flat_width), "ctx", scatter_dimension=0, tiled=True
        ),
    )
    top_dk = summed[0].reshape(-1, head_count, HEAD_DIM)
    top_dv = summed[1].reshape(-1, head_count, HEAD_DIM)
    query_grad = (
        base_dq + place_rows(mid_dq, R1, mid_shift) + place_rows(top_dq, ctx_size, top_shift)
    )
    key_grad = base_dk + place_rows(mid_dk, R1, mid_shift) + place_rows(top_dk, ctx_size, top_shift)
    value_grad = (
        base_dv + place_rows(mid_dv, R1, mid_shift) + place_rows(top_dv, ctx_size, top_shift)
    )
    out_shape = (1, tokens, flat_width)
    return (
        attended,
        query_grad.astype(jnp.bfloat16).reshape(out_shape),
        key_grad.astype(jnp.bfloat16).reshape(out_shape),
        value_grad.astype(jnp.bfloat16).reshape(out_shape),
        gain_grad,
    )


VMEM_SPEC = pl.BlockSpec(memory_space=pltpu.VMEM)
PEERS = SPAN - 1
OWNED = SPAN
TILE = 8
STAT_TILES = 2 * TILE
PIECES = 3
NEVER = -1e30
START_ORDER = (3, 1, 2)
LOW = jnp.bfloat16
WIDE = jnp.float32
PLAIN_VMEM = 16 * 1024 * 1024


def contract(left, right, left_dim, right_dim):
    return lax.dot_general(
        left, right, (((left_dim,), (right_dim,)), ((), ())), preferred_element_type=WIDE
    )


def head_cols(head):
    return pl.ds(head * HEAD_DIM, HEAD_DIM)


def picked_counts(tokens, top_step):
    return tokens // top_step, tokens // R1


def offset_of(offsets_ref, level, head):
    return offsets_ref[level : level + 1, head : head + 1]


def pick_matrix(offsets_ref, head, tokens, top_step, picked_axis):
    top_rows, _ = picked_counts(tokens, top_step)
    row = lax.broadcasted_iota(jnp.int32, (tokens, tokens), picked_axis)
    position = lax.broadcasted_iota(jnp.int32, (tokens, tokens), 1 - picked_axis)
    wanted = jnp.where(
        row < top_rows,
        row * top_step + offset_of(offsets_ref, 1, head),
        (row - top_rows) * R1 + offset_of(offsets_ref, 0, head),
    )
    return jnp.where(position == wanted, 1.0, 0.0).astype(LOW)


def rolled(row, shift):
    return pltpu.roll(row, shift % row.shape[1], 1)


def lane_window(row, start, count):
    lane = lax.broadcasted_iota(jnp.int32, row.shape, 1)
    return jnp.where((lane >= start) & (lane < start + count), row, 0.0)


def hit_row(offset, step, tokens):
    position = lax.broadcasted_iota(jnp.int32, (1, tokens), 1)
    return jnp.where(position % step == offset, 1.0, 0.0)


def piece_rows(row, others=None):
    pieces = []
    for _ in range(PIECES):
        piece = row.astype(LOW).astype(WIDE)
        pieces.append(piece)
        row = row - piece
    if others is None:
        others = jnp.zeros((TILE - PIECES, row.shape[1]), WIDE)
    return jnp.concatenate(pieces + [others], 0)


def gain_pieces(rows):
    high = rows.astype(LOW)
    return high, (rows - high.astype(WIDE)).astype(LOW)


def joined_row(rows, first):
    total = rows[first : first + 1]
    for piece in range(1, PIECES):
        total = total + rows[first + piece : first + piece + 1]
    return total


def gain_row_of(ones, product):
    high, rest = gain_pieces(product)
    return (contract(ones, high, 1, 1) + contract(ones, rest, 1, 1))[:1]


def column_mean(block):
    return jnp.mean(block, axis=0, keepdims=True)


def norm_backward(attn, grad_norm):
    inv_rms = lax.rsqrt(column_mean(attn * attn) + EPS)
    normed = attn * inv_rms
    product = grad_norm * normed
    grad_attn = inv_rms * (grad_norm - normed * column_mean(product))
    inner = jnp.sum(grad_attn * attn, axis=0, keepdims=True)
    return normed, product, grad_attn, inner


def nearest_first(refs):
    by_distance = dict(zip(START_ORDER, refs[1:]))
    return [refs[0], *[by_distance[distance] for distance in range(1, SPAN)]]


def picks_kernel(top_step, offsets_ref, picks_ref):
    tokens = picks_ref.shape[0]
    last = offsets_ref.shape[1] - 1
    for head in range(last + 1):
        picks_ref[:, head_cols(head)] = pick_matrix(offsets_ref, head, tokens, top_step, 0)
    key_row = lax.broadcasted_iota(jnp.int32, (tokens, 1), 0)
    times = 1.0
    for level, step in ((0, R1), (1, top_step)):
        offset = offset_of(offsets_ref, level, last)
        hit_column = jnp.where(key_row % step == offset, 1.0, 0.0)
        times = times + hit_column * hit_row(offset, step, tokens)
    picks_ref[:, head_cols(last + 1)] = times.astype(LOW)


def pack_kernel(top_step, picks_ref, q_ref, k_ref, v_ref, grad_ref, *refs):
    payload_refs, held_ref = refs[:SPAN], refs[SPAN]
    tokens, width = q_ref.shape[1:]
    heads = range(width // HEAD_DIM)
    owned = range(OWNED)
    me = lax.axis_index("ctx")
    picked = sum(picked_counts(tokens, top_step))
    score_scale = 1.0 / math.sqrt(HEAD_DIM)
    q_rows, k_rows, v_rows, grad_rows = [
        [ref[0, :, head_cols(head)] for head in heads] for ref in (q_ref, k_ref, v_ref, grad_ref)
    ]
    picks = [picks_ref[:, head_cols(head)] for head in heads]
    scores = [contract(k_rows[head], q_rows[head], 1, 1) * score_scale for head in owned]
    moved = [
        contract(
            picks[head][:picked],
            jnp.concatenate([q_rows[head], k_rows[head], v_rows[head], grad_rows[head]], 1),
            1,
            0,
        ).astype(LOW)
        for head in owned
    ]
    shared = [
        contract(
            picks[head][:picked], jnp.concatenate([k_rows[head], v_rows[head]], 1), 1, 0
        ).astype(LOW)
        for head in heads[OWNED:]
    ]
    top_scores = [jnp.max(block, axis=0, keepdims=True) for block in scores]
    expos = [jnp.exp(scores[head] - top_scores[head]) for head in owned]
    expo_lows = [expo.astype(LOW) for expo in expos]
    outs = [contract(v_rows[head], expo_lows[head], 0, 0) for head in owned]
    totals = [jnp.sum(expo, axis=0, keepdims=True) for expo in expos]
    outs = [(outs[head] * (1.0 / totals[head])).astype(LOW) for head in owned]
    picked_outs = [
        contract(picks[head][:picked], outs[head], 1, 1).astype(LOW) for head in owned
    ]
    for head in owned:
        pieces = piece_rows(top_scores[head] + jnp.log(totals[head])).astype(LOW)
        stat_rows = contract(pieces, picks[head], 1, 1)
        blocks = [moved[head][:, block * HEAD_DIM : (block + 1) * HEAD_DIM] for block in range(4)]
        blocks.append(picked_outs[head])
        blocks += [shared[0][:, :HEAD_DIM], shared[0][:, HEAD_DIM:]]
        blocks.append(jnp.concatenate([stat_rows, jnp.zeros_like(stat_rows)], 0).astype(LOW))
        held_ref[head] = jnp.concatenate(blocks, 0)
    for distance, payload_ref in enumerate(payload_refs):
        payload_ref[...] = held_ref[me ^ distance]


def prepare_kernel(top_step, offsets_ref, q_ref, k_ref, v_ref, grad_ref, gain_ref, *refs):
    picks_ref, grad_norm_ref, gain_part_ref, place_ref, masks_ref, expo_ref, out_ref, stats_ref = refs
    tokens, width = grad_ref.shape[1:]
    heads = range(width // HEAD_DIM)
    score_scale = 1.0 / math.sqrt(HEAD_DIM)
    every = [head_cols(head) for head in heads]
    scores = [
        contract(k_ref[0, :, cols], q_ref[0, :, cols], 1, 1) * score_scale for cols in every
    ]
    top_scores = [jnp.max(block, axis=0, keepdims=True) for block in scores]
    expos = [jnp.exp(scores[head] - top_scores[head]) for head in heads]
    times = picks_ref[:, head_cols(len(heads))].astype(WIDE)
    for head in heads[OWNED:]:
        expos[head] = times * expos[head]
    expo_lows = [expo.astype(LOW) for expo in expos]
    outs = [contract(v_ref[0, :, cols], expo_lows[head], 0, 0) for head, cols in enumerate(every)]
    totals = [jnp.sum(expo, axis=0, keepdims=True) for expo in expos]
    for head in range(OWNED):
        outs[head] = outs[head] * (1.0 / totals[head])
    outs = [out.astype(LOW) for out in outs]
    for head, cols in enumerate(every):
        expo_ref[:, cols] = expo_lows[head]
        out_ref[:, cols] = outs[head]
        stats_ref[head : head + 1, :] = top_scores[head]
        stats_ref[TILE + head : TILE + head + 1, :] = totals[head]
    top_rows = tokens // top_step
    ones = jnp.ones((TILE, tokens), LOW)
    column = lax.broadcasted_iota(jnp.int32, (tokens, tokens), 1)
    gain_part_ref[...] = jnp.zeros(gain_part_ref.shape, WIDE)
    me = lax.axis_index("ctx")
    mid_rows = tokens // R1
    top_all, queries = SPAN * top_rows, SPAN * (top_rows + mid_rows)
    mid_offset, top_offset = [
        sum(
            jnp.where(me == head, offset_of(offsets_ref, level, head), 0) for head in range(OWNED)
        )
        for level in (0, 1)
    ]
    lane = lax.broadcasted_iota(jnp.int32, (1, queries), 1)
    is_top = jnp.where(lane < top_all, 1.0, 0.0)
    top_in_mid = jnp.where(((lane % top_rows) * top_step + top_offset) % R1 == mid_offset, 1.0, 0.0)
    both_flag = jnp.where(mid_offset % top_step == top_offset, 1.0, 0.0)
    sees_top = is_top + (1.0 - is_top) * both_flag
    sees_mid = is_top * top_in_mid + (1.0 - is_top)
    masks_ref[0:1, :queries] = (1.0 - sees_top) * NEVER
    masks_ref[1:2, :queries] = (1.0 - sees_mid) * NEVER
    masks_ref[2:3, :queries] = is_top + (1.0 - is_top) * (1.0 - both_flag)
    last = len(heads) - 1
    for row, (level, step) in enumerate(((1, top_step), (0, R1))):
        hits = hit_row(offset_of(offsets_ref, level, last), step, tokens)
        masks_ref[3 + row : 4 + row, :tokens] = (1.0 - hits) * NEVER
    grad_norms = [
        (grad_ref[0, :, head_cols(head)].astype(WIDE) * gain_ref[:, head_cols(head)]).T
        for head in heads
    ]
    for head in heads:
        cols = head_cols(head)
        grad_norm_ref[:, cols] = grad_norms[head]
        picks = pick_matrix(offsets_ref, head, tokens, top_step, 1)
        place_ref[:, cols] = picks
    for head in range(OWNED):
        cols = head_cols(head)
        mid_offset, top_offset = [offset_of(offsets_ref, level, head) for level in (0, 1)]
        seen = jnp.maximum(
            hit_row(top_offset, top_step, tokens), hit_row(mid_offset, R1, tokens)
        )
        masks_ref[TILE + head : TILE + head + 1, :tokens] = seen
        attn = outs[head].astype(WIDE)
        normed = attn * lax.rsqrt(column_mean(attn * attn) + EPS)
        product = grad_norms[head] * normed * (1.0 - seen)
        gain_part_ref[:, cols] = gain_row_of(ones, product) / gain_ref[:, cols]
        both = mid_offset % top_step == top_offset
        kept = jnp.where(column < top_rows, 1.0, jnp.where(both, 0.0, 1.0)).astype(LOW)
        picks = pick_matrix(offsets_ref, head, tokens, top_step, 1)
        place_ref[:, head_cols(len(heads) + head)] = picks * kept


def owner_kernel(top_step, q_ref, gain_ref, out_ref, grad_norm_ref, *refs):
    stats_ref, gain_base_ref, masks_ref = refs[:3]
    payload_refs, refs = nearest_first(refs[3 : 3 + SPAN]), refs[3 + SPAN :]
    normed_ref, grad_low_ref, score_grad_ref, kept_ref = refs[:4]
    return_refs = refs[4:]
    tokens = q_ref.shape[1]
    heads = q_ref.shape[2] // HEAD_DIM
    top_rows, mid_rows = picked_counts(tokens, top_step)
    picked = top_rows + mid_rows
    top_all, mid_all = SPAN * top_rows, SPAN * mid_rows
    queries = top_all + mid_all
    score_scale = 1.0 / math.sqrt(HEAD_DIM)
    me = lax.axis_index("ctx")
    ones = jnp.ones((TILE, tokens), LOW)

    def by_level(block):
        start = block * picked
        return jnp.concatenate(
            [ref[start : start + top_rows] for ref in payload_refs]
            + [ref[start + top_rows : start + picked] for ref in payload_refs],
            0,
        )

    def per_level(top_row, mid_row):
        return jnp.concatenate(
            [
                jnp.broadcast_to(top_row, (top_all, queries)),
                jnp.broadcast_to(mid_row, (mid_all, queries)),
            ],
            0,
        )

    q_rows, k_rows, v_rows, grad_rows, base_rows = [by_level(block) for block in range(5)]
    stat_start = 7 * picked
    logs = [
        joined_row(ref[stat_start : stat_start + STAT_TILES].astype(WIDE), 0)
        for ref in payload_refs
    ]
    base_top_log = sum(
        rolled(lane_window(log, 0, top_rows), slot * top_rows) for slot, log in enumerate(logs)
    )
    base_mid_log = sum(
        rolled(lane_window(log, top_rows, mid_rows), slot * mid_rows - top_rows)
        for slot, log in enumerate(logs)
    )
    base_log = jnp.concatenate([base_top_log, base_mid_log[:, :mid_all]], 1)
    gain_row = jnp.zeros((1, HEAD_DIM), WIDE)
    for head in range(OWNED):
        gain_row = gain_row + jnp.where(me == head, 1.0, 0.0) * gain_ref[:, head_cols(head)]
    lane = lax.broadcasted_iota(jnp.int32, (1, queries), 1)
    is_top = jnp.where(lane < top_all, 1.0, 0.0)
    bias = per_level(masks_ref[0:1, :queries], masks_ref[1:2, :queries])
    last = heads - 1
    cols = head_cols(last)
    peers = payload_refs[1:]
    q_last = q_ref[0, :, cols]
    k_peers = jnp.concatenate([ref[5 * picked : 6 * picked] for ref in peers], 0)
    v_peers = jnp.concatenate([ref[6 * picked : 7 * picked] for ref in peers], 0)
    last_biases = [
        jnp.broadcast_to(masks_ref[row : row + 1, :tokens], (count, tokens))
        for row, count in ((3, top_rows), (4, mid_rows))
    ]
    scores = contract(k_rows, q_rows, 1, 1) * score_scale + bias
    scores_last = contract(k_peers, q_last, 1, 1) * score_scale + jnp.concatenate(
        last_biases * PEERS, 0
    )
    base_attn = base_rows.astype(WIDE).T
    grad_norm = (grad_rows.astype(WIDE) * gain_row).T
    top_score = jnp.maximum(base_log, jnp.max(scores, axis=0, keepdims=True))
    base_top, base_total = stats_ref[last : last + 1, :], stats_ref[TILE + last : TILE + last + 1, :]
    top_last = jnp.maximum(base_top, jnp.max(scores_last, axis=0, keepdims=True))
    expo = jnp.exp(scores - top_score)
    expo_last = jnp.exp(scores_last - top_last)
    factor = jnp.exp(base_log - top_score)
    factor_last = jnp.exp(base_top - top_last)
    total = factor + jnp.sum(expo, axis=0, keepdims=True)
    total_last = factor_last * base_total + jnp.sum(expo_last, axis=0, keepdims=True)
    inv_total, inv_last = 1.0 / total, 1.0 / total_last
    expo_low, expo_last_low = expo.astype(LOW), expo_last.astype(LOW)
    attn = (factor * base_attn + contract(v_rows, expo_low, 0, 0)) * inv_total
    attn_last = (
        factor_last * out_ref[:, cols].astype(WIDE) + contract(v_peers, expo_last_low, 0, 0)
    ) * inv_last
    _, product, grad_attn, inner = norm_backward(attn, grad_norm)
    normed_last, product_last, grad_attn_last, inner_last = norm_backward(
        attn_last, grad_norm_ref[:, cols]
    )
    grad_low, inner = (grad_attn * inv_total).astype(LOW), inner * inv_total
    grad_last_low = (grad_attn_last * inv_last).astype(LOW)
    base_factor = factor_last * inv_last
    spans = (slice(0, top_all), slice(top_all, queries))
    prob_grads = [contract(v_rows[span], grad_low[:, span], 1, 0) for span in spans]
    prob_grad_last = contract(v_peers, grad_last_low, 1, 0)
    score_grads = [
        (expo[span, span] * (prob_grad - inner[:, span]) * score_scale).astype(LOW)
        for span, prob_grad in zip(spans, prob_grads)
    ]
    score_grad_last = (
        expo_last * (prob_grad_last - inner_last * inv_last) * score_scale
    ).astype(LOW)
    dks = [
        contract(score_grad, q_rows[span], 1, 0).astype(LOW)
        for span, score_grad in zip(spans, score_grads)
    ]
    dk_last = contract(score_grad_last, q_last, 1, 0).astype(LOW)
    dvs = [
        contract(expo_low[span, span], grad_low[:, span], 1, 1).astype(LOW) for span in spans
    ]
    dv_last = contract(expo_last_low, grad_last_low, 1, 1).astype(LOW)
    dqs = [
        contract(score_grad, k_rows[span], 0, 0).astype(LOW)
        for span, score_grad in zip(spans, score_grads)
    ]
    attn_rows = attn.T.astype(LOW)
    attn_parts = [attn_rows[span] for span in spans]
    log_total = top_score + jnp.log(total)
    padding = jnp.zeros((1, top_all - mid_all), WIDE)
    once = masks_ref[2:3, :queries]
    ones_all = jnp.ones((TILE, queries), LOW)
    own_gain = gain_row_of(ones_all, product * once) / gain_row
    gain_rows = [
        gain_base_ref[:, head_cols(head)] + jnp.where(me == head, 1.0, 0.0) * own_gain
        for head in range(OWNED)
    ]
    gain_rows.append(gain_row_of(ones, product_last) / gain_ref[:, cols])
    gain_high, gain_rest = [
        rows.astype(WIDE) for rows in gain_pieces(jnp.concatenate(gain_rows, 0))
    ]
    top_log, mid_log = log_total[:, :top_all], jnp.concatenate(
        [log_total[:, top_all:], padding], 1
    )
    empty = jnp.zeros((PIECES, HEAD_DIM), WIDE)
    for distance, return_ref in enumerate(return_refs):
        blocks = []
        for top_block, mid_block in (dqs, dks, dvs, attn_parts):
            blocks.append(top_block[distance * top_rows : (distance + 1) * top_rows])
            blocks.append(mid_block[distance * mid_rows : (distance + 1) * mid_rows])
        start = max(distance - 1, 0) * picked
        blocks += [dk_last[start : start + picked], dv_last[start : start + picked]]
        log_row = lane_window(rolled(top_log, -distance * top_rows), 0, top_rows) + lane_window(
            rolled(mid_log, top_rows - distance * mid_rows), top_rows, mid_rows
        )
        log_rows = [piece_rows(log_row, gain_high), empty, gain_rest]
        blocks.append(jnp.concatenate(log_rows, 0).astype(LOW))
        return_ref[...] = jnp.concatenate(blocks, 0)
    normed_ref[...] = normed_last
    grad_low_ref[...] = (grad_attn_last * base_factor).astype(LOW)
    score_grad_ref[...] = score_grad_last
    kept_ref[0:1, :] = inner_last * base_factor


def last_head_kernel(top_step, q_ref, k_ref, v_ref, gain_ref, expo_ref, *refs):
    normed_ref, grad_low_ref, peer_score_grad_ref, kept_ref, *peers = refs[: 4 + PEERS]
    peers = nearest_first([None, *peers])[1:]
    attended_ref, dq_ref, dk_ref, dv_ref = refs[4 + PEERS :]
    picked = sum(picked_counts(q_ref.shape[1], top_step))
    score_scale = 1.0 / math.sqrt(HEAD_DIM)
    cols = head_cols(q_ref.shape[2] // HEAD_DIM - 1)
    attended_ref[...] = (normed_ref[...].T * gain_ref[:, cols]).astype(LOW)
    k_peers = jnp.concatenate([ref[5 * picked : 6 * picked] for ref in peers], 0)
    grad_low = grad_low_ref[...]
    expo_low = expo_ref[:, cols]
    prob_grad = contract(v_ref[0, :, cols], grad_low, 1, 0)
    score_grad = (
        expo_low.astype(WIDE) * (prob_grad - kept_ref[0:1, :]) * score_scale
    ).astype(LOW)
    dk_ref[...] = contract(score_grad, q_ref[0, :, cols], 1, 0)
    dv_ref[...] = contract(expo_low, grad_low, 1, 1)
    dq_ref[...] = (
        contract(score_grad, k_ref[0, :, cols], 0, 0)
        + contract(peer_score_grad_ref[...], k_peers, 0, 0)
    ).astype(LOW)


def gain_kernel(picked, *refs):
    return_refs, gain_ref = nearest_first(refs[:SPAN]), refs[SPAN]
    tiles = [ref[6 * picked : 6 * picked + STAT_TILES].astype(WIDE) for ref in return_refs]
    parts = [tile[PIECES:TILE] + tile[TILE + PIECES :] for tile in tiles]
    total = (parts[0] + parts[1]) + (parts[2] + parts[3])
    for head in range(gain_ref.shape[1] // HEAD_DIM):
        gain_ref[:, head_cols(head)] = total[head : head + 1]


def mix_kernel(top_step, q_ref, k_ref, v_ref, gain_ref, expo_ref, out_ref, *refs):
    grad_norm_ref, stats_ref, place_ref, masks_ref = refs[:4]
    last_attended_ref, last_dq_ref, last_dk_ref, last_dv_ref = refs[4:8]
    return_refs, refs = nearest_first(refs[8 : 8 + SPAN]), refs[8 + SPAN :]
    attended_ref, dq_ref, dk_ref, dv_ref, placed_ref = refs
    tokens, width = v_ref.shape[1:]
    count = width // HEAD_DIM
    picked = sum(picked_counts(tokens, top_step))
    score_scale = 1.0 / math.sqrt(HEAD_DIM)
    me = lax.axis_index("ctx")
    heads = range(OWNED)
    every = [head_cols(head) for head in heads]
    for distance, return_ref in enumerate(return_refs):
        placed_ref[me ^ distance] = return_ref[...]
    once = [place_ref[:, head_cols(count + head)] for head in heads]
    attn_parts = [
        contract(placed_ref[head, 3 * picked : 4 * picked], once[head][:, :picked], 0, 1)
        for head in heads
    ]
    log_parts = [
        contract(placed_ref[head, 6 * picked : 6 * picked + STAT_TILES], once[head], 1, 1)
        for head in heads
    ]
    normeds, grad_lows, inners, inv_totals = [], [], [], []
    for head in heads:
        seen = masks_ref[TILE + head : TILE + head + 1, :tokens] > 0.5
        top_score, total = stats_ref[head : head + 1, :], stats_ref[TILE + head : TILE + head + 1, :]
        base_log = top_score + jnp.log(total)
        log_total = jnp.where(seen, joined_row(log_parts[head], 0), base_log)
        share = jnp.exp(base_log - log_total)
        inv_totals.append(1.0 / total)
        attn = jnp.where(seen, attn_parts[head], out_ref[:, every[head]].astype(WIDE))
        normed, _, grad_attn, inner = norm_backward(attn, grad_norm_ref[:, every[head]])
        normeds.append(normed)
        grad_lows.append((share * grad_attn).astype(LOW))
        inners.append(share * inner)
    prob_grads = [contract(v_ref[0, :, every[head]], grad_lows[head], 1, 0) for head in heads]
    softs = [expo_ref[:, every[head]].astype(WIDE) * inv_totals[head] for head in heads]
    soft_lows = [soft.astype(LOW) for soft in softs]
    score_grads = [
        (softs[head] * (prob_grads[head] - inners[head]) * score_scale).astype(LOW)
        for head in heads
    ]
    dqs = [contract(score_grads[head], k_ref[0, :, every[head]], 0, 0) for head in heads]
    placed = [
        contract(
            place_ref[:, pl.ds(head * HEAD_DIM, picked)],
            jnp.concatenate(
                [placed_ref[head, block * picked : (block + 1) * picked] for block in range(3)], 1
            ),
            1,
            0,
        )
        for head in heads
    ]
    dks = [contract(score_grads[head], q_ref[0, :, every[head]], 1, 0) for head in heads]
    dvs = [contract(soft_lows[head], grad_lows[head], 1, 1) for head in heads]
    last = count - 1
    total = sum(ref[4 * picked : 6 * picked].astype(WIDE) for ref in return_refs[1:]).astype(LOW)
    rows = contract(
        place_ref[:, pl.ds(last * HEAD_DIM, picked)],
        jnp.concatenate([total[:picked], total[picked:]], 1),
        1,
        0,
    )
    for head in heads:
        cols = every[head]
        attended_ref[:, cols] = (normeds[head].T * gain_ref[:, cols]).astype(LOW)
        for which, (block, out_block_ref) in enumerate(
            ((dqs[head], dq_ref), (dks[head], dk_ref), (dvs[head], dv_ref))
        ):
            part = placed[head][:, which * HEAD_DIM : (which + 1) * HEAD_DIM]
            out_block_ref[:, cols] = (block + part).astype(LOW)
    cols = head_cols(last)
    attended_ref[:, cols] = last_attended_ref[...]
    dq_ref[:, cols] = last_dq_ref[...]
    dk_ref[:, cols] = (last_dk_ref[...] + rows[:, :HEAD_DIM]).astype(LOW)
    dv_ref[:, cols] = (last_dv_ref[...] + rows[:, HEAD_DIM:]).astype(LOW)


def finish_kernel(gain_ref, gain_rest_ref, *refs):
    block_refs, result_refs, gain_out_ref = refs[:4], refs[4:8], refs[8]
    for block_ref, result_ref in zip(block_refs, result_refs):
        result_ref[0] = block_ref[...]
    gain_out_ref[...] = (gain_ref[...] + gain_rest_ref[...]).reshape(gain_out_ref.shape)


def across(block, axis, distance):
    route = [(place, place ^ distance) for place in range(lax.axis_size(axis))]
    return lax.ppermute(block, axis, route)


def to_peers(blocks):
    return [across(blocks[distance - 1], "ctx", distance) for distance in START_ORDER]


def call(kernel, name, operands, results, microseconds, vmem=PLAIN_VMEM, scratch=()):
    return pl.pallas_call(
        kernel,
        out_shape=results,
        in_specs=[VMEM_SPEC] * len(operands),
        out_specs=[VMEM_SPEC] * len(results),
        scratch_shapes=scratch,
        compiler_params=pltpu.CompilerParams(vmem_limit_bytes=vmem),
        cost_estimate=pl.CostEstimate(
            flops=int(microseconds * 10**9), bytes_accessed=0, transcendentals=0
        ),
        name=name,
    )(*operands)


def one_segment_shards(queries, keys, values, grad_y, out_gain, offsets):
    tokens, width = queries.shape[1:]
    heads = width // HEAD_DIM
    top_step = lax.axis_size("ctx")
    picked = sum(picked_counts(tokens, top_step))
    shape = jax.ShapeDtypeStruct
    row_block = shape((1, tokens, width), LOW)
    low_block, wide_block = shape((tokens, width), LOW), shape((tokens, width), WIDE)
    low_head, wide_head = shape((tokens, HEAD_DIM), LOW), shape((tokens, HEAD_DIM), WIDE)
    gain_block = shape((1, width), WIDE)
    stats_block = shape((2 * TILE, tokens), WIDE)
    payload = shape((7 * picked + STAT_TILES, HEAD_DIM), LOW)
    answer = shape((6 * picked + STAT_TILES, HEAD_DIM), LOW)
    bind = functools.partial
    gain_row = out_gain.reshape(1, width)
    (picks,) = call(
        bind(picks_kernel, top_step), "picks", (offsets,), [shape((tokens, width + tokens), LOW)], 20
    )
    own, *sent = call(
        bind(pack_kernel, top_step),
        "pack",
        (picks, queries, keys, values, grad_y),
        [payload] * SPAN,
        1,
        scratch=[pltpu.VMEM((OWNED, *payload.shape), LOW)],
    )
    received = to_peers(sent)
    grad_norm, gain_base, place, masks, expo, base_out, stats = call(
        bind(prepare_kernel, top_step),
        "prepare",
        (offsets, queries, keys, values, grad_y, gain_row, picks),
        [
            wide_block,
            gain_block,
            shape((tokens, 2 * width), LOW),
            shape((2 * TILE, 2 * tokens), WIDE),
            low_block,
            low_block,
            stats_block,
        ],
        2,
    )
    normed, grad_low, score_grad, kept, own_answer, *answers = call(
        bind(owner_kernel, top_step),
        "owner",
        (queries, gain_row, base_out, grad_norm, stats, gain_base, masks, own, *received),
        [
            wide_head,
            low_head,
            shape((PEERS * picked, HEAD_DIM), LOW),
            shape((TILE, tokens), WIDE),
        ]
        + [answer] * SPAN,
        3,
    )
    returned = to_peers(answers)
    last_results = call(
        bind(last_head_kernel, top_step),
        "last_head",
        (queries, keys, values, gain_row, expo, normed, grad_low, score_grad, kept, *received),
        [low_head, low_head, wide_head, wide_head],
        20,
    )
    (gain_sum,) = call(bind(gain_kernel, picked), "gain", (own_answer, *returned), [gain_block], 1)
    gain_rest = across(gain_sum, "dp", 1)
    mixed = call(
        bind(mix_kernel, top_step),
        "mix",
        (
            queries,
            keys,
            values,
            gain_row,
            expo,
            base_out,
            grad_norm,
            stats,
            place,
            masks,
            *last_results,
            own_answer,
            *returned,
        ),
        [low_block] * 4,
        20,
        scratch=[pltpu.VMEM((OWNED, *answer.shape), LOW)],
    )
    attended, query_grad, key_grad, value_grad, gain_grad = call(
        finish_kernel,
        "finish",
        (gain_sum, gain_rest, *mixed),
        [row_block] * 4 + [shape((width,), WIDE)],
        1,
    )
    return attended, query_grad, key_grad, value_grad, gain_grad


def shards(*operands):
    one_segment = lax.axis_size("ctx") == SPAN
    if one_segment and operands[0].shape[2] == (OWNED + 1) * HEAD_DIM:
        return one_segment_shards(*operands)
    return general_shards(*operands)


def solution(mesh):
    in_specs = (
        P("dp", "ctx", "head"),
        P("dp", "ctx", "head"),
        P("dp", "ctx", "head"),
        P("dp", "ctx", "head"),
        P("head"),
        P(None, "head"),
    )
    out_specs = (
        P("dp", "ctx", "head"),
        P("dp", "ctx", "head"),
        P("dp", "ctx", "head"),
        P("dp", "ctx", "head"),
        P("head"),
    )
    return jax.shard_map(shards, mesh=mesh, in_specs=in_specs, out_specs=out_specs, check_vma=False)
```

```python
import functools
import math

import jax
import jax.numpy as jnp
from jax import lax
from jax.experimental import pallas as pl
from jax.experimental.pallas import tpu as pltpu
from jax.sharding import PartitionSpec as P

HEAD_DIM = 128
SPAN = 4
R1 = 8


EPS = 1e-06


def swapped(block, axis, bit):
    count = lax.axis_size(axis)
    route = []
    for low in range(count):
        high = low | 1 << bit
        if high != low and high < count:
            route += [(low, high), (high, low)]
    return lax.ppermute(block, axis, route)


def pick_rows(source_rows, dilation, shifts):
    row_count, head_count, head_width = source_rows.shape
    grouped = source_rows.reshape(row_count // dilation, dilation, head_count, head_width)
    hit_mask = jnp.arange(dilation, dtype=jnp.int32).reshape(1, dilation, 1, 1) == shifts.reshape(
        1, 1, head_count, 1
    )
    chosen = jnp.where(hit_mask, grouped, jnp.zeros((), source_rows.dtype))
    return jnp.sum(chosen, axis=1, dtype=source_rows.dtype)


def place_rows(row_values, dilation, shifts):
    row_count, head_count, head_width = row_values.shape
    hit_mask = jnp.arange(dilation, dtype=jnp.int32).reshape(1, dilation, 1, 1) == shifts.reshape(
        1, 1, head_count, 1
    )
    spread = jnp.where(hit_mask, row_values[:, None], jnp.zeros((), row_values.dtype))
    return spread.reshape(row_count * dilation, head_count, head_width)


def level_scores(q_rows, k_rows):
    score_scale = 1.0 / math.sqrt(q_rows.shape[-1])
    return (
        jnp.einsum("qhe,khe->hqk", q_rows, k_rows, preferred_element_type=jnp.float32) * score_scale
    )


def attend(q_rows, k_rows, v_rows):
    scores = level_scores(q_rows, k_rows)
    row_max = jnp.max(scores, axis=-1, keepdims=True)
    log_total = row_max[..., 0] + jnp.log(jnp.sum(jnp.exp(scores - row_max), axis=-1))
    soft_rows = jnp.exp(scores - log_total[..., None]).astype(jnp.bfloat16)
    level_out = jnp.einsum("hqk,khe->qhe", soft_rows, v_rows, preferred_element_type=jnp.float32)
    return (level_out, log_total.T)


def score_grads(q_rows, k_rows, v_rows, log_total, grad_low, row_shift):
    score_scale = 1.0 / math.sqrt(q_rows.shape[-1])
    scores = level_scores(q_rows, k_rows)
    exact_soft = jnp.exp(scores - log_total.T[..., None])
    prob_grad = jnp.einsum("qhe,khe->hqk", grad_low, v_rows, preferred_element_type=jnp.float32)
    score_grad = (exact_soft * (prob_grad + row_shift.T[..., None]) * score_scale).astype(
        jnp.bfloat16
    )
    return (score_grad, exact_soft.astype(jnp.bfloat16))


def key_parts(score_grad, soft_low, q_rows, grad_low):
    k_part = jnp.einsum("hqk,qhe->khe", score_grad, q_rows, preferred_element_type=jnp.float32)
    v_part = jnp.einsum("hqk,qhe->khe", soft_low, grad_low, preferred_element_type=jnp.float32)
    return (k_part, v_part)


def query_part(score_grad, k_rows):
    return jnp.einsum("hqk,khe->qhe", score_grad, k_rows, preferred_element_type=jnp.float32)


def general_shards(queries, keys, values, grad_y, out_gain, offsets):
    tokens = queries.shape[1]
    flat_width = queries.shape[2]
    head_count = flat_width // HEAD_DIM
    row_shape = (tokens, head_count, HEAD_DIM)
    q_own = queries[0].reshape(row_shape)
    k_own = keys[0].reshape(row_shape)
    v_own = values[0].reshape(row_shape)
    ctx_size = lax.axis_size("ctx")
    span_bits = SPAN.bit_length() - 1
    my_place = lax.axis_index("ctx")
    mid_shift = offsets[0]
    top_shift = offsets[1]
    positions = jnp.arange(tokens, dtype=jnp.int32)
    mid_hit = (positions % R1)[:, None] == mid_shift[None, :]
    top_hit = (positions % ctx_size)[:, None] == top_shift[None, :]
    mid_q = pick_rows(q_own, R1, mid_shift)
    mid_k = pick_rows(k_own, R1, mid_shift)
    mid_v = pick_rows(v_own, R1, mid_shift)
    top_q = pick_rows(q_own, ctx_size, top_shift)
    top_k = pick_rows(k_own, ctx_size, top_shift)
    top_v = pick_rows(v_own, ctx_size, top_shift)
    mid_keys = mid_k.reshape(-1, flat_width)
    mid_vals = mid_v.reshape(-1, flat_width)
    top_keys = top_k.reshape(-1, flat_width)
    top_vals = top_v.reshape(-1, flat_width)

    def append_peer(mine, received, level_bit):
        upper_side = my_place >> level_bit & 1 == 1
        return jnp.where(
            upper_side, jnp.concatenate([received, mine], 0), jnp.concatenate([mine, received], 0)
        )

    for level_bit in range(span_bits):
        received = swapped((mid_keys, mid_vals), "ctx", level_bit)
        mid_keys = append_peer(mid_keys, received[0], level_bit)
        mid_vals = append_peer(mid_vals, received[1], level_bit)
    top_keys, top_vals = (
        lax.all_gather(top_keys, "ctx", axis=0, tiled=True),
        lax.all_gather(top_vals, "ctx", axis=0, tiled=True),
    )
    mid_keys = mid_keys.reshape(-1, head_count, HEAD_DIM)
    mid_vals = mid_vals.reshape(-1, head_count, HEAD_DIM)
    top_keys = top_keys.reshape(-1, head_count, HEAD_DIM)
    top_vals = top_vals.reshape(-1, head_count, HEAD_DIM)
    base_out, base_total = attend(q_own, k_own, v_own)
    mid_out, mid_total = attend(mid_q, mid_keys, mid_vals)
    top_out, top_total = attend(top_q, top_keys, top_vals)
    mid_full = place_rows(mid_total[..., None], R1, mid_shift)[..., 0]
    top_full = place_rows(top_total[..., None], ctx_size, top_shift)[..., 0]
    row_max = jnp.maximum(base_total, jnp.where(mid_hit, mid_full, base_total))
    row_max = jnp.maximum(row_max, jnp.where(top_hit, top_full, base_total))
    base_expo = jnp.exp(base_total - row_max)
    mid_expo = jnp.where(mid_hit, jnp.exp(mid_full - row_max), 0.0)
    top_expo = jnp.where(top_hit, jnp.exp(top_full - row_max), 0.0)
    denom = base_expo + mid_expo + top_expo
    base_share = base_expo / denom
    mid_share = mid_expo / denom
    top_share = top_expo / denom
    attn = (
        base_share[..., None] * base_out
        + mid_share[..., None] * place_rows(mid_out, R1, mid_shift)
        + top_share[..., None] * place_rows(top_out, ctx_size, top_shift)
    )
    inv_rms = lax.rsqrt(jnp.mean(attn * attn, axis=-1, keepdims=True) + EPS)
    normed = attn * inv_rms
    gain_rows = out_gain.reshape(head_count, HEAD_DIM)
    attended = (normed * gain_rows).astype(jnp.bfloat16).reshape(1, tokens, flat_width)
    grad_full = grad_y[0].reshape(row_shape).astype(jnp.float32)
    gain_part = jnp.sum(grad_full * normed, axis=0).reshape(flat_width)
    gain_grad = lax.psum(gain_part, ("dp", "ctx"))
    grad_norm = grad_full * gain_rows
    grad_attn = inv_rms * (
        grad_norm - normed * jnp.mean(grad_norm * normed, axis=-1, keepdims=True)
    )
    inner = jnp.sum(grad_attn * attn, axis=-1)
    base_low = (base_share[..., None] * grad_attn).astype(jnp.bfloat16)
    base_shift = -(base_share * inner)
    base_grad, base_soft = score_grads(q_own, k_own, v_own, base_total, base_low, base_shift)
    base_dq = query_part(base_grad, k_own)
    base_dk, base_dv = key_parts(base_grad, base_soft, q_own, base_low)
    mid_sel = pick_rows(mid_share[..., None], R1, mid_shift)[..., 0]
    mid_low = (mid_sel[..., None] * pick_rows(grad_attn, R1, mid_shift)).astype(jnp.bfloat16)
    mid_row_shift = -(mid_sel * pick_rows(inner[..., None], R1, mid_shift)[..., 0])
    mid_grad, mid_soft = score_grads(mid_q, mid_keys, mid_vals, mid_total, mid_low, mid_row_shift)
    mid_dq = query_part(mid_grad, mid_keys)
    mid_dk, mid_dv = key_parts(mid_grad, mid_soft, mid_q, mid_low)
    mid_dk = mid_dk.reshape(-1, flat_width)
    mid_dv = mid_dv.reshape(-1, flat_width)
    for level_bit in reversed(range(span_bits)):
        half_rows = mid_dk.shape[0] // 2
        upper_side = my_place >> level_bit & 1 == 1
        keep_k = jnp.where(upper_side, mid_dk[half_rows:], mid_dk[:half_rows])
        keep_v = jnp.where(upper_side, mid_dv[half_rows:], mid_dv[:half_rows])
        send_k = jnp.where(upper_side, mid_dk[:half_rows], mid_dk[half_rows:])
        send_v = jnp.where(upper_side, mid_dv[:half_rows], mid_dv[half_rows:])
        received = (
            swapped(send_k.astype(jnp.bfloat16), "ctx", level_bit).astype(send_k.dtype),
            swapped(send_v.astype(jnp.bfloat16), "ctx", level_bit).astype(send_v.dtype),
        )
        mid_dk = keep_k + received[0]
        mid_dv = keep_v + received[1]
    mid_dk = mid_dk.reshape(-1, head_count, HEAD_DIM)
    mid_dv = mid_dv.reshape(-1, head_count, HEAD_DIM)
    top_sel = pick_rows(top_share[..., None], ctx_size, top_shift)[..., 0]
    top_low = (top_sel[..., None] * pick_rows(grad_attn, ctx_size, top_shift)).astype(jnp.bfloat16)
    top_row_shift = -(top_sel * pick_rows(inner[..., None], ctx_size, top_shift)[..., 0])
    top_grad, top_soft = score_grads(top_q, top_keys, top_vals, top_total, top_low, top_row_shift)
    top_dq = query_part(top_grad, top_keys)
    gathered_dk, gathered_dv = key_parts(top_grad, top_soft, top_q, top_low)
    summed = (
        lax.psum_scatter(
            gathered_dk.reshape(-1, flat_width), "ctx", scatter_dimension=0, tiled=True
        ),
        lax.psum_scatter(
            gathered_dv.reshape(-1, flat_width), "ctx", scatter_dimension=0, tiled=True
        ),
    )
    top_dk = summed[0].reshape(-1, head_count, HEAD_DIM)
    top_dv = summed[1].reshape(-1, head_count, HEAD_DIM)
    query_grad = (
        base_dq + place_rows(mid_dq, R1, mid_shift) + place_rows(top_dq, ctx_size, top_shift)
    )
    key_grad = base_dk + place_rows(mid_dk, R1, mid_shift) + place_rows(top_dk, ctx_size, top_shift)
    value_grad = (
        base_dv + place_rows(mid_dv, R1, mid_shift) + place_rows(top_dv, ctx_size, top_shift)
    )
    out_shape = (1, tokens, flat_width)
    return (
        attended,
        query_grad.astype(jnp.bfloat16).reshape(out_shape),
        key_grad.astype(jnp.bfloat16).reshape(out_shape),
        value_grad.astype(jnp.bfloat16).reshape(out_shape),
        gain_grad,
    )


VMEM_SPEC = pl.BlockSpec(memory_space=pltpu.VMEM)
PEERS = SPAN - 1
OWNED = SPAN
TILE = 8
STAT_TILES = 2 * TILE
PIECES = 3
NEVER = -1e30
START_ORDER = (3, 1, 2)
LOW = jnp.bfloat16
WIDE = jnp.float32
PLAIN_VMEM = 16 * 1024 * 1024


def contract(left, right, left_dim, right_dim):
    return lax.dot_general(
        left, right, (((left_dim,), (right_dim,)), ((), ())), preferred_element_type=WIDE
    )


def head_cols(head):
    return pl.ds(head * HEAD_DIM, HEAD_DIM)


def picked_counts(tokens, top_step):
    return tokens // top_step, tokens // R1


def offset_of(offsets_ref, level, head):
    return offsets_ref[level : level + 1, head : head + 1]


def pick_matrix(offsets_ref, head, tokens, top_step, picked_axis):
    top_rows, _ = picked_counts(tokens, top_step)
    row = lax.broadcasted_iota(jnp.int32, (tokens, tokens), picked_axis)
    position = lax.broadcasted_iota(jnp.int32, (tokens, tokens), 1 - picked_axis)
    wanted = jnp.where(
        row < top_rows,
        row * top_step + offset_of(offsets_ref, 1, head),
        (row - top_rows) * R1 + offset_of(offsets_ref, 0, head),
    )
    return jnp.where(position == wanted, 1.0, 0.0).astype(LOW)


def rolled(row, shift):
    return pltpu.roll(row, shift % row.shape[1], 1)


def lane_window(row, start, count):
    lane = lax.broadcasted_iota(jnp.int32, row.shape, 1)
    return jnp.where((lane >= start) & (lane < start + count), row, 0.0)


def hit_row(offset, step, tokens):
    position = lax.broadcasted_iota(jnp.int32, (1, tokens), 1)
    return jnp.where(position % step == offset, 1.0, 0.0)


def piece_rows(row, others=None):
    pieces = []
    for _ in range(PIECES):
        piece = row.astype(LOW).astype(WIDE)
        pieces.append(piece)
        row = row - piece
    if others is None:
        others = jnp.zeros((TILE - PIECES, row.shape[1]), WIDE)
    return jnp.concatenate(pieces + [others], 0)


def gain_pieces(rows):
    high = rows.astype(LOW)
    return high, (rows - high.astype(WIDE)).astype(LOW)


def joined_row(rows, first):
    total = rows[first : first + 1]
    for piece in range(1, PIECES):
        total = total + rows[first + piece : first + piece + 1]
    return total


def gain_row_of(ones, product):
    high, rest = gain_pieces(product)
    return (contract(ones, high, 1, 1) + contract(ones, rest, 1, 1))[:1]


def column_mean(block):
    return jnp.mean(block, axis=0, keepdims=True)


def norm_backward(attn, grad_norm):
    inv_rms = lax.rsqrt(column_mean(attn * attn) + EPS)
    normed = attn * inv_rms
    product = grad_norm * normed
    grad_attn = inv_rms * (grad_norm - normed * column_mean(product))
    inner = jnp.sum(grad_attn * attn, axis=0, keepdims=True)
    return normed, product, grad_attn, inner


def nearest_first(refs):
    by_distance = dict(zip(START_ORDER, refs[1:]))
    return [refs[0], *[by_distance[distance] for distance in range(1, SPAN)]]


def picks_kernel(top_step, offsets_ref, picks_ref):
    tokens = picks_ref.shape[0]
    last = offsets_ref.shape[1] - 1
    for head in range(last + 1):
        picks_ref[:, head_cols(head)] = pick_matrix(offsets_ref, head, tokens, top_step, 0)
    key_row = lax.broadcasted_iota(jnp.int32, (tokens, 1), 0)
    times = 1.0
    for level, step in ((0, R1), (1, top_step)):
        offset = offset_of(offsets_ref, level, last)
        hit_column = jnp.where(key_row % step == offset, 1.0, 0.0)
        times = times + hit_column * hit_row(offset, step, tokens)
    picks_ref[:, head_cols(last + 1)] = times.astype(LOW)


def pack_kernel(top_step, picks_ref, q_ref, k_ref, v_ref, grad_ref, *payload_refs):
    tokens, width = q_ref.shape[1:]
    me = lax.axis_index("ctx")
    picked = sum(picked_counts(tokens, top_step))
    score_scale = 1.0 / math.sqrt(HEAD_DIM)
    places = range(SPAN)
    sent_cols = [
        pl.ds(pl.multiple_of((me ^ distance) * HEAD_DIM, HEAD_DIM), HEAD_DIM) for distance in places
    ]
    last_cols = head_cols(width // HEAD_DIM - 1)
    q_rows, k_rows, v_rows, grad_rows = [
        [ref[0, :, cols] for cols in sent_cols] for ref in (q_ref, k_ref, v_ref, grad_ref)
    ]
    picks = [picks_ref[:, cols] for cols in sent_cols]
    scores = [contract(k_rows[i], q_rows[i], 1, 1) * score_scale for i in places]
    moved = [
        contract(
            picks[i][:picked],
            jnp.concatenate([q_rows[i], k_rows[i], v_rows[i], grad_rows[i]], 1),
            1,
            0,
        ).astype(LOW)
        for i in places
    ]
    shared = contract(
        picks_ref[:picked, last_cols],
        jnp.concatenate([k_ref[0, :, last_cols], v_ref[0, :, last_cols]], 1),
        1,
        0,
    ).astype(LOW)
    top_scores = [jnp.max(block, axis=0, keepdims=True) for block in scores]
    expos = [jnp.exp(scores[i] - top_scores[i]) for i in places]
    expo_lows = [expo.astype(LOW) for expo in expos]
    outs = [contract(v_rows[i], expo_lows[i], 0, 0) for i in places]
    totals = [jnp.sum(expo, axis=0, keepdims=True) for expo in expos]
    outs = [(outs[i] * (1.0 / totals[i])).astype(LOW) for i in places]
    picked_outs = [contract(picks[i][:picked], outs[i], 1, 1).astype(LOW) for i in places]
    pieces = [piece_rows(top_scores[i] + jnp.log(totals[i])).astype(LOW) for i in places]
    stat_rows = [contract(pieces[i], picks[i], 1, 1) for i in places]
    for i, payload_ref in enumerate(payload_refs):
        for block in range(4):
            payload_ref[block * picked : (block + 1) * picked] = moved[i][
                :, block * HEAD_DIM : (block + 1) * HEAD_DIM
            ]
        payload_ref[4 * picked : 5 * picked] = picked_outs[i]
        payload_ref[5 * picked : 6 * picked] = shared[:, :HEAD_DIM]
        payload_ref[6 * picked : 7 * picked] = shared[:, HEAD_DIM:]
        payload_ref[7 * picked :] = jnp.concatenate(
            [stat_rows[i], jnp.zeros_like(stat_rows[i])], 0
        ).astype(LOW)


def prepare_kernel(top_step, offsets_ref, q_ref, k_ref, v_ref, grad_ref, gain_ref, *refs):
    picks_ref, grad_norm_ref, gain_part_ref, place_ref, masks_ref, expo_ref, out_ref, stats_ref = refs
    tokens, width = grad_ref.shape[1:]
    heads = range(width // HEAD_DIM)
    score_scale = 1.0 / math.sqrt(HEAD_DIM)
    every = [head_cols(head) for head in heads]
    scores = [
        contract(k_ref[0, :, cols], q_ref[0, :, cols], 1, 1) * score_scale for cols in every
    ]
    top_scores = [jnp.max(block, axis=0, keepdims=True) for block in scores]
    expos = [jnp.exp(scores[head] - top_scores[head]) for head in heads]
    times = picks_ref[:, head_cols(len(heads))].astype(WIDE)
    for head in heads[OWNED:]:
        expos[head] = times * expos[head]
    expo_lows = [expo.astype(LOW) for expo in expos]
    outs = [contract(v_ref[0, :, cols], expo_lows[head], 0, 0) for head, cols in enumerate(every)]
    totals = [jnp.sum(expo, axis=0, keepdims=True) for expo in expos]
    for head in range(OWNED):
        outs[head] = outs[head] * (1.0 / totals[head])
    outs = [out.astype(LOW) for out in outs]
    for head, cols in enumerate(every):
        expo_ref[:, cols] = expo_lows[head]
        out_ref[:, cols] = outs[head]
        stats_ref[head : head + 1, :] = top_scores[head]
        stats_ref[TILE + head : TILE + head + 1, :] = totals[head]
    top_rows = tokens // top_step
    ones = jnp.ones((TILE, tokens), LOW)
    column = lax.broadcasted_iota(jnp.int32, (tokens, tokens), 1)
    gain_part_ref[...] = jnp.zeros(gain_part_ref.shape, WIDE)
    me = lax.axis_index("ctx")
    mid_rows = tokens // R1
    top_all, queries = SPAN * top_rows, SPAN * (top_rows + mid_rows)
    mid_offset, top_offset = [
        sum(
            jnp.where(me == head, offset_of(offsets_ref, level, head), 0) for head in range(OWNED)
        )
        for level in (0, 1)
    ]
    lane = lax.broadcasted_iota(jnp.int32, (1, queries), 1)
    is_top = jnp.where(lane < top_all, 1.0, 0.0)
    top_in_mid = jnp.where(((lane % top_rows) * top_step + top_offset) % R1 == mid_offset, 1.0, 0.0)
    both_flag = jnp.where(mid_offset % top_step == top_offset, 1.0, 0.0)
    sees_top = is_top + (1.0 - is_top) * both_flag
    sees_mid = is_top * top_in_mid + (1.0 - is_top)
    masks_ref[0:1, :queries] = (1.0 - sees_top) * NEVER
    masks_ref[1:2, :queries] = (1.0 - sees_mid) * NEVER
    masks_ref[2:3, :queries] = is_top + (1.0 - is_top) * (1.0 - both_flag)
    last = len(heads) - 1
    for row, (level, step) in enumerate(((1, top_step), (0, R1))):
        hits = hit_row(offset_of(offsets_ref, level, last), step, tokens)
        masks_ref[3 + row : 4 + row, :tokens] = (1.0 - hits) * NEVER
    grad_norms = [
        (grad_ref[0, :, head_cols(head)].astype(WIDE) * gain_ref[:, head_cols(head)]).T
        for head in heads
    ]
    for head in heads:
        cols = head_cols(head)
        grad_norm_ref[:, cols] = grad_norms[head]
        picks = pick_matrix(offsets_ref, head, tokens, top_step, 1)
        place_ref[:, cols] = picks
    for head in range(OWNED):
        cols = head_cols(head)
        mid_offset, top_offset = [offset_of(offsets_ref, level, head) for level in (0, 1)]
        seen = jnp.maximum(
            hit_row(top_offset, top_step, tokens), hit_row(mid_offset, R1, tokens)
        )
        masks_ref[TILE + head : TILE + head + 1, :tokens] = seen
        attn = outs[head].astype(WIDE)
        normed = attn * lax.rsqrt(column_mean(attn * attn) + EPS)
        product = grad_norms[head] * normed * (1.0 - seen)
        gain_part_ref[:, cols] = gain_row_of(ones, product) / gain_ref[:, cols]
        both = mid_offset % top_step == top_offset
        kept = jnp.where(column < top_rows, 1.0, jnp.where(both, 0.0, 1.0)).astype(LOW)
        picks = pick_matrix(offsets_ref, head, tokens, top_step, 1)
        place_ref[:, head_cols(len(heads) + head)] = picks * kept


def owner_kernel(top_step, q_ref, gain_ref, out_ref, grad_norm_ref, *refs):
    stats_ref, gain_base_ref, masks_ref = refs[:3]
    payload_refs, refs = nearest_first(refs[3 : 3 + SPAN]), refs[3 + SPAN :]
    normed_ref, grad_low_ref, score_grad_ref, kept_ref = refs[:4]
    return_refs = refs[4:]
    tokens = q_ref.shape[1]
    heads = q_ref.shape[2] // HEAD_DIM
    top_rows, mid_rows = picked_counts(tokens, top_step)
    picked = top_rows + mid_rows
    top_all, mid_all = SPAN * top_rows, SPAN * mid_rows
    queries = top_all + mid_all
    score_scale = 1.0 / math.sqrt(HEAD_DIM)
    me = lax.axis_index("ctx")
    ones = jnp.ones((TILE, tokens), LOW)

    def by_level(block):
        start = block * picked
        return jnp.concatenate(
            [ref[start : start + top_rows] for ref in payload_refs]
            + [ref[start + top_rows : start + picked] for ref in payload_refs],
            0,
        )

    def per_level(top_row, mid_row):
        return jnp.concatenate(
            [
                jnp.broadcast_to(top_row, (top_all, queries)),
                jnp.broadcast_to(mid_row, (mid_all, queries)),
            ],
            0,
        )

    q_rows, k_rows, v_rows, grad_rows, base_rows = [by_level(block) for block in range(5)]
    stat_start = 7 * picked
    logs = [
        joined_row(ref[stat_start : stat_start + STAT_TILES].astype(WIDE), 0)
        for ref in payload_refs
    ]
    base_top_log = sum(
        rolled(lane_window(log, 0, top_rows), slot * top_rows) for slot, log in enumerate(logs)
    )
    base_mid_log = sum(
        rolled(lane_window(log, top_rows, mid_rows), slot * mid_rows - top_rows)
        for slot, log in enumerate(logs)
    )
    base_log = jnp.concatenate([base_top_log, base_mid_log[:, :mid_all]], 1)
    gain_row = jnp.zeros((1, HEAD_DIM), WIDE)
    for head in range(OWNED):
        gain_row = gain_row + jnp.where(me == head, 1.0, 0.0) * gain_ref[:, head_cols(head)]
    lane = lax.broadcasted_iota(jnp.int32, (1, queries), 1)
    is_top = jnp.where(lane < top_all, 1.0, 0.0)
    bias = per_level(masks_ref[0:1, :queries], masks_ref[1:2, :queries])
    last = heads - 1
    cols = head_cols(last)
    peers = payload_refs[1:]
    q_last = q_ref[0, :, cols]
    k_peers = jnp.concatenate([ref[5 * picked : 6 * picked] for ref in peers], 0)
    v_peers = jnp.concatenate([ref[6 * picked : 7 * picked] for ref in peers], 0)
    last_biases = [
        jnp.broadcast_to(masks_ref[row : row + 1, :tokens], (count, tokens))
        for row, count in ((3, top_rows), (4, mid_rows))
    ]
    scores = contract(k_rows, q_rows, 1, 1) * score_scale + bias
    scores_last = contract(k_peers, q_last, 1, 1) * score_scale + jnp.concatenate(
        last_biases * PEERS, 0
    )
    base_attn = base_rows.astype(WIDE).T
    grad_norm = (grad_rows.astype(WIDE) * gain_row).T
    top_score = jnp.maximum(base_log, jnp.max(scores, axis=0, keepdims=True))
    base_top, base_total = stats_ref[last : last + 1, :], stats_ref[TILE + last : TILE + last + 1, :]
    top_last = jnp.maximum(base_top, jnp.max(scores_last, axis=0, keepdims=True))
    expo = jnp.exp(scores - top_score)
    expo_last = jnp.exp(scores_last - top_last)
    factor = jnp.exp(base_log - top_score)
    factor_last = jnp.exp(base_top - top_last)
    total = factor + jnp.sum(expo, axis=0, keepdims=True)
    total_last = factor_last * base_total + jnp.sum(expo_last, axis=0, keepdims=True)
    inv_total, inv_last = 1.0 / total, 1.0 / total_last
    expo_low, expo_last_low = expo.astype(LOW), expo_last.astype(LOW)
    attn = (factor * base_attn + contract(v_rows, expo_low, 0, 0)) * inv_total
    attn_last = (
        factor_last * out_ref[:, cols].astype(WIDE) + contract(v_peers, expo_last_low, 0, 0)
    ) * inv_last
    _, product, grad_attn, inner = norm_backward(attn, grad_norm)
    normed_last, product_last, grad_attn_last, inner_last = norm_backward(
        attn_last, grad_norm_ref[:, cols]
    )
    grad_low, inner = (grad_attn * inv_total).astype(LOW), inner * inv_total
    grad_last_low = (grad_attn_last * inv_last).astype(LOW)
    base_factor = factor_last * inv_last
    spans = (slice(0, top_all), slice(top_all, queries))
    prob_grads = [contract(v_rows[span], grad_low[:, span], 1, 0) for span in spans]
    prob_grad_last = contract(v_peers, grad_last_low, 1, 0)
    score_grads = [
        (expo[span, span] * (prob_grad - inner[:, span]) * score_scale).astype(LOW)
        for span, prob_grad in zip(spans, prob_grads)
    ]
    score_grad_last = (
        expo_last * (prob_grad_last - inner_last * inv_last) * score_scale
    ).astype(LOW)
    dks = [
        contract(score_grad, q_rows[span], 1, 0).astype(LOW)
        for span, score_grad in zip(spans, score_grads)
    ]
    dk_last = contract(score_grad_last, q_last, 1, 0).astype(LOW)
    dvs = [
        contract(expo_low[span, span], grad_low[:, span], 1, 1).astype(LOW) for span in spans
    ]
    dv_last = contract(expo_last_low, grad_last_low, 1, 1).astype(LOW)
    dqs = [
        contract(score_grad, k_rows[span], 0, 0).astype(LOW)
        for span, score_grad in zip(spans, score_grads)
    ]
    attn_rows = attn.T.astype(LOW)
    attn_parts = [attn_rows[span] for span in spans]
    log_total = top_score + jnp.log(total)
    padding = jnp.zeros((1, top_all - mid_all), WIDE)
    once = masks_ref[2:3, :queries]
    ones_all = jnp.ones((TILE, queries), LOW)
    own_gain = gain_row_of(ones_all, product * once) / gain_row
    gain_rows = [
        gain_base_ref[:, head_cols(head)] + jnp.where(me == head, 1.0, 0.0) * own_gain
        for head in range(OWNED)
    ]
    gain_rows.append(gain_row_of(ones, product_last) / gain_ref[:, cols])
    gain_high, gain_rest = [
        rows.astype(WIDE) for rows in gain_pieces(jnp.concatenate(gain_rows, 0))
    ]
    top_log, mid_log = log_total[:, :top_all], jnp.concatenate(
        [log_total[:, top_all:], padding], 1
    )
    empty = jnp.zeros((PIECES, HEAD_DIM), WIDE)
    for distance, return_ref in enumerate(return_refs):
        blocks = []
        for top_block, mid_block in (dqs, dks, dvs, attn_parts):
            blocks.append(top_block[distance * top_rows : (distance + 1) * top_rows])
            blocks.append(mid_block[distance * mid_rows : (distance + 1) * mid_rows])
        start = max(distance - 1, 0) * picked
        blocks += [dk_last[start : start + picked], dv_last[start : start + picked]]
        log_row = lane_window(rolled(top_log, -distance * top_rows), 0, top_rows) + lane_window(
            rolled(mid_log, top_rows - distance * mid_rows), top_rows, mid_rows
        )
        log_rows = [piece_rows(log_row, gain_high), empty, gain_rest]
        blocks.append(jnp.concatenate(log_rows, 0).astype(LOW))
        return_ref[...] = jnp.concatenate(blocks, 0)
    normed_ref[...] = normed_last
    grad_low_ref[...] = (grad_attn_last * base_factor).astype(LOW)
    score_grad_ref[...] = score_grad_last
    kept_ref[0:1, :] = inner_last * base_factor


def last_head_kernel(top_step, q_ref, k_ref, v_ref, gain_ref, expo_ref, *refs):
    normed_ref, grad_low_ref, peer_score_grad_ref, kept_ref, *peers = refs[: 4 + PEERS]
    peers = nearest_first([None, *peers])[1:]
    attended_ref, dq_ref, dk_ref, dv_ref = refs[4 + PEERS :]
    picked = sum(picked_counts(q_ref.shape[1], top_step))
    score_scale = 1.0 / math.sqrt(HEAD_DIM)
    cols = head_cols(q_ref.shape[2] // HEAD_DIM - 1)
    attended_ref[...] = (normed_ref[...].T * gain_ref[:, cols]).astype(LOW)
    k_peers = jnp.concatenate([ref[5 * picked : 6 * picked] for ref in peers], 0)
    grad_low = grad_low_ref[...]
    expo_low = expo_ref[:, cols]
    prob_grad = contract(v_ref[0, :, cols], grad_low, 1, 0)
    score_grad = (
        expo_low.astype(WIDE) * (prob_grad - kept_ref[0:1, :]) * score_scale
    ).astype(LOW)
    dk_ref[...] = contract(score_grad, q_ref[0, :, cols], 1, 0)
    dv_ref[...] = contract(expo_low, grad_low, 1, 1)
    dq_ref[...] = (
        contract(score_grad, k_ref[0, :, cols], 0, 0)
        + contract(peer_score_grad_ref[...], k_peers, 0, 0)
    ).astype(LOW)


def gain_kernel(picked, *refs):
    return_refs, gain_ref = nearest_first(refs[:SPAN]), refs[SPAN]
    tiles = [ref[6 * picked : 6 * picked + STAT_TILES].astype(WIDE) for ref in return_refs]
    parts = [tile[PIECES:TILE] + tile[TILE + PIECES :] for tile in tiles]
    total = (parts[0] + parts[1]) + (parts[2] + parts[3])
    for head in range(gain_ref.shape[1] // HEAD_DIM):
        gain_ref[:, head_cols(head)] = total[head : head + 1]


def mix_kernel(top_step, q_ref, k_ref, v_ref, gain_ref, expo_ref, out_ref, *refs):
    grad_norm_ref, stats_ref, place_ref, masks_ref = refs[:4]
    last_attended_ref, last_dq_ref, last_dk_ref, last_dv_ref = refs[4:8]
    return_refs, refs = nearest_first(refs[8 : 8 + SPAN]), refs[8 + SPAN :]
    attended_ref, dq_ref, dk_ref, dv_ref, placed_ref = refs
    tokens, width = v_ref.shape[1:]
    count = width // HEAD_DIM
    picked = sum(picked_counts(tokens, top_step))
    score_scale = 1.0 / math.sqrt(HEAD_DIM)
    me = lax.axis_index("ctx")
    heads = range(OWNED)
    every = [head_cols(head) for head in heads]
    for distance, return_ref in enumerate(return_refs):
        placed_ref[me ^ distance] = return_ref[...]
    once = [place_ref[:, head_cols(count + head)] for head in heads]
    attn_parts = [
        contract(placed_ref[head, 3 * picked : 4 * picked], once[head][:, :picked], 0, 1)
        for head in heads
    ]
    log_parts = [
        contract(placed_ref[head, 6 * picked : 6 * picked + STAT_TILES], once[head], 1, 1)
        for head in heads
    ]
    normeds, grad_lows, inners, inv_totals = [], [], [], []
    for head in heads:
        seen = masks_ref[TILE + head : TILE + head + 1, :tokens] > 0.5
        top_score, total = stats_ref[head : head + 1, :], stats_ref[TILE + head : TILE + head + 1, :]
        base_log = top_score + jnp.log(total)
        log_total = jnp.where(seen, joined_row(log_parts[head], 0), base_log)
        share = jnp.exp(base_log - log_total)
        inv_totals.append(1.0 / total)
        attn = jnp.where(seen, attn_parts[head], out_ref[:, every[head]].astype(WIDE))
        normed, _, grad_attn, inner = norm_backward(attn, grad_norm_ref[:, every[head]])
        normeds.append(normed)
        grad_lows.append((share * grad_attn).astype(LOW))
        inners.append(share * inner)
    prob_grads = [contract(v_ref[0, :, every[head]], grad_lows[head], 1, 0) for head in heads]
    softs = [expo_ref[:, every[head]].astype(WIDE) * inv_totals[head] for head in heads]
    soft_lows = [soft.astype(LOW) for soft in softs]
    score_grads = [
        (softs[head] * (prob_grads[head] - inners[head]) * score_scale).astype(LOW)
        for head in heads
    ]
    dqs = [contract(score_grads[head], k_ref[0, :, every[head]], 0, 0) for head in heads]
    placed = [
        contract(
            place_ref[:, pl.ds(head * HEAD_DIM, picked)],
            jnp.concatenate(
                [placed_ref[head, block * picked : (block + 1) * picked] for block in range(3)], 1
            ),
            1,
            0,
        )
        for head in heads
    ]
    dks = [contract(score_grads[head], q_ref[0, :, every[head]], 1, 0) for head in heads]
    dvs = [contract(soft_lows[head], grad_lows[head], 1, 1) for head in heads]
    last = count - 1
    total = sum(ref[4 * picked : 6 * picked].astype(WIDE) for ref in return_refs[1:]).astype(LOW)
    rows = contract(
        place_ref[:, pl.ds(last * HEAD_DIM, picked)],
        jnp.concatenate([total[:picked], total[picked:]], 1),
        1,
        0,
    )
    for head in heads:
        cols = every[head]
        attended_ref[:, cols] = (normeds[head].T * gain_ref[:, cols]).astype(LOW)
        for which, (block, out_block_ref) in enumerate(
            ((dqs[head], dq_ref), (dks[head], dk_ref), (dvs[head], dv_ref))
        ):
            part = placed[head][:, which * HEAD_DIM : (which + 1) * HEAD_DIM]
            out_block_ref[:, cols] = (block + part).astype(LOW)
    cols = head_cols(last)
    attended_ref[:, cols] = last_attended_ref[...]
    dq_ref[:, cols] = last_dq_ref[...]
    dk_ref[:, cols] = (last_dk_ref[...] + rows[:, :HEAD_DIM]).astype(LOW)
    dv_ref[:, cols] = (last_dv_ref[...] + rows[:, HEAD_DIM:]).astype(LOW)


def finish_kernel(gain_ref, gain_rest_ref, *refs):
    block_refs, result_refs, gain_out_ref = refs[:4], refs[4:8], refs[8]
    for block_ref, result_ref in zip(block_refs, result_refs):
        result_ref[0] = block_ref[...]
    gain_out_ref[...] = (gain_ref[...] + gain_rest_ref[...]).reshape(gain_out_ref.shape)


def across(block, axis, distance):
    route = [(place, place ^ distance) for place in range(lax.axis_size(axis))]
    return lax.ppermute(block, axis, route)


def to_peers(blocks):
    return [across(blocks[distance - 1], "ctx", distance) for distance in START_ORDER]


def call(kernel, name, operands, results, microseconds, vmem=PLAIN_VMEM, scratch=()):
    return pl.pallas_call(
        kernel,
        out_shape=results,
        in_specs=[VMEM_SPEC] * len(operands),
        out_specs=[VMEM_SPEC] * len(results),
        scratch_shapes=scratch,
        compiler_params=pltpu.CompilerParams(vmem_limit_bytes=vmem),
        cost_estimate=pl.CostEstimate(
            flops=int(microseconds * 10**9), bytes_accessed=0, transcendentals=0
        ),
        name=name,
    )(*operands)


def one_segment_shards(queries, keys, values, grad_y, out_gain, offsets):
    tokens, width = queries.shape[1:]
    heads = width // HEAD_DIM
    top_step = lax.axis_size("ctx")
    picked = sum(picked_counts(tokens, top_step))
    shape = jax.ShapeDtypeStruct
    row_block = shape((1, tokens, width), LOW)
    low_block, wide_block = shape((tokens, width), LOW), shape((tokens, width), WIDE)
    low_head, wide_head = shape((tokens, HEAD_DIM), LOW), shape((tokens, HEAD_DIM), WIDE)
    gain_block = shape((1, width), WIDE)
    stats_block = shape((2 * TILE, tokens), WIDE)
    payload = shape((7 * picked + STAT_TILES, HEAD_DIM), LOW)
    answer = shape((6 * picked + STAT_TILES, HEAD_DIM), LOW)
    bind = functools.partial
    gain_row = out_gain.reshape(1, width)
    (picks,) = call(
        bind(picks_kernel, top_step), "picks", (offsets,), [shape((tokens, width + tokens), LOW)], 20
    )
    own, *sent = call(
        bind(pack_kernel, top_step),
        "pack",
        (picks, queries, keys, values, grad_y),
        [payload] * SPAN,
        1,
    )
    received = to_peers(sent)
    grad_norm, gain_base, place, masks, expo, base_out, stats = call(
        bind(prepare_kernel, top_step),
        "prepare",
        (offsets, queries, keys, values, grad_y, gain_row, picks),
        [
            wide_block,
            gain_block,
            shape((tokens, 2 * width), LOW),
            shape((2 * TILE, 2 * tokens), WIDE),
            low_block,
            low_block,
            stats_block,
        ],
        2,
    )
    normed, grad_low, score_grad, kept, own_answer, *answers = call(
        bind(owner_kernel, top_step),
        "owner",
        (queries, gain_row, base_out, grad_norm, stats, gain_base, masks, own, *received),
        [
            wide_head,
            low_head,
            shape((PEERS * picked, HEAD_DIM), LOW),
            shape((TILE, tokens), WIDE),
        ]
        + [answer] * SPAN,
        3,
    )
    returned = to_peers(answers)
    last_results = call(
        bind(last_head_kernel, top_step),
        "last_head",
        (queries, keys, values, gain_row, expo, normed, grad_low, score_grad, kept, *received),
        [low_head, low_head, wide_head, wide_head],
        20,
    )
    (gain_sum,) = call(bind(gain_kernel, picked), "gain", (own_answer, *returned), [gain_block], 1)
    gain_rest = across(gain_sum, "dp", 1)
    mixed = call(
        bind(mix_kernel, top_step),
        "mix",
        (
            queries,
            keys,
            values,
            gain_row,
            expo,
            base_out,
            grad_norm,
            stats,
            place,
            masks,
            *last_results,
            own_answer,
            *returned,
        ),
        [low_block] * 4,
        20,
        scratch=[pltpu.VMEM((OWNED, *answer.shape), LOW)],
    )
    attended, query_grad, key_grad, value_grad, gain_grad = call(
        finish_kernel,
        "finish",
        (gain_sum, gain_rest, *mixed),
        [row_block] * 4 + [shape((width,), WIDE)],
        1,
    )
    return attended, query_grad, key_grad, value_grad, gain_grad


def shards(*operands):
    one_segment = lax.axis_size("ctx") == SPAN
    if one_segment and operands[0].shape[2] == (OWNED + 1) * HEAD_DIM:
        return one_segment_shards(*operands)
    return general_shards(*operands)


def solution(mesh):
    in_specs = (
        P("dp", "ctx", "head"),
        P("dp", "ctx", "head"),
        P("dp", "ctx", "head"),
        P("dp", "ctx", "head"),
        P("head"),
        P(None, "head"),
    )
    out_specs = (
        P("dp", "ctx", "head"),
        P("dp", "ctx", "head"),
        P("dp", "ctx", "head"),
        P("dp", "ctx", "head"),
        P("head"),
    )
    return jax.shard_map(shards, mesh=mesh, in_specs=in_specs, out_specs=out_specs, check_vma=False)
```

```python
import functools
import math

import jax
import jax.numpy as jnp
from jax import lax
from jax.experimental import pallas as pl
from jax.experimental.pallas import tpu as pltpu
from jax.sharding import PartitionSpec as P

HEAD_DIM = 128
SPAN = 4
R1 = 8


EPS = 1e-06


def swapped(block, axis, bit):
    count = lax.axis_size(axis)
    route = []
    for low in range(count):
        high = low | 1 << bit
        if high != low and high < count:
            route += [(low, high), (high, low)]
    return lax.ppermute(block, axis, route)


def pick_rows(source_rows, dilation, shifts):
    row_count, head_count, head_width = source_rows.shape
    grouped = source_rows.reshape(row_count // dilation, dilation, head_count, head_width)
    hit_mask = jnp.arange(dilation, dtype=jnp.int32).reshape(1, dilation, 1, 1) == shifts.reshape(
        1, 1, head_count, 1
    )
    chosen = jnp.where(hit_mask, grouped, jnp.zeros((), source_rows.dtype))
    return jnp.sum(chosen, axis=1, dtype=source_rows.dtype)


def place_rows(row_values, dilation, shifts):
    row_count, head_count, head_width = row_values.shape
    hit_mask = jnp.arange(dilation, dtype=jnp.int32).reshape(1, dilation, 1, 1) == shifts.reshape(
        1, 1, head_count, 1
    )
    spread = jnp.where(hit_mask, row_values[:, None], jnp.zeros((), row_values.dtype))
    return spread.reshape(row_count * dilation, head_count, head_width)


def level_scores(q_rows, k_rows):
    score_scale = 1.0 / math.sqrt(q_rows.shape[-1])
    return (
        jnp.einsum("qhe,khe->hqk", q_rows, k_rows, preferred_element_type=jnp.float32) * score_scale
    )


def attend(q_rows, k_rows, v_rows):
    scores = level_scores(q_rows, k_rows)
    row_max = jnp.max(scores, axis=-1, keepdims=True)
    log_total = row_max[..., 0] + jnp.log(jnp.sum(jnp.exp(scores - row_max), axis=-1))
    soft_rows = jnp.exp(scores - log_total[..., None]).astype(jnp.bfloat16)
    level_out = jnp.einsum("hqk,khe->qhe", soft_rows, v_rows, preferred_element_type=jnp.float32)
    return (level_out, log_total.T)


def score_grads(q_rows, k_rows, v_rows, log_total, grad_low, row_shift):
    score_scale = 1.0 / math.sqrt(q_rows.shape[-1])
    scores = level_scores(q_rows, k_rows)
    exact_soft = jnp.exp(scores - log_total.T[..., None])
    prob_grad = jnp.einsum("qhe,khe->hqk", grad_low, v_rows, preferred_element_type=jnp.float32)
    score_grad = (exact_soft * (prob_grad + row_shift.T[..., None]) * score_scale).astype(
        jnp.bfloat16
    )
    return (score_grad, exact_soft.astype(jnp.bfloat16))


def key_parts(score_grad, soft_low, q_rows, grad_low):
    k_part = jnp.einsum("hqk,qhe->khe", score_grad, q_rows, preferred_element_type=jnp.float32)
    v_part = jnp.einsum("hqk,qhe->khe", soft_low, grad_low, preferred_element_type=jnp.float32)
    return (k_part, v_part)


def query_part(score_grad, k_rows):
    return jnp.einsum("hqk,khe->qhe", score_grad, k_rows, preferred_element_type=jnp.float32)


def general_shards(queries, keys, values, grad_y, out_gain, offsets):
    tokens = queries.shape[1]
    flat_width = queries.shape[2]
    head_count = flat_width // HEAD_DIM
    row_shape = (tokens, head_count, HEAD_DIM)
    q_own = queries[0].reshape(row_shape)
    k_own = keys[0].reshape(row_shape)
    v_own = values[0].reshape(row_shape)
    ctx_size = lax.axis_size("ctx")
    span_bits = SPAN.bit_length() - 1
    my_place = lax.axis_index("ctx")
    mid_shift = offsets[0]
    top_shift = offsets[1]
    positions = jnp.arange(tokens, dtype=jnp.int32)
    mid_hit = (positions % R1)[:, None] == mid_shift[None, :]
    top_hit = (positions % ctx_size)[:, None] == top_shift[None, :]
    mid_q = pick_rows(q_own, R1, mid_shift)
    mid_k = pick_rows(k_own, R1, mid_shift)
    mid_v = pick_rows(v_own, R1, mid_shift)
    top_q = pick_rows(q_own, ctx_size, top_shift)
    top_k = pick_rows(k_own, ctx_size, top_shift)
    top_v = pick_rows(v_own, ctx_size, top_shift)
    mid_keys = mid_k.reshape(-1, flat_width)
    mid_vals = mid_v.reshape(-1, flat_width)
    top_keys = top_k.reshape(-1, flat_width)
    top_vals = top_v.reshape(-1, flat_width)

    def append_peer(mine, received, level_bit):
        upper_side = my_place >> level_bit & 1 == 1
        return jnp.where(
            upper_side, jnp.concatenate([received, mine], 0), jnp.concatenate([mine, received], 0)
        )

    for level_bit in range(span_bits):
        received = swapped((mid_keys, mid_vals), "ctx", level_bit)
        mid_keys = append_peer(mid_keys, received[0], level_bit)
        mid_vals = append_peer(mid_vals, received[1], level_bit)
    top_keys, top_vals = (
        lax.all_gather(top_keys, "ctx", axis=0, tiled=True),
        lax.all_gather(top_vals, "ctx", axis=0, tiled=True),
    )
    mid_keys = mid_keys.reshape(-1, head_count, HEAD_DIM)
    mid_vals = mid_vals.reshape(-1, head_count, HEAD_DIM)
    top_keys = top_keys.reshape(-1, head_count, HEAD_DIM)
    top_vals = top_vals.reshape(-1, head_count, HEAD_DIM)
    base_out, base_total = attend(q_own, k_own, v_own)
    mid_out, mid_total = attend(mid_q, mid_keys, mid_vals)
    top_out, top_total = attend(top_q, top_keys, top_vals)
    mid_full = place_rows(mid_total[..., None], R1, mid_shift)[..., 0]
    top_full = place_rows(top_total[..., None], ctx_size, top_shift)[..., 0]
    row_max = jnp.maximum(base_total, jnp.where(mid_hit, mid_full, base_total))
    row_max = jnp.maximum(row_max, jnp.where(top_hit, top_full, base_total))
    base_expo = jnp.exp(base_total - row_max)
    mid_expo = jnp.where(mid_hit, jnp.exp(mid_full - row_max), 0.0)
    top_expo = jnp.where(top_hit, jnp.exp(top_full - row_max), 0.0)
    denom = base_expo + mid_expo + top_expo
    base_share = base_expo / denom
    mid_share = mid_expo / denom
    top_share = top_expo / denom
    attn = (
        base_share[..., None] * base_out
        + mid_share[..., None] * place_rows(mid_out, R1, mid_shift)
        + top_share[..., None] * place_rows(top_out, ctx_size, top_shift)
    )
    inv_rms = lax.rsqrt(jnp.mean(attn * attn, axis=-1, keepdims=True) + EPS)
    normed = attn * inv_rms
    gain_rows = out_gain.reshape(head_count, HEAD_DIM)
    attended = (normed * gain_rows).astype(jnp.bfloat16).reshape(1, tokens, flat_width)
    grad_full = grad_y[0].reshape(row_shape).astype(jnp.float32)
    gain_part = jnp.sum(grad_full * normed, axis=0).reshape(flat_width)
    gain_grad = lax.psum(gain_part, ("dp", "ctx"))
    grad_norm = grad_full * gain_rows
    grad_attn = inv_rms * (
        grad_norm - normed * jnp.mean(grad_norm * normed, axis=-1, keepdims=True)
    )
    inner = jnp.sum(grad_attn * attn, axis=-1)
    base_low = (base_share[..., None] * grad_attn).astype(jnp.bfloat16)
    base_shift = -(base_share * inner)
    base_grad, base_soft = score_grads(q_own, k_own, v_own, base_total, base_low, base_shift)
    base_dq = query_part(base_grad, k_own)
    base_dk, base_dv = key_parts(base_grad, base_soft, q_own, base_low)
    mid_sel = pick_rows(mid_share[..., None], R1, mid_shift)[..., 0]
    mid_low = (mid_sel[..., None] * pick_rows(grad_attn, R1, mid_shift)).astype(jnp.bfloat16)
    mid_row_shift = -(mid_sel * pick_rows(inner[..., None], R1, mid_shift)[..., 0])
    mid_grad, mid_soft = score_grads(mid_q, mid_keys, mid_vals, mid_total, mid_low, mid_row_shift)
    mid_dq = query_part(mid_grad, mid_keys)
    mid_dk, mid_dv = key_parts(mid_grad, mid_soft, mid_q, mid_low)
    mid_dk = mid_dk.reshape(-1, flat_width)
    mid_dv = mid_dv.reshape(-1, flat_width)
    for level_bit in reversed(range(span_bits)):
        half_rows = mid_dk.shape[0] // 2
        upper_side = my_place >> level_bit & 1 == 1
        keep_k = jnp.where(upper_side, mid_dk[half_rows:], mid_dk[:half_rows])
        keep_v = jnp.where(upper_side, mid_dv[half_rows:], mid_dv[:half_rows])
        send_k = jnp.where(upper_side, mid_dk[:half_rows], mid_dk[half_rows:])
        send_v = jnp.where(upper_side, mid_dv[:half_rows], mid_dv[half_rows:])
        received = (
            swapped(send_k.astype(jnp.bfloat16), "ctx", level_bit).astype(send_k.dtype),
            swapped(send_v.astype(jnp.bfloat16), "ctx", level_bit).astype(send_v.dtype),
        )
        mid_dk = keep_k + received[0]
        mid_dv = keep_v + received[1]
    mid_dk = mid_dk.reshape(-1, head_count, HEAD_DIM)
    mid_dv = mid_dv.reshape(-1, head_count, HEAD_DIM)
    top_sel = pick_rows(top_share[..., None], ctx_size, top_shift)[..., 0]
    top_low = (top_sel[..., None] * pick_rows(grad_attn, ctx_size, top_shift)).astype(jnp.bfloat16)
    top_row_shift = -(top_sel * pick_rows(inner[..., None], ctx_size, top_shift)[..., 0])
    top_grad, top_soft = score_grads(top_q, top_keys, top_vals, top_total, top_low, top_row_shift)
    top_dq = query_part(top_grad, top_keys)
    gathered_dk, gathered_dv = key_parts(top_grad, top_soft, top_q, top_low)
    summed = (
        lax.psum_scatter(
            gathered_dk.reshape(-1, flat_width), "ctx", scatter_dimension=0, tiled=True
        ),
        lax.psum_scatter(
            gathered_dv.reshape(-1, flat_width), "ctx", scatter_dimension=0, tiled=True
        ),
    )
    top_dk = summed[0].reshape(-1, head_count, HEAD_DIM)
    top_dv = summed[1].reshape(-1, head_count, HEAD_DIM)
    query_grad = (
        base_dq + place_rows(mid_dq, R1, mid_shift) + place_rows(top_dq, ctx_size, top_shift)
    )
    key_grad = base_dk + place_rows(mid_dk, R1, mid_shift) + place_rows(top_dk, ctx_size, top_shift)
    value_grad = (
        base_dv + place_rows(mid_dv, R1, mid_shift) + place_rows(top_dv, ctx_size, top_shift)
    )
    out_shape = (1, tokens, flat_width)
    return (
        attended,
        query_grad.astype(jnp.bfloat16).reshape(out_shape),
        key_grad.astype(jnp.bfloat16).reshape(out_shape),
        value_grad.astype(jnp.bfloat16).reshape(out_shape),
        gain_grad,
    )


VMEM_SPEC = pl.BlockSpec(memory_space=pltpu.VMEM)
PEERS = SPAN - 1
OWNED = SPAN
TILE = 8
STAT_TILES = 2 * TILE
PIECES = 3
NEVER = -1e30
START_ORDER = (3, 1, 2)
LOW = jnp.bfloat16
WIDE = jnp.float32
PLAIN_VMEM = 16 * 1024 * 1024


def contract(left, right, left_dim, right_dim):
    return lax.dot_general(
        left, right, (((left_dim,), (right_dim,)), ((), ())), preferred_element_type=WIDE
    )


def head_cols(head):
    return pl.ds(head * HEAD_DIM, HEAD_DIM)


def picked_counts(tokens, top_step):
    return tokens // top_step, tokens // R1


def offset_of(offsets_ref, level, head):
    return offsets_ref[level : level + 1, head : head + 1]


def pick_matrix(offsets_ref, head, tokens, top_step, picked_axis):
    top_rows, _ = picked_counts(tokens, top_step)
    row = lax.broadcasted_iota(jnp.int32, (tokens, tokens), picked_axis)
    position = lax.broadcasted_iota(jnp.int32, (tokens, tokens), 1 - picked_axis)
    wanted = jnp.where(
        row < top_rows,
        row * top_step + offset_of(offsets_ref, 1, head),
        (row - top_rows) * R1 + offset_of(offsets_ref, 0, head),
    )
    return jnp.where(position == wanted, 1.0, 0.0).astype(LOW)


def rolled(row, shift):
    return pltpu.roll(row, shift % row.shape[1], 1)


def lane_window(row, start, count):
    lane = lax.broadcasted_iota(jnp.int32, row.shape, 1)
    return jnp.where((lane >= start) & (lane < start + count), row, 0.0)


def hit_row(offset, step, tokens):
    position = lax.broadcasted_iota(jnp.int32, (1, tokens), 1)
    return jnp.where(position % step == offset, 1.0, 0.0)


def piece_rows(row, others=None):
    pieces = []
    for _ in range(PIECES):
        piece = row.astype(LOW).astype(WIDE)
        pieces.append(piece)
        row = row - piece
    if others is None:
        others = jnp.zeros((TILE - PIECES, row.shape[1]), WIDE)
    return jnp.concatenate(pieces + [others], 0)


def gain_pieces(rows):
    high = rows.astype(LOW)
    return high, (rows - high.astype(WIDE)).astype(LOW)


def joined_row(rows, first):
    total = rows[first : first + 1]
    for piece in range(1, PIECES):
        total = total + rows[first + piece : first + piece + 1]
    return total


def gain_row_of(ones, product):
    high, rest = gain_pieces(product)
    return (contract(ones, high, 1, 1) + contract(ones, rest, 1, 1))[:1]


def column_mean(block):
    return jnp.mean(block, axis=0, keepdims=True)


def norm_backward(attn, grad_norm):
    inv_rms = lax.rsqrt(column_mean(attn * attn) + EPS)
    normed = attn * inv_rms
    product = grad_norm * normed
    grad_attn = inv_rms * (grad_norm - normed * column_mean(product))
    inner = jnp.sum(grad_attn * attn, axis=0, keepdims=True)
    return normed, product, grad_attn, inner


def nearest_first(refs):
    by_distance = dict(zip(START_ORDER, refs[1:]))
    return [refs[0], *[by_distance[distance] for distance in range(1, SPAN)]]


def picks_kernel(top_step, offsets_ref, picks_ref):
    tokens = picks_ref.shape[0]
    last = offsets_ref.shape[1] - 1
    for head in range(last + 1):
        picks_ref[:, head_cols(head)] = pick_matrix(offsets_ref, head, tokens, top_step, 0)
    key_row = lax.broadcasted_iota(jnp.int32, (tokens, 1), 0)
    times = 1.0
    for level, step in ((0, R1), (1, top_step)):
        offset = offset_of(offsets_ref, level, last)
        hit_column = jnp.where(key_row % step == offset, 1.0, 0.0)
        times = times + hit_column * hit_row(offset, step, tokens)
    picks_ref[:, head_cols(last + 1)] = times.astype(LOW)


def pack_kernel(top_step, picks_ref, q_ref, k_ref, v_ref, grad_ref, *refs):
    payload_refs, held_ref = refs[:SPAN], refs[SPAN]
    tokens, width = q_ref.shape[1:]
    heads = range(width // HEAD_DIM)
    owned = range(OWNED)
    me = lax.axis_index("ctx")
    picked = sum(picked_counts(tokens, top_step))
    score_scale = 1.0 / math.sqrt(HEAD_DIM)
    q_rows, k_rows, v_rows, grad_rows = [
        [ref[0, :, head_cols(head)] for head in heads] for ref in (q_ref, k_ref, v_ref, grad_ref)
    ]
    picks = [picks_ref[:, head_cols(head)] for head in heads]
    scores = [contract(k_rows[head], q_rows[head], 1, 1) * score_scale for head in owned]
    moved = [
        contract(
            picks[head][:picked],
            jnp.concatenate([q_rows[head], k_rows[head], v_rows[head], grad_rows[head]], 1),
            1,
            0,
        ).astype(LOW)
        for head in owned
    ]
    shared = [
        contract(
            picks[head][:picked], jnp.concatenate([k_rows[head], v_rows[head]], 1), 1, 0
        ).astype(LOW)
        for head in heads[OWNED:]
    ]
    top_scores = [jnp.max(block, axis=0, keepdims=True) for block in scores]
    expos = [jnp.exp(scores[head] - top_scores[head]) for head in owned]
    expo_lows = [expo.astype(LOW) for expo in expos]
    outs = [contract(v_rows[head], expo_lows[head], 0, 0) for head in owned]
    totals = [jnp.sum(expo, axis=0, keepdims=True) for expo in expos]
    outs = [(outs[head] * (1.0 / totals[head])).astype(LOW) for head in owned]
    picked_outs = [
        contract(picks[head][:picked], outs[head], 1, 1).astype(LOW) for head in owned
    ]
    for head in owned:
        pieces = piece_rows(top_scores[head] + jnp.log(totals[head])).astype(LOW)
        stat_rows = contract(pieces, picks[head], 1, 1)
        blocks = [moved[head][:, block * HEAD_DIM : (block + 1) * HEAD_DIM] for block in range(4)]
        blocks.append(picked_outs[head])
        blocks += [shared[0][:, :HEAD_DIM], shared[0][:, HEAD_DIM:]]
        blocks.append(jnp.concatenate([stat_rows, jnp.zeros_like(stat_rows)], 0).astype(LOW))
        held_ref[head] = jnp.concatenate(blocks, 0)
    for distance, payload_ref in enumerate(payload_refs):
        payload_ref[...] = held_ref[me ^ distance]


def prepare_kernel(top_step, offsets_ref, q_ref, k_ref, v_ref, grad_ref, gain_ref, *refs):
    picks_ref, grad_norm_ref, gain_part_ref, place_ref, masks_ref, expo_ref, out_ref, stats_ref = refs
    tokens, width = grad_ref.shape[1:]
    heads = range(width // HEAD_DIM)
    score_scale = 1.0 / math.sqrt(HEAD_DIM)
    every = [head_cols(head) for head in heads]
    scores = [
        contract(k_ref[0, :, cols], q_ref[0, :, cols], 1, 1) * score_scale for cols in every
    ]
    top_scores = [jnp.max(block, axis=0, keepdims=True) for block in scores]
    expos = [jnp.exp(scores[head] - top_scores[head]) for head in heads]
    times = picks_ref[:, head_cols(len(heads))].astype(WIDE)
    for head in heads[OWNED:]:
        expos[head] = times * expos[head]
    expo_lows = [expo.astype(LOW) for expo in expos]
    outs = [contract(v_ref[0, :, cols], expo_lows[head], 0, 0) for head, cols in enumerate(every)]
    totals = [jnp.sum(expo, axis=0, keepdims=True) for expo in expos]
    for head in range(OWNED):
        outs[head] = outs[head] * (1.0 / totals[head])
    outs = [out.astype(LOW) for out in outs]
    for head, cols in enumerate(every):
        expo_ref[:, cols] = expo_lows[head]
        out_ref[:, cols] = outs[head]
        stats_ref[head : head + 1, :] = top_scores[head]
        stats_ref[TILE + head : TILE + head + 1, :] = totals[head]
    top_rows = tokens // top_step
    ones = jnp.ones((TILE, tokens), LOW)
    column = lax.broadcasted_iota(jnp.int32, (tokens, tokens), 1)
    gain_part_ref[...] = jnp.zeros(gain_part_ref.shape, WIDE)
    me = lax.axis_index("ctx")
    mid_rows = tokens // R1
    top_all, queries = SPAN * top_rows, SPAN * (top_rows + mid_rows)
    mid_offset, top_offset = [
        sum(
            jnp.where(me == head, offset_of(offsets_ref, level, head), 0) for head in range(OWNED)
        )
        for level in (0, 1)
    ]
    lane = lax.broadcasted_iota(jnp.int32, (1, queries), 1)
    is_top = jnp.where(lane < top_all, 1.0, 0.0)
    top_in_mid = jnp.where(((lane % top_rows) * top_step + top_offset) % R1 == mid_offset, 1.0, 0.0)
    both_flag = jnp.where(mid_offset % top_step == top_offset, 1.0, 0.0)
    sees_top = is_top + (1.0 - is_top) * both_flag
    sees_mid = is_top * top_in_mid + (1.0 - is_top)
    masks_ref[0:1, :queries] = (1.0 - sees_top) * NEVER
    masks_ref[1:2, :queries] = (1.0 - sees_mid) * NEVER
    masks_ref[2:3, :queries] = is_top + (1.0 - is_top) * (1.0 - both_flag)
    last = len(heads) - 1
    for row, (level, step) in enumerate(((1, top_step), (0, R1))):
        hits = hit_row(offset_of(offsets_ref, level, last), step, tokens)
        masks_ref[3 + row : 4 + row, :tokens] = (1.0 - hits) * NEVER
    grad_norms = [
        (grad_ref[0, :, head_cols(head)].astype(WIDE) * gain_ref[:, head_cols(head)]).T
        for head in heads
    ]
    for head in heads:
        cols = head_cols(head)
        grad_norm_ref[:, cols] = grad_norms[head]
        picks = pick_matrix(offsets_ref, head, tokens, top_step, 1)
        place_ref[:, cols] = picks
    for head in range(OWNED):
        cols = head_cols(head)
        mid_offset, top_offset = [offset_of(offsets_ref, level, head) for level in (0, 1)]
        seen = jnp.maximum(
            hit_row(top_offset, top_step, tokens), hit_row(mid_offset, R1, tokens)
        )
        masks_ref[TILE + head : TILE + head + 1, :tokens] = seen
        attn = outs[head].astype(WIDE)
        normed = attn * lax.rsqrt(column_mean(attn * attn) + EPS)
        product = grad_norms[head] * normed * (1.0 - seen)
        gain_part_ref[:, cols] = gain_row_of(ones, product) / gain_ref[:, cols]
        both = mid_offset % top_step == top_offset
        kept = jnp.where(column < top_rows, 1.0, jnp.where(both, 0.0, 1.0)).astype(LOW)
        picks = pick_matrix(offsets_ref, head, tokens, top_step, 1)
        place_ref[:, head_cols(len(heads) + head)] = picks * kept


def owner_kernel(top_step, q_ref, gain_ref, out_ref, grad_norm_ref, *refs):
    stats_ref, gain_base_ref, masks_ref = refs[:3]
    payload_refs, refs = nearest_first(refs[3 : 3 + SPAN]), refs[3 + SPAN :]
    normed_ref, grad_low_ref, score_grad_ref, kept_ref = refs[:4]
    return_refs = refs[4:]
    tokens = q_ref.shape[1]
    heads = q_ref.shape[2] // HEAD_DIM
    top_rows, mid_rows = picked_counts(tokens, top_step)
    picked = top_rows + mid_rows
    top_all, mid_all = SPAN * top_rows, SPAN * mid_rows
    queries = top_all + mid_all
    score_scale = 1.0 / math.sqrt(HEAD_DIM)
    me = lax.axis_index("ctx")
    ones = jnp.ones((TILE, tokens), LOW)

    def by_level(block):
        start = block * picked
        return jnp.concatenate(
            [ref[start : start + top_rows] for ref in payload_refs]
            + [ref[start + top_rows : start + picked] for ref in payload_refs],
            0,
        )

    def per_level(top_row, mid_row):
        return jnp.concatenate(
            [
                jnp.broadcast_to(top_row, (top_all, queries)),
                jnp.broadcast_to(mid_row, (mid_all, queries)),
            ],
            0,
        )

    q_rows, k_rows, v_rows, grad_rows, base_rows = [by_level(block) for block in range(5)]
    stat_start = 7 * picked
    logs = [
        joined_row(ref[stat_start : stat_start + STAT_TILES].astype(WIDE), 0)
        for ref in payload_refs
    ]
    base_top_log = sum(
        rolled(lane_window(log, 0, top_rows), slot * top_rows) for slot, log in enumerate(logs)
    )
    base_mid_log = sum(
        rolled(lane_window(log, top_rows, mid_rows), slot * mid_rows - top_rows)
        for slot, log in enumerate(logs)
    )
    base_log = jnp.concatenate([base_top_log, base_mid_log[:, :mid_all]], 1)
    gain_row = jnp.zeros((1, HEAD_DIM), WIDE)
    for head in range(OWNED):
        gain_row = gain_row + jnp.where(me == head, 1.0, 0.0) * gain_ref[:, head_cols(head)]
    lane = lax.broadcasted_iota(jnp.int32, (1, queries), 1)
    is_top = jnp.where(lane < top_all, 1.0, 0.0)
    bias = per_level(masks_ref[0:1, :queries], masks_ref[1:2, :queries])
    last = heads - 1
    cols = head_cols(last)
    peers = payload_refs[1:]
    q_last = q_ref[0, :, cols]
    k_peers = jnp.concatenate([ref[5 * picked : 6 * picked] for ref in peers], 0)
    v_peers = jnp.concatenate([ref[6 * picked : 7 * picked] for ref in peers], 0)
    last_biases = [
        jnp.broadcast_to(masks_ref[row : row + 1, :tokens], (count, tokens))
        for row, count in ((3, top_rows), (4, mid_rows))
    ]
    scores = contract(k_rows, q_rows, 1, 1) * score_scale + bias
    scores_last = contract(k_peers, q_last, 1, 1) * score_scale + jnp.concatenate(
        last_biases * PEERS, 0
    )
    base_attn = base_rows.astype(WIDE).T
    grad_norm = (grad_rows.astype(WIDE) * gain_row).T
    top_score = jnp.maximum(base_log, jnp.max(scores, axis=0, keepdims=True))
    base_top, base_total = stats_ref[last : last + 1, :], stats_ref[TILE + last : TILE + last + 1, :]
    top_last = jnp.maximum(base_top, jnp.max(scores_last, axis=0, keepdims=True))
    expo = jnp.exp(scores - top_score)
    expo_last = jnp.exp(scores_last - top_last)
    factor = jnp.exp(base_log - top_score)
    factor_last = jnp.exp(base_top - top_last)
    total = factor + jnp.sum(expo, axis=0, keepdims=True)
    total_last = factor_last * base_total + jnp.sum(expo_last, axis=0, keepdims=True)
    inv_total, inv_last = 1.0 / total, 1.0 / total_last
    expo_low, expo_last_low = expo.astype(LOW), expo_last.astype(LOW)
    attn = (factor * base_attn + contract(v_rows, expo_low, 0, 0)) * inv_total
    attn_last = (
        factor_last * out_ref[:, cols].astype(WIDE) + contract(v_peers, expo_last_low, 0, 0)
    ) * inv_last
    _, product, grad_attn, inner = norm_backward(attn, grad_norm)
    normed_last, product_last, grad_attn_last, inner_last = norm_backward(
        attn_last, grad_norm_ref[:, cols]
    )
    grad_low, inner = (grad_attn * inv_total).astype(LOW), inner * inv_total
    grad_last_low = (grad_attn_last * inv_last).astype(LOW)
    base_factor = factor_last * inv_last
    spans = (slice(0, top_all), slice(top_all, queries))
    prob_grads = [contract(v_rows[span], grad_low[:, span], 1, 0) for span in spans]
    prob_grad_last = contract(v_peers, grad_last_low, 1, 0)
    score_grads = [
        (expo[span, span] * (prob_grad - inner[:, span]) * score_scale).astype(LOW)
        for span, prob_grad in zip(spans, prob_grads)
    ]
    score_grad_last = (
        expo_last * (prob_grad_last - inner_last * inv_last) * score_scale
    ).astype(LOW)
    dks = [
        contract(score_grad, q_rows[span], 1, 0).astype(LOW)
        for span, score_grad in zip(spans, score_grads)
    ]
    dk_last = contract(score_grad_last, q_last, 1, 0).astype(LOW)
    dvs = [
        contract(expo_low[span, span], grad_low[:, span], 1, 1).astype(LOW) for span in spans
    ]
    dv_last = contract(expo_last_low, grad_last_low, 1, 1).astype(LOW)
    dqs = [
        contract(score_grad, k_rows[span], 0, 0).astype(LOW)
        for span, score_grad in zip(spans, score_grads)
    ]
    attn_rows = attn.T.astype(LOW)
    attn_parts = [attn_rows[span] for span in spans]
    log_total = top_score + jnp.log(total)
    padding = jnp.zeros((1, top_all - mid_all), WIDE)
    once = masks_ref[2:3, :queries]
    ones_all = jnp.ones((TILE, queries), LOW)
    own_gain = gain_row_of(ones_all, product * once) / gain_row
    gain_rows = [
        gain_base_ref[:, head_cols(head)] + jnp.where(me == head, 1.0, 0.0) * own_gain
        for head in range(OWNED)
    ]
    gain_rows.append(gain_row_of(ones, product_last) / gain_ref[:, cols])
    gain_high, gain_rest = [
        rows.astype(WIDE) for rows in gain_pieces(jnp.concatenate(gain_rows, 0))
    ]
    top_log, mid_log = log_total[:, :top_all], jnp.concatenate(
        [log_total[:, top_all:], padding], 1
    )
    empty = jnp.zeros((PIECES, HEAD_DIM), WIDE)
    for distance, return_ref in enumerate(return_refs):
        blocks = []
        for top_block, mid_block in (dqs, dks, dvs, attn_parts):
            blocks.append(top_block[distance * top_rows : (distance + 1) * top_rows])
            blocks.append(mid_block[distance * mid_rows : (distance + 1) * mid_rows])
        start = max(distance - 1, 0) * picked
        blocks += [dk_last[start : start + picked], dv_last[start : start + picked]]
        log_row = lane_window(rolled(top_log, -distance * top_rows), 0, top_rows) + lane_window(
            rolled(mid_log, top_rows - distance * mid_rows), top_rows, mid_rows
        )
        log_rows = [piece_rows(log_row, gain_high), empty, gain_rest]
        blocks.append(jnp.concatenate(log_rows, 0).astype(LOW))
        return_ref[...] = jnp.concatenate(blocks, 0)
    normed_ref[...] = normed_last
    grad_low_ref[...] = (grad_attn_last * base_factor).astype(LOW)
    score_grad_ref[...] = score_grad_last
    kept_ref[0:1, :] = inner_last * base_factor


def last_head_kernel(top_step, q_ref, k_ref, v_ref, gain_ref, expo_ref, *refs):
    normed_ref, grad_low_ref, peer_score_grad_ref, kept_ref, *peers = refs[: 4 + PEERS]
    peers = nearest_first([None, *peers])[1:]
    attended_ref, dq_ref, dk_ref, dv_ref = refs[4 + PEERS :]
    picked = sum(picked_counts(q_ref.shape[1], top_step))
    score_scale = 1.0 / math.sqrt(HEAD_DIM)
    cols = head_cols(q_ref.shape[2] // HEAD_DIM - 1)
    attended_ref[...] = (normed_ref[...].T * gain_ref[:, cols]).astype(LOW)
    k_peers = jnp.concatenate([ref[5 * picked : 6 * picked] for ref in peers], 0)
    grad_low = grad_low_ref[...]
    expo_low = expo_ref[:, cols]
    prob_grad = contract(v_ref[0, :, cols], grad_low, 1, 0)
    score_grad = (
        expo_low.astype(WIDE) * (prob_grad - kept_ref[0:1, :]) * score_scale
    ).astype(LOW)
    dk_ref[...] = contract(score_grad, q_ref[0, :, cols], 1, 0)
    dv_ref[...] = contract(expo_low, grad_low, 1, 1)
    dq_ref[...] = (
        contract(score_grad, k_ref[0, :, cols], 0, 0)
        + contract(peer_score_grad_ref[...], k_peers, 0, 0)
    ).astype(LOW)


def gain_kernel(picked, *refs):
    return_refs, gain_ref = nearest_first(refs[:SPAN]), refs[SPAN]
    tiles = [ref[6 * picked : 6 * picked + STAT_TILES].astype(WIDE) for ref in return_refs]
    parts = [tile[PIECES:TILE] + tile[TILE + PIECES :] for tile in tiles]
    total = (parts[0] + parts[1]) + (parts[2] + parts[3])
    for head in range(gain_ref.shape[1] // HEAD_DIM):
        gain_ref[:, head_cols(head)] = total[head : head + 1]


def mix_kernel(top_step, q_ref, k_ref, v_ref, gain_ref, expo_ref, out_ref, *refs):
    grad_norm_ref, stats_ref, place_ref, masks_ref = refs[:4]
    last_attended_ref, last_dq_ref, last_dk_ref, last_dv_ref = refs[4:8]
    return_refs, refs = nearest_first(refs[8 : 8 + SPAN]), refs[8 + SPAN :]
    attended_ref, dq_ref, dk_ref, dv_ref, placed_ref = refs
    tokens, width = v_ref.shape[1:]
    count = width // HEAD_DIM
    picked = sum(picked_counts(tokens, top_step))
    score_scale = 1.0 / math.sqrt(HEAD_DIM)
    me = lax.axis_index("ctx")
    heads = range(OWNED)
    every = [head_cols(head) for head in heads]
    for distance, return_ref in enumerate(return_refs):
        placed_ref[me ^ distance] = return_ref[...]
    once = [place_ref[:, head_cols(count + head)] for head in heads]
    attn_parts = [
        contract(placed_ref[head, 3 * picked : 4 * picked], once[head][:, :picked], 0, 1)
        for head in heads
    ]
    log_parts = [
        contract(placed_ref[head, 6 * picked : 6 * picked + STAT_TILES], once[head], 1, 1)
        for head in heads
    ]
    normeds, grad_lows, inners, inv_totals = [], [], [], []
    for head in heads:
        seen = masks_ref[TILE + head : TILE + head + 1, :tokens] > 0.5
        top_score, total = stats_ref[head : head + 1, :], stats_ref[TILE + head : TILE + head + 1, :]
        base_log = top_score + jnp.log(total)
        log_total = jnp.where(seen, joined_row(log_parts[head], 0), base_log)
        share = jnp.exp(base_log - log_total)
        inv_totals.append(1.0 / total)
        attn = jnp.where(seen, attn_parts[head], out_ref[:, every[head]].astype(WIDE))
        normed, _, grad_attn, inner = norm_backward(attn, grad_norm_ref[:, every[head]])
        normeds.append(normed)
        grad_lows.append((share * grad_attn).astype(LOW))
        inners.append(share * inner)
    prob_grads = [contract(v_ref[0, :, every[head]], grad_lows[head], 1, 0) for head in heads]
    softs = [expo_ref[:, every[head]].astype(WIDE) * inv_totals[head] for head in heads]
    soft_lows = [soft.astype(LOW) for soft in softs]
    score_grads = [
        (softs[head] * (prob_grads[head] - inners[head]) * score_scale).astype(LOW)
        for head in heads
    ]
    dqs = [contract(score_grads[head], k_ref[0, :, every[head]], 0, 0) for head in heads]
    placed = [
        contract(
            place_ref[:, pl.ds(head * HEAD_DIM, picked)],
            jnp.concatenate(
                [placed_ref[head, block * picked : (block + 1) * picked] for block in range(3)], 1
            ),
            1,
            0,
        )
        for head in heads
    ]
    dks = [contract(score_grads[head], q_ref[0, :, every[head]], 1, 0) for head in heads]
    dvs = [contract(soft_lows[head], grad_lows[head], 1, 1) for head in heads]
    last = count - 1
    total = sum(ref[4 * picked : 6 * picked].astype(WIDE) for ref in return_refs[1:]).astype(LOW)
    rows = contract(
        place_ref[:, pl.ds(last * HEAD_DIM, picked)],
        jnp.concatenate([total[:picked], total[picked:]], 1),
        1,
        0,
    )
    for head in heads:
        cols = every[head]
        attended_ref[:, cols] = (normeds[head].T * gain_ref[:, cols]).astype(LOW)
        for which, (block, out_block_ref) in enumerate(
            ((dqs[head], dq_ref), (dks[head], dk_ref), (dvs[head], dv_ref))
        ):
            part = placed[head][:, which * HEAD_DIM : (which + 1) * HEAD_DIM]
            out_block_ref[:, cols] = (block + part).astype(LOW)
    cols = head_cols(last)
    attended_ref[:, cols] = last_attended_ref[...]
    dq_ref[:, cols] = last_dq_ref[...]
    dk_ref[:, cols] = (last_dk_ref[...] + rows[:, :HEAD_DIM]).astype(LOW)
    dv_ref[:, cols] = (last_dv_ref[...] + rows[:, HEAD_DIM:]).astype(LOW)


def finish_kernel(gain_ref, gain_rest_ref, *refs):
    block_refs, result_refs, gain_out_ref = refs[:4], refs[4:8], refs[8]
    half = result_refs[0].shape[1]
    rows = pl.ds(pl.multiple_of(pl.program_id(0) * half, half), half)
    for block_ref, result_ref in zip(block_refs, result_refs):
        result_ref[0] = block_ref[rows, :]
    gain_out_ref[...] = (gain_ref[...] + gain_rest_ref[...]).reshape(gain_out_ref.shape)


def across(block, axis, distance):
    route = [(place, place ^ distance) for place in range(lax.axis_size(axis))]
    return lax.ppermute(block, axis, route)


def to_peers(blocks):
    return [across(blocks[distance - 1], "ctx", distance) for distance in START_ORDER]


def row_spec(block, row_steps):
    if not row_steps or len(block.shape) < 3:
        return VMEM_SPEC
    count, rows, width = block.shape
    return pl.BlockSpec((count, rows // row_steps, width), lambda step: (0, step, 0))


def call(
    kernel, name, operands, results, microseconds, vmem=PLAIN_VMEM, scratch=(), row_steps=0
):
    return pl.pallas_call(
        kernel,
        out_shape=results,
        in_specs=[VMEM_SPEC] * len(operands),
        out_specs=[row_spec(block, row_steps) for block in results],
        grid=(row_steps,) if row_steps else (),
        scratch_shapes=scratch,
        compiler_params=pltpu.CompilerParams(vmem_limit_bytes=vmem),
        cost_estimate=pl.CostEstimate(
            flops=int(microseconds * 10**9), bytes_accessed=0, transcendentals=0
        ),
        name=name,
    )(*operands)


def one_segment_shards(queries, keys, values, grad_y, out_gain, offsets):
    tokens, width = queries.shape[1:]
    heads = width // HEAD_DIM
    top_step = lax.axis_size("ctx")
    picked = sum(picked_counts(tokens, top_step))
    shape = jax.ShapeDtypeStruct
    row_block = shape((1, tokens, width), LOW)
    low_block, wide_block = shape((tokens, width), LOW), shape((tokens, width), WIDE)
    low_head, wide_head = shape((tokens, HEAD_DIM), LOW), shape((tokens, HEAD_DIM), WIDE)
    gain_block = shape((1, width), WIDE)
    stats_block = shape((2 * TILE, tokens), WIDE)
    payload = shape((7 * picked + STAT_TILES, HEAD_DIM), LOW)
    answer = shape((6 * picked + STAT_TILES, HEAD_DIM), LOW)
    bind = functools.partial
    gain_row = out_gain.reshape(1, width)
    (picks,) = call(
        bind(picks_kernel, top_step), "picks", (offsets,), [shape((tokens, width + tokens), LOW)], 20
    )
    own, *sent = call(
        bind(pack_kernel, top_step),
        "pack",
        (picks, queries, keys, values, grad_y),
        [payload] * SPAN,
        1,
        scratch=[pltpu.VMEM((OWNED, *payload.shape), LOW)],
    )
    received = to_peers(sent)
    grad_norm, gain_base, place, masks, expo, base_out, stats = call(
        bind(prepare_kernel, top_step),
        "prepare",
        (offsets, queries, keys, values, grad_y, gain_row, picks),
        [
            wide_block,
            gain_block,
            shape((tokens, 2 * width), LOW),
            shape((2 * TILE, 2 * tokens), WIDE),
            low_block,
            low_block,
            stats_block,
        ],
        2,
    )
    normed, grad_low, score_grad, kept, own_answer, *answers = call(
        bind(owner_kernel, top_step),
        "owner",
        (queries, gain_row, base_out, grad_norm, stats, gain_base, masks, own, *received),
        [
            wide_head,
            low_head,
            shape((PEERS * picked, HEAD_DIM), LOW),
            shape((TILE, tokens), WIDE),
        ]
        + [answer] * SPAN,
        3,
    )
    returned = to_peers(answers)
    last_results = call(
        bind(last_head_kernel, top_step),
        "last_head",
        (queries, keys, values, gain_row, expo, normed, grad_low, score_grad, kept, *received),
        [low_head, low_head, wide_head, wide_head],
        20,
    )
    (gain_sum,) = call(bind(gain_kernel, picked), "gain", (own_answer, *returned), [gain_block], 1)
    gain_rest = across(gain_sum, "dp", 1)
    mixed = call(
        bind(mix_kernel, top_step),
        "mix",
        (
            queries,
            keys,
            values,
            gain_row,
            expo,
            base_out,
            grad_norm,
            stats,
            place,
            masks,
            *last_results,
            own_answer,
            *returned,
        ),
        [low_block] * 4,
        20,
        scratch=[pltpu.VMEM((OWNED, *answer.shape), LOW)],
    )
    attended, query_grad, key_grad, value_grad, gain_grad = call(
        finish_kernel,
        "finish",
        (gain_sum, gain_rest, *mixed),
        [row_block] * 4 + [shape((width,), WIDE)],
        1,
        row_steps=2,
    )
    return attended, query_grad, key_grad, value_grad, gain_grad


def shards(*operands):
    one_segment = lax.axis_size("ctx") == SPAN
    if one_segment and operands[0].shape[2] == (OWNED + 1) * HEAD_DIM:
        return one_segment_shards(*operands)
    return general_shards(*operands)


def solution(mesh):
    in_specs = (
        P("dp", "ctx", "head"),
        P("dp", "ctx", "head"),
        P("dp", "ctx", "head"),
        P("dp", "ctx", "head"),
        P("head"),
        P(None, "head"),
    )
    out_specs = (
        P("dp", "ctx", "head"),
        P("dp", "ctx", "head"),
        P("dp", "ctx", "head"),
        P("dp", "ctx", "head"),
        P("head"),
    )
    return jax.shard_map(shards, mesh=mesh, in_specs=in_specs, out_specs=out_specs, check_vma=False)
```

```python
import functools
import math

import jax
import jax.numpy as jnp
from jax import lax
from jax.experimental import pallas as pl
from jax.experimental.pallas import tpu as pltpu
from jax.sharding import PartitionSpec as P

HEAD_DIM = 128
SPAN = 4
R1 = 8


EPS = 1e-06


def swapped(block, axis, bit):
    count = lax.axis_size(axis)
    route = []
    for low in range(count):
        high = low | 1 << bit
        if high != low and high < count:
            route += [(low, high), (high, low)]
    return lax.ppermute(block, axis, route)


def pick_rows(source_rows, dilation, shifts):
    row_count, head_count, head_width = source_rows.shape
    grouped = source_rows.reshape(row_count // dilation, dilation, head_count, head_width)
    hit_mask = jnp.arange(dilation, dtype=jnp.int32).reshape(1, dilation, 1, 1) == shifts.reshape(
        1, 1, head_count, 1
    )
    chosen = jnp.where(hit_mask, grouped, jnp.zeros((), source_rows.dtype))
    return jnp.sum(chosen, axis=1, dtype=source_rows.dtype)


def place_rows(row_values, dilation, shifts):
    row_count, head_count, head_width = row_values.shape
    hit_mask = jnp.arange(dilation, dtype=jnp.int32).reshape(1, dilation, 1, 1) == shifts.reshape(
        1, 1, head_count, 1
    )
    spread = jnp.where(hit_mask, row_values[:, None], jnp.zeros((), row_values.dtype))
    return spread.reshape(row_count * dilation, head_count, head_width)


def level_scores(q_rows, k_rows):
    score_scale = 1.0 / math.sqrt(q_rows.shape[-1])
    return (
        jnp.einsum("qhe,khe->hqk", q_rows, k_rows, preferred_element_type=jnp.float32) * score_scale
    )


def attend(q_rows, k_rows, v_rows):
    scores = level_scores(q_rows, k_rows)
    row_max = jnp.max(scores, axis=-1, keepdims=True)
    log_total = row_max[..., 0] + jnp.log(jnp.sum(jnp.exp(scores - row_max), axis=-1))
    soft_rows = jnp.exp(scores - log_total[..., None]).astype(jnp.bfloat16)
    level_out = jnp.einsum("hqk,khe->qhe", soft_rows, v_rows, preferred_element_type=jnp.float32)
    return (level_out, log_total.T)


def score_grads(q_rows, k_rows, v_rows, log_total, grad_low, row_shift):
    score_scale = 1.0 / math.sqrt(q_rows.shape[-1])
    scores = level_scores(q_rows, k_rows)
    exact_soft = jnp.exp(scores - log_total.T[..., None])
    prob_grad = jnp.einsum("qhe,khe->hqk", grad_low, v_rows, preferred_element_type=jnp.float32)
    score_grad = (exact_soft * (prob_grad + row_shift.T[..., None]) * score_scale).astype(
        jnp.bfloat16
    )
    return (score_grad, exact_soft.astype(jnp.bfloat16))


def key_parts(score_grad, soft_low, q_rows, grad_low):
    k_part = jnp.einsum("hqk,qhe->khe", score_grad, q_rows, preferred_element_type=jnp.float32)
    v_part = jnp.einsum("hqk,qhe->khe", soft_low, grad_low, preferred_element_type=jnp.float32)
    return (k_part, v_part)


def query_part(score_grad, k_rows):
    return jnp.einsum("hqk,khe->qhe", score_grad, k_rows, preferred_element_type=jnp.float32)


def general_shards(queries, keys, values, grad_y, out_gain, offsets):
    tokens = queries.shape[1]
    flat_width = queries.shape[2]
    head_count = flat_width // HEAD_DIM
    row_shape = (tokens, head_count, HEAD_DIM)
    q_own = queries[0].reshape(row_shape)
    k_own = keys[0].reshape(row_shape)
    v_own = values[0].reshape(row_shape)
    ctx_size = lax.axis_size("ctx")
    span_bits = SPAN.bit_length() - 1
    my_place = lax.axis_index("ctx")
    mid_shift = offsets[0]
    top_shift = offsets[1]
    positions = jnp.arange(tokens, dtype=jnp.int32)
    mid_hit = (positions % R1)[:, None] == mid_shift[None, :]
    top_hit = (positions % ctx_size)[:, None] == top_shift[None, :]
    mid_q = pick_rows(q_own, R1, mid_shift)
    mid_k = pick_rows(k_own, R1, mid_shift)
    mid_v = pick_rows(v_own, R1, mid_shift)
    top_q = pick_rows(q_own, ctx_size, top_shift)
    top_k = pick_rows(k_own, ctx_size, top_shift)
    top_v = pick_rows(v_own, ctx_size, top_shift)
    mid_keys = mid_k.reshape(-1, flat_width)
    mid_vals = mid_v.reshape(-1, flat_width)
    top_keys = top_k.reshape(-1, flat_width)
    top_vals = top_v.reshape(-1, flat_width)

    def append_peer(mine, received, level_bit):
        upper_side = my_place >> level_bit & 1 == 1
        return jnp.where(
            upper_side, jnp.concatenate([received, mine], 0), jnp.concatenate([mine, received], 0)
        )

    for level_bit in range(span_bits):
        received = swapped((mid_keys, mid_vals), "ctx", level_bit)
        mid_keys = append_peer(mid_keys, received[0], level_bit)
        mid_vals = append_peer(mid_vals, received[1], level_bit)
    top_keys, top_vals = (
        lax.all_gather(top_keys, "ctx", axis=0, tiled=True),
        lax.all_gather(top_vals, "ctx", axis=0, tiled=True),
    )
    mid_keys = mid_keys.reshape(-1, head_count, HEAD_DIM)
    mid_vals = mid_vals.reshape(-1, head_count, HEAD_DIM)
    top_keys = top_keys.reshape(-1, head_count, HEAD_DIM)
    top_vals = top_vals.reshape(-1, head_count, HEAD_DIM)
    base_out, base_total = attend(q_own, k_own, v_own)
    mid_out, mid_total = attend(mid_q, mid_keys, mid_vals)
    top_out, top_total = attend(top_q, top_keys, top_vals)
    mid_full = place_rows(mid_total[..., None], R1, mid_shift)[..., 0]
    top_full = place_rows(top_total[..., None], ctx_size, top_shift)[..., 0]
    row_max = jnp.maximum(base_total, jnp.where(mid_hit, mid_full, base_total))
    row_max = jnp.maximum(row_max, jnp.where(top_hit, top_full, base_total))
    base_expo = jnp.exp(base_total - row_max)
    mid_expo = jnp.where(mid_hit, jnp.exp(mid_full - row_max), 0.0)
    top_expo = jnp.where(top_hit, jnp.exp(top_full - row_max), 0.0)
    denom = base_expo + mid_expo + top_expo
    base_share = base_expo / denom
    mid_share = mid_expo / denom
    top_share = top_expo / denom
    attn = (
        base_share[..., None] * base_out
        + mid_share[..., None] * place_rows(mid_out, R1, mid_shift)
        + top_share[..., None] * place_rows(top_out, ctx_size, top_shift)
    )
    inv_rms = lax.rsqrt(jnp.mean(attn * attn, axis=-1, keepdims=True) + EPS)
    normed = attn * inv_rms
    gain_rows = out_gain.reshape(head_count, HEAD_DIM)
    attended = (normed * gain_rows).astype(jnp.bfloat16).reshape(1, tokens, flat_width)
    grad_full = grad_y[0].reshape(row_shape).astype(jnp.float32)
    gain_part = jnp.sum(grad_full * normed, axis=0).reshape(flat_width)
    gain_grad = lax.psum(gain_part, ("dp", "ctx"))
    grad_norm = grad_full * gain_rows
    grad_attn = inv_rms * (
        grad_norm - normed * jnp.mean(grad_norm * normed, axis=-1, keepdims=True)
    )
    inner = jnp.sum(grad_attn * attn, axis=-1)
    base_low = (base_share[..., None] * grad_attn).astype(jnp.bfloat16)
    base_shift = -(base_share * inner)
    base_grad, base_soft = score_grads(q_own, k_own, v_own, base_total, base_low, base_shift)
    base_dq = query_part(base_grad, k_own)
    base_dk, base_dv = key_parts(base_grad, base_soft, q_own, base_low)
    mid_sel = pick_rows(mid_share[..., None], R1, mid_shift)[..., 0]
    mid_low = (mid_sel[..., None] * pick_rows(grad_attn, R1, mid_shift)).astype(jnp.bfloat16)
    mid_row_shift = -(mid_sel * pick_rows(inner[..., None], R1, mid_shift)[..., 0])
    mid_grad, mid_soft = score_grads(mid_q, mid_keys, mid_vals, mid_total, mid_low, mid_row_shift)
    mid_dq = query_part(mid_grad, mid_keys)
    mid_dk, mid_dv = key_parts(mid_grad, mid_soft, mid_q, mid_low)
    mid_dk = mid_dk.reshape(-1, flat_width)
    mid_dv = mid_dv.reshape(-1, flat_width)
    for level_bit in reversed(range(span_bits)):
        half_rows = mid_dk.shape[0] // 2
        upper_side = my_place >> level_bit & 1 == 1
        keep_k = jnp.where(upper_side, mid_dk[half_rows:], mid_dk[:half_rows])
        keep_v = jnp.where(upper_side, mid_dv[half_rows:], mid_dv[:half_rows])
        send_k = jnp.where(upper_side, mid_dk[:half_rows], mid_dk[half_rows:])
        send_v = jnp.where(upper_side, mid_dv[:half_rows], mid_dv[half_rows:])
        received = (
            swapped(send_k.astype(jnp.bfloat16), "ctx", level_bit).astype(send_k.dtype),
            swapped(send_v.astype(jnp.bfloat16), "ctx", level_bit).astype(send_v.dtype),
        )
        mid_dk = keep_k + received[0]
        mid_dv = keep_v + received[1]
    mid_dk = mid_dk.reshape(-1, head_count, HEAD_DIM)
    mid_dv = mid_dv.reshape(-1, head_count, HEAD_DIM)
    top_sel = pick_rows(top_share[..., None], ctx_size, top_shift)[..., 0]
    top_low = (top_sel[..., None] * pick_rows(grad_attn, ctx_size, top_shift)).astype(jnp.bfloat16)
    top_row_shift = -(top_sel * pick_rows(inner[..., None], ctx_size, top_shift)[..., 0])
    top_grad, top_soft = score_grads(top_q, top_keys, top_vals, top_total, top_low, top_row_shift)
    top_dq = query_part(top_grad, top_keys)
    gathered_dk, gathered_dv = key_parts(top_grad, top_soft, top_q, top_low)
    summed = (
        lax.psum_scatter(
            gathered_dk.reshape(-1, flat_width), "ctx", scatter_dimension=0, tiled=True
        ),
        lax.psum_scatter(
            gathered_dv.reshape(-1, flat_width), "ctx", scatter_dimension=0, tiled=True
        ),
    )
    top_dk = summed[0].reshape(-1, head_count, HEAD_DIM)
    top_dv = summed[1].reshape(-1, head_count, HEAD_DIM)
    query_grad = (
        base_dq + place_rows(mid_dq, R1, mid_shift) + place_rows(top_dq, ctx_size, top_shift)
    )
    key_grad = base_dk + place_rows(mid_dk, R1, mid_shift) + place_rows(top_dk, ctx_size, top_shift)
    value_grad = (
        base_dv + place_rows(mid_dv, R1, mid_shift) + place_rows(top_dv, ctx_size, top_shift)
    )
    out_shape = (1, tokens, flat_width)
    return (
        attended,
        query_grad.astype(jnp.bfloat16).reshape(out_shape),
        key_grad.astype(jnp.bfloat16).reshape(out_shape),
        value_grad.astype(jnp.bfloat16).reshape(out_shape),
        gain_grad,
    )


VMEM_SPEC = pl.BlockSpec(memory_space=pltpu.VMEM)
PEERS = SPAN - 1
OWNED = SPAN
TILE = 8
STAT_TILES = 2 * TILE
PIECES = 3
NEVER = -1e30
START_ORDER = (3, 1, 2)
LOW = jnp.bfloat16
WIDE = jnp.float32
PLAIN_VMEM = 16 * 1024 * 1024


def contract(left, right, left_dim, right_dim):
    return lax.dot_general(
        left, right, (((left_dim,), (right_dim,)), ((), ())), preferred_element_type=WIDE
    )


def head_cols(head):
    return pl.ds(head * HEAD_DIM, HEAD_DIM)


def picked_counts(tokens, top_step):
    return tokens // top_step, tokens // R1


def offset_of(offsets_ref, level, head):
    return offsets_ref[level : level + 1, head : head + 1]


def pick_matrix(offsets_ref, head, tokens, top_step, picked_axis):
    top_rows, _ = picked_counts(tokens, top_step)
    row = lax.broadcasted_iota(jnp.int32, (tokens, tokens), picked_axis)
    position = lax.broadcasted_iota(jnp.int32, (tokens, tokens), 1 - picked_axis)
    wanted = jnp.where(
        row < top_rows,
        row * top_step + offset_of(offsets_ref, 1, head),
        (row - top_rows) * R1 + offset_of(offsets_ref, 0, head),
    )
    return jnp.where(position == wanted, 1.0, 0.0).astype(LOW)


def rolled(row, shift):
    return pltpu.roll(row, shift % row.shape[1], 1)


def lane_window(row, start, count):
    lane = lax.broadcasted_iota(jnp.int32, row.shape, 1)
    return jnp.where((lane >= start) & (lane < start + count), row, 0.0)


def hit_row(offset, step, tokens):
    position = lax.broadcasted_iota(jnp.int32, (1, tokens), 1)
    return jnp.where(position % step == offset, 1.0, 0.0)


def piece_rows(row, others=None):
    pieces = []
    for _ in range(PIECES):
        piece = row.astype(LOW).astype(WIDE)
        pieces.append(piece)
        row = row - piece
    if others is None:
        others = jnp.zeros((TILE - PIECES, row.shape[1]), WIDE)
    return jnp.concatenate(pieces + [others], 0)


def gain_pieces(rows):
    high = rows.astype(LOW)
    return high, (rows - high.astype(WIDE)).astype(LOW)


def joined_row(rows, first):
    total = rows[first : first + 1]
    for piece in range(1, PIECES):
        total = total + rows[first + piece : first + piece + 1]
    return total


def gain_row_of(ones, product):
    high, rest = gain_pieces(product)
    return (contract(ones, high, 1, 1) + contract(ones, rest, 1, 1))[:1]


def column_mean(block):
    return jnp.mean(block, axis=0, keepdims=True)


def norm_backward(attn, grad_norm):
    inv_rms = lax.rsqrt(column_mean(attn * attn) + EPS)
    normed = attn * inv_rms
    product = grad_norm * normed
    grad_attn = inv_rms * (grad_norm - normed * column_mean(product))
    inner = jnp.sum(grad_attn * attn, axis=0, keepdims=True)
    return normed, product, grad_attn, inner


def nearest_first(refs):
    by_distance = dict(zip(START_ORDER, refs[1:]))
    return [refs[0], *[by_distance[distance] for distance in range(1, SPAN)]]


def picks_kernel(top_step, offsets_ref, picks_ref):
    tokens = picks_ref.shape[0]
    last = offsets_ref.shape[1] - 1
    for head in range(last + 1):
        picks_ref[:, head_cols(head)] = pick_matrix(offsets_ref, head, tokens, top_step, 0)
    key_row = lax.broadcasted_iota(jnp.int32, (tokens, 1), 0)
    times = 1.0
    for level, step in ((0, R1), (1, top_step)):
        offset = offset_of(offsets_ref, level, last)
        hit_column = jnp.where(key_row % step == offset, 1.0, 0.0)
        times = times + hit_column * hit_row(offset, step, tokens)
    picks_ref[:, head_cols(last + 1)] = times.astype(LOW)


def pack_kernel(top_step, picks_ref, q_ref, k_ref, v_ref, grad_ref, *payload_refs):
    tokens, width = q_ref.shape[1:]
    me = lax.axis_index("ctx")
    picked = sum(picked_counts(tokens, top_step))
    score_scale = 1.0 / math.sqrt(HEAD_DIM)
    places = range(SPAN)
    sent_cols = [
        pl.ds(pl.multiple_of((me ^ distance) * HEAD_DIM, HEAD_DIM), HEAD_DIM) for distance in places
    ]
    last_cols = head_cols(width // HEAD_DIM - 1)
    q_rows, k_rows, v_rows, grad_rows = [
        [ref[0, :, cols] for cols in sent_cols] for ref in (q_ref, k_ref, v_ref, grad_ref)
    ]
    picks = [picks_ref[:, cols] for cols in sent_cols]
    scores = [contract(k_rows[i], q_rows[i], 1, 1) * score_scale for i in places]
    moved = [
        contract(
            picks[i][:picked],
            jnp.concatenate([q_rows[i], k_rows[i], v_rows[i], grad_rows[i]], 1),
            1,
            0,
        ).astype(LOW)
        for i in places
    ]
    shared = contract(
        picks_ref[:picked, last_cols],
        jnp.concatenate([k_ref[0, :, last_cols], v_ref[0, :, last_cols]], 1),
        1,
        0,
    ).astype(LOW)
    top_scores = [jnp.max(block, axis=0, keepdims=True) for block in scores]
    expos = [jnp.exp(scores[i] - top_scores[i]) for i in places]
    expo_lows = [expo.astype(LOW) for expo in expos]
    outs = [contract(v_rows[i], expo_lows[i], 0, 0) for i in places]
    totals = [jnp.sum(expo, axis=0, keepdims=True) for expo in expos]
    outs = [(outs[i] * (1.0 / totals[i])).astype(LOW) for i in places]
    picked_outs = [contract(picks[i][:picked], outs[i], 1, 1).astype(LOW) for i in places]
    pieces = [piece_rows(top_scores[i] + jnp.log(totals[i])).astype(LOW) for i in places]
    stat_rows = [contract(pieces[i], picks[i], 1, 1) for i in places]
    for i, payload_ref in enumerate(payload_refs):
        for block in range(4):
            payload_ref[block * picked : (block + 1) * picked] = moved[i][
                :, block * HEAD_DIM : (block + 1) * HEAD_DIM
            ]
        payload_ref[4 * picked : 5 * picked] = picked_outs[i]
        payload_ref[5 * picked : 6 * picked] = shared[:, :HEAD_DIM]
        payload_ref[6 * picked : 7 * picked] = shared[:, HEAD_DIM:]
        payload_ref[7 * picked :] = jnp.concatenate(
            [stat_rows[i], jnp.zeros_like(stat_rows[i])], 0
        ).astype(LOW)


def prepare_kernel(top_step, offsets_ref, q_ref, k_ref, v_ref, grad_ref, gain_ref, *refs):
    picks_ref, grad_norm_ref, gain_part_ref, place_ref, masks_ref, expo_ref, out_ref, stats_ref = refs
    tokens, width = grad_ref.shape[1:]
    heads = range(width // HEAD_DIM)
    score_scale = 1.0 / math.sqrt(HEAD_DIM)
    every = [head_cols(head) for head in heads]
    scores = [
        contract(k_ref[0, :, cols], q_ref[0, :, cols], 1, 1) * score_scale for cols in every
    ]
    top_scores = [jnp.max(block, axis=0, keepdims=True) for block in scores]
    expos = [jnp.exp(scores[head] - top_scores[head]) for head in heads]
    times = picks_ref[:, head_cols(len(heads))].astype(WIDE)
    for head in heads[OWNED:]:
        expos[head] = times * expos[head]
    expo_lows = [expo.astype(LOW) for expo in expos]
    outs = [contract(v_ref[0, :, cols], expo_lows[head], 0, 0) for head, cols in enumerate(every)]
    totals = [jnp.sum(expo, axis=0, keepdims=True) for expo in expos]
    for head in range(OWNED):
        outs[head] = outs[head] * (1.0 / totals[head])
    outs = [out.astype(LOW) for out in outs]
    for head, cols in enumerate(every):
        expo_ref[:, cols] = expo_lows[head]
        out_ref[:, cols] = outs[head]
        stats_ref[head : head + 1, :] = top_scores[head]
        stats_ref[TILE + head : TILE + head + 1, :] = totals[head]
    top_rows = tokens // top_step
    ones = jnp.ones((TILE, tokens), LOW)
    column = lax.broadcasted_iota(jnp.int32, (tokens, tokens), 1)
    gain_part_ref[...] = jnp.zeros(gain_part_ref.shape, WIDE)
    me = lax.axis_index("ctx")
    mid_rows = tokens // R1
    top_all, queries = SPAN * top_rows, SPAN * (top_rows + mid_rows)
    mid_offset, top_offset = [
        sum(
            jnp.where(me == head, offset_of(offsets_ref, level, head), 0) for head in range(OWNED)
        )
        for level in (0, 1)
    ]
    lane = lax.broadcasted_iota(jnp.int32, (1, queries), 1)
    is_top = jnp.where(lane < top_all, 1.0, 0.0)
    top_in_mid = jnp.where(((lane % top_rows) * top_step + top_offset) % R1 == mid_offset, 1.0, 0.0)
    both_flag = jnp.where(mid_offset % top_step == top_offset, 1.0, 0.0)
    sees_top = is_top + (1.0 - is_top) * both_flag
    sees_mid = is_top * top_in_mid + (1.0 - is_top)
    masks_ref[0:1, :queries] = (1.0 - sees_top) * NEVER
    masks_ref[1:2, :queries] = (1.0 - sees_mid) * NEVER
    masks_ref[2:3, :queries] = is_top + (1.0 - is_top) * (1.0 - both_flag)
    last = len(heads) - 1
    for row, (level, step) in enumerate(((1, top_step), (0, R1))):
        hits = hit_row(offset_of(offsets_ref, level, last), step, tokens)
        masks_ref[3 + row : 4 + row, :tokens] = (1.0 - hits) * NEVER
    grad_norms = [
        (grad_ref[0, :, head_cols(head)].astype(WIDE) * gain_ref[:, head_cols(head)]).T
        for head in heads
    ]
    for head in heads:
        cols = head_cols(head)
        grad_norm_ref[:, cols] = grad_norms[head]
        picks = pick_matrix(offsets_ref, head, tokens, top_step, 1)
        place_ref[:, cols] = picks
    for head in range(OWNED):
        cols = head_cols(head)
        mid_offset, top_offset = [offset_of(offsets_ref, level, head) for level in (0, 1)]
        seen = jnp.maximum(
            hit_row(top_offset, top_step, tokens), hit_row(mid_offset, R1, tokens)
        )
        masks_ref[TILE + head : TILE + head + 1, :tokens] = seen
        attn = outs[head].astype(WIDE)
        normed = attn * lax.rsqrt(column_mean(attn * attn) + EPS)
        product = grad_norms[head] * normed * (1.0 - seen)
        gain_part_ref[:, cols] = gain_row_of(ones, product) / gain_ref[:, cols]
        both = mid_offset % top_step == top_offset
        kept = jnp.where(column < top_rows, 1.0, jnp.where(both, 0.0, 1.0)).astype(LOW)
        picks = pick_matrix(offsets_ref, head, tokens, top_step, 1)
        place_ref[:, head_cols(len(heads) + head)] = picks * kept


def owner_kernel(top_step, q_ref, gain_ref, out_ref, grad_norm_ref, *refs):
    stats_ref, gain_base_ref, masks_ref = refs[:3]
    payload_refs, refs = nearest_first(refs[3 : 3 + SPAN]), refs[3 + SPAN :]
    normed_ref, grad_low_ref, score_grad_ref, kept_ref = refs[:4]
    return_refs = refs[4:]
    tokens = q_ref.shape[1]
    heads = q_ref.shape[2] // HEAD_DIM
    top_rows, mid_rows = picked_counts(tokens, top_step)
    picked = top_rows + mid_rows
    top_all, mid_all = SPAN * top_rows, SPAN * mid_rows
    queries = top_all + mid_all
    score_scale = 1.0 / math.sqrt(HEAD_DIM)
    me = lax.axis_index("ctx")
    ones = jnp.ones((TILE, tokens), LOW)

    def by_level(block):
        start = block * picked
        return jnp.concatenate(
            [ref[start : start + top_rows] for ref in payload_refs]
            + [ref[start + top_rows : start + picked] for ref in payload_refs],
            0,
        )

    def per_level(top_row, mid_row):
        return jnp.concatenate(
            [
                jnp.broadcast_to(top_row, (top_all, queries)),
                jnp.broadcast_to(mid_row, (mid_all, queries)),
            ],
            0,
        )

    q_rows, k_rows, v_rows, grad_rows, base_rows = [by_level(block) for block in range(5)]
    stat_start = 7 * picked
    logs = [
        joined_row(ref[stat_start : stat_start + STAT_TILES].astype(WIDE), 0)
        for ref in payload_refs
    ]
    base_top_log = sum(
        rolled(lane_window(log, 0, top_rows), slot * top_rows) for slot, log in enumerate(logs)
    )
    base_mid_log = sum(
        rolled(lane_window(log, top_rows, mid_rows), slot * mid_rows - top_rows)
        for slot, log in enumerate(logs)
    )
    base_log = jnp.concatenate([base_top_log, base_mid_log[:, :mid_all]], 1)
    gain_row = jnp.zeros((1, HEAD_DIM), WIDE)
    for head in range(OWNED):
        gain_row = gain_row + jnp.where(me == head, 1.0, 0.0) * gain_ref[:, head_cols(head)]
    lane = lax.broadcasted_iota(jnp.int32, (1, queries), 1)
    is_top = jnp.where(lane < top_all, 1.0, 0.0)
    bias = per_level(masks_ref[0:1, :queries], masks_ref[1:2, :queries])
    last = heads - 1
    cols = head_cols(last)
    peers = payload_refs[1:]
    q_last = q_ref[0, :, cols]
    k_peers = jnp.concatenate([ref[5 * picked : 6 * picked] for ref in peers], 0)
    v_peers = jnp.concatenate([ref[6 * picked : 7 * picked] for ref in peers], 0)
    last_biases = [
        jnp.broadcast_to(masks_ref[row : row + 1, :tokens], (count, tokens))
        for row, count in ((3, top_rows), (4, mid_rows))
    ]
    scores = contract(k_rows, q_rows, 1, 1) * score_scale + bias
    scores_last = contract(k_peers, q_last, 1, 1) * score_scale + jnp.concatenate(
        last_biases * PEERS, 0
    )
    base_attn = base_rows.astype(WIDE).T
    grad_norm = (grad_rows.astype(WIDE) * gain_row).T
    top_score = jnp.maximum(base_log, jnp.max(scores, axis=0, keepdims=True))
    base_top, base_total = stats_ref[last : last + 1, :], stats_ref[TILE + last : TILE + last + 1, :]
    top_last = jnp.maximum(base_top, jnp.max(scores_last, axis=0, keepdims=True))
    expo = jnp.exp(scores - top_score)
    expo_last = jnp.exp(scores_last - top_last)
    factor = jnp.exp(base_log - top_score)
    factor_last = jnp.exp(base_top - top_last)
    total = factor + jnp.sum(expo, axis=0, keepdims=True)
    total_last = factor_last * base_total + jnp.sum(expo_last, axis=0, keepdims=True)
    inv_total, inv_last = 1.0 / total, 1.0 / total_last
    expo_low, expo_last_low = expo.astype(LOW), expo_last.astype(LOW)
    attn = (factor * base_attn + contract(v_rows, expo_low, 0, 0)) * inv_total
    attn_last = (
        factor_last * out_ref[:, cols].astype(WIDE) + contract(v_peers, expo_last_low, 0, 0)
    ) * inv_last
    _, product, grad_attn, inner = norm_backward(attn, grad_norm)
    normed_last, product_last, grad_attn_last, inner_last = norm_backward(
        attn_last, grad_norm_ref[:, cols]
    )
    grad_low, inner = (grad_attn * inv_total).astype(LOW), inner * inv_total
    grad_last_low = (grad_attn_last * inv_last).astype(LOW)
    base_factor = factor_last * inv_last
    spans = (slice(0, top_all), slice(top_all, queries))
    prob_grads = [contract(v_rows[span], grad_low[:, span], 1, 0) for span in spans]
    prob_grad_last = contract(v_peers, grad_last_low, 1, 0)
    score_grads = [
        (expo[span, span] * (prob_grad - inner[:, span]) * score_scale).astype(LOW)
        for span, prob_grad in zip(spans, prob_grads)
    ]
    score_grad_last = (
        expo_last * (prob_grad_last - inner_last * inv_last) * score_scale
    ).astype(LOW)
    dks = [
        contract(score_grad, q_rows[span], 1, 0).astype(LOW)
        for span, score_grad in zip(spans, score_grads)
    ]
    dk_last = contract(score_grad_last, q_last, 1, 0).astype(LOW)
    dvs = [
        contract(expo_low[span, span], grad_low[:, span], 1, 1).astype(LOW) for span in spans
    ]
    dv_last = contract(expo_last_low, grad_last_low, 1, 1).astype(LOW)
    dqs = [
        contract(score_grad, k_rows[span], 0, 0).astype(LOW)
        for span, score_grad in zip(spans, score_grads)
    ]
    attn_rows = attn.T.astype(LOW)
    attn_parts = [attn_rows[span] for span in spans]
    log_total = top_score + jnp.log(total)
    padding = jnp.zeros((1, top_all - mid_all), WIDE)
    once = masks_ref[2:3, :queries]
    ones_all = jnp.ones((TILE, queries), LOW)
    own_gain = gain_row_of(ones_all, product * once) / gain_row
    gain_rows = [
        gain_base_ref[:, head_cols(head)] + jnp.where(me == head, 1.0, 0.0) * own_gain
        for head in range(OWNED)
    ]
    gain_rows.append(gain_row_of(ones, product_last) / gain_ref[:, cols])
    gain_high, gain_rest = [
        rows.astype(WIDE) for rows in gain_pieces(jnp.concatenate(gain_rows, 0))
    ]
    top_log, mid_log = log_total[:, :top_all], jnp.concatenate(
        [log_total[:, top_all:], padding], 1
    )
    empty = jnp.zeros((PIECES, HEAD_DIM), WIDE)
    for distance, return_ref in enumerate(return_refs):
        blocks = []
        for top_block, mid_block in (dqs, dks, dvs, attn_parts):
            blocks.append(top_block[distance * top_rows : (distance + 1) * top_rows])
            blocks.append(mid_block[distance * mid_rows : (distance + 1) * mid_rows])
        start = max(distance - 1, 0) * picked
        blocks += [dk_last[start : start + picked], dv_last[start : start + picked]]
        log_row = lane_window(rolled(top_log, -distance * top_rows), 0, top_rows) + lane_window(
            rolled(mid_log, top_rows - distance * mid_rows), top_rows, mid_rows
        )
        log_rows = [piece_rows(log_row, gain_high), empty, gain_rest]
        blocks.append(jnp.concatenate(log_rows, 0).astype(LOW))
        return_ref[...] = jnp.concatenate(blocks, 0)
    normed_ref[...] = normed_last
    grad_low_ref[...] = (grad_attn_last * base_factor).astype(LOW)
    score_grad_ref[...] = score_grad_last
    kept_ref[0:1, :] = inner_last * base_factor


def last_head_kernel(top_step, q_ref, k_ref, v_ref, gain_ref, expo_ref, *refs):
    normed_ref, grad_low_ref, peer_score_grad_ref, kept_ref, *peers = refs[: 4 + PEERS]
    peers = nearest_first([None, *peers])[1:]
    attended_ref, dq_ref, dk_ref, dv_ref = refs[4 + PEERS :]
    picked = sum(picked_counts(q_ref.shape[1], top_step))
    score_scale = 1.0 / math.sqrt(HEAD_DIM)
    cols = head_cols(q_ref.shape[2] // HEAD_DIM - 1)
    attended_ref[...] = (normed_ref[...].T * gain_ref[:, cols]).astype(LOW)
    k_peers = jnp.concatenate([ref[5 * picked : 6 * picked] for ref in peers], 0)
    grad_low = grad_low_ref[...]
    expo_low = expo_ref[:, cols]
    prob_grad = contract(v_ref[0, :, cols], grad_low, 1, 0)
    score_grad = (
        expo_low.astype(WIDE) * (prob_grad - kept_ref[0:1, :]) * score_scale
    ).astype(LOW)
    dk_ref[...] = contract(score_grad, q_ref[0, :, cols], 1, 0)
    dv_ref[...] = contract(expo_low, grad_low, 1, 1)
    dq_ref[...] = (
        contract(score_grad, k_ref[0, :, cols], 0, 0)
        + contract(peer_score_grad_ref[...], k_peers, 0, 0)
    ).astype(LOW)


def gain_kernel(picked, *refs):
    return_refs, gain_ref = nearest_first(refs[:SPAN]), refs[SPAN]
    tiles = [ref[6 * picked : 6 * picked + STAT_TILES].astype(WIDE) for ref in return_refs]
    parts = [tile[PIECES:TILE] + tile[TILE + PIECES :] for tile in tiles]
    total = (parts[0] + parts[1]) + (parts[2] + parts[3])
    for head in range(gain_ref.shape[1] // HEAD_DIM):
        gain_ref[:, head_cols(head)] = total[head : head + 1]


def mix_kernel(top_step, q_ref, k_ref, v_ref, gain_ref, expo_ref, out_ref, *refs):
    grad_norm_ref, stats_ref, place_ref, masks_ref = refs[:4]
    last_attended_ref, last_dq_ref, last_dk_ref, last_dv_ref = refs[4:8]
    return_refs, refs = nearest_first(refs[8 : 8 + SPAN]), refs[8 + SPAN :]
    attended_ref, dq_ref, dk_ref, dv_ref, placed_ref = refs
    tokens, width = v_ref.shape[1:]
    count = width // HEAD_DIM
    picked = sum(picked_counts(tokens, top_step))
    score_scale = 1.0 / math.sqrt(HEAD_DIM)
    me = lax.axis_index("ctx")
    heads = range(OWNED)
    every = [head_cols(head) for head in heads]
    for distance, return_ref in enumerate(return_refs):
        placed_ref[me ^ distance] = return_ref[...]
    once = [place_ref[:, head_cols(count + head)] for head in heads]
    attn_parts = [
        contract(placed_ref[head, 3 * picked : 4 * picked], once[head][:, :picked], 0, 1)
        for head in heads
    ]
    log_parts = [
        contract(placed_ref[head, 6 * picked : 6 * picked + STAT_TILES], once[head], 1, 1)
        for head in heads
    ]
    normeds, grad_lows, inners, inv_totals = [], [], [], []
    for head in heads:
        seen = masks_ref[TILE + head : TILE + head + 1, :tokens] > 0.5
        top_score, total = stats_ref[head : head + 1, :], stats_ref[TILE + head : TILE + head + 1, :]
        base_log = top_score + jnp.log(total)
        log_total = jnp.where(seen, joined_row(log_parts[head], 0), base_log)
        share = jnp.exp(base_log - log_total)
        inv_totals.append(1.0 / total)
        attn = jnp.where(seen, attn_parts[head], out_ref[:, every[head]].astype(WIDE))
        normed, _, grad_attn, inner = norm_backward(attn, grad_norm_ref[:, every[head]])
        normeds.append(normed)
        grad_lows.append((share * grad_attn).astype(LOW))
        inners.append(share * inner)
    prob_grads = [contract(v_ref[0, :, every[head]], grad_lows[head], 1, 0) for head in heads]
    softs = [expo_ref[:, every[head]].astype(WIDE) * inv_totals[head] for head in heads]
    soft_lows = [soft.astype(LOW) for soft in softs]
    score_grads = [
        (softs[head] * (prob_grads[head] - inners[head]) * score_scale).astype(LOW)
        for head in heads
    ]
    dqs = [contract(score_grads[head], k_ref[0, :, every[head]], 0, 0) for head in heads]
    placed = [
        contract(
            place_ref[:, pl.ds(head * HEAD_DIM, picked)],
            jnp.concatenate(
                [placed_ref[head, block * picked : (block + 1) * picked] for block in range(3)], 1
            ),
            1,
            0,
        )
        for head in heads
    ]
    dks = [contract(score_grads[head], q_ref[0, :, every[head]], 1, 0) for head in heads]
    dvs = [contract(soft_lows[head], grad_lows[head], 1, 1) for head in heads]
    last = count - 1
    total = sum(ref[4 * picked : 6 * picked].astype(WIDE) for ref in return_refs[1:]).astype(LOW)
    rows = contract(
        place_ref[:, pl.ds(last * HEAD_DIM, picked)],
        jnp.concatenate([total[:picked], total[picked:]], 1),
        1,
        0,
    )
    for head in heads:
        cols = every[head]
        attended_ref[:, cols] = (normeds[head].T * gain_ref[:, cols]).astype(LOW)
        for which, (block, out_block_ref) in enumerate(
            ((dqs[head], dq_ref), (dks[head], dk_ref), (dvs[head], dv_ref))
        ):
            part = placed[head][:, which * HEAD_DIM : (which + 1) * HEAD_DIM]
            out_block_ref[:, cols] = (block + part).astype(LOW)
    cols = head_cols(last)
    attended_ref[:, cols] = last_attended_ref[...]
    dq_ref[:, cols] = last_dq_ref[...]
    dk_ref[:, cols] = (last_dk_ref[...] + rows[:, :HEAD_DIM]).astype(LOW)
    dv_ref[:, cols] = (last_dv_ref[...] + rows[:, HEAD_DIM:]).astype(LOW)


def finish_kernel(gain_ref, gain_rest_ref, *refs):
    block_refs, result_refs, gain_out_ref = refs[:4], refs[4:8], refs[8]
    half = result_refs[0].shape[1]
    rows = pl.ds(pl.multiple_of(pl.program_id(0) * half, half), half)
    for block_ref, result_ref in zip(block_refs, result_refs):
        result_ref[0] = block_ref[rows, :]
    gain_out_ref[...] = (gain_ref[...] + gain_rest_ref[...]).reshape(gain_out_ref.shape)


def across(block, axis, distance):
    route = [(place, place ^ distance) for place in range(lax.axis_size(axis))]
    return lax.ppermute(block, axis, route)


def to_peers(blocks):
    return [across(blocks[distance - 1], "ctx", distance) for distance in START_ORDER]


def row_spec(block, row_steps):
    if not row_steps or len(block.shape) < 3:
        return VMEM_SPEC
    count, rows, width = block.shape
    return pl.BlockSpec((count, rows // row_steps, width), lambda step: (0, step, 0))


def call(
    kernel, name, operands, results, microseconds, vmem=PLAIN_VMEM, scratch=(), row_steps=0
):
    return pl.pallas_call(
        kernel,
        out_shape=results,
        in_specs=[VMEM_SPEC] * len(operands),
        out_specs=[row_spec(block, row_steps) for block in results],
        grid=(row_steps,) if row_steps else (),
        scratch_shapes=scratch,
        compiler_params=pltpu.CompilerParams(vmem_limit_bytes=vmem),
        cost_estimate=pl.CostEstimate(
            flops=int(microseconds * 10**9), bytes_accessed=0, transcendentals=0
        ),
        name=name,
    )(*operands)


def one_segment_shards(queries, keys, values, grad_y, out_gain, offsets):
    tokens, width = queries.shape[1:]
    heads = width // HEAD_DIM
    top_step = lax.axis_size("ctx")
    picked = sum(picked_counts(tokens, top_step))
    shape = jax.ShapeDtypeStruct
    row_block = shape((1, tokens, width), LOW)
    low_block, wide_block = shape((tokens, width), LOW), shape((tokens, width), WIDE)
    low_head, wide_head = shape((tokens, HEAD_DIM), LOW), shape((tokens, HEAD_DIM), WIDE)
    gain_block = shape((1, width), WIDE)
    stats_block = shape((2 * TILE, tokens), WIDE)
    payload = shape((7 * picked + STAT_TILES, HEAD_DIM), LOW)
    answer = shape((6 * picked + STAT_TILES, HEAD_DIM), LOW)
    bind = functools.partial
    gain_row = out_gain.reshape(1, width)
    (picks,) = call(
        bind(picks_kernel, top_step), "picks", (offsets,), [shape((tokens, width + tokens), LOW)], 20
    )
    own, *sent = call(
        bind(pack_kernel, top_step),
        "pack",
        (picks, queries, keys, values, grad_y),
        [payload] * SPAN,
        1,
    )
    received = to_peers(sent)
    grad_norm, gain_base, place, masks, expo, base_out, stats = call(
        bind(prepare_kernel, top_step),
        "prepare",
        (offsets, queries, keys, values, grad_y, gain_row, picks),
        [
            wide_block,
            gain_block,
            shape((tokens, 2 * width), LOW),
            shape((2 * TILE, 2 * tokens), WIDE),
            low_block,
            low_block,
            stats_block,
        ],
        2,
    )
    normed, grad_low, score_grad, kept, own_answer, *answers = call(
        bind(owner_kernel, top_step),
        "owner",
        (queries, gain_row, base_out, grad_norm, stats, gain_base, masks, own, *received),
        [
            wide_head,
            low_head,
            shape((PEERS * picked, HEAD_DIM), LOW),
            shape((TILE, tokens), WIDE),
        ]
        + [answer] * SPAN,
        3,
    )
    returned = to_peers(answers)
    last_results = call(
        bind(last_head_kernel, top_step),
        "last_head",
        (queries, keys, values, gain_row, expo, normed, grad_low, score_grad, kept, *received),
        [low_head, low_head, wide_head, wide_head],
        20,
    )
    (gain_sum,) = call(bind(gain_kernel, picked), "gain", (own_answer, *returned), [gain_block], 1)
    gain_rest = across(gain_sum, "dp", 1)
    mixed = call(
        bind(mix_kernel, top_step),
        "mix",
        (
            queries,
            keys,
            values,
            gain_row,
            expo,
            base_out,
            grad_norm,
            stats,
            place,
            masks,
            *last_results,
            own_answer,
            *returned,
        ),
        [low_block] * 4,
        20,
        scratch=[pltpu.VMEM((OWNED, *answer.shape), LOW)],
    )
    attended, query_grad, key_grad, value_grad, gain_grad = call(
        finish_kernel,
        "finish",
        (gain_sum, gain_rest, *mixed),
        [row_block] * 4 + [shape((width,), WIDE)],
        1,
        row_steps=2,
    )
    return attended, query_grad, key_grad, value_grad, gain_grad


def shards(*operands):
    one_segment = lax.axis_size("ctx") == SPAN
    if one_segment and operands[0].shape[2] == (OWNED + 1) * HEAD_DIM:
        return one_segment_shards(*operands)
    return general_shards(*operands)


def solution(mesh):
    in_specs = (
        P("dp", "ctx", "head"),
        P("dp", "ctx", "head"),
        P("dp", "ctx", "head"),
        P("dp", "ctx", "head"),
        P("head"),
        P(None, "head"),
    )
    out_specs = (
        P("dp", "ctx", "head"),
        P("dp", "ctx", "head"),
        P("dp", "ctx", "head"),
        P("dp", "ctx", "head"),
        P("head"),
    )
    return jax.shard_map(shards, mesh=mesh, in_specs=in_specs, out_specs=out_specs, check_vma=False)
```
